32 devices in a mesh: dp: 8 (over z, x), tensor: 4 (over y, core).
Axes of the slice: x: 2, y: 2, z: 4, core: 2. Of those that a mesh axis runs over, the one named last changes fastest.
Arguments:
- layer_input: bfloat16 [2, 8192, 768], P(None, 'dp'), may hold values from -6 to 6
- out_grad: bfloat16 [2, 8192, 768], P(None, 'dp'), may hold values from -6 to 6
- first_gain: bfloat16 [768], P('dp'), may hold values from 0.099609375 to 1.8984375
- query_weight: bfloat16 [768, 768], P('dp', 'tensor'), may hold values from -0.21875 to 0.21875
- key_weight: bfloat16 [768, 768], P('dp', 'tensor'), may hold values from -0.21875 to 0.21875
- value_weight: bfloat16 [768, 768], P('dp', 'tensor'), may hold values from -0.21875 to 0.21875
- output_weight: bfloat16 [768, 768], P('tensor', 'dp'), may hold values from -0.875 to 0.875
- position_bias: bfloat16 [12, 32], P('tensor'), may hold values from -4 to 4
- second_gain: bfloat16 [768], P('dp'), may hold values from 0.099609375 to 1.8984375
- router_weight: bfloat16 [768, 8], P('dp'), may hold values from -0.15625 to 0.15625
- expert_in: bfloat16 [8, 768, 3072], P('dp', None, 'tensor'), may hold values from -0.21875 to 0.21875
- expert_out: bfloat16 [8, 3072, 768], P('dp', 'tensor'), may hold values from -0.109375 to 0.109375
- seq_lengths: int32 [2, 8], P(None, 'dp'), may hold values from 512 to 1024, as said below
- routes: int32 [2, 8192, 2], P(None, 'dp'), may hold values from 0 to 7, all different within a row; in each aligned block of 1024 rows (0 to 1023, 1024 to 2047, ..., all dimensions but the last counted through in order) at most 320 rows name the same one
Outputs:
- layer_output: bfloat16 [2, 8192, 768], P(None, 'dp')
- input_grad: bfloat16 [2, 8192, 768], P(None, 'dp')
- first_gain_grad: float32 [768], P('dp')
- query_weight_grad: float32 [768, 768], P('dp', 'tensor')
- key_weight_grad: float32 [768, 768], P('dp', 'tensor')
- value_weight_grad: float32 [768, 768], P('dp', 'tensor')
- output_weight_grad: float32 [768, 768], P('tensor', 'dp')
- position_bias_grad: float32 [12, 32], P('tensor')
- second_gain_grad: float32 [768], P('dp')
- router_weight_grad: float32 [768, 8], P('dp')
- expert_in_grad: float32 [8, 768, 3072], P('dp', None, 'tensor')
- expert_out_grad: float32 [8, 3072, 768], P('dp', 'tensor')
The draws below stay inside these ranges and needn't reach their ends.
Inputs may be any that keep to these rules, and one draw needn't show every extreme that they name: `seq_lengths`: in each micro-batch some sequence has all 1024 slots used. `routes`: A slot's two experts differ. In each micro-batch the 1024 slots of one index of dp name one expert at most 320 times, a bound that some block reaches.
All inputs are finite; a program needn't handle non-finite values.
Results may differ from the reference program's by a relative error of at most 0.017.
Values may be sent and summed in bfloat16 or wider, within the bound.
No kernel may reach another device: no remote copies, remote signals or barrier semaphores. Data moves between devices by JAX's collectives and lax.ppermute only.
A program may use at most 320 MiB of HBM per device.

```python
import math
import jax
import jax.numpy as jnp
import numpy as np
from jax import lax

D = 768
HEADS = 12
HEAD_DIM = 64
FF = 3072
NB = 32
SEQ = 1024
MB = 2
EXPERTS = 8
TOK_MB = 1024
TOKENS = 8192
NSEQ = 8
CAP = 320
N_DP = 8


def draw_seq_lengths(key, part):
    key = jax.random.fold_in(key, 7)
    first_key, second_key = jax.random.split(key)
    values = jax.random.randint(first_key, (MB, NSEQ), SEQ // 2, SEQ + 1)
    chosen = jax.random.randint(second_key, (MB, 1), 0, NSEQ)
    return jnp.where(jnp.arange(NSEQ)[None, :] == chosen, SEQ, values).astype(jnp.int32)


def levels(key, extent, cuts, low, largest):
    loudness = 1.0
    for dim, shards_of in cuts:
        heights = jax.random.uniform(jax.random.fold_in(jax.random.fold_in(key, 6), dim), (shards_of,), jnp.float32, low / len(cuts), largest / len(cuts))
        loudness = loudness * jnp.repeat(jnp.exp(heights), extent[dim] // shards_of).reshape((-1,) + (1,) * (len(extent) - 1 - dim))
    return loudness


def routed_block(stream_key, own, number, rows, amount, top, most, slope):
    sequence = jax.random.permutation(stream_key, amount)
    packed, common = load_shares(amount, rows * top, most, slope, True), load_shares(amount, rows * top, most, slope, False)
    places = jnp.arange(amount)

    def named(sizes, offset_by):
        used = int((sizes > 0).sum())
        fixed = max(1, used // 4)
        moved = fixed + (places - fixed + offset_by * (used - fixed)) % max(1, amount - fixed)
        return jnp.zeros((amount,), jnp.int32).at[sequence[jnp.where(places < fixed, places, moved)]].set(jnp.asarray(sizes, jnp.int32))

    sizes = jnp.where(number % 4 == 0, named(packed, number // 4), named(common, number - number // 4 - 1))
    mixed = jax.random.permutation(jax.random.fold_in(own, 3), amount)
    giver, taker = mixed[0:amount // 2 * 2:2], mixed[1:amount // 2 * 2:2]
    margin = jnp.minimum(sizes[giver] - 1, most - sizes[taker]) // 2
    margin = jnp.where((giver == sequence[0]) | (taker == sequence[0]) | (sizes[taker] == 0), 0, jnp.maximum(margin, 0))
    moved = jax.random.randint(jax.random.fold_in(own, 4), (amount // 2,), 0, 1 << 20) % (margin + 1)
    sizes = sizes.at[giver].add(-moved).at[taker].add(moved)
    items = jnp.searchsorted(jnp.cumsum(sizes), jnp.arange(rows * top), side="right").astype(jnp.int32)
    listing = items.reshape(top, rows).T
    listing = listing[jax.random.permutation(jax.random.fold_in(own, 1), rows)]
    offset_by = jax.random.randint(jax.random.fold_in(own, 2), (rows, 1), 0, top)
    return jnp.take_along_axis(listing, (jnp.arange(top)[None, :] + offset_by) % top, axis=1)


def load_shares(number_of, total, bound, lean, full):
    loads = [(1 << 20) // math.isqrt(grade ** lean) + 1 for grade in range(1, number_of + 1)]
    largest = bound if full else min(bound, max(-(-total // number_of), total * loads[0] // sum(loads)))
    least = 1 if total - largest >= number_of - 1 else 0
    counts, rest = [largest] + [least] * (number_of - 1), total - largest - least * (number_of - 1)
    while rest > 0:
        free = [i for i in range(1, number_of) if counts[i] < largest] or [i for i in range(1, number_of) if counts[i] < bound]
        mass, left = sum([loads[i] for i in free]), rest
        for i in free:
            addition = min(bound - counts[i], max(1, left * loads[i] // mass), rest)
            counts[i] = counts[i] + addition
            rest = rest - addition
    return np.array(counts)


def gaussian(key, extent, scale, most, cuts=(), kind=jnp.bfloat16):
    values = jax.random.normal(key, extent, jnp.float32) * scale
    if len(cuts) > 0:
        values = levels(key, extent, cuts, -0.22, 0.18) * values
    return jnp.clip(values, min=-most, max=most).astype(kind)


def setup_inputs(seed: int = 0) -> dict:
    seeds = jax.random.split(jax.random.key(seed), 15)
    layer_input = gaussian(seeds[0], (MB, TOKENS, D), 1.0, 6.0, ((1, 8),))
    out_grad = gaussian(seeds[1], (MB, TOKENS, D), 1.0, 6.0, ((1, 8),))
    first_gain = jnp.clip(1.0 + 0.18 * jax.random.normal(seeds[2], (D,), jnp.float32), 0.099609375, 1.8984375).astype(jnp.bfloat16)
    query_weight = gaussian(seeds[3], (D, D), D ** -0.5, 0.21875, ((0, 8), (1, 4)))
    key_weight = gaussian(seeds[4], (D, D), D ** -0.5, 0.21875, ((0, 8), (1, 4)))
    value_weight = gaussian(seeds[5], (D, D), D ** -0.5, 0.21875, ((0, 8), (1, 4)))
    output_weight = gaussian(seeds[6], (D, D), (D // 16) ** -0.5, 0.875, ((0, 4), (1, 8)))
    position_bias = gaussian(seeds[7], (HEADS, NB), 1.0, 4.0, ((0, 4),))
    second_gain = jnp.clip(1.0 + 0.18 * jax.random.normal(seeds[8], (D,), jnp.float32), 0.099609375, 1.8984375).astype(jnp.bfloat16)
    router_weight = gaussian(seeds[9], (D, EXPERTS), (2 * D) ** -0.5, 0.15625, ((0, 8),))
    expert_in = gaussian(seeds[10], (EXPERTS, D, FF), D ** -0.5, 0.21875, ((0, 8), (2, 4)))
    expert_out = gaussian(seeds[11], (EXPERTS, FF, D), FF ** -0.5, 0.109375, ((0, 8), (1, 4)))
    seq_lengths = draw_seq_lengths(jax.random.fold_in(seeds[14], 71), 0)
    routes_keys = jax.random.split(jax.random.fold_in(seeds[13], 1), MB * TOKENS // TOK_MB)
    routes_turns = jax.random.permutation(jax.random.fold_in(seeds[13], 3), MB * TOKENS // TOK_MB)
    routes = jax.vmap(lambda own, number: routed_block(jax.random.fold_in(seeds[13], 2), own, number, TOK_MB, EXPERTS, 2, CAP, 1))(routes_keys, routes_turns).reshape((MB, TOKENS, 2))
    return {"layer_input": layer_input, "out_grad": out_grad, "first_gain": first_gain, "query_weight": query_weight, "key_weight": key_weight, "value_weight": value_weight, "output_weight": output_weight, "position_bias": position_bias, "second_gain": second_gain, "router_weight": router_weight, "expert_in": expert_in, "expert_out": expert_out, "seq_lengths": seq_lengths, "routes": routes}


@jax.custom_vjp
def low(v):
    return lax.optimization_barrier(v.astype(jnp.bfloat16)).astype(jnp.float32)

@jax.custom_vjp
def low_back(v):
    return v

def low_keep(v):
    return (low(v), None)

def low_pass(kept, grad):
    return (grad,)

def back_keep(v):
    return (v, None)

def back_low(kept, grad):
    return (low(grad),)
low.defvjp(low_keep, low_pass)
low_back.defvjp(back_keep, back_low)
bucket_edges = np.ceil(16.0 * 8.0 ** (np.arange(1, 16) / 16.0)).astype(np.int32)
highest = lax.Precision.HIGHEST

def bucket_of(distance):
    clipped = jnp.maximum(distance, 0)
    reached = lax.optimization_barrier(jnp.sum((clipped[..., None] >= jnp.asarray(bucket_edges, dtype=jnp.int32)).astype(jnp.int32), axis=-1, dtype=jnp.int32))
    return (jnp.minimum(clipped, 16) + reached).astype(jnp.int32)

def rms_norm(values, scale_gain):
    inverse = lax.rsqrt(lax.optimization_barrier(jnp.mean(values * values, axis=-1, keepdims=True)) + 1e-06)
    return values * inverse * scale_gain

def capacity_slots(route_rows, expert_count):
    named_hot = (route_rows[:, :, None] == jnp.arange(expert_count, dtype=jnp.int32)).astype(jnp.int32)
    per_token = lax.optimization_barrier(jnp.sum(named_hot, axis=1, dtype=jnp.int32))
    earlier = jnp.cumsum(per_token, axis=0, dtype=jnp.int32) - per_token
    return lax.optimization_barrier(jnp.sum(named_hot * earlier[:, None, :], axis=2, dtype=jnp.int32))

def matmul(left_side, right_side):
    return jnp.dot(left_side, right_side, precision=highest, preferred_element_type=jnp.float32)

def attend_sequence(query_seq, key_seq, value_seq, seq_length, bias_table):
    places = jnp.arange(SEQ, dtype=jnp.int32)
    bucket_grid = bucket_of(places[:, None] - places[None, :])
    scores = jnp.einsum('qhd,khd->hqk', query_seq, key_seq, precision=highest) * HEAD_DIM ** (-0.5)
    scores = low_back(scores + bias_table[:, bucket_grid])
    visible = (places[None, :] <= places[:, None]) & (places[None, :] < seq_length)
    scores = jnp.where(visible[None], scores, -1e+30)
    softmax_low = low(jax.nn.softmax(scores, axis=-1))
    mixed_rows = jnp.einsum('hqk,khd->qhd', softmax_low, value_seq, precision=highest)
    return low(low_back(mixed_rows))

def expert_forward(expert_rows, first_weight, second_weight):
    hidden = low_back(matmul(expert_rows, first_weight))
    active = low(jax.nn.gelu(hidden))
    return low(low_back(matmul(active, second_weight)))

def layer_forward(tokens, gain_one, query_weight, key_weight, value_weight, output_weight, bias_table, gain_two, router_weight, expert_in, expert_out, length_row, route_now, slot_pick, valid_rows):
    normed_one = low(rms_norm(tokens, gain_one))
    query_all = low(low_back(matmul(normed_one, query_weight))).reshape(NSEQ, SEQ, HEADS, HEAD_DIM)
    key_all = low(low_back(matmul(normed_one, key_weight))).reshape(NSEQ, SEQ, HEADS, HEAD_DIM)
    value_all = low(low_back(matmul(normed_one, value_weight))).reshape(NSEQ, SEQ, HEADS, HEAD_DIM)
    attend_step = jax.checkpoint(lambda item_set: attend_sequence(item_set[0], item_set[1], item_set[2], item_set[3], bias_table))
    mixed_rows = lax.map(attend_step, (query_all, key_all, value_all, length_row)).reshape(TOKENS, D)
    residual = tokens + low_back(matmul(mixed_rows, output_weight))
    normed_two = low(rms_norm(residual, gain_two))
    logits = low_back(matmul(normed_two, router_weight))
    picked = jnp.take_along_axis(logits, route_now, axis=1)
    gate_vals = jax.nn.softmax(picked, axis=-1)
    source = (jnp.arange(TOKENS, dtype=jnp.int32) // TOK_MB)[:, None] * jnp.ones((1, 2), jnp.int32)
    spread = jnp.broadcast_to(normed_two[:, None, :], (TOKENS, 2, D))
    buffer_rows = jnp.zeros((EXPERTS, N_DP, CAP, D), jnp.float32).at[route_now, source, slot_pick].add(spread)
    buffer_rows = low_back(buffer_rows).reshape(EXPERTS, N_DP * CAP, D)
    expert_step = jax.checkpoint(lambda item_set: expert_forward(item_set[0], item_set[1], item_set[2]))
    results = lax.map(expert_step, (buffer_rows, expert_in, expert_out)).reshape(EXPERTS, N_DP, CAP, D)
    picked_rows = results[route_now, source, slot_pick]
    mixture = lax.optimization_barrier(jnp.sum(gate_vals[:, :, None] * picked_rows, axis=1))
    return (residual + mixture) * valid_rows[:, None]

def reference(layer_input, out_grad, first_gain, query_weight, key_weight, value_weight, output_weight, position_bias, second_gain, router_weight, expert_in, expert_out, seq_lengths, routes):
    weights = tuple((item.astype(jnp.float32) for item in (first_gain, query_weight, key_weight, value_weight, output_weight, position_bias, second_gain, router_weight, expert_in, expert_out)))
    places = jnp.arange(SEQ, dtype=jnp.int32)
    outputs = []
    input_grads = []
    totals = None
    for micro_num in range(MB):
        length_row = seq_lengths[micro_num]
        route_now = routes[micro_num]
        valid_rows = (places[None, :] < length_row[:, None]).astype(jnp.float32).reshape(TOKENS)
        slot_pick = jax.vmap(lambda route_block: capacity_slots(route_block, EXPERTS))(route_now.reshape(N_DP, TOK_MB, 2)).reshape(TOKENS, 2)

        def forward(tokens, *params):
            return layer_forward(tokens, *params, length_row, route_now, slot_pick, valid_rows)
        result, pullback = jax.vjp(forward, layer_input[micro_num].astype(jnp.float32), *weights)
        gradients = pullback(out_grad[micro_num].astype(jnp.float32))
        outputs.append(result.astype(jnp.bfloat16))
        input_grads.append(gradients[0].astype(jnp.bfloat16))
        if totals is None:
            totals = gradients[1:]
        else:
            totals = tuple((before + after for before, after in zip(totals, gradients[1:])))
    return (jnp.stack(outputs), jnp.stack(input_grads), totals[0], totals[1], totals[2], totals[3], totals[4], totals[5], totals[6], totals[7], totals[8], totals[9])
```

```python
import functools

import jax
import jax.numpy as jnp
import numpy as np
from jax import lax
from jax.experimental import pallas as pl
from jax.experimental.pallas import tpu as pltpu
from jax.sharding import PartitionSpec as P

HEAD_DIM = 64
NB = 32
SEQ = 1024
TILE = 128
QROWS = 256
NEG = -1e30
GELU_C = 0.7978845608028654
GELU_A = 0.044715

BF = jnp.bfloat16
F32 = jnp.float32

bucket_edges = np.ceil(16.0 * 8.0 ** (np.arange(1, 16) / 16.0)).astype(np.int32)


def near_tables():
    rows = np.arange(TILE)[:, None]
    cols = np.arange(TILE)[None, :]
    hots = []
    for shift in (0, TILE):
        distance = rows - cols + shift
        clipped = np.maximum(distance, 0)
        reached = np.sum(clipped[..., None] >= bucket_edges, axis=-1)
        bucket = np.minimum(clipped, 16) + reached
        hots.append(bucket[..., None] == np.arange(NB))
    hot = np.stack(hots).reshape(2 * TILE * TILE, NB).T
    return hot


NEAR_HOT = near_tables()
assert bucket_edges[-1] <= TILE


def dot(a, b, dims=((1,), (0,))):
    return lax.dot_general(a, b, (dims, ((), ())), preferred_element_type=F32)


NT = ((1,), (1,))
TN = ((0,), (0,))


def score_tiles(block, half, q_half, key_ref, near_one, near_two, length):
    tiles = []
    for j in range(block + 1):
        s = dot(q_half, key_ref[j * QROWS : (j + 1) * QROWS, :], NT)
        if j == block:
            top = jnp.concatenate([s[:TILE, :TILE] + near_one, jnp.full((TILE, TILE), NEG, F32)], 1)
            low = jnp.concatenate([s[TILE:, :TILE] + near_two, s[TILE:, TILE:] + near_one], 1)
            s = jnp.concatenate([top, low], 0)
        elif j == block - 1:
            top = jnp.concatenate([s[:TILE, :TILE], s[:TILE, TILE:] + near_two], 1)
            s = jnp.concatenate([top, s[TILE:]], 0)
        if (j + 1) * QROWS > SEQ // 2:
            place = lax.broadcasted_iota(jnp.int32, (1, QROWS), 1) + j * QROWS
            s = s + jnp.where(place < length, 0.0, NEG)
        tiles.append(s)
    return tiles


def lane_half(rows):
    return lax.broadcasted_iota(jnp.int32, (rows, 2 * HEAD_DIM), 1) < HEAD_DIM


def attend_kernel(length_ref, query_ref, key_ref, value_ref, near_ref, out_ref, log_ref):
    length = length_ref[0]
    lanes = lane_half(QROWS)
    ones = jnp.ones((SEQ, TILE), BF)
    value_ext = jnp.concatenate([value_ref[...], ones], 1)
    for i in range(SEQ // QROWS):
        q_rows = query_ref[i * QROWS : (i + 1) * QROWS, :] * BF(0.125)
        outs, logs = [], []
        for h in range(2):
            keep = lanes if h == 0 else ~lanes
            q_half = jnp.where(keep, q_rows, BF(0))
            tiles = score_tiles(i, h, q_half, key_ref, near_ref[h, 0], near_ref[h, 1], length)
            top = tiles[0]
            for s in tiles[1:]:
                top = jnp.maximum(top, s)
            top = jnp.max(top, axis=1, keepdims=True)
            total = None
            for j, s in enumerate(tiles):
                p = jnp.exp(s - top).astype(BF)
                part = dot(p, value_ext[j * QROWS : (j + 1) * QROWS, :])
                total = part if total is None else total + part
            row_sum = total[:, TILE:]
            outs.append(total[:, :TILE] / row_sum)
            logs.append(top + jnp.log(row_sum))
        out_ref[i * QROWS : (i + 1) * QROWS, :] = jnp.where(lanes, outs[0], outs[1]).astype(BF)
        log_ref[i * QROWS : (i + 1) * QROWS, :] = jnp.where(lanes, logs[0], logs[1])


def attend(length, qkv, near):
    pairs = qkv.shape[1] // (3 * TILE)
    cols = pairs * TILE
    return pl.pallas_call(
        attend_kernel,
        grid=(pairs,),
        in_specs=[
            pl.BlockSpec(memory_space=pltpu.SMEM),
            pl.BlockSpec((SEQ, TILE), lambda p: (0, p)),
            pl.BlockSpec((SEQ, TILE), lambda p: (0, pairs + p)),
            pl.BlockSpec((SEQ, TILE), lambda p: (0, 2 * pairs + p)),
            pl.BlockSpec((2, 2, TILE, TILE), lambda p: (p, 0, 0, 0)),
        ],
        out_specs=[
            pl.BlockSpec((SEQ, TILE), lambda p: (0, p)),
            pl.BlockSpec((SEQ, TILE), lambda p: (0, p)),
        ],
        out_shape=[
            jax.ShapeDtypeStruct((SEQ, cols), BF),
            jax.ShapeDtypeStruct((SEQ, cols), F32),
        ],
        compiler_params=pltpu.CompilerParams(vmem_limit_bytes=40 * 2**20),
        cost_estimate=pl.CostEstimate(
            flops=pairs * 2 * 4 * 64 * SEQ * SEQ * 3, bytes_accessed=6 * SEQ * cols * 2, transcendentals=pairs * SEQ * SEQ
        ),
        name="attend",
    )(length, qkv, qkv, qkv, near)


def attend_back_kernel(
    length_ref, query_ref, key_ref, value_ref, near_ref, out_ref, log_ref, grad_ref,
    dq_ref, dk_ref, dv_ref, tile_ref, sum_ref, dk_acc, dv_acc,
):
    length = length_ref[0]
    lanes = lane_half(QROWS)
    lanes_all = lane_half(SEQ)
    ones = jnp.ones((SEQ, TILE), BF)
    key_ext = [
        jnp.concatenate([jnp.where(lanes_all, key_ref[...], BF(0)), ones], 1),
        jnp.concatenate([jnp.where(lanes_all, BF(0), key_ref[...]), ones], 1),
    ]
    near_sums = [[None, None], [None, None]]
    all_sums = [None, None]

    def put(a, b):
        return b if a is None else a + b

    for i in range(SEQ // QROWS):
        rows = slice(i * QROWS, (i + 1) * QROWS)
        q_rows = query_ref[rows, :] * BF(0.125)
        g_rows = grad_ref[rows, :]
        mass = g_rows.astype(F32) * out_ref[rows, :].astype(F32)
        dq = None
        for h in range(2):
            keep = lanes if h == 0 else ~lanes
            q_half = jnp.where(keep, q_rows, BF(0))
            g_half = jnp.where(keep, g_rows, BF(0))
            delta = jnp.sum(jnp.where(keep, mass, 0.0), axis=1, keepdims=True)
            log_col = log_ref[rows, h * HEAD_DIM : h * HEAD_DIM + 1]
            tiles = score_tiles(i, h, q_half, key_ref, near_ref[h, 0], near_ref[h, 1], length)
            for j, s in enumerate(tiles):
                keys = slice(j * QROWS, (j + 1) * QROWS)
                p = jnp.exp(s - log_col)
                dp = dot(g_half, value_ref[keys, :], NT)
                ds = (p * (dp - delta)).astype(BF)
                part = dot(ds, key_ext[h][keys, :])
                dq = put(dq, part[:, :TILE])
                all_sums[h] = put(all_sums[h], jnp.sum(part[:, TILE:].reshape(QROWS // 8, 8, TILE), axis=0))
                dk_part = dot(ds, q_half, TN)
                dv_part = dot(p.astype(BF), g_half, TN)
                if i == j and h == 0:
                    dk_acc[keys, :] = dk_part
                    dv_acc[keys, :] = dv_part
                else:
                    dk_acc[keys, :] += dk_part
                    dv_acc[keys, :] += dv_part
                if j == i:
                    wide = ds.astype(F32)
                    near_sums[h][0] = put(near_sums[h][0], wide[:TILE, :TILE] + wide[TILE:, TILE:])
                    near_sums[h][1] = put(near_sums[h][1], wide[TILE:, :TILE])
                elif j == i - 1:
                    near_sums[h][1] = put(near_sums[h][1], ds[:TILE, TILE:].astype(F32))
        dq_ref[rows, :] = (dq * 0.125).astype(BF)
    dk_ref[...] = dk_acc[...].astype(BF)
    dv_ref[...] = dv_acc[...].astype(BF)
    for h in range(2):
        tile_ref[h, 0] = near_sums[h][0]
        tile_ref[h, 1] = near_sums[h][1]
        sum_ref[h] = all_sums[h]


def attend_back(length, qkv, near, mixed, logs, grad):
    pairs = qkv.shape[1] // (3 * TILE)
    cols = pairs * TILE
    col = pl.BlockSpec((SEQ, TILE), lambda p: (0, p))
    return pl.pallas_call(
        attend_back_kernel,
        grid=(pairs,),
        in_specs=[
            pl.BlockSpec(memory_space=pltpu.SMEM),
            col,
            pl.BlockSpec((SEQ, TILE), lambda p: (0, pairs + p)),
            pl.BlockSpec((SEQ, TILE), lambda p: (0, 2 * pairs + p)),
            pl.BlockSpec((2, 2, TILE, TILE), lambda p: (p, 0, 0, 0)),
            col,
            col,
            col,
        ],
        out_specs=[
            col,
            col,
            col,
            pl.BlockSpec((2, 2, TILE, TILE), lambda p: (p, 0, 0, 0)),
            pl.BlockSpec((2, 8, TILE), lambda p: (p, 0, 0)),
        ],
        out_shape=[
            jax.ShapeDtypeStruct((SEQ, cols), BF),
            jax.ShapeDtypeStruct((SEQ, cols), BF),
            jax.ShapeDtypeStruct((SEQ, cols), BF),
            jax.ShapeDtypeStruct((2 * pairs, 2, TILE, TILE), F32),
            jax.ShapeDtypeStruct((2 * pairs, 8, TILE), F32),
        ],
        scratch_shapes=[pltpu.VMEM((SEQ, TILE), F32), pltpu.VMEM((SEQ, TILE), F32)],
        compiler_params=pltpu.CompilerParams(vmem_limit_bytes=40 * 2**20),
        cost_estimate=pl.CostEstimate(
            flops=pairs * 2 * 10 * 64 * SEQ * SEQ * 3, bytes_accessed=12 * SEQ * cols * 2, transcendentals=pairs * SEQ * SEQ
        ),
        name="attend_back",
    )(length, qkv, qkv, qkv, near, mixed, logs, grad)


def swap(value, axis, count, bit):
    return lax.ppermute(value, axis, [(i, i ^ bit) for i in range(count)])


def gather_rows(value, count, me):
    bit = count // 2
    stacked = value[None]
    while bit:
        other = swap(stacked, "dp", count, bit)
        mine_high = (me & bit) != 0
        pair = jnp.where(mine_high, jnp.stack([other, stacked], 1), jnp.stack([stacked, other], 1))
        stacked = pair.reshape((-1,) + value.shape)
        bit //= 2
    return stacked.reshape((-1,) + value.shape[1:])


def exchange(blocks, count):
    if count <= 8:
        return [blocks[0]] + [swap(blocks[p], "dp", count, p) for p in range(1, count)]
    moved = lax.all_to_all(jnp.stack(blocks), "dp", split_axis=0, concat_axis=0, tiled=True)
    return [moved[p] for p in range(count)]


def local(
    layer_input, out_grad, first_gain, query_weight, key_weight, value_weight, output_weight,
    position_bias, second_gain, router_weight, expert_in, expert_out, seq_lengths, routes,
):
    micro_count, tok_rows, width = layer_input.shape
    dp_count = lax.axis_size("dp")
    expert_count = router_weight.shape[1]
    shard = query_weight.shape[1]
    heads_here = position_bias.shape[0]
    assert lax.axis_size("tensor") == 4 and micro_count == 2 and expert_count == dp_count
    assert tok_rows == SEQ and seq_lengths.shape[1] == 1
    capacity = max(8, 8 * (10 * tok_rows // (32 * expert_count)))
    half = capacity // 2
    slots = expert_count * half
    me = lax.axis_index("dp")
    rank = lax.axis_index("tensor")
    micro = rank // 2
    core = rank % 2
    low_micro = micro == 0
    low_core = core == 0
    by_place = dp_count <= 8

    def swap_y(value):
        return swap(value, "tensor", 4, 2)

    def swap_core(value):
        return swap(value, "tensor", 4, 1)

    rows_here = query_weight.shape[0]
    small_cols = 128 * -(-(2 + expert_count) // 128)
    small = jnp.concatenate([first_gain[:, None], second_gain[:, None], router_weight], 1)
    small = jnp.pad(small, ((0, 0), (0, small_cols - 2 - expert_count)))
    packed = jnp.concatenate([query_weight, key_weight, value_weight, output_weight.T, small], 1)
    gathered = gather_rows(packed, dp_count, me)
    own_weights = gathered[:, : 4 * shard]
    gain_one = gathered[:, 4 * shard].astype(F32)
    gain_two = gathered[:, 4 * shard + 1].astype(F32)
    router = gathered[:, 4 * shard + 2 : 4 * shard + 2 + expert_count]
    other_weights = swap_y(own_weights)

    def in_order(mine, other, first):
        return jnp.where(first, mine, other), jnp.where(first, other, mine)

    weights_low, weights_high = in_order(own_weights, other_weights, low_micro)

    def kind(k):
        return jnp.concatenate(
            [weights_low[:, k * shard : (k + 1) * shard], weights_high[:, k * shard : (k + 1) * shard]], 1
        )

    qkv_weight = jnp.concatenate([kind(0), kind(1), kind(2)], 1)
    output_own = kind(3)
    output_other = swap_core(output_own)
    bias_low, bias_high = in_order(position_bias, swap_y(position_bias), low_micro)
    bias = jnp.concatenate([bias_low, bias_high], 0)
    head_total = bias.shape[0]
    hot_const = jnp.asarray(NEAR_HOT, dtype=BF)
    near = dot(bias, hot_const) - bias[:, NB - 1 :].astype(F32)
    near = near.reshape(head_total, 2, TILE, TILE)
    places = jnp.arange(TILE, dtype=jnp.int32)
    causal = jnp.stack([places[None, :] <= places[:, None], jnp.ones((TILE, TILE), bool)])
    near = jnp.where(causal[None], near, NEG)

    def gather_hidden(mine, axis):
        pair = jnp.concatenate(in_order(mine, swap_y(mine), low_micro), axis)
        size = mine.shape[axis]
        pieces = in_order(pair, swap_core(pair), low_core)
        cut = [lax.slice_in_dim(p, y * size, (y + 1) * size, axis=axis) for y in range(2) for p in pieces]
        return jnp.concatenate(cut, axis)

    first_mat = gather_hidden(expert_in[0], 1)
    second_mat = gather_hidden(expert_out[0], 0)

    tokens_low = lax.dynamic_index_in_dim(layer_input, micro, 0, keepdims=False)
    tokens = tokens_low.astype(F32)
    grad_low = lax.dynamic_index_in_dim(out_grad, micro, 0, keepdims=False)
    length = lax.dynamic_index_in_dim(seq_lengths, micro, 0, keepdims=False)
    route = lax.dynamic_index_in_dim(routes, micro, 0, keepdims=False)
    valid = (jnp.arange(SEQ, dtype=jnp.int32) < length[0])[:, None]
    grad_low = jnp.where(valid, grad_low, BF(0))
    grad_out = grad_low.astype(F32)

    expert_ids = jnp.arange(expert_count, dtype=jnp.int32)
    named = (route[:, :, None] == expert_ids).astype(jnp.int32)
    per_token = jnp.sum(named, axis=1, dtype=jnp.int32)
    earlier = jnp.cumsum(per_token, axis=0, dtype=jnp.int32) - per_token
    slot = jnp.sum(named * earlier[:, None, :], axis=2, dtype=jnp.int32)
    place = (route ^ me) if by_place else route
    slot_half = slot // half
    spot = place * half + slot % half
    code_send = jnp.where(slot_half == core, spot, -1)
    code_all = spot + jnp.where(slot_half == core, 0, slots)
    slot_ids = jnp.arange(slots, dtype=jnp.int32)
    send_hot = (
        (slot_ids[:, None] == code_send[None, :, 0]) | (slot_ids[:, None] == code_send[None, :, 1])
    ).astype(BF)
    all_ids = jnp.arange(2 * slots, dtype=jnp.int32)
    take_first = code_all[:, :1] == all_ids[None, :]
    take_second = code_all[:, 1:] == all_ids[None, :]
    take_hot = (take_first | take_second).astype(BF)

    def dispatch(rows):
        moved = exchange([rows[p * half : (p + 1) * half] for p in range(expert_count)], dp_count)
        return jnp.concatenate(moved, 0)

    grads_sent = dot(send_hot, grad_low).astype(BF)
    grads_here = dispatch(grads_sent)
    hit_first = slot_ids[:, None] == code_send[None, :, 0]
    hit_second = slot_ids[:, None] == code_send[None, :, 1]
    partner = jnp.sum(
        jnp.where(hit_first, route[None, :, 1], 0) + jnp.where(hit_second, route[None, :, 0], 0), axis=1, dtype=jnp.int32
    )
    partner_here = dispatch(partner)

    inverse_one = lax.rsqrt(jnp.mean(tokens * tokens, axis=-1, keepdims=True) + 1e-06)
    normed_one = (tokens * inverse_one * gain_one).astype(BF)
    qkv = dot(normed_one, qkv_weight).astype(BF)
    mixed, logs = attend(length, qkv, near)
    mixed_other = swap_core(mixed)
    residual = tokens + dot(mixed, output_own, NT) + dot(mixed_other, output_other, NT)
    inverse_two = lax.rsqrt(jnp.mean(residual * residual, axis=-1, keepdims=True) + 1e-06)
    normed_two = (residual * inverse_two * gain_two).astype(BF)
    logits = dot(normed_two, router)
    route_hot = (route[:, :, None] == expert_ids).astype(F32)
    picked = jnp.sum(route_hot * logits[:, None, :], axis=-1)
    gates = jax.nn.softmax(picked, axis=-1)

    rows_here_moe = dispatch(dot(send_hot, normed_two).astype(BF))
    owner_logits = dot(rows_here_moe, router)
    other_logit = jnp.sum(jnp.where(partner_here[:, None] == expert_ids[None, :], owner_logits, 0.0), axis=1)
    own_logit = jnp.sum(jnp.where(expert_ids[None, :] == me, owner_logits, 0.0), axis=1)
    gate_here = jax.nn.softmax(jnp.stack([own_logit, other_logit], 1), axis=-1)[:, :1]

    hidden = dot(rows_here_moe, first_mat)
    inner = GELU_C * (hidden + GELU_A * hidden * hidden * hidden)
    bent = jnp.tanh(inner)
    active_wide = 0.5 * hidden * (1.0 + bent)
    slope = 0.5 * (1.0 + bent) + 0.5 * hidden * (1.0 - bent * bent) * GELU_C * (1.0 + 3.0 * GELU_A * hidden * hidden)
    active = active_wide.astype(BF)
    plain_grad = dot(grads_here, second_mat, NT)
    gate_grad_here = jnp.sum(active.astype(F32) * plain_grad, axis=1)
    hidden_grad = (gate_here * plain_grad * slope).astype(BF)
    rows_grad = dot(hidden_grad, first_mat, NT).astype(BF)
    back_own = dispatch(rows_grad)
    gate_back = dispatch(gate_grad_here)
    results = (gate_here * dot(active, second_mat)).astype(BF)
    results_own = dispatch(results)
    result_grad = (gate_here * grads_here.astype(F32)).astype(BF)
    expert_in_part = dot(rows_here_moe, hidden_grad, TN)
    expert_out_part = dot(active, result_grad, TN)

    def scatter_hidden(part, axis):
        size = part.shape[axis] // 4
        cut = [lax.slice_in_dim(part, t * size, (t + 1) * size, axis=axis) for t in range(4)]
        even = jnp.concatenate([cut[0], cut[2]], axis)
        odd = jnp.concatenate([cut[1], cut[3]], axis)
        mine = jnp.where(low_core, even, odd)
        sent = jnp.where(low_core, odd, even).astype(BF)
        mine = mine + swap_core(sent).astype(F32)
        first = lax.slice_in_dim(mine, 0, size, axis=axis)
        second = lax.slice_in_dim(mine, size, 2 * size, axis=axis)
        keep = jnp.where(low_micro, first, second)
        sent = jnp.where(low_micro, second, first).astype(BF)
        return keep + swap_y(sent).astype(F32)

    expert_in_grad = scatter_hidden(expert_in_part, 1)
    expert_out_grad = scatter_hidden(expert_out_part, 0)

    back_other = swap_core(back_own)
    back_rows = jnp.concatenate([back_own, back_other], 0)
    gate_rows = jnp.concatenate([gate_back, swap_core(gate_back)], 0)
    difference = jnp.sum(
        jnp.where(take_first, gate_rows[None, :], 0.0) - jnp.where(take_second, gate_rows[None, :], 0.0), axis=1
    )
    picked_grad = gates[:, 0] * gates[:, 1] * difference
    signs = route_hot[:, 0] - route_hot[:, 1]
    logit_grad = (signs * picked_grad[:, None]).astype(BF)
    normed_two_grad = dot(take_hot, back_rows) + dot(logit_grad, router, NT)
    router_part = dot(normed_two, logit_grad, TN)
    scaled = normed_two_grad * gain_two
    gain_two_part = jnp.sum(normed_two_grad * residual * inverse_two, axis=0)
    residual_grad = (
        grad_out
        + inverse_two * scaled
        - residual * (inverse_two**3) * jnp.mean(scaled * residual, axis=-1, keepdims=True)
    )
    branch_grad = residual_grad.astype(BF)
    output_part = dot(branch_grad, mixed, TN)
    mixed_grad = dot(branch_grad, output_own).astype(BF)

    results_all = jnp.concatenate([results_own, swap_core(results_own)], 0)
    mixture = dot(take_hot, results_all)
    layer_rows = jnp.where(valid, residual + mixture, 0.0).astype(BF)

    def both_micros(rows):
        across = swap_y(rows)
        halves = jnp.stack([rows, across])
        other = swap_core(halves)
        low, high = in_order(halves, other, low_core)
        full = jnp.concatenate([low, high], 1)
        return jnp.where(low_micro, full, full[::-1])

    tok_half = SEQ // 2

    def core_half(rows):
        return lax.dynamic_slice_in_dim(rows, core * tok_half, tok_half, 0)

    layer_output = both_micros(core_half(layer_rows))

    dq, dk, dv, tiles, sums = attend_back(length, qkv, near, mixed, logs, mixed_grad)
    cols = dq.shape[1]
    query_part = dot(normed_one, dq, TN)
    key_part = dot(normed_one, dk, TN)
    value_part = dot(normed_one, dv, TN)
    normed_part = (
        dot(dq, qkv_weight[:, :cols], NT)
        + dot(dk, qkv_weight[:, cols : 2 * cols], NT)
        + dot(dv, qkv_weight[:, 2 * cols :], NT)
    )
    part_low, part_high = normed_part[:tok_half], normed_part[tok_half:]
    kept, sent = in_order(part_low, part_high, low_core)
    normed_one_grad = kept + swap_core(sent)
    tokens_half = core_half(tokens)
    inverse_half = core_half(inverse_one)
    scaled_one = normed_one_grad * gain_one
    gain_one_part = jnp.sum(normed_one_grad * tokens_half * inverse_half, axis=0)
    input_half = (
        core_half(residual_grad)
        + inverse_half * scaled_one
        - tokens_half * (inverse_half**3) * jnp.mean(scaled_one * tokens_half, axis=-1, keepdims=True)
    ).astype(BF)
    input_grad = both_micros(input_half)

    tiles_flat = tiles.reshape(head_total, 2 * TILE * TILE)
    tiles_high = tiles_flat.astype(BF)
    tiles_rest = (tiles_flat - tiles_high.astype(F32)).astype(BF)
    table = dot(tiles_high, hot_const, NT) + dot(tiles_rest, hot_const, NT)
    far = jnp.sum(sums[:, :, 0], axis=1) - jnp.sum(table[:, : NB - 1], axis=1)
    table = jnp.concatenate([table[:, : NB - 1], far[:, None]], 1)

    def shares(part, y):
        return part[:, y * shard : (y + 1) * shard]

    parts = (query_part, key_part, value_part, output_part)
    large = [jnp.concatenate([shares(p, y) for p in parts], 1) for y in range(2)]
    kept, sent = in_order(large[0], large[1], low_micro)
    large_sum = (kept + swap_y(sent.astype(BF)).astype(F32)).astype(BF)
    table_kept, table_sent = in_order(table[:heads_here], table[heads_here:], low_micro)
    gain_one_both = gain_one_part + swap_core(gain_one_part)
    extras = jnp.concatenate([gain_one_both[:, None], gain_two_part[:, None], router_part], 1)
    extras = extras + swap_y(extras)
    table_sum = table_kept + swap_y(table_sent)
    table_cols = heads_here * NB // rows_here
    table_block = jnp.tile(table_sum.reshape(rows_here, table_cols), (dp_count, 1))
    extras = jnp.concatenate([extras, table_block], 1)
    extras_high = extras.astype(BF)
    extras_rest = (extras - extras_high.astype(F32)).astype(BF)
    extra_cols = extras.shape[1]
    filled = 128 * -(-2 * extra_cols // 128) - 2 * extra_cols
    grads = jnp.concatenate([large_sum, extras_high, extras_rest, jnp.zeros((width, filled), BF)], 1)
    blocks = grads.reshape(dp_count, rows_here, grads.shape[1])
    if by_place:
        sent_blocks = [lax.dynamic_index_in_dim(blocks, p ^ me, 0, keepdims=False) for p in range(dp_count)]
    else:
        sent_blocks = [blocks[p] for p in range(dp_count)]
    arrived = exchange(sent_blocks, dp_count)
    total = arrived[0].astype(F32)
    for block in arrived[1:]:
        total = total + block.astype(F32)
    base = 4 * shard
    small_total = total[:, base : base + extra_cols] + total[:, base + extra_cols : base + 2 * extra_cols]
    return (
        layer_output,
        input_grad,
        small_total[:, 0],
        total[:, :shard],
        total[:, shard : 2 * shard],
        total[:, 2 * shard : 3 * shard],
        total[:, 3 * shard : 4 * shard].T,
        small_total[:, 2 + expert_count :].reshape(heads_here, NB),
        small_total[:, 1],
        small_total[:, 2 : 2 + expert_count],
        expert_in_grad[None],
        expert_out_grad[None],
    )


def solution(mesh):
    return jax.shard_map(
        local,
        mesh=mesh,
        in_specs=(
            P(None, "dp", None),
            P(None, "dp", None),
            P("dp"),
            P("dp", "tensor"),
            P("dp", "tensor"),
            P("dp", "tensor"),
            P("tensor", "dp"),
            P("tensor", None),
            P("dp"),
            P("dp", None),
            P("dp", None, "tensor"),
            P("dp", "tensor", None),
            P(None, "dp"),
            P(None, "dp", None),
        ),
        out_specs=(
            P(None, "dp", None),
            P(None, "dp", None),
            P("dp"),
            P("dp", "tensor"),
            P("dp", "tensor"),
            P("dp", "tensor"),
            P("tensor", "dp"),
            P("tensor", None),
            P("dp"),
            P("dp", None),
            P("dp", None, "tensor"),
            P("dp", "tensor", None),
        ),
        check_vma=False,
    )
```

```python
import functools

import jax
import jax.numpy as jnp
import numpy as np
from jax import lax
from jax.experimental import pallas as pl
from jax.experimental.pallas import tpu as pltpu
from jax.sharding import PartitionSpec as P

HEAD_DIM = 64
NB = 32
SEQ = 1024
TILE = 128
QROWS = 256
NEG = -1e30
GELU_C = 0.7978845608028654
GELU_A = 0.044715

BF = jnp.bfloat16
F32 = jnp.float32

bucket_edges = np.ceil(16.0 * 8.0 ** (np.arange(1, 16) / 16.0)).astype(np.int32)


def near_tables():
    rows = np.arange(TILE)[:, None]
    cols = np.arange(TILE)[None, :]
    hots = []
    for shift in (0, TILE):
        distance = rows - cols + shift
        clipped = np.maximum(distance, 0)
        reached = np.sum(clipped[..., None] >= bucket_edges, axis=-1)
        bucket = np.minimum(clipped, 16) + reached
        hots.append(bucket[..., None] == np.arange(NB))
    hot = np.stack(hots).reshape(2 * TILE * TILE, NB).T
    return hot


NEAR_HOT = near_tables()
assert bucket_edges[-1] <= TILE


def dot(a, b, dims=((1,), (0,))):
    return lax.dot_general(a, b, (dims, ((), ())), preferred_element_type=F32)


NT = ((1,), (1,))
TN = ((0,), (0,))


def score_tiles(block, half, q_half, key_ref, near_one, near_two, length):
    tiles = []
    for j in range(block + 1):
        s = dot(q_half, key_ref[j * QROWS : (j + 1) * QROWS, :], NT)
        if j == block:
            top = jnp.concatenate([s[:TILE, :TILE] + near_one, jnp.full((TILE, TILE), NEG, F32)], 1)
            low = jnp.concatenate([s[TILE:, :TILE] + near_two, s[TILE:, TILE:] + near_one], 1)
            s = jnp.concatenate([top, low], 0)
        elif j == block - 1:
            top = jnp.concatenate([s[:TILE, :TILE], s[:TILE, TILE:] + near_two], 1)
            s = jnp.concatenate([top, s[TILE:]], 0)
        if (j + 1) * QROWS > SEQ // 2:
            place = lax.broadcasted_iota(jnp.int32, (1, QROWS), 1) + j * QROWS
            s = s + jnp.where(place < length, 0.0, NEG)
        tiles.append(s)
    return tiles


def lane_half(rows):
    return lax.broadcasted_iota(jnp.int32, (rows, 2 * HEAD_DIM), 1) < HEAD_DIM


def attend_kernel(length_ref, query_ref, key_ref, value_ref, near_ref, out_ref, log_ref):
    length = length_ref[0]
    lanes = lane_half(QROWS)
    ones = jnp.ones((SEQ, TILE), BF)
    value_ext = jnp.concatenate([value_ref[...], ones], 1)
    for i in range(SEQ // QROWS):
        q_rows = query_ref[i * QROWS : (i + 1) * QROWS, :] * BF(0.125)
        outs, logs = [], []
        for h in range(2):
            keep = lanes if h == 0 else ~lanes
            q_half = jnp.where(keep, q_rows, BF(0))
            tiles = score_tiles(i, h, q_half, key_ref, near_ref[h, 0], near_ref[h, 1], length)
            top = tiles[0]
            for s in tiles[1:]:
                top = jnp.maximum(top, s)
            top = jnp.max(top, axis=1, keepdims=True)
            total = None
            for j, s in enumerate(tiles):
                p = jnp.exp(s - top).astype(BF)
                part = dot(p, value_ext[j * QROWS : (j + 1) * QROWS, :])
                total = part if total is None else total + part
            row_sum = total[:, TILE:]
            outs.append(total[:, :TILE] / row_sum)
            logs.append(top + jnp.log(row_sum))
        out_ref[i * QROWS : (i + 1) * QROWS, :] = jnp.where(lanes, outs[0], outs[1]).astype(BF)
        log_ref[i * QROWS : (i + 1) * QROWS, :] = jnp.where(lanes, logs[0], logs[1])


def attend(length, qkv, near):
    pairs = qkv.shape[1] // (3 * TILE)
    cols = pairs * TILE
    return pl.pallas_call(
        attend_kernel,
        grid=(pairs,),
        in_specs=[
            pl.BlockSpec(memory_space=pltpu.SMEM),
            pl.BlockSpec((SEQ, TILE), lambda p: (0, p)),
            pl.BlockSpec((SEQ, TILE), lambda p: (0, pairs + p)),
            pl.BlockSpec((SEQ, TILE), lambda p: (0, 2 * pairs + p)),
            pl.BlockSpec((2, 2, TILE, TILE), lambda p: (p, 0, 0, 0)),
        ],
        out_specs=[
            pl.BlockSpec((SEQ, TILE), lambda p: (0, p)),
            pl.BlockSpec((SEQ, TILE), lambda p: (0, p)),
        ],
        out_shape=[
            jax.ShapeDtypeStruct((SEQ, cols), BF),
            jax.ShapeDtypeStruct((SEQ, cols), F32),
        ],
        compiler_params=pltpu.CompilerParams(vmem_limit_bytes=40 * 2**20),
        cost_estimate=pl.CostEstimate(
            flops=pairs * 2 * 4 * 64 * SEQ * SEQ * 3, bytes_accessed=6 * SEQ * cols * 2, transcendentals=pairs * SEQ * SEQ
        ),
        name="attend",
    )(length, qkv, qkv, qkv, near)


def attend_back_kernel(
    length_ref, query_ref, key_ref, value_ref, near_ref, out_ref, log_ref, grad_ref,
    dq_ref, dk_ref, dv_ref, tile_ref, sum_ref, dk_acc, dv_acc,
):
    length = length_ref[0]
    lanes = lane_half(QROWS)
    lanes_all = lane_half(SEQ)
    ones = jnp.ones((SEQ, TILE), BF)
    key_ext = [
        jnp.concatenate([jnp.where(lanes_all, key_ref[...], BF(0)), ones], 1),
        jnp.concatenate([jnp.where(lanes_all, BF(0), key_ref[...]), ones], 1),
    ]
    near_sums = [[None, None], [None, None]]
    all_sums = [None, None]

    def put(a, b):
        return b if a is None else a + b

    for i in range(SEQ // QROWS):
        rows = slice(i * QROWS, (i + 1) * QROWS)
        q_rows = query_ref[rows, :] * BF(0.125)
        g_rows = grad_ref[rows, :]
        mass = g_rows.astype(F32) * out_ref[rows, :].astype(F32)
        dq = None
        for h in range(2):
            keep = lanes if h == 0 else ~lanes
            q_half = jnp.where(keep, q_rows, BF(0))
            g_half = jnp.where(keep, g_rows, BF(0))
            delta = jnp.sum(jnp.where(keep, mass, 0.0), axis=1, keepdims=True)
            log_col = log_ref[rows, h * HEAD_DIM : h * HEAD_DIM + 1]
            tiles = score_tiles(i, h, q_half, key_ref, near_ref[h, 0], near_ref[h, 1], length)
            for j, s in enumerate(tiles):
                keys = slice(j * QROWS, (j + 1) * QROWS)
                p = jnp.exp(s - log_col)
                dp = dot(g_half, value_ref[keys, :], NT)
                ds = (p * (dp - delta)).astype(BF)
                part = dot(ds, key_ext[h][keys, :])
                dq = put(dq, part[:, :TILE])
                all_sums[h] = put(all_sums[h], jnp.sum(part[:, TILE:].reshape(QROWS // 8, 8, TILE), axis=0))
                dk_part = dot(ds, q_half, TN)
                dv_part = dot(p.astype(BF), g_half, TN)
                if i == j and h == 0:
                    dk_acc[keys, :] = dk_part
                    dv_acc[keys, :] = dv_part
                else:
                    dk_acc[keys, :] += dk_part
                    dv_acc[keys, :] += dv_part
                if j == i:
                    wide = ds.astype(F32)
                    near_sums[h][0] = put(near_sums[h][0], wide[:TILE, :TILE] + wide[TILE:, TILE:])
                    near_sums[h][1] = put(near_sums[h][1], wide[TILE:, :TILE])
                elif j == i - 1:
                    near_sums[h][1] = put(near_sums[h][1], ds[:TILE, TILE:].astype(F32))
        dq_ref[rows, :] = (dq * 0.125).astype(BF)
    dk_ref[...] = dk_acc[...].astype(BF)
    dv_ref[...] = dv_acc[...].astype(BF)
    for h in range(2):
        tile_ref[h, 0] = near_sums[h][0]
        tile_ref[h, 1] = near_sums[h][1]
        sum_ref[h] = all_sums[h]


def attend_back(length, qkv, near, mixed, logs, grad):
    pairs = qkv.shape[1] // (3 * TILE)
    cols = pairs * TILE
    col = pl.BlockSpec((SEQ, TILE), lambda p: (0, p))
    return pl.pallas_call(
        attend_back_kernel,
        grid=(pairs,),
        in_specs=[
            pl.BlockSpec(memory_space=pltpu.SMEM),
            col,
            pl.BlockSpec((SEQ, TILE), lambda p: (0, pairs + p)),
            pl.BlockSpec((SEQ, TILE), lambda p: (0, 2 * pairs + p)),
            pl.BlockSpec((2, 2, TILE, TILE), lambda p: (p, 0, 0, 0)),
            col,
            col,
            col,
        ],
        out_specs=[
            col,
            col,
            col,
            pl.BlockSpec((2, 2, TILE, TILE), lambda p: (p, 0, 0, 0)),
            pl.BlockSpec((2, 8, TILE), lambda p: (p, 0, 0)),
        ],
        out_shape=[
            jax.ShapeDtypeStruct((SEQ, cols), BF),
            jax.ShapeDtypeStruct((SEQ, cols), BF),
            jax.ShapeDtypeStruct((SEQ, cols), BF),
            jax.ShapeDtypeStruct((2 * pairs, 2, TILE, TILE), F32),
            jax.ShapeDtypeStruct((2 * pairs, 8, TILE), F32),
        ],
        scratch_shapes=[pltpu.VMEM((SEQ, TILE), F32), pltpu.VMEM((SEQ, TILE), F32)],
        compiler_params=pltpu.CompilerParams(vmem_limit_bytes=40 * 2**20),
        cost_estimate=pl.CostEstimate(
            flops=pairs * 2 * 10 * 64 * SEQ * SEQ * 3, bytes_accessed=12 * SEQ * cols * 2, transcendentals=pairs * SEQ * SEQ
        ),
        name="attend_back",
    )(length, qkv, qkv, qkv, near, mixed, logs, grad)


def pair_gate(logits, own, other):
    lanes = lax.broadcasted_iota(jnp.int32, logits.shape, 1)
    gap = jnp.sum(
        jnp.where(lanes == own, logits, 0.0) - jnp.where(lanes == other, logits, 0.0), axis=1, keepdims=True
    )
    small = jnp.exp(-jnp.abs(gap))
    return jnp.where(gap >= 0.0, 1.0, small) / (1.0 + small)


def expert_kernel(
    me_ref, partner_ref, rows_ref, grads_ref, router_ref, a0, a1, a2, a3, b0, b1, b2, b3,
    back_ref, active_ref, slope_ref, gated_ref, scalar_ref,
):
    rows = rows_ref[...]
    grads = grads_ref[...]
    gate = pair_gate(dot(rows, router_ref[...]), me_ref[0], partner_ref[...])
    gated_ref[...] = (gate * grads.astype(F32)).astype(BF)
    gate_grad = None
    back = None
    step = 256
    for r, (first, second) in enumerate(((a0, b0), (a1, b1), (a2, b2), (a3, b3))):
        width = first.shape[1]
        for c in range(0, width, step):
            x = dot(rows, first[:, c : c + step])
            plain = dot(grads, second[c : c + step, :], NT)
            square = x * x
            bent = jnp.tanh(x * (GELU_C + (GELU_C * GELU_A) * square))
            rise = 0.5 + 0.5 * bent
            active = x * rise
            slope = rise + active * (1.0 - bent) * (GELU_C + (3.0 * GELU_C * GELU_A) * square)
            low = active.astype(BF)
            place = slice(r * width + c, r * width + c + step)
            active_ref[:, place] = low
            slope_ref[:, place] = (gate * plain * slope).astype(BF)
            mass = low.astype(F32) * plain
            mass = sum(mass[:, k : k + TILE] for k in range(TILE, step, TILE)) + mass[:, :TILE]
            gate_grad = mass if gate_grad is None else gate_grad + mass
        part = dot(slope_ref[:, r * width : (r + 1) * width], first[...], NT)
        back = part if back is None else back + part
    back_ref[...] = back.astype(BF)
    lanes = lax.broadcasted_iota(jnp.int32, (rows.shape[0], TILE), 1)
    scalar_ref[...] = jnp.where(lanes == 0, jnp.sum(gate_grad, axis=1, keepdims=True), gate)


def row_block(total):
    return total // 4


def expert_rows_pass(me, partner, rows, grads, router, firsts, seconds):
    total, width = rows.shape
    block = row_block(total)
    hidden = sum(f.shape[1] for f in firsts)
    here = lambda cols: pl.BlockSpec((block, cols), lambda i: (i, 0))
    whole = lambda arr: pl.BlockSpec(arr.shape, lambda i: (0, 0))
    return pl.pallas_call(
        expert_kernel,
        grid=(total // block,),
        in_specs=[pl.BlockSpec(memory_space=pltpu.SMEM), here(1), here(width), here(width), whole(router)]
        + [whole(w) for w in firsts]
        + [whole(w) for w in seconds],
        out_specs=[here(width), here(hidden), here(hidden), here(width), here(TILE)],
        out_shape=[
            jax.ShapeDtypeStruct((total, width), BF),
            jax.ShapeDtypeStruct((total, hidden), BF),
            jax.ShapeDtypeStruct((total, hidden), BF),
            jax.ShapeDtypeStruct((total, width), BF),
            jax.ShapeDtypeStruct((total, TILE), F32),
        ],
        compiler_params=pltpu.CompilerParams(vmem_limit_bytes=56 * 2**20),
        cost_estimate=pl.CostEstimate(
            flops=6 * total * width * hidden, bytes_accessed=4 * total * hidden + 4 * width * hidden, transcendentals=total * hidden
        ),
        name="expert_rows",
    )(me, partner, rows, grads, router, *firsts, *seconds)


def result_kernel(active_ref, scalar_ref, b0, b1, b2, b3, out_ref):
    width = b0.shape[0]
    total = None
    for r, second in enumerate((b0, b1, b2, b3)):
        part = dot(active_ref[:, r * width : (r + 1) * width], second[...])
        total = part if total is None else total + part
    out_ref[...] = (total * scalar_ref[:, 1:2]).astype(BF)


def expert_results(active, scalars, seconds):
    total, hidden = active.shape
    width = seconds[0].shape[1]
    block = row_block(total)
    here = lambda cols: pl.BlockSpec((block, cols), lambda i: (i, 0))
    return pl.pallas_call(
        result_kernel,
        grid=(total // block,),
        in_specs=[here(hidden), here(TILE)] + [pl.BlockSpec(w.shape, lambda i: (0, 0)) for w in seconds],
        out_specs=here(width),
        out_shape=jax.ShapeDtypeStruct((total, width), BF),
        compiler_params=pltpu.CompilerParams(vmem_limit_bytes=56 * 2**20),
        cost_estimate=pl.CostEstimate(
            flops=2 * total * width * hidden, bytes_accessed=2 * total * hidden + 2 * width * hidden, transcendentals=0
        ),
        name="expert_results",
    )(active, scalars, *seconds)


def weight_kernel(rows_ref, slope_ref, active_ref, gated_ref, out_ref):
    out_ref[0, 0] = dot(rows_ref[...], slope_ref[...], TN).astype(out_ref.dtype)
    out_ref[0, 1] = dot(active_ref[...], gated_ref[...], TN).astype(out_ref.dtype)


def expert_weight_grads(rows, slopes, active, gated, first_quarter, kind):
    total, width = rows.shape
    hidden = slopes.shape[1] // 4
    whole = pl.BlockSpec((total, width), lambda i: (0, 0))
    part = pl.BlockSpec((total, hidden), lambda i: (0, first_quarter + i))
    return pl.pallas_call(
        weight_kernel,
        grid=(2,),
        in_specs=[whole, part, part, whole],
        out_specs=pl.BlockSpec((1, 2, width, hidden), lambda i: (i, 0, 0, 0)),
        out_shape=jax.ShapeDtypeStruct((2, 2, width, hidden), kind),
        compiler_params=pltpu.CompilerParams(vmem_limit_bytes=56 * 2**20),
        cost_estimate=pl.CostEstimate(
            flops=8 * total * width * hidden, bytes_accessed=8 * total * hidden + 16 * width * hidden, transcendentals=0
        ),
        name="expert_weight_grads",
    )(rows, slopes, active, gated)


def place_kernel(place_ref, a_ref, b_ref, c_ref, d_ref, out_ref):
    for n, piece in enumerate((a_ref, b_ref, c_ref, d_ref)):

        @pl.when(pl.program_id(0) == n)
        def _(piece=piece):
            out_ref[0] = piece[...]


def place_pieces(places, pieces):
    shape = pieces[0].shape
    whole = pl.BlockSpec(shape, lambda i, place_ref: (0, 0))
    return pl.pallas_call(
        place_kernel,
        grid_spec=pltpu.PrefetchScalarGridSpec(
            num_scalar_prefetch=1,
            grid=(4,),
            in_specs=[whole] * 4,
            out_specs=pl.BlockSpec((1,) + shape, lambda i, place_ref: (place_ref[i], 0, 0)),
        ),
        out_shape=jax.ShapeDtypeStruct((4,) + shape, pieces[0].dtype),
        compiler_params=pltpu.CompilerParams(vmem_limit_bytes=32 * 2**20),
        name="place_pieces",
    )(places, *pieces)


def swap(value, axis, count, bit):
    return lax.ppermute(value, axis, [(i, i ^ bit) for i in range(count)])


def all_to_all(value):
    return lax.all_to_all(value, "dp", split_axis=0, concat_axis=0, tiled=True)


def together(*values):
    return lax.optimization_barrier(values)


def local(
    layer_input, out_grad, first_gain, query_weight, key_weight, value_weight, output_weight,
    position_bias, second_gain, router_weight, expert_in, expert_out, seq_lengths, routes,
):
    micro_count, tok_rows, width = layer_input.shape
    dp_count = lax.axis_size("dp")
    expert_count = router_weight.shape[1]
    shard = query_weight.shape[1]
    heads_here = position_bias.shape[0]
    assert lax.axis_size("tensor") == 4 and micro_count == 2 and expert_count == dp_count
    assert tok_rows == SEQ and seq_lengths.shape[1] == 1
    capacity = max(8, 8 * (10 * tok_rows // (32 * expert_count)))
    half = capacity // 2
    stride = 8 * (half // 8 + 1)
    slots = expert_count * stride
    me = lax.axis_index("dp")
    rank = lax.axis_index("tensor")
    micro = rank // 2
    core = rank % 2

    def swap_y(value):
        return swap(value, "tensor", 4, 2)

    def swap_core(value):
        return swap(value, "tensor", 4, 1)

    rows_here = query_weight.shape[0]
    small_cols = 128 * -(-(2 + expert_count) // 128)
    small = jnp.concatenate([first_gain[:, None], second_gain[:, None], router_weight], 1)
    small = jnp.pad(small, ((0, 0), (0, small_cols - 2 - expert_count)))
    packed = jnp.concatenate([value_weight, output_weight.T, query_weight, key_weight, small], 1)
    two = 2 * shard

    def doubled(stacked, bit, axis=0):
        other = swap(stacked, "dp", dp_count, bit)
        high = (me & bit) != 0
        pair = jnp.where(high, jnp.stack([other, stacked], axis + 1), jnp.stack([stacked, other], axis + 1))
        return pair.reshape(stacked.shape[:axis] + (-1,) + stacked.shape[axis + 1 :])

    stacked = packed[None]
    bit = dp_count // 2
    while bit > 1:
        stacked = doubled(stacked, bit)
        bit //= 2
    first_own = expert_in[0]
    second_own = expert_out[0]
    first_y = swap_y(first_own)
    stacked, first_y = together(stacked, first_y)
    part_b = stacked[:, :, :two]
    part_a = doubled(stacked[:, :, two:], 1)
    pair_b = jnp.stack([part_b, swap_y(part_b)])
    query_key_own = part_a[:, :, :two]
    query_key_other = swap_y(query_key_own).reshape(width, two)
    query_key_own = query_key_own.reshape(width, two)
    pair_b = doubled(pair_b, 1, 1).reshape(2, width, two)
    small_all = part_a[:, :, two:].reshape(width, small_cols)
    gain_one = small_all[:, 0].astype(F32)
    gain_two = small_all[:, 1].astype(F32)
    router = small_all[:, 2 : 2 + expert_count]
    router_wide = jnp.pad(router, ((0, 0), (0, TILE - expert_count)))
    qkv_weight = jnp.concatenate(
        [
            query_key_own[:, :shard], query_key_other[:, :shard],
            query_key_own[:, shard:], query_key_other[:, shard:],
            pair_b[0, :, :shard], pair_b[1, :, :shard],
        ],
        1,
    )
    output_own = jnp.concatenate([pair_b[0, :, shard:], pair_b[1, :, shard:]], 1)
    output_other = swap_core(output_own)
    bias = jnp.concatenate([position_bias, swap_y(position_bias)], 0)
    head_total = bias.shape[0]
    hot_const = jnp.asarray(NEAR_HOT, dtype=BF)
    near = dot(bias, hot_const) - bias[:, NB - 1 :].astype(F32)
    near = near.reshape(head_total, 2, TILE, TILE)
    places = jnp.arange(TILE, dtype=jnp.int32)
    causal = jnp.stack([places[None, :] <= places[:, None], jnp.ones((TILE, TILE), bool)])
    near = jnp.where(causal[None], near, NEG)

    second_late, _ = together(second_own, pair_b)
    second_y = swap_y(second_late)

    tokens_low = lax.dynamic_index_in_dim(layer_input, micro, 0, keepdims=False)
    tokens = tokens_low.astype(F32)
    grad_low = lax.dynamic_index_in_dim(out_grad, micro, 0, keepdims=False)
    length = lax.dynamic_index_in_dim(seq_lengths, micro, 0, keepdims=False)
    route = lax.dynamic_index_in_dim(routes, micro, 0, keepdims=False)
    valid = (jnp.arange(SEQ, dtype=jnp.int32) < length[0])[:, None]
    grad_low = jnp.where(valid, grad_low, BF(0))
    grad_out = grad_low.astype(F32)

    expert_ids = jnp.arange(expert_count, dtype=jnp.int32)
    named = (route[:, :, None] == expert_ids).astype(jnp.int32)
    per_token = jnp.sum(named, axis=1, dtype=jnp.int32)
    earlier = jnp.cumsum(per_token, axis=0, dtype=jnp.int32) - per_token
    slot = jnp.sum(named * earlier[:, None, :], axis=2, dtype=jnp.int32)
    slot_half = slot // half
    spot = route * stride + slot % half
    code_send = jnp.where(slot_half == core, spot, -1)
    code_all = spot + jnp.where(slot_half == core, 0, slots)
    slot_ids = jnp.arange(slots, dtype=jnp.int32)
    hit_first = slot_ids[:, None] == code_send[None, :, 0]
    hit_second = slot_ids[:, None] == code_send[None, :, 1]
    send_hot = (hit_first | hit_second).astype(BF)
    all_ids = jnp.arange(2 * slots, dtype=jnp.int32)
    take_first = code_all[:, :1] == all_ids[None, :]
    take_second = code_all[:, 1:] == all_ids[None, :]
    take_hot = (take_first | take_second).astype(BF)

    def blocks_of(rows):
        return rows.reshape((expert_count, stride) + rows.shape[1:])

    partner = jnp.sum(
        jnp.where(hit_first, route[None, :, 1], 0) + jnp.where(hit_second, route[None, :, 0], 0), axis=1, dtype=jnp.int32
    )
    grads_sent = blocks_of(dot(send_hot, grad_low).astype(BF))
    partner_row = jnp.pad(blocks_of(partner)[:, :half].astype(BF), ((0, 0), (0, width - half)))
    grads_sent = grads_sent.at[:, half].set(partner_row)
    grads_sent, _ = together(grads_sent, part_a)
    grads_here = all_to_all(grads_sent)
    partner_here = jnp.pad(grads_here[:, half, :half], ((0, 0), (0, stride - half))).astype(jnp.int32).reshape(slots, 1)
    grads_here = grads_here.reshape(slots, width)

    inverse_one = lax.rsqrt(jnp.mean(tokens * tokens, axis=-1, keepdims=True) + 1e-06)
    normed_one = (tokens * inverse_one * gain_one).astype(BF)
    qkv = dot(normed_one, qkv_weight).astype(BF)
    mixed, logs = attend(length, qkv, near)
    mixed, second_y = together(mixed, second_y)
    mixed_other = swap_core(mixed)
    firsts = (first_own, first_y, swap_core(first_own), swap_core(first_y))
    seconds = (second_own, second_y, swap_core(second_own), swap_core(second_y))
    residual = tokens + dot(mixed, output_own, NT) + dot(mixed_other, output_other, NT)
    inverse_two = lax.rsqrt(jnp.mean(residual * residual, axis=-1, keepdims=True) + 1e-06)
    normed_two = (residual * inverse_two * gain_two).astype(BF)

    rows_moe = all_to_all(blocks_of(dot(send_hot, normed_two).astype(BF))).reshape(slots, width)
    logits = dot(normed_two, router)
    route_hot = (route[:, :, None] == expert_ids).astype(F32)
    picked = jnp.sum(route_hot * logits[:, None, :], axis=-1)
    gates = jax.nn.softmax(picked, axis=-1)
    back, active, slopes, gated, scalars = expert_rows_pass(
        me.reshape(1).astype(jnp.int32), partner_here, rows_moe, grads_here, router_wide, firsts, seconds
    )
    gate_grad = blocks_of(scalars[:, 0])[:, :half]
    pieces = []
    for _ in range(3):
        piece = gate_grad.astype(BF)
        pieces.append(piece)
        gate_grad = gate_grad - piece.astype(F32)
    gate_row = jnp.pad(jnp.concatenate(pieces, 1), ((0, 0), (0, width - 3 * half)))
    back_own = all_to_all(blocks_of(back).at[:, half].set(gate_row))
    results = expert_results(active, scalars, seconds)
    grads_cross = expert_weight_grads(rows_moe, slopes, active, gated, 2, BF)
    grads_kept = expert_weight_grads(rows_moe, slopes, active, gated, 0, F32)

    grads_in = swap_core(grads_cross).astype(F32)
    y_first = swap_y((grads_kept[1, 0] + grads_in[1, 0]).astype(BF))
    back_own, results, y_first = together(back_own, results, y_first)
    y_second, _ = together((grads_kept[1, 1] + grads_in[1, 1]).astype(BF), y_first)
    y_second = swap_y(y_second)
    expert_in_grad = grads_kept[0, 0] + grads_in[0, 0] + y_first.astype(F32)
    back_other = swap_core(back_own)
    results_own = all_to_all(blocks_of(results))

    back_rows = jnp.concatenate([back_own, back_other], 0)
    gate_rows = back_rows[:, half, : 3 * half].reshape(2 * expert_count, 3, half).astype(F32)
    gate_rows = jnp.pad(jnp.sum(gate_rows, axis=1), ((0, 0), (0, stride - half))).reshape(2 * slots)
    back_rows = back_rows.reshape(2 * slots, width)
    difference = jnp.sum(
        jnp.where(take_first, gate_rows[None, :], 0.0) - jnp.where(take_second, gate_rows[None, :], 0.0), axis=1
    )
    picked_grad = gates[:, 0] * gates[:, 1] * difference
    signs = route_hot[:, 0] - route_hot[:, 1]
    logit_grad = (signs * picked_grad[:, None]).astype(BF)
    normed_two_grad = dot(take_hot, back_rows) + dot(logit_grad, router, NT)
    router_part = dot(normed_two, logit_grad, TN)
    scaled = normed_two_grad * gain_two
    gain_two_part = jnp.sum(normed_two_grad * residual * inverse_two, axis=0)
    residual_grad = (
        grad_out
        + inverse_two * scaled
        - residual * (inverse_two**3) * jnp.mean(scaled * residual, axis=-1, keepdims=True)
    )
    branch_grad = residual_grad.astype(BF)
    mixed_grad = dot(branch_grad, output_own).astype(BF)
    output_part = dot(branch_grad, mixed, TN)
    output_far = swap_y(output_part[:, shard:].astype(BF))

    dq, dk, dv, tiles, sums = attend_back(length, qkv, near, mixed, logs, mixed_grad)
    dq, y_second, output_far = together(dq, y_second, output_far)
    expert_out_grad = grads_kept[0, 1] + grads_in[0, 1] + y_second.astype(F32)
    cols = dq.shape[1]

    tok_half = SEQ // 2
    corner = micro * 2 + core
    corners = jnp.stack([corner, corner ^ 1, corner ^ 2, corner ^ 3]).astype(jnp.int32)

    def core_half(rows, flip=0):
        return lax.dynamic_slice_in_dim(rows, (core ^ flip) * tok_half, tok_half, 0)

    def placed(own, beside):
        across = swap_y(own)
        far = swap_core(across)
        return place_pieces(corners, (own, beside, across, far)).reshape(2, SEQ, width)

    grads_qkv = [dot(normed_one, d, TN) for d in (dq, dk, dv)]
    far_part = jnp.concatenate([g[:, shard:] for g in grads_qkv], 1).astype(BF)
    results_own, far_part = together(results_own, far_part)
    far_part = swap_y(far_part)
    results_all = jnp.concatenate([results_own, swap_core(results_own)], 0).reshape(2 * slots, width)
    mixture = dot(take_hot, results_all)
    layer_rows = jnp.where(valid, residual + mixture, 0.0).astype(BF)
    layer_output = placed(core_half(layer_rows), core_half(layer_rows, 1))

    large = jnp.concatenate([g[:, :shard] for g in grads_qkv], 1) + far_part.astype(F32)
    output_sum = output_part[:, :shard] + output_far.astype(F32)

    normed_part = (
        dot(dq, qkv_weight[:, :cols], NT)
        + dot(dk, qkv_weight[:, cols : 2 * cols], NT)
        + dot(dv, qkv_weight[:, 2 * cols :], NT)
    )
    normed_one_grad = core_half(normed_part) + swap_core(core_half(normed_part, 1))
    tokens_half = core_half(tokens)
    inverse_half = core_half(inverse_one)
    scaled_one = normed_one_grad * gain_one
    gain_one_part = jnp.sum(normed_one_grad * tokens_half * inverse_half, axis=0)
    input_half = (
        core_half(residual_grad)
        + inverse_half * scaled_one
        - tokens_half * (inverse_half**3) * jnp.mean(scaled_one * tokens_half, axis=-1, keepdims=True)
    ).astype(BF)
    input_grad = placed(input_half, swap_core(input_half))

    tiles_flat = tiles.reshape(head_total, 2 * TILE * TILE)
    tiles_high = tiles_flat.astype(BF)
    tiles_rest = (tiles_flat - tiles_high.astype(F32)).astype(BF)
    table = dot(tiles_high, hot_const, NT) + dot(tiles_rest, hot_const, NT)
    far_sum = jnp.sum(sums[:, :, 0], axis=1) - jnp.sum(table[:, : NB - 1], axis=1)
    table = jnp.concatenate([table[:, : NB - 1], far_sum[:, None]], 1)
    table_cols = heads_here * NB // rows_here
    table_own = table[:heads_here].reshape(rows_here, table_cols)
    table_far = table[heads_here:].reshape(rows_here, table_cols)

    gain_one_both = gain_one_part + swap_core(gain_one_part)
    rest = jnp.concatenate([gain_one_both[:, None], gain_two_part[:, None], router_part], 1)
    spread = lambda t: jnp.tile(t, (dp_count, 1))
    extras = jnp.concatenate([rest, spread(table_own)], 1)
    extras = extras + swap_y(jnp.concatenate([rest, spread(table_far)], 1))
    extras_high = extras.astype(BF)
    extras_rest = (extras - extras_high.astype(F32)).astype(BF)
    extra_cols = extras.shape[1]
    filled = 128 * -(-2 * extra_cols // 128) - 2 * extra_cols
    grads = jnp.concatenate(
        [large.astype(BF), output_sum.astype(BF), extras_high, extras_rest, jnp.zeros((width, filled), BF)], 1
    )
    arrived = all_to_all(grads.reshape(dp_count, rows_here, grads.shape[1]))
    total = jnp.sum(arrived.astype(F32), axis=0)
    base = 4 * shard
    small_total = total[:, base : base + extra_cols] + total[:, base + extra_cols : base + 2 * extra_cols]
    return (
        layer_output,
        input_grad,
        small_total[:, 0],
        total[:, :shard],
        total[:, shard : 2 * shard],
        total[:, 2 * shard : 3 * shard],
        total[:, 3 * shard : 4 * shard].T,
        small_total[:, 2 + expert_count :].reshape(heads_here, NB),
        small_total[:, 1],
        small_total[:, 2 : 2 + expert_count],
        expert_in_grad[None],
        expert_out_grad[None],
    )


def solution(mesh):
    return jax.shard_map(
        local,
        mesh=mesh,
        in_specs=(
            P(None, "dp", None),
            P(None, "dp", None),
            P("dp"),
            P("dp", "tensor"),
            P("dp", "tensor"),
            P("dp", "tensor"),
            P("tensor", "dp"),
            P("tensor", None),
            P("dp"),
            P("dp", None),
            P("dp", None, "tensor"),
            P("dp", "tensor", None),
            P(None, "dp"),
            P(None, "dp", None),
        ),
        out_specs=(
            P(None, "dp", None),
            P(None, "dp", None),
            P("dp"),
            P("dp", "tensor"),
            P("dp", "tensor"),
            P("dp", "tensor"),
            P("tensor", "dp"),
            P("tensor", None),
            P("dp"),
            P("dp", None),
            P("dp", None, "tensor"),
            P("dp", "tensor", None),
        ),
        check_vma=False,
    )
```

```python
import functools

import jax
import jax.numpy as jnp
import numpy as np
from jax import lax
from jax.experimental import pallas as pl
from jax.experimental.pallas import tpu as pltpu
from jax.sharding import PartitionSpec as P

HEAD_DIM = 64
NB = 32
SEQ = 1024
TILE = 128
QROWS = 256
NEG = -1e30
GELU_C = 0.7978845608028654
GELU_A = 0.044715

BF = jnp.bfloat16
F32 = jnp.float32

bucket_edges = np.ceil(16.0 * 8.0 ** (np.arange(1, 16) / 16.0)).astype(np.int32)


def near_tables():
    rows = np.arange(TILE)[:, None]
    cols = np.arange(TILE)[None, :]
    hots = []
    for shift in (0, TILE):
        distance = rows - cols + shift
        clipped = np.maximum(distance, 0)
        reached = np.sum(clipped[..., None] >= bucket_edges, axis=-1)
        bucket = np.minimum(clipped, 16) + reached
        hots.append(bucket[..., None] == np.arange(NB))
    hot = np.stack(hots).reshape(2 * TILE * TILE, NB).T
    return hot


NEAR_HOT = near_tables()
assert bucket_edges[-1] <= TILE


def dot(a, b, dims=((1,), (0,))):
    return lax.dot_general(a, b, (dims, ((), ())), preferred_element_type=F32)


NT = ((1,), (1,))
TN = ((0,), (0,))


SMALL_COST = pl.CostEstimate(flops=1_000_000, bytes_accessed=1_000_000, transcendentals=0)


def score_tiles(block, half, q_half, key_ref, near_one, near_two, length):
    tiles = []
    for j in range(block + 1):
        s = dot(q_half, key_ref[j * QROWS : (j + 1) * QROWS, :], NT)
        if j == block:
            top = jnp.concatenate([s[:TILE, :TILE] + near_one, jnp.full((TILE, TILE), NEG, F32)], 1)
            low = jnp.concatenate([s[TILE:, :TILE] + near_two, s[TILE:, TILE:] + near_one], 1)
            s = jnp.concatenate([top, low], 0)
        elif j == block - 1:
            top = jnp.concatenate([s[:TILE, :TILE], s[:TILE, TILE:] + near_two], 1)
            s = jnp.concatenate([top, s[TILE:]], 0)
        if (j + 1) * QROWS > SEQ // 2:
            place = lax.broadcasted_iota(jnp.int32, (1, QROWS), 1) + j * QROWS
            s = s + jnp.where(place < length, 0.0, NEG)
        tiles.append(s)
    return tiles


def lane_half(rows):
    return lax.broadcasted_iota(jnp.int32, (rows, 2 * HEAD_DIM), 1) < HEAD_DIM


def attend_kernel(length_ref, query_ref, key_ref, value_ref, near_ref, out_ref, log_ref):
    length = length_ref[0]
    lanes = lane_half(QROWS)
    ones = jnp.ones((SEQ, TILE), BF)
    value_ext = jnp.concatenate([value_ref[...], ones], 1)
    for i in range(SEQ // QROWS):
        q_rows = query_ref[i * QROWS : (i + 1) * QROWS, :] * BF(0.125)
        outs, logs = [], []
        for h in range(2):
            keep = lanes if h == 0 else ~lanes
            q_half = jnp.where(keep, q_rows, BF(0))
            tiles = score_tiles(i, h, q_half, key_ref, near_ref[h, 0], near_ref[h, 1], length)
            top = tiles[0]
            for s in tiles[1:]:
                top = jnp.maximum(top, s)
            top = jnp.max(top, axis=1, keepdims=True)
            total = None
            for j, s in enumerate(tiles):
                p = jnp.exp(s - top).astype(BF)
                part = dot(p, value_ext[j * QROWS : (j + 1) * QROWS, :])
                total = part if total is None else total + part
            row_sum = total[:, TILE:]
            outs.append(total[:, :TILE] / row_sum)
            logs.append(top + jnp.log(row_sum))
        out_ref[i * QROWS : (i + 1) * QROWS, :] = jnp.where(lanes, outs[0], outs[1]).astype(BF)
        log_ref[i * QROWS : (i + 1) * QROWS, :] = jnp.where(lanes, logs[0], logs[1])


def attend(length, qkv, near):
    pairs = qkv.shape[1] // (3 * TILE)
    cols = pairs * TILE
    return pl.pallas_call(
        attend_kernel,
        grid=(pairs,),
        in_specs=[
            pl.BlockSpec(memory_space=pltpu.SMEM),
            pl.BlockSpec((SEQ, TILE), lambda p: (0, p)),
            pl.BlockSpec((SEQ, TILE), lambda p: (0, pairs + p)),
            pl.BlockSpec((SEQ, TILE), lambda p: (0, 2 * pairs + p)),
            pl.BlockSpec((2, 2, TILE, TILE), lambda p: (p, 0, 0, 0)),
        ],
        out_specs=[
            pl.BlockSpec((SEQ, TILE), lambda p: (0, p)),
            pl.BlockSpec((SEQ, TILE), lambda p: (0, p)),
        ],
        out_shape=[
            jax.ShapeDtypeStruct((SEQ, cols), BF),
            jax.ShapeDtypeStruct((SEQ, cols), F32),
        ],
        compiler_params=pltpu.CompilerParams(vmem_limit_bytes=40 * 2**20),
        cost_estimate=SMALL_COST,
        name="attend",
    )(length, qkv, qkv, qkv, near)


def attend_back_kernel(
    length_ref, query_ref, key_ref, value_ref, near_ref, out_ref, log_ref, grad_ref,
    dq_ref, dk_ref, dv_ref, tile_ref, sum_ref, dk_acc, dv_acc,
):
    length = length_ref[0]
    lanes = lane_half(QROWS)
    lanes_all = lane_half(SEQ)
    ones = jnp.ones((SEQ, TILE), BF)
    key_ext = [
        jnp.concatenate([jnp.where(lanes_all, key_ref[...], BF(0)), ones], 1),
        jnp.concatenate([jnp.where(lanes_all, BF(0), key_ref[...]), ones], 1),
    ]
    near_sums = [[None, None], [None, None]]
    all_sums = [None, None]

    for i in range(SEQ // QROWS):
        rows = slice(i * QROWS, (i + 1) * QROWS)
        q_rows = query_ref[rows, :] * BF(0.125)
        g_rows = grad_ref[rows, :]
        mass = g_rows.astype(F32) * out_ref[rows, :].astype(F32)
        dq = None
        for h in range(2):
            keep = lanes if h == 0 else ~lanes
            q_half = jnp.where(keep, q_rows, BF(0))
            g_half = jnp.where(keep, g_rows, BF(0))
            delta = jnp.sum(jnp.where(keep, mass, 0.0), axis=1, keepdims=True)
            log_col = log_ref[rows, h * HEAD_DIM : h * HEAD_DIM + 1]
            tiles = score_tiles(i, h, q_half, key_ref, near_ref[h, 0], near_ref[h, 1], length)
            for j, s in enumerate(tiles):
                keys = slice(j * QROWS, (j + 1) * QROWS)
                p = jnp.exp(s - log_col)
                dp = dot(g_half, value_ref[keys, :], NT)
                ds = (p * (dp - delta)).astype(BF)
                part = dot(ds, key_ext[h][keys, :])
                dq = put(dq, part[:, :TILE])
                all_sums[h] = put(all_sums[h], jnp.sum(part[:, TILE:].reshape(QROWS // 8, 8, TILE), axis=0))
                dk_part = dot(ds, q_half, TN)
                dv_part = dot(p.astype(BF), g_half, TN)
                if i == j and h == 0:
                    dk_acc[keys, :] = dk_part
                    dv_acc[keys, :] = dv_part
                else:
                    dk_acc[keys, :] += dk_part
                    dv_acc[keys, :] += dv_part
                if j == i:
                    wide = ds.astype(F32)
                    near_sums[h][0] = put(near_sums[h][0], wide[:TILE, :TILE] + wide[TILE:, TILE:])
                    near_sums[h][1] = put(near_sums[h][1], wide[TILE:, :TILE])
                elif j == i - 1:
                    near_sums[h][1] = put(near_sums[h][1], ds[:TILE, TILE:].astype(F32))
        dq_ref[rows, :] = (dq * 0.125).astype(BF)
    dk_ref[...] = dk_acc[...].astype(BF)
    dv_ref[...] = dv_acc[...].astype(BF)
    for h in range(2):
        tile_ref[h, 0] = near_sums[h][0]
        tile_ref[h, 1] = near_sums[h][1]
        sum_ref[h] = all_sums[h]


def attend_back(length, qkv, near, mixed, logs, grad, first, count):
    pairs = qkv.shape[1] // (3 * TILE)
    cols = count * TILE
    col = pl.BlockSpec((SEQ, TILE), lambda p: (0, first + p))
    out = pl.BlockSpec((SEQ, TILE), lambda p: (0, p))
    return pl.pallas_call(
        attend_back_kernel,
        grid=(count,),
        in_specs=[
            pl.BlockSpec(memory_space=pltpu.SMEM),
            col,
            pl.BlockSpec((SEQ, TILE), lambda p: (0, pairs + first + p)),
            pl.BlockSpec((SEQ, TILE), lambda p: (0, 2 * pairs + first + p)),
            pl.BlockSpec((2, 2, TILE, TILE), lambda p: (first + p, 0, 0, 0)),
            col,
            col,
            col,
        ],
        out_specs=[
            out,
            out,
            out,
            pl.BlockSpec((2, 2, TILE, TILE), lambda p: (p, 0, 0, 0)),
            pl.BlockSpec((2, 8, TILE), lambda p: (p, 0, 0)),
        ],
        out_shape=[
            jax.ShapeDtypeStruct((SEQ, cols), BF),
            jax.ShapeDtypeStruct((SEQ, cols), BF),
            jax.ShapeDtypeStruct((SEQ, cols), BF),
            jax.ShapeDtypeStruct((2 * count, 2, TILE, TILE), F32),
            jax.ShapeDtypeStruct((2 * count, 8, TILE), F32),
        ],
        scratch_shapes=[pltpu.VMEM((SEQ, TILE), F32), pltpu.VMEM((SEQ, TILE), F32)],
        compiler_params=pltpu.CompilerParams(vmem_limit_bytes=40 * 2**20),
        cost_estimate=SMALL_COST,
        name="attend_back",
    )(length, qkv, qkv, qkv, near, mixed, logs, grad)


def low_lanes(shape):
    return lax.broadcasted_iota(jnp.int32, shape, 1) < HEAD_DIM


def turned(tile):
    return pltpu.roll(tile, HEAD_DIM, 1)


def pack_kernel(q_ref, k_ref, v_ref, o_ref, one_ref, two_ref, router_ref, out_ref):
    shard = q_ref.shape[1]
    rows = q_ref.shape[0]
    source = lax.broadcasted_iota(jnp.int32, (shard, 6 * TILE), 0)
    target = lax.broadcasted_iota(jnp.int32, (shard, 6 * TILE), 1)

    def moved(pair_base, last_base):
        want = jnp.where(source < TILE, source + pair_base, source - TILE + last_base)
        return jnp.where(target == want, 1.0, 0.0).astype(BF)

    total = dot(v_ref[...], moved(0, 2 * TILE)) + dot(o_ref[...], moved(TILE, 2 * TILE + HEAD_DIM), TN)
    total = total + dot(q_ref[...], moved(3 * TILE, 5 * TILE)) + dot(k_ref[...], moved(4 * TILE, 5 * TILE + HEAD_DIM))
    out_ref[:, : 6 * TILE] = total.astype(BF)
    experts = router_ref.shape[1]
    own_row = lax.broadcasted_iota(jnp.int32, (rows, rows), 0) == lax.broadcasted_iota(jnp.int32, (rows, rows), 1)

    def column(ref):
        return jnp.sum(jnp.where(own_row, ref[...].astype(F32), 0.0), axis=1, keepdims=True)

    lanes = lax.broadcasted_iota(jnp.int32, (experts, TILE), 1)
    spread = jnp.where(lanes == lax.broadcasted_iota(jnp.int32, (experts, TILE), 0), 1.0, 0.0).astype(BF)
    place = lax.broadcasted_iota(jnp.int32, (rows, TILE), 1)
    small = dot(router_ref[...], spread)
    small = jnp.where(place == experts, column(one_ref), jnp.where(place == experts + 1, column(two_ref), small))
    out_ref[:, 6 * TILE :] = small.astype(BF)


def pack_weights(query, key, value, output, one, two, router):
    rows = query.shape[0]
    return pl.pallas_call(
        pack_kernel,
        out_shape=jax.ShapeDtypeStruct((rows, 7 * TILE), BF),
        cost_estimate=SMALL_COST,
        name="pack_weights",
    )(query, key, value, output, one[None], two[None], router)


def qkv_kernel(micro_ref, tokens_ref, gain_ref, a_own, a_far, b_own, b_far, qkv_ref, normed_ref, weight_ref, output_ref):
    width = tokens_ref.shape[2]

    @pl.when(pl.program_id(0) == 0)
    def _():
        low = low_lanes((width, TILE))

        def tiles(own, far, pair, low_half):
            at = slice(pair * TILE, (pair + 1) * TILE)
            one, two = own[:, 2 * TILE :].astype(F32), far[:, 2 * TILE :].astype(F32)
            last = jnp.where(low, one, turned(two)) if low_half else jnp.where(low, turned(one), two)
            return own[:, at], far[:, at], last.astype(BF)

        for n, (own, far, pair, low_half) in enumerate(
            ((a_own, a_far, 0, True), (a_own, a_far, 1, False), (b_own, b_far, 0, True))
        ):
            for t, tile in enumerate(tiles(own[...], far[...], pair, low_half)):
                at = 3 * n + t
                weight_ref[:, at * TILE : (at + 1) * TILE] = tile
        for t, tile in enumerate(tiles(b_own[...], b_far[...], 1, False)):
            output_ref[:, t * TILE : (t + 1) * TILE] = tile

    x = tokens_ref[0].astype(F32)
    inverse = lax.rsqrt(jnp.mean(x * x, axis=-1, keepdims=True) + 1e-06)
    normed = (x * inverse * gain_ref[...]).astype(BF)
    normed_ref[...] = normed
    qkv_ref[...] = dot(normed, weight_ref[...]).astype(BF)


def norm_and_project(micro, layer_input, gain, a_own, a_far, b_own, b_far):
    width = layer_input.shape[2]
    block = 256
    cols = 3 * TILE
    whole = lambda rows, n: pl.BlockSpec((rows, n), lambda i, m: (0, 0))
    here = lambda n: pl.BlockSpec((block, n), lambda i, m: (i, 0))
    return pl.pallas_call(
        qkv_kernel,
        grid_spec=pltpu.PrefetchScalarGridSpec(
            num_scalar_prefetch=1,
            grid=(SEQ // block,),
            in_specs=[pl.BlockSpec((1, block, width), lambda i, m: (m[0], i, 0)), whole(1, width)] + [whole(width, cols)] * 4,
            out_specs=[here(3 * cols), here(width), whole(width, 3 * cols), whole(width, cols)],
        ),
        out_shape=[
            jax.ShapeDtypeStruct((SEQ, 3 * cols), BF),
            jax.ShapeDtypeStruct((SEQ, width), BF),
            jax.ShapeDtypeStruct((width, 3 * cols), BF),
            jax.ShapeDtypeStruct((width, cols), BF),
        ],
        compiler_params=pltpu.CompilerParams(vmem_limit_bytes=40 * 2**20),
        cost_estimate=SMALL_COST,
        name="norm_and_project",
    )(micro, layer_input, gain, a_own, a_far, b_own, b_far)


def middle_kernel(micro_ref, tokens_ref, mixed_ref, other_ref, own_ref, far_ref, gain_ref, residual_ref, normed_ref):
    total = tokens_ref[0].astype(F32) + dot(mixed_ref[...], own_ref[...], NT) + dot(other_ref[...], far_ref[...], NT)
    residual_ref[...] = total
    inverse = lax.rsqrt(jnp.mean(total * total, axis=-1, keepdims=True) + 1e-06)
    normed_ref[...] = (total * inverse * gain_ref[...]).astype(BF)


def residual_and_norm(micro, layer_input, mixed, other, output_own, output_far, gain):
    width = layer_input.shape[2]
    block = 256
    cols = mixed.shape[1]
    whole = lambda rows, n: pl.BlockSpec((rows, n), lambda i, m: (0, 0))
    here = lambda n: pl.BlockSpec((block, n), lambda i, m: (i, 0))
    return pl.pallas_call(
        middle_kernel,
        grid_spec=pltpu.PrefetchScalarGridSpec(
            num_scalar_prefetch=1,
            grid=(SEQ // block,),
            in_specs=[
                pl.BlockSpec((1, block, width), lambda i, m: (m[0], i, 0)),
                here(cols), here(cols), whole(width, cols), whole(width, cols), whole(1, width),
            ],
            out_specs=[here(width), here(width)],
        ),
        out_shape=[jax.ShapeDtypeStruct((SEQ, width), F32), jax.ShapeDtypeStruct((SEQ, width), BF)],
        compiler_params=pltpu.CompilerParams(vmem_limit_bytes=40 * 2**20),
        cost_estimate=SMALL_COST,
        name="residual_and_norm",
    )(micro, layer_input, mixed, other, output_own, output_far, gain)


def picked_rows(code, segments, start=0):
    total = None
    for ref in segments:
        length = ref.shape[0]
        ids = lax.broadcasted_iota(jnp.int32, (1, length), 1) + start
        hot = jnp.where((code[:, :1] == ids) | (code[:, 1:2] == ids), 1.0, 0.0).astype(BF)
        part = dot(hot, ref[...])
        total = part if total is None else total + part
        start += length
    return total


def put(a, b):
    return b if a is None else a + b


def column_sum(product):
    ones = jnp.ones((product.shape[0], TILE), BF)
    high = product.astype(BF)
    rest = (product - high.astype(F32)).astype(BF)
    return dot(high, ones, TN) + dot(rest, ones, TN)


def combine_kernel(experts, half, micro_ref, core_ref, length_ref, *refs):
    (code_ref, route_ref, slot_ref, product_ref, grad_ref, residual_ref, mixed_ref, gain_ref, router_ref, output_ref,
     gates_own, gates_far) = refs[:12]
    segments = refs[12:-6]
    total_ref, mixed_grad_ref, extra_ref, far_ref, own_ref, acc_ref = refs[-6:]
    block = code_ref.shape[0]
    step = pl.program_id(0)
    columns = lax.broadcasted_iota(jnp.int32, (1, half), 1)
    lanes = lax.broadcasted_iota(jnp.int32, (1, experts), 1)
    values = []
    for k in range(2):
        slot = slot_ref[:, k : k + 1]
        hot = jnp.where(columns == lax.rem(slot, half), 1.0, 0.0).astype(BF)
        mine = slot // half == core_ref[0]
        found = []
        for table in (gates_own, gates_far):
            found.append(sum(dot(hot, table[:, n * half : (n + 1) * half], NT) for n in range(3)))
        value = jnp.where(mine, found[0], found[1])
        values.append(jnp.sum(jnp.where(lanes == route_ref[:, k : k + 1], value, 0.0), axis=1, keepdims=True))
    logit = product_ref[...] * (values[0] - values[1])
    wide = lax.broadcasted_iota(jnp.int32, (1, TILE), 1)
    logit_grad = (
        jnp.where(wide == route_ref[:, :1], logit, 0.0) - jnp.where(wide == route_ref[:, 1:2], logit, 0.0)
    ).astype(BF)
    normed_grad = picked_rows(code_ref[...], segments) + dot(logit_grad, router_ref[...], NT)
    residual = residual_ref[...]
    gain = gain_ref[...]
    inverse = lax.rsqrt(jnp.mean(residual * residual, axis=-1, keepdims=True) + 1e-06)
    plain = residual * inverse
    scaled = normed_grad * gain
    mean = jnp.mean(scaled * plain, axis=-1, keepdims=True)
    place = lax.broadcasted_iota(jnp.int32, (block, 1), 0) + step * block
    grad_out = jnp.where(place < length_ref[0], grad_ref[0].astype(F32), 0.0)
    total = grad_out + inverse * (scaled - plain * mean)
    total_ref[...] = total
    branch = total.astype(BF)
    mixed_grad_ref[...] = dot(branch, output_ref[...]).astype(BF)
    router_part = dot((plain * gain).astype(BF), logit_grad, TN)
    gain_part = column_sum(normed_grad * plain)
    extra = router_part + jnp.where(wide == experts + 1, gain_part, 0.0)
    output_part = dot(branch, mixed_ref[...], TN)

    @pl.when(step == 0)
    def _():
        extra_ref[...] = extra
        acc_ref[...] = output_part

    @pl.when(step > 0)
    def _():
        extra_ref[...] += extra
        acc_ref[...] += output_part

    @pl.when(step == pl.num_programs(0) - 1)
    def _():
        far_ref[...] = acc_ref[:, TILE:].astype(BF)
        own_ref[:, :TILE] = acc_ref[:, :TILE]
        own_ref[:, TILE:] = acc_ref[:, 2 * TILE :]


def combine(micro, core, length, code, route, slot, product, out_grad, residual, mixed, gain, router, output_own, gates, segments, half):
    width = residual.shape[1]
    block = 256
    cols = mixed.shape[1]
    whole = lambda arr: pl.BlockSpec(arr.shape, lambda i, *_: (0, 0))
    fixed = lambda rows, n: pl.BlockSpec((rows, n), lambda i, *_: (0, 0))
    here = lambda n: pl.BlockSpec((block, n), lambda i, *_: (i, 0))
    experts = gates[0].shape[0]
    return pl.pallas_call(
        functools.partial(combine_kernel, experts, half),
        grid_spec=pltpu.PrefetchScalarGridSpec(
            num_scalar_prefetch=3,
            grid=(SEQ // block,),
            in_specs=[
                here(2), here(2), here(2), here(1),
                pl.BlockSpec((1, block, width), lambda i, m, *_: (m[0], i, 0)),
                here(width), here(cols), whole(gain), whole(router), whole(output_own),
            ]
            + [whole(g) for g in gates]
            + [whole(x) for x in segments],
            out_specs=[here(width), here(cols), fixed(width, TILE), fixed(width, 2 * TILE), fixed(width, 2 * TILE)],
            scratch_shapes=[pltpu.VMEM((width, cols), F32)],
        ),
        out_shape=[
            jax.ShapeDtypeStruct((SEQ, width), F32),
            jax.ShapeDtypeStruct((SEQ, cols), BF),
            jax.ShapeDtypeStruct((width, TILE), F32),
            jax.ShapeDtypeStruct((width, 2 * TILE), BF),
            jax.ShapeDtypeStruct((width, 2 * TILE), F32),
        ],
        compiler_params=pltpu.CompilerParams(vmem_limit_bytes=56 * 2**20),
        cost_estimate=SMALL_COST,
        name="combine",
    )(micro, core, length, code, route, slot, product, out_grad, residual, mixed, gain, router, output_own, *gates, *segments)


def output_kernel(core_ref, length_ref, code_ref, residual_ref, own_ref, far_ref, out_ref):
    block = code_ref.shape[0]
    place = lax.broadcasted_iota(jnp.int32, (block, 1), 0) + (core_ref[0] * 2 + pl.program_id(0)) * block
    rows = residual_ref[...] + picked_rows(code_ref[...], (own_ref, far_ref))
    out_ref[...] = jnp.where(place < length_ref[0], rows, 0.0).astype(BF)


def output_rows(core, length, code, residual, own, far):
    width = residual.shape[1]
    block = 256
    here = lambda n: pl.BlockSpec((block, n), lambda i, c, *_: (c[0] * 2 + i, 0))
    whole = lambda arr: pl.BlockSpec(arr.shape, lambda i, *_: (0, 0))
    return pl.pallas_call(
        output_kernel,
        grid_spec=pltpu.PrefetchScalarGridSpec(
            num_scalar_prefetch=2,
            grid=(2,),
            in_specs=[here(2), here(width), whole(own), whole(far)],
            out_specs=pl.BlockSpec((block, width), lambda i, *_: (i, 0)),
        ),
        out_shape=jax.ShapeDtypeStruct((2 * block, width), BF),
        compiler_params=pltpu.CompilerParams(vmem_limit_bytes=40 * 2**20),
        cost_estimate=SMALL_COST,
        name="output_rows",
    )(core, length, code, residual, own, far)


def far_weight_kernel(normed_ref, q_ref, k_ref, v_ref, far_ref, own_ref):
    rows = normed_ref.shape[1]
    low = low_lanes((rows, TILE))
    q, k, v = (dot(normed_ref[...], d[...], TN) for d in (q_ref, k_ref, v_ref))
    for n, part in enumerate((q, k, v)):
        far_ref[:, n * TILE : (n + 1) * TILE] = part[:, :TILE].astype(BF)
    q, k, v = (part[:, TILE:] for part in (q, k, v))
    far_ref[:, 3 * TILE : 4 * TILE] = jnp.where(low, turned(q), k).astype(BF)
    far_ref[:, 4 * TILE :] = jnp.where(low, turned(v), 0.0).astype(BF)
    own_ref[:, :TILE] = jnp.where(low, q, turned(k))
    own_ref[:, TILE:] = jnp.where(low, v, 0.0)


def far_weight_grads(normed, q, k, v):
    width = normed.shape[1]
    block = 256
    whole = lambda arr: pl.BlockSpec(arr.shape, lambda i: (0, 0))
    here = lambda n: pl.BlockSpec((block, n), lambda i: (i, 0))
    return pl.pallas_call(
        far_weight_kernel,
        grid=(width // block,),
        in_specs=[pl.BlockSpec((SEQ, block), lambda i: (0, i)), whole(q), whole(k), whole(v)],
        out_specs=[here(5 * TILE), here(2 * TILE)],
        out_shape=[jax.ShapeDtypeStruct((width, 5 * TILE), BF), jax.ShapeDtypeStruct((width, 2 * TILE), F32)],
        compiler_params=pltpu.CompilerParams(vmem_limit_bytes=40 * 2**20),
        cost_estimate=SMALL_COST,
        name="far_weight_grads",
    )(normed, q, k, v)


def own_weight_kernel(normed_ref, q_ref, k_ref, v_ref, own_ref):
    for n, d in enumerate((q_ref, k_ref, v_ref)):
        own_ref[:, n * TILE : (n + 1) * TILE] = dot(normed_ref[...], d[...], TN)


def own_weight_grads(normed, q, k, v):
    width = normed.shape[1]
    block = 256
    whole = lambda arr: pl.BlockSpec(arr.shape, lambda i: (0, 0))
    return pl.pallas_call(
        own_weight_kernel,
        grid=(width // block,),
        in_specs=[pl.BlockSpec((SEQ, block), lambda i: (0, i)), whole(q), whole(k), whole(v)],
        out_specs=pl.BlockSpec((block, 3 * TILE), lambda i: (i, 0)),
        out_shape=jax.ShapeDtypeStruct((width, 3 * TILE), F32),
        compiler_params=pltpu.CompilerParams(vmem_limit_bytes=40 * 2**20),
        cost_estimate=SMALL_COST,
        name="own_weight_grads",
    )(normed, q, k, v)


def projected_back(weight_ref, first, last):
    total = None
    for n in range(3):
        base = 3 * n * TILE
        total = put(total, dot(first[n][...], weight_ref[:, base : base + TILE], NT))
        total = put(total, dot(last[n][...], weight_ref[:, base + TILE : base + 3 * TILE], NT))
    return total


def sent_kernel(core_ref, weight_ref, q0, k0, v0, q1, k1, v1, out_ref):
    out_ref[...] = projected_back(weight_ref, (q0, k0, v0), (q1, k1, v1))


def sent_half(core, weight, first, last):
    width = weight.shape[0]
    block = 256
    here = lambda n: pl.BlockSpec((block, n), lambda i, c: ((1 - c[0]) * 2 + i, 0))
    return pl.pallas_call(
        sent_kernel,
        grid_spec=pltpu.PrefetchScalarGridSpec(
            num_scalar_prefetch=1,
            grid=(2,),
            in_specs=[pl.BlockSpec(weight.shape, lambda i, c: (0, 0))] + [here(TILE)] * 3 + [here(2 * TILE)] * 3,
            out_specs=pl.BlockSpec((block, width), lambda i, c: (i, 0)),
        ),
        out_shape=jax.ShapeDtypeStruct((2 * block, width), F32),
        compiler_params=pltpu.CompilerParams(vmem_limit_bytes=40 * 2**20),
        cost_estimate=SMALL_COST,
        name="sent_half",
    )(core, weight, *first, *last)


def input_kernel(
    lane, micro_ref, core_ref, weight_ref, q0, k0, v0, q1, k1, v1, got_ref, tokens_ref, gain_ref, grad_ref, out_ref, extra_ref
):
    normed_grad = got_ref[...] + projected_back(weight_ref, (q0, k0, v0), (q1, k1, v1))
    x = tokens_ref[0].astype(F32)
    inverse = lax.rsqrt(jnp.mean(x * x, axis=-1, keepdims=True) + 1e-06)
    plain = x * inverse
    scaled = normed_grad * gain_ref[...]
    mean = jnp.mean(scaled * plain, axis=-1, keepdims=True)
    out_ref[...] = (grad_ref[...] + inverse * (scaled - plain * mean)).astype(BF)
    wide = lax.broadcasted_iota(jnp.int32, (1, TILE), 1)
    extra = jnp.where(wide == lane, column_sum(normed_grad * plain), 0.0)

    @pl.when(pl.program_id(0) == 0)
    def _():
        extra_ref[...] = extra

    @pl.when(pl.program_id(0) > 0)
    def _():
        extra_ref[...] += extra


def input_half(lane, micro, core, weight, first, last, got, layer_input, gain, residual_grad):
    width = weight.shape[0]
    block = 256
    here = lambda n: pl.BlockSpec((block, n), lambda i, m, c: (c[0] * 2 + i, 0))
    plain = pl.BlockSpec((block, width), lambda i, *_: (i, 0))
    return pl.pallas_call(
        functools.partial(input_kernel, lane),
        grid_spec=pltpu.PrefetchScalarGridSpec(
            num_scalar_prefetch=2,
            grid=(2,),
            in_specs=[pl.BlockSpec(weight.shape, lambda i, *_: (0, 0))]
            + [here(TILE)] * 3
            + [here(2 * TILE)] * 3
            + [
                plain,
                pl.BlockSpec((1, block, width), lambda i, m, c: (m[0], c[0] * 2 + i, 0)),
                pl.BlockSpec(gain.shape, lambda i, *_: (0, 0)),
                here(width),
            ],
            out_specs=[plain, pl.BlockSpec((width, TILE), lambda i, *_: (0, 0))],
        ),
        out_shape=[jax.ShapeDtypeStruct((2 * block, width), BF), jax.ShapeDtypeStruct((width, TILE), F32)],
        compiler_params=pltpu.CompilerParams(vmem_limit_bytes=40 * 2**20),
        cost_estimate=SMALL_COST,
        name="input_half",
    )(micro, core, weight, *first, *last, got, layer_input, gain, residual_grad)


def sum_kernel(kept, own01, own2, got, out_own, out_got, early, late, table, sum_ref):
    low = low_lanes(early.shape)
    sum_ref[:, : 3 * TILE] = (own01[...] + got[:, : 3 * TILE].astype(F32)).astype(BF)
    sum_ref[:, 3 * TILE : 4 * TILE] = (own2[:, :TILE] + got[:, 3 * TILE : 4 * TILE].astype(F32)).astype(BF)
    values = own2[:, TILE:] + got[:, 4 * TILE :].astype(F32)
    outputs = turned(out_own[:, TILE:]) + out_got[:, TILE:].astype(F32)
    sum_ref[:, 4 * TILE : 5 * TILE] = jnp.where(low, values, outputs).astype(BF)
    sum_ref[:, 5 * TILE : 6 * TILE] = (out_own[:, :TILE] + out_got[:, :TILE].astype(F32)).astype(BF)
    extra = early[...] + late[...] + table[...]
    high = extra.astype(BF)
    rest = extra - high.astype(F32)
    if kept <= HEAD_DIM:
        sum_ref[:, 6 * TILE :] = jnp.where(low, high.astype(F32), turned(rest)).astype(BF)
    else:
        sum_ref[:, 6 * TILE : 7 * TILE] = high
        sum_ref[:, 7 * TILE :] = rest.astype(BF)


def packed_sums(kept, own01, own2, got, out_own, out_got, early, late, table):
    width = own01.shape[0]
    cols = (7 if kept <= HEAD_DIM else 8) * TILE
    block = 256
    here = lambda n: pl.BlockSpec((block, n), lambda i: (i, 0))
    parts = (own01, own2, got, out_own, out_got, early, late, table)
    return pl.pallas_call(
        functools.partial(sum_kernel, kept),
        grid=(width // block,),
        in_specs=[here(x.shape[1]) for x in parts],
        out_specs=here(cols),
        out_shape=jax.ShapeDtypeStruct((width, cols), BF),
        cost_estimate=SMALL_COST,
        name="packed_sums",
    )(*parts)


def pair_gate(logits, own, other):
    lanes = lax.broadcasted_iota(jnp.int32, logits.shape, 1)
    gap = jnp.sum(
        jnp.where(lanes == own, logits, 0.0) - jnp.where(lanes == other, logits, 0.0), axis=1, keepdims=True
    )
    small = jnp.exp(-jnp.abs(gap))
    return jnp.where(gap >= 0.0, 1.0, small) / (1.0 + small)


def expert_kernel(
    me_ref, partner_ref, rows_ref, grads_ref, router_ref, a0, a1, a2, a3, b0, b1, b2, b3,
    back_ref, active_ref, slope_ref, gated_ref, scalar_ref, firsts, seconds, total, gate, mass_ref, sems,
):
    quarter = pl.program_id(0)
    copies = [
        (pltpu.make_async_copy(f, firsts.at[r], sems.at[0, r]), pltpu.make_async_copy(s, seconds.at[r], sems.at[1, r]))
        for r, (f, s) in enumerate(((a0, b0), (a1, b1), (a2, b2), (a3, b3)))
    ]

    @pl.when(quarter == 0)
    def _():
        for pair in copies:
            for copy in pair:
                copy.start()
        gate[...] = pair_gate(dot(rows_ref[...], router_ref[...]), me_ref[0], partner_ref[...])
        gated_ref[...] = (gate[...] * grads_ref[...].astype(F32)).astype(BF)

    for r, pair in enumerate(copies):

        @pl.when(quarter == r)
        def _(pair=pair):
            for copy in pair:
                copy.wait()

    rows = rows_ref[...]
    grads = grads_ref[...]
    width = firsts.shape[2]
    step = 256
    mass = None
    for c in range(0, width, step):
        x = dot(rows, firsts[quarter, :, c : c + step])
        plain = dot(grads, seconds[quarter, c : c + step, :], NT)
        square = x * x
        bent = jnp.tanh(x * (GELU_C + (GELU_C * GELU_A) * square))
        rise = 0.5 + 0.5 * bent
        active = x * rise
        slope = rise + active * (1.0 - bent) * (GELU_C + (3.0 * GELU_C * GELU_A) * square)
        low = active.astype(BF)
        active_ref[:, c : c + step] = low
        slope_ref[:, c : c + step] = (gate[...] * plain * slope).astype(BF)
        part = low.astype(F32) * plain
        mass = put(mass, part[:, :TILE] + part[:, TILE:])
    back = dot(slope_ref[...], firsts[quarter], NT)

    @pl.when(quarter == 0)
    def _():
        total[...] = back
        mass_ref[...] = mass

    @pl.when(quarter > 0)
    def _():
        total[...] += back
        mass_ref[...] += mass

    @pl.when(quarter == 3)
    def _():
        back_ref[...] = total[...].astype(BF)
        lanes = lax.broadcasted_iota(jnp.int32, mass_ref.shape, 1)
        scalar_ref[...] = jnp.where(lanes == 0, jnp.sum(mass_ref[...], axis=1, keepdims=True), gate[...])


def expert_rows_pass(me, partner, rows, grads, router, firsts, seconds):
    total, width = rows.shape
    part = firsts[0].shape[1]
    whole = lambda n: pl.BlockSpec((total, n), lambda i: (0, 0))
    here = pl.BlockSpec((total, part), lambda i: (0, i))
    return pl.pallas_call(
        expert_kernel,
        grid=(4,),
        in_specs=[
            pl.BlockSpec(memory_space=pltpu.SMEM), whole(1), whole(width), whole(width),
            pl.BlockSpec(router.shape, lambda i: (0, 0)),
        ]
        + [pl.BlockSpec(memory_space=pl.ANY)] * 8,
        out_specs=[whole(width), here, here, whole(width), whole(TILE)],
        out_shape=[
            jax.ShapeDtypeStruct((total, width), BF),
            jax.ShapeDtypeStruct((total, 4 * part), BF),
            jax.ShapeDtypeStruct((total, 4 * part), BF),
            jax.ShapeDtypeStruct((total, width), BF),
            jax.ShapeDtypeStruct((total, TILE), F32),
        ],
        scratch_shapes=[
            pltpu.VMEM((4, width, part), BF),
            pltpu.VMEM((4, part, width), BF),
            pltpu.VMEM((total, width), F32),
            pltpu.VMEM((total, 1), F32),
            pltpu.VMEM((total, TILE), F32),
            pltpu.SemaphoreType.DMA((2, 4)),
        ],
        compiler_params=pltpu.CompilerParams(vmem_limit_bytes=56 * 2**20),
        cost_estimate=SMALL_COST,
        name="expert_rows",
    )(me, partner, rows, grads, router, *firsts, *seconds)


def row_block(total):
    return 320 if total % 320 == 0 else total


def result_kernel(active_ref, scalar_ref, b0, b1, b2, b3, out_ref):
    width = b0.shape[0]
    total = None
    for r, second in enumerate((b0, b1, b2, b3)):
        part = dot(active_ref[:, r * width : (r + 1) * width], second[...])
        total = part if total is None else total + part
    out_ref[...] = (total * scalar_ref[:, 1:2]).astype(BF)


def expert_results(active, scalars, seconds):
    total, hidden = active.shape
    width = seconds[0].shape[1]
    block = row_block(total)
    here = lambda cols: pl.BlockSpec((block, cols), lambda i: (i, 0))
    return pl.pallas_call(
        result_kernel,
        grid=(total // block,),
        in_specs=[here(hidden), here(TILE)] + [pl.BlockSpec(w.shape, lambda i: (0, 0)) for w in seconds],
        out_specs=here(width),
        out_shape=jax.ShapeDtypeStruct((total, width), BF),
        compiler_params=pltpu.CompilerParams(vmem_limit_bytes=56 * 2**20),
        cost_estimate=SMALL_COST,
        name="expert_results",
    )(active, scalars, *seconds)


def weight_kernel(count, *refs):
    rows, slopes, active, gated = (refs[n * count : (n + 1) * count] for n in range(4))
    out_ref = refs[-1]
    first, second = None, None
    for n in range(count):
        first = put(first, dot(rows[n][...], slopes[n][...], TN))
        second = put(second, dot(active[n][...], gated[n][...], TN))
    out_ref[0, 0] = first.astype(out_ref.dtype)
    out_ref[0, 1] = second.astype(out_ref.dtype)


def expert_weight_grads(rows, slopes, active, gated, first_quarter, kind):
    total, width = rows[0].shape
    hidden = slopes[0].shape[1] // 4
    whole = pl.BlockSpec((total, width), lambda i: (0, 0))
    part = pl.BlockSpec((total, hidden), lambda i: (0, first_quarter + i))
    count = len(rows)
    return pl.pallas_call(
        functools.partial(weight_kernel, count),
        grid=(2,),
        in_specs=[whole] * count + [part] * (2 * count) + [whole] * count,
        out_specs=pl.BlockSpec((1, 2, width, hidden), lambda i: (i, 0, 0, 0)),
        out_shape=jax.ShapeDtypeStruct((2, 2, width, hidden), kind),
        compiler_params=pltpu.CompilerParams(vmem_limit_bytes=56 * 2**20),
        cost_estimate=SMALL_COST,
        name="expert_weight_grads",
    )(*rows, *slopes, *active, *gated)


def place_kernel(place_ref, a_ref, b_ref, c_ref, d_ref, out_ref):
    for n, piece in enumerate((a_ref, b_ref, c_ref, d_ref)):

        @pl.when(pl.program_id(0) == n)
        def _(piece=piece):
            out_ref[0] = piece[...]


def place_pieces(places, pieces):
    shape = pieces[0].shape
    whole = pl.BlockSpec(shape, lambda i, place_ref: (0, 0))
    return pl.pallas_call(
        place_kernel,
        grid_spec=pltpu.PrefetchScalarGridSpec(
            num_scalar_prefetch=1,
            grid=(4,),
            in_specs=[whole] * 4,
            out_specs=pl.BlockSpec((1,) + shape, lambda i, place_ref: (place_ref[i], 0, 0)),
        ),
        out_shape=jax.ShapeDtypeStruct((4,) + shape, pieces[0].dtype),
        compiler_params=pltpu.CompilerParams(vmem_limit_bytes=32 * 2**20),
        cost_estimate=SMALL_COST,
        name="place_pieces",
    )(places, *pieces)


def swap(value, axis, count, bit):
    return lax.ppermute(value, axis, [(i, i ^ bit) for i in range(count)])


def all_to_all(value):
    return lax.all_to_all(value, "dp", split_axis=0, concat_axis=0, tiled=True)


def together(*values):
    return lax.optimization_barrier(values)


def local(
    layer_input, out_grad, first_gain, query_weight, key_weight, value_weight, output_weight,
    position_bias, second_gain, router_weight, expert_in, expert_out, seq_lengths, routes,
):
    micro_count, tok_rows, width = layer_input.shape
    dp_count = lax.axis_size("dp")
    expert_count = router_weight.shape[1]
    shard = query_weight.shape[1]
    heads_here = position_bias.shape[0]
    assert lax.axis_size("tensor") == 4 and micro_count == 2 and expert_count == dp_count
    assert tok_rows == SEQ and seq_lengths.shape[1] == 1
    capacity = max(8, 8 * (10 * tok_rows // (32 * expert_count)))
    half = capacity // 2
    stride = 8 * (half // 8 + 1)
    chunks = 2 if half % 32 == 0 else 1
    chunk = half // chunks
    chunk_rows = expert_count * chunk
    rows_here = query_weight.shape[0]
    me = lax.axis_index("dp")
    rank = lax.axis_index("tensor")
    micro = rank // 2
    core = rank % 2

    def swap_y(value):
        return swap(value, "tensor", 4, 2)

    def swap_core(value):
        return swap(value, "tensor", 4, 1)

    micro_arg = micro.reshape(1).astype(jnp.int32)
    core_arg = core.reshape(1).astype(jnp.int32)

    packed = pack_weights(query_weight, key_weight, value_weight, output_weight, first_gain, second_gain, router_weight)
    three = 3 * TILE

    def doubled(stacked, bit, axis=0):
        other = swap(stacked, "dp", dp_count, bit)
        high = (me & bit) != 0
        pair = jnp.where(high, jnp.stack([other, stacked], axis + 1), jnp.stack([stacked, other], axis + 1))
        return pair.reshape(stacked.shape[:axis] + (-1,) + stacked.shape[axis + 1 :])

    stacked = packed[None]
    bit = dp_count // 2
    while bit > 1:
        stacked = doubled(stacked, bit)
        bit //= 2
    first_own = expert_in[0]
    second_own = expert_out[0]
    first_y = swap_y(first_own)
    stacked, first_y = together(stacked, first_y)
    part_b = stacked[:, :, :three]
    part_a = doubled(stacked[:, :, three:], 1)
    pair_b = jnp.stack([part_b, swap_y(part_b)])
    a_own = part_a[:, :, :three]
    a_far = swap_y(a_own).reshape(width, three)
    a_own = a_own.reshape(width, three)
    pair_b = doubled(pair_b, 1, 1).reshape(2, width, three)
    small_all = part_a[:, :, three:].reshape(width, TILE)
    gain_one = small_all[:, expert_count].astype(F32)[None]
    gain_two = small_all[:, expert_count + 1].astype(F32)[None]
    router_wide = small_all
    far_bias = swap_y(position_bias)
    bias = jnp.concatenate([position_bias[:2], far_bias[:2], position_bias[2:], far_bias[2:]], 0)
    head_total = bias.shape[0]
    hot_const = jnp.asarray(NEAR_HOT, dtype=BF)
    near = dot(bias, hot_const) - bias[:, NB - 1 :].astype(F32)
    near = near.reshape(head_total, 2, TILE, TILE)
    places = jnp.arange(TILE, dtype=jnp.int32)
    causal = jnp.stack([places[None, :] <= places[:, None], jnp.ones((TILE, TILE), bool)])
    near = jnp.where(causal[None], near, NEG)

    second_late, _ = together(second_own, pair_b)
    second_y = swap_y(second_late)

    grad_low = lax.dynamic_index_in_dim(out_grad, micro, 0, keepdims=False)
    length = lax.dynamic_index_in_dim(seq_lengths, micro, 0, keepdims=False)
    route = lax.dynamic_index_in_dim(routes, micro, 0, keepdims=False)
    valid = (jnp.arange(SEQ, dtype=jnp.int32) < length[0])[:, None]
    grad_low = jnp.where(valid, grad_low, BF(0))

    expert_ids = jnp.arange(expert_count, dtype=jnp.int32)
    named = (route[:, :, None] == expert_ids).astype(jnp.int32)
    per_token = jnp.sum(named, axis=1, dtype=jnp.int32)
    earlier = jnp.cumsum(per_token, axis=0, dtype=jnp.int32) - per_token
    slot = jnp.sum(named * earlier[:, None, :], axis=2, dtype=jnp.int32)
    here = slot // half == core
    within = slot % half
    chunk_of = within // chunk
    inside = within % chunk

    def hots(code, count):
        ids = jnp.arange(count, dtype=jnp.int32)
        return ids[:, None] == code[None, :, 0], ids[:, None] == code[None, :, 1]

    hit_first, hit_second = hots(jnp.where(here, route * stride + within, -1), expert_count * stride)
    partner = jnp.sum(
        jnp.where(hit_first, route[None, :, 1], 0) + jnp.where(hit_second, route[None, :, 0], 0), axis=1, dtype=jnp.int32
    )
    grads_sent = dot((hit_first | hit_second).astype(BF), grad_low).astype(BF).reshape(expert_count, stride, width)
    partner_row = jnp.pad(partner.reshape(expert_count, stride)[:, :half].astype(BF), ((0, 0), (0, width - half)))
    grads_sent = grads_sent.at[:, half].set(partner_row)
    grads_sent, _ = together(grads_sent, part_a)
    grads_here = all_to_all(grads_sent)
    partner_here = grads_here[:, half, :half].astype(jnp.int32)

    def chunk_grads(c):
        at = slice(c * chunk, (c + 1) * chunk)
        return grads_here[:, at].reshape(chunk_rows, width), partner_here[:, at].reshape(chunk_rows, 1)

    qkv, normed_one, qkv_weight, output_own = norm_and_project(
        micro_arg, layer_input, gain_one, a_own, a_far, pair_b[0], pair_b[1]
    )
    output_far = swap_core(output_own)
    mixed, logs = attend(length, qkv, near)
    mixed, second_y = together(mixed, second_y)
    mixed_far = swap_core(mixed)
    firsts = (first_own, first_y, swap_core(first_own), swap_core(first_y))
    seconds = (second_own, second_y, swap_core(second_own), swap_core(second_y))
    residual, normed_two = residual_and_norm(micro_arg, layer_input, mixed, mixed_far, output_own, output_far, gain_two)

    arrived = []
    for c in range(chunks):
        first, second = hots(jnp.where(here & (chunk_of == c), route * chunk + inside, -1), chunk_rows)
        sent = dot((first | second).astype(BF), normed_two).astype(BF).reshape(expert_count, chunk, width)
        if arrived:
            sent, arrived[-1] = together(sent, arrived[-1])
        arrived.append(all_to_all(sent))
    gap = dot(normed_two, router_wide)
    lanes = jnp.arange(TILE, dtype=jnp.int32)
    gap = jnp.sum(
        jnp.where(lanes == route[:, :1], gap, 0.0) - jnp.where(lanes == route[:, 1:], gap, 0.0), axis=1, keepdims=True
    )
    product = jnp.exp(-jnp.abs(gap))
    product = product / ((1.0 + product) * (1.0 + product))

    me_arg = me.reshape(1).astype(jnp.int32)
    rows_all, slopes, active, gated, scalars, backs = [], [], [], [], [], []
    for c in range(chunks):
        grads_c, partner_c = chunk_grads(c)
        rows_c = arrived[c].reshape(chunk_rows, width)
        back, act, slo, gat, sca = expert_rows_pass(me_arg, partner_c, rows_c, grads_c, router_wide, firsts, seconds)
        rows_all.append(rows_c)
        slopes.append(slo)
        active.append(act)
        gated.append(gat)
        scalars.append(sca)
        back = back.reshape(expert_count, chunk, width)
        if c == chunks - 1:
            gate_grad = jnp.concatenate([x[:, 0].reshape(expert_count, chunk) for x in scalars], 1)
            pieces = []
            for _ in range(3):
                piece = gate_grad.astype(BF)
                pieces.append(piece)
                gate_grad = gate_grad - piece.astype(F32)
            gate_row = jnp.pad(jnp.concatenate(pieces, 1), ((0, 0), (0, width - 3 * half)))
            back = jnp.concatenate([back, jnp.pad(gate_row[:, None], ((0, 0), (0, 7), (0, 0)))], 1)
        backs.append(all_to_all(back))
    grads_cross = expert_weight_grads(rows_all, slopes, active, gated, 2, BF)
    grads_in = swap_core(grads_cross).astype(F32)
    grads_kept = expert_weight_grads(rows_all, slopes, active, gated, 0, F32)
    results = [expert_results(active[c], scalars[c], seconds).reshape(expert_count, chunk, width) for c in range(chunks)]
    results = jnp.concatenate(results, 1) if chunks > 1 else results[0]

    y_first = swap_y((grads_kept[1, 0] + grads_in[1, 0]).astype(BF))
    backs[-1], results, y_first = together(backs[-1], results, y_first)
    y_second, _ = together((grads_kept[1, 1] + grads_in[1, 1]).astype(BF), y_first)
    y_second = swap_y(y_second)
    expert_in_grad = grads_kept[0, 0] + grads_in[0, 0] + y_first.astype(F32)
    results_own = all_to_all(results).reshape(expert_count * half, width)

    backs_far = [swap_core(b) for b in backs]
    gate_tables = [b[-1][:, chunk] for b in (backs, backs_far)]
    segments = [b.reshape(-1, width) for b in backs + backs_far]
    last_stride = chunk + 8
    code = jnp.where(
        chunk_of == chunks - 1,
        (chunks - 1) * chunk_rows + route * last_stride + inside,
        chunk_of * chunk_rows + route * chunk + inside,
    )
    code = code + jnp.where(here, 0, (chunks - 1) * chunk_rows + expert_count * last_stride)
    residual_grad, mixed_grad, extra_early, output_sent, output_kept = combine(
        micro_arg, core_arg, length, code, route, slot, product, out_grad, residual, mixed, gain_two, router_wide,
        output_own, gate_tables, segments, half,
    )
    output_got = swap_y(output_sent)

    q1, k1, v1, tiles1, sums1 = attend_back(length, qkv, near, mixed, logs, mixed_grad, 1, 2)
    q1, y_second, output_got = together(q1, y_second, output_got)
    expert_out_grad = grads_kept[0, 1] + grads_in[0, 1] + y_second.astype(F32)
    far_sent, own_last = far_weight_grads(normed_one, q1, k1, v1)
    far_got = swap_y(far_sent)
    mixed_grad, far_sent = together(mixed_grad, far_sent)
    q0, k0, v0, tiles0, sums0 = attend_back(length, qkv, near, mixed, logs, mixed_grad, 0, 1)
    first, last = (q0, k0, v0), (q1, k1, v1)
    got = swap_core(sent_half(core_arg, qkv_weight, first, last))
    own_pair = own_weight_grads(normed_one, q0, k0, v0)
    corner = micro * 2 + core
    corners = jnp.stack([corner, corner ^ 1, corner ^ 2, corner ^ 3]).astype(jnp.int32)

    def placed(own):
        across = swap_y(own)
        return place_pieces(corners, (own, swap_core(own), across, swap_core(across))).reshape(2, SEQ, width)

    input_rows, extra_late = input_half(
        expert_count, micro_arg, core_arg, qkv_weight, first, last, got, layer_input, gain_one, residual_grad
    )
    input_grad = placed(input_rows)

    results_own, _ = together(results_own, q0)
    result_code = route * half + within + jnp.where(here, 0, expert_count * half)
    layer_rows = output_rows(core_arg, length, result_code, residual, results_own, swap_core(results_own))
    layer_output = placed(layer_rows)

    tiles = jnp.concatenate([tiles0, tiles1], 0).reshape(head_total, 2 * TILE * TILE)
    sums = jnp.concatenate([sums0, sums1], 0)
    tiles_high = tiles.astype(BF)
    tiles_rest = (tiles - tiles_high.astype(F32)).astype(BF)
    table = dot(tiles_high, hot_const, NT) + dot(tiles_rest, hot_const, NT)
    far_sum = jnp.sum(sums[:, :, 0], axis=1) - jnp.sum(table[:, : NB - 1], axis=1)
    table = jnp.concatenate([table[:, : NB - 1], far_sum[:, None]], 1)
    table_own = jnp.concatenate([table[0:2], table[4:5]], 0)
    table_far = jnp.concatenate([table[2:4], table[5:6]], 0)
    table_cols = heads_here * NB // rows_here
    table_both = jnp.concatenate([table_own.reshape(rows_here, table_cols), table_far.reshape(rows_here, table_cols)], 1)
    base = expert_count + 2
    kept = base + 2 * table_cols
    table_tile = jnp.tile(jnp.pad(table_both, ((0, 0), (base, TILE - kept))), (dp_count, 1))

    grads = packed_sums(kept, own_pair, own_last, far_got, output_kept, output_got, extra_early, extra_late, table_tile)
    arrived_grads = all_to_all(grads.reshape(dp_count, rows_here, grads.shape[1]))
    total = jnp.sum(arrived_grads.astype(F32), axis=0)
    wide = HEAD_DIM if kept <= HEAD_DIM else TILE
    small = total[:, 6 * TILE : 6 * TILE + kept] + total[:, 6 * TILE + wide : 6 * TILE + wide + kept]
    small_y = swap_y(small)
    gain_one_half = small[:, expert_count] + small_y[:, expert_count]
    column = lambda t: total[:, t * TILE : (t + 1) * TILE]
    pair_of = lambda t, last_tile, high: jnp.concatenate(
        [column(t), column(last_tile)[:, HEAD_DIM:] if high else column(last_tile)[:, :HEAD_DIM]], 1
    )
    return (
        layer_output,
        input_grad,
        gain_one_half + swap_core(gain_one_half),
        pair_of(0, 3, False),
        pair_of(1, 3, True),
        pair_of(2, 4, False),
        pair_of(5, 4, True).T,
        (small[:, base : base + table_cols] + small_y[:, base + table_cols :]).reshape(heads_here, NB),
        small[:, expert_count + 1] + small_y[:, expert_count + 1],
        small[:, :expert_count] + small_y[:, :expert_count],
        expert_in_grad[None],
        expert_out_grad[None],
    )


def solution(mesh):
    return jax.shard_map(
        local,
        mesh=mesh,
        in_specs=(
            P(None, "dp", None),
            P(None, "dp", None),
            P("dp"),
            P("dp", "tensor"),
            P("dp", "tensor"),
            P("dp", "tensor"),
            P("tensor", "dp"),
            P("tensor", None),
            P("dp"),
            P("dp", None),
            P("dp", None, "tensor"),
            P("dp", "tensor", None),
            P(None, "dp"),
            P(None, "dp", None),
        ),
        out_specs=(
            P(None, "dp", None),
            P(None, "dp", None),
            P("dp"),
            P("dp", "tensor"),
            P("dp", "tensor"),
            P("dp", "tensor"),
            P("tensor", "dp"),
            P("tensor", None),
            P("dp"),
            P("dp", None),
            P("dp", None, "tensor"),
            P("dp", "tensor", None),
        ),
        check_vma=False,
    )
```

```python
import functools

import jax
import jax.numpy as jnp
import numpy as np
from jax import lax
from jax.experimental import pallas as pl
from jax.experimental.pallas import tpu as pltpu
from jax.sharding import PartitionSpec as P

HEAD_DIM = 64
NB = 32
SEQ = 1024
TILE = 128
QROWS = 256
NEG = -1e30
GELU_C = 0.7978845608028654
GELU_A = 0.044715

BF = jnp.bfloat16
F32 = jnp.float32

bucket_edges = np.ceil(16.0 * 8.0 ** (np.arange(1, 16) / 16.0)).astype(np.int32)


def near_tables():
    rows = np.arange(TILE)[:, None]
    cols = np.arange(TILE)[None, :]
    hots = []
    for shift in (0, TILE):
        distance = rows - cols + shift
        clipped = np.maximum(distance, 0)
        reached = np.sum(clipped[..., None] >= bucket_edges, axis=-1)
        bucket = np.minimum(clipped, 16) + reached
        hots.append(bucket[..., None] == np.arange(NB))
    hot = np.stack(hots).reshape(2 * TILE * TILE, NB).T
    return hot


NEAR_HOT = near_tables()
assert bucket_edges[-1] <= TILE


def dot(a, b, dims=((1,), (0,))):
    return lax.dot_general(a, b, (dims, ((), ())), preferred_element_type=F32)


NT = ((1,), (1,))
TN = ((0,), (0,))


VMEM_LIMIT = 60 * 2**20
SMALL_COST = pl.CostEstimate(flops=1_000_000, bytes_accessed=1_000_000, transcendentals=0)


def score_tiles(block, half, q_half, key_ref, near_one, near_two, length):
    tiles = []
    for j in range(block + 1):
        s = dot(q_half, key_ref[j * QROWS : (j + 1) * QROWS, :], NT)
        if j == block:
            top = jnp.concatenate([s[:TILE, :TILE] + near_one, jnp.full((TILE, TILE), NEG, F32)], 1)
            low = jnp.concatenate([s[TILE:, :TILE] + near_two, s[TILE:, TILE:] + near_one], 1)
            s = jnp.concatenate([top, low], 0)
        elif j == block - 1:
            top = jnp.concatenate([s[:TILE, :TILE], s[:TILE, TILE:] + near_two], 1)
            s = jnp.concatenate([top, s[TILE:]], 0)
        if (j + 1) * QROWS > SEQ // 2:
            place = lax.broadcasted_iota(jnp.int32, (1, QROWS), 1) + j * QROWS
            s = s + jnp.where(place < length, 0.0, NEG)
        tiles.append(s)
    return tiles


def lane_half(rows):
    return lax.broadcasted_iota(jnp.int32, (rows, 2 * HEAD_DIM), 1) < HEAD_DIM


def attend_kernel(length_ref, query_ref, key_ref, value_ref, near_ref, out_ref, log_ref):
    length = length_ref[0]
    lanes = lane_half(QROWS)
    ones = jnp.ones((SEQ, TILE), BF)
    value_ext = jnp.concatenate([value_ref[...], ones], 1)
    for i in range(SEQ // QROWS):
        q_rows = query_ref[i * QROWS : (i + 1) * QROWS, :] * BF(0.125)
        outs, logs = [], []
        for h in range(2):
            keep = lanes if h == 0 else ~lanes
            q_half = jnp.where(keep, q_rows, BF(0))
            tiles = score_tiles(i, h, q_half, key_ref, near_ref[h, 0], near_ref[h, 1], length)
            top = tiles[0]
            for s in tiles[1:]:
                top = jnp.maximum(top, s)
            top = jnp.max(top, axis=1, keepdims=True)
            total = None
            for j, s in enumerate(tiles):
                p = jnp.exp(s - top).astype(BF)
                part = dot(p, value_ext[j * QROWS : (j + 1) * QROWS, :])
                total = part if total is None else total + part
            row_sum = total[:, TILE:]
            outs.append(total[:, :TILE] / row_sum)
            logs.append(top + jnp.log(row_sum))
        out_ref[i * QROWS : (i + 1) * QROWS, :] = jnp.where(lanes, outs[0], outs[1]).astype(BF)
        log_ref[i * QROWS : (i + 1) * QROWS, :] = jnp.where(lanes, logs[0], logs[1])


def attend(length, qkv, near):
    pairs = qkv.shape[1] // (3 * TILE)
    cols = pairs * TILE
    return pl.pallas_call(
        attend_kernel,
        grid=(pairs,),
        in_specs=[
            pl.BlockSpec(memory_space=pltpu.SMEM),
            pl.BlockSpec((SEQ, TILE), lambda p: (0, p)),
            pl.BlockSpec((SEQ, TILE), lambda p: (0, pairs + p)),
            pl.BlockSpec((SEQ, TILE), lambda p: (0, 2 * pairs + p)),
            pl.BlockSpec((2, 2, TILE, TILE), lambda p: (p, 0, 0, 0)),
        ],
        out_specs=[
            pl.BlockSpec((SEQ, TILE), lambda p: (0, p)),
            pl.BlockSpec((SEQ, TILE), lambda p: (0, p)),
        ],
        out_shape=[
            jax.ShapeDtypeStruct((SEQ, cols), BF),
            jax.ShapeDtypeStruct((SEQ, cols), F32),
        ],
        compiler_params=pltpu.CompilerParams(vmem_limit_bytes=VMEM_LIMIT),
        cost_estimate=SMALL_COST,
        name="attend",
    )(length, qkv, qkv, qkv, near)


def attend_back_kernel(
    length_ref, query_ref, key_ref, value_ref, near_ref, out_ref, log_ref, grad_ref,
    dq_ref, dk_ref, dv_ref, tile_ref, sum_ref, dk_acc, dv_acc,
):
    length = length_ref[0]
    lanes = lane_half(QROWS)
    lanes_all = lane_half(SEQ)
    ones = jnp.ones((SEQ, TILE), BF)
    key_ext = [
        jnp.concatenate([jnp.where(lanes_all, key_ref[...], BF(0)), ones], 1),
        jnp.concatenate([jnp.where(lanes_all, BF(0), key_ref[...]), ones], 1),
    ]
    near_sums = [[None, None], [None, None]]
    all_sums = [None, None]

    for i in range(SEQ // QROWS):
        rows = slice(i * QROWS, (i + 1) * QROWS)
        q_rows = query_ref[rows, :] * BF(0.125)
        g_rows = grad_ref[rows, :]
        mass = g_rows.astype(F32) * out_ref[rows, :].astype(F32)
        dq = None
        for h in range(2):
            keep = lanes if h == 0 else ~lanes
            q_half = jnp.where(keep, q_rows, BF(0))
            g_half = jnp.where(keep, g_rows, BF(0))
            delta = jnp.sum(jnp.where(keep, mass, 0.0), axis=1, keepdims=True)
            log_col = log_ref[rows, h * HEAD_DIM : h * HEAD_DIM + 1]
            tiles = score_tiles(i, h, q_half, key_ref, near_ref[h, 0], near_ref[h, 1], length)
            for j, s in enumerate(tiles):
                keys = slice(j * QROWS, (j + 1) * QROWS)
                p = jnp.exp(s - log_col)
                dp = dot(g_half, value_ref[keys, :], NT)
                ds = (p * (dp - delta)).astype(BF)
                part = dot(ds, key_ext[h][keys, :])
                dq = put(dq, part[:, :TILE])
                all_sums[h] = put(all_sums[h], jnp.sum(part[:, TILE:].reshape(QROWS // 8, 8, TILE), axis=0))
                dk_part = dot(ds, q_half, TN)
                dv_part = dot(p.astype(BF), g_half, TN)
                if i == j and h == 0:
                    dk_acc[keys, :] = dk_part
                    dv_acc[keys, :] = dv_part
                else:
                    dk_acc[keys, :] += dk_part
                    dv_acc[keys, :] += dv_part
                if j == i:
                    wide = ds.astype(F32)
                    near_sums[h][0] = put(near_sums[h][0], wide[:TILE, :TILE] + wide[TILE:, TILE:])
                    near_sums[h][1] = put(near_sums[h][1], wide[TILE:, :TILE])
                elif j == i - 1:
                    near_sums[h][1] = put(near_sums[h][1], ds[:TILE, TILE:].astype(F32))
        dq_ref[rows, :] = (dq * 0.125).astype(BF)
    dk_ref[...] = dk_acc[...].astype(BF)
    dv_ref[...] = dv_acc[...].astype(BF)
    for h in range(2):
        tile_ref[h, 0] = near_sums[h][0]
        tile_ref[h, 1] = near_sums[h][1]
        sum_ref[h] = all_sums[h]


def attend_back(length, qkv, near, mixed, logs, grad, first, count):
    pairs = qkv.shape[1] // (3 * TILE)
    cols = count * TILE
    col = pl.BlockSpec((SEQ, TILE), lambda p: (0, first + p))
    out = pl.BlockSpec((SEQ, TILE), lambda p: (0, p))
    return pl.pallas_call(
        attend_back_kernel,
        grid=(count,),
        in_specs=[
            pl.BlockSpec(memory_space=pltpu.SMEM),
            col,
            pl.BlockSpec((SEQ, TILE), lambda p: (0, pairs + first + p)),
            pl.BlockSpec((SEQ, TILE), lambda p: (0, 2 * pairs + first + p)),
            pl.BlockSpec((2, 2, TILE, TILE), lambda p: (first + p, 0, 0, 0)),
            col,
            col,
            col,
        ],
        out_specs=[
            out,
            out,
            out,
            pl.BlockSpec((2, 2, TILE, TILE), lambda p: (p, 0, 0, 0)),
            pl.BlockSpec((2, 8, TILE), lambda p: (p, 0, 0)),
        ],
        out_shape=[
            jax.ShapeDtypeStruct((SEQ, cols), BF),
            jax.ShapeDtypeStruct((SEQ, cols), BF),
            jax.ShapeDtypeStruct((SEQ, cols), BF),
            jax.ShapeDtypeStruct((2 * count, 2, TILE, TILE), F32),
            jax.ShapeDtypeStruct((2 * count, 8, TILE), F32),
        ],
        scratch_shapes=[pltpu.VMEM((SEQ, TILE), F32), pltpu.VMEM((SEQ, TILE), F32)],
        compiler_params=pltpu.CompilerParams(vmem_limit_bytes=VMEM_LIMIT),
        cost_estimate=SMALL_COST,
        name="attend_back",
    )(length, qkv, qkv, qkv, near, mixed, logs, grad)


def low_lanes(shape):
    return lax.broadcasted_iota(jnp.int32, shape, 1) < HEAD_DIM


def turned(tile):
    return pltpu.roll(tile, HEAD_DIM, 1)


def pack_kernel(q_ref, k_ref, v_ref, o_ref, one_ref, two_ref, router_ref, out_ref):
    shard = q_ref.shape[1]
    rows = q_ref.shape[0]
    source = lax.broadcasted_iota(jnp.int32, (shard, 6 * TILE), 0)
    target = lax.broadcasted_iota(jnp.int32, (shard, 6 * TILE), 1)

    def moved(pair_base, last_base):
        want = jnp.where(source < TILE, source + pair_base, source - TILE + last_base)
        return jnp.where(target == want, 1.0, 0.0).astype(BF)

    total = dot(v_ref[...], moved(0, 2 * TILE)) + dot(o_ref[...], moved(TILE, 2 * TILE + HEAD_DIM), TN)
    total = total + dot(q_ref[...], moved(3 * TILE, 5 * TILE)) + dot(k_ref[...], moved(4 * TILE, 5 * TILE + HEAD_DIM))
    out_ref[:, : 6 * TILE] = total.astype(BF)
    experts = router_ref.shape[0]
    own_row = lax.broadcasted_iota(jnp.int32, (rows, rows), 0) == lax.broadcasted_iota(jnp.int32, (rows, rows), 1)

    def column(ref):
        return jnp.sum(jnp.where(own_row, ref[...].astype(F32), 0.0), axis=1, keepdims=True)

    lanes = lax.broadcasted_iota(jnp.int32, (experts, TILE), 1)
    spread = jnp.where(lanes == lax.broadcasted_iota(jnp.int32, (experts, TILE), 0), 1.0, 0.0).astype(BF)
    place = lax.broadcasted_iota(jnp.int32, (rows, TILE), 1)
    small = dot(router_ref[...], spread, TN)
    small = jnp.where(place == experts, column(one_ref), jnp.where(place == experts + 1, column(two_ref), small))
    out_ref[:, 6 * TILE :] = small.astype(BF)


def pack_weights(query, key, value, output, one, two, router):
    rows = query.shape[0]
    return pl.pallas_call(
        pack_kernel,
        out_shape=jax.ShapeDtypeStruct((rows, 7 * TILE), BF),
        compiler_params=pltpu.CompilerParams(vmem_limit_bytes=VMEM_LIMIT),
        cost_estimate=SMALL_COST,
        name="pack_weights",
    )(query, key, value, output, one[None], two[None], router.T)


def qkv_kernel(micro_ref, tokens_ref, gain_ref, a_own, a_far, b_own, b_far, qkv_ref, normed_ref, weight_ref, output_ref):
    width = tokens_ref.shape[2]

    @pl.when(pl.program_id(0) == 0)
    def _():
        low = low_lanes((width, TILE))

        def tiles(own, far, pair, low_half):
            at = slice(pair * TILE, (pair + 1) * TILE)
            one, two = own[:, 2 * TILE :].astype(F32), far[:, 2 * TILE :].astype(F32)
            last = jnp.where(low, one, turned(two)) if low_half else jnp.where(low, turned(one), two)
            return own[:, at], far[:, at], last.astype(BF)

        for n, (own, far, pair, low_half) in enumerate(
            ((a_own, a_far, 0, True), (a_own, a_far, 1, False), (b_own, b_far, 0, True))
        ):
            for t, tile in enumerate(tiles(own[...], far[...], pair, low_half)):
                at = 3 * n + t
                weight_ref[:, at * TILE : (at + 1) * TILE] = tile
        for t, tile in enumerate(tiles(b_own[...], b_far[...], 1, False)):
            output_ref[:, t * TILE : (t + 1) * TILE] = tile

    x = tokens_ref[0].astype(F32)
    inverse = lax.rsqrt(jnp.mean(x * x, axis=-1, keepdims=True) + 1e-06)
    normed = (x * inverse * gain_ref[...]).astype(BF)
    normed_ref[...] = normed
    qkv_ref[...] = dot(normed, weight_ref[...]).astype(BF)


def norm_and_project(micro, layer_input, gain, a_own, a_far, b_own, b_far):
    width = layer_input.shape[2]
    block = 256
    cols = 3 * TILE
    whole = lambda rows, n: pl.BlockSpec((rows, n), lambda i, m: (0, 0))
    here = lambda n: pl.BlockSpec((block, n), lambda i, m: (i, 0))
    return pl.pallas_call(
        qkv_kernel,
        grid_spec=pltpu.PrefetchScalarGridSpec(
            num_scalar_prefetch=1,
            grid=(SEQ // block,),
            in_specs=[pl.BlockSpec((1, block, width), lambda i, m: (m[0], i, 0)), whole(1, width)] + [whole(width, cols)] * 4,
            out_specs=[here(3 * cols), here(width), whole(width, 3 * cols), whole(width, cols)],
        ),
        out_shape=[
            jax.ShapeDtypeStruct((SEQ, 3 * cols), BF),
            jax.ShapeDtypeStruct((SEQ, width), BF),
            jax.ShapeDtypeStruct((width, 3 * cols), BF),
            jax.ShapeDtypeStruct((width, cols), BF),
        ],
        compiler_params=pltpu.CompilerParams(vmem_limit_bytes=VMEM_LIMIT),
        cost_estimate=SMALL_COST,
        name="norm_and_project",
    )(micro, layer_input, gain, a_own, a_far, b_own, b_far)


def middle_kernel(micro_ref, tokens_ref, mixed_ref, other_ref, own_ref, far_ref, gain_ref, residual_ref, normed_ref):
    total = tokens_ref[0].astype(F32) + dot(mixed_ref[...], own_ref[...], NT) + dot(other_ref[...], far_ref[...], NT)
    residual_ref[...] = total
    inverse = lax.rsqrt(jnp.mean(total * total, axis=-1, keepdims=True) + 1e-06)
    normed_ref[...] = (total * inverse * gain_ref[...]).astype(BF)


def residual_and_norm(micro, layer_input, mixed, other, output_own, output_far, gain):
    width = layer_input.shape[2]
    block = 256
    cols = mixed.shape[1]
    whole = lambda rows, n: pl.BlockSpec((rows, n), lambda i, m: (0, 0))
    here = lambda n: pl.BlockSpec((block, n), lambda i, m: (i, 0))
    return pl.pallas_call(
        middle_kernel,
        grid_spec=pltpu.PrefetchScalarGridSpec(
            num_scalar_prefetch=1,
            grid=(SEQ // block,),
            in_specs=[
                pl.BlockSpec((1, block, width), lambda i, m: (m[0], i, 0)),
                here(cols), here(cols), whole(width, cols), whole(width, cols), whole(1, width),
            ],
            out_specs=[here(width), here(width)],
        ),
        out_shape=[jax.ShapeDtypeStruct((SEQ, width), F32), jax.ShapeDtypeStruct((SEQ, width), BF)],
        compiler_params=pltpu.CompilerParams(vmem_limit_bytes=VMEM_LIMIT),
        cost_estimate=SMALL_COST,
        name="residual_and_norm",
    )(micro, layer_input, mixed, other, output_own, output_far, gain)


def picked_rows(first, second, segments):
    total = None
    start = 0
    for rows in segments:
        length = rows.shape[0]
        ids = lax.broadcasted_iota(jnp.int32, (1, length), 1) + start
        hot = jnp.where((first == ids) | (second == ids), 1.0, 0.0).astype(BF)
        total = put(total, dot(hot, rows))
        start += length
    return total


def put(a, b):
    return b if a is None else a + b


def folded(product):
    return jnp.sum(product.reshape(product.shape[0] // 8, 8, product.shape[1]), axis=0)


def as_column(eight):
    ones = jnp.ones((16, TILE), BF)
    high = eight.astype(BF)
    rest = (eight - high.astype(F32)).astype(BF)
    return dot(jnp.concatenate([high, rest], 0), ones, TN)


def combine_kernel(experts, half, spare, micro_ref, core_ref, length_ref, *refs):
    info_ref, grad_ref, residual_ref, mixed_ref, gain_ref, router_ref, output_ref = refs[:7]
    backs = refs[7:-9]
    (total_ref, mixed_grad_ref, extra_ref, far_ref, own_ref, acc_ref, router_acc, gain_acc, tables) = refs[-9:]
    block = residual_ref.shape[0]
    step = pl.program_id(0)
    count = len(backs) // 2

    @pl.when(step == 0)
    def _():
        place = lax.broadcasted_iota(jnp.int32, (experts, 1), 0)
        for n, back in enumerate((backs[count - 1], backs[2 * count - 1])):
            table = jnp.zeros((experts, back.shape[2]), F32)
            for e in range(experts):
                row = back[e, spare : spare + 16, :].astype(F32)[:1]
                table = jnp.where(place == e, row, table)
            tables[n] = table.astype(BF)

    info = jnp.transpose(info_ref[...])
    number = lambda n: info[:, n : n + 1]
    columns = lax.broadcasted_iota(jnp.int32, (1, half), 1)
    lanes = lax.broadcasted_iota(jnp.int32, (1, experts), 1)
    values = []
    for k in range(2):
        slot = number(4 + k)
        hot = jnp.where(columns == lax.rem(slot, half), 1.0, 0.0).astype(BF)
        found = []
        for table in (tables[0], tables[1]):
            found.append(sum(dot(hot, table[:, n * half : (n + 1) * half], NT) for n in range(3)))
        value = jnp.where(slot // half == core_ref[0], found[0], found[1])
        values.append(jnp.sum(jnp.where(lanes == number(2 + k), value, 0.0), axis=1, keepdims=True))
    wide = lax.broadcasted_iota(jnp.int32, (1, TILE), 1)
    is_first, is_second = wide == number(2), wide == number(3)
    residual = residual_ref[...]
    gain = gain_ref[...]
    inverse = lax.rsqrt(jnp.mean(residual * residual, axis=-1, keepdims=True) + 1e-06)
    plain = residual * inverse
    normed = (plain * gain).astype(BF)
    logits = dot(normed, router_ref[...])
    gap = jnp.sum(jnp.where(is_first, logits, 0.0) - jnp.where(is_second, logits, 0.0), axis=1, keepdims=True)
    small = jnp.exp(-jnp.abs(gap))
    logit = small / ((1.0 + small) * (1.0 + small)) * (values[0] - values[1])
    logit_grad = jnp.where(is_first, logit, jnp.where(is_second, -logit, 0.0)).astype(BF)
    segments = [b[...].reshape(b.shape[0] * b.shape[1], b.shape[2]) for b in backs]
    normed_grad = picked_rows(number(0), number(1), segments) + dot(logit_grad, router_ref[...], NT)
    scaled = normed_grad * gain
    mean = jnp.mean(scaled * plain, axis=-1, keepdims=True)
    place = lax.broadcasted_iota(jnp.int32, (block, 1), 0) + step * block
    grad_out = jnp.where(place < length_ref[0], grad_ref[0].astype(F32), 0.0)
    total = grad_out + inverse * (scaled - plain * mean)
    total_ref[...] = total
    branch = total.astype(BF)
    mixed_grad_ref[...] = dot(branch, output_ref[...]).astype(BF)
    router_part = dot(logit_grad, normed, TN)
    gain_part = folded(normed_grad * plain)
    output_part = dot(mixed_ref[...], branch, TN)

    @pl.when(step == 0)
    def _():
        router_acc[...] = router_part
        gain_acc[...] = gain_part
        acc_ref[...] = output_part

    @pl.when(step > 0)
    def _():
        router_acc[...] += router_part
        gain_acc[...] += gain_part
        acc_ref[...] += output_part

    @pl.when(step == pl.num_programs(0) - 1)
    def _():
        extra_ref[...] = jnp.transpose(router_acc[...]) + jnp.where(wide == experts + 1, as_column(gain_acc[...]), 0.0)
        parts = jnp.transpose(acc_ref[...])
        far_ref[...] = parts[:, TILE:].astype(BF)
        own_ref[:, :TILE] = parts[:, :TILE]
        own_ref[:, TILE:] = parts[:, 2 * TILE :]


def combine(micro, core, length, info, out_grad, residual, mixed, gain, router, output_own, backs, half, spare):
    width = residual.shape[1]
    block = 256
    cols = mixed.shape[1]
    whole = lambda arr: pl.BlockSpec(arr.shape, lambda i, *_: (0,) * arr.ndim)
    fixed = lambda rows, n: pl.BlockSpec((rows, n), lambda i, *_: (0, 0))
    here = lambda n: pl.BlockSpec((block, n), lambda i, *_: (i, 0))
    experts = backs[0].shape[0]
    return pl.pallas_call(
        functools.partial(combine_kernel, experts, half, spare),
        grid_spec=pltpu.PrefetchScalarGridSpec(
            num_scalar_prefetch=3,
            grid=(SEQ // block,),
            in_specs=[
                pl.BlockSpec((8, block), lambda i, *_: (0, i)),
                pl.BlockSpec((1, block, width), lambda i, m, *_: (m[0], i, 0)),
                here(width), here(cols), whole(gain), whole(router), whole(output_own),
            ]
            + [whole(x) for x in backs],
            out_specs=[here(width), here(cols), fixed(width, TILE), fixed(width, 2 * TILE), fixed(width, 2 * TILE)],
            scratch_shapes=[
                pltpu.VMEM((cols, width), F32),
                pltpu.VMEM((TILE, width), F32),
                pltpu.VMEM((8, width), F32),
                pltpu.VMEM((2, experts, width), BF),
            ],
        ),
        out_shape=[
            jax.ShapeDtypeStruct((SEQ, width), F32),
            jax.ShapeDtypeStruct((SEQ, cols), BF),
            jax.ShapeDtypeStruct((width, TILE), F32),
            jax.ShapeDtypeStruct((width, 2 * TILE), BF),
            jax.ShapeDtypeStruct((width, 2 * TILE), F32),
        ],
        compiler_params=pltpu.CompilerParams(vmem_limit_bytes=VMEM_LIMIT),
        cost_estimate=SMALL_COST,
        name="combine",
    )(micro, core, length, info, out_grad, residual, mixed, gain, router, output_own, *backs)


def output_kernel(core_ref, length_ref, info_ref, residual_ref, own_ref, far_ref, out_ref):
    block = residual_ref.shape[0]
    info = jnp.transpose(info_ref[...])
    place = lax.broadcasted_iota(jnp.int32, (block, 1), 0) + (core_ref[0] * 2 + pl.program_id(0)) * block
    rows = residual_ref[...] + picked_rows(info[:, 6:7], info[:, 7:8], (own_ref[...], far_ref[...]))
    out_ref[...] = jnp.where(place < length_ref[0], rows, 0.0).astype(BF)


def output_rows(core, length, info, residual, own, far):
    width = residual.shape[1]
    block = 256
    here = lambda n: pl.BlockSpec((block, n), lambda i, c, *_: (c[0] * 2 + i, 0))
    whole = lambda arr: pl.BlockSpec(arr.shape, lambda i, *_: (0, 0))
    return pl.pallas_call(
        output_kernel,
        grid_spec=pltpu.PrefetchScalarGridSpec(
            num_scalar_prefetch=2,
            grid=(2,),
            in_specs=[
                pl.BlockSpec((8, block), lambda i, c, *_: (0, c[0] * 2 + i)), here(width), whole(own), whole(far),
            ],
            out_specs=pl.BlockSpec((block, width), lambda i, *_: (i, 0)),
        ),
        out_shape=jax.ShapeDtypeStruct((2 * block, width), BF),
        compiler_params=pltpu.CompilerParams(vmem_limit_bytes=VMEM_LIMIT),
        cost_estimate=SMALL_COST,
        name="output_rows",
    )(core, length, info, residual, own, far)


def far_weight_kernel(normed_ref, q_ref, k_ref, v_ref, far_ref, own_ref):
    rows = normed_ref.shape[1]
    low = low_lanes((rows, TILE))
    q, k, v = (dot(normed_ref[...], d[...], TN) for d in (q_ref, k_ref, v_ref))
    for n, part in enumerate((q, k, v)):
        far_ref[:, n * TILE : (n + 1) * TILE] = part[:, :TILE].astype(BF)
    q, k, v = (part[:, TILE:] for part in (q, k, v))
    far_ref[:, 3 * TILE : 4 * TILE] = jnp.where(low, turned(q), k).astype(BF)
    far_ref[:, 4 * TILE :] = jnp.where(low, turned(v), 0.0).astype(BF)
    own_ref[:, :TILE] = jnp.where(low, q, turned(k))
    own_ref[:, TILE:] = jnp.where(low, v, 0.0)


def far_weight_grads(normed, q, k, v):
    width = normed.shape[1]
    block = 256
    whole = lambda arr: pl.BlockSpec(arr.shape, lambda i: (0, 0))
    here = lambda n: pl.BlockSpec((block, n), lambda i: (i, 0))
    return pl.pallas_call(
        far_weight_kernel,
        grid=(width // block,),
        in_specs=[pl.BlockSpec((SEQ, block), lambda i: (0, i)), whole(q), whole(k), whole(v)],
        out_specs=[here(5 * TILE), here(2 * TILE)],
        out_shape=[jax.ShapeDtypeStruct((width, 5 * TILE), BF), jax.ShapeDtypeStruct((width, 2 * TILE), F32)],
        compiler_params=pltpu.CompilerParams(vmem_limit_bytes=VMEM_LIMIT),
        cost_estimate=SMALL_COST,
        name="far_weight_grads",
    )(normed, q, k, v)


def own_weight_kernel(normed_ref, q_ref, k_ref, v_ref, own_ref):
    for n, d in enumerate((q_ref, k_ref, v_ref)):
        own_ref[:, n * TILE : (n + 1) * TILE] = dot(normed_ref[...], d[...], TN)


def own_weight_grads(normed, q, k, v):
    width = normed.shape[1]
    block = 256
    whole = lambda arr: pl.BlockSpec(arr.shape, lambda i: (0, 0))
    return pl.pallas_call(
        own_weight_kernel,
        grid=(width // block,),
        in_specs=[pl.BlockSpec((SEQ, block), lambda i: (0, i)), whole(q), whole(k), whole(v)],
        out_specs=pl.BlockSpec((block, 3 * TILE), lambda i: (i, 0)),
        out_shape=jax.ShapeDtypeStruct((width, 3 * TILE), F32),
        compiler_params=pltpu.CompilerParams(vmem_limit_bytes=VMEM_LIMIT),
        cost_estimate=SMALL_COST,
        name="own_weight_grads",
    )(normed, q, k, v)


def projected_back(weight_ref, first, last):
    total = None
    for n in range(3):
        base = 3 * n * TILE
        total = put(total, dot(first[n][...], weight_ref[:, base : base + TILE], NT))
        total = put(total, dot(last[n][...], weight_ref[:, base + TILE : base + 3 * TILE], NT))
    return total


def sent_kernel(core_ref, weight_ref, q0, k0, v0, q1, k1, v1, out_ref):
    out_ref[...] = projected_back(weight_ref, (q0, k0, v0), (q1, k1, v1))


def sent_half(core, weight, first, last):
    width = weight.shape[0]
    block = 256
    here = lambda n: pl.BlockSpec((block, n), lambda i, c: ((1 - c[0]) * 2 + i, 0))
    return pl.pallas_call(
        sent_kernel,
        grid_spec=pltpu.PrefetchScalarGridSpec(
            num_scalar_prefetch=1,
            grid=(2,),
            in_specs=[pl.BlockSpec(weight.shape, lambda i, c: (0, 0))] + [here(TILE)] * 3 + [here(2 * TILE)] * 3,
            out_specs=pl.BlockSpec((block, width), lambda i, c: (i, 0)),
        ),
        out_shape=jax.ShapeDtypeStruct((2 * block, width), F32),
        compiler_params=pltpu.CompilerParams(vmem_limit_bytes=VMEM_LIMIT),
        cost_estimate=SMALL_COST,
        name="sent_half",
    )(core, weight, *first, *last)


def input_kernel(
    lane, micro_ref, core_ref, weight_ref, q0, k0, v0, q1, k1, v1, got_ref, tokens_ref, gain_ref, grad_ref,
    out_ref, extra_ref, acc_ref,
):
    normed_grad = got_ref[...] + projected_back(weight_ref, (q0, k0, v0), (q1, k1, v1))
    x = tokens_ref[0].astype(F32)
    inverse = lax.rsqrt(jnp.mean(x * x, axis=-1, keepdims=True) + 1e-06)
    plain = x * inverse
    scaled = normed_grad * gain_ref[...]
    mean = jnp.mean(scaled * plain, axis=-1, keepdims=True)
    out_ref[...] = (grad_ref[...] + inverse * (scaled - plain * mean)).astype(BF)
    wide = lax.broadcasted_iota(jnp.int32, (1, TILE), 1)
    part = folded(normed_grad * plain)

    @pl.when(pl.program_id(0) == 0)
    def _():
        acc_ref[...] = part

    @pl.when(pl.program_id(0) == 1)
    def _():
        extra_ref[...] = jnp.where(wide == lane, as_column(acc_ref[...] + part), 0.0)


def input_half(lane, micro, core, weight, first, last, got, layer_input, gain, residual_grad):
    width = weight.shape[0]
    block = 256
    here = lambda n: pl.BlockSpec((block, n), lambda i, m, c: (c[0] * 2 + i, 0))
    plain = pl.BlockSpec((block, width), lambda i, *_: (i, 0))
    return pl.pallas_call(
        functools.partial(input_kernel, lane),
        grid_spec=pltpu.PrefetchScalarGridSpec(
            num_scalar_prefetch=2,
            grid=(2,),
            in_specs=[pl.BlockSpec(weight.shape, lambda i, *_: (0, 0))]
            + [here(TILE)] * 3
            + [here(2 * TILE)] * 3
            + [
                plain,
                pl.BlockSpec((1, block, width), lambda i, m, c: (m[0], c[0] * 2 + i, 0)),
                pl.BlockSpec(gain.shape, lambda i, *_: (0, 0)),
                here(width),
            ],
            out_specs=[plain, pl.BlockSpec((width, TILE), lambda i, *_: (0, 0))],
            scratch_shapes=[pltpu.VMEM((8, width), F32)],
        ),
        out_shape=[jax.ShapeDtypeStruct((2 * block, width), BF), jax.ShapeDtypeStruct((width, TILE), F32)],
        compiler_params=pltpu.CompilerParams(vmem_limit_bytes=VMEM_LIMIT),
        cost_estimate=SMALL_COST,
        name="input_half",
    )(micro, core, weight, *first, *last, got, layer_input, gain, residual_grad)


def sum_kernel(kept, own01, own2, got, out_own, out_got, early, late, table, sum_ref):
    low = low_lanes(early.shape)
    sum_ref[:, : 3 * TILE] = (own01[...] + got[:, : 3 * TILE].astype(F32)).astype(BF)
    sum_ref[:, 3 * TILE : 4 * TILE] = (own2[:, :TILE] + got[:, 3 * TILE : 4 * TILE].astype(F32)).astype(BF)
    values = own2[:, TILE:] + got[:, 4 * TILE :].astype(F32)
    outputs = turned(out_own[:, TILE:]) + out_got[:, TILE:].astype(F32)
    sum_ref[:, 4 * TILE : 5 * TILE] = jnp.where(low, values, outputs).astype(BF)
    sum_ref[:, 5 * TILE : 6 * TILE] = (out_own[:, :TILE] + out_got[:, :TILE].astype(F32)).astype(BF)
    extra = early[...] + late[...] + table[...]
    high = extra.astype(BF)
    rest = extra - high.astype(F32)
    if kept <= HEAD_DIM:
        sum_ref[:, 6 * TILE :] = jnp.where(low, high.astype(F32), turned(rest)).astype(BF)
    else:
        sum_ref[:, 6 * TILE : 7 * TILE] = high
        sum_ref[:, 7 * TILE :] = rest.astype(BF)


def packed_sums(kept, own01, own2, got, out_own, out_got, early, late, table):
    width = own01.shape[0]
    cols = (7 if kept <= HEAD_DIM else 8) * TILE
    block = 256
    here = lambda n: pl.BlockSpec((block, n), lambda i: (i, 0))
    parts = (own01, own2, got, out_own, out_got, early, late, table)
    return pl.pallas_call(
        functools.partial(sum_kernel, kept),
        grid=(width // block,),
        in_specs=[here(x.shape[1]) for x in parts],
        out_specs=here(cols),
        out_shape=jax.ShapeDtypeStruct((width, cols), BF),
        compiler_params=pltpu.CompilerParams(vmem_limit_bytes=VMEM_LIMIT),
        cost_estimate=SMALL_COST,
        name="packed_sums",
    )(*parts)


def pair_gate(logits, own, other):
    lanes = lax.broadcasted_iota(jnp.int32, logits.shape, 1)
    gap = jnp.sum(
        jnp.where(lanes == own, logits, 0.0) - jnp.where(lanes == other, logits, 0.0), axis=1, keepdims=True
    )
    small = jnp.exp(-jnp.abs(gap))
    return jnp.where(gap >= 0.0, 1.0, small) / (1.0 + small)


def expert_kernel(
    me_ref, partner_ref, rows_ref, grads_ref, router_ref, a0, a1, a2, a3, b0, b1, b2, b3,
    back_ref, active_ref, slope_ref, gated_ref, scalar_ref,
):
    rows = rows_ref[...]
    grads = grads_ref[...]
    gate = pair_gate(dot(rows, router_ref[...]), me_ref[0], partner_ref[...])
    gated_ref[...] = (gate * grads.astype(F32)).astype(BF)
    mass = None
    back = None
    step = 256
    for r, (first, second) in enumerate(((a0, b0), (a1, b1), (a2, b2), (a3, b3))):
        width = first.shape[1]
        for c in range(0, width, step):
            x = dot(rows, first[:, c : c + step])
            plain = dot(grads, second[c : c + step, :], NT)
            square = x * x
            bent = jnp.tanh(x * (GELU_C + (GELU_C * GELU_A) * square))
            rise = 0.5 + 0.5 * bent
            active = x * rise
            slope = rise + active * (1.0 - bent) * (GELU_C + (3.0 * GELU_C * GELU_A) * square)
            low = active.astype(BF)
            place = slice(r * width + c, r * width + c + step)
            active_ref[:, place] = low
            slope_ref[:, place] = (gate * plain * slope).astype(BF)
            part = low.astype(F32) * plain
            mass = put(mass, part[:, :TILE] + part[:, TILE:])
        back = put(back, dot(slope_ref[:, r * width : (r + 1) * width], first[...], NT))
    back_ref[...] = back.astype(BF)
    lanes = lax.broadcasted_iota(jnp.int32, (rows.shape[0], TILE), 1)
    scalar_ref[...] = jnp.where(lanes == 0, jnp.sum(mass, axis=1, keepdims=True), gate)


def row_block(total):
    return 320 if total % 320 == 0 else total


def expert_rows_pass(me, partner, rows, grads, router, firsts, seconds):
    total, width = rows.shape
    block = row_block(total)
    hidden = sum(f.shape[1] for f in firsts)
    here = lambda cols: pl.BlockSpec((block, cols), lambda i: (i, 0))
    whole = lambda arr: pl.BlockSpec(arr.shape, lambda i: (0, 0))
    return pl.pallas_call(
        expert_kernel,
        grid=(total // block,),
        in_specs=[pl.BlockSpec(memory_space=pltpu.SMEM), here(1), here(width), here(width), whole(router)]
        + [whole(w) for w in firsts]
        + [whole(w) for w in seconds],
        out_specs=[here(width), here(hidden), here(hidden), here(width), here(TILE)],
        out_shape=[
            jax.ShapeDtypeStruct((total, width), BF),
            jax.ShapeDtypeStruct((total, hidden), BF),
            jax.ShapeDtypeStruct((total, hidden), BF),
            jax.ShapeDtypeStruct((total, width), BF),
            jax.ShapeDtypeStruct((total, TILE), F32),
        ],
        compiler_params=pltpu.CompilerParams(vmem_limit_bytes=VMEM_LIMIT),
        cost_estimate=SMALL_COST,
        name="expert_rows",
    )(me, partner, rows, grads, router, *firsts, *seconds)


def result_kernel(chunks, *refs):
    active, scalars, seconds, out_ref = refs[:chunks], refs[chunks : 2 * chunks], refs[2 * chunks : -1], refs[-1]
    for c in range(chunks):

        @pl.when(pl.program_id(0) == c)
        def _(c=c):
            width = seconds[0].shape[0]
            total = None
            for r, second in enumerate(seconds):
                total = put(total, dot(active[c][:, r * width : (r + 1) * width], second[...]))
            rows = (total * scalars[c][:, 1:2]).astype(BF)
            if chunks > 1:
                out_ref[:, 0] = rows.reshape(out_ref.shape[0], out_ref.shape[2], out_ref.shape[3])
            else:
                out_ref[...] = rows


def expert_results(active, scalars, seconds, experts):
    chunks = len(active)
    total, hidden = active[0].shape
    width = seconds[0].shape[1]
    block = row_block(total)
    steps = total // block

    def here(c, cols):
        return pl.BlockSpec((block, cols), lambda g, i: (jnp.where(g == c, i, jnp.where(g < c, 0, steps - 1)), 0))

    chunk = total // experts
    if chunks > 1:
        shape = (experts, chunks, chunk, width)
        out_spec = pl.BlockSpec((block // chunk, 1, chunk, width), lambda g, i: (i, g, 0, 0))
    else:
        shape = (total, width)
        out_spec = pl.BlockSpec((block, width), lambda g, i: (i, 0))
    out = pl.pallas_call(
        functools.partial(result_kernel, chunks),
        grid=(chunks, steps),
        in_specs=[here(c, hidden) for c in range(chunks)]
        + [here(c, TILE) for c in range(chunks)]
        + [pl.BlockSpec(w.shape, lambda g, i: (0, 0)) for w in seconds],
        out_specs=out_spec,
        out_shape=jax.ShapeDtypeStruct(shape, BF),
        compiler_params=pltpu.CompilerParams(vmem_limit_bytes=VMEM_LIMIT),
        cost_estimate=SMALL_COST,
        name="expert_results",
    )(*active, *scalars, *seconds)
    return out.reshape(experts, chunks * chunk, width)


def weight_parts(count, refs):
    rows, slopes, active, gated = (refs[n * count : (n + 1) * count] for n in range(4))
    first, second = None, None
    for n in range(count):
        first = put(first, dot(rows[n][...], slopes[n][...], TN))
        second = put(second, dot(active[n][...], gated[n][...], TN))
    return first, second


def cross_kernel(count, *refs):
    first, second = weight_parts(count, refs)
    refs[-1][0, 0] = first.astype(BF)
    refs[-1][0, 1] = second.astype(BF)


def kept_kernel(count, *refs):
    got_ref, far_first, far_second, kept_ref = refs[-4:]
    first, second = weight_parts(count, refs)
    first = first + got_ref[0, 0].astype(F32)
    second = second + got_ref[0, 1].astype(F32)

    @pl.when(pl.program_id(0) == 0)
    def _():
        far_first[...] = first.astype(BF)
        far_second[...] = second.astype(BF)

    @pl.when(pl.program_id(0) == 1)
    def _():
        kept_ref[0] = first
        kept_ref[1] = second


def weight_specs(rows, slopes, quarter):
    total, width = rows[0].shape
    hidden = slopes[0].shape[1] // 4
    whole = pl.BlockSpec((total, width), lambda i: (0, 0))
    part = pl.BlockSpec((total, hidden), lambda i: (0, quarter(i)))
    count = len(rows)
    return width, hidden, [whole] * count + [part] * (2 * count) + [whole] * count


def cross_weight_grads(rows, slopes, active, gated):
    width, hidden, specs = weight_specs(rows, slopes, lambda i: 2 + i)
    return pl.pallas_call(
        functools.partial(cross_kernel, len(rows)),
        grid=(2,),
        in_specs=specs,
        out_specs=pl.BlockSpec((1, 2, width, hidden), lambda i: (i, 0, 0, 0)),
        out_shape=jax.ShapeDtypeStruct((2, 2, width, hidden), BF),
        compiler_params=pltpu.CompilerParams(vmem_limit_bytes=VMEM_LIMIT),
        cost_estimate=SMALL_COST,
        name="cross_weight_grads",
    )(*rows, *slopes, *active, *gated)


def kept_weight_grads(rows, slopes, active, gated, got):
    width, hidden, specs = weight_specs(rows, slopes, lambda i: 1 - i)
    fixed = pl.BlockSpec((width, hidden), lambda i: (0, 0))
    return pl.pallas_call(
        functools.partial(kept_kernel, len(rows)),
        grid=(2,),
        in_specs=specs + [pl.BlockSpec((1, 2, width, hidden), lambda i: (1 - i, 0, 0, 0))],
        out_specs=[fixed, fixed, pl.BlockSpec((2, width, hidden), lambda i: (0, 0, 0))],
        out_shape=[
            jax.ShapeDtypeStruct((width, hidden), BF),
            jax.ShapeDtypeStruct((hidden, width), BF),
            jax.ShapeDtypeStruct((2, width, hidden), F32),
        ],
        compiler_params=pltpu.CompilerParams(vmem_limit_bytes=VMEM_LIMIT),
        cost_estimate=SMALL_COST,
        name="kept_weight_grads",
    )(*rows, *slopes, *active, *gated, got)


def last_sum_kernel(kept_ref, first_ref, second_ref, out_first, out_second):
    out_first[...] = kept_ref[0] + first_ref[...].astype(F32)
    out_second[...] = kept_ref[1] + second_ref[...].astype(F32)


def last_sums(kept, first, second):
    width, hidden = first.shape
    block = 256
    here = pl.BlockSpec((block, hidden), lambda i: (i, 0))
    return pl.pallas_call(
        last_sum_kernel,
        grid=(width // block,),
        in_specs=[pl.BlockSpec((2, block, hidden), lambda i: (0, i, 0)), here, here],
        out_specs=[here, here],
        out_shape=[jax.ShapeDtypeStruct((width, hidden), F32)] * 2,
        compiler_params=pltpu.CompilerParams(vmem_limit_bytes=VMEM_LIMIT),
        cost_estimate=SMALL_COST,
        name="last_sums",
    )(kept, first, second)


def send_kernel(micro_ref, code_ref, rows_ref, out_ref):
    block = out_ref.shape[0]
    ids = lax.broadcasted_iota(jnp.int32, (block, 1), 0) + pl.program_id(0) * block
    hot = jnp.where((ids == code_ref[:1]) | (ids == code_ref[1:2]), 1.0, 0.0).astype(BF)
    out_ref[...] = dot(hot, rows_ref[0]).astype(BF)


def send_rows(micro, code, rows, count):
    width = rows.shape[2]
    block = next(b for b in (336, 320, 384, count) if count % b == 0)
    return pl.pallas_call(
        send_kernel,
        grid_spec=pltpu.PrefetchScalarGridSpec(
            num_scalar_prefetch=1,
            grid=(count // block,),
            in_specs=[
                pl.BlockSpec(code.shape, lambda i, m: (0, 0)),
                pl.BlockSpec((1, SEQ, width), lambda i, m: (m[0], 0, 0)),
            ],
            out_specs=pl.BlockSpec((block, width), lambda i, m: (i, 0)),
        ),
        out_shape=jax.ShapeDtypeStruct((count, width), BF),
        compiler_params=pltpu.CompilerParams(vmem_limit_bytes=VMEM_LIMIT),
        cost_estimate=SMALL_COST,
        name="send_rows",
    )(micro, code, rows)


def place_kernel(place_ref, a_ref, b_ref, c_ref, d_ref, out_ref):
    for n, piece in enumerate((a_ref, b_ref, c_ref, d_ref)):

        @pl.when(pl.program_id(0) == n)
        def _(piece=piece):
            out_ref[0] = piece[...]


def place_pieces(places, pieces):
    shape = pieces[0].shape
    whole = pl.BlockSpec(shape, lambda i, place_ref: (0, 0))
    return pl.pallas_call(
        place_kernel,
        grid_spec=pltpu.PrefetchScalarGridSpec(
            num_scalar_prefetch=1,
            grid=(4,),
            in_specs=[whole] * 4,
            out_specs=pl.BlockSpec((1,) + shape, lambda i, place_ref: (place_ref[i], 0, 0)),
        ),
        out_shape=jax.ShapeDtypeStruct((4,) + shape, pieces[0].dtype),
        compiler_params=pltpu.CompilerParams(vmem_limit_bytes=VMEM_LIMIT),
        cost_estimate=SMALL_COST,
        name="place_pieces",
    )(places, *pieces)


def swap(value, axis, count, bit):
    return lax.ppermute(value, axis, [(i, i ^ bit) for i in range(count)])


def all_to_all(value):
    return lax.all_to_all(value, "dp", split_axis=0, concat_axis=0, tiled=True)


def together(*values):
    return lax.optimization_barrier(values)


def local(
    layer_input, out_grad, first_gain, query_weight, key_weight, value_weight, output_weight,
    position_bias, second_gain, router_weight, expert_in, expert_out, seq_lengths, routes,
):
    micro_count, tok_rows, width = layer_input.shape
    dp_count = lax.axis_size("dp")
    expert_count = router_weight.shape[1]
    shard = query_weight.shape[1]
    heads_here = position_bias.shape[0]
    assert lax.axis_size("tensor") == 4 and micro_count == 2 and expert_count == dp_count
    assert tok_rows == SEQ and seq_lengths.shape[1] == 1
    capacity = max(8, 8 * (10 * tok_rows // (32 * expert_count)))
    half = capacity // 2
    stride = 8 * (half // 8 + 1)
    chunks = 2 if half % 32 == 0 else 1
    chunk = half // chunks
    chunk_rows = expert_count * chunk
    rows_here = query_weight.shape[0]
    me = lax.axis_index("dp")
    rank = lax.axis_index("tensor")
    micro = rank // 2
    core = rank % 2

    def swap_y(value):
        return swap(value, "tensor", 4, 2)

    def swap_core(value):
        return swap(value, "tensor", 4, 1)

    micro_arg = micro.reshape(1).astype(jnp.int32)
    core_arg = core.reshape(1).astype(jnp.int32)

    packed = pack_weights(query_weight, key_weight, value_weight, output_weight, first_gain, second_gain, router_weight)
    three = 3 * TILE

    def doubled(stacked, bit, axis=0):
        other = swap(stacked, "dp", dp_count, bit)
        high = (me & bit) != 0
        pair = jnp.where(high, jnp.stack([other, stacked], axis + 1), jnp.stack([stacked, other], axis + 1))
        return pair.reshape(stacked.shape[:axis] + (-1,) + stacked.shape[axis + 1 :])

    stacked = packed[None]
    bit = dp_count // 2
    while bit > 1:
        stacked = doubled(stacked, bit)
        if bit == dp_count // 2:
            stacked, routes, position_bias = together(stacked, routes, position_bias)
        bit //= 2
    first_own = expert_in[0]
    second_own = expert_out[0]
    first_y = swap_y(first_own)
    part_b = stacked[:, :, :three]
    part_a = doubled(stacked[:, :, three:], 1)
    part_a, first_y = together(part_a, first_y)
    pair_b = jnp.stack([part_b, swap_y(part_b)])
    a_own = part_a[:, :, :three]
    a_far = swap_y(a_own).reshape(width, three)
    a_own = a_own.reshape(width, three)
    pair_b = doubled(pair_b, 1, 1).reshape(2, width, three)
    small_all = part_a[:, :, three:].reshape(width, TILE)
    gain_one = small_all[:, expert_count].astype(F32)[None]
    gain_two = small_all[:, expert_count + 1].astype(F32)[None]
    router_wide = small_all
    far_bias = swap_y(position_bias)
    bias = jnp.concatenate([position_bias[:2], far_bias[:2], position_bias[2:], far_bias[2:]], 0)
    head_total = bias.shape[0]
    hot_const = jnp.asarray(NEAR_HOT, dtype=BF)
    near = dot(bias, hot_const) - bias[:, NB - 1 :].astype(F32)
    near = near.reshape(head_total, 2, TILE, TILE)
    places = jnp.arange(TILE, dtype=jnp.int32)
    causal = jnp.stack([places[None, :] <= places[:, None], jnp.ones((TILE, TILE), bool)])
    near = jnp.where(causal[None], near, NEG)

    length = lax.dynamic_index_in_dim(seq_lengths, micro, 0, keepdims=False)
    route = lax.dynamic_index_in_dim(routes, micro, 0, keepdims=False).T
    expert_ids = jnp.arange(expert_count, dtype=jnp.int32)
    named = (expert_ids[:, None, None] == route[None]).astype(jnp.int32)
    per_token = jnp.sum(named, axis=1, dtype=jnp.int32)
    earlier = jnp.cumsum(per_token, axis=1, dtype=jnp.int32) - per_token
    slot = jnp.sum(named * earlier[:, None, :], axis=0, dtype=jnp.int32)
    here = slot // half == core
    within = slot % half
    chunk_of = within // chunk
    inside = within % chunk
    spare = 16 * -(-chunk // 16)
    last_stride = spare + 16
    last = (chunks - 1) * chunk_rows
    code_back = jnp.where(
        chunk_of == chunks - 1, last + route * last_stride + inside, chunk_of * chunk_rows + route * chunk + inside
    )
    code_back = code_back + jnp.where(here, 0, last + expert_count * last_stride)
    code_result = route * half + within + jnp.where(here, 0, expert_count * half)
    info = jnp.concatenate([code_back, route, slot, code_result], 0)

    valid = jnp.arange(SEQ, dtype=jnp.int32) < length[0]
    code_grads = jnp.where(here, route * stride + within, -1)
    ids = jnp.arange(expert_count * stride, dtype=jnp.int32)[:, None]
    partner = jnp.sum(
        jnp.where(ids == code_grads[:1], route[1:], 0) + jnp.where(ids == code_grads[1:], route[:1], 0), axis=1, dtype=jnp.int32
    )
    grads_sent = send_rows(micro_arg, jnp.where(valid[None], code_grads, -1), out_grad, expert_count * stride)
    grads_sent = grads_sent.reshape(expert_count, stride, width)
    partner_row = jnp.pad(partner.reshape(expert_count, stride)[:, :half].astype(BF), ((0, 0), (0, width - half)))
    grads_sent = grads_sent.at[:, half].set(partner_row)
    grads_sent, a_own, pair_b = together(grads_sent, a_own, pair_b)
    grads_here = all_to_all(grads_sent)

    qkv, normed_one, qkv_weight, output_own = norm_and_project(
        micro_arg, layer_input, gain_one, a_own, a_far, pair_b[0], pair_b[1]
    )
    second_late, qkv = together(second_own, qkv)
    second_y = swap_y(second_late)
    output_far = swap_core(output_own)
    mixed, logs = attend(length, qkv, near)
    mixed, output_far = together(mixed, output_far)
    mixed_far = swap_core(mixed)
    residual, normed_two = residual_and_norm(micro_arg, layer_input, mixed, mixed_far, output_own, output_far, gain_two)
    normed_two, grads_here, second_y = together(normed_two, grads_here, second_y)

    arrived = []
    zero = jnp.zeros((1,), jnp.int32)
    for c in range(chunks):
        code_chunk = jnp.where(here & (chunk_of == c), route * chunk + inside, -1)
        sent = send_rows(zero, code_chunk, normed_two[None], chunk_rows).reshape(expert_count, chunk, width)
        if arrived:
            sent, arrived[-1] = together(sent, arrived[-1])
        arrived.append(all_to_all(sent))

    firsts = (first_own, first_y, swap_core(first_own), swap_core(first_y))
    seconds = (second_own, second_y, swap_core(second_own), swap_core(second_y))

    partner_here = grads_here[:, half, :half].astype(jnp.int32)

    def chunk_grads(c):
        at = slice(c * chunk, (c + 1) * chunk)
        return grads_here[:, at].reshape(chunk_rows, width), partner_here[:, at].reshape(chunk_rows, 1)

    me_arg = me.reshape(1).astype(jnp.int32)
    rows_all, slopes, active, gated, scalars, backs = [], [], [], [], [], []
    for c in range(chunks):
        grads_c, partner_c = chunk_grads(c)
        rows_c = arrived[c].reshape(chunk_rows, width)
        back, act, slo, gat, sca = expert_rows_pass(me_arg, partner_c, rows_c, grads_c, router_wide, firsts, seconds)
        rows_all.append(rows_c)
        slopes.append(slo)
        active.append(act)
        gated.append(gat)
        scalars.append(sca)
        back = back.reshape(expert_count, chunk, width)
        if c == chunks - 1:
            gate_grad = jnp.concatenate([x[:, 0].reshape(expert_count, chunk) for x in scalars], 1)
            pieces = []
            for _ in range(3):
                piece = gate_grad.astype(BF)
                pieces.append(piece)
                gate_grad = gate_grad - piece.astype(F32)
            gate_row = jnp.pad(jnp.concatenate(pieces, 1), ((0, 0), (0, width - 3 * half)))
            back = jnp.pad(back, ((0, 0), (0, last_stride - chunk), (0, 0)))
            back = back.at[:, spare].set(gate_row)
            back, rows_all[-1] = together(back, rows_all[-1])
        backs.append(all_to_all(back))
    grads_in = swap_core(cross_weight_grads(rows_all, slopes, active, gated))
    results = expert_results(active, scalars, seconds, expert_count)
    results, grads_in = together(results, grads_in)
    first_sent, second_sent, grads_kept = kept_weight_grads(rows_all, slopes, active, gated, grads_in)

    first_got = swap_y(first_sent)
    backs[-1], results, first_got = together(backs[-1], results, first_got)
    second_sent, first_got = together(second_sent, first_got)
    second_got = swap_y(second_sent)
    results_own = all_to_all(results).reshape(expert_count * half, width)

    backs_far = [swap_core(b) for b in backs]
    residual_grad, mixed_grad, extra_early, output_sent, output_kept = combine(
        micro_arg, core_arg, length, info, out_grad, residual, mixed, gain_two, router_wide, output_own,
        backs + backs_far, half, spare,
    )
    output_got = swap_y(output_sent)

    q1, k1, v1, tiles1, sums1 = attend_back(length, qkv, near, mixed, logs, mixed_grad, 1, 2)
    q1, second_got, output_got = together(q1, second_got, output_got)
    far_sent, own_last = far_weight_grads(normed_one, q1, k1, v1)
    mixed_grad, far_sent = together(mixed_grad, far_sent)
    far_got = swap_y(far_sent)
    q0, k0, v0, tiles0, sums0 = attend_back(length, qkv, near, mixed, logs, mixed_grad, 0, 1)
    first, last = (q0, k0, v0), (q1, k1, v1)
    sent = sent_half(core_arg, qkv_weight, first, last)
    sent, residual, results_own = together(sent, residual, results_own)
    got = swap_core(sent)
    layer_rows = output_rows(core_arg, length, info, residual, results_own, swap_core(results_own))
    got, layer_rows = together(got, layer_rows)
    corner = micro * 2 + core
    corners = jnp.stack([corner, corner ^ 1, corner ^ 2, corner ^ 3]).astype(jnp.int32)

    def placed(own):
        across = swap_y(own)
        return place_pieces(corners, (own, swap_core(own), across, swap_core(across))).reshape(2, SEQ, width)

    input_rows, extra_late = input_half(
        expert_count, micro_arg, core_arg, qkv_weight, first, last, got, layer_input, gain_one, residual_grad
    )
    input_rows, normed_one, far_got = together(input_rows, normed_one, far_got)
    own_pair = own_weight_grads(normed_one, q0, k0, v0)
    input_grad = placed(input_rows)
    layer_output = placed(layer_rows)
    expert_in_grad, expert_out_grad = last_sums(grads_kept, first_got, second_got)

    tiles = jnp.concatenate([tiles0, tiles1], 0).reshape(head_total, 2 * TILE * TILE)
    sums = jnp.concatenate([sums0, sums1], 0)
    tiles_high = tiles.astype(BF)
    tiles_rest = (tiles - tiles_high.astype(F32)).astype(BF)
    table = dot(tiles_high, hot_const, NT) + dot(tiles_rest, hot_const, NT)
    far_sum = jnp.sum(sums[:, :, 0], axis=1) - jnp.sum(table[:, : NB - 1], axis=1)
    table = jnp.concatenate([table[:, : NB - 1], far_sum[:, None]], 1)
    table_own = jnp.concatenate([table[0:2], table[4:5]], 0)
    table_far = jnp.concatenate([table[2:4], table[5:6]], 0)
    table_cols = heads_here * NB // rows_here
    table_both = jnp.concatenate([table_own.reshape(rows_here, table_cols), table_far.reshape(rows_here, table_cols)], 1)
    base = expert_count + 2
    kept = base + 2 * table_cols
    table_tile = jnp.tile(jnp.pad(table_both, ((0, 0), (base, TILE - kept))), (dp_count, 1))

    grads = packed_sums(kept, own_pair, own_last, far_got, output_kept, output_got, extra_early, extra_late, table_tile)
    arrived_grads = all_to_all(grads.reshape(dp_count, rows_here, grads.shape[1]))
    total = jnp.sum(arrived_grads.astype(F32), axis=0)
    wide = HEAD_DIM if kept <= HEAD_DIM else TILE
    small = total[:, 6 * TILE : 6 * TILE + kept] + total[:, 6 * TILE + wide : 6 * TILE + wide + kept]
    small_y = swap_y(small)
    gain_one_half = small[:, expert_count] + small_y[:, expert_count]
    column = lambda t: total[:, t * TILE : (t + 1) * TILE]
    pair_of = lambda t, last_tile, high: jnp.concatenate(
        [column(t), column(last_tile)[:, HEAD_DIM:] if high else column(last_tile)[:, :HEAD_DIM]], 1
    )
    return (
        layer_output,
        input_grad,
        gain_one_half + swap_core(gain_one_half),
        pair_of(0, 3, False),
        pair_of(1, 3, True),
        pair_of(2, 4, False),
        pair_of(5, 4, True).T,
        (small[:, base : base + table_cols] + small_y[:, base + table_cols :]).reshape(heads_here, NB),
        small[:, expert_count + 1] + small_y[:, expert_count + 1],
        small[:, :expert_count] + small_y[:, :expert_count],
        expert_in_grad[None],
        expert_out_grad[None],
    )


def solution(mesh):
    return jax.shard_map(
        local,
        mesh=mesh,
        in_specs=(
            P(None, "dp", None),
            P(None, "dp", None),
            P("dp"),
            P("dp", "tensor"),
            P("dp", "tensor"),
            P("dp", "tensor"),
            P("tensor", "dp"),
            P("tensor", None),
            P("dp"),
            P("dp", None),
            P("dp", None, "tensor"),
            P("dp", "tensor", None),
            P(None, "dp"),
            P(None, "dp", None),
        ),
        out_specs=(
            P(None, "dp", None),
            P(None, "dp", None),
            P("dp"),
            P("dp", "tensor"),
            P("dp", "tensor"),
            P("dp", "tensor"),
            P("tensor", "dp"),
            P("tensor", None),
            P("dp"),
            P("dp", None),
            P("dp", None, "tensor"),
            P("dp", "tensor", None),
        ),
        check_vma=False,
    )
```

```python
import functools

import jax
import jax.numpy as jnp
import numpy as np
from jax import lax
from jax.experimental import pallas as pl
from jax.experimental.pallas import tpu as pltpu
from jax.sharding import PartitionSpec as P

HEAD_DIM = 64
NB = 32
SEQ = 1024
TILE = 128
QROWS = 256
NEG = -1e30
GELU_C = 0.7978845608028654
GELU_A = 0.044715

BF = jnp.bfloat16
F32 = jnp.float32

bucket_edges = np.ceil(16.0 * 8.0 ** (np.arange(1, 16) / 16.0)).astype(np.int32)


def near_tables():
    rows = np.arange(TILE)[:, None]
    cols = np.arange(TILE)[None, :]
    hots = []
    for shift in (0, TILE):
        distance = rows - cols + shift
        clipped = np.maximum(distance, 0)
        reached = np.sum(clipped[..., None] >= bucket_edges, axis=-1)
        bucket = np.minimum(clipped, 16) + reached
        hots.append(bucket[..., None] == np.arange(NB))
    hot = np.stack(hots).reshape(2 * TILE * TILE, NB).T
    return hot


NEAR_HOT = near_tables()
assert bucket_edges[-1] <= TILE


def dot(a, b, dims=((1,), (0,))):
    return lax.dot_general(a, b, (dims, ((), ())), preferred_element_type=F32)


NT = ((1,), (1,))
TN = ((0,), (0,))


MIB = 2**20
SMALL_COST = pl.CostEstimate(flops=1_000_000, bytes_accessed=1_000_000, transcendentals=0)


def score_tiles(block, half, q_half, key_ref, near_one, near_two, length):
    tiles = []
    for j in range(block + 1):
        s = dot(q_half, key_ref[j * QROWS : (j + 1) * QROWS, :], NT)
        if j == block:
            top = jnp.concatenate([s[:TILE, :TILE] + near_one, jnp.full((TILE, TILE), NEG, F32)], 1)
            low = jnp.concatenate([s[TILE:, :TILE] + near_two, s[TILE:, TILE:] + near_one], 1)
            s = jnp.concatenate([top, low], 0)
        elif j == block - 1:
            top = jnp.concatenate([s[:TILE, :TILE], s[:TILE, TILE:] + near_two], 1)
            s = jnp.concatenate([top, s[TILE:]], 0)
        if (j + 1) * QROWS > SEQ // 2:
            place = lax.broadcasted_iota(jnp.int32, (1, QROWS), 1) + j * QROWS
            s = s + jnp.where(place < length, 0.0, NEG)
        tiles.append(s)
    return tiles


def lane_half(rows):
    return lax.broadcasted_iota(jnp.int32, (rows, 2 * HEAD_DIM), 1) < HEAD_DIM


def attend_kernel(length_ref, query_ref, key_ref, value_ref, near_ref, out_ref, log_ref):
    length = length_ref[0]
    lanes = lane_half(QROWS)
    ones = jnp.ones((SEQ, TILE), BF)
    value_ext = jnp.concatenate([value_ref[...], ones], 1)
    for i in range(SEQ // QROWS):
        q_rows = query_ref[i * QROWS : (i + 1) * QROWS, :] * BF(0.125)
        outs, logs = [], []
        for h in range(2):
            keep = lanes if h == 0 else ~lanes
            q_half = jnp.where(keep, q_rows, BF(0))
            tiles = score_tiles(i, h, q_half, key_ref, near_ref[h, 0], near_ref[h, 1], length)
            top = tiles[0]
            for s in tiles[1:]:
                top = jnp.maximum(top, s)
            top = jnp.max(top, axis=1, keepdims=True)
            total = None
            for j, s in enumerate(tiles):
                p = jnp.exp(s - top).astype(BF)
                part = dot(p, value_ext[j * QROWS : (j + 1) * QROWS, :])
                total = part if total is None else total + part
            row_sum = total[:, TILE:]
            outs.append(total[:, :TILE] / row_sum)
            logs.append(top + jnp.log(row_sum))
        out_ref[i * QROWS : (i + 1) * QROWS, :] = jnp.where(lanes, outs[0], outs[1]).astype(BF)
        log_ref[i * QROWS : (i + 1) * QROWS, :] = jnp.where(lanes, logs[0], logs[1])


def attend(length, qkv, near):
    pairs = qkv.shape[1] // (3 * TILE)
    cols = pairs * TILE
    return pl.pallas_call(
        attend_kernel,
        grid=(pairs,),
        in_specs=[
            pl.BlockSpec(memory_space=pltpu.SMEM),
            pl.BlockSpec((SEQ, TILE), lambda p: (0, p)),
            pl.BlockSpec((SEQ, TILE), lambda p: (0, pairs + p)),
            pl.BlockSpec((SEQ, TILE), lambda p: (0, 2 * pairs + p)),
            pl.BlockSpec((2, 2, TILE, TILE), lambda p: (p, 0, 0, 0)),
        ],
        out_specs=[
            pl.BlockSpec((SEQ, TILE), lambda p: (0, p)),
            pl.BlockSpec((SEQ, TILE), lambda p: (0, p)),
        ],
        out_shape=[
            jax.ShapeDtypeStruct((SEQ, cols), BF),
            jax.ShapeDtypeStruct((SEQ, cols), F32),
        ],
        compiler_params=pltpu.CompilerParams(vmem_limit_bytes=24 * MIB),
        cost_estimate=SMALL_COST,
        name="attend",
    )(length, qkv, qkv, qkv, near)


def attend_back_kernel(
    length_ref, query_ref, key_ref, value_ref, near_ref, out_ref, log_ref, grad_ref,
    dq_ref, dk_ref, dv_ref, tile_ref, sum_ref, dk_acc, dv_acc,
):
    length = length_ref[0]
    lanes = lane_half(QROWS)
    lanes_all = lane_half(SEQ)
    ones = jnp.ones((SEQ, TILE), BF)
    key_ext = [
        jnp.concatenate([jnp.where(lanes_all, key_ref[...], BF(0)), ones], 1),
        jnp.concatenate([jnp.where(lanes_all, BF(0), key_ref[...]), ones], 1),
    ]
    near_sums = [[None, None], [None, None]]
    all_sums = [None, None]

    for i in range(SEQ // QROWS):
        rows = slice(i * QROWS, (i + 1) * QROWS)
        q_rows = query_ref[rows, :] * BF(0.125)
        g_rows = grad_ref[rows, :]
        mass = g_rows.astype(F32) * out_ref[rows, :].astype(F32)
        dq = None
        for h in range(2):
            keep = lanes if h == 0 else ~lanes
            q_half = jnp.where(keep, q_rows, BF(0))
            g_half = jnp.where(keep, g_rows, BF(0))
            delta = jnp.sum(jnp.where(keep, mass, 0.0), axis=1, keepdims=True)
            log_col = log_ref[rows, h * HEAD_DIM : h * HEAD_DIM + 1]
            tiles = score_tiles(i, h, q_half, key_ref, near_ref[h, 0], near_ref[h, 1], length)
            for j, s in enumerate(tiles):
                keys = slice(j * QROWS, (j + 1) * QROWS)
                p = jnp.exp(s - log_col)
                dp = dot(g_half, value_ref[keys, :], NT)
                ds = (p * (dp - delta)).astype(BF)
                part = dot(ds, key_ext[h][keys, :])
                dq = put(dq, part[:, :TILE])
                all_sums[h] = put(all_sums[h], jnp.sum(part[:, TILE:].reshape(QROWS // 8, 8, TILE), axis=0))
                dk_part = dot(ds, q_half, TN)
                dv_part = dot(p.astype(BF), g_half, TN)
                if i == j and h == 0:
                    dk_acc[keys, :] = dk_part
                    dv_acc[keys, :] = dv_part
                else:
                    dk_acc[keys, :] += dk_part
                    dv_acc[keys, :] += dv_part
                if j == i:
                    wide = ds.astype(F32)
                    near_sums[h][0] = put(near_sums[h][0], wide[:TILE, :TILE] + wide[TILE:, TILE:])
                    near_sums[h][1] = put(near_sums[h][1], wide[TILE:, :TILE])
                elif j == i - 1:
                    near_sums[h][1] = put(near_sums[h][1], ds[:TILE, TILE:].astype(F32))
        dq_ref[rows, :] = (dq * 0.125).astype(BF)
    dk_ref[...] = dk_acc[...].astype(BF)
    dv_ref[...] = dv_acc[...].astype(BF)
    for h in range(2):
        tile_ref[h, 0] = near_sums[h][0]
        tile_ref[h, 1] = near_sums[h][1]
        sum_ref[h] = all_sums[h]


def attend_back(length, qkv, near, mixed, logs, grad, first, count):
    pairs = qkv.shape[1] // (3 * TILE)
    cols = count * TILE
    col = pl.BlockSpec((SEQ, TILE), lambda p: (0, first + p))
    out = pl.BlockSpec((SEQ, TILE), lambda p: (0, p))
    return pl.pallas_call(
        attend_back_kernel,
        grid=(count,),
        in_specs=[
            pl.BlockSpec(memory_space=pltpu.SMEM),
            col,
            pl.BlockSpec((SEQ, TILE), lambda p: (0, pairs + first + p)),
            pl.BlockSpec((SEQ, TILE), lambda p: (0, 2 * pairs + first + p)),
            pl.BlockSpec((2, 2, TILE, TILE), lambda p: (first + p, 0, 0, 0)),
            col,
            col,
            col,
        ],
        out_specs=[
            out,
            out,
            out,
            pl.BlockSpec((2, 2, TILE, TILE), lambda p: (p, 0, 0, 0)),
            pl.BlockSpec((2, 8, TILE), lambda p: (p, 0, 0)),
        ],
        out_shape=[
            jax.ShapeDtypeStruct((SEQ, cols), BF),
            jax.ShapeDtypeStruct((SEQ, cols), BF),
            jax.ShapeDtypeStruct((SEQ, cols), BF),
            jax.ShapeDtypeStruct((2 * count, 2, TILE, TILE), F32),
            jax.ShapeDtypeStruct((2 * count, 8, TILE), F32),
        ],
        scratch_shapes=[pltpu.VMEM((SEQ, TILE), F32), pltpu.VMEM((SEQ, TILE), F32)],
        compiler_params=pltpu.CompilerParams(vmem_limit_bytes=24 * MIB),
        cost_estimate=SMALL_COST,
        name="attend_back",
    )(length, qkv, qkv, qkv, near, mixed, logs, grad)


def low_lanes(shape):
    return lax.broadcasted_iota(jnp.int32, shape, 1) < HEAD_DIM


def turned(tile):
    return pltpu.roll(tile, HEAD_DIM, 1)


def pack_kernel(q_ref, k_ref, v_ref, o_ref, one_ref, two_ref, router_ref, out_ref):
    shard = q_ref.shape[1]
    rows = q_ref.shape[0]
    source = lax.broadcasted_iota(jnp.int32, (shard, 6 * TILE), 0)
    target = lax.broadcasted_iota(jnp.int32, (shard, 6 * TILE), 1)

    def moved(pair_base, last_base):
        want = jnp.where(source < TILE, source + pair_base, source - TILE + last_base)
        return jnp.where(target == want, 1.0, 0.0).astype(BF)

    total = dot(v_ref[...], moved(0, 2 * TILE)) + dot(o_ref[...], moved(TILE, 2 * TILE + HEAD_DIM), TN)
    total = total + dot(q_ref[...], moved(3 * TILE, 5 * TILE)) + dot(k_ref[...], moved(4 * TILE, 5 * TILE + HEAD_DIM))
    out_ref[:, : 6 * TILE] = total.astype(BF)
    experts = router_ref.shape[0]
    own_row = lax.broadcasted_iota(jnp.int32, (rows, rows), 0) == lax.broadcasted_iota(jnp.int32, (rows, rows), 1)

    def column(ref):
        return jnp.sum(jnp.where(own_row, ref[...].astype(F32), 0.0), axis=1, keepdims=True)

    lanes = lax.broadcasted_iota(jnp.int32, (experts, TILE), 1)
    spread = jnp.where(lanes == lax.broadcasted_iota(jnp.int32, (experts, TILE), 0), 1.0, 0.0).astype(BF)
    place = lax.broadcasted_iota(jnp.int32, (rows, TILE), 1)
    small = dot(router_ref[...], spread, TN)
    small = jnp.where(place == experts, column(one_ref), jnp.where(place == experts + 1, column(two_ref), small))
    out_ref[:, 6 * TILE :] = small.astype(BF)


def pack_weights(query, key, value, output, one, two, router):
    rows = query.shape[0]
    return pl.pallas_call(
        pack_kernel,
        out_shape=jax.ShapeDtypeStruct((rows, 7 * TILE), BF),
        compiler_params=pltpu.CompilerParams(vmem_limit_bytes=16 * MIB),
        cost_estimate=SMALL_COST,
        name="pack_weights",
    )(query, key, value, output, one[None], two[None], router.T)


def qkv_kernel(micro_ref, tokens_ref, gain_ref, a_own, a_far, b_own, b_far, qkv_ref, normed_ref, weight_ref, output_ref):
    width = tokens_ref.shape[2]

    @pl.when(pl.program_id(0) == 0)
    def _():
        low = low_lanes((width, TILE))

        def tiles(own, far, pair, low_half):
            at = slice(pair * TILE, (pair + 1) * TILE)
            one, two = own[:, 2 * TILE :].astype(F32), far[:, 2 * TILE :].astype(F32)
            last = jnp.where(low, one, turned(two)) if low_half else jnp.where(low, turned(one), two)
            return own[:, at], far[:, at], last.astype(BF)

        for n, (own, far, pair, low_half) in enumerate(
            ((a_own, a_far, 0, True), (a_own, a_far, 1, False), (b_own, b_far, 0, True))
        ):
            for t, tile in enumerate(tiles(own[...], far[...], pair, low_half)):
                at = 3 * n + t
                weight_ref[:, at * TILE : (at + 1) * TILE] = tile
        for t, tile in enumerate(tiles(b_own[...], b_far[...], 1, False)):
            output_ref[:, t * TILE : (t + 1) * TILE] = tile

    x = tokens_ref[0].astype(F32)
    inverse = lax.rsqrt(jnp.mean(x * x, axis=-1, keepdims=True) + 1e-06)
    normed = (x * inverse * gain_ref[...]).astype(BF)
    normed_ref[...] = normed
    qkv_ref[...] = dot(normed, weight_ref[...]).astype(BF)


def norm_and_project(micro, layer_input, gain, a_own, a_far, b_own, b_far):
    width = layer_input.shape[2]
    block = 256
    cols = 3 * TILE
    whole = lambda rows, n: pl.BlockSpec((rows, n), lambda i, m: (0, 0))
    here = lambda n: pl.BlockSpec((block, n), lambda i, m: (i, 0))
    return pl.pallas_call(
        qkv_kernel,
        grid_spec=pltpu.PrefetchScalarGridSpec(
            num_scalar_prefetch=1,
            grid=(SEQ // block,),
            in_specs=[pl.BlockSpec((1, block, width), lambda i, m: (m[0], i, 0)), whole(1, width)] + [whole(width, cols)] * 4,
            out_specs=[here(3 * cols), here(width), whole(width, 3 * cols), whole(width, cols)],
        ),
        out_shape=[
            jax.ShapeDtypeStruct((SEQ, 3 * cols), BF),
            jax.ShapeDtypeStruct((SEQ, width), BF),
            jax.ShapeDtypeStruct((width, 3 * cols), BF),
            jax.ShapeDtypeStruct((width, cols), BF),
        ],
        compiler_params=pltpu.CompilerParams(vmem_limit_bytes=24 * MIB),
        cost_estimate=SMALL_COST,
        name="norm_and_project",
    )(micro, layer_input, gain, a_own, a_far, b_own, b_far)


def middle_kernel(micro_ref, tokens_ref, mixed_ref, other_ref, own_ref, far_ref, gain_ref, residual_ref, normed_ref):
    total = tokens_ref[0].astype(F32) + dot(mixed_ref[...], own_ref[...], NT) + dot(other_ref[...], far_ref[...], NT)
    residual_ref[...] = total
    inverse = lax.rsqrt(jnp.mean(total * total, axis=-1, keepdims=True) + 1e-06)
    normed_ref[...] = (total * inverse * gain_ref[...]).astype(BF)


def residual_and_norm(micro, layer_input, mixed, other, output_own, output_far, gain):
    width = layer_input.shape[2]
    block = 256
    cols = mixed.shape[1]
    whole = lambda rows, n: pl.BlockSpec((rows, n), lambda i, m: (0, 0))
    here = lambda n: pl.BlockSpec((block, n), lambda i, m: (i, 0))
    return pl.pallas_call(
        middle_kernel,
        grid_spec=pltpu.PrefetchScalarGridSpec(
            num_scalar_prefetch=1,
            grid=(SEQ // block,),
            in_specs=[
                pl.BlockSpec((1, block, width), lambda i, m: (m[0], i, 0)),
                here(cols), here(cols), whole(width, cols), whole(width, cols), whole(1, width),
            ],
            out_specs=[here(width), here(width)],
        ),
        out_shape=[jax.ShapeDtypeStruct((SEQ, width), F32), jax.ShapeDtypeStruct((SEQ, width), BF)],
        compiler_params=pltpu.CompilerParams(vmem_limit_bytes=24 * MIB),
        cost_estimate=SMALL_COST,
        name="residual_and_norm",
    )(micro, layer_input, mixed, other, output_own, output_far, gain)


def picked_rows(first, second, segments):
    total = None
    start = 0
    for rows in segments:
        length = rows.shape[0]
        ids = lax.broadcasted_iota(jnp.int32, (1, length), 1) + start
        hot = jnp.where((first == ids) | (second == ids), 1.0, 0.0).astype(BF)
        total = put(total, dot(hot, rows))
        start += length
    return total


def put(a, b):
    return b if a is None else a + b


def folded(product):
    return jnp.sum(product.reshape(product.shape[0] // 8, 8, product.shape[1]), axis=0)


def as_column(eight):
    ones = jnp.ones((16, TILE), BF)
    high = eight.astype(BF)
    rest = (eight - high.astype(F32)).astype(BF)
    return dot(jnp.concatenate([high, rest], 0), ones, TN)


def combine_kernel(experts, half, spare, micro_ref, core_ref, length_ref, *refs):
    info_ref, grad_ref, residual_ref, mixed_ref, gain_ref, router_ref, output_ref = refs[:7]
    backs = refs[7:-9]
    (total_ref, mixed_grad_ref, extra_ref, far_ref, own_ref, acc_ref, router_acc, gain_acc, tables) = refs[-9:]
    block = residual_ref.shape[0]
    step = pl.program_id(0)
    count = len(backs) // 2

    @pl.when(step == 0)
    def _():
        place = lax.broadcasted_iota(jnp.int32, (experts, 1), 0)
        for n, back in enumerate((backs[count - 1], backs[2 * count - 1])):
            table = jnp.zeros((experts, back.shape[2]), F32)
            for e in range(experts):
                row = back[e, spare : spare + 16, :].astype(F32)[:1]
                table = jnp.where(place == e, row, table)
            for piece in range(3):
                at = (3 * n + piece) * experts
                tables[at : at + experts] = table[:, piece * half : (piece + 1) * half]

    info = jnp.transpose(info_ref[...])
    number = lambda n: info[:, n : n + 1]
    columns = lax.broadcasted_iota(jnp.int32, (1, half), 1)
    lanes = lax.broadcasted_iota(jnp.int32, (1, 6 * experts), 1)
    table = tables[...].astype(BF)
    values = []
    for k in range(2):
        slot = number(4 + k)
        hot = jnp.where(columns == lax.rem(slot, half), 1.0, 0.0).astype(BF)
        found = dot(hot, table, NT)
        wanted = jnp.where(slot // half == core_ref[0], 0, 3 * experts) + number(2 + k)
        away = lanes - wanted
        hit = (away == 0) | (away == experts) | (away == 2 * experts)
        values.append(jnp.sum(jnp.where(hit, found, 0.0), axis=1, keepdims=True))
    wide = lax.broadcasted_iota(jnp.int32, (1, TILE), 1)
    is_first, is_second = wide == number(2), wide == number(3)
    residual = residual_ref[...]
    gain = gain_ref[...]
    inverse = lax.rsqrt(jnp.mean(residual * residual, axis=-1, keepdims=True) + 1e-06)
    plain = residual * inverse
    normed = (plain * gain).astype(BF)
    logits = dot(normed, router_ref[...])
    gap = jnp.sum(jnp.where(is_first, logits, 0.0) - jnp.where(is_second, logits, 0.0), axis=1, keepdims=True)
    small = jnp.exp(-jnp.abs(gap))
    logit = small / ((1.0 + small) * (1.0 + small)) * (values[0] - values[1])
    logit_grad = jnp.where(is_first, logit, jnp.where(is_second, -logit, 0.0)).astype(BF)
    segments = [b[...].reshape(b.shape[0] * b.shape[1], b.shape[2]) for b in backs]
    normed_grad = picked_rows(number(0), number(1), segments) + dot(logit_grad, router_ref[...], NT)
    scaled = normed_grad * gain
    mean = jnp.mean(scaled * plain, axis=-1, keepdims=True)
    place = lax.broadcasted_iota(jnp.int32, (block, 1), 0) + step * block
    grad_out = jnp.where(place < length_ref[0], grad_ref[0].astype(F32), 0.0)
    total = grad_out + inverse * (scaled - plain * mean)
    total_ref[...] = total
    branch = total.astype(BF)
    mixed_grad_ref[...] = dot(branch, output_ref[...]).astype(BF)
    router_part = dot(logit_grad, normed, TN)
    gain_part = folded(normed_grad * plain)
    output_part = dot(mixed_ref[...], branch, TN)

    @pl.when(step == 0)
    def _():
        router_acc[...] = router_part
        gain_acc[...] = gain_part
        acc_ref[...] = output_part

    @pl.when(step > 0)
    def _():
        router_acc[...] += router_part
        gain_acc[...] += gain_part
        acc_ref[...] += output_part

    @pl.when(step == pl.num_programs(0) - 1)
    def _():
        extra_ref[...] = jnp.transpose(router_acc[...]) + jnp.where(wide == experts + 1, as_column(gain_acc[...]), 0.0)
        parts = jnp.transpose(acc_ref[...])
        far_ref[...] = parts[:, TILE:].astype(BF)
        own_ref[:, :TILE] = parts[:, :TILE]
        own_ref[:, TILE:] = parts[:, 2 * TILE :]


def combine(micro, core, length, info, out_grad, residual, mixed, gain, router, output_own, backs, half, spare):
    width = residual.shape[1]
    block = 256
    cols = mixed.shape[1]
    whole = lambda arr: pl.BlockSpec(arr.shape, lambda i, *_: (0,) * arr.ndim)
    fixed = lambda rows, n: pl.BlockSpec((rows, n), lambda i, *_: (0, 0))
    here = lambda n: pl.BlockSpec((block, n), lambda i, *_: (i, 0))
    experts = backs[0].shape[0]
    return pl.pallas_call(
        functools.partial(combine_kernel, experts, half, spare),
        grid_spec=pltpu.PrefetchScalarGridSpec(
            num_scalar_prefetch=3,
            grid=(SEQ // block,),
            in_specs=[
                pl.BlockSpec((8, block), lambda i, *_: (0, i)),
                pl.BlockSpec((1, block, width), lambda i, m, *_: (m[0], i, 0)),
                here(width), here(cols), whole(gain), whole(router), whole(output_own),
            ]
            + [whole(x) for x in backs],
            out_specs=[here(width), here(cols), fixed(width, TILE), fixed(width, 2 * TILE), fixed(width, 2 * TILE)],
            scratch_shapes=[
                pltpu.VMEM((cols, width), F32),
                pltpu.VMEM((TILE, width), F32),
                pltpu.VMEM((8, width), F32),
                pltpu.VMEM((6 * experts, half), F32),
            ],
        ),
        out_shape=[
            jax.ShapeDtypeStruct((SEQ, width), F32),
            jax.ShapeDtypeStruct((SEQ, cols), BF),
            jax.ShapeDtypeStruct((width, TILE), F32),
            jax.ShapeDtypeStruct((width, 2 * TILE), BF),
            jax.ShapeDtypeStruct((width, 2 * TILE), F32),
        ],
        compiler_params=pltpu.CompilerParams(vmem_limit_bytes=32 * MIB),
        cost_estimate=SMALL_COST,
        name="combine",
    )(micro, core, length, info, out_grad, residual, mixed, gain, router, output_own, *backs)


def output_kernel(core_ref, length_ref, info_ref, residual_ref, own_ref, far_ref, out_ref):
    block = residual_ref.shape[0]
    info = jnp.transpose(info_ref[...])
    place = lax.broadcasted_iota(jnp.int32, (block, 1), 0) + (core_ref[0] * 2 + pl.program_id(0)) * block
    rows = residual_ref[...] + picked_rows(info[:, 6:7], info[:, 7:8], (own_ref[...], far_ref[...]))
    out_ref[...] = jnp.where(place < length_ref[0], rows, 0.0).astype(BF)


def output_rows(core, length, info, residual, own, far):
    width = residual.shape[1]
    block = 256
    here = lambda n: pl.BlockSpec((block, n), lambda i, c, *_: (c[0] * 2 + i, 0))
    whole = lambda arr: pl.BlockSpec(arr.shape, lambda i, *_: (0, 0))
    return pl.pallas_call(
        output_kernel,
        grid_spec=pltpu.PrefetchScalarGridSpec(
            num_scalar_prefetch=2,
            grid=(2,),
            in_specs=[
                pl.BlockSpec((8, block), lambda i, c, *_: (0, c[0] * 2 + i)), here(width), whole(own), whole(far),
            ],
            out_specs=pl.BlockSpec((block, width), lambda i, *_: (i, 0)),
        ),
        out_shape=jax.ShapeDtypeStruct((2 * block, width), BF),
        compiler_params=pltpu.CompilerParams(vmem_limit_bytes=24 * MIB),
        cost_estimate=SMALL_COST,
        name="output_rows",
    )(core, length, info, residual, own, far)


def far_weight_kernel(normed_ref, q_ref, k_ref, v_ref, output_ref, far_ref, own_ref):
    rows = normed_ref.shape[1]
    low = low_lanes((rows, TILE))
    q, k, v = (dot(normed_ref[...], d[...], TN) for d in (q_ref, k_ref, v_ref))
    for n, part in enumerate((q, k, v)):
        far_ref[:, n * TILE : (n + 1) * TILE] = part[:, :TILE].astype(BF)
    q, k, v = (part[:, TILE:] for part in (q, k, v))
    far_ref[:, 3 * TILE : 4 * TILE] = jnp.where(low, turned(q), k).astype(BF)
    far_ref[:, 4 * TILE : 5 * TILE] = jnp.where(low, turned(v), output_ref[:, TILE:].astype(F32)).astype(BF)
    far_ref[:, 5 * TILE :] = output_ref[:, :TILE]
    own_ref[:, :TILE] = jnp.where(low, q, turned(k))
    own_ref[:, TILE:] = jnp.where(low, v, 0.0)


def far_weight_grads(normed, q, k, v, output):
    width = normed.shape[1]
    block = 256
    whole = lambda arr: pl.BlockSpec(arr.shape, lambda i: (0, 0))
    here = lambda n: pl.BlockSpec((block, n), lambda i: (i, 0))
    return pl.pallas_call(
        far_weight_kernel,
        grid=(width // block,),
        in_specs=[pl.BlockSpec((SEQ, block), lambda i: (0, i)), whole(q), whole(k), whole(v), here(2 * TILE)],
        out_specs=[here(6 * TILE), here(2 * TILE)],
        out_shape=[jax.ShapeDtypeStruct((width, 6 * TILE), BF), jax.ShapeDtypeStruct((width, 2 * TILE), F32)],
        compiler_params=pltpu.CompilerParams(vmem_limit_bytes=20 * MIB),
        cost_estimate=SMALL_COST,
        name="far_weight_grads",
    )(normed, q, k, v, output)


def own_weight_kernel(normed_ref, q_ref, k_ref, v_ref, own_ref):
    for n, d in enumerate((q_ref, k_ref, v_ref)):
        own_ref[:, n * TILE : (n + 1) * TILE] = dot(normed_ref[...], d[...], TN)


def own_weight_grads(normed, q, k, v):
    width = normed.shape[1]
    block = 256
    whole = lambda arr: pl.BlockSpec(arr.shape, lambda i: (0, 0))
    return pl.pallas_call(
        own_weight_kernel,
        grid=(width // block,),
        in_specs=[pl.BlockSpec((SEQ, block), lambda i: (0, i)), whole(q), whole(k), whole(v)],
        out_specs=pl.BlockSpec((block, 3 * TILE), lambda i: (i, 0)),
        out_shape=jax.ShapeDtypeStruct((width, 3 * TILE), F32),
        compiler_params=pltpu.CompilerParams(vmem_limit_bytes=20 * MIB),
        cost_estimate=SMALL_COST,
        name="own_weight_grads",
    )(normed, q, k, v)


def projected_back(weight_ref, first, last):
    total = None
    for n in range(3):
        base = 3 * n * TILE
        total = put(total, dot(first[n][...], weight_ref[:, base : base + TILE], NT))
        total = put(total, dot(last[n][...], weight_ref[:, base + TILE : base + 3 * TILE], NT))
    return total


def sent_kernel(core_ref, weight_ref, q0, k0, v0, q1, k1, v1, out_ref):
    out_ref[...] = projected_back(weight_ref, (q0, k0, v0), (q1, k1, v1))


def sent_half(core, weight, first, last):
    width = weight.shape[0]
    block = 256
    here = lambda n: pl.BlockSpec((block, n), lambda i, c: ((1 - c[0]) * 2 + i, 0))
    return pl.pallas_call(
        sent_kernel,
        grid_spec=pltpu.PrefetchScalarGridSpec(
            num_scalar_prefetch=1,
            grid=(2,),
            in_specs=[pl.BlockSpec(weight.shape, lambda i, c: (0, 0))] + [here(TILE)] * 3 + [here(2 * TILE)] * 3,
            out_specs=pl.BlockSpec((block, width), lambda i, c: (i, 0)),
        ),
        out_shape=jax.ShapeDtypeStruct((2 * block, width), F32),
        compiler_params=pltpu.CompilerParams(vmem_limit_bytes=20 * MIB),
        cost_estimate=SMALL_COST,
        name="sent_half",
    )(core, weight, *first, *last)


def input_kernel(
    lane, micro_ref, core_ref, weight_ref, q0, k0, v0, q1, k1, v1, got_ref, tokens_ref, gain_ref, grad_ref,
    out_ref, extra_ref, acc_ref,
):
    normed_grad = got_ref[...] + projected_back(weight_ref, (q0, k0, v0), (q1, k1, v1))
    x = tokens_ref[0].astype(F32)
    inverse = lax.rsqrt(jnp.mean(x * x, axis=-1, keepdims=True) + 1e-06)
    plain = x * inverse
    scaled = normed_grad * gain_ref[...]
    mean = jnp.mean(scaled * plain, axis=-1, keepdims=True)
    out_ref[...] = (grad_ref[...] + inverse * (scaled - plain * mean)).astype(BF)
    wide = lax.broadcasted_iota(jnp.int32, (1, TILE), 1)
    part = folded(normed_grad * plain)

    @pl.when(pl.program_id(0) == 0)
    def _():
        acc_ref[...] = part

    @pl.when(pl.program_id(0) == 1)
    def _():
        extra_ref[...] = jnp.where(wide == lane, as_column(acc_ref[...] + part), 0.0)


def input_half(lane, micro, core, weight, first, last, got, layer_input, gain, residual_grad):
    width = weight.shape[0]
    block = 256
    here = lambda n: pl.BlockSpec((block, n), lambda i, m, c: (c[0] * 2 + i, 0))
    plain = pl.BlockSpec((block, width), lambda i, *_: (i, 0))
    return pl.pallas_call(
        functools.partial(input_kernel, lane),
        grid_spec=pltpu.PrefetchScalarGridSpec(
            num_scalar_prefetch=2,
            grid=(2,),
            in_specs=[pl.BlockSpec(weight.shape, lambda i, *_: (0, 0))]
            + [here(TILE)] * 3
            + [here(2 * TILE)] * 3
            + [
                plain,
                pl.BlockSpec((1, block, width), lambda i, m, c: (m[0], c[0] * 2 + i, 0)),
                pl.BlockSpec(gain.shape, lambda i, *_: (0, 0)),
                here(width),
            ],
            out_specs=[plain, pl.BlockSpec((width, TILE), lambda i, *_: (0, 0))],
            scratch_shapes=[pltpu.VMEM((8, width), F32)],
        ),
        out_shape=[jax.ShapeDtypeStruct((2 * block, width), BF), jax.ShapeDtypeStruct((width, TILE), F32)],
        compiler_params=pltpu.CompilerParams(vmem_limit_bytes=24 * MIB),
        cost_estimate=SMALL_COST,
        name="input_half",
    )(micro, core, weight, *first, *last, got, layer_input, gain, residual_grad)


def sum_kernel(kept, own01, own2, got, out_own, early, late, late_far, table, sum_ref):
    low = low_lanes(early.shape)
    sum_ref[:, : 3 * TILE] = (own01[...] + got[:, : 3 * TILE].astype(F32)).astype(BF)
    sum_ref[:, 3 * TILE : 4 * TILE] = (own2[:, :TILE] + got[:, 3 * TILE : 4 * TILE].astype(F32)).astype(BF)
    mixed = jnp.where(low, own2[:, TILE:], turned(out_own[:, TILE:]))
    sum_ref[:, 4 * TILE : 5 * TILE] = (mixed + got[:, 4 * TILE : 5 * TILE].astype(F32)).astype(BF)
    sum_ref[:, 5 * TILE : 6 * TILE] = (out_own[:, :TILE] + got[:, 5 * TILE :].astype(F32)).astype(BF)
    extra = early[...] + late[...] + late_far[...] + table[...]
    high = extra.astype(BF)
    rest = extra - high.astype(F32)
    if kept <= HEAD_DIM:
        sum_ref[:, 6 * TILE :] = jnp.where(low, high.astype(F32), turned(rest)).astype(BF)
    else:
        sum_ref[:, 6 * TILE : 7 * TILE] = high
        sum_ref[:, 7 * TILE :] = rest.astype(BF)


def packed_sums(kept, *parts):
    width = parts[0].shape[0]
    cols = (7 if kept <= HEAD_DIM else 8) * TILE
    block = 256
    here = lambda n: pl.BlockSpec((block, n), lambda i: (i, 0))
    return pl.pallas_call(
        functools.partial(sum_kernel, kept),
        grid=(width // block,),
        in_specs=[here(x.shape[1]) for x in parts],
        out_specs=here(cols),
        out_shape=jax.ShapeDtypeStruct((width, cols), BF),
        compiler_params=pltpu.CompilerParams(vmem_limit_bytes=16 * MIB),
        cost_estimate=SMALL_COST,
        name="packed_sums",
    )(*parts)


def final_kernel(kept, parts_ref, q_ref, k_ref, v_ref, o_ref, small_ref):
    total = parts_ref[0].astype(F32)
    for n in range(1, parts_ref.shape[0]):
        total = total + parts_ref[n].astype(F32)
    tile = lambda t: total[:, t * TILE : (t + 1) * TILE]
    q_ref[:, :TILE] = tile(0)
    q_ref[:, TILE:] = tile(3)[:, :HEAD_DIM]
    k_ref[:, :TILE] = tile(1)
    k_ref[:, TILE:] = turned(tile(3))[:, :HEAD_DIM]
    v_ref[:, :TILE] = tile(2)
    v_ref[:, TILE:] = tile(4)[:, :HEAD_DIM]
    o_ref[:, :TILE] = tile(5)
    o_ref[:, TILE:] = turned(tile(4))[:, :HEAD_DIM]
    small_ref[...] = tile(6) + (turned(tile(6)) if kept <= HEAD_DIM else tile(7))


def final_sums(kept, parts, shard):
    rows = parts.shape[1]
    return pl.pallas_call(
        functools.partial(final_kernel, kept),
        out_shape=[jax.ShapeDtypeStruct((rows, shard), F32)] * 4 + [jax.ShapeDtypeStruct((rows, TILE), F32)],
        compiler_params=pltpu.CompilerParams(vmem_limit_bytes=16 * MIB),
        cost_estimate=SMALL_COST,
        name="final_sums",
    )(parts)


def pair_gate(logits, own, other):
    lanes = lax.broadcasted_iota(jnp.int32, logits.shape, 1)
    gap = jnp.sum(
        jnp.where(lanes == own, logits, 0.0) - jnp.where(lanes == other, logits, 0.0), axis=1, keepdims=True
    )
    small = jnp.exp(-jnp.abs(gap))
    return jnp.where(gap >= 0.0, 1.0, small) / (1.0 + small)


def expert_kernel(
    me_ref, partner_ref, rows_ref, grads_ref, router_ref, a0, a1, a2, a3, b0, b1, b2, b3,
    back_ref, active_ref, slope_ref, gated_ref, scalar_ref,
):
    rows = rows_ref[...]
    grads = grads_ref[...]
    gate = pair_gate(dot(rows, router_ref[...]), me_ref[0], partner_ref[...])
    gated_ref[...] = (gate * grads.astype(F32)).astype(BF)
    mass = None
    back = None
    step = 256
    for r, (first, second) in enumerate(((a0, b0), (a1, b1), (a2, b2), (a3, b3))):
        width = first.shape[1]
        for c in range(0, width, step):
            x = dot(rows, first[:, c : c + step])
            plain = dot(grads, second[c : c + step, :], NT)
            square = x * x
            bent = jnp.tanh(x * (GELU_C + (GELU_C * GELU_A) * square))
            rise = 0.5 + 0.5 * bent
            active = x * rise
            slope = rise + active * (1.0 - bent) * (GELU_C + (3.0 * GELU_C * GELU_A) * square)
            low = active.astype(BF)
            place = slice(r * width + c, r * width + c + step)
            active_ref[:, place] = low
            slope_ref[:, place] = (gate * plain * slope).astype(BF)
            part = low.astype(F32) * plain
            mass = put(mass, part[:, :TILE] + part[:, TILE:])
        back = put(back, dot(slope_ref[:, r * width : (r + 1) * width], first[...], NT))
    back_ref[...] = back.astype(BF)
    lanes = lax.broadcasted_iota(jnp.int32, (rows.shape[0], TILE), 1)
    scalar_ref[...] = jnp.where(lanes == 0, jnp.sum(mass, axis=1, keepdims=True), gate)


def row_block(total):
    return 320 if total % 320 == 0 else total


def expert_rows_pass(me, partner, rows, grads, router, firsts, seconds):
    total, width = rows.shape
    block = row_block(total)
    hidden = sum(f.shape[1] for f in firsts)
    here = lambda cols: pl.BlockSpec((block, cols), lambda i: (i, 0))
    whole = lambda arr: pl.BlockSpec(arr.shape, lambda i: (0, 0))
    return pl.pallas_call(
        expert_kernel,
        grid=(total // block,),
        in_specs=[pl.BlockSpec(memory_space=pltpu.SMEM), here(1), here(width), here(width), whole(router)]
        + [whole(w) for w in firsts]
        + [whole(w) for w in seconds],
        out_specs=[here(width), here(hidden), here(hidden), here(width), here(TILE)],
        out_shape=[
            jax.ShapeDtypeStruct((total, width), BF),
            jax.ShapeDtypeStruct((total, hidden), BF),
            jax.ShapeDtypeStruct((total, hidden), BF),
            jax.ShapeDtypeStruct((total, width), BF),
            jax.ShapeDtypeStruct((total, TILE), F32),
        ],
        compiler_params=pltpu.CompilerParams(vmem_limit_bytes=48 * MIB),
        cost_estimate=SMALL_COST,
        name="expert_rows",
    )(me, partner, rows, grads, router, *firsts, *seconds)


def result_kernel(chunks, *refs):
    active, scalars, seconds, out_ref = refs[:chunks], refs[chunks : 2 * chunks], refs[2 * chunks : -1], refs[-1]
    for c in range(chunks):

        @pl.when(pl.program_id(0) == c)
        def _(c=c):
            width = seconds[0].shape[0]
            total = None
            for r, second in enumerate(seconds):
                total = put(total, dot(active[c][:, r * width : (r + 1) * width], second[...]))
            rows = (total * scalars[c][:, 1:2]).astype(BF)
            if chunks > 1:
                out_ref[:, 0] = rows.reshape(out_ref.shape[0], out_ref.shape[2], out_ref.shape[3])
            else:
                out_ref[...] = rows


def expert_results(active, scalars, seconds, experts):
    chunks = len(active)
    total, hidden = active[0].shape
    width = seconds[0].shape[1]
    block = row_block(total)
    steps = total // block

    def here(c, cols):
        return pl.BlockSpec((block, cols), lambda g, i: (jnp.where(g == c, i, jnp.where(g < c, 0, steps - 1)), 0))

    chunk = total // experts
    if chunks > 1:
        shape = (experts, chunks, chunk, width)
        out_spec = pl.BlockSpec((block // chunk, 1, chunk, width), lambda g, i: (i, g, 0, 0))
    else:
        shape = (total, width)
        out_spec = pl.BlockSpec((block, width), lambda g, i: (i, 0))
    out = pl.pallas_call(
        functools.partial(result_kernel, chunks),
        grid=(chunks, steps),
        in_specs=[here(c, hidden) for c in range(chunks)]
        + [here(c, TILE) for c in range(chunks)]
        + [pl.BlockSpec(w.shape, lambda g, i: (0, 0)) for w in seconds],
        out_specs=out_spec,
        out_shape=jax.ShapeDtypeStruct(shape, BF),
        compiler_params=pltpu.CompilerParams(vmem_limit_bytes=32 * MIB),
        cost_estimate=SMALL_COST,
        name="expert_results",
    )(*active, *scalars, *seconds)
    return out.reshape(experts, chunks * chunk, width)


def weight_parts(count, refs):
    rows, slopes, active, gated = (refs[n * count : (n + 1) * count] for n in range(4))
    first, second = None, None
    for n in range(count):
        first = put(first, dot(rows[n][...], slopes[n][...], TN))
        second = put(second, dot(active[n][...], gated[n][...], TN))
    return first, second


def cross_kernel(count, *refs):
    first, second = weight_parts(count, refs)
    refs[-1][0, 0] = first.astype(BF)
    refs[-1][0, 1] = second.astype(BF)


def kept_kernel(count, *refs):
    got_ref, far_first, far_second, kept_ref = refs[-4:]
    first, second = weight_parts(count, refs)
    first = first + got_ref[0, 0].astype(F32)
    second = second + got_ref[0, 1].astype(F32)

    @pl.when(pl.program_id(0) == 0)
    def _():
        far_first[...] = first.astype(BF)
        far_second[...] = second.astype(BF)

    @pl.when(pl.program_id(0) == 1)
    def _():
        kept_ref[0] = first
        kept_ref[1] = second


def weight_specs(rows, slopes, quarter):
    total, width = rows[0].shape
    hidden = slopes[0].shape[1] // 4
    whole = pl.BlockSpec((total, width), lambda i: (0, 0))
    part = pl.BlockSpec((total, hidden), lambda i: (0, quarter(i)))
    count = len(rows)
    return width, hidden, [whole] * count + [part] * (2 * count) + [whole] * count


def cross_weight_grads(rows, slopes, active, gated):
    width, hidden, specs = weight_specs(rows, slopes, lambda i: 2 + i)
    return pl.pallas_call(
        functools.partial(cross_kernel, len(rows)),
        grid=(2,),
        in_specs=specs,
        out_specs=pl.BlockSpec((1, 2, width, hidden), lambda i: (i, 0, 0, 0)),
        out_shape=jax.ShapeDtypeStruct((2, 2, width, hidden), BF),
        compiler_params=pltpu.CompilerParams(vmem_limit_bytes=44 * MIB),
        cost_estimate=SMALL_COST,
        name="cross_weight_grads",
    )(*rows, *slopes, *active, *gated)


def kept_weight_grads(rows, slopes, active, gated, got):
    width, hidden, specs = weight_specs(rows, slopes, lambda i: 1 - i)
    fixed = pl.BlockSpec((width, hidden), lambda i: (0, 0))
    return pl.pallas_call(
        functools.partial(kept_kernel, len(rows)),
        grid=(2,),
        in_specs=specs + [pl.BlockSpec((1, 2, width, hidden), lambda i: (1 - i, 0, 0, 0))],
        out_specs=[fixed, fixed, pl.BlockSpec((2, width, hidden), lambda i: (0, 0, 0))],
        out_shape=[
            jax.ShapeDtypeStruct((width, hidden), BF),
            jax.ShapeDtypeStruct((hidden, width), BF),
            jax.ShapeDtypeStruct((2, width, hidden), F32),
        ],
        compiler_params=pltpu.CompilerParams(vmem_limit_bytes=48 * MIB),
        cost_estimate=SMALL_COST,
        name="kept_weight_grads",
    )(*rows, *slopes, *active, *gated, got)


def last_sum_kernel(kept_ref, first_ref, second_ref, out_first, out_second):
    out_first[...] = kept_ref[0] + first_ref[...].astype(F32)
    out_second[...] = kept_ref[1] + second_ref[...].astype(F32)


def last_sums(kept, first, second):
    width, hidden = first.shape
    block = 256
    here = pl.BlockSpec((block, hidden), lambda i: (i, 0))
    return pl.pallas_call(
        last_sum_kernel,
        grid=(width // block,),
        in_specs=[pl.BlockSpec((2, block, hidden), lambda i: (0, i, 0)), here, here],
        out_specs=[here, here],
        out_shape=[jax.ShapeDtypeStruct((width, hidden), F32)] * 2,
        compiler_params=pltpu.CompilerParams(vmem_limit_bytes=24 * MIB),
        cost_estimate=SMALL_COST,
        name="last_sums",
    )(kept, first, second)


def send_kernel(micro_ref, code_ref, rows_ref, out_ref):
    block = out_ref.shape[0]
    ids = lax.broadcasted_iota(jnp.int32, (block, 1), 0) + pl.program_id(0) * block
    hot = jnp.where((ids == code_ref[:1]) | (ids == code_ref[1:2]), 1.0, 0.0).astype(BF)
    out_ref[...] = dot(hot, rows_ref[0]).astype(BF)


def send_rows(micro, code, rows, count):
    width = rows.shape[2]
    block = next(b for b in (336, 320, 384, count) if count % b == 0)
    return pl.pallas_call(
        send_kernel,
        grid_spec=pltpu.PrefetchScalarGridSpec(
            num_scalar_prefetch=1,
            grid=(count // block,),
            in_specs=[
                pl.BlockSpec(code.shape, lambda i, m: (0, 0)),
                pl.BlockSpec((1, SEQ, width), lambda i, m: (m[0], 0, 0)),
            ],
            out_specs=pl.BlockSpec((block, width), lambda i, m: (i, 0)),
        ),
        out_shape=jax.ShapeDtypeStruct((count, width), BF),
        compiler_params=pltpu.CompilerParams(vmem_limit_bytes=20 * MIB),
        cost_estimate=SMALL_COST,
        name="send_rows",
    )(micro, code, rows)


def place_kernel(place_ref, a_ref, b_ref, c_ref, d_ref, out_ref):
    for n, piece in enumerate((a_ref, b_ref, c_ref, d_ref)):

        @pl.when(pl.program_id(0) == n)
        def _(piece=piece):
            out_ref[0] = piece[...]


def place_pieces(places, pieces):
    shape = pieces[0].shape
    whole = pl.BlockSpec(shape, lambda i, place_ref: (0, 0))
    return pl.pallas_call(
        place_kernel,
        grid_spec=pltpu.PrefetchScalarGridSpec(
            num_scalar_prefetch=1,
            grid=(4,),
            in_specs=[whole] * 4,
            out_specs=pl.BlockSpec((1,) + shape, lambda i, place_ref: (place_ref[i], 0, 0)),
        ),
        out_shape=jax.ShapeDtypeStruct((4,) + shape, pieces[0].dtype),
        compiler_params=pltpu.CompilerParams(vmem_limit_bytes=20 * MIB),
        cost_estimate=SMALL_COST,
        name="place_pieces",
    )(places, *pieces)


def swap(value, axis, count, bit):
    return lax.ppermute(value, axis, [(i, i ^ bit) for i in range(count)])


def all_to_all(value):
    return lax.all_to_all(value, "dp", split_axis=0, concat_axis=0, tiled=True)


def together(*values):
    return lax.optimization_barrier(values)


def local(
    layer_input, out_grad, first_gain, query_weight, key_weight, value_weight, output_weight,
    position_bias, second_gain, router_weight, expert_in, expert_out, seq_lengths, routes,
):
    micro_count, tok_rows, width = layer_input.shape
    dp_count = lax.axis_size("dp")
    expert_count = router_weight.shape[1]
    shard = query_weight.shape[1]
    heads_here = position_bias.shape[0]
    assert lax.axis_size("tensor") == 4 and micro_count == 2 and expert_count == dp_count
    assert tok_rows == SEQ and seq_lengths.shape[1] == 1
    capacity = max(8, 8 * (10 * tok_rows // (32 * expert_count)))
    half = capacity // 2
    stride = 8 * (half // 8 + 1)
    chunks = 2 if half % 32 == 0 else 1
    chunk = half // chunks
    chunk_rows = expert_count * chunk
    rows_here = query_weight.shape[0]
    me = lax.axis_index("dp")
    rank = lax.axis_index("tensor")
    micro = rank // 2
    core = rank % 2

    def swap_y(value):
        return swap(value, "tensor", 4, 2)

    def swap_core(value):
        return swap(value, "tensor", 4, 1)

    micro_arg = micro.reshape(1).astype(jnp.int32)
    core_arg = core.reshape(1).astype(jnp.int32)

    packed = pack_weights(query_weight, key_weight, value_weight, output_weight, first_gain, second_gain, router_weight)
    three = 3 * TILE

    def doubled(stacked, bit, axis=0):
        other = swap(stacked, "dp", dp_count, bit)
        high = (me & bit) != 0
        pair = jnp.where(high, jnp.stack([other, stacked], axis + 1), jnp.stack([stacked, other], axis + 1))
        return pair.reshape(stacked.shape[:axis] + (-1,) + stacked.shape[axis + 1 :])

    stacked = packed[None]
    bit = dp_count // 2
    while bit > 1:
        stacked = doubled(stacked, bit)
        if bit == dp_count // 2:
            stacked, routes, position_bias = together(stacked, routes, position_bias)
        bit //= 2
    length = lax.dynamic_index_in_dim(seq_lengths, micro, 0, keepdims=False)
    route = lax.dynamic_index_in_dim(routes, micro, 0, keepdims=False).T
    expert_ids = jnp.arange(expert_count, dtype=jnp.int32)
    named = (expert_ids[:, None, None] == route[None]).astype(jnp.int32)
    per_token = jnp.sum(named, axis=1, dtype=jnp.int32)
    earlier = jnp.cumsum(per_token, axis=1, dtype=jnp.int32) - per_token
    slot = jnp.sum(named * earlier[:, None, :], axis=0, dtype=jnp.int32)
    here = slot // half == core
    within = slot % half
    chunk_of = within // chunk
    inside = within % chunk
    spare = 16 * -(-chunk // 16)
    last_stride = spare + 16
    last = (chunks - 1) * chunk_rows
    code_back = jnp.where(
        chunk_of == chunks - 1, last + route * last_stride + inside, chunk_of * chunk_rows + route * chunk + inside
    )
    code_back = code_back + jnp.where(here, 0, last + expert_count * last_stride)
    code_result = route * half + within + jnp.where(here, 0, expert_count * half)
    info = jnp.concatenate([code_back, route, slot, code_result], 0)

    code_grads = jnp.where(here, route * stride + within, -1)
    stacked, code_grads = together(stacked, code_grads)
    valid = jnp.arange(SEQ, dtype=jnp.int32) < length[0]
    ids = jnp.arange(expert_count * stride, dtype=jnp.int32)[:, None]
    partner = jnp.sum(
        jnp.where(ids == code_grads[:1], route[1:], 0) + jnp.where(ids == code_grads[1:], route[:1], 0), axis=1, dtype=jnp.int32
    )
    grads_sent = send_rows(micro_arg, jnp.where(valid[None], code_grads, -1), out_grad, expert_count * stride)
    grads_sent = grads_sent.reshape(expert_count, stride, width)
    partner_row = jnp.pad(partner.reshape(expert_count, stride)[:, :half].astype(BF), ((0, 0), (0, width - half)))
    grads_sent = grads_sent.at[:, half].set(partner_row)

    first_own = expert_in[0]
    second_own = expert_out[0]
    first_y = swap_y(first_own)
    part_b = stacked[:, :, :three]
    part_a = doubled(stacked[:, :, three:], 1)
    part_a, first_y, grads_sent = together(part_a, first_y, grads_sent)
    pair_b = jnp.stack([part_b, swap_y(part_b)])
    a_own = part_a[:, :, :three]
    a_far = swap_y(a_own).reshape(width, three)
    a_own = a_own.reshape(width, three)
    pair_b = doubled(pair_b, 1, 1).reshape(2, width, three)
    small_all = part_a[:, :, three:].reshape(width, TILE)
    gain_one = small_all[:, expert_count].astype(F32)[None]
    gain_two = small_all[:, expert_count + 1].astype(F32)[None]
    router_wide = small_all
    far_bias = swap_y(position_bias)
    bias = jnp.concatenate([position_bias[:2], far_bias[:2], position_bias[2:], far_bias[2:]], 0)
    head_total = bias.shape[0]
    hot_const = jnp.asarray(NEAR_HOT, dtype=BF)
    near = dot(bias, hot_const) - bias[:, NB - 1 :].astype(F32)
    near = near.reshape(head_total, 2, TILE, TILE)
    places = jnp.arange(TILE, dtype=jnp.int32)
    causal = jnp.stack([places[None, :] <= places[:, None], jnp.ones((TILE, TILE), bool)])
    near = jnp.where(causal[None], near, NEG)

    grads_here = all_to_all(grads_sent)

    qkv, normed_one, qkv_weight, output_own = norm_and_project(
        micro_arg, layer_input, gain_one, a_own, a_far, pair_b[0], pair_b[1]
    )
    second_late, qkv = together(second_own, qkv)
    second_y = swap_y(second_late)
    output_far = swap_core(output_own)
    mixed, logs = attend(length, qkv, near)
    mixed, output_far = together(mixed, output_far)
    mixed_far = swap_core(mixed)
    residual, normed_two = residual_and_norm(micro_arg, layer_input, mixed, mixed_far, output_own, output_far, gain_two)
    normed_two, grads_here, second_y = together(normed_two, grads_here, second_y)

    arrived = []
    zero = jnp.zeros((1,), jnp.int32)
    for c in range(chunks):
        code_chunk = jnp.where(here & (chunk_of == c), route * chunk + inside, -1)
        sent = send_rows(zero, code_chunk, normed_two[None], chunk_rows).reshape(expert_count, chunk, width)
        if arrived:
            sent, arrived[-1] = together(sent, arrived[-1])
        arrived.append(all_to_all(sent))

    firsts = (first_own, first_y, swap_core(first_own), swap_core(first_y))
    seconds = (second_own, second_y, swap_core(second_own), swap_core(second_y))

    partner_here = grads_here[:, half, :half].astype(jnp.int32)

    def chunk_grads(c):
        at = slice(c * chunk, (c + 1) * chunk)
        return grads_here[:, at].reshape(chunk_rows, width), partner_here[:, at].reshape(chunk_rows, 1)

    me_arg = me.reshape(1).astype(jnp.int32)
    rows_all, slopes, active, gated, scalars, backs = [], [], [], [], [], []
    for c in range(chunks):
        grads_c, partner_c = chunk_grads(c)
        rows_c = arrived[c].reshape(chunk_rows, width)
        back, act, slo, gat, sca = expert_rows_pass(me_arg, partner_c, rows_c, grads_c, router_wide, firsts, seconds)
        rows_all.append(rows_c)
        slopes.append(slo)
        active.append(act)
        gated.append(gat)
        scalars.append(sca)
        back = back.reshape(expert_count, chunk, width)
        if c + 1 < chunks:
            back, arrived[c + 1] = together(back, arrived[c + 1])
        if c == chunks - 1:
            gate_grad = jnp.concatenate([x[:, 0].reshape(expert_count, chunk) for x in scalars], 1)
            pieces = []
            for _ in range(3):
                piece = gate_grad.astype(BF)
                pieces.append(piece)
                gate_grad = gate_grad - piece.astype(F32)
            gate_row = jnp.pad(jnp.concatenate(pieces, 1), ((0, 0), (0, width - 3 * half)))
            back = jnp.pad(back, ((0, 0), (0, last_stride - chunk), (0, 0)))
            back = back.at[:, spare].set(gate_row)
            back, rows_all[-1], backs = together(back, rows_all[-1], backs)
        backs.append(all_to_all(back))
    grads_in = swap_core(cross_weight_grads(rows_all, slopes, active, gated))
    results = expert_results(active, scalars, seconds, expert_count)
    results, grads_in = together(results, grads_in)
    first_sent, second_sent, grads_kept = kept_weight_grads(rows_all, slopes, active, gated, grads_in)

    first_got = swap_y(first_sent)
    backs[-1], results = together(backs[-1], results)
    results_own = all_to_all(results).reshape(expert_count * half, width)

    backs_far = [swap_core(b) for b in backs]
    residual_grad, mixed_grad, extra_early, output_sent, output_kept = combine(
        micro_arg, core_arg, length, info, out_grad, residual, mixed, gain_two, router_wide, output_own,
        backs + backs_far, half, spare,
    )
    mixed_grad, first_got, second_sent = together(mixed_grad, first_got, second_sent)
    second_got = swap_y(second_sent)

    q1, k1, v1, tiles1, sums1 = attend_back(length, qkv, near, mixed, logs, mixed_grad, 1, 2)
    far_sent, own_last = far_weight_grads(normed_one, q1, k1, v1, output_sent)
    mixed_grad, far_sent = together(mixed_grad, far_sent)
    far_got = swap_y(far_sent)
    q0, k0, v0, tiles0, sums0 = attend_back(length, qkv, near, mixed, logs, mixed_grad, 0, 1)
    q0, second_got = together(q0, second_got)
    first, last = (q0, k0, v0), (q1, k1, v1)
    sent = sent_half(core_arg, qkv_weight, first, last)
    sent, residual, results_own = together(sent, residual, results_own)
    got = swap_core(sent)
    layer_rows = output_rows(core_arg, length, info, residual, results_own, swap_core(results_own))
    got, layer_rows = together(got, layer_rows)
    corner = micro * 2 + core
    corners = jnp.stack([corner, corner ^ 1, corner ^ 2, corner ^ 3]).astype(jnp.int32)

    def placed(own):
        across = swap_y(own)
        return place_pieces(corners, (own, swap_core(own), across, swap_core(across))).reshape(2, SEQ, width)

    input_rows, extra_late = input_half(
        expert_count, micro_arg, core_arg, qkv_weight, first, last, got, layer_input, gain_one, residual_grad
    )
    late_far = swap_core(extra_late)
    input_rows, normed_one, tiles0 = together(input_rows, normed_one, tiles0)
    own_pair = own_weight_grads(normed_one, q0, k0, v0)
    input_grad = placed(input_rows)
    layer_output = placed(layer_rows)
    expert_in_grad, expert_out_grad = last_sums(grads_kept, first_got, second_got)

    tiles = jnp.concatenate([tiles0, tiles1], 0).reshape(head_total, 2 * TILE * TILE)
    sums = jnp.concatenate([sums0, sums1], 0)
    tiles_high = tiles.astype(BF)
    tiles_rest = (tiles - tiles_high.astype(F32)).astype(BF)
    table = dot(tiles_high, hot_const, NT) + dot(tiles_rest, hot_const, NT)
    far_sum = jnp.sum(sums[:, :, 0], axis=1) - jnp.sum(table[:, : NB - 1], axis=1)
    table = jnp.concatenate([table[:, : NB - 1], far_sum[:, None]], 1)
    table_own = jnp.concatenate([table[0:2], table[4:5]], 0)
    table_far = jnp.concatenate([table[2:4], table[5:6]], 0)
    table_cols = heads_here * NB // rows_here
    table_both = jnp.concatenate([table_own.reshape(rows_here, table_cols), table_far.reshape(rows_here, table_cols)], 1)
    base = expert_count + 2
    kept = base + 2 * table_cols
    table_tile = jnp.tile(jnp.pad(table_both, ((0, 0), (base, TILE - kept))), (dp_count, 1))

    grads = packed_sums(kept, own_pair, own_last, far_got, output_kept, extra_early, extra_late, late_far, table_tile)
    arrived_grads = all_to_all(grads.reshape(dp_count, rows_here, grads.shape[1]))
    arrived_grads, layer_output = together(arrived_grads, layer_output)
    query_grad, key_grad, value_grad, output_grad, small = final_sums(kept, arrived_grads, shard)
    small_y = swap_y(small)
    both = small + small_y
    table_sum = small[:, base : base + table_cols] + small_y[:, base + table_cols : kept]
    return (
        layer_output,
        input_grad,
        both[:, expert_count],
        query_grad,
        key_grad,
        value_grad,
        output_grad.T,
        table_sum.reshape(heads_here, NB),
        both[:, expert_count + 1],
        both[:, :expert_count],
        expert_in_grad[None],
        expert_out_grad[None],
    )


def solution(mesh):
    return jax.shard_map(
        local,
        mesh=mesh,
        in_specs=(
            P(None, "dp", None),
            P(None, "dp", None),
            P("dp"),
            P("dp", "tensor"),
            P("dp", "tensor"),
            P("dp", "tensor"),
            P("tensor", "dp"),
            P("tensor", None),
            P("dp"),
            P("dp", None),
            P("dp", None, "tensor"),
            P("dp", "tensor", None),
            P(None, "dp"),
            P(None, "dp", None),
        ),
        out_specs=(
            P(None, "dp", None),
            P(None, "dp", None),
            P("dp"),
            P("dp", "tensor"),
            P("dp", "tensor"),
            P("dp", "tensor"),
            P("tensor", "dp"),
            P("tensor", None),
            P("dp"),
            P("dp", None),
            P("dp", None, "tensor"),
            P("dp", "tensor", None),
        ),
        check_vma=False,
    )
```

```python
import functools

import jax
import jax.numpy as jnp
import numpy as np
from jax import lax
from jax.experimental import pallas as pl
from jax.experimental.pallas import tpu as pltpu
from jax.sharding import PartitionSpec as P

HEAD_DIM = 64
NB = 32
SEQ = 1024
TILE = 128
QROWS = 256
NEG = -1e30
GELU_C = 0.7978845608028654
GELU_A = 0.044715

BF = jnp.bfloat16
F32 = jnp.float32

bucket_edges = np.ceil(16.0 * 8.0 ** (np.arange(1, 16) / 16.0)).astype(np.int32)


def near_tables():
    rows = np.arange(TILE)[:, None]
    cols = np.arange(TILE)[None, :]
    hots = []
    for shift in (0, TILE):
        distance = rows - cols + shift
        clipped = np.maximum(distance, 0)
        reached = np.sum(clipped[..., None] >= bucket_edges, axis=-1)
        bucket = np.minimum(clipped, 16) + reached
        hots.append(bucket[..., None] == np.arange(NB))
    hot = np.stack(hots).reshape(2 * TILE * TILE, NB).T
    return hot


NEAR_HOT = near_tables()
assert bucket_edges[-1] <= TILE


def dot(a, b, dims=((1,), (0,))):
    return lax.dot_general(a, b, (dims, ((), ())), preferred_element_type=F32)


NT = ((1,), (1,))
TN = ((0,), (0,))


MIB = 2**20
SMALL_COST = pl.CostEstimate(flops=1_000_000, bytes_accessed=1_000_000, transcendentals=0)


def score_tiles(block, half, q_half, key_ref, near_one, near_two, length):
    tiles = []
    for j in range(block + 1):
        s = dot(q_half, key_ref[j * QROWS : (j + 1) * QROWS, :], NT)
        if j == block:
            top = jnp.concatenate([s[:TILE, :TILE] + near_one, jnp.full((TILE, TILE), NEG, F32)], 1)
            low = jnp.concatenate([s[TILE:, :TILE] + near_two, s[TILE:, TILE:] + near_one], 1)
            s = jnp.concatenate([top, low], 0)
        elif j == block - 1:
            top = jnp.concatenate([s[:TILE, :TILE], s[:TILE, TILE:] + near_two], 1)
            s = jnp.concatenate([top, s[TILE:]], 0)
        if (j + 1) * QROWS > SEQ // 2:
            place = lax.broadcasted_iota(jnp.int32, (1, QROWS), 1) + j * QROWS
            s = s + jnp.where(place < length, 0.0, NEG)
        tiles.append(s)
    return tiles


def lane_half(rows):
    return lax.broadcasted_iota(jnp.int32, (rows, 2 * HEAD_DIM), 1) < HEAD_DIM


def attend_kernel(length_ref, query_ref, key_ref, value_ref, near_ref, out_ref, log_ref):
    length = length_ref[0]
    lanes = lane_half(QROWS)
    ones = jnp.ones((SEQ, TILE), BF)
    value_ext = jnp.concatenate([value_ref[...], ones], 1)
    for i in range(SEQ // QROWS):
        q_rows = query_ref[i * QROWS : (i + 1) * QROWS, :] * BF(0.125)
        outs, logs = [], []
        for h in range(2):
            keep = lanes if h == 0 else ~lanes
            q_half = jnp.where(keep, q_rows, BF(0))
            tiles = score_tiles(i, h, q_half, key_ref, near_ref[h, 0], near_ref[h, 1], length)
            top = tiles[0]
            for s in tiles[1:]:
                top = jnp.maximum(top, s)
            top = jnp.max(top, axis=1, keepdims=True)
            total = None
            for j, s in enumerate(tiles):
                p = jnp.exp(s - top).astype(BF)
                part = dot(p, value_ext[j * QROWS : (j + 1) * QROWS, :])
                total = part if total is None else total + part
            row_sum = total[:, TILE:]
            outs.append(total[:, :TILE] / row_sum)
            logs.append(top + jnp.log(row_sum))
        out_ref[i * QROWS : (i + 1) * QROWS, :] = jnp.where(lanes, outs[0], outs[1]).astype(BF)
        log_ref[i * QROWS : (i + 1) * QROWS, :] = jnp.where(lanes, logs[0], logs[1])


def attend(length, qkv, near):
    pairs = qkv.shape[1] // (3 * TILE)
    cols = pairs * TILE
    return pl.pallas_call(
        attend_kernel,
        grid=(pairs,),
        in_specs=[
            pl.BlockSpec(memory_space=pltpu.SMEM),
            pl.BlockSpec((SEQ, TILE), lambda p: (0, p)),
            pl.BlockSpec((SEQ, TILE), lambda p: (0, pairs + p)),
            pl.BlockSpec((SEQ, TILE), lambda p: (0, 2 * pairs + p)),
            pl.BlockSpec((2, 2, TILE, TILE), lambda p: (p, 0, 0, 0)),
        ],
        out_specs=[
            pl.BlockSpec((SEQ, TILE), lambda p: (0, p)),
            pl.BlockSpec((SEQ, TILE), lambda p: (0, p)),
        ],
        out_shape=[
            jax.ShapeDtypeStruct((SEQ, cols), BF),
            jax.ShapeDtypeStruct((SEQ, cols), F32),
        ],
        compiler_params=pltpu.CompilerParams(vmem_limit_bytes=40 * MIB),
        cost_estimate=SMALL_COST,
        name="attend",
    )(length, qkv, qkv, qkv, near)


def attend_back_kernel(
    length_ref, query_ref, key_ref, value_ref, near_ref, out_ref, log_ref, grad_ref,
    dq_ref, dk_ref, dv_ref, tile_ref, sum_ref, dk_acc, dv_acc,
):
    length = length_ref[0]
    lanes = lane_half(QROWS)
    lanes_all = lane_half(SEQ)
    ones = jnp.ones((SEQ, TILE), BF)
    key_ext = [
        jnp.concatenate([jnp.where(lanes_all, key_ref[...], BF(0)), ones], 1),
        jnp.concatenate([jnp.where(lanes_all, BF(0), key_ref[...]), ones], 1),
    ]
    near_sums = [[None, None], [None, None]]
    all_sums = [None, None]

    for i in range(SEQ // QROWS):
        rows = slice(i * QROWS, (i + 1) * QROWS)
        q_rows = query_ref[rows, :] * BF(0.125)
        g_rows = grad_ref[rows, :]
        mass = g_rows.astype(F32) * out_ref[rows, :].astype(F32)
        dq = None
        for h in range(2):
            keep = lanes if h == 0 else ~lanes
            q_half = jnp.where(keep, q_rows, BF(0))
            g_half = jnp.where(keep, g_rows, BF(0))
            delta = jnp.sum(jnp.where(keep, mass, 0.0), axis=1, keepdims=True)
            log_col = log_ref[rows, h * HEAD_DIM : h * HEAD_DIM + 1]
            tiles = score_tiles(i, h, q_half, key_ref, near_ref[h, 0], near_ref[h, 1], length)
            for j, s in enumerate(tiles):
                keys = slice(j * QROWS, (j + 1) * QROWS)
                p = jnp.exp(s - log_col)
                dp = dot(g_half, value_ref[keys, :], NT)
                ds = (p * (dp - delta)).astype(BF)
                part = dot(ds, key_ext[h][keys, :])
                dq = put(dq, part[:, :TILE])
                all_sums[h] = put(all_sums[h], jnp.sum(part[:, TILE:].reshape(QROWS // 8, 8, TILE), axis=0))
                dk_part = dot(ds, q_half, TN)
                dv_part = dot(p.astype(BF), g_half, TN)
                if i == j and h == 0:
                    dk_acc[keys, :] = dk_part
                    dv_acc[keys, :] = dv_part
                else:
                    dk_acc[keys, :] += dk_part
                    dv_acc[keys, :] += dv_part
                if j == i:
                    wide = ds.astype(F32)
                    near_sums[h][0] = put(near_sums[h][0], wide[:TILE, :TILE] + wide[TILE:, TILE:])
                    near_sums[h][1] = put(near_sums[h][1], wide[TILE:, :TILE])
                elif j == i - 1:
                    near_sums[h][1] = put(near_sums[h][1], ds[:TILE, TILE:].astype(F32))
        dq_ref[rows, :] = (dq * 0.125).astype(BF)
    dk_ref[...] = dk_acc[...].astype(BF)
    dv_ref[...] = dv_acc[...].astype(BF)
    for h in range(2):
        tile_ref[h, 0] = near_sums[h][0]
        tile_ref[h, 1] = near_sums[h][1]
        sum_ref[h] = all_sums[h]


def attend_back(length, qkv, near, mixed, logs, grad, first, count):
    pairs = qkv.shape[1] // (3 * TILE)
    cols = count * TILE
    col = pl.BlockSpec((SEQ, TILE), lambda p: (0, first + p))
    out = pl.BlockSpec((SEQ, TILE), lambda p: (0, p))
    return pl.pallas_call(
        attend_back_kernel,
        grid=(count,),
        in_specs=[
            pl.BlockSpec(memory_space=pltpu.SMEM),
            col,
            pl.BlockSpec((SEQ, TILE), lambda p: (0, pairs + first + p)),
            pl.BlockSpec((SEQ, TILE), lambda p: (0, 2 * pairs + first + p)),
            pl.BlockSpec((2, 2, TILE, TILE), lambda p: (first + p, 0, 0, 0)),
            col,
            col,
            col,
        ],
        out_specs=[
            out,
            out,
            out,
            pl.BlockSpec((2, 2, TILE, TILE), lambda p: (p, 0, 0, 0)),
            pl.BlockSpec((2, 8, TILE), lambda p: (p, 0, 0)),
        ],
        out_shape=[
            jax.ShapeDtypeStruct((SEQ, cols), BF),
            jax.ShapeDtypeStruct((SEQ, cols), BF),
            jax.ShapeDtypeStruct((SEQ, cols), BF),
            jax.ShapeDtypeStruct((2 * count, 2, TILE, TILE), F32),
            jax.ShapeDtypeStruct((2 * count, 8, TILE), F32),
        ],
        scratch_shapes=[pltpu.VMEM((SEQ, TILE), F32), pltpu.VMEM((SEQ, TILE), F32)],
        compiler_params=pltpu.CompilerParams(vmem_limit_bytes=40 * MIB),
        cost_estimate=SMALL_COST,
        name="attend_back",
    )(length, qkv, qkv, qkv, near, mixed, logs, grad)


def low_lanes(shape):
    return lax.broadcasted_iota(jnp.int32, shape, 1) < HEAD_DIM


def turned(tile):
    return pltpu.roll(tile, HEAD_DIM, 1)


def pack_kernel(q_ref, k_ref, v_ref, o_ref, one_ref, two_ref, router_ref, out_ref):
    shard = q_ref.shape[1]
    rows = q_ref.shape[0]
    source = lax.broadcasted_iota(jnp.int32, (shard, 6 * TILE), 0)
    target = lax.broadcasted_iota(jnp.int32, (shard, 6 * TILE), 1)

    def moved(pair_base, last_base):
        want = jnp.where(source < TILE, source + pair_base, source - TILE + last_base)
        return jnp.where(target == want, 1.0, 0.0).astype(BF)

    total = dot(v_ref[...], moved(0, 2 * TILE)) + dot(o_ref[...], moved(TILE, 2 * TILE + HEAD_DIM), TN)
    total = total + dot(q_ref[...], moved(3 * TILE, 5 * TILE)) + dot(k_ref[...], moved(4 * TILE, 5 * TILE + HEAD_DIM))
    out_ref[:, : 6 * TILE] = total.astype(BF)
    experts = router_ref.shape[0]
    own_row = lax.broadcasted_iota(jnp.int32, (rows, rows), 0) == lax.broadcasted_iota(jnp.int32, (rows, rows), 1)

    def column(ref):
        return jnp.sum(jnp.where(own_row, ref[...].astype(F32), 0.0), axis=1, keepdims=True)

    lanes = lax.broadcasted_iota(jnp.int32, (experts, TILE), 1)
    spread = jnp.where(lanes == lax.broadcasted_iota(jnp.int32, (experts, TILE), 0), 1.0, 0.0).astype(BF)
    place = lax.broadcasted_iota(jnp.int32, (rows, TILE), 1)
    small = dot(router_ref[...], spread, TN)
    small = jnp.where(place == experts, column(one_ref), jnp.where(place == experts + 1, column(two_ref), small))
    out_ref[:, 6 * TILE :] = small.astype(BF)


def pack_weights(query, key, value, output, one, two, router):
    rows = query.shape[0]
    return pl.pallas_call(
        pack_kernel,
        out_shape=jax.ShapeDtypeStruct((rows, 7 * TILE), BF),
        compiler_params=pltpu.CompilerParams(vmem_limit_bytes=60 * MIB),
        cost_estimate=SMALL_COST,
        name="pack_weights",
    )(query, key, value, output, one[None], two[None], router.T)


def qkv_kernel(micro_ref, tokens_ref, gain_ref, a_own, a_far, b_own, b_far, qkv_ref, normed_ref, weight_ref, output_ref):
    width = tokens_ref.shape[2]

    @pl.when(pl.program_id(0) == 0)
    def _():
        low = low_lanes((width, TILE))

        def tiles(own, far, pair, low_half):
            at = slice(pair * TILE, (pair + 1) * TILE)
            one, two = own[:, 2 * TILE :].astype(F32), far[:, 2 * TILE :].astype(F32)
            last = jnp.where(low, one, turned(two)) if low_half else jnp.where(low, turned(one), two)
            return own[:, at], far[:, at], last.astype(BF)

        for n, (own, far, pair, low_half) in enumerate(
            ((a_own, a_far, 0, True), (a_own, a_far, 1, False), (b_own, b_far, 0, True))
        ):
            for t, tile in enumerate(tiles(own[...], far[...], pair, low_half)):
                at = 3 * n + t
                weight_ref[:, at * TILE : (at + 1) * TILE] = tile
        for t, tile in enumerate(tiles(b_own[...], b_far[...], 1, False)):
            output_ref[:, t * TILE : (t + 1) * TILE] = tile

    x = tokens_ref[0].astype(F32)
    inverse = lax.rsqrt(jnp.mean(x * x, axis=-1, keepdims=True) + 1e-06)
    normed = (x * inverse * gain_ref[...]).astype(BF)
    normed_ref[...] = normed
    qkv_ref[...] = dot(normed, weight_ref[...]).astype(BF)


def norm_and_project(micro, layer_input, gain, a_own, a_far, b_own, b_far):
    width = layer_input.shape[2]
    block = 256
    cols = 3 * TILE
    whole = lambda rows, n: pl.BlockSpec((rows, n), lambda i, m: (0, 0))
    here = lambda n: pl.BlockSpec((block, n), lambda i, m: (i, 0))
    return pl.pallas_call(
        qkv_kernel,
        grid_spec=pltpu.PrefetchScalarGridSpec(
            num_scalar_prefetch=1,
            grid=(SEQ // block,),
            in_specs=[pl.BlockSpec((1, block, width), lambda i, m: (m[0], i, 0)), whole(1, width)] + [whole(width, cols)] * 4,
            out_specs=[here(3 * cols), here(width), whole(width, 3 * cols), whole(width, cols)],
        ),
        out_shape=[
            jax.ShapeDtypeStruct((SEQ, 3 * cols), BF),
            jax.ShapeDtypeStruct((SEQ, width), BF),
            jax.ShapeDtypeStruct((width, 3 * cols), BF),
            jax.ShapeDtypeStruct((width, cols), BF),
        ],
        compiler_params=pltpu.CompilerParams(vmem_limit_bytes=40 * MIB),
        cost_estimate=SMALL_COST,
        name="norm_and_project",
    )(micro, layer_input, gain, a_own, a_far, b_own, b_far)


def middle_kernel(micro_ref, tokens_ref, mixed_ref, other_ref, own_ref, far_ref, gain_ref, residual_ref, normed_ref):
    total = tokens_ref[0].astype(F32) + dot(mixed_ref[...], own_ref[...], NT) + dot(other_ref[...], far_ref[...], NT)
    residual_ref[...] = total
    inverse = lax.rsqrt(jnp.mean(total * total, axis=-1, keepdims=True) + 1e-06)
    normed_ref[...] = (total * inverse * gain_ref[...]).astype(BF)


def residual_and_norm(micro, layer_input, mixed, other, output_own, output_far, gain):
    width = layer_input.shape[2]
    block = 256
    cols = mixed.shape[1]
    whole = lambda rows, n: pl.BlockSpec((rows, n), lambda i, m: (0, 0))
    here = lambda n: pl.BlockSpec((block, n), lambda i, m: (i, 0))
    return pl.pallas_call(
        middle_kernel,
        grid_spec=pltpu.PrefetchScalarGridSpec(
            num_scalar_prefetch=1,
            grid=(SEQ // block,),
            in_specs=[
                pl.BlockSpec((1, block, width), lambda i, m: (m[0], i, 0)),
                here(cols), here(cols), whole(width, cols), whole(width, cols), whole(1, width),
            ],
            out_specs=[here(width), here(width)],
        ),
        out_shape=[jax.ShapeDtypeStruct((SEQ, width), F32), jax.ShapeDtypeStruct((SEQ, width), BF)],
        compiler_params=pltpu.CompilerParams(vmem_limit_bytes=40 * MIB),
        cost_estimate=SMALL_COST,
        name="residual_and_norm",
    )(micro, layer_input, mixed, other, output_own, output_far, gain)


def picked_rows(first, second, segments):
    total = None
    start = 0
    for rows in segments:
        length = rows.shape[0]
        ids = lax.broadcasted_iota(jnp.int32, (1, length), 1) + start
        hot = jnp.where((first == ids) | (second == ids), 1.0, 0.0).astype(BF)
        total = put(total, dot(hot, rows))
        start += length
    return total


def put(a, b):
    return b if a is None else a + b


def folded(product):
    return jnp.sum(product.reshape(product.shape[0] // 8, 8, product.shape[1]), axis=0)


def as_column(eight):
    ones = jnp.ones((16, TILE), BF)
    high = eight.astype(BF)
    rest = (eight - high.astype(F32)).astype(BF)
    return dot(jnp.concatenate([high, rest], 0), ones, TN)


def combine_kernel(experts, half, spare, micro_ref, core_ref, length_ref, *refs):
    info_ref, grad_ref, residual_ref, mixed_ref, gain_ref, router_ref, output_ref = refs[:7]
    backs = refs[7:-9]
    (total_ref, mixed_grad_ref, extra_ref, far_ref, own_ref, acc_ref, router_acc, gain_acc, tables) = refs[-9:]
    block = residual_ref.shape[0]
    step = pl.program_id(0)
    count = len(backs) // 2

    @pl.when(step == 0)
    def _():
        place = lax.broadcasted_iota(jnp.int32, (experts, 1), 0)
        for n, back in enumerate((backs[count - 1], backs[2 * count - 1])):
            table = jnp.zeros((experts, back.shape[2]), F32)
            for e in range(experts):
                row = back[e, spare : spare + 16, :].astype(F32)[:1]
                table = jnp.where(place == e, row, table)
            for piece in range(3):
                at = (3 * n + piece) * experts
                tables[at : at + experts] = table[:, piece * half : (piece + 1) * half]

    info = jnp.transpose(info_ref[...])
    number = lambda n: info[:, n : n + 1]
    columns = lax.broadcasted_iota(jnp.int32, (1, half), 1)
    lanes = lax.broadcasted_iota(jnp.int32, (1, 6 * experts), 1)
    table = tables[...].astype(BF)
    values = []
    for k in range(2):
        slot = number(4 + k)
        hot = jnp.where(columns == lax.rem(slot, half), 1.0, 0.0).astype(BF)
        found = dot(hot, table, NT)
        wanted = jnp.where(slot // half == core_ref[0], 0, 3 * experts) + number(2 + k)
        away = lanes - wanted
        hit = (away == 0) | (away == experts) | (away == 2 * experts)
        values.append(jnp.sum(jnp.where(hit, found, 0.0), axis=1, keepdims=True))
    wide = lax.broadcasted_iota(jnp.int32, (1, TILE), 1)
    is_first, is_second = wide == number(2), wide == number(3)
    residual = residual_ref[...]
    gain = gain_ref[...]
    inverse = lax.rsqrt(jnp.mean(residual * residual, axis=-1, keepdims=True) + 1e-06)
    plain = residual * inverse
    normed = (plain * gain).astype(BF)
    logits = dot(normed, router_ref[...])
    gap = jnp.sum(jnp.where(is_first, logits, 0.0) - jnp.where(is_second, logits, 0.0), axis=1, keepdims=True)
    small = jnp.exp(-jnp.abs(gap))
    logit = small / ((1.0 + small) * (1.0 + small)) * (values[0] - values[1])
    logit_grad = jnp.where(is_first, logit, jnp.where(is_second, -logit, 0.0)).astype(BF)
    segments = [b[...].reshape(b.shape[0] * b.shape[1], b.shape[2]) for b in backs]
    normed_grad = picked_rows(number(0), number(1), segments) + dot(logit_grad, router_ref[...], NT)
    scaled = normed_grad * gain
    mean = jnp.mean(scaled * plain, axis=-1, keepdims=True)
    place = lax.broadcasted_iota(jnp.int32, (block, 1), 0) + step * block
    grad_out = jnp.where(place < length_ref[0], grad_ref[0].astype(F32), 0.0)
    total = grad_out + inverse * (scaled - plain * mean)
    total_ref[...] = total
    branch = total.astype(BF)
    mixed_grad_ref[...] = dot(branch, output_ref[...]).astype(BF)
    router_part = dot(logit_grad, normed, TN)
    gain_part = folded(normed_grad * plain)
    output_part = dot(mixed_ref[...], branch, TN)

    @pl.when(step == 0)
    def _():
        router_acc[...] = router_part
        gain_acc[...] = gain_part
        acc_ref[...] = output_part

    @pl.when(step > 0)
    def _():
        router_acc[...] += router_part
        gain_acc[...] += gain_part
        acc_ref[...] += output_part

    @pl.when(step == pl.num_programs(0) - 1)
    def _():
        extra_ref[...] = jnp.transpose(router_acc[...]) + jnp.where(wide == experts + 1, as_column(gain_acc[...]), 0.0)
        parts = jnp.transpose(acc_ref[...])
        far_ref[...] = parts[:, TILE:].astype(BF)
        own_ref[:, :TILE] = parts[:, :TILE]
        own_ref[:, TILE:] = parts[:, 2 * TILE :]


def combine(micro, core, length, info, out_grad, residual, mixed, gain, router, output_own, backs, half, spare):
    width = residual.shape[1]
    block = 512
    cols = mixed.shape[1]
    whole = lambda arr: pl.BlockSpec(arr.shape, lambda i, *_: (0,) * arr.ndim)
    fixed = lambda rows, n: pl.BlockSpec((rows, n), lambda i, *_: (0, 0))
    here = lambda n: pl.BlockSpec((block, n), lambda i, *_: (i, 0))
    experts = backs[0].shape[0]
    return pl.pallas_call(
        functools.partial(combine_kernel, experts, half, spare),
        grid_spec=pltpu.PrefetchScalarGridSpec(
            num_scalar_prefetch=3,
            grid=(SEQ // block,),
            in_specs=[
                pl.BlockSpec((8, block), lambda i, *_: (0, i)),
                pl.BlockSpec((1, block, width), lambda i, m, *_: (m[0], i, 0)),
                here(width), here(cols), whole(gain), whole(router), whole(output_own),
            ]
            + [whole(x) for x in backs],
            out_specs=[here(width), here(cols), fixed(width, TILE), fixed(width, 2 * TILE), fixed(width, 2 * TILE)],
            scratch_shapes=[
                pltpu.VMEM((cols, width), F32),
                pltpu.VMEM((TILE, width), F32),
                pltpu.VMEM((8, width), F32),
                pltpu.VMEM((6 * experts, half), F32),
            ],
        ),
        out_shape=[
            jax.ShapeDtypeStruct((SEQ, width), F32),
            jax.ShapeDtypeStruct((SEQ, cols), BF),
            jax.ShapeDtypeStruct((width, TILE), F32),
            jax.ShapeDtypeStruct((width, 2 * TILE), BF),
            jax.ShapeDtypeStruct((width, 2 * TILE), F32),
        ],
        compiler_params=pltpu.CompilerParams(vmem_limit_bytes=40 * MIB),
        cost_estimate=SMALL_COST,
        name="combine",
    )(micro, core, length, info, out_grad, residual, mixed, gain, router, output_own, *backs)


def attention_weight_kernel(normed_ref, q_ref, k_ref, v_ref, output_ref, far_ref, own_ref):
    rows = normed_ref.shape[1]
    low = low_lanes((rows, TILE))
    q, k, v = (dot(normed_ref[...], d[...], TN) for d in (q_ref, k_ref, v_ref))
    for n, part in enumerate((q, k, v)):
        own_ref[:, n * TILE : (n + 1) * TILE] = part[:, :TILE]
        far_ref[:, n * TILE : (n + 1) * TILE] = part[:, TILE : 2 * TILE].astype(BF)
    q, k, v = (part[:, 2 * TILE :] for part in (q, k, v))
    far_ref[:, 3 * TILE : 4 * TILE] = jnp.where(low, turned(q), k).astype(BF)
    far_ref[:, 4 * TILE : 5 * TILE] = jnp.where(low, turned(v), output_ref[:, TILE:].astype(F32)).astype(BF)
    far_ref[:, 5 * TILE :] = output_ref[:, :TILE]
    own_ref[:, 3 * TILE : 4 * TILE] = jnp.where(low, q, turned(k))
    own_ref[:, 4 * TILE :] = jnp.where(low, v, 0.0)


def attention_weight_grads(normed, q, k, v, output):
    width = normed.shape[1]
    block = 256
    whole = lambda arr: pl.BlockSpec(arr.shape, lambda i: (0, 0))
    here = lambda n: pl.BlockSpec((block, n), lambda i: (i, 0))
    return pl.pallas_call(
        attention_weight_kernel,
        grid=(width // block,),
        in_specs=[pl.BlockSpec((SEQ, block), lambda i: (0, i)), whole(q), whole(k), whole(v), here(2 * TILE)],
        out_specs=[here(6 * TILE), here(5 * TILE)],
        out_shape=[jax.ShapeDtypeStruct((width, 6 * TILE), BF), jax.ShapeDtypeStruct((width, 5 * TILE), F32)],
        compiler_params=pltpu.CompilerParams(vmem_limit_bytes=40 * MIB),
        cost_estimate=SMALL_COST,
        name="attention_weight_grads",
    )(normed, q, k, v, output)


def projected_back(weight_ref, grads):
    total = None
    for n, grad in enumerate(grads):
        cols = grad.shape[1]
        total = put(total, dot(grad[...], weight_ref[:, n * cols : (n + 1) * cols], NT))
    return total


def sent_kernel(core_ref, weight_ref, q, k, v, out_ref):
    out_ref[...] = projected_back(weight_ref, (q, k, v))


def sent_half(core, weight, grads):
    width = weight.shape[0]
    block = 256
    here = lambda n: pl.BlockSpec((block, n), lambda i, c: ((1 - c[0]) * 2 + i, 0))
    return pl.pallas_call(
        sent_kernel,
        grid_spec=pltpu.PrefetchScalarGridSpec(
            num_scalar_prefetch=1,
            grid=(2,),
            in_specs=[pl.BlockSpec(weight.shape, lambda i, c: (0, 0))] + [here(grads[0].shape[1])] * 3,
            out_specs=pl.BlockSpec((block, width), lambda i, c: (i, 0)),
        ),
        out_shape=jax.ShapeDtypeStruct((2 * block, width), F32),
        compiler_params=pltpu.CompilerParams(vmem_limit_bytes=40 * MIB),
        cost_estimate=SMALL_COST,
        name="sent_half",
    )(core, weight, *grads)


def both_kernel(
    lane, micro_ref, core_ref, length_ref, weight_ref, q, k, v, got_ref, tokens_ref, gain_ref, grad_ref,
    info_ref, residual_ref, own_ref, far_ref, out_ref, extra_ref, acc_ref,
):
    block = residual_ref.shape[0]
    info = jnp.transpose(info_ref[...])
    place = lax.broadcasted_iota(jnp.int32, (block, 1), 0) + (core_ref[0] * 2 + pl.program_id(0)) * block
    rows = residual_ref[...] + picked_rows(info[:, 6:7], info[:, 7:8], (own_ref[...], far_ref[...]))
    out_ref[0] = jnp.where(place < length_ref[0], rows, 0.0).astype(BF)
    normed_grad = got_ref[...] + projected_back(weight_ref, (q, k, v))
    x = tokens_ref[0].astype(F32)
    inverse = lax.rsqrt(jnp.mean(x * x, axis=-1, keepdims=True) + 1e-06)
    plain = x * inverse
    scaled = normed_grad * gain_ref[...]
    mean = jnp.mean(scaled * plain, axis=-1, keepdims=True)
    out_ref[1] = (grad_ref[...] + inverse * (scaled - plain * mean)).astype(BF)
    wide = lax.broadcasted_iota(jnp.int32, (1, TILE), 1)
    part = folded(normed_grad * plain)

    @pl.when(pl.program_id(0) == 0)
    def _():
        acc_ref[...] = part

    @pl.when(pl.program_id(0) == 1)
    def _():
        extra_ref[...] = jnp.where(wide == lane, as_column(acc_ref[...] + part), 0.0)


def both_rows(lane, micro, core, length, weight, grads, got, layer_input, gain, residual_grad, info, residual, own, far):
    width = weight.shape[0]
    block = 256
    here = lambda n: pl.BlockSpec((block, n), lambda i, m, c, *_: (c[0] * 2 + i, 0))
    whole = lambda arr: pl.BlockSpec(arr.shape, lambda i, *_: (0, 0))
    return pl.pallas_call(
        functools.partial(both_kernel, lane),
        grid_spec=pltpu.PrefetchScalarGridSpec(
            num_scalar_prefetch=3,
            grid=(2,),
            in_specs=[whole(weight)]
            + [here(grads[0].shape[1])] * 3
            + [
                pl.BlockSpec((block, width), lambda i, *_: (i, 0)),
                pl.BlockSpec((1, block, width), lambda i, m, c, *_: (m[0], c[0] * 2 + i, 0)),
                whole(gain),
                here(width),
                pl.BlockSpec((8, block), lambda i, m, c, *_: (0, c[0] * 2 + i)),
                here(width),
                whole(own),
                whole(far),
            ],
            out_specs=[
                pl.BlockSpec((2, block, width), lambda i, *_: (0, i, 0)),
                pl.BlockSpec((width, TILE), lambda i, *_: (0, 0)),
            ],
            scratch_shapes=[pltpu.VMEM((8, width), F32)],
        ),
        out_shape=[jax.ShapeDtypeStruct((2, 2 * block, width), BF), jax.ShapeDtypeStruct((width, TILE), F32)],
        compiler_params=pltpu.CompilerParams(vmem_limit_bytes=40 * MIB),
        cost_estimate=SMALL_COST,
        name="both_rows",
    )(micro, core, length, weight, *grads, got, layer_input, gain, residual_grad, info, residual, own, far)


def sum_kernel(kept, own, got, out_own, early, late, late_far, table, sum_ref):
    low = low_lanes(early.shape)
    sum_ref[:, : 4 * TILE] = (own[:, : 4 * TILE] + got[:, : 4 * TILE].astype(F32)).astype(BF)
    mixed = jnp.where(low, own[:, 4 * TILE :], turned(out_own[:, TILE:]))
    sum_ref[:, 4 * TILE : 5 * TILE] = (mixed + got[:, 4 * TILE : 5 * TILE].astype(F32)).astype(BF)
    sum_ref[:, 5 * TILE : 6 * TILE] = (out_own[:, :TILE] + got[:, 5 * TILE :].astype(F32)).astype(BF)
    extra = early[...] + late[...] + late_far[...] + table[...]
    high = extra.astype(BF)
    rest = extra - high.astype(F32)
    if kept <= HEAD_DIM:
        sum_ref[:, 6 * TILE :] = jnp.where(low, high.astype(F32), turned(rest)).astype(BF)
    else:
        sum_ref[:, 6 * TILE : 7 * TILE] = high
        sum_ref[:, 7 * TILE :] = rest.astype(BF)


def packed_sums(kept, *parts):
    width = parts[0].shape[0]
    cols = (7 if kept <= HEAD_DIM else 8) * TILE
    block = 256
    here = lambda n: pl.BlockSpec((block, n), lambda i: (i, 0))
    return pl.pallas_call(
        functools.partial(sum_kernel, kept),
        grid=(width // block,),
        in_specs=[here(x.shape[1]) for x in parts],
        out_specs=here(cols),
        out_shape=jax.ShapeDtypeStruct((width, cols), BF),
        compiler_params=pltpu.CompilerParams(vmem_limit_bytes=40 * MIB),
        cost_estimate=SMALL_COST,
        name="packed_sums",
    )(*parts)


def final_kernel(kept, parts_ref, q_ref, k_ref, v_ref, o_ref, small_ref):
    total = parts_ref[0].astype(F32)
    for n in range(1, parts_ref.shape[0]):
        total = total + parts_ref[n].astype(F32)
    tile = lambda t: total[:, t * TILE : (t + 1) * TILE]
    q_ref[:, :TILE] = tile(0)
    q_ref[:, TILE:] = tile(3)[:, :HEAD_DIM]
    k_ref[:, :TILE] = tile(1)
    k_ref[:, TILE:] = turned(tile(3))[:, :HEAD_DIM]
    v_ref[:, :TILE] = tile(2)
    v_ref[:, TILE:] = tile(4)[:, :HEAD_DIM]
    o_ref[:, :TILE] = tile(5)
    o_ref[:, TILE:] = turned(tile(4))[:, :HEAD_DIM]
    small_ref[...] = tile(6) + (turned(tile(6)) if kept <= HEAD_DIM else tile(7))


def final_sums(kept, parts, shard):
    rows = parts.shape[1]
    return pl.pallas_call(
        functools.partial(final_kernel, kept),
        out_shape=[jax.ShapeDtypeStruct((rows, shard), F32)] * 4 + [jax.ShapeDtypeStruct((rows, TILE), F32)],
        compiler_params=pltpu.CompilerParams(vmem_limit_bytes=40 * MIB),
        cost_estimate=SMALL_COST,
        name="final_sums",
    )(parts)


def pair_gate(logits, own, other):
    lanes = lax.broadcasted_iota(jnp.int32, logits.shape, 1)
    gap = jnp.sum(
        jnp.where(lanes == own, logits, 0.0) - jnp.where(lanes == other, logits, 0.0), axis=1, keepdims=True
    )
    small = jnp.exp(-jnp.abs(gap))
    return jnp.where(gap >= 0.0, 1.0, small) / (1.0 + small)


def expert_kernel(lead, chunk, half, me_ref, partner_ref, rows_ref, grads_ref, router_ref, *refs):
    before, refs = (refs[0], refs[1:]) if lead is not None and lead > 0 else (None, refs)
    a0, a1, a2, a3, b0, b1, b2, b3, back_ref, active_ref, slope_ref, gated_ref, gate_ref, mass_ref = refs
    rows = rows_ref[...]
    grads = grads_ref[...]
    gate = pair_gate(dot(rows, router_ref[...]), me_ref[0], partner_ref[...])
    gated_ref[...] = (gate * grads.astype(F32)).astype(BF)
    gate_ref[...] = jnp.broadcast_to(gate, gate_ref.shape)
    mass = None
    back = None
    step = 256
    for r, (first, second) in enumerate(((a0, b0), (a1, b1), (a2, b2), (a3, b3))):
        width = first.shape[1]
        for c in range(0, width, step):
            x = dot(rows, first[:, c : c + step])
            plain = dot(grads, second[c : c + step, :], NT)
            square = x * x
            bent = jnp.tanh(x * (GELU_C + (GELU_C * GELU_A) * square))
            rise = 0.5 + 0.5 * bent
            active = x * rise
            slope = rise + active * (1.0 - bent) * (GELU_C + (3.0 * GELU_C * GELU_A) * square)
            low = active.astype(BF)
            place = slice(r * width + c, r * width + c + step)
            active_ref[:, place] = low
            slope_ref[:, place] = (gate * plain * slope).astype(BF)
            part = low.astype(F32) * plain
            mass = put(mass, part[:, :TILE] + part[:, TILE:])
        back = put(back, dot(slope_ref[:, r * width : (r + 1) * width], first[...], NT))
    back = back.astype(BF)
    mass = jnp.sum(mass, axis=1, keepdims=True)
    if lead is None:
        back_ref[...] = back
        mass_ref[...] = jnp.broadcast_to(mass, mass_ref.shape)
        return
    count = rows.shape[0] // chunk
    number = lax.broadcasted_iota(jnp.int32, (rows.shape[0], 1), 0)
    lanes = lax.broadcasted_iota(jnp.int32, (1, rows.shape[1]), 1)
    inside = lax.rem(number, chunk)
    spread = jnp.zeros(rows.shape, F32)
    for piece in range(3):
        high = mass.astype(BF).astype(F32)
        spread = jnp.where(lanes == piece * half + lead + inside, high, spread)
        mass = mass - high
    own = jnp.where(number // chunk == lax.broadcasted_iota(jnp.int32, (1, TILE), 1), 1.0, 0.0).astype(BF)
    line = dot(own, spread.astype(BF), TN)
    if before is None:
        back_ref[...] = back
        for e in range(count):
            mass_ref[e] = line[e : e + 1].astype(BF)
    else:
        back_ref[:, :chunk] = back.reshape(count, chunk, back.shape[1])
        row = lax.broadcasted_iota(jnp.int32, (16, 1), 0)
        for e in range(count):
            both = line[e : e + 1] + before[e].astype(F32)
            back_ref[e, chunk:] = jnp.where(row == 0, both, 0.0).astype(BF)


def row_block(total):
    return 320 if total % 320 == 0 else total


def expert_rows_pass(lead, chunk, half, me, partner, rows, grads, router, before, firsts, seconds):
    total, width = rows.shape
    block = row_block(total)
    experts = total // chunk
    hidden = sum(f.shape[1] for f in firsts)
    here = lambda cols: pl.BlockSpec((block, cols), lambda i: (i, 0))
    whole = lambda arr: pl.BlockSpec(arr.shape, lambda i: (0, 0))
    lines = pl.BlockSpec((block // chunk, 1, width), lambda i: (i, 0, 0))
    back_shape, back_spec = (total, width), here(width)
    mass_shape, mass_spec, mass_kind = (experts, 1, width), lines, BF
    if lead is None:
        mass_shape, mass_spec, mass_kind = (total, TILE), here(TILE), F32
    elif before is not None:
        back_shape = (experts, chunk + 16, width)
        back_spec = pl.BlockSpec((block // chunk, chunk + 16, width), lambda i: (i, 0, 0))
    return pl.pallas_call(
        functools.partial(expert_kernel, lead, chunk, half),
        grid=(total // block,),
        in_specs=[pl.BlockSpec(memory_space=pltpu.SMEM), here(1), here(width), here(width), whole(router)]
        + ([lines] if before is not None else [])
        + [whole(w) for w in firsts]
        + [whole(w) for w in seconds],
        out_specs=[back_spec, here(hidden), here(hidden), here(width), here(TILE), mass_spec],
        out_shape=[
            jax.ShapeDtypeStruct(back_shape, BF),
            jax.ShapeDtypeStruct((total, hidden), BF),
            jax.ShapeDtypeStruct((total, hidden), BF),
            jax.ShapeDtypeStruct((total, width), BF),
            jax.ShapeDtypeStruct((total, TILE), F32),
            jax.ShapeDtypeStruct(mass_shape, mass_kind),
        ],
        compiler_params=pltpu.CompilerParams(vmem_limit_bytes=56 * MIB),
        cost_estimate=SMALL_COST,
        name="expert_rows",
    )(me, partner, rows, grads, router, *([before] if before is not None else []), *firsts, *seconds)


def expert_rest_kernel(count, *refs):
    rows, slopes, active, gated, gates = (refs[n * count : (n + 1) * count] for n in range(5))
    seconds = refs[5 * count : 5 * count + 4]
    cross_ref, kept_ref, result_ref, total = refs[5 * count + 4 :]
    step = pl.program_id(0)
    first, second = None, None
    for n in range(count):
        first = put(first, dot(rows[n][...], slopes[n][...], TN))
        second = put(second, dot(active[n][...], gated[n][...], TN))

    @pl.when(step < 2)
    def _():
        cross_ref[0, 0] = first.astype(BF)
        cross_ref[0, 1] = second.astype(BF)

    @pl.when(step >= 2)
    def _():
        kept_ref[0, 0] = first
        kept_ref[0, 1] = second

    for k in range(4):

        @pl.when(step == k)
        def _(k=k):
            for n in range(count):
                part = dot(active[n][...], seconds[QUARTERS[k]][...])
                if k == 0:
                    total[n] = part
                elif k < 3:
                    total[n] += part
                else:
                    out = ((total[n] + part) * gates[n][:, :1]).astype(BF)
                    if count > 1:
                        result_ref[:, n] = out.reshape(result_ref.shape[0], result_ref.shape[2], result_ref.shape[3])
                    else:
                        result_ref[...] = out


QUARTERS = (2, 3, 1, 0)


def expert_rest(rows, slopes, active, gated, gates, seconds, experts):
    total, width = rows[0].shape
    hidden = slopes[0].shape[1] // 4
    count = len(rows)
    chunk = total // experts
    whole = lambda cols: pl.BlockSpec((total, cols), lambda i: (0, 0))
    part = pl.BlockSpec((total, hidden), lambda i: (0, jnp.where(i < 2, 2 + i, 3 - i)))
    shape = (experts, count, chunk, width) if count > 1 else (total, width)
    out = pl.pallas_call(
        functools.partial(expert_rest_kernel, count),
        grid=(4,),
        in_specs=[whole(width)] * count
        + [part] * (2 * count)
        + [whole(width)] * count
        + [whole(TILE)] * count
        + [pl.BlockSpec(w.shape, lambda i: (0, 0)) for w in seconds],
        out_specs=[
            pl.BlockSpec((1, 2, width, hidden), lambda i: (jnp.minimum(i, 1), 0, 0, 0)),
            pl.BlockSpec((1, 2, width, hidden), lambda i: (jnp.maximum(i, 2) - 2, 0, 0, 0)),
            pl.BlockSpec(shape, lambda i: (0,) * len(shape)),
        ],
        out_shape=[
            jax.ShapeDtypeStruct((2, 2, width, hidden), BF),
            jax.ShapeDtypeStruct((2, 2, width, hidden), F32),
            jax.ShapeDtypeStruct(shape, BF),
        ],
        scratch_shapes=[pltpu.VMEM((count, total, width), F32)],
        compiler_params=pltpu.CompilerParams(vmem_limit_bytes=60 * MIB),
        cost_estimate=SMALL_COST,
        name="expert_rest",
    )(*rows, *slopes, *active, *gated, *gates, *seconds)
    return out[0], out[1], out[2].reshape(experts, count * chunk, width)


def cross_sum_kernel(kept_ref, got_ref, out_ref):
    out_ref[...] = (kept_ref[0] + got_ref[0].astype(F32)).astype(BF)


def cross_sums(kept, got):
    _, _, width, hidden = kept.shape
    block = 256
    return pl.pallas_call(
        cross_sum_kernel,
        grid=(width // block,),
        in_specs=[
            pl.BlockSpec((1, 2, block, hidden), lambda i: (0, 0, i, 0)),
            pl.BlockSpec((1, 2, block, hidden), lambda i: (1, 0, i, 0)),
        ],
        out_specs=pl.BlockSpec((2, block, hidden), lambda i: (0, i, 0)),
        out_shape=jax.ShapeDtypeStruct((2, width, hidden), BF),
        compiler_params=pltpu.CompilerParams(vmem_limit_bytes=40 * MIB),
        cost_estimate=SMALL_COST,
        name="cross_sums",
    )(kept, got)


def last_sum_kernel(kept_ref, core_ref, y_ref, out_first, out_second):
    for n, out in enumerate((out_first, out_second)):
        out[...] = kept_ref[0, n] + core_ref[0, n].astype(F32) + y_ref[n].astype(F32)


def last_sums(kept, got_core, got_y):
    _, _, width, hidden = kept.shape
    block = 256
    here = pl.BlockSpec((block, hidden), lambda i: (i, 0))
    return pl.pallas_call(
        last_sum_kernel,
        grid=(width // block,),
        in_specs=[
            pl.BlockSpec((1, 2, block, hidden), lambda i: (1, 0, i, 0)),
            pl.BlockSpec((1, 2, block, hidden), lambda i: (0, 0, i, 0)),
            pl.BlockSpec((2, block, hidden), lambda i: (0, i, 0)),
        ],
        out_specs=[here, here],
        out_shape=[jax.ShapeDtypeStruct((width, hidden), F32)] * 2,
        compiler_params=pltpu.CompilerParams(vmem_limit_bytes=40 * MIB),
        cost_estimate=SMALL_COST,
        name="last_sums",
    )(kept, got_core, got_y)


def send_kernel(micro_ref, code_ref, rows_ref, out_ref):
    block = out_ref.shape[0]
    ids = lax.broadcasted_iota(jnp.int32, (block, 1), 0) + pl.program_id(0) * block
    hot = jnp.where((ids == code_ref[:1]) | (ids == code_ref[1:2]), 1.0, 0.0).astype(BF)
    out_ref[...] = dot(hot, rows_ref[0]).astype(BF)


def send_rows(micro, code, rows, count):
    width = rows.shape[2]
    block = next(b for b in (336, 320, 384, count) if count % b == 0)
    return pl.pallas_call(
        send_kernel,
        grid_spec=pltpu.PrefetchScalarGridSpec(
            num_scalar_prefetch=1,
            grid=(count // block,),
            in_specs=[
                pl.BlockSpec(code.shape, lambda i, m: (0, 0)),
                pl.BlockSpec((1, SEQ, width), lambda i, m: (m[0], 0, 0)),
            ],
            out_specs=pl.BlockSpec((block, width), lambda i, m: (i, 0)),
        ),
        out_shape=jax.ShapeDtypeStruct((count, width), BF),
        compiler_params=pltpu.CompilerParams(vmem_limit_bytes=40 * MIB),
        cost_estimate=SMALL_COST,
        name="send_rows",
    )(micro, code, rows)


def place_kernel(place_ref, *refs):
    for n, piece in enumerate(refs[:4]):

        @pl.when(pl.program_id(0) == n)
        def _(piece=piece):
            for k, out_ref in enumerate(refs[4:]):
                out_ref[0] = piece[k]


def place_pieces(places, pieces):
    two, rows, width = pieces[0].shape
    whole = pl.BlockSpec(pieces[0].shape, lambda i, place_ref: (0, 0, 0))
    return pl.pallas_call(
        place_kernel,
        grid_spec=pltpu.PrefetchScalarGridSpec(
            num_scalar_prefetch=1,
            grid=(4,),
            in_specs=[whole] * 4,
            out_specs=[pl.BlockSpec((1, rows, width), lambda i, place_ref: (place_ref[i], 0, 0))] * two,
        ),
        out_shape=[jax.ShapeDtypeStruct((4, rows, width), pieces[0].dtype)] * two,
        compiler_params=pltpu.CompilerParams(vmem_limit_bytes=40 * MIB),
        cost_estimate=SMALL_COST,
        name="place_pieces",
    )(places, *pieces)


def swap(value, axis, count, bit):
    return lax.ppermute(value, axis, [(i, i ^ bit) for i in range(count)])


def all_to_all(value):
    return lax.all_to_all(value, "dp", split_axis=0, concat_axis=0, tiled=True)


def together(*values):
    return lax.optimization_barrier(values)


def local(
    layer_input, out_grad, first_gain, query_weight, key_weight, value_weight, output_weight,
    position_bias, second_gain, router_weight, expert_in, expert_out, seq_lengths, routes,
):
    micro_count, tok_rows, width = layer_input.shape
    dp_count = lax.axis_size("dp")
    expert_count = router_weight.shape[1]
    shard = query_weight.shape[1]
    heads_here = position_bias.shape[0]
    assert lax.axis_size("tensor") == 4 and micro_count == 2 and expert_count == dp_count
    assert tok_rows == SEQ and seq_lengths.shape[1] == 1
    capacity = max(8, 8 * (10 * tok_rows // (32 * expert_count)))
    half = capacity // 2
    stride = 8 * (half // 8 + 1)
    chunks = 2 if half % 32 == 0 else 1
    chunk = half // chunks
    chunk_rows = expert_count * chunk
    rows_here = query_weight.shape[0]
    me = lax.axis_index("dp")
    rank = lax.axis_index("tensor")
    micro = rank // 2
    core = rank % 2

    def swap_y(value):
        return swap(value, "tensor", 4, 2)

    def swap_core(value):
        return swap(value, "tensor", 4, 1)

    micro_arg = micro.reshape(1).astype(jnp.int32)
    core_arg = core.reshape(1).astype(jnp.int32)

    packed = pack_weights(query_weight, key_weight, value_weight, output_weight, first_gain, second_gain, router_weight)
    three = 3 * TILE

    def doubled(stacked, bit, axis=0):
        other = swap(stacked, "dp", dp_count, bit)
        high = (me & bit) != 0
        pair = jnp.where(high, jnp.stack([other, stacked], axis + 1), jnp.stack([stacked, other], axis + 1))
        return pair.reshape(stacked.shape[:axis] + (-1,) + stacked.shape[axis + 1 :])

    stacked = packed[None]
    bit = dp_count // 2
    while bit > 1:
        stacked = doubled(stacked, bit)
        if bit == dp_count // 2:
            stacked, routes, position_bias = together(stacked, routes, position_bias)
        bit //= 2
    length = lax.dynamic_index_in_dim(seq_lengths, micro, 0, keepdims=False)
    route = lax.dynamic_index_in_dim(routes, micro, 0, keepdims=False).T
    expert_ids = jnp.arange(expert_count, dtype=jnp.int32)
    named = (expert_ids[:, None, None] == route[None]).astype(jnp.int32)
    per_token = jnp.sum(named, axis=1, dtype=jnp.int32)
    earlier = jnp.cumsum(per_token, axis=1, dtype=jnp.int32) - per_token
    slot = jnp.sum(named * earlier[:, None, :], axis=0, dtype=jnp.int32)
    here = slot // half == core
    within = slot % half
    chunk_of = within // chunk
    inside = within % chunk
    spare = 16 * -(-chunk // 16)
    last_stride = spare + 16
    last = (chunks - 1) * chunk_rows
    code_back = jnp.where(
        chunk_of == chunks - 1, last + route * last_stride + inside, chunk_of * chunk_rows + route * chunk + inside
    )
    code_back = code_back + jnp.where(here, 0, last + expert_count * last_stride)
    code_result = route * half + within + jnp.where(here, 0, expert_count * half)
    info = jnp.concatenate([code_back, route, slot, code_result], 0)

    code_grads = jnp.where(here, route * stride + within, -1)
    stacked, code_grads = together(stacked, code_grads)
    valid = jnp.arange(SEQ, dtype=jnp.int32) < length[0]
    ids = jnp.arange(expert_count * stride, dtype=jnp.int32)[:, None]
    partner = jnp.sum(
        jnp.where(ids == code_grads[:1], route[1:], 0) + jnp.where(ids == code_grads[1:], route[:1], 0), axis=1, dtype=jnp.int32
    )
    grads_sent = send_rows(micro_arg, jnp.where(valid[None], code_grads, -1), out_grad, expert_count * stride)
    grads_sent = grads_sent.reshape(expert_count, stride, width)
    partner_row = jnp.pad(partner.reshape(expert_count, stride)[:, :half].astype(BF), ((0, 0), (0, width - half)))
    grads_sent = grads_sent.at[:, half].set(partner_row)

    first_own = expert_in[0]
    second_own = expert_out[0]
    first_y = swap_y(first_own)
    part_b = stacked[:, :, :three]
    far_b = swap_y(part_b)
    part_a = doubled(stacked[:, :, three:], 1)
    part_a, far_b, first_y, grads_sent = together(part_a, far_b, first_y, grads_sent)
    pair_b = jnp.stack([part_b, far_b])
    a_own = part_a[:, :, :three]
    a_far = swap_y(a_own).reshape(width, three)
    a_own = a_own.reshape(width, three)
    pair_b = doubled(pair_b, 1, 1).reshape(2, width, three)
    a_far, pair_b, grads_sent, position_bias = together(a_far, pair_b, grads_sent, position_bias)
    small_all = part_a[:, :, three:].reshape(width, TILE)
    gain_one = small_all[:, expert_count].astype(F32)[None]
    gain_two = small_all[:, expert_count + 1].astype(F32)[None]
    router_wide = small_all
    far_bias = swap_y(position_bias)
    bias = jnp.concatenate([position_bias[:2], far_bias[:2], position_bias[2:], far_bias[2:]], 0)
    head_total = bias.shape[0]
    hot_const = jnp.asarray(NEAR_HOT, dtype=BF)
    near = dot(bias, hot_const) - bias[:, NB - 1 :].astype(F32)
    near = near.reshape(head_total, 2, TILE, TILE)
    places = jnp.arange(TILE, dtype=jnp.int32)
    causal = jnp.stack([places[None, :] <= places[:, None], jnp.ones((TILE, TILE), bool)])
    near = jnp.where(causal[None], near, NEG)

    grads_here = all_to_all(grads_sent)

    qkv, normed_one, qkv_weight, output_own = norm_and_project(
        micro_arg, layer_input, gain_one, a_own, a_far, pair_b[0], pair_b[1]
    )
    second_late, qkv = together(second_own, qkv)
    second_y = swap_y(second_late)
    output_far = swap_core(output_own)
    mixed, logs = attend(length, qkv, near)
    mixed, output_far = together(mixed, output_far)
    mixed_far = swap_core(mixed)
    residual, normed_two = residual_and_norm(micro_arg, layer_input, mixed, mixed_far, output_own, output_far, gain_two)
    normed_two, grads_here = together(normed_two, grads_here)

    arrived = []
    zero = jnp.zeros((1,), jnp.int32)
    parts = []
    for c in range(chunks):
        code_chunk = jnp.where(here & (chunk_of == c), route * chunk + inside, -1)
        parts.append(send_rows(zero, code_chunk, normed_two[None], chunk_rows).reshape(expert_count, chunk, width))
    arrived.append(all_to_all(parts[0]))
    partner_here = grads_here[:, half, :half].astype(jnp.int32)

    def chunk_grads(c):
        at = slice(c * chunk, (c + 1) * chunk)
        return grads_here[:, at].reshape(chunk_rows, width), partner_here[:, at].reshape(chunk_rows, 1)

    grads_parts = [chunk_grads(c) for c in range(chunks)]
    arrived[0], second_y, grads_parts = together(arrived[0], second_y, grads_parts)

    firsts = (first_own, first_y, swap_core(first_own), swap_core(first_y))
    seconds = (second_own, second_y, swap_core(second_own), swap_core(second_y))

    for c in range(1, chunks):
        sent, arrived[-1] = together(parts[c], arrived[-1])
        arrived.append(all_to_all(sent))

    me_arg = me.reshape(1).astype(jnp.int32)
    rows_all, slopes, active, gated, gates, backs = [], [], [], [], [], []
    line = None
    for c in range(chunks):
        grads_c, partner_c = grads_parts[c]
        rows_c = arrived[c].reshape(chunk_rows, width)
        back, act, slo, gat, gte, line = expert_rows_pass(
            c * chunk if chunks > 1 else None, chunk, half, me_arg, partner_c, rows_c, grads_c, router_wide, line, firsts, seconds
        )
        rows_all.append(rows_c)
        slopes.append(slo)
        active.append(act)
        gated.append(gat)
        gates.append(gte)
        if chunks == 1:
            gate_grad = line[:, 0].reshape(expert_count, chunk)
            pieces = []
            for _ in range(3):
                piece = gate_grad.astype(BF)
                pieces.append(piece)
                gate_grad = gate_grad - piece.astype(F32)
            gate_row = jnp.pad(jnp.concatenate(pieces, 1), ((0, 0), (0, width - 3 * half)))
            back = jnp.pad(back.reshape(expert_count, chunk, width), ((0, 0), (0, last_stride - chunk), (0, 0)))
            back = back.at[:, spare].set(gate_row)
        if c + 1 < chunks:
            back, arrived[c + 1] = together(back.reshape(expert_count, chunk, width), arrived[c + 1])
        else:
            back, rows_all[-1], backs = together(back, rows_all[-1], backs)
        backs.append(all_to_all(back))
    grads_cross, grads_kept, results = expert_rest(rows_all, slopes, active, gated, gates, seconds, expert_count)
    backs[-1], results = together(backs[-1], results)
    results_own = all_to_all(results).reshape(expert_count * half, width)

    grads_in = swap_core(grads_cross)
    across_y = swap_y(cross_sums(grads_kept, grads_in))

    backs_far = [swap_core(b) for b in backs]
    residual_grad, mixed_grad, extra_early, output_sent, output_kept = combine(
        micro_arg, core_arg, length, info, out_grad, residual, mixed, gain_two, router_wide, output_own,
        backs + backs_far, half, spare,
    )

    dq, dk, dv, tiles, sums = attend_back(length, qkv, near, mixed, logs, mixed_grad, 0, head_total // 2)
    far_sent, own_parts = attention_weight_grads(normed_one, dq, dk, dv, output_sent)
    far_got = swap_y(far_sent)
    sent = sent_half(core_arg, qkv_weight, (dq, dk, dv))
    sent, results_own = together(sent, results_own)
    got = swap_core(sent)
    rows_both, extra_late = both_rows(
        expert_count, micro_arg, core_arg, length, qkv_weight, (dq, dk, dv), got, layer_input, gain_one, residual_grad,
        info, residual, results_own, swap_core(results_own),
    )
    rows_both, across_y, tiles = together(rows_both, across_y, tiles)
    late_far = swap_core(extra_late)
    corner = micro * 2 + core
    corners = jnp.stack([corner, corner ^ 1, corner ^ 2, corner ^ 3]).astype(jnp.int32)
    rows_y = swap_y(rows_both)
    layer_output, input_grad = place_pieces(corners, (rows_both, swap_core(rows_both), rows_y, swap_core(rows_y)))
    layer_output = layer_output.reshape(2, SEQ, width)
    input_grad = input_grad.reshape(2, SEQ, width)
    expert_in_grad, expert_out_grad = last_sums(grads_kept, grads_in, across_y)

    tiles = tiles.reshape(head_total, 2 * TILE * TILE)
    tiles_high = tiles.astype(BF)
    tiles_rest = (tiles - tiles_high.astype(F32)).astype(BF)
    table = dot(tiles_high, hot_const, NT) + dot(tiles_rest, hot_const, NT)
    far_sum = jnp.sum(sums[:, :, 0], axis=1) - jnp.sum(table[:, : NB - 1], axis=1)
    table = jnp.concatenate([table[:, : NB - 1], far_sum[:, None]], 1)
    table_own = jnp.concatenate([table[0:2], table[4:5]], 0)
    table_far = jnp.concatenate([table[2:4], table[5:6]], 0)
    table_cols = heads_here * NB // rows_here
    table_both = jnp.concatenate([table_own.reshape(rows_here, table_cols), table_far.reshape(rows_here, table_cols)], 1)
    base = expert_count + 2
    kept = base + 2 * table_cols
    table_tile = jnp.tile(jnp.pad(table_both, ((0, 0), (base, TILE - kept))), (dp_count, 1))

    grads = packed_sums(kept, own_parts, far_got, output_kept, extra_early, extra_late, late_far, table_tile)
    arrived_grads = all_to_all(grads.reshape(dp_count, rows_here, grads.shape[1]))
    query_grad, key_grad, value_grad, output_grad, small = final_sums(kept, arrived_grads, shard)
    small_y = swap_y(small)
    both = small + small_y
    table_sum = small[:, base : base + table_cols] + small_y[:, base + table_cols : kept]
    return (
        layer_output,
        input_grad,
        both[:, expert_count],
        query_grad,
        key_grad,
        value_grad,
        output_grad.T,
        table_sum.reshape(heads_here, NB),
        both[:, expert_count + 1],
        both[:, :expert_count],
        expert_in_grad[None],
        expert_out_grad[None],
    )


def solution(mesh):
    return jax.shard_map(
        local,
        mesh=mesh,
        in_specs=(
            P(None, "dp", None),
            P(None, "dp", None),
            P("dp"),
            P("dp", "tensor"),
            P("dp", "tensor"),
            P("dp", "tensor"),
            P("tensor", "dp"),
            P("tensor", None),
            P("dp"),
            P("dp", None),
            P("dp", None, "tensor"),
            P("dp", "tensor", None),
            P(None, "dp"),
            P(None, "dp", None),
        ),
        out_specs=(
            P(None, "dp", None),
            P(None, "dp", None),
            P("dp"),
            P("dp", "tensor"),
            P("dp", "tensor"),
            P("dp", "tensor"),
            P("tensor", "dp"),
            P("tensor", None),
            P("dp"),
            P("dp", None),
            P("dp", None, "tensor"),
            P("dp", "tensor", None),
        ),
        check_vma=False,
    )
```

```python
import functools

import jax
import jax.numpy as jnp
import numpy as np
from jax import lax
from jax.experimental import pallas as pl
from jax.experimental.pallas import tpu as pltpu
from jax.sharding import PartitionSpec as P

HEAD_DIM = 64
NB = 32
SEQ = 1024
TILE = 128
QROWS = 256
NEG = -1e30
GELU_C = 0.7978845608028654
GELU_A = 0.044715

BF = jnp.bfloat16
F32 = jnp.float32

bucket_edges = np.ceil(16.0 * 8.0 ** (np.arange(1, 16) / 16.0)).astype(np.int32)


def near_tables():
    rows = np.arange(TILE)[:, None]
    cols = np.arange(TILE)[None, :]
    hots = []
    for shift in (0, TILE):
        distance = rows - cols + shift
        clipped = np.maximum(distance, 0)
        reached = np.sum(clipped[..., None] >= bucket_edges, axis=-1)
        bucket = np.minimum(clipped, 16) + reached
        hots.append(bucket[..., None] == np.arange(NB))
    hot = np.stack(hots).reshape(2 * TILE * TILE, NB).T
    return hot


NEAR_HOT = near_tables()
assert bucket_edges[-1] <= TILE


def dot(a, b, dims=((1,), (0,))):
    return lax.dot_general(a, b, (dims, ((), ())), preferred_element_type=F32)


NT = ((1,), (1,))
TN = ((0,), (0,))


MIB = 2**20
SMALL_COST = pl.CostEstimate(flops=1_000_000, bytes_accessed=1_000_000, transcendentals=0)


def score_tiles(block, half, q_half, key_ref, near_one, near_two, length):
    tiles = []
    for j in range(block + 1):
        s = dot(q_half, key_ref[j * QROWS : (j + 1) * QROWS, :], NT)
        if j == block:
            top = jnp.concatenate([s[:TILE, :TILE] + near_one, jnp.full((TILE, TILE), NEG, F32)], 1)
            low = jnp.concatenate([s[TILE:, :TILE] + near_two, s[TILE:, TILE:] + near_one], 1)
            s = jnp.concatenate([top, low], 0)
        elif j == block - 1:
            top = jnp.concatenate([s[:TILE, :TILE], s[:TILE, TILE:] + near_two], 1)
            s = jnp.concatenate([top, s[TILE:]], 0)
        if (j + 1) * QROWS > SEQ // 2:
            place = lax.broadcasted_iota(jnp.int32, (1, QROWS), 1) + j * QROWS
            s = s + jnp.where(place < length, 0.0, NEG)
        tiles.append(s)
    return tiles


def lane_half(rows):
    return lax.broadcasted_iota(jnp.int32, (rows, 2 * HEAD_DIM), 1) < HEAD_DIM


def attend_kernel(length_ref, query_ref, key_ref, value_ref, near_ref, out_ref, log_ref):
    length = length_ref[0]
    lanes = lane_half(QROWS)
    ones = jnp.ones((SEQ, TILE), BF)
    value_ext = jnp.concatenate([value_ref[...], ones], 1)
    for i in range(SEQ // QROWS):
        q_rows = query_ref[i * QROWS : (i + 1) * QROWS, :] * BF(0.125)
        outs, logs = [], []
        for h in range(2):
            keep = lanes if h == 0 else ~lanes
            q_half = jnp.where(keep, q_rows, BF(0))
            tiles = score_tiles(i, h, q_half, key_ref, near_ref[h, 0], near_ref[h, 1], length)
            top = tiles[0]
            for s in tiles[1:]:
                top = jnp.maximum(top, s)
            top = jnp.max(top, axis=1, keepdims=True)
            total = None
            for j, s in enumerate(tiles):
                p = jnp.exp(s - top).astype(BF)
                part = dot(p, value_ext[j * QROWS : (j + 1) * QROWS, :])
                total = part if total is None else total + part
            row_sum = total[:, TILE:]
            outs.append(total[:, :TILE] / row_sum)
            logs.append(top + jnp.log(row_sum))
        out_ref[i * QROWS : (i + 1) * QROWS, :] = jnp.where(lanes, outs[0], outs[1]).astype(BF)
        log_ref[i * QROWS : (i + 1) * QROWS, :] = jnp.where(lanes, logs[0], logs[1])


def attend(length, qkv, near):
    pairs = qkv.shape[1] // (3 * TILE)
    cols = pairs * TILE
    return pl.pallas_call(
        attend_kernel,
        grid=(pairs,),
        in_specs=[
            pl.BlockSpec(memory_space=pltpu.SMEM),
            pl.BlockSpec((SEQ, TILE), lambda p: (0, p)),
            pl.BlockSpec((SEQ, TILE), lambda p: (0, pairs + p)),
            pl.BlockSpec((SEQ, TILE), lambda p: (0, 2 * pairs + p)),
            pl.BlockSpec((2, 2, TILE, TILE), lambda p: (p, 0, 0, 0)),
        ],
        out_specs=[
            pl.BlockSpec((SEQ, TILE), lambda p: (0, p)),
            pl.BlockSpec((SEQ, TILE), lambda p: (0, p)),
        ],
        out_shape=[
            jax.ShapeDtypeStruct((SEQ, cols), BF),
            jax.ShapeDtypeStruct((SEQ, cols), F32),
        ],
        compiler_params=pltpu.CompilerParams(vmem_limit_bytes=40 * MIB),
        cost_estimate=SMALL_COST,
        name="attend",
    )(length, qkv, qkv, qkv, near)


def attend_back_kernel(
    length_ref, query_ref, key_ref, value_ref, near_ref, out_ref, log_ref, grad_ref,
    dq_ref, dk_ref, dv_ref, tile_ref, sum_ref, dk_acc, dv_acc,
):
    length = length_ref[0]
    lanes = lane_half(QROWS)
    lanes_all = lane_half(SEQ)
    ones = jnp.ones((SEQ, TILE), BF)
    key_ext = [
        jnp.concatenate([jnp.where(lanes_all, key_ref[...], BF(0)), ones], 1),
        jnp.concatenate([jnp.where(lanes_all, BF(0), key_ref[...]), ones], 1),
    ]
    near_sums = [[None, None], [None, None]]
    all_sums = [None, None]

    for i in range(SEQ // QROWS):
        rows = slice(i * QROWS, (i + 1) * QROWS)
        q_rows = query_ref[rows, :] * BF(0.125)
        g_rows = grad_ref[rows, :]
        mass = g_rows.astype(F32) * out_ref[rows, :].astype(F32)
        dq = None
        for h in range(2):
            keep = lanes if h == 0 else ~lanes
            q_half = jnp.where(keep, q_rows, BF(0))
            g_half = jnp.where(keep, g_rows, BF(0))
            delta = jnp.sum(jnp.where(keep, mass, 0.0), axis=1, keepdims=True)
            log_col = log_ref[rows, h * HEAD_DIM : h * HEAD_DIM + 1]
            tiles = score_tiles(i, h, q_half, key_ref, near_ref[h, 0], near_ref[h, 1], length)
            for j, s in enumerate(tiles):
                keys = slice(j * QROWS, (j + 1) * QROWS)
                p = jnp.exp(s - log_col)
                dp = dot(g_half, value_ref[keys, :], NT)
                ds = (p * (dp - delta)).astype(BF)
                part = dot(ds, key_ext[h][keys, :])
                dq = put(dq, part[:, :TILE])
                all_sums[h] = put(all_sums[h], jnp.sum(part[:, TILE:].reshape(QROWS // 8, 8, TILE), axis=0))
                dk_part = dot(ds, q_half, TN)
                dv_part = dot(p.astype(BF), g_half, TN)
                if i == j and h == 0:
                    dk_acc[keys, :] = dk_part
                    dv_acc[keys, :] = dv_part
                else:
                    dk_acc[keys, :] += dk_part
                    dv_acc[keys, :] += dv_part
                if j == i:
                    wide = ds.astype(F32)
                    near_sums[h][0] = put(near_sums[h][0], wide[:TILE, :TILE] + wide[TILE:, TILE:])
                    near_sums[h][1] = put(near_sums[h][1], wide[TILE:, :TILE])
                elif j == i - 1:
                    near_sums[h][1] = put(near_sums[h][1], ds[:TILE, TILE:].astype(F32))
        dq_ref[rows, :] = (dq * 0.125).astype(BF)
    dk_ref[...] = dk_acc[...].astype(BF)
    dv_ref[...] = dv_acc[...].astype(BF)
    for h in range(2):
        tile_ref[h, 0] = near_sums[h][0]
        tile_ref[h, 1] = near_sums[h][1]
        sum_ref[h] = all_sums[h]


def attend_back(length, qkv, near, mixed, logs, grad, first, count):
    pairs = qkv.shape[1] // (3 * TILE)
    cols = count * TILE
    col = pl.BlockSpec((SEQ, TILE), lambda p: (0, first + p))
    out = pl.BlockSpec((SEQ, TILE), lambda p: (0, p))
    return pl.pallas_call(
        attend_back_kernel,
        grid=(count,),
        in_specs=[
            pl.BlockSpec(memory_space=pltpu.SMEM),
            col,
            pl.BlockSpec((SEQ, TILE), lambda p: (0, pairs + first + p)),
            pl.BlockSpec((SEQ, TILE), lambda p: (0, 2 * pairs + first + p)),
            pl.BlockSpec((2, 2, TILE, TILE), lambda p: (first + p, 0, 0, 0)),
            col,
            col,
            col,
        ],
        out_specs=[
            out,
            out,
            out,
            pl.BlockSpec((2, 2, TILE, TILE), lambda p: (p, 0, 0, 0)),
            pl.BlockSpec((2, 8, TILE), lambda p: (p, 0, 0)),
        ],
        out_shape=[
            jax.ShapeDtypeStruct((SEQ, cols), BF),
            jax.ShapeDtypeStruct((SEQ, cols), BF),
            jax.ShapeDtypeStruct((SEQ, cols), BF),
            jax.ShapeDtypeStruct((2 * count, 2, TILE, TILE), F32),
            jax.ShapeDtypeStruct((2 * count, 8, TILE), F32),
        ],
        scratch_shapes=[pltpu.VMEM((SEQ, TILE), F32), pltpu.VMEM((SEQ, TILE), F32)],
        compiler_params=pltpu.CompilerParams(vmem_limit_bytes=40 * MIB),
        cost_estimate=SMALL_COST,
        name="attend_back",
    )(length, qkv, qkv, qkv, near, mixed, logs, grad)


def low_lanes(shape):
    return lax.broadcasted_iota(jnp.int32, shape, 1) < HEAD_DIM


def turned(tile):
    return pltpu.roll(tile, HEAD_DIM, 1)


def pack_kernel(q_ref, k_ref, v_ref, o_ref, one_ref, two_ref, router_ref, out_ref):
    shard = q_ref.shape[1]
    rows = q_ref.shape[0]
    source = lax.broadcasted_iota(jnp.int32, (shard, 6 * TILE), 0)
    target = lax.broadcasted_iota(jnp.int32, (shard, 6 * TILE), 1)

    def moved(pair_base, last_base):
        want = jnp.where(source < TILE, source + pair_base, source - TILE + last_base)
        return jnp.where(target == want, 1.0, 0.0).astype(BF)

    total = dot(v_ref[...], moved(0, 2 * TILE)) + dot(o_ref[...], moved(TILE, 2 * TILE + HEAD_DIM), TN)
    total = total + dot(q_ref[...], moved(3 * TILE, 5 * TILE)) + dot(k_ref[...], moved(4 * TILE, 5 * TILE + HEAD_DIM))
    out_ref[:, : 6 * TILE] = total.astype(BF)
    experts = router_ref.shape[0]
    own_row = lax.broadcasted_iota(jnp.int32, (rows, rows), 0) == lax.broadcasted_iota(jnp.int32, (rows, rows), 1)

    def column(ref):
        return jnp.sum(jnp.where(own_row, ref[...].astype(F32), 0.0), axis=1, keepdims=True)

    lanes = lax.broadcasted_iota(jnp.int32, (experts, TILE), 1)
    spread = jnp.where(lanes == lax.broadcasted_iota(jnp.int32, (experts, TILE), 0), 1.0, 0.0).astype(BF)
    place = lax.broadcasted_iota(jnp.int32, (rows, TILE), 1)
    small = dot(router_ref[...], spread, TN)
    small = jnp.where(place == experts, column(one_ref), jnp.where(place == experts + 1, column(two_ref), small))
    out_ref[:, 6 * TILE :] = small.astype(BF)


def pack_weights(query, key, value, output, one, two, router):
    rows = query.shape[0]
    return pl.pallas_call(
        pack_kernel,
        out_shape=jax.ShapeDtypeStruct((rows, 7 * TILE), BF),
        compiler_params=pltpu.CompilerParams(vmem_limit_bytes=60 * MIB),
        cost_estimate=SMALL_COST,
        name="pack_weights",
    )(query, key, value, output, one[None], two[None], router.T)


def qkv_kernel(micro_ref, tokens_ref, gain_ref, a_own, a_far, b_own, b_far, qkv_ref, normed_ref, weight_ref, output_ref):
    width = tokens_ref.shape[2]

    @pl.when(pl.program_id(0) == 0)
    def _():
        low = low_lanes((width, TILE))

        def tiles(own, far, pair, low_half):
            at = slice(pair * TILE, (pair + 1) * TILE)
            one, two = own[:, 2 * TILE :].astype(F32), far[:, 2 * TILE :].astype(F32)
            last = jnp.where(low, one, turned(two)) if low_half else jnp.where(low, turned(one), two)
            return own[:, at], far[:, at], last.astype(BF)

        for n, (own, far, pair, low_half) in enumerate(
            ((a_own, a_far, 0, True), (a_own, a_far, 1, False), (b_own, b_far, 0, True))
        ):
            for t, tile in enumerate(tiles(own[...], far[...], pair, low_half)):
                at = 3 * n + t
                weight_ref[:, at * TILE : (at + 1) * TILE] = tile
        for t, tile in enumerate(tiles(b_own[...], b_far[...], 1, False)):
            output_ref[:, t * TILE : (t + 1) * TILE] = tile

    x = tokens_ref[0].astype(F32)
    inverse = lax.rsqrt(jnp.mean(x * x, axis=-1, keepdims=True) + 1e-06)
    normed = (x * inverse * gain_ref[...]).astype(BF)
    normed_ref[...] = normed
    qkv_ref[...] = dot(normed, weight_ref[...]).astype(BF)


def norm_and_project(micro, layer_input, gain, a_own, a_far, b_own, b_far):
    width = layer_input.shape[2]
    block = 256
    cols = 3 * TILE
    whole = lambda rows, n: pl.BlockSpec((rows, n), lambda i, m: (0, 0))
    here = lambda n: pl.BlockSpec((block, n), lambda i, m: (i, 0))
    return pl.pallas_call(
        qkv_kernel,
        grid_spec=pltpu.PrefetchScalarGridSpec(
            num_scalar_prefetch=1,
            grid=(SEQ // block,),
            in_specs=[pl.BlockSpec((1, block, width), lambda i, m: (m[0], i, 0)), whole(1, width)] + [whole(width, cols)] * 4,
            out_specs=[here(3 * cols), here(width), whole(width, 3 * cols), whole(width, cols)],
        ),
        out_shape=[
            jax.ShapeDtypeStruct((SEQ, 3 * cols), BF),
            jax.ShapeDtypeStruct((SEQ, width), BF),
            jax.ShapeDtypeStruct((width, 3 * cols), BF),
            jax.ShapeDtypeStruct((width, cols), BF),
        ],
        compiler_params=pltpu.CompilerParams(vmem_limit_bytes=40 * MIB),
        cost_estimate=SMALL_COST,
        name="norm_and_project",
    )(micro, layer_input, gain, a_own, a_far, b_own, b_far)


def middle_kernel(
    blocks, micro_ref, tokens_ref, mixed_ref, other_ref, own_ref, far_ref, gain_ref, code_ref, residual_ref, sent_ref, normed
):
    step = pl.program_id(0)
    rows = tokens_ref.shape[1]

    @pl.when(step < blocks)
    def _():
        total = tokens_ref[0].astype(F32) + dot(mixed_ref[...], own_ref[...], NT) + dot(other_ref[...], far_ref[...], NT)
        residual_ref[...] = total
        inverse = lax.rsqrt(jnp.mean(total * total, axis=-1, keepdims=True) + 1e-06)
        normed[pl.ds(pl.multiple_of(step * rows, rows), rows), :] = (total * inverse * gain_ref[...]).astype(BF)

    @pl.when(step >= blocks)
    def _():
        block = sent_ref.shape[0]
        ids = lax.broadcasted_iota(jnp.int32, (block, 1), 0) + (step - blocks) * block
        hot = jnp.where((ids == code_ref[:1]) | (ids == code_ref[1:2]), 1.0, 0.0).astype(BF)
        sent_ref[...] = dot(hot, normed[...]).astype(BF)


def residual_and_rows(micro, layer_input, mixed, other, output_own, output_far, gain, code, count):
    width = layer_input.shape[2]
    block = 256
    blocks = SEQ // block
    send = 320
    cols = mixed.shape[1]
    at = lambda i: jnp.minimum(i, blocks - 1)
    whole = lambda arr: pl.BlockSpec(arr.shape, lambda i, m: (0, 0))
    here = lambda n: pl.BlockSpec((block, n), lambda i, m: (at(i), 0))
    return pl.pallas_call(
        functools.partial(middle_kernel, blocks),
        grid_spec=pltpu.PrefetchScalarGridSpec(
            num_scalar_prefetch=1,
            grid=(blocks + count // send,),
            in_specs=[
                pl.BlockSpec((1, block, width), lambda i, m: (m[0], at(i), 0)),
                here(cols), here(cols), whole(output_own), whole(output_far), whole(gain), whole(code),
            ],
            out_specs=[here(width), pl.BlockSpec((send, width), lambda i, m: (jnp.maximum(i, blocks) - blocks, 0))],
            scratch_shapes=[pltpu.VMEM((SEQ, width), BF)],
        ),
        out_shape=[jax.ShapeDtypeStruct((SEQ, width), F32), jax.ShapeDtypeStruct((count, width), BF)],
        compiler_params=pltpu.CompilerParams(vmem_limit_bytes=40 * MIB),
        cost_estimate=SMALL_COST,
        name="residual_and_rows",
    )(micro, layer_input, mixed, other, output_own, output_far, gain, code)


def picked_rows(first, second, segments):
    total = None
    start = 0
    for rows in segments:
        length = rows.shape[0]
        ids = lax.broadcasted_iota(jnp.int32, (1, length), 1) + start
        hot = jnp.where((first == ids) | (second == ids), 1.0, 0.0).astype(BF)
        total = put(total, dot(hot, rows))
        start += length
    return total


def put(a, b):
    return b if a is None else a + b


def folded(product):
    return jnp.sum(product.reshape(product.shape[0] // 8, 8, product.shape[1]), axis=0)


def as_column(eight):
    ones = jnp.ones((16, TILE), BF)
    high = eight.astype(BF)
    rest = (eight - high.astype(F32)).astype(BF)
    return dot(jnp.concatenate([high, rest], 0), ones, TN)


def combine_kernel(experts, half, spare, micro_ref, core_ref, length_ref, *refs):
    info_ref, grad_ref, residual_ref, mixed_ref, gain_ref, router_ref, output_ref = refs[:7]
    backs = refs[7:-9]
    (total_ref, mixed_grad_ref, extra_ref, far_ref, own_ref, acc_ref, router_acc, gain_acc, tables) = refs[-9:]
    block = residual_ref.shape[0]
    step = pl.program_id(0)
    count = len(backs) // 2

    @pl.when(step == 0)
    def _():
        place = lax.broadcasted_iota(jnp.int32, (experts, 1), 0)
        for n, back in enumerate((backs[count - 1], backs[2 * count - 1])):
            table = jnp.zeros((experts, back.shape[2]), F32)
            for e in range(experts):
                row = back[e, spare : spare + 16, :].astype(F32)[:1]
                table = jnp.where(place == e, row, table)
            for piece in range(3):
                at = (3 * n + piece) * experts
                tables[at : at + experts] = table[:, piece * half : (piece + 1) * half]

    info = jnp.transpose(info_ref[...])
    number = lambda n: info[:, n : n + 1]
    columns = lax.broadcasted_iota(jnp.int32, (1, half), 1)
    lanes = lax.broadcasted_iota(jnp.int32, (1, 6 * experts), 1)
    table = tables[...].astype(BF)
    values = []
    for k in range(2):
        slot = number(4 + k)
        hot = jnp.where(columns == lax.rem(slot, half), 1.0, 0.0).astype(BF)
        found = dot(hot, table, NT)
        wanted = jnp.where(slot // half == core_ref[0], 0, 3 * experts) + number(2 + k)
        away = lanes - wanted
        hit = (away == 0) | (away == experts) | (away == 2 * experts)
        values.append(jnp.sum(jnp.where(hit, found, 0.0), axis=1, keepdims=True))
    wide = lax.broadcasted_iota(jnp.int32, (1, TILE), 1)
    is_first, is_second = wide == number(2), wide == number(3)
    residual = residual_ref[...]
    gain = gain_ref[...]
    inverse = lax.rsqrt(jnp.mean(residual * residual, axis=-1, keepdims=True) + 1e-06)
    plain = residual * inverse
    normed = (plain * gain).astype(BF)
    logits = dot(normed, router_ref[...])
    gap = jnp.sum(jnp.where(is_first, logits, 0.0) - jnp.where(is_second, logits, 0.0), axis=1, keepdims=True)
    small = jnp.exp(-jnp.abs(gap))
    logit = small / ((1.0 + small) * (1.0 + small)) * (values[0] - values[1])
    logit_grad = jnp.where(is_first, logit, jnp.where(is_second, -logit, 0.0)).astype(BF)
    segments = [b[...].reshape(b.shape[0] * b.shape[1], b.shape[2]) for b in backs]
    normed_grad = picked_rows(number(0), number(1), segments) + dot(logit_grad, router_ref[...], NT)
    scaled = normed_grad * gain
    mean = jnp.mean(scaled * plain, axis=-1, keepdims=True)
    place = lax.broadcasted_iota(jnp.int32, (block, 1), 0) + step * block
    grad_out = jnp.where(place < length_ref[0], grad_ref[0].astype(F32), 0.0)
    total = grad_out + inverse * (scaled - plain * mean)
    total_ref[...] = total
    branch = total.astype(BF)
    mixed_grad_ref[...] = dot(branch, output_ref[...]).astype(BF)
    router_part = dot(logit_grad, normed, TN)
    gain_part = folded(normed_grad * plain)
    output_part = dot(mixed_ref[...], branch, TN)

    @pl.when(step == 0)
    def _():
        router_acc[...] = router_part
        gain_acc[...] = gain_part
        acc_ref[...] = output_part

    @pl.when(step > 0)
    def _():
        router_acc[...] += router_part
        gain_acc[...] += gain_part
        acc_ref[...] += output_part

    @pl.when(step == pl.num_programs(0) - 1)
    def _():
        extra_ref[...] = jnp.transpose(router_acc[...]) + jnp.where(wide == experts + 1, as_column(gain_acc[...]), 0.0)
        parts = jnp.transpose(acc_ref[...])
        far_ref[...] = parts[:, TILE:].astype(BF)
        own_ref[:, :TILE] = parts[:, :TILE]
        own_ref[:, TILE:] = parts[:, 2 * TILE :]


def combine(micro, core, length, info, out_grad, residual, mixed, gain, router, output_own, backs, half, spare):
    width = residual.shape[1]
    block = 512
    cols = mixed.shape[1]
    whole = lambda arr: pl.BlockSpec(arr.shape, lambda i, *_: (0,) * arr.ndim)
    fixed = lambda rows, n: pl.BlockSpec((rows, n), lambda i, *_: (0, 0))
    here = lambda n: pl.BlockSpec((block, n), lambda i, *_: (i, 0))
    experts = backs[0].shape[0]
    return pl.pallas_call(
        functools.partial(combine_kernel, experts, half, spare),
        grid_spec=pltpu.PrefetchScalarGridSpec(
            num_scalar_prefetch=3,
            grid=(SEQ // block,),
            in_specs=[
                pl.BlockSpec((8, block), lambda i, *_: (0, i)),
                pl.BlockSpec((1, block, width), lambda i, m, *_: (m[0], i, 0)),
                here(width), here(cols), whole(gain), whole(router), whole(output_own),
            ]
            + [whole(x) for x in backs],
            out_specs=[here(width), here(cols), fixed(width, TILE), fixed(width, 2 * TILE), fixed(width, 2 * TILE)],
            scratch_shapes=[
                pltpu.VMEM((cols, width), F32),
                pltpu.VMEM((TILE, width), F32),
                pltpu.VMEM((8, width), F32),
                pltpu.VMEM((6 * experts, half), F32),
            ],
        ),
        out_shape=[
            jax.ShapeDtypeStruct((SEQ, width), F32),
            jax.ShapeDtypeStruct((SEQ, cols), BF),
            jax.ShapeDtypeStruct((width, TILE), F32),
            jax.ShapeDtypeStruct((width, 2 * TILE), BF),
            jax.ShapeDtypeStruct((width, 2 * TILE), F32),
        ],
        compiler_params=pltpu.CompilerParams(vmem_limit_bytes=40 * MIB),
        cost_estimate=SMALL_COST,
        name="combine",
    )(micro, core, length, info, out_grad, residual, mixed, gain, router, output_own, *backs)


def projected_back(weight_ref, grads):
    total = None
    for n, grad in enumerate(grads):
        cols = grad.shape[1]
        total = put(total, dot(grad[...], weight_ref[:, n * cols : (n + 1) * cols], NT))
    return total


def attention_weight_kernel(
    blocks, core_ref, normed_ref, q_ref, k_ref, v_ref, output_ref, weight_ref, q_rows, k_rows, v_rows, far_ref, own_ref, sent_ref
):
    step = pl.program_id(0)

    @pl.when(step < blocks)
    def _():
        low = low_lanes((normed_ref.shape[1], TILE))
        q, k, v = (dot(normed_ref[...], d[...], TN) for d in (q_ref, k_ref, v_ref))
        for n, part in enumerate((q, k, v)):
            own_ref[:, n * TILE : (n + 1) * TILE] = part[:, :TILE]
            far_ref[:, n * TILE : (n + 1) * TILE] = part[:, TILE : 2 * TILE].astype(BF)
        q, k, v = (part[:, 2 * TILE :] for part in (q, k, v))
        far_ref[:, 3 * TILE : 4 * TILE] = jnp.where(low, turned(q), k).astype(BF)
        far_ref[:, 4 * TILE : 5 * TILE] = jnp.where(low, turned(v), output_ref[:, TILE:].astype(F32)).astype(BF)
        far_ref[:, 5 * TILE :] = output_ref[:, :TILE]
        own_ref[:, 3 * TILE : 4 * TILE] = jnp.where(low, q, turned(k))
        own_ref[:, 4 * TILE :] = jnp.where(low, v, 0.0)

    @pl.when(step >= blocks)
    def _():
        sent_ref[...] = projected_back(weight_ref, (q_rows, k_rows, v_rows))


def attention_weight_grads(core, normed, q, k, v, output, weight):
    width = normed.shape[1]
    block = 256
    blocks = width // block
    at = lambda i: jnp.minimum(i, blocks - 1)
    later = lambda i: jnp.maximum(i, blocks) - blocks
    whole = lambda arr: pl.BlockSpec(arr.shape, lambda i, c: (0, 0))
    here = lambda n: pl.BlockSpec((block, n), lambda i, c: (at(i), 0))
    rows = pl.BlockSpec((block, q.shape[1]), lambda i, c: ((1 - c[0]) * 2 + later(i), 0))
    return pl.pallas_call(
        functools.partial(attention_weight_kernel, blocks),
        grid_spec=pltpu.PrefetchScalarGridSpec(
            num_scalar_prefetch=1,
            grid=(blocks + 2,),
            in_specs=[
                pl.BlockSpec((SEQ, block), lambda i, c: (0, at(i))),
                whole(q), whole(k), whole(v), here(2 * TILE), whole(weight), rows, rows, rows,
            ],
            out_specs=[here(6 * TILE), here(5 * TILE), pl.BlockSpec((block, width), lambda i, c: (later(i), 0))],
        ),
        out_shape=[
            jax.ShapeDtypeStruct((width, 6 * TILE), BF),
            jax.ShapeDtypeStruct((width, 5 * TILE), F32),
            jax.ShapeDtypeStruct((2 * block, width), F32),
        ],
        compiler_params=pltpu.CompilerParams(vmem_limit_bytes=40 * MIB),
        cost_estimate=SMALL_COST,
        name="attention_weight_grads",
    )(core, normed, q, k, v, output, weight, q, k, v)


def both_kernel(
    lane, micro_ref, core_ref, length_ref, weight_ref, q, k, v, got_ref, tokens_ref, gain_ref, grad_ref,
    info_ref, residual_ref, own_ref, far_ref, out_ref, extra_ref, acc_ref,
):
    block = residual_ref.shape[0]
    info = jnp.transpose(info_ref[...])
    place = lax.broadcasted_iota(jnp.int32, (block, 1), 0) + (core_ref[0] * 2 + pl.program_id(0)) * block
    rows = residual_ref[...] + picked_rows(info[:, 6:7], info[:, 7:8], (own_ref[...], far_ref[...]))
    out_ref[0] = jnp.where(place < length_ref[0], rows, 0.0).astype(BF)
    normed_grad = got_ref[...] + projected_back(weight_ref, (q, k, v))
    x = tokens_ref[0].astype(F32)
    inverse = lax.rsqrt(jnp.mean(x * x, axis=-1, keepdims=True) + 1e-06)
    plain = x * inverse
    scaled = normed_grad * gain_ref[...]
    mean = jnp.mean(scaled * plain, axis=-1, keepdims=True)
    out_ref[1] = (grad_ref[...] + inverse * (scaled - plain * mean)).astype(BF)
    wide = lax.broadcasted_iota(jnp.int32, (1, TILE), 1)
    part = folded(normed_grad * plain)

    @pl.when(pl.program_id(0) == 0)
    def _():
        acc_ref[...] = part

    @pl.when(pl.program_id(0) == 1)
    def _():
        extra_ref[...] = jnp.where(wide == lane, as_column(acc_ref[...] + part), 0.0)


def both_rows(lane, micro, core, length, weight, grads, got, layer_input, gain, residual_grad, info, residual, own, far):
    width = weight.shape[0]
    block = 256
    here = lambda n: pl.BlockSpec((block, n), lambda i, m, c, *_: (c[0] * 2 + i, 0))
    whole = lambda arr: pl.BlockSpec(arr.shape, lambda i, *_: (0, 0))
    return pl.pallas_call(
        functools.partial(both_kernel, lane),
        grid_spec=pltpu.PrefetchScalarGridSpec(
            num_scalar_prefetch=3,
            grid=(2,),
            in_specs=[whole(weight)]
            + [here(grads[0].shape[1])] * 3
            + [
                pl.BlockSpec((block, width), lambda i, *_: (i, 0)),
                pl.BlockSpec((1, block, width), lambda i, m, c, *_: (m[0], c[0] * 2 + i, 0)),
                whole(gain),
                here(width),
                pl.BlockSpec((8, block), lambda i, m, c, *_: (0, c[0] * 2 + i)),
                here(width),
                whole(own),
                whole(far),
            ],
            out_specs=[
                pl.BlockSpec((2, block, width), lambda i, *_: (0, i, 0)),
                pl.BlockSpec((width, TILE), lambda i, *_: (0, 0)),
            ],
            scratch_shapes=[pltpu.VMEM((8, width), F32)],
        ),
        out_shape=[jax.ShapeDtypeStruct((2, 2 * block, width), BF), jax.ShapeDtypeStruct((width, TILE), F32)],
        compiler_params=pltpu.CompilerParams(vmem_limit_bytes=40 * MIB),
        cost_estimate=SMALL_COST,
        name="both_rows",
    )(micro, core, length, weight, *grads, got, layer_input, gain, residual_grad, info, residual, own, far)


def sum_kernel(kept, own, got, out_own, early, late, late_far, table, sum_ref):
    low = low_lanes(early.shape)
    sum_ref[:, : 4 * TILE] = (own[:, : 4 * TILE] + got[:, : 4 * TILE].astype(F32)).astype(BF)
    mixed = jnp.where(low, own[:, 4 * TILE :], turned(out_own[:, TILE:]))
    sum_ref[:, 4 * TILE : 5 * TILE] = (mixed + got[:, 4 * TILE : 5 * TILE].astype(F32)).astype(BF)
    sum_ref[:, 5 * TILE : 6 * TILE] = (out_own[:, :TILE] + got[:, 5 * TILE :].astype(F32)).astype(BF)
    extra = early[...] + late[...] + late_far[...] + table[...]
    high = extra.astype(BF)
    rest = extra - high.astype(F32)
    if kept <= HEAD_DIM:
        sum_ref[:, 6 * TILE :] = jnp.where(low, high.astype(F32), turned(rest)).astype(BF)
    else:
        sum_ref[:, 6 * TILE : 7 * TILE] = high
        sum_ref[:, 7 * TILE :] = rest.astype(BF)


def packed_sums(kept, *parts):
    width = parts[0].shape[0]
    cols = (7 if kept <= HEAD_DIM else 8) * TILE
    block = 256
    here = lambda n: pl.BlockSpec((block, n), lambda i: (i, 0))
    return pl.pallas_call(
        functools.partial(sum_kernel, kept),
        grid=(width // block,),
        in_specs=[here(x.shape[1]) for x in parts],
        out_specs=here(cols),
        out_shape=jax.ShapeDtypeStruct((width, cols), BF),
        compiler_params=pltpu.CompilerParams(vmem_limit_bytes=40 * MIB),
        cost_estimate=SMALL_COST,
        name="packed_sums",
    )(*parts)


def final_kernel(kept, parts_ref, q_ref, k_ref, v_ref, o_ref, small_ref):
    total = parts_ref[0].astype(F32)
    for n in range(1, parts_ref.shape[0]):
        total = total + parts_ref[n].astype(F32)
    tile = lambda t: total[:, t * TILE : (t + 1) * TILE]
    q_ref[:, :TILE] = tile(0)
    q_ref[:, TILE:] = tile(3)[:, :HEAD_DIM]
    k_ref[:, :TILE] = tile(1)
    k_ref[:, TILE:] = turned(tile(3))[:, :HEAD_DIM]
    v_ref[:, :TILE] = tile(2)
    v_ref[:, TILE:] = tile(4)[:, :HEAD_DIM]
    o_ref[:, :TILE] = tile(5)
    o_ref[:, TILE:] = turned(tile(4))[:, :HEAD_DIM]
    small_ref[...] = tile(6) + (turned(tile(6)) if kept <= HEAD_DIM else tile(7))


def final_sums(kept, parts, shard):
    rows = parts.shape[1]
    return pl.pallas_call(
        functools.partial(final_kernel, kept),
        out_shape=[jax.ShapeDtypeStruct((rows, shard), F32)] * 4 + [jax.ShapeDtypeStruct((rows, TILE), F32)],
        compiler_params=pltpu.CompilerParams(vmem_limit_bytes=40 * MIB),
        cost_estimate=SMALL_COST,
        name="final_sums",
    )(parts)


def pair_gate(logits, own, other):
    lanes = lax.broadcasted_iota(jnp.int32, logits.shape, 1)
    gap = jnp.sum(
        jnp.where(lanes == own, logits, 0.0) - jnp.where(lanes == other, logits, 0.0), axis=1, keepdims=True
    )
    small = jnp.exp(-jnp.abs(gap))
    return jnp.where(gap >= 0.0, 1.0, small) / (1.0 + small)


def expert_kernel(lead, chunk, half, me_ref, partner_ref, rows_ref, grads_ref, router_ref, *refs):
    before, refs = (refs[0], refs[1:]) if lead is not None and lead > 0 else (None, refs)
    sources = refs[:8]
    back_ref, active_ref, slope_ref, gated_ref, gate_ref, mass_ref, firsts, seconds, sems = refs[8:]
    copies = [
        (
            pltpu.make_async_copy(sources[r], firsts.at[r], sems.at[0, r]),
            pltpu.make_async_copy(sources[4 + r], seconds.at[r], sems.at[1, r]),
        )
        for r in range(4)
    ]

    @pl.when(pl.program_id(0) == 0)
    def _():
        for pair in copies:
            for copy in pair:
                copy.start()

    rows = rows_ref[...]
    grads = grads_ref[...]
    gate = pair_gate(dot(rows, router_ref[...]), me_ref[0], partner_ref[...])
    gated_ref[...] = (gate * grads.astype(F32)).astype(BF)
    gate_ref[...] = jnp.broadcast_to(gate, gate_ref.shape)
    mass = None
    back = None
    step = 256
    for r, pair in enumerate(copies):

        @pl.when(pl.program_id(0) == 0)
        def _(pair=pair):
            for copy in pair:
                copy.wait()

        width = firsts.shape[2]
        for c in range(0, width, step):
            x = dot(rows, firsts[r, :, c : c + step])
            plain = dot(grads, seconds[r, c : c + step, :], NT)
            square = x * x
            bent = jnp.tanh(x * (GELU_C + (GELU_C * GELU_A) * square))
            rise = 0.5 + 0.5 * bent
            active = x * rise
            slope = rise + active * (1.0 - bent) * (GELU_C + (3.0 * GELU_C * GELU_A) * square)
            low = active.astype(BF)
            place = slice(r * width + c, r * width + c + step)
            active_ref[:, place] = low
            slope_ref[:, place] = (gate * plain * slope).astype(BF)
            part = low.astype(F32) * plain
            mass = put(mass, part[:, :TILE] + part[:, TILE:])
        back = put(back, dot(slope_ref[:, r * width : (r + 1) * width], firsts[r], NT))
    back = back.astype(BF)
    mass = jnp.sum(mass, axis=1, keepdims=True)
    if lead is None:
        back_ref[...] = back
        mass_ref[...] = jnp.broadcast_to(mass, mass_ref.shape)
        return
    count = rows.shape[0] // chunk
    number = lax.broadcasted_iota(jnp.int32, (rows.shape[0], 1), 0)
    lanes = lax.broadcasted_iota(jnp.int32, (1, rows.shape[1]), 1)
    inside = lax.rem(number, chunk)
    spread = jnp.zeros(rows.shape, F32)
    for piece in range(3):
        high = mass.astype(BF).astype(F32)
        spread = jnp.where(lanes == piece * half + lead + inside, high, spread)
        mass = mass - high
    own = jnp.where(number // chunk == lax.broadcasted_iota(jnp.int32, (1, TILE), 1), 1.0, 0.0).astype(BF)
    line = dot(own, spread.astype(BF), TN)
    if before is None:
        back_ref[...] = back
        for e in range(count):
            mass_ref[e] = line[e : e + 1].astype(BF)
    else:
        back_ref[:, :chunk] = back.reshape(count, chunk, back.shape[1])
        row = lax.broadcasted_iota(jnp.int32, (16, 1), 0)
        for e in range(count):
            both = line[e : e + 1] + before[e].astype(F32)
            back_ref[e, chunk:] = jnp.where(row == 0, both, 0.0).astype(BF)


def row_block(total):
    return 320 if total % 320 == 0 else total


def expert_rows_pass(lead, chunk, half, me, partner, rows, grads, router, before, firsts, seconds):
    total, width = rows.shape
    block = row_block(total)
    experts = total // chunk
    hidden = sum(f.shape[1] for f in firsts)
    here = lambda cols: pl.BlockSpec((block, cols), lambda i: (i, 0))
    whole = lambda arr: pl.BlockSpec(arr.shape, lambda i: (0, 0))
    lines = pl.BlockSpec((block // chunk, 1, width), lambda i: (i, 0, 0))
    back_shape, back_spec = (total, width), here(width)
    mass_shape, mass_spec, mass_kind = (experts, 1, width), lines, BF
    if lead is None:
        mass_shape, mass_spec, mass_kind = (total, TILE), here(TILE), F32
    elif before is not None:
        back_shape = (experts, chunk + 16, width)
        back_spec = pl.BlockSpec((block // chunk, chunk + 16, width), lambda i: (i, 0, 0))
    return pl.pallas_call(
        functools.partial(expert_kernel, lead, chunk, half),
        grid=(total // block,),
        in_specs=[pl.BlockSpec(memory_space=pltpu.SMEM), here(1), here(width), here(width), whole(router)]
        + ([lines] if before is not None else [])
        + [pl.BlockSpec(memory_space=pl.ANY)] * 8,
        out_specs=[back_spec, here(hidden), here(hidden), here(width), here(TILE), mass_spec],
        out_shape=[
            jax.ShapeDtypeStruct(back_shape, BF),
            jax.ShapeDtypeStruct((total, hidden), BF),
            jax.ShapeDtypeStruct((total, hidden), BF),
            jax.ShapeDtypeStruct((total, width), BF),
            jax.ShapeDtypeStruct((total, TILE), F32),
            jax.ShapeDtypeStruct(mass_shape, mass_kind),
        ],
        scratch_shapes=[
            pltpu.VMEM((4,) + firsts[0].shape, BF),
            pltpu.VMEM((4,) + seconds[0].shape, BF),
            pltpu.SemaphoreType.DMA((2, 4)),
        ],
        compiler_params=pltpu.CompilerParams(vmem_limit_bytes=56 * MIB),
        cost_estimate=SMALL_COST,
        name="expert_rows",
    )(me, partner, rows, grads, router, *([before] if before is not None else []), *firsts, *seconds)


def expert_rest_kernel(count, *refs):
    rows, slopes, active, gated, gates = (refs[n * count : (n + 1) * count] for n in range(5))
    seconds = refs[5 * count : 5 * count + 4]
    cross_ref, kept_ref, result_ref, total = refs[5 * count + 4 :]
    step = pl.program_id(0)
    first, second = None, None
    for n in range(count):
        first = put(first, dot(rows[n][...], slopes[n][...], TN))
        second = put(second, dot(active[n][...], gated[n][...], TN))

    @pl.when(step < 2)
    def _():
        cross_ref[0, 0] = first.astype(BF)
        cross_ref[0, 1] = second.astype(BF)

    @pl.when(step >= 2)
    def _():
        kept_ref[0, 0] = first
        kept_ref[0, 1] = second

    for k in range(4):

        @pl.when(step == k)
        def _(k=k):
            for n in range(count):
                part = dot(active[n][...], seconds[QUARTERS[k]][...])
                if k == 0:
                    total[n] = part
                elif k < 3:
                    total[n] += part
                else:
                    out = ((total[n] + part) * gates[n][:, :1]).astype(BF)
                    if count > 1:
                        result_ref[:, n] = out.reshape(result_ref.shape[0], result_ref.shape[2], result_ref.shape[3])
                    else:
                        result_ref[...] = out


QUARTERS = (2, 3, 1, 0)


def expert_rest(rows, slopes, active, gated, gates, seconds, experts):
    total, width = rows[0].shape
    hidden = slopes[0].shape[1] // 4
    count = len(rows)
    chunk = total // experts
    whole = lambda cols: pl.BlockSpec((total, cols), lambda i: (0, 0))
    part = pl.BlockSpec((total, hidden), lambda i: (0, jnp.where(i < 2, 2 + i, 3 - i)))
    shape = (experts, count, chunk, width) if count > 1 else (total, width)
    out = pl.pallas_call(
        functools.partial(expert_rest_kernel, count),
        grid=(4,),
        in_specs=[whole(width)] * count
        + [part] * (2 * count)
        + [whole(width)] * count
        + [whole(TILE)] * count
        + [pl.BlockSpec(w.shape, lambda i: (0, 0)) for w in seconds],
        out_specs=[
            pl.BlockSpec((1, 2, width, hidden), lambda i: (jnp.minimum(i, 1), 0, 0, 0)),
            pl.BlockSpec((1, 2, width, hidden), lambda i: (jnp.maximum(i, 2) - 2, 0, 0, 0)),
            pl.BlockSpec(shape, lambda i: (0,) * len(shape)),
        ],
        out_shape=[
            jax.ShapeDtypeStruct((2, 2, width, hidden), BF),
            jax.ShapeDtypeStruct((2, 2, width, hidden), F32),
            jax.ShapeDtypeStruct(shape, BF),
        ],
        scratch_shapes=[pltpu.VMEM((count, total, width), F32)],
        compiler_params=pltpu.CompilerParams(vmem_limit_bytes=60 * MIB),
        cost_estimate=SMALL_COST,
        name="expert_rest",
    )(*rows, *slopes, *active, *gated, *gates, *seconds)
    return out[0], out[1], out[2].reshape(experts, count * chunk, width)


def cross_sum_kernel(kept_ref, got_ref, out_ref):
    out_ref[...] = (kept_ref[0] + got_ref[0].astype(F32)).astype(BF)


def cross_sums(kept, got):
    _, _, width, hidden = kept.shape
    block = 256
    return pl.pallas_call(
        cross_sum_kernel,
        grid=(width // block,),
        in_specs=[
            pl.BlockSpec((1, 2, block, hidden), lambda i: (0, 0, i, 0)),
            pl.BlockSpec((1, 2, block, hidden), lambda i: (1, 0, i, 0)),
        ],
        out_specs=pl.BlockSpec((2, block, hidden), lambda i: (0, i, 0)),
        out_shape=jax.ShapeDtypeStruct((2, width, hidden), BF),
        compiler_params=pltpu.CompilerParams(vmem_limit_bytes=40 * MIB),
        cost_estimate=SMALL_COST,
        name="cross_sums",
    )(kept, got)


def last_sum_kernel(kept_ref, core_ref, y_ref, out_first, out_second):
    for n, out in enumerate((out_first, out_second)):
        out[...] = kept_ref[0, n] + core_ref[0, n].astype(F32) + y_ref[n].astype(F32)


def last_sums(kept, got_core, got_y):
    _, _, width, hidden = kept.shape
    block = 256
    here = pl.BlockSpec((block, hidden), lambda i: (i, 0))
    return pl.pallas_call(
        last_sum_kernel,
        grid=(width // block,),
        in_specs=[
            pl.BlockSpec((1, 2, block, hidden), lambda i: (1, 0, i, 0)),
            pl.BlockSpec((1, 2, block, hidden), lambda i: (0, 0, i, 0)),
            pl.BlockSpec((2, block, hidden), lambda i: (0, i, 0)),
        ],
        out_specs=[here, here],
        out_shape=[jax.ShapeDtypeStruct((width, hidden), F32)] * 2,
        compiler_params=pltpu.CompilerParams(vmem_limit_bytes=40 * MIB),
        cost_estimate=SMALL_COST,
        name="last_sums",
    )(kept, got_core, got_y)


def send_kernel(micro_ref, code_ref, rows_ref, out_ref):
    block = out_ref.shape[0]
    ids = lax.broadcasted_iota(jnp.int32, (block, 1), 0) + pl.program_id(0) * block
    hot = jnp.where((ids == code_ref[:1]) | (ids == code_ref[1:2]), 1.0, 0.0).astype(BF)
    out_ref[...] = dot(hot, rows_ref[0]).astype(BF)


def send_rows(micro, code, rows, count):
    width = rows.shape[2]
    block = next(b for b in (336, 320, 384, count) if count % b == 0)
    return pl.pallas_call(
        send_kernel,
        grid_spec=pltpu.PrefetchScalarGridSpec(
            num_scalar_prefetch=1,
            grid=(count // block,),
            in_specs=[
                pl.BlockSpec(code.shape, lambda i, m: (0, 0)),
                pl.BlockSpec((1, SEQ, width), lambda i, m: (m[0], 0, 0)),
            ],
            out_specs=pl.BlockSpec((block, width), lambda i, m: (i, 0)),
        ),
        out_shape=jax.ShapeDtypeStruct((count, width), BF),
        compiler_params=pltpu.CompilerParams(vmem_limit_bytes=40 * MIB),
        cost_estimate=SMALL_COST,
        name="send_rows",
    )(micro, code, rows)


def place_kernel(place_ref, *refs):
    for n, piece in enumerate(refs[:4]):

        @pl.when(pl.program_id(0) == n)
        def _(piece=piece):
            for k, out_ref in enumerate(refs[4:]):
                out_ref[0] = piece[k]


def place_pieces(places, pieces):
    two, rows, width = pieces[0].shape
    whole = pl.BlockSpec(pieces[0].shape, lambda i, place_ref: (0, 0, 0))
    return pl.pallas_call(
        place_kernel,
        grid_spec=pltpu.PrefetchScalarGridSpec(
            num_scalar_prefetch=1,
            grid=(4,),
            in_specs=[whole] * 4,
            out_specs=[pl.BlockSpec((1, rows, width), lambda i, place_ref: (place_ref[i], 0, 0))] * two,
        ),
        out_shape=[jax.ShapeDtypeStruct((4, rows, width), pieces[0].dtype)] * two,
        compiler_params=pltpu.CompilerParams(vmem_limit_bytes=40 * MIB),
        cost_estimate=SMALL_COST,
        name="place_pieces",
    )(places, *pieces)


def swap(value, axis, count, bit):
    return lax.ppermute(value, axis, [(i, i ^ bit) for i in range(count)])


def all_to_all(value):
    return lax.all_to_all(value, "dp", split_axis=0, concat_axis=0, tiled=True)


def together(*values):
    return lax.optimization_barrier(values)


def local(
    layer_input, out_grad, first_gain, query_weight, key_weight, value_weight, output_weight,
    position_bias, second_gain, router_weight, expert_in, expert_out, seq_lengths, routes,
):
    micro_count, tok_rows, width = layer_input.shape
    dp_count = lax.axis_size("dp")
    expert_count = router_weight.shape[1]
    shard = query_weight.shape[1]
    heads_here = position_bias.shape[0]
    assert lax.axis_size("tensor") == 4 and micro_count == 2 and expert_count == dp_count
    assert tok_rows == SEQ and seq_lengths.shape[1] == 1
    capacity = max(8, 8 * (10 * tok_rows // (32 * expert_count)))
    half = capacity // 2
    stride = 8 * (half // 8 + 1)
    by_lines = dp_count == 8
    chunks = 2 if half % 32 == 0 else 1
    chunk = half // chunks
    chunk_rows = expert_count * chunk
    rows_here = query_weight.shape[0]
    me = lax.axis_index("dp")
    rank = lax.axis_index("tensor")
    micro = rank // 2
    core = rank % 2

    def swap_y(value):
        return swap(value, "tensor", 4, 2)

    def swap_core(value):
        return swap(value, "tensor", 4, 1)

    micro_arg = micro.reshape(1).astype(jnp.int32)
    core_arg = core.reshape(1).astype(jnp.int32)

    packed = pack_weights(query_weight, key_weight, value_weight, output_weight, first_gain, second_gain, router_weight)
    three = 3 * TILE

    def doubled(stacked, bit, axis=0):
        other = swap(stacked, "dp", dp_count, bit)
        high = (me & bit) != 0
        pair = jnp.where(high, jnp.stack([other, stacked], axis + 1), jnp.stack([stacked, other], axis + 1))
        return pair.reshape(stacked.shape[:axis] + (-1,) + stacked.shape[axis + 1 :])

    stacked = packed[None]
    bit = dp_count // 2
    while bit > 1:
        stacked = doubled(stacked, bit)
        bit //= 2
    length = lax.dynamic_index_in_dim(seq_lengths, micro, 0, keepdims=False)
    route = lax.dynamic_index_in_dim(routes, micro, 0, keepdims=False).T
    expert_ids = jnp.arange(expert_count, dtype=jnp.int32)
    named = (expert_ids[:, None, None] == route[None]).astype(jnp.int32)
    per_token = jnp.sum(named, axis=1, dtype=jnp.int32)
    earlier = jnp.cumsum(per_token, axis=1, dtype=jnp.int32) - per_token
    slot = jnp.sum(named * earlier[:, None, :], axis=0, dtype=jnp.int32)
    here = slot // half == core
    within = slot % half
    chunk_of = within // chunk
    inside = within % chunk
    spare = 16 * -(-chunk // 16)
    last_stride = spare + 16
    last = (chunks - 1) * chunk_rows
    code_back = jnp.where(
        chunk_of == chunks - 1, last + route * last_stride + inside, chunk_of * chunk_rows + route * chunk + inside
    )
    code_back = code_back + jnp.where(here, 0, last + expert_count * last_stride)
    code_result = route * half + within + jnp.where(here, 0, expert_count * half)
    info = jnp.concatenate([code_back, route, slot, code_result], 0)

    code_grads = jnp.where(here, route * stride + within, -1)
    valid = jnp.arange(SEQ, dtype=jnp.int32) < length[0]
    ids = jnp.arange(expert_count * stride, dtype=jnp.int32)[:, None]
    partner = jnp.sum(
        jnp.where(ids == code_grads[:1], route[1:], 0) + jnp.where(ids == code_grads[1:], route[:1], 0), axis=1, dtype=jnp.int32
    )
    grads_sent = send_rows(micro_arg, jnp.where(valid[None], code_grads, -1), out_grad, expert_count * stride)
    grads_sent = grads_sent.reshape(expert_count, stride, width)
    partner_row = jnp.pad(partner.reshape(expert_count, stride)[:, :half].astype(BF), ((0, 0), (0, width - half)))
    grads_sent = grads_sent.at[:, half].set(partner_row)
    stacked, grads_sent, position_bias = together(stacked, grads_sent, position_bias)
    if by_lines:
        lines = [list(range(x, dp_count, 2)) for x in range(2)]
        grads_z = lax.all_to_all(
            grads_sent.reshape(dp_count // 2, 2, stride, width), "dp", split_axis=0, concat_axis=0,
            axis_index_groups=lines, tiled=True,
        )

    first_own = expert_in[0]
    second_own = expert_out[0]
    first_y = swap_y(first_own)
    part_b = stacked[:, :, :three]
    far_b = swap_y(part_b)
    part_a = doubled(stacked[:, :, three:], 1)
    part_a, far_b, first_y = together(part_a, far_b, first_y)
    pair_b = jnp.stack([part_b, far_b])
    a_own = part_a[:, :, :three]
    a_far = swap_y(a_own).reshape(width, three)
    a_own = a_own.reshape(width, three)
    pair_b = doubled(pair_b, 1, 1).reshape(2, width, three)
    if by_lines:
        a_far, pair_b, grads_z, second_own = together(a_far, pair_b, grads_z, second_own)
    else:
        a_far, pair_b, grads_sent, second_own = together(a_far, pair_b, grads_sent, second_own)
    second_y = swap_y(second_own)
    small_all = part_a[:, :, three:].reshape(width, TILE)
    gain_one = small_all[:, expert_count].astype(F32)[None]
    gain_two = small_all[:, expert_count + 1].astype(F32)[None]
    router_wide = small_all
    far_bias = swap_y(position_bias)
    bias = jnp.concatenate([position_bias[:2], far_bias[:2], position_bias[2:], far_bias[2:]], 0)
    head_total = bias.shape[0]
    hot_const = jnp.asarray(NEAR_HOT, dtype=BF)
    near = dot(bias, hot_const) - bias[:, NB - 1 :].astype(F32)
    near = near.reshape(head_total, 2, TILE, TILE)
    places = jnp.arange(TILE, dtype=jnp.int32)
    causal = jnp.stack([places[None, :] <= places[:, None], jnp.ones((TILE, TILE), bool)])
    near = jnp.where(causal[None], near, NEG)

    if by_lines:
        high = (me & 1) != 0
        kept_x = jnp.where(high, grads_z[:, 1], grads_z[:, 0])
        got_x = swap(jnp.where(high, grads_z[:, 0], grads_z[:, 1]), "dp", dp_count, 1)
    else:
        grads_here = all_to_all(grads_sent)

    qkv, normed_one, qkv_weight, output_own = norm_and_project(
        micro_arg, layer_input, gain_one, a_own, a_far, pair_b[0], pair_b[1]
    )
    output_far = swap_core(output_own)
    mixed, logs = attend(length, qkv, near)
    mixed, output_far = together(mixed, output_far)
    mixed_far = swap_core(mixed)
    code_chunks = jnp.where(here, chunk_of * chunk_rows + route * chunk + inside, -1)
    residual, parts = residual_and_rows(
        micro_arg, layer_input, mixed, mixed_far, output_own, output_far, gain_two, code_chunks, chunks * chunk_rows
    )

    if by_lines:
        parts, kept_x, got_x, second_y = together(parts, kept_x, got_x, second_y)
        pair_x = jnp.where(high, jnp.stack([got_x, kept_x], 1), jnp.stack([kept_x, got_x], 1))
        grads_here = pair_x.reshape(dp_count, stride, width)
    else:
        parts, grads_here, second_y = together(parts, grads_here, second_y)
    parts = parts.reshape(chunks, expert_count, chunk, width)
    arrived = [all_to_all(parts[0])]
    partner_here = grads_here[:, half, :half].astype(jnp.int32)

    def chunk_grads(c):
        at = slice(c * chunk, (c + 1) * chunk)
        return grads_here[:, at].reshape(chunk_rows, width), partner_here[:, at].reshape(chunk_rows, 1)

    grads_parts = [chunk_grads(c) for c in range(chunks)]
    arrived[0], grads_parts = together(arrived[0], grads_parts)

    firsts = (first_own, first_y, swap_core(first_own), swap_core(first_y))
    seconds = (second_own, second_y, swap_core(second_own), swap_core(second_y))

    for c in range(1, chunks):
        sent, arrived[-1] = together(parts[c], arrived[-1])
        arrived.append(all_to_all(sent))

    me_arg = me.reshape(1).astype(jnp.int32)
    rows_all, slopes, active, gated, gates, backs = [], [], [], [], [], []
    line = None
    for c in range(chunks):
        grads_c, partner_c = grads_parts[c]
        rows_c = arrived[c].reshape(chunk_rows, width)
        back, act, slo, gat, gte, line = expert_rows_pass(
            c * chunk if chunks > 1 else None, chunk, half, me_arg, partner_c, rows_c, grads_c, router_wide, line, firsts, seconds
        )
        rows_all.append(rows_c)
        slopes.append(slo)
        active.append(act)
        gated.append(gat)
        gates.append(gte)
        if chunks == 1:
            gate_grad = line[:, 0].reshape(expert_count, chunk)
            pieces = []
            for _ in range(3):
                piece = gate_grad.astype(BF)
                pieces.append(piece)
                gate_grad = gate_grad - piece.astype(F32)
            gate_row = jnp.pad(jnp.concatenate(pieces, 1), ((0, 0), (0, width - 3 * half)))
            back = jnp.pad(back.reshape(expert_count, chunk, width), ((0, 0), (0, last_stride - chunk), (0, 0)))
            back = back.at[:, spare].set(gate_row)
        if c + 1 < chunks:
            back, arrived[c + 1] = together(back.reshape(expert_count, chunk, width), arrived[c + 1])
        else:
            back, rows_all[-1], backs = together(back, rows_all[-1], backs)
        backs.append(all_to_all(back))
    grads_cross, grads_kept, results = expert_rest(rows_all, slopes, active, gated, gates, seconds, expert_count)
    backs[-1], results = together(backs[-1], results)
    results_own = all_to_all(results).reshape(expert_count * half, width)

    grads_in = swap_core(grads_cross)
    across_y = swap_y(cross_sums(grads_kept, grads_in))

    backs_far = [swap_core(b) for b in backs]
    residual_grad, mixed_grad, extra_early, output_sent, output_kept = combine(
        micro_arg, core_arg, length, info, out_grad, residual, mixed, gain_two, router_wide, output_own,
        backs + backs_far, half, spare,
    )

    dq, dk, dv, tiles, sums = attend_back(length, qkv, near, mixed, logs, mixed_grad, 0, head_total // 2)
    far_sent, own_parts, sent = attention_weight_grads(core_arg, normed_one, dq, dk, dv, output_sent, qkv_weight)
    far_got = swap_y(far_sent)
    sent, results_own = together(sent, results_own)
    got = swap_core(sent)
    rows_both, extra_late = both_rows(
        expert_count, micro_arg, core_arg, length, qkv_weight, (dq, dk, dv), got, layer_input, gain_one, residual_grad,
        info, residual, results_own, swap_core(results_own),
    )
    rows_both, across_y, tiles = together(rows_both, across_y, tiles)
    late_far = swap_core(extra_late)
    corner = micro * 2 + core
    corners = jnp.stack([corner, corner ^ 1, corner ^ 2, corner ^ 3]).astype(jnp.int32)
    rows_y = swap_y(rows_both)
    layer_output, input_grad = place_pieces(corners, (rows_both, swap_core(rows_both), rows_y, swap_core(rows_y)))
    layer_output = layer_output.reshape(2, SEQ, width)
    input_grad = input_grad.reshape(2, SEQ, width)
    expert_in_grad, expert_out_grad = last_sums(grads_kept, grads_in, across_y)
    far_got, expert_in_grad, expert_out_grad = together(far_got, expert_in_grad, expert_out_grad)

    tiles = tiles.reshape(head_total, 2 * TILE * TILE)
    tiles_high = tiles.astype(BF)
    tiles_rest = (tiles - tiles_high.astype(F32)).astype(BF)
    table = dot(tiles_high, hot_const, NT) + dot(tiles_rest, hot_const, NT)
    far_sum = jnp.sum(sums[:, :, 0], axis=1) - jnp.sum(table[:, : NB - 1], axis=1)
    table = jnp.concatenate([table[:, : NB - 1], far_sum[:, None]], 1)
    table_own = jnp.concatenate([table[0:2], table[4:5]], 0)
    table_far = jnp.concatenate([table[2:4], table[5:6]], 0)
    table_cols = heads_here * NB // rows_here
    table_both = jnp.concatenate([table_own.reshape(rows_here, table_cols), table_far.reshape(rows_here, table_cols)], 1)
    base = expert_count + 2
    kept = base + 2 * table_cols
    table_tile = jnp.tile(jnp.pad(table_both, ((0, 0), (base, TILE - kept))), (dp_count, 1))

    grads = packed_sums(kept, own_parts, far_got, output_kept, extra_early, extra_late, late_far, table_tile)
    arrived_grads = all_to_all(grads.reshape(dp_count, rows_here, grads.shape[1]))
    query_grad, key_grad, value_grad, output_grad, small = final_sums(kept, arrived_grads, shard)
    small_y = swap_y(small)
    both = small + small_y
    table_sum = small[:, base : base + table_cols] + small_y[:, base + table_cols : kept]
    return (
        layer_output,
        input_grad,
        both[:, expert_count],
        query_grad,
        key_grad,
        value_grad,
        output_grad.T,
        table_sum.reshape(heads_here, NB),
        both[:, expert_count + 1],
        both[:, :expert_count],
        expert_in_grad[None],
        expert_out_grad[None],
    )


def solution(mesh):
    return jax.shard_map(
        local,
        mesh=mesh,
        in_specs=(
            P(None, "dp", None),
            P(None, "dp", None),
            P("dp"),
            P("dp", "tensor"),
            P("dp", "tensor"),
            P("dp", "tensor"),
            P("tensor", "dp"),
            P("tensor", None),
            P("dp"),
            P("dp", None),
            P("dp", None, "tensor"),
            P("dp", "tensor", None),
            P(None, "dp"),
            P(None, "dp", None),
        ),
        out_specs=(
            P(None, "dp", None),
            P(None, "dp", None),
            P("dp"),
            P("dp", "tensor"),
            P("dp", "tensor"),
            P("dp", "tensor"),
            P("tensor", "dp"),
            P("tensor", None),
            P("dp"),
            P("dp", None),
            P("dp", None, "tensor"),
            P("dp", "tensor", None),
        ),
        check_vma=False,
    )
```

```python
import functools

import jax
import jax.numpy as jnp
import numpy as np
from jax import lax
from jax.experimental import pallas as pl
from jax.experimental.pallas import tpu as pltpu
from jax.sharding import PartitionSpec as P

HEAD_DIM = 64
NB = 32
SEQ = 1024
TILE = 128
QROWS = 256
NEG = -1e30
GELU_C = 0.7978845608028654
GELU_A = 0.044715

BF = jnp.bfloat16
F32 = jnp.float32

bucket_edges = np.ceil(16.0 * 8.0 ** (np.arange(1, 16) / 16.0)).astype(np.int32)


def near_tables():
    rows = np.arange(TILE)[:, None]
    cols = np.arange(TILE)[None, :]
    hots = []
    for shift in (0, TILE):
        distance = rows - cols + shift
        clipped = np.maximum(distance, 0)
        reached = np.sum(clipped[..., None] >= bucket_edges, axis=-1)
        bucket = np.minimum(clipped, 16) + reached
        hots.append(bucket[..., None] == np.arange(NB))
    hot = np.stack(hots).reshape(2 * TILE * TILE, NB).T
    return hot


NEAR_HOT = near_tables()
assert bucket_edges[-1] <= TILE


def dot(a, b, dims=((1,), (0,))):
    return lax.dot_general(a, b, (dims, ((), ())), preferred_element_type=F32)


NT = ((1,), (1,))
TN = ((0,), (0,))


MIB = 2**20
SMALL_COST = pl.CostEstimate(flops=1_000_000, bytes_accessed=1_000_000, transcendentals=0)


def score_tiles(block, half, q_half, key_ref, near_one, near_two, length):
    tiles = []
    for j in range(block + 1):
        s = dot(q_half, key_ref[j * QROWS : (j + 1) * QROWS, :], NT)
        if j == block:
            top = jnp.concatenate([s[:TILE, :TILE] + near_one, jnp.full((TILE, TILE), NEG, F32)], 1)
            low = jnp.concatenate([s[TILE:, :TILE] + near_two, s[TILE:, TILE:] + near_one], 1)
            s = jnp.concatenate([top, low], 0)
        elif j == block - 1:
            top = jnp.concatenate([s[:TILE, :TILE], s[:TILE, TILE:] + near_two], 1)
            s = jnp.concatenate([top, s[TILE:]], 0)
        if (j + 1) * QROWS > SEQ // 2:
            place = lax.broadcasted_iota(jnp.int32, (1, QROWS), 1) + j * QROWS
            s = s + jnp.where(place < length, 0.0, NEG)
        tiles.append(s)
    return tiles


def lane_half(rows):
    return lax.broadcasted_iota(jnp.int32, (rows, 2 * HEAD_DIM), 1) < HEAD_DIM


def attend_kernel(length_ref, query_ref, key_ref, value_ref, near_ref, out_ref, log_ref):
    length = length_ref[0]
    lanes = lane_half(QROWS)
    ones = jnp.ones((SEQ, TILE), BF)
    value_ext = jnp.concatenate([value_ref[...], ones], 1)
    for i in range(SEQ // QROWS):
        q_rows = query_ref[i * QROWS : (i + 1) * QROWS, :] * BF(0.125)
        outs, logs = [], []
        for h in range(2):
            keep = lanes if h == 0 else ~lanes
            q_half = jnp.where(keep, q_rows, BF(0))
            tiles = score_tiles(i, h, q_half, key_ref, near_ref[h, 0], near_ref[h, 1], length)
            top = tiles[0]
            for s in tiles[1:]:
                top = jnp.maximum(top, s)
            top = jnp.max(top, axis=1, keepdims=True)
            total = None
            for j, s in enumerate(tiles):
                p = jnp.exp(s - top).astype(BF)
                part = dot(p, value_ext[j * QROWS : (j + 1) * QROWS, :])
                total = part if total is None else total + part
            row_sum = total[:, TILE:]
            outs.append(total[:, :TILE] / row_sum)
            logs.append(top + jnp.log(row_sum))
        out_ref[i * QROWS : (i + 1) * QROWS, :] = jnp.where(lanes, outs[0], outs[1]).astype(BF)
        log_ref[i * QROWS : (i + 1) * QROWS, :] = jnp.where(lanes, logs[0], logs[1])


def attend(length, qkv, near):
    pairs = qkv.shape[1] // (3 * TILE)
    cols = pairs * TILE
    return pl.pallas_call(
        attend_kernel,
        grid=(pairs,),
        in_specs=[
            pl.BlockSpec(memory_space=pltpu.SMEM),
            pl.BlockSpec((SEQ, TILE), lambda p: (0, p)),
            pl.BlockSpec((SEQ, TILE), lambda p: (0, pairs + p)),
            pl.BlockSpec((SEQ, TILE), lambda p: (0, 2 * pairs + p)),
            pl.BlockSpec((2, 2, TILE, TILE), lambda p: (p, 0, 0, 0)),
        ],
        out_specs=[
            pl.BlockSpec((SEQ, TILE), lambda p: (0, p)),
            pl.BlockSpec((SEQ, TILE), lambda p: (0, p)),
        ],
        out_shape=[
            jax.ShapeDtypeStruct((SEQ, cols), BF),
            jax.ShapeDtypeStruct((SEQ, cols), F32),
        ],
        compiler_params=pltpu.CompilerParams(vmem_limit_bytes=40 * MIB),
        cost_estimate=SMALL_COST,
        name="attend",
    )(length, qkv, qkv, qkv, near)


def attend_back_kernel(
    length_ref, query_ref, key_ref, value_ref, near_ref, out_ref, log_ref, grad_ref,
    dq_ref, dk_ref, dv_ref, tile_ref, sum_ref, dk_acc, dv_acc,
):
    length = length_ref[0]
    lanes = lane_half(QROWS)
    lanes_all = lane_half(SEQ)
    ones = jnp.ones((SEQ, TILE), BF)
    key_ext = [
        jnp.concatenate([jnp.where(lanes_all, key_ref[...], BF(0)), ones], 1),
        jnp.concatenate([jnp.where(lanes_all, BF(0), key_ref[...]), ones], 1),
    ]
    near_sums = [[None, None], [None, None]]
    all_sums = [None, None]

    for i in range(SEQ // QROWS):
        rows = slice(i * QROWS, (i + 1) * QROWS)
        q_rows = query_ref[rows, :] * BF(0.125)
        g_rows = grad_ref[rows, :]
        mass = g_rows.astype(F32) * out_ref[rows, :].astype(F32)
        dq = None
        for h in range(2):
            keep = lanes if h == 0 else ~lanes
            q_half = jnp.where(keep, q_rows, BF(0))
            g_half = jnp.where(keep, g_rows, BF(0))
            delta = jnp.sum(jnp.where(keep, mass, 0.0), axis=1, keepdims=True)
            log_col = log_ref[rows, h * HEAD_DIM : h * HEAD_DIM + 1]
            tiles = score_tiles(i, h, q_half, key_ref, near_ref[h, 0], near_ref[h, 1], length)
            for j, s in enumerate(tiles):
                keys = slice(j * QROWS, (j + 1) * QROWS)
                p = jnp.exp(s - log_col)
                dp = dot(g_half, value_ref[keys, :], NT)
                ds = (p * (dp - delta)).astype(BF)
                part = dot(ds, key_ext[h][keys, :])
                dq = put(dq, part[:, :TILE])
                all_sums[h] = put(all_sums[h], jnp.sum(part[:, TILE:].reshape(QROWS // 8, 8, TILE), axis=0))
                dk_part = dot(ds, q_half, TN)
                dv_part = dot(p.astype(BF), g_half, TN)
                if i == j and h == 0:
                    dk_acc[keys, :] = dk_part
                    dv_acc[keys, :] = dv_part
                else:
                    dk_acc[keys, :] += dk_part
                    dv_acc[keys, :] += dv_part
                if j == i:
                    wide = ds.astype(F32)
                    near_sums[h][0] = put(near_sums[h][0], wide[:TILE, :TILE] + wide[TILE:, TILE:])
                    near_sums[h][1] = put(near_sums[h][1], wide[TILE:, :TILE])
                elif j == i - 1:
                    near_sums[h][1] = put(near_sums[h][1], ds[:TILE, TILE:].astype(F32))
        dq_ref[rows, :] = (dq * 0.125).astype(BF)
    dk_ref[...] = dk_acc[...].astype(BF)
    dv_ref[...] = dv_acc[...].astype(BF)
    for h in range(2):
        tile_ref[h, 0] = near_sums[h][0]
        tile_ref[h, 1] = near_sums[h][1]
        sum_ref[h] = all_sums[h]


def attend_back(length, qkv, near, mixed, logs, grad, first, count):
    pairs = qkv.shape[1] // (3 * TILE)
    cols = count * TILE
    col = pl.BlockSpec((SEQ, TILE), lambda p: (0, first + p))
    out = pl.BlockSpec((SEQ, TILE), lambda p: (0, p))
    return pl.pallas_call(
        attend_back_kernel,
        grid=(count,),
        in_specs=[
            pl.BlockSpec(memory_space=pltpu.SMEM),
            col,
            pl.BlockSpec((SEQ, TILE), lambda p: (0, pairs + first + p)),
            pl.BlockSpec((SEQ, TILE), lambda p: (0, 2 * pairs + first + p)),
            pl.BlockSpec((2, 2, TILE, TILE), lambda p: (first + p, 0, 0, 0)),
            col,
            col,
            col,
        ],
        out_specs=[
            out,
            out,
            out,
            pl.BlockSpec((2, 2, TILE, TILE), lambda p: (p, 0, 0, 0)),
            pl.BlockSpec((2, 8, TILE), lambda p: (p, 0, 0)),
        ],
        out_shape=[
            jax.ShapeDtypeStruct((SEQ, cols), BF),
            jax.ShapeDtypeStruct((SEQ, cols), BF),
            jax.ShapeDtypeStruct((SEQ, cols), BF),
            jax.ShapeDtypeStruct((2 * count, 2, TILE, TILE), F32),
            jax.ShapeDtypeStruct((2 * count, 8, TILE), F32),
        ],
        scratch_shapes=[pltpu.VMEM((SEQ, TILE), F32), pltpu.VMEM((SEQ, TILE), F32)],
        compiler_params=pltpu.CompilerParams(vmem_limit_bytes=40 * MIB),
        cost_estimate=SMALL_COST,
        name="attend_back",
    )(length, qkv, qkv, qkv, near, mixed, logs, grad)


def low_lanes(shape):
    return lax.broadcasted_iota(jnp.int32, shape, 1) < HEAD_DIM


def turned(tile):
    return pltpu.roll(tile, HEAD_DIM, 1)


def pack_kernel(q_ref, k_ref, v_ref, o_ref, one_ref, two_ref, router_ref, out_ref):
    shard = q_ref.shape[1]
    rows = q_ref.shape[0]
    source = lax.broadcasted_iota(jnp.int32, (shard, 6 * TILE), 0)
    target = lax.broadcasted_iota(jnp.int32, (shard, 6 * TILE), 1)

    def moved(pair_base, last_base):
        want = jnp.where(source < TILE, source + pair_base, source - TILE + last_base)
        return jnp.where(target == want, 1.0, 0.0).astype(BF)

    total = dot(v_ref[...], moved(0, 2 * TILE)) + dot(o_ref[...], moved(TILE, 2 * TILE + HEAD_DIM), TN)
    total = total + dot(q_ref[...], moved(3 * TILE, 5 * TILE)) + dot(k_ref[...], moved(4 * TILE, 5 * TILE + HEAD_DIM))
    out_ref[:, : 6 * TILE] = total.astype(BF)
    experts = router_ref.shape[0]
    own_row = lax.broadcasted_iota(jnp.int32, (rows, rows), 0) == lax.broadcasted_iota(jnp.int32, (rows, rows), 1)

    def column(ref):
        return jnp.sum(jnp.where(own_row, ref[...].astype(F32), 0.0), axis=1, keepdims=True)

    lanes = lax.broadcasted_iota(jnp.int32, (experts, TILE), 1)
    spread = jnp.where(lanes == lax.broadcasted_iota(jnp.int32, (experts, TILE), 0), 1.0, 0.0).astype(BF)
    place = lax.broadcasted_iota(jnp.int32, (rows, TILE), 1)
    small = dot(router_ref[...], spread, TN)
    small = jnp.where(place == experts, column(one_ref), jnp.where(place == experts + 1, column(two_ref), small))
    out_ref[:, 6 * TILE :] = small.astype(BF)


def pack_weights(query, key, value, output, one, two, router):
    rows = query.shape[0]
    return pl.pallas_call(
        pack_kernel,
        out_shape=jax.ShapeDtypeStruct((rows, 7 * TILE), BF),
        compiler_params=pltpu.CompilerParams(vmem_limit_bytes=60 * MIB),
        cost_estimate=SMALL_COST,
        name="pack_weights",
    )(query, key, value, output, one[None], two[None], router.T)


def qkv_kernel(micro_ref, tokens_ref, gain_ref, a_own, a_far, b_own, b_far, qkv_ref, normed_ref, weight_ref, output_ref):
    width = tokens_ref.shape[2]

    @pl.when(pl.program_id(0) == 0)
    def _():
        low = low_lanes((width, TILE))

        def tiles(own, far, pair, low_half):
            at = slice(pair * TILE, (pair + 1) * TILE)
            one, two = own[:, 2 * TILE :].astype(F32), far[:, 2 * TILE :].astype(F32)
            last = jnp.where(low, one, turned(two)) if low_half else jnp.where(low, turned(one), two)
            return own[:, at], far[:, at], last.astype(BF)

        for n, (own, far, pair, low_half) in enumerate(
            ((a_own, a_far, 0, True), (a_own, a_far, 1, False), (b_own, b_far, 0, True))
        ):
            for t, tile in enumerate(tiles(own[...], far[...], pair, low_half)):
                at = 3 * n + t
                weight_ref[:, at * TILE : (at + 1) * TILE] = tile
        for t, tile in enumerate(tiles(b_own[...], b_far[...], 1, False)):
            output_ref[:, t * TILE : (t + 1) * TILE] = tile

    x = tokens_ref[0].astype(F32)
    inverse = lax.rsqrt(jnp.mean(x * x, axis=-1, keepdims=True) + 1e-06)
    normed = (x * inverse * gain_ref[...]).astype(BF)
    normed_ref[...] = normed
    qkv_ref[...] = dot(normed, weight_ref[...]).astype(BF)


def norm_and_project(micro, layer_input, gain, a_own, a_far, b_own, b_far):
    width = layer_input.shape[2]
    block = 256
    cols = 3 * TILE
    whole = lambda rows, n: pl.BlockSpec((rows, n), lambda i, m: (0, 0))
    here = lambda n: pl.BlockSpec((block, n), lambda i, m: (i, 0))
    return pl.pallas_call(
        qkv_kernel,
        grid_spec=pltpu.PrefetchScalarGridSpec(
            num_scalar_prefetch=1,
            grid=(SEQ // block,),
            in_specs=[pl.BlockSpec((1, block, width), lambda i, m: (m[0], i, 0)), whole(1, width)] + [whole(width, cols)] * 4,
            out_specs=[here(3 * cols), here(width), whole(width, 3 * cols), whole(width, cols)],
        ),
        out_shape=[
            jax.ShapeDtypeStruct((SEQ, 3 * cols), BF),
            jax.ShapeDtypeStruct((SEQ, width), BF),
            jax.ShapeDtypeStruct((width, 3 * cols), BF),
            jax.ShapeDtypeStruct((width, cols), BF),
        ],
        compiler_params=pltpu.CompilerParams(vmem_limit_bytes=40 * MIB),
        cost_estimate=SMALL_COST,
        name="norm_and_project",
    )(micro, layer_input, gain, a_own, a_far, b_own, b_far)


def middle_kernel(
    blocks, micro_ref, tokens_ref, mixed_ref, other_ref, own_ref, far_ref, gain_ref, code_ref, residual_ref, sent_ref, normed
):
    step = pl.program_id(0)
    rows = tokens_ref.shape[1]

    @pl.when(step < blocks)
    def _():
        total = tokens_ref[0].astype(F32) + dot(mixed_ref[...], own_ref[...], NT) + dot(other_ref[...], far_ref[...], NT)
        residual_ref[...] = total
        inverse = lax.rsqrt(jnp.mean(total * total, axis=-1, keepdims=True) + 1e-06)
        normed[pl.ds(pl.multiple_of(step * rows, rows), rows), :] = (total * inverse * gain_ref[...]).astype(BF)

    @pl.when(step >= blocks)
    def _():
        block = sent_ref.shape[0]
        ids = lax.broadcasted_iota(jnp.int32, (block, 1), 0) + (step - blocks) * block
        hot = jnp.where((ids == code_ref[:1]) | (ids == code_ref[1:2]), 1.0, 0.0).astype(BF)
        sent_ref[...] = dot(hot, normed[...]).astype(BF)


def residual_and_rows(micro, layer_input, mixed, other, output_own, output_far, gain, code, count):
    width = layer_input.shape[2]
    block = 256
    blocks = SEQ // block
    send = 320
    cols = mixed.shape[1]
    at = lambda i: jnp.minimum(i, blocks - 1)
    whole = lambda arr: pl.BlockSpec(arr.shape, lambda i, m: (0, 0))
    here = lambda n: pl.BlockSpec((block, n), lambda i, m: (at(i), 0))
    return pl.pallas_call(
        functools.partial(middle_kernel, blocks),
        grid_spec=pltpu.PrefetchScalarGridSpec(
            num_scalar_prefetch=1,
            grid=(blocks + count // send,),
            in_specs=[
                pl.BlockSpec((1, block, width), lambda i, m: (m[0], at(i), 0)),
                here(cols), here(cols), whole(output_own), whole(output_far), whole(gain), whole(code),
            ],
            out_specs=[here(width), pl.BlockSpec((send, width), lambda i, m: (jnp.maximum(i, blocks) - blocks, 0))],
            scratch_shapes=[pltpu.VMEM((SEQ, width), BF)],
        ),
        out_shape=[jax.ShapeDtypeStruct((SEQ, width), F32), jax.ShapeDtypeStruct((count, width), BF)],
        compiler_params=pltpu.CompilerParams(vmem_limit_bytes=40 * MIB),
        cost_estimate=SMALL_COST,
        name="residual_and_rows",
    )(micro, layer_input, mixed, other, output_own, output_far, gain, code)


def picked_rows(first, second, segments):
    total = None
    start = 0
    for rows in segments:
        length = rows.shape[0]
        ids = lax.broadcasted_iota(jnp.int32, (1, length), 1) + start
        hot = jnp.where((first == ids) | (second == ids), 1.0, 0.0).astype(BF)
        total = put(total, dot(hot, rows))
        start += length
    return total


def put(a, b):
    return b if a is None else a + b


def folded(product):
    return jnp.sum(product.reshape(product.shape[0] // 8, 8, product.shape[1]), axis=0)


def as_column(eight):
    ones = jnp.ones((16, TILE), BF)
    high = eight.astype(BF)
    rest = (eight - high.astype(F32)).astype(BF)
    return dot(jnp.concatenate([high, rest], 0), ones, TN)


def combine_kernel(experts, half, spare, micro_ref, core_ref, length_ref, *refs):
    info_ref, grad_ref, residual_ref, mixed_ref, gain_ref, router_ref, output_ref = refs[:7]
    backs = refs[7:-9]
    (total_ref, mixed_grad_ref, extra_ref, far_ref, own_ref, acc_ref, router_acc, gain_acc, tables) = refs[-9:]
    block = residual_ref.shape[0]
    step = pl.program_id(0)
    count = len(backs) // 2

    @pl.when(step == 0)
    def _():
        place = lax.broadcasted_iota(jnp.int32, (experts, 1), 0)
        for n, back in enumerate((backs[count - 1], backs[2 * count - 1])):
            table = jnp.zeros((experts, back.shape[2]), F32)
            for e in range(experts):
                row = back[e, spare : spare + 16, :].astype(F32)[:1]
                table = jnp.where(place == e, row, table)
            for piece in range(3):
                at = (3 * n + piece) * experts
                tables[at : at + experts] = table[:, piece * half : (piece + 1) * half]

    info = jnp.transpose(info_ref[...])
    number = lambda n: info[:, n : n + 1]
    columns = lax.broadcasted_iota(jnp.int32, (1, half), 1)
    lanes = lax.broadcasted_iota(jnp.int32, (1, 6 * experts), 1)
    table = tables[...].astype(BF)
    values = []
    for k in range(2):
        slot = number(4 + k)
        hot = jnp.where(columns == lax.rem(slot, half), 1.0, 0.0).astype(BF)
        found = dot(hot, table, NT)
        wanted = jnp.where(slot // half == core_ref[0], 0, 3 * experts) + number(2 + k)
        away = lanes - wanted
        hit = (away == 0) | (away == experts) | (away == 2 * experts)
        values.append(jnp.sum(jnp.where(hit, found, 0.0), axis=1, keepdims=True))
    wide = lax.broadcasted_iota(jnp.int32, (1, TILE), 1)
    is_first, is_second = wide == number(2), wide == number(3)
    residual = residual_ref[...]
    gain = gain_ref[...]
    inverse = lax.rsqrt(jnp.mean(residual * residual, axis=-1, keepdims=True) + 1e-06)
    plain = residual * inverse
    normed = (plain * gain).astype(BF)
    logits = dot(normed, router_ref[...])
    gap = jnp.sum(jnp.where(is_first, logits, 0.0) - jnp.where(is_second, logits, 0.0), axis=1, keepdims=True)
    small = jnp.exp(-jnp.abs(gap))
    logit = small / ((1.0 + small) * (1.0 + small)) * (values[0] - values[1])
    logit_grad = jnp.where(is_first, logit, jnp.where(is_second, -logit, 0.0)).astype(BF)
    segments = [b[...].reshape(b.shape[0] * b.shape[1], b.shape[2]) for b in backs]
    normed_grad = picked_rows(number(0), number(1), segments) + dot(logit_grad, router_ref[...], NT)
    scaled = normed_grad * gain
    mean = jnp.mean(scaled * plain, axis=-1, keepdims=True)
    place = lax.broadcasted_iota(jnp.int32, (block, 1), 0) + step * block
    grad_out = jnp.where(place < length_ref[0], grad_ref[0].astype(F32), 0.0)
    total = grad_out + inverse * (scaled - plain * mean)
    total_ref[...] = total
    branch = total.astype(BF)
    mixed_grad_ref[...] = dot(branch, output_ref[...]).astype(BF)
    router_part = dot(logit_grad, normed, TN)
    gain_part = folded(normed_grad * plain)
    output_part = dot(mixed_ref[...], branch, TN)

    @pl.when(step == 0)
    def _():
        router_acc[...] = router_part
        gain_acc[...] = gain_part
        acc_ref[...] = output_part

    @pl.when(step > 0)
    def _():
        router_acc[...] += router_part
        gain_acc[...] += gain_part
        acc_ref[...] += output_part

    @pl.when(step == pl.num_programs(0) - 1)
    def _():
        extra_ref[...] = jnp.transpose(router_acc[...]) + jnp.where(wide == experts + 1, as_column(gain_acc[...]), 0.0)
        parts = jnp.transpose(acc_ref[...])
        far_ref[...] = parts[:, TILE:].astype(BF)
        own_ref[:, :TILE] = parts[:, :TILE]
        own_ref[:, TILE:] = parts[:, 2 * TILE :]


def combine(micro, core, length, info, out_grad, residual, mixed, gain, router, output_own, backs, half, spare):
    width = residual.shape[1]
    block = 512
    cols = mixed.shape[1]
    whole = lambda arr: pl.BlockSpec(arr.shape, lambda i, *_: (0,) * arr.ndim)
    fixed = lambda rows, n: pl.BlockSpec((rows, n), lambda i, *_: (0, 0))
    here = lambda n: pl.BlockSpec((block, n), lambda i, *_: (i, 0))
    experts = backs[0].shape[0]
    return pl.pallas_call(
        functools.partial(combine_kernel, experts, half, spare),
        grid_spec=pltpu.PrefetchScalarGridSpec(
            num_scalar_prefetch=3,
            grid=(SEQ // block,),
            in_specs=[
                pl.BlockSpec((8, block), lambda i, *_: (0, i)),
                pl.BlockSpec((1, block, width), lambda i, m, *_: (m[0], i, 0)),
                here(width), here(cols), whole(gain), whole(router), whole(output_own),
            ]
            + [whole(x) for x in backs],
            out_specs=[here(width), here(cols), fixed(width, TILE), fixed(width, 2 * TILE), fixed(width, 2 * TILE)],
            scratch_shapes=[
                pltpu.VMEM((cols, width), F32),
                pltpu.VMEM((TILE, width), F32),
                pltpu.VMEM((8, width), F32),
                pltpu.VMEM((6 * experts, half), F32),
            ],
        ),
        out_shape=[
            jax.ShapeDtypeStruct((SEQ, width), F32),
            jax.ShapeDtypeStruct((SEQ, cols), BF),
            jax.ShapeDtypeStruct((width, TILE), F32),
            jax.ShapeDtypeStruct((width, 2 * TILE), BF),
            jax.ShapeDtypeStruct((width, 2 * TILE), F32),
        ],
        compiler_params=pltpu.CompilerParams(vmem_limit_bytes=40 * MIB),
        cost_estimate=SMALL_COST,
        name="combine",
    )(micro, core, length, info, out_grad, residual, mixed, gain, router, output_own, *backs)


def projected_back(weight_ref, grads):
    total = None
    for n, grad in enumerate(grads):
        cols = grad.shape[1]
        total = put(total, dot(grad[...], weight_ref[:, n * cols : (n + 1) * cols], NT))
    return total


def attention_weight_kernel(
    blocks, core_ref, normed_ref, q_ref, k_ref, v_ref, output_ref, weight_ref, q_rows, k_rows, v_rows, far_ref, own_ref, sent_ref
):
    step = pl.program_id(0)

    @pl.when(step < blocks)
    def _():
        low = low_lanes((normed_ref.shape[1], TILE))
        q, k, v = (dot(normed_ref[...], d[...], TN) for d in (q_ref, k_ref, v_ref))
        for n, part in enumerate((q, k, v)):
            own_ref[:, n * TILE : (n + 1) * TILE] = part[:, :TILE]
            far_ref[:, n * TILE : (n + 1) * TILE] = part[:, TILE : 2 * TILE].astype(BF)
        q, k, v = (part[:, 2 * TILE :] for part in (q, k, v))
        far_ref[:, 3 * TILE : 4 * TILE] = jnp.where(low, turned(q), k).astype(BF)
        far_ref[:, 4 * TILE : 5 * TILE] = jnp.where(low, turned(v), output_ref[:, TILE:].astype(F32)).astype(BF)
        far_ref[:, 5 * TILE :] = output_ref[:, :TILE]
        own_ref[:, 3 * TILE : 4 * TILE] = jnp.where(low, q, turned(k))
        own_ref[:, 4 * TILE :] = jnp.where(low, v, 0.0)

    @pl.when(step >= blocks)
    def _():
        sent_ref[...] = projected_back(weight_ref, (q_rows, k_rows, v_rows))


def attention_weight_grads(core, normed, q, k, v, output, weight):
    width = normed.shape[1]
    block = 256
    blocks = width // block
    at = lambda i: jnp.minimum(i, blocks - 1)
    later = lambda i: jnp.maximum(i, blocks) - blocks
    whole = lambda arr: pl.BlockSpec(arr.shape, lambda i, c: (0, 0))
    here = lambda n: pl.BlockSpec((block, n), lambda i, c: (at(i), 0))
    rows = pl.BlockSpec((block, q.shape[1]), lambda i, c: ((1 - c[0]) * 2 + later(i), 0))
    return pl.pallas_call(
        functools.partial(attention_weight_kernel, blocks),
        grid_spec=pltpu.PrefetchScalarGridSpec(
            num_scalar_prefetch=1,
            grid=(blocks + 2,),
            in_specs=[
                pl.BlockSpec((SEQ, block), lambda i, c: (0, at(i))),
                whole(q), whole(k), whole(v), here(2 * TILE), whole(weight), rows, rows, rows,
            ],
            out_specs=[here(6 * TILE), here(5 * TILE), pl.BlockSpec((block, width), lambda i, c: (later(i), 0))],
        ),
        out_shape=[
            jax.ShapeDtypeStruct((width, 6 * TILE), BF),
            jax.ShapeDtypeStruct((width, 5 * TILE), F32),
            jax.ShapeDtypeStruct((2 * block, width), F32),
        ],
        compiler_params=pltpu.CompilerParams(vmem_limit_bytes=40 * MIB),
        cost_estimate=SMALL_COST,
        name="attention_weight_grads",
    )(core, normed, q, k, v, output, weight, q, k, v)


def both_kernel(
    lane, micro_ref, core_ref, length_ref, weight_ref, q, k, v, got_ref, tokens_ref, gain_ref, grad_ref,
    info_ref, residual_ref, own_ref, far_ref, out_ref, extra_ref, acc_ref,
):
    block = residual_ref.shape[0]
    info = jnp.transpose(info_ref[...])
    place = lax.broadcasted_iota(jnp.int32, (block, 1), 0) + (core_ref[0] * 2 + pl.program_id(0)) * block
    rows = residual_ref[...] + picked_rows(info[:, 6:7], info[:, 7:8], (own_ref[...], far_ref[...]))
    out_ref[0] = jnp.where(place < length_ref[0], rows, 0.0).astype(BF)
    normed_grad = got_ref[...] + projected_back(weight_ref, (q, k, v))
    x = tokens_ref[0].astype(F32)
    inverse = lax.rsqrt(jnp.mean(x * x, axis=-1, keepdims=True) + 1e-06)
    plain = x * inverse
    scaled = normed_grad * gain_ref[...]
    mean = jnp.mean(scaled * plain, axis=-1, keepdims=True)
    out_ref[1] = (grad_ref[...] + inverse * (scaled - plain * mean)).astype(BF)
    wide = lax.broadcasted_iota(jnp.int32, (1, TILE), 1)
    part = folded(normed_grad * plain)

    @pl.when(pl.program_id(0) == 0)
    def _():
        acc_ref[...] = part

    @pl.when(pl.program_id(0) == 1)
    def _():
        extra_ref[...] = jnp.where(wide == lane, as_column(acc_ref[...] + part), 0.0)


def both_rows(lane, micro, core, length, weight, grads, got, layer_input, gain, residual_grad, info, residual, own, far):
    width = weight.shape[0]
    block = 256
    here = lambda n: pl.BlockSpec((block, n), lambda i, m, c, *_: (c[0] * 2 + i, 0))
    whole = lambda arr: pl.BlockSpec(arr.shape, lambda i, *_: (0, 0))
    return pl.pallas_call(
        functools.partial(both_kernel, lane),
        grid_spec=pltpu.PrefetchScalarGridSpec(
            num_scalar_prefetch=3,
            grid=(2,),
            in_specs=[whole(weight)]
            + [here(grads[0].shape[1])] * 3
            + [
                pl.BlockSpec((block, width), lambda i, *_: (i, 0)),
                pl.BlockSpec((1, block, width), lambda i, m, c, *_: (m[0], c[0] * 2 + i, 0)),
                whole(gain),
                here(width),
                pl.BlockSpec((8, block), lambda i, m, c, *_: (0, c[0] * 2 + i)),
                here(width),
                whole(own),
                whole(far),
            ],
            out_specs=[
                pl.BlockSpec((2, block, width), lambda i, *_: (0, i, 0)),
                pl.BlockSpec((width, TILE), lambda i, *_: (0, 0)),
            ],
            scratch_shapes=[pltpu.VMEM((8, width), F32)],
        ),
        out_shape=[jax.ShapeDtypeStruct((2, 2 * block, width), BF), jax.ShapeDtypeStruct((width, TILE), F32)],
        compiler_params=pltpu.CompilerParams(vmem_limit_bytes=40 * MIB),
        cost_estimate=SMALL_COST,
        name="both_rows",
    )(micro, core, length, weight, *grads, got, layer_input, gain, residual_grad, info, residual, own, far)


def sum_kernel(kept, own, got, out_own, early, late, late_far, table, sum_ref):
    low = low_lanes(early.shape)
    sum_ref[:, : 4 * TILE] = (own[:, : 4 * TILE] + got[:, : 4 * TILE].astype(F32)).astype(BF)
    mixed = jnp.where(low, own[:, 4 * TILE :], turned(out_own[:, TILE:]))
    sum_ref[:, 4 * TILE : 5 * TILE] = (mixed + got[:, 4 * TILE : 5 * TILE].astype(F32)).astype(BF)
    sum_ref[:, 5 * TILE : 6 * TILE] = (out_own[:, :TILE] + got[:, 5 * TILE :].astype(F32)).astype(BF)
    extra = early[...] + late[...] + late_far[...] + table[...]
    high = extra.astype(BF)
    rest = extra - high.astype(F32)
    if kept <= HEAD_DIM:
        sum_ref[:, 6 * TILE :] = jnp.where(low, high.astype(F32), turned(rest)).astype(BF)
    else:
        sum_ref[:, 6 * TILE : 7 * TILE] = high
        sum_ref[:, 7 * TILE :] = rest.astype(BF)


def packed_sums(kept, *parts):
    width = parts[0].shape[0]
    cols = (7 if kept <= HEAD_DIM else 8) * TILE
    block = 256
    here = lambda n: pl.BlockSpec((block, n), lambda i: (i, 0))
    return pl.pallas_call(
        functools.partial(sum_kernel, kept),
        grid=(width // block,),
        in_specs=[here(x.shape[1]) for x in parts],
        out_specs=here(cols),
        out_shape=jax.ShapeDtypeStruct((width, cols), BF),
        compiler_params=pltpu.CompilerParams(vmem_limit_bytes=40 * MIB),
        cost_estimate=SMALL_COST,
        name="packed_sums",
    )(*parts)


def final_kernel(kept, parts_ref, q_ref, k_ref, v_ref, o_ref, small_ref):
    total = parts_ref[0].astype(F32)
    for n in range(1, parts_ref.shape[0]):
        total = total + parts_ref[n].astype(F32)
    tile = lambda t: total[:, t * TILE : (t + 1) * TILE]
    q_ref[:, :TILE] = tile(0)
    q_ref[:, TILE:] = tile(3)[:, :HEAD_DIM]
    k_ref[:, :TILE] = tile(1)
    k_ref[:, TILE:] = turned(tile(3))[:, :HEAD_DIM]
    v_ref[:, :TILE] = tile(2)
    v_ref[:, TILE:] = tile(4)[:, :HEAD_DIM]
    o_ref[:, :TILE] = tile(5)
    o_ref[:, TILE:] = turned(tile(4))[:, :HEAD_DIM]
    small_ref[...] = tile(6) + (turned(tile(6)) if kept <= HEAD_DIM else tile(7))


def final_sums(kept, parts, shard):
    rows = parts.shape[1]
    return pl.pallas_call(
        functools.partial(final_kernel, kept),
        out_shape=[jax.ShapeDtypeStruct((rows, shard), F32)] * 4 + [jax.ShapeDtypeStruct((rows, TILE), F32)],
        compiler_params=pltpu.CompilerParams(vmem_limit_bytes=40 * MIB),
        cost_estimate=SMALL_COST,
        name="final_sums",
    )(parts)


def pair_gate(logits, own, other):
    lanes = lax.broadcasted_iota(jnp.int32, logits.shape, 1)
    gap = jnp.sum(
        jnp.where(lanes == own, logits, 0.0) - jnp.where(lanes == other, logits, 0.0), axis=1, keepdims=True
    )
    small = jnp.exp(-jnp.abs(gap))
    return jnp.where(gap >= 0.0, 1.0, small) / (1.0 + small)


def expert_kernel(lead, chunk, half, me_ref, partner_ref, rows_ref, grads_ref, router_ref, *refs):
    before, refs = (refs[0], refs[1:]) if lead is not None and lead > 0 else (None, refs)
    firsts, seconds = refs[:4], refs[4:8]
    back_ref, active_ref, slope_ref, gated_ref, gate_ref, mass_ref = refs[8:]
    rows = rows_ref[...]
    grads = grads_ref[...]
    gate = pair_gate(dot(rows, router_ref[...]), me_ref[0], partner_ref[...])
    gated_ref[...] = (gate * grads.astype(F32)).astype(BF)
    gate_ref[...] = jnp.broadcast_to(gate, gate_ref.shape)
    mass = None
    back = None
    width = firsts[0].shape[1]
    step = 256
    places = [(r, c) for r in range(4) for c in range(0, width, step)]

    def products(r, c):
        return dot(rows, firsts[r][:, c : c + step]), dot(grads, seconds[r][c : c + step, :], NT)

    ahead = products(*places[0])
    for n, (r, c) in enumerate(places):
        x, plain = ahead
        if n + 1 < len(places):
            ahead = products(*places[n + 1])
        square = x * x
        bent = jnp.tanh(x * (GELU_C + (GELU_C * GELU_A) * square))
        rise = 0.5 + 0.5 * bent
        active = x * rise
        slope = rise + active * (1.0 - bent) * (GELU_C + (3.0 * GELU_C * GELU_A) * square)
        low = active.astype(BF)
        place = slice(r * width + c, r * width + c + step)
        active_ref[:, place] = low
        slope_ref[:, place] = (gate * plain * slope).astype(BF)
        part = low.astype(F32) * plain
        mass = put(mass, part[:, :TILE] + part[:, TILE:])
        if c + step == width and r > 0:
            back = put(back, dot(slope_ref[:, (r - 1) * width : r * width], firsts[r - 1][...], NT))
    back = put(back, dot(slope_ref[:, 3 * width :], firsts[3][...], NT))
    back = back.astype(BF)
    mass = jnp.sum(mass, axis=1, keepdims=True)
    if lead is None:
        back_ref[...] = back
        mass_ref[...] = jnp.broadcast_to(mass, mass_ref.shape)
        return
    count = rows.shape[0] // chunk
    number = lax.broadcasted_iota(jnp.int32, (rows.shape[0], 1), 0)
    lanes = lax.broadcasted_iota(jnp.int32, (1, rows.shape[1]), 1)
    inside = lax.rem(number, chunk)
    spread = jnp.zeros(rows.shape, F32)
    for piece in range(3):
        high = mass.astype(BF).astype(F32)
        spread = jnp.where(lanes == piece * half + lead + inside, high, spread)
        mass = mass - high
    own = jnp.where(number // chunk == lax.broadcasted_iota(jnp.int32, (1, TILE), 1), 1.0, 0.0).astype(BF)
    line = dot(own, spread.astype(BF), TN)
    if before is None:
        back_ref[...] = back
        for e in range(count):
            mass_ref[e] = line[e : e + 1].astype(BF)
    else:
        back_ref[:, :chunk] = back.reshape(count, chunk, back.shape[1])
        row = lax.broadcasted_iota(jnp.int32, (16, 1), 0)
        for e in range(count):
            both = line[e : e + 1] + before[e].astype(F32)
            back_ref[e, chunk:] = jnp.where(row == 0, both, 0.0).astype(BF)


def row_block(total):
    return 320 if total % 320 == 0 else total


def expert_rows_pass(lead, chunk, half, me, partner, rows, grads, router, before, firsts, seconds):
    total, width = rows.shape
    block = row_block(total)
    experts = total // chunk
    hidden = sum(f.shape[1] for f in firsts)
    here = lambda cols: pl.BlockSpec((block, cols), lambda i: (i, 0))
    whole = lambda arr: pl.BlockSpec(arr.shape, lambda i: (0, 0))
    lines = pl.BlockSpec((block // chunk, 1, width), lambda i: (i, 0, 0))
    back_shape, back_spec = (total, width), here(width)
    mass_shape, mass_spec, mass_kind = (experts, 1, width), lines, BF
    if lead is None:
        mass_shape, mass_spec, mass_kind = (total, TILE), here(TILE), F32
    elif before is not None:
        back_shape = (experts, chunk + 16, width)
        back_spec = pl.BlockSpec((block // chunk, chunk + 16, width), lambda i: (i, 0, 0))
    return pl.pallas_call(
        functools.partial(expert_kernel, lead, chunk, half),
        grid=(total // block,),
        in_specs=[pl.BlockSpec(memory_space=pltpu.SMEM), here(1), here(width), here(width), whole(router)]
        + ([lines] if before is not None else [])
        + [whole(w) for w in firsts]
        + [whole(w) for w in seconds],
        out_specs=[back_spec, here(hidden), here(hidden), here(width), here(TILE), mass_spec],
        out_shape=[
            jax.ShapeDtypeStruct(back_shape, BF),
            jax.ShapeDtypeStruct((total, hidden), BF),
            jax.ShapeDtypeStruct((total, hidden), BF),
            jax.ShapeDtypeStruct((total, width), BF),
            jax.ShapeDtypeStruct((total, TILE), F32),
            jax.ShapeDtypeStruct(mass_shape, mass_kind),
        ],
        compiler_params=pltpu.CompilerParams(vmem_limit_bytes=56 * MIB),
        cost_estimate=SMALL_COST,
        name="expert_rows",
    )(me, partner, rows, grads, router, *([before] if before is not None else []), *firsts, *seconds)


def expert_weight_kernel(count, *refs):
    rows, slopes, active, gated = (refs[n * count : (n + 1) * count] for n in range(4))
    cross_ref, kept_ref = refs[4 * count :]
    step = pl.program_id(0)
    first, second = None, None
    for n in range(count):
        first = put(first, dot(rows[n][...], slopes[n][...], TN))
        second = put(second, dot(active[n][...], gated[n][...], TN))

    @pl.when(step < 2)
    def _():
        cross_ref[0, 0] = first.astype(BF)
        cross_ref[0, 1] = second.astype(BF)

    @pl.when(step >= 2)
    def _():
        kept_ref[0, 0] = first
        kept_ref[0, 1] = second


def expert_weight_grads(rows, slopes, active, gated):
    total, width = rows[0].shape
    hidden = slopes[0].shape[1] // 4
    count = len(rows)
    whole = pl.BlockSpec((total, width), lambda i: (0, 0))
    part = pl.BlockSpec((total, hidden), lambda i: (0, jnp.where(i < 2, 2 + i, 3 - i)))
    return pl.pallas_call(
        functools.partial(expert_weight_kernel, count),
        grid=(4,),
        in_specs=[whole] * count + [part] * (2 * count) + [whole] * count,
        out_specs=[
            pl.BlockSpec((1, 2, width, hidden), lambda i: (jnp.minimum(i, 1), 0, 0, 0)),
            pl.BlockSpec((1, 2, width, hidden), lambda i: (jnp.maximum(i, 2) - 2, 0, 0, 0)),
        ],
        out_shape=[
            jax.ShapeDtypeStruct((2, 2, width, hidden), BF),
            jax.ShapeDtypeStruct((2, 2, width, hidden), F32),
        ],
        compiler_params=pltpu.CompilerParams(vmem_limit_bytes=56 * MIB),
        cost_estimate=SMALL_COST,
        name="expert_weight_grads",
    )(*rows, *slopes, *active, *gated)


def result_kernel(chunks, *refs):
    active, gates, seconds, out_ref = refs[:chunks], refs[chunks : 2 * chunks], refs[2 * chunks : -1], refs[-1]
    for c in range(chunks):

        @pl.when(pl.program_id(0) == c)
        def _(c=c):
            width = seconds[0].shape[0]
            total = None
            for r, second in enumerate(seconds):
                total = put(total, dot(active[c][:, r * width : (r + 1) * width], second[...]))
            rows = (total * gates[c][:, :1]).astype(BF)
            if chunks > 1:
                out_ref[:, 0] = rows.reshape(out_ref.shape[0], out_ref.shape[2], out_ref.shape[3])
            else:
                out_ref[...] = rows


def expert_results(active, gates, seconds, experts):
    chunks = len(active)
    total, hidden = active[0].shape
    width = seconds[0].shape[1]
    block = row_block(total)
    steps = total // block

    def here(c, cols):
        return pl.BlockSpec((block, cols), lambda g, i: (jnp.where(g == c, i, jnp.where(g < c, 0, steps - 1)), 0))

    chunk = total // experts
    if chunks > 1:
        shape = (experts, chunks, chunk, width)
        out_spec = pl.BlockSpec((block // chunk, 1, chunk, width), lambda g, i: (i, g, 0, 0))
    else:
        shape = (total, width)
        out_spec = pl.BlockSpec((block, width), lambda g, i: (i, 0))
    out = pl.pallas_call(
        functools.partial(result_kernel, chunks),
        grid=(chunks, steps),
        in_specs=[here(c, hidden) for c in range(chunks)]
        + [here(c, TILE) for c in range(chunks)]
        + [pl.BlockSpec(w.shape, lambda g, i: (0, 0)) for w in seconds],
        out_specs=out_spec,
        out_shape=jax.ShapeDtypeStruct(shape, BF),
        compiler_params=pltpu.CompilerParams(vmem_limit_bytes=56 * MIB),
        cost_estimate=SMALL_COST,
        name="expert_results",
    )(*active, *gates, *seconds)
    return out.reshape(experts, chunks * chunk, width)


def cross_sum_kernel(kept_ref, got_ref, out_ref):
    out_ref[...] = (kept_ref[0] + got_ref[0].astype(F32)).astype(BF)


def cross_sums(kept, got):
    _, _, width, hidden = kept.shape
    block = 256
    return pl.pallas_call(
        cross_sum_kernel,
        grid=(width // block,),
        in_specs=[
            pl.BlockSpec((1, 2, block, hidden), lambda i: (0, 0, i, 0)),
            pl.BlockSpec((1, 2, block, hidden), lambda i: (1, 0, i, 0)),
        ],
        out_specs=pl.BlockSpec((2, block, hidden), lambda i: (0, i, 0)),
        out_shape=jax.ShapeDtypeStruct((2, width, hidden), BF),
        compiler_params=pltpu.CompilerParams(vmem_limit_bytes=40 * MIB),
        cost_estimate=SMALL_COST,
        name="cross_sums",
    )(kept, got)


def last_sum_kernel(kept_ref, core_ref, y_ref, out_first, out_second):
    for n, out in enumerate((out_first, out_second)):
        out[...] = kept_ref[0, n] + core_ref[0, n].astype(F32) + y_ref[n].astype(F32)


def last_sums(kept, got_core, got_y):
    _, _, width, hidden = kept.shape
    block = 256
    here = pl.BlockSpec((block, hidden), lambda i: (i, 0))
    return pl.pallas_call(
        last_sum_kernel,
        grid=(width // block,),
        in_specs=[
            pl.BlockSpec((1, 2, block, hidden), lambda i: (1, 0, i, 0)),
            pl.BlockSpec((1, 2, block, hidden), lambda i: (0, 0, i, 0)),
            pl.BlockSpec((2, block, hidden), lambda i: (0, i, 0)),
        ],
        out_specs=[here, here],
        out_shape=[jax.ShapeDtypeStruct((width, hidden), F32)] * 2,
        compiler_params=pltpu.CompilerParams(vmem_limit_bytes=40 * MIB),
        cost_estimate=SMALL_COST,
        name="last_sums",
    )(kept, got_core, got_y)


def send_kernel(micro_ref, code_ref, rows_ref, out_ref):
    block = out_ref.shape[0]
    ids = lax.broadcasted_iota(jnp.int32, (block, 1), 0) + pl.program_id(0) * block
    hot = jnp.where((ids == code_ref[:1]) | (ids == code_ref[1:2]), 1.0, 0.0).astype(BF)
    out_ref[...] = dot(hot, rows_ref[0]).astype(BF)


def send_rows(micro, code, rows, count):
    width = rows.shape[2]
    block = next(b for b in (336, 320, 384, count) if count % b == 0)
    return pl.pallas_call(
        send_kernel,
        grid_spec=pltpu.PrefetchScalarGridSpec(
            num_scalar_prefetch=1,
            grid=(count // block,),
            in_specs=[
                pl.BlockSpec(code.shape, lambda i, m: (0, 0)),
                pl.BlockSpec((1, SEQ, width), lambda i, m: (m[0], 0, 0)),
            ],
            out_specs=pl.BlockSpec((block, width), lambda i, m: (i, 0)),
        ),
        out_shape=jax.ShapeDtypeStruct((count, width), BF),
        compiler_params=pltpu.CompilerParams(vmem_limit_bytes=40 * MIB),
        cost_estimate=SMALL_COST,
        name="send_rows",
    )(micro, code, rows)


def place_kernel(place_ref, *refs):
    for n, piece in enumerate(refs[:4]):

        @pl.when(pl.program_id(0) == n)
        def _(piece=piece):
            for k, out_ref in enumerate(refs[4:]):
                out_ref[0] = piece[k]


def place_pieces(places, pieces):
    two, rows, width = pieces[0].shape
    whole = pl.BlockSpec(pieces[0].shape, lambda i, place_ref: (0, 0, 0))
    return pl.pallas_call(
        place_kernel,
        grid_spec=pltpu.PrefetchScalarGridSpec(
            num_scalar_prefetch=1,
            grid=(4,),
            in_specs=[whole] * 4,
            out_specs=[pl.BlockSpec((1, rows, width), lambda i, place_ref: (place_ref[i], 0, 0))] * two,
        ),
        out_shape=[jax.ShapeDtypeStruct((4, rows, width), pieces[0].dtype)] * two,
        compiler_params=pltpu.CompilerParams(vmem_limit_bytes=40 * MIB),
        cost_estimate=SMALL_COST,
        name="place_pieces",
    )(places, *pieces)


def swap(value, axis, count, bit):
    return lax.ppermute(value, axis, [(i, i ^ bit) for i in range(count)])


def all_to_all(value):
    return lax.all_to_all(value, "dp", split_axis=0, concat_axis=0, tiled=True)


def together(*values):
    return lax.optimization_barrier(values)


def local(
    layer_input, out_grad, first_gain, query_weight, key_weight, value_weight, output_weight,
    position_bias, second_gain, router_weight, expert_in, expert_out, seq_lengths, routes,
):
    micro_count, tok_rows, width = layer_input.shape
    dp_count = lax.axis_size("dp")
    expert_count = router_weight.shape[1]
    shard = query_weight.shape[1]
    heads_here = position_bias.shape[0]
    assert lax.axis_size("tensor") == 4 and micro_count == 2 and expert_count == dp_count
    assert tok_rows == SEQ and seq_lengths.shape[1] == 1
    capacity = max(8, 8 * (10 * tok_rows // (32 * expert_count)))
    half = capacity // 2
    stride = 8 * (half // 8 + 1)
    by_lines = dp_count == 8
    chunks = 2 if half % 32 == 0 else 1
    chunk = half // chunks
    chunk_rows = expert_count * chunk
    rows_here = query_weight.shape[0]
    me = lax.axis_index("dp")
    rank = lax.axis_index("tensor")
    micro = rank // 2
    core = rank % 2

    def swap_y(value):
        return swap(value, "tensor", 4, 2)

    def swap_core(value):
        return swap(value, "tensor", 4, 1)

    micro_arg = micro.reshape(1).astype(jnp.int32)
    core_arg = core.reshape(1).astype(jnp.int32)

    packed = pack_weights(query_weight, key_weight, value_weight, output_weight, first_gain, second_gain, router_weight)
    three = 3 * TILE

    def doubled(stacked, bit, axis=0):
        other = swap(stacked, "dp", dp_count, bit)
        high = (me & bit) != 0
        pair = jnp.where(high, jnp.stack([other, stacked], axis + 1), jnp.stack([stacked, other], axis + 1))
        return pair.reshape(stacked.shape[:axis] + (-1,) + stacked.shape[axis + 1 :])

    stacked = packed[None]
    bit = dp_count // 2
    while bit > 1:
        stacked = doubled(stacked, bit)
        bit //= 2
    length = lax.dynamic_index_in_dim(seq_lengths, micro, 0, keepdims=False)
    route = lax.dynamic_index_in_dim(routes, micro, 0, keepdims=False).T
    expert_ids = jnp.arange(expert_count, dtype=jnp.int32)
    named = (expert_ids[:, None, None] == route[None]).astype(jnp.int32)
    per_token = jnp.sum(named, axis=1, dtype=jnp.int32)
    earlier = jnp.cumsum(per_token, axis=1, dtype=jnp.int32) - per_token
    slot = jnp.sum(named * earlier[:, None, :], axis=0, dtype=jnp.int32)
    here = slot // half == core
    within = slot % half
    chunk_of = within // chunk
    inside = within % chunk
    spare = 16 * -(-chunk // 16)
    last_stride = spare + 16
    last = (chunks - 1) * chunk_rows
    code_back = jnp.where(
        chunk_of == chunks - 1, last + route * last_stride + inside, chunk_of * chunk_rows + route * chunk + inside
    )
    code_back = code_back + jnp.where(here, 0, last + expert_count * last_stride)
    code_result = route * half + within + jnp.where(here, 0, expert_count * half)
    info = jnp.concatenate([code_back, route, slot, code_result], 0)

    code_grads = jnp.where(here, route * stride + within, -1)
    valid = jnp.arange(SEQ, dtype=jnp.int32) < length[0]
    ids = jnp.arange(expert_count * stride, dtype=jnp.int32)[:, None]
    partner = jnp.sum(
        jnp.where(ids == code_grads[:1], route[1:], 0) + jnp.where(ids == code_grads[1:], route[:1], 0), axis=1, dtype=jnp.int32
    )
    grads_sent = send_rows(micro_arg, jnp.where(valid[None], code_grads, -1), out_grad, expert_count * stride)
    grads_sent = grads_sent.reshape(expert_count, stride, width)
    partner_row = jnp.pad(partner.reshape(expert_count, stride)[:, :half].astype(BF), ((0, 0), (0, width - half)))
    grads_sent = grads_sent.at[:, half].set(partner_row)
    stacked, grads_sent, position_bias = together(stacked, grads_sent, position_bias)
    if by_lines:
        lines = [list(range(x, dp_count, 2)) for x in range(2)]
        grads_z = lax.all_to_all(
            grads_sent.reshape(dp_count // 2, 2, stride, width), "dp", split_axis=0, concat_axis=0,
            axis_index_groups=lines, tiled=True,
        )

    first_own = expert_in[0]
    second_own = expert_out[0]
    part_b = stacked[:, :, :three]
    far_b = swap_y(part_b)
    part_a = doubled(stacked[:, :, three:], 1)
    part_a, far_b = together(part_a, far_b)
    pair_b = jnp.stack([part_b, far_b])
    a_own = part_a[:, :, :three]
    a_far = swap_y(a_own).reshape(width, three)
    a_own = a_own.reshape(width, three)
    pair_b = doubled(pair_b, 1, 1).reshape(2, width, three)
    if by_lines:
        a_far, pair_b, grads_z, first_own = together(a_far, pair_b, grads_z, first_own)
    else:
        a_far, pair_b, grads_sent, first_own = together(a_far, pair_b, grads_sent, first_own)
    first_y = swap_y(first_own)
    small_all = part_a[:, :, three:].reshape(width, TILE)
    gain_one = small_all[:, expert_count].astype(F32)[None]
    gain_two = small_all[:, expert_count + 1].astype(F32)[None]
    router_wide = small_all
    far_bias = swap_y(position_bias)
    bias = jnp.concatenate([position_bias[:2], far_bias[:2], position_bias[2:], far_bias[2:]], 0)
    head_total = bias.shape[0]
    hot_const = jnp.asarray(NEAR_HOT, dtype=BF)
    near = dot(bias, hot_const) - bias[:, NB - 1 :].astype(F32)
    near = near.reshape(head_total, 2, TILE, TILE)
    places = jnp.arange(TILE, dtype=jnp.int32)
    causal = jnp.stack([places[None, :] <= places[:, None], jnp.ones((TILE, TILE), bool)])
    near = jnp.where(causal[None], near, NEG)

    if by_lines:
        high = (me & 1) != 0
        kept_x = jnp.where(high, grads_z[:, 1], grads_z[:, 0])
        got_x = swap(jnp.where(high, grads_z[:, 0], grads_z[:, 1]), "dp", dp_count, 1)
    else:
        grads_here = all_to_all(grads_sent)

    qkv, normed_one, qkv_weight, output_own = norm_and_project(
        micro_arg, layer_input, gain_one, a_own, a_far, pair_b[0], pair_b[1]
    )
    output_far = swap_core(output_own)
    mixed, logs = attend(length, qkv, near)
    mixed, output_far = together(mixed, output_far)
    mixed_far = swap_core(mixed)
    code_chunks = jnp.where(here, chunk_of * chunk_rows + route * chunk + inside, -1)
    residual, parts = residual_and_rows(
        micro_arg, layer_input, mixed, mixed_far, output_own, output_far, gain_two, code_chunks, chunks * chunk_rows
    )

    if by_lines:
        parts, kept_x, got_x, first_y, second_own = together(parts, kept_x, got_x, first_y, second_own)
        pair_x = jnp.where(high, jnp.stack([got_x, kept_x], 1), jnp.stack([kept_x, got_x], 1))
        grads_here = pair_x.reshape(dp_count, stride, width)
    else:
        parts, grads_here, first_y, second_own = together(parts, grads_here, first_y, second_own)
    second_y = swap_y(second_own)
    parts = parts.reshape(chunks, expert_count, chunk, width)
    arrived = [all_to_all(parts[0])]
    partner_here = grads_here[:, half, :half].astype(jnp.int32)

    def chunk_grads(c):
        at = slice(c * chunk, (c + 1) * chunk)
        return grads_here[:, at].reshape(chunk_rows, width), partner_here[:, at].reshape(chunk_rows, 1)

    grads_parts = [chunk_grads(c) for c in range(chunks)]
    arrived[0], grads_parts, second_y = together(arrived[0], grads_parts, second_y)

    firsts = (first_own, first_y, swap_core(first_own), swap_core(first_y))
    seconds = (second_own, second_y, swap_core(second_own), swap_core(second_y))

    for c in range(1, chunks):
        sent, arrived[-1] = together(parts[c], arrived[-1])
        arrived.append(all_to_all(sent))

    me_arg = me.reshape(1).astype(jnp.int32)
    rows_all, slopes, active, gated, gates, backs = [], [], [], [], [], []
    line = None
    for c in range(chunks):
        grads_c, partner_c = grads_parts[c]
        rows_c = arrived[c].reshape(chunk_rows, width)
        back, act, slo, gat, gte, line = expert_rows_pass(
            c * chunk if chunks > 1 else None, chunk, half, me_arg, partner_c, rows_c, grads_c, router_wide, line, firsts, seconds
        )
        rows_all.append(rows_c)
        slopes.append(slo)
        active.append(act)
        gated.append(gat)
        gates.append(gte)
        if chunks == 1:
            gate_grad = line[:, 0].reshape(expert_count, chunk)
            pieces = []
            for _ in range(3):
                piece = gate_grad.astype(BF)
                pieces.append(piece)
                gate_grad = gate_grad - piece.astype(F32)
            gate_row = jnp.pad(jnp.concatenate(pieces, 1), ((0, 0), (0, width - 3 * half)))
            back = jnp.pad(back.reshape(expert_count, chunk, width), ((0, 0), (0, last_stride - chunk), (0, 0)))
            back = back.at[:, spare].set(gate_row)
        if c + 1 < chunks:
            back, arrived[c + 1] = together(back.reshape(expert_count, chunk, width), arrived[c + 1])
        else:
            back, rows_all[-1], backs = together(back, rows_all[-1], backs)
        backs.append(all_to_all(back))
    grads_cross, grads_kept = expert_weight_grads(rows_all, slopes, active, gated)
    gates, grads_cross = together(gates, grads_cross)
    grads_in = swap_core(grads_cross)
    results = expert_results(active, gates, seconds, expert_count)
    backs[-1], results = together(backs[-1], results)
    results_own = all_to_all(results).reshape(expert_count * half, width)

    across_y = swap_y(cross_sums(grads_kept, grads_in))

    backs_far = [swap_core(b) for b in backs]
    residual_grad, mixed_grad, extra_early, output_sent, output_kept = combine(
        micro_arg, core_arg, length, info, out_grad, residual, mixed, gain_two, router_wide, output_own,
        backs + backs_far, half, spare,
    )

    dq, dk, dv, tiles, sums = attend_back(length, qkv, near, mixed, logs, mixed_grad, 0, head_total // 2)
    far_sent, own_parts, sent = attention_weight_grads(core_arg, normed_one, dq, dk, dv, output_sent, qkv_weight)
    far_got = swap_y(far_sent)
    sent, results_own = together(sent, results_own)
    got = swap_core(sent)
    rows_both, extra_late = both_rows(
        expert_count, micro_arg, core_arg, length, qkv_weight, (dq, dk, dv), got, layer_input, gain_one, residual_grad,
        info, residual, results_own, swap_core(results_own),
    )
    rows_both, across_y, tiles = together(rows_both, across_y, tiles)
    late_far = swap_core(extra_late)
    corner = micro * 2 + core
    corners = jnp.stack([corner, corner ^ 1, corner ^ 2, corner ^ 3]).astype(jnp.int32)
    rows_y = swap_y(rows_both)
    layer_output, input_grad = place_pieces(corners, (rows_both, swap_core(rows_both), rows_y, swap_core(rows_y)))
    layer_output = layer_output.reshape(2, SEQ, width)
    input_grad = input_grad.reshape(2, SEQ, width)
    expert_in_grad, expert_out_grad = last_sums(grads_kept, grads_in, across_y)
    far_got, expert_in_grad, expert_out_grad = together(far_got, expert_in_grad, expert_out_grad)

    tiles = tiles.reshape(head_total, 2 * TILE * TILE)
    tiles_high = tiles.astype(BF)
    tiles_rest = (tiles - tiles_high.astype(F32)).astype(BF)
    table = dot(tiles_high, hot_const, NT) + dot(tiles_rest, hot_const, NT)
    far_sum = jnp.sum(sums[:, :, 0], axis=1) - jnp.sum(table[:, : NB - 1], axis=1)
    table = jnp.concatenate([table[:, : NB - 1], far_sum[:, None]], 1)
    table_own = jnp.concatenate([table[0:2], table[4:5]], 0)
    table_far = jnp.concatenate([table[2:4], table[5:6]], 0)
    table_cols = heads_here * NB // rows_here
    table_both = jnp.concatenate([table_own.reshape(rows_here, table_cols), table_far.reshape(rows_here, table_cols)], 1)
    base = expert_count + 2
    kept = base + 2 * table_cols
    table_tile = jnp.tile(jnp.pad(table_both, ((0, 0), (base, TILE - kept))), (dp_count, 1))

    grads = packed_sums(kept, own_parts, far_got, output_kept, extra_early, extra_late, late_far, table_tile)
    arrived_grads = all_to_all(grads.reshape(dp_count, rows_here, grads.shape[1]))
    arrived_grads, layer_output, input_grad = together(arrived_grads, layer_output, input_grad)
    query_grad, key_grad, value_grad, output_grad, small = final_sums(kept, arrived_grads, shard)
    small_y = swap_y(small)
    both = small + small_y
    table_sum = small[:, base : base + table_cols] + small_y[:, base + table_cols : kept]
    return (
        layer_output,
        input_grad,
        both[:, expert_count],
        query_grad,
        key_grad,
        value_grad,
        output_grad.T,
        table_sum.reshape(heads_here, NB),
        both[:, expert_count + 1],
        both[:, :expert_count],
        expert_in_grad[None],
        expert_out_grad[None],
    )


def solution(mesh):
    return jax.shard_map(
        local,
        mesh=mesh,
        in_specs=(
            P(None, "dp", None),
            P(None, "dp", None),
            P("dp"),
            P("dp", "tensor"),
            P("dp", "tensor"),
            P("dp", "tensor"),
            P("tensor", "dp"),
            P("tensor", None),
            P("dp"),
            P("dp", None),
            P("dp", None, "tensor"),
            P("dp", "tensor", None),
            P(None, "dp"),
            P(None, "dp", None),
        ),
        out_specs=(
            P(None, "dp", None),
            P(None, "dp", None),
            P("dp"),
            P("dp", "tensor"),
            P("dp", "tensor"),
            P("dp", "tensor"),
            P("tensor", "dp"),
            P("tensor", None),
            P("dp"),
            P("dp", None),
            P("dp", None, "tensor"),
            P("dp", "tensor", None),
        ),
        check_vma=False,
    )
```

```python
import functools

import jax
import jax.numpy as jnp
import numpy as np
from jax import lax
from jax.experimental import pallas as pl
from jax.experimental.pallas import tpu as pltpu
from jax.sharding import PartitionSpec as P

HEAD_DIM = 64
NB = 32
SEQ = 1024
TILE = 128
QROWS = 256
NEG = -1e30
GELU_C = 0.7978845608028654
GELU_A = 0.044715

BF = jnp.bfloat16
F32 = jnp.float32

bucket_edges = np.ceil(16.0 * 8.0 ** (np.arange(1, 16) / 16.0)).astype(np.int32)


def near_tables():
    rows = np.arange(TILE)[:, None]
    cols = np.arange(TILE)[None, :]
    hots = []
    for shift in (0, TILE):
        distance = rows - cols + shift
        clipped = np.maximum(distance, 0)
        reached = np.sum(clipped[..., None] >= bucket_edges, axis=-1)
        bucket = np.minimum(clipped, 16) + reached
        hots.append(bucket[..., None] == np.arange(NB))
    hot = np.stack(hots).reshape(2 * TILE * TILE, NB).T
    return hot


NEAR_HOT = near_tables()
assert bucket_edges[-1] <= TILE


def dot(a, b, dims=((1,), (0,))):
    return lax.dot_general(a, b, (dims, ((), ())), preferred_element_type=F32)


NT = ((1,), (1,))
TN = ((0,), (0,))


MIB = 2**20
SMALL_COST = pl.CostEstimate(flops=1_000_000, bytes_accessed=1_000_000, transcendentals=0)


STRIP = 32


def score_strip(s, block, j, start, near_ref, half, length):
    rows = slice(start, start + STRIP)
    part = s[rows]
    near = slice(start % TILE, start % TILE + STRIP)
    if j == block:
        if start < TILE:
            left = part[:, :TILE] + near_ref[half, 0, near, :]
            right = jnp.full((STRIP, TILE), NEG, F32)
        else:
            left = part[:, :TILE] + near_ref[half, 1, near, :]
            right = part[:, TILE:] + near_ref[half, 0, near, :]
        part = jnp.concatenate([left, right], 1)
    elif j == block - 1 and start < TILE:
        part = jnp.concatenate([part[:, :TILE], part[:, TILE:] + near_ref[half, 1, near, :]], 1)
    if (j + 1) * QROWS > SEQ // 2:
        place = lax.broadcasted_iota(jnp.int32, (1, QROWS), 1) + j * QROWS
        part = part + jnp.where(place < length, 0.0, NEG)
    return part


def lane_half(rows):
    return lax.broadcasted_iota(jnp.int32, (rows, 2 * HEAD_DIM), 1) < HEAD_DIM


def attend_kernel(length_ref, query_ref, key_ref, value_ref, near_ref, out_ref, log_ref):
    length = length_ref[0]
    lanes = lane_half(QROWS)
    ones = jnp.ones((SEQ, TILE), BF)
    value_ext = jnp.concatenate([value_ref[...], ones], 1)
    for i in range(SEQ // QROWS):
        q_rows = query_ref[i * QROWS : (i + 1) * QROWS, :] * BF(0.125)
        outs, logs = [], []
        for h in range(2):
            keep = lanes if h == 0 else ~lanes
            q_half = jnp.where(keep, q_rows, BF(0))
            tiles = [dot(q_half, key_ref[j * QROWS : (j + 1) * QROWS, :], NT) for j in range(i + 1)]
            tops = []
            weights = [[] for _ in tiles]
            for start in range(0, QROWS, STRIP):
                strips = [score_strip(s, i, j, start, near_ref, h, length) for j, s in enumerate(tiles)]
                top = strips[0]
                for s in strips[1:]:
                    top = jnp.maximum(top, s)
                top = jnp.max(top, axis=1, keepdims=True)
                tops.append(top)
                for j, s in enumerate(strips):
                    weights[j].append(jnp.exp(s - top).astype(BF))
            top = jnp.concatenate(tops, 0)
            total = None
            for j, strips in enumerate(weights):
                part = dot(jnp.concatenate(strips, 0), value_ext[j * QROWS : (j + 1) * QROWS, :])
                total = part if total is None else total + part
            row_sum = total[:, TILE:]
            outs.append(total[:, :TILE] / row_sum)
            logs.append(top + jnp.log(row_sum))
        out_ref[i * QROWS : (i + 1) * QROWS, :] = jnp.where(lanes, outs[0], outs[1]).astype(BF)
        log_ref[i * QROWS : (i + 1) * QROWS, :] = jnp.where(lanes, logs[0], logs[1])


def attend(length, qkv, near):
    pairs = qkv.shape[1] // (3 * TILE)
    cols = pairs * TILE
    return pl.pallas_call(
        attend_kernel,
        grid=(pairs,),
        in_specs=[
            pl.BlockSpec(memory_space=pltpu.SMEM),
            pl.BlockSpec((SEQ, TILE), lambda p: (0, p)),
            pl.BlockSpec((SEQ, TILE), lambda p: (0, pairs + p)),
            pl.BlockSpec((SEQ, TILE), lambda p: (0, 2 * pairs + p)),
            pl.BlockSpec((2, 2, TILE, TILE), lambda p: (p, 0, 0, 0)),
        ],
        out_specs=[
            pl.BlockSpec((SEQ, TILE), lambda p: (0, p)),
            pl.BlockSpec((SEQ, TILE), lambda p: (0, p)),
        ],
        out_shape=[
            jax.ShapeDtypeStruct((SEQ, cols), BF),
            jax.ShapeDtypeStruct((SEQ, cols), F32),
        ],
        compiler_params=pltpu.CompilerParams(vmem_limit_bytes=40 * MIB),
        cost_estimate=SMALL_COST,
        name="attend",
    )(length, qkv, qkv, qkv, near)


def attend_back_kernel(
    length_ref, query_ref, key_ref, value_ref, near_ref, out_ref, log_ref, grad_ref,
    dq_ref, dk_ref, dv_ref, tile_ref, sum_ref, dk_acc, dv_acc,
):
    length = length_ref[0]
    lanes = lane_half(QROWS)
    lanes_all = lane_half(SEQ)
    ones = jnp.ones((SEQ, TILE), BF)
    key_ext = [
        jnp.concatenate([jnp.where(lanes_all, key_ref[...], BF(0)), ones], 1),
        jnp.concatenate([jnp.where(lanes_all, BF(0), key_ref[...]), ones], 1),
    ]
    near_sums = [[None, None], [None, None]]
    all_sums = [None, None]

    for i in range(SEQ // QROWS):
        rows = slice(i * QROWS, (i + 1) * QROWS)
        q_rows = query_ref[rows, :] * BF(0.125)
        g_rows = grad_ref[rows, :]
        mass = g_rows.astype(F32) * out_ref[rows, :].astype(F32)
        dq = None
        for h in range(2):
            keep = lanes if h == 0 else ~lanes
            q_half = jnp.where(keep, q_rows, BF(0))
            g_half = jnp.where(keep, g_rows, BF(0))
            delta = jnp.sum(jnp.where(keep, mass, 0.0), axis=1, keepdims=True)
            log_col = log_ref[rows, h * HEAD_DIM : h * HEAD_DIM + 1]
            for j in range(i + 1):
                keys = slice(j * QROWS, (j + 1) * QROWS)
                s = dot(q_half, key_ref[keys, :], NT)
                dp = dot(g_half, value_ref[keys, :], NT)
                p_strips, d_strips = [], []
                for start in range(0, QROWS, STRIP):
                    strip = slice(start, start + STRIP)
                    p = jnp.exp(score_strip(s, i, j, start, near_ref, h, length) - log_col[strip])
                    p_strips.append(p.astype(BF))
                    d_strips.append((p * (dp[strip] - delta[strip])).astype(BF))
                p, ds = jnp.concatenate(p_strips, 0), jnp.concatenate(d_strips, 0)
                part = dot(ds, key_ext[h][keys, :])
                dq = put(dq, part[:, :TILE])
                all_sums[h] = put(all_sums[h], jnp.sum(part[:, TILE:].reshape(QROWS // 8, 8, TILE), axis=0))
                dk_part = dot(ds, q_half, TN)
                dv_part = dot(p, g_half, TN)
                if i == j and h == 0:
                    dk_acc[keys, :] = dk_part
                    dv_acc[keys, :] = dv_part
                else:
                    dk_acc[keys, :] += dk_part
                    dv_acc[keys, :] += dv_part
                if j == i:
                    wide = ds.astype(F32)
                    near_sums[h][0] = put(near_sums[h][0], wide[:TILE, :TILE] + wide[TILE:, TILE:])
                    near_sums[h][1] = put(near_sums[h][1], wide[TILE:, :TILE])
                elif j == i - 1:
                    near_sums[h][1] = put(near_sums[h][1], ds[:TILE, TILE:].astype(F32))
        dq_ref[rows, :] = (dq * 0.125).astype(BF)
    dk_ref[...] = dk_acc[...].astype(BF)
    dv_ref[...] = dv_acc[...].astype(BF)
    for h in range(2):
        tile_ref[h, 0] = near_sums[h][0]
        tile_ref[h, 1] = near_sums[h][1]
        sum_ref[h] = all_sums[h]


def attend_back(length, qkv, near, mixed, logs, grad, first, count):
    pairs = qkv.shape[1] // (3 * TILE)
    cols = count * TILE
    col = pl.BlockSpec((SEQ, TILE), lambda p: (0, first + p))
    out = pl.BlockSpec((SEQ, TILE), lambda p: (0, p))
    return pl.pallas_call(
        attend_back_kernel,
        grid=(count,),
        in_specs=[
            pl.BlockSpec(memory_space=pltpu.SMEM),
            col,
            pl.BlockSpec((SEQ, TILE), lambda p: (0, pairs + first + p)),
            pl.BlockSpec((SEQ, TILE), lambda p: (0, 2 * pairs + first + p)),
            pl.BlockSpec((2, 2, TILE, TILE), lambda p: (first + p, 0, 0, 0)),
            col,
            col,
            col,
        ],
        out_specs=[
            out,
            out,
            out,
            pl.BlockSpec((2, 2, TILE, TILE), lambda p: (p, 0, 0, 0)),
            pl.BlockSpec((2, 8, TILE), lambda p: (p, 0, 0)),
        ],
        out_shape=[
            jax.ShapeDtypeStruct((SEQ, cols), BF),
            jax.ShapeDtypeStruct((SEQ, cols), BF),
            jax.ShapeDtypeStruct((SEQ, cols), BF),
            jax.ShapeDtypeStruct((2 * count, 2, TILE, TILE), F32),
            jax.ShapeDtypeStruct((2 * count, 8, TILE), F32),
        ],
        scratch_shapes=[pltpu.VMEM((SEQ, TILE), F32), pltpu.VMEM((SEQ, TILE), F32)],
        compiler_params=pltpu.CompilerParams(vmem_limit_bytes=40 * MIB),
        cost_estimate=SMALL_COST,
        name="attend_back",
    )(length, qkv, qkv, qkv, near, mixed, logs, grad)


def low_lanes(shape):
    return lax.broadcasted_iota(jnp.int32, shape, 1) < HEAD_DIM


def turned(tile):
    return pltpu.roll(tile, HEAD_DIM, 1)


def pack_kernel(q_ref, k_ref, v_ref, o_ref, one_ref, two_ref, router_ref, out_ref):
    shard = q_ref.shape[1]
    rows = q_ref.shape[0]
    source = lax.broadcasted_iota(jnp.int32, (shard, 6 * TILE), 0)
    target = lax.broadcasted_iota(jnp.int32, (shard, 6 * TILE), 1)

    def moved(pair_base, last_base):
        want = jnp.where(source < TILE, source + pair_base, source - TILE + last_base)
        return jnp.where(target == want, 1.0, 0.0).astype(BF)

    total = dot(v_ref[...], moved(0, 2 * TILE)) + dot(o_ref[...], moved(TILE, 2 * TILE + HEAD_DIM), TN)
    total = total + dot(q_ref[...], moved(3 * TILE, 5 * TILE)) + dot(k_ref[...], moved(4 * TILE, 5 * TILE + HEAD_DIM))
    out_ref[:, : 6 * TILE] = total.astype(BF)
    experts = router_ref.shape[0]
    own_row = lax.broadcasted_iota(jnp.int32, (rows, rows), 0) == lax.broadcasted_iota(jnp.int32, (rows, rows), 1)

    def column(ref):
        return jnp.sum(jnp.where(own_row, ref[...].astype(F32), 0.0), axis=1, keepdims=True)

    lanes = lax.broadcasted_iota(jnp.int32, (experts, TILE), 1)
    spread = jnp.where(lanes == lax.broadcasted_iota(jnp.int32, (experts, TILE), 0), 1.0, 0.0).astype(BF)
    place = lax.broadcasted_iota(jnp.int32, (rows, TILE), 1)
    small = dot(router_ref[...], spread, TN)
    small = jnp.where(place == experts, column(one_ref), jnp.where(place == experts + 1, column(two_ref), small))
    out_ref[:, 6 * TILE :] = small.astype(BF)


def pack_weights(query, key, value, output, one, two, router):
    rows = query.shape[0]
    return pl.pallas_call(
        pack_kernel,
        out_shape=jax.ShapeDtypeStruct((rows, 7 * TILE), BF),
        compiler_params=pltpu.CompilerParams(vmem_limit_bytes=60 * MIB),
        cost_estimate=SMALL_COST,
        name="pack_weights",
    )(query, key, value, output, one[None], two[None], router.T)


def qkv_kernel(micro_ref, tokens_ref, gain_ref, a_own, a_far, b_own, b_far, qkv_ref, normed_ref, weight_ref, output_ref):
    width = tokens_ref.shape[2]

    @pl.when(pl.program_id(0) == 0)
    def _():
        low = low_lanes((width, TILE))

        def tiles(own, far, pair, low_half):
            at = slice(pair * TILE, (pair + 1) * TILE)
            one, two = own[:, 2 * TILE :].astype(F32), far[:, 2 * TILE :].astype(F32)
            last = jnp.where(low, one, turned(two)) if low_half else jnp.where(low, turned(one), two)
            return own[:, at], far[:, at], last.astype(BF)

        for n, (own, far, pair, low_half) in enumerate(
            ((a_own, a_far, 0, True), (a_own, a_far, 1, False), (b_own, b_far, 0, True))
        ):
            for t, tile in enumerate(tiles(own[...], far[...], pair, low_half)):
                at = 3 * n + t
                weight_ref[:, at * TILE : (at + 1) * TILE] = tile
        for t, tile in enumerate(tiles(b_own[...], b_far[...], 1, False)):
            output_ref[:, t * TILE : (t + 1) * TILE] = tile

    x = tokens_ref[0].astype(F32)
    inverse = lax.rsqrt(jnp.mean(x * x, axis=-1, keepdims=True) + 1e-06)
    normed = (x * inverse * gain_ref[...]).astype(BF)
    normed_ref[...] = normed
    qkv_ref[...] = dot(normed, weight_ref[...]).astype(BF)


def norm_and_project(micro, layer_input, gain, a_own, a_far, b_own, b_far):
    width = layer_input.shape[2]
    block = 256
    cols = 3 * TILE
    whole = lambda rows, n: pl.BlockSpec((rows, n), lambda i, m: (0, 0))
    here = lambda n: pl.BlockSpec((block, n), lambda i, m: (i, 0))
    return pl.pallas_call(
        qkv_kernel,
        grid_spec=pltpu.PrefetchScalarGridSpec(
            num_scalar_prefetch=1,
            grid=(SEQ // block,),
            in_specs=[pl.BlockSpec((1, block, width), lambda i, m: (m[0], i, 0)), whole(1, width)] + [whole(width, cols)] * 4,
            out_specs=[here(3 * cols), here(width), whole(width, 3 * cols), whole(width, cols)],
        ),
        out_shape=[
            jax.ShapeDtypeStruct((SEQ, 3 * cols), BF),
            jax.ShapeDtypeStruct((SEQ, width), BF),
            jax.ShapeDtypeStruct((width, 3 * cols), BF),
            jax.ShapeDtypeStruct((width, cols), BF),
        ],
        compiler_params=pltpu.CompilerParams(vmem_limit_bytes=40 * MIB),
        cost_estimate=SMALL_COST,
        name="norm_and_project",
    )(micro, layer_input, gain, a_own, a_far, b_own, b_far)


def middle_kernel(
    blocks, micro_ref, tokens_ref, mixed_ref, other_ref, own_ref, far_ref, gain_ref, code_ref, residual_ref, sent_ref, normed
):
    step = pl.program_id(0)
    rows = tokens_ref.shape[1]

    @pl.when(step < blocks)
    def _():
        total = tokens_ref[0].astype(F32) + dot(mixed_ref[...], own_ref[...], NT) + dot(other_ref[...], far_ref[...], NT)
        residual_ref[...] = total
        inverse = lax.rsqrt(jnp.mean(total * total, axis=-1, keepdims=True) + 1e-06)
        normed[pl.ds(pl.multiple_of(step * rows, rows), rows), :] = (total * inverse * gain_ref[...]).astype(BF)

    @pl.when(step >= blocks)
    def _():
        block = sent_ref.shape[0]
        ids = lax.broadcasted_iota(jnp.int32, (block, 1), 0) + (step - blocks) * block
        hot = jnp.where((ids == code_ref[:1]) | (ids == code_ref[1:2]), 1.0, 0.0).astype(BF)
        sent_ref[...] = dot(hot, normed[...]).astype(BF)


def residual_and_rows(micro, layer_input, mixed, other, output_own, output_far, gain, code, count):
    width = layer_input.shape[2]
    block = 256
    blocks = SEQ // block
    send = 320
    cols = mixed.shape[1]
    at = lambda i: jnp.minimum(i, blocks - 1)
    whole = lambda arr: pl.BlockSpec(arr.shape, lambda i, m: (0, 0))
    here = lambda n: pl.BlockSpec((block, n), lambda i, m: (at(i), 0))
    return pl.pallas_call(
        functools.partial(middle_kernel, blocks),
        grid_spec=pltpu.PrefetchScalarGridSpec(
            num_scalar_prefetch=1,
            grid=(blocks + count // send,),
            in_specs=[
                pl.BlockSpec((1, block, width), lambda i, m: (m[0], at(i), 0)),
                here(cols), here(cols), whole(output_own), whole(output_far), whole(gain), whole(code),
            ],
            out_specs=[here(width), pl.BlockSpec((send, width), lambda i, m: (jnp.maximum(i, blocks) - blocks, 0))],
            scratch_shapes=[pltpu.VMEM((SEQ, width), BF)],
        ),
        out_shape=[jax.ShapeDtypeStruct((SEQ, width), F32), jax.ShapeDtypeStruct((count, width), BF)],
        compiler_params=pltpu.CompilerParams(vmem_limit_bytes=40 * MIB),
        cost_estimate=SMALL_COST,
        name="residual_and_rows",
    )(micro, layer_input, mixed, other, output_own, output_far, gain, code)


def picked_rows(first, second, segments):
    total = None
    start = 0
    for rows in segments:
        length = rows.shape[0]
        ids = lax.broadcasted_iota(jnp.int32, (1, length), 1) + start
        hot = []
        for at in range(0, first.shape[0], STRIP):
            one, two = first[at : at + STRIP], second[at : at + STRIP]
            hot.append(jnp.where((one == ids) | (two == ids), 1.0, 0.0).astype(BF))
        total = put(total, dot(jnp.concatenate(hot, 0), rows))
        start += length
    return total


def put(a, b):
    return b if a is None else a + b


def folded(product):
    return jnp.sum(product.reshape(product.shape[0] // 8, 8, product.shape[1]), axis=0)


def as_column(eight):
    ones = jnp.ones((16, TILE), BF)
    high = eight.astype(BF)
    rest = (eight - high.astype(F32)).astype(BF)
    return dot(jnp.concatenate([high, rest], 0), ones, TN)


def combine_kernel(experts, half, spare, micro_ref, core_ref, length_ref, *refs):
    info_ref, grad_ref, residual_ref, mixed_ref, gain_ref, router_ref, output_ref = refs[:7]
    backs = refs[7:-9]
    (total_ref, mixed_grad_ref, extra_ref, far_ref, own_ref, acc_ref, router_acc, gain_acc, tables) = refs[-9:]
    block = residual_ref.shape[0]
    step = pl.program_id(0)
    count = len(backs) // 2

    @pl.when(step == 0)
    def _():
        place = lax.broadcasted_iota(jnp.int32, (experts, 1), 0)
        for n, back in enumerate((backs[count - 1], backs[2 * count - 1])):
            table = jnp.zeros((experts, back.shape[2]), F32)
            for e in range(experts):
                row = back[e, spare : spare + 16, :].astype(F32)[:1]
                table = jnp.where(place == e, row, table)
            for piece in range(3):
                at = (3 * n + piece) * experts
                tables[at : at + experts] = table[:, piece * half : (piece + 1) * half]

    info = jnp.transpose(info_ref[...])
    number = lambda n: info[:, n : n + 1]
    columns = lax.broadcasted_iota(jnp.int32, (1, half), 1)
    lanes = lax.broadcasted_iota(jnp.int32, (1, 6 * experts), 1)
    table = tables[...].astype(BF)
    values = []
    for k in range(2):
        slot = number(4 + k)
        hot = jnp.where(columns == lax.rem(slot, half), 1.0, 0.0).astype(BF)
        found = dot(hot, table, NT)
        wanted = jnp.where(slot // half == core_ref[0], 0, 3 * experts) + number(2 + k)
        away = lanes - wanted
        hit = (away == 0) | (away == experts) | (away == 2 * experts)
        values.append(jnp.sum(jnp.where(hit, found, 0.0), axis=1, keepdims=True))
    wide = lax.broadcasted_iota(jnp.int32, (1, TILE), 1)
    is_first, is_second = wide == number(2), wide == number(3)
    residual = residual_ref[...]
    gain = gain_ref[...]
    inverse = lax.rsqrt(jnp.mean(residual * residual, axis=-1, keepdims=True) + 1e-06)
    plain = residual * inverse
    normed = (plain * gain).astype(BF)
    logits = dot(normed, router_ref[...])
    gap = jnp.sum(jnp.where(is_first, logits, 0.0) - jnp.where(is_second, logits, 0.0), axis=1, keepdims=True)
    small = jnp.exp(-jnp.abs(gap))
    logit = small / ((1.0 + small) * (1.0 + small)) * (values[0] - values[1])
    logit_grad = jnp.where(is_first, logit, jnp.where(is_second, -logit, 0.0)).astype(BF)
    segments = [b[...].reshape(b.shape[0] * b.shape[1], b.shape[2]) for b in backs]
    normed_grad = picked_rows(number(0), number(1), segments) + dot(logit_grad, router_ref[...], NT)
    scaled = normed_grad * gain
    mean = jnp.mean(scaled * plain, axis=-1, keepdims=True)
    place = lax.broadcasted_iota(jnp.int32, (block, 1), 0) + step * block
    grad_out = jnp.where(place < length_ref[0], grad_ref[0].astype(F32), 0.0)
    total = grad_out + inverse * (scaled - plain * mean)
    total_ref[...] = total
    branch = total.astype(BF)
    mixed_grad_ref[...] = dot(branch, output_ref[...]).astype(BF)
    router_part = dot(logit_grad, normed, TN)
    gain_part = folded(normed_grad * plain)
    output_part = dot(mixed_ref[...], branch, TN)

    @pl.when(step == 0)
    def _():
        router_acc[...] = router_part
        gain_acc[...] = gain_part
        acc_ref[...] = output_part

    @pl.when(step > 0)
    def _():
        router_acc[...] += router_part
        gain_acc[...] += gain_part
        acc_ref[...] += output_part

    @pl.when(step == pl.num_programs(0) - 1)
    def _():
        extra_ref[...] = jnp.transpose(router_acc[...]) + jnp.where(wide == experts + 1, as_column(gain_acc[...]), 0.0)
        parts = jnp.transpose(acc_ref[...])
        far_ref[...] = parts[:, TILE:].astype(BF)
        own_ref[:, :TILE] = parts[:, :TILE]
        own_ref[:, TILE:] = parts[:, 2 * TILE :]


def combine(micro, core, length, info, out_grad, residual, mixed, gain, router, output_own, backs, half, spare):
    width = residual.shape[1]
    block = 512
    cols = mixed.shape[1]
    whole = lambda arr: pl.BlockSpec(arr.shape, lambda i, *_: (0,) * arr.ndim)
    fixed = lambda rows, n: pl.BlockSpec((rows, n), lambda i, *_: (0, 0))
    here = lambda n: pl.BlockSpec((block, n), lambda i, *_: (i, 0))
    experts = backs[0].shape[0]
    return pl.pallas_call(
        functools.partial(combine_kernel, experts, half, spare),
        grid_spec=pltpu.PrefetchScalarGridSpec(
            num_scalar_prefetch=3,
            grid=(SEQ // block,),
            in_specs=[
                pl.BlockSpec((8, block), lambda i, *_: (0, i)),
                pl.BlockSpec((1, block, width), lambda i, m, *_: (m[0], i, 0)),
                here(width), here(cols), whole(gain), whole(router), whole(output_own),
            ]
            + [whole(x) for x in backs],
            out_specs=[here(width), here(cols), fixed(width, TILE), fixed(width, 2 * TILE), fixed(width, 2 * TILE)],
            scratch_shapes=[
                pltpu.VMEM((cols, width), F32),
                pltpu.VMEM((TILE, width), F32),
                pltpu.VMEM((8, width), F32),
                pltpu.VMEM((6 * experts, half), F32),
            ],
        ),
        out_shape=[
            jax.ShapeDtypeStruct((SEQ, width), F32),
            jax.ShapeDtypeStruct((SEQ, cols), BF),
            jax.ShapeDtypeStruct((width, TILE), F32),
            jax.ShapeDtypeStruct((width, 2 * TILE), BF),
            jax.ShapeDtypeStruct((width, 2 * TILE), F32),
        ],
        compiler_params=pltpu.CompilerParams(vmem_limit_bytes=40 * MIB),
        cost_estimate=SMALL_COST,
        name="combine",
    )(micro, core, length, info, out_grad, residual, mixed, gain, router, output_own, *backs)


def projected_back(weight_ref, grads):
    total = None
    for n, grad in enumerate(grads):
        cols = grad.shape[1]
        total = put(total, dot(grad[...], weight_ref[:, n * cols : (n + 1) * cols], NT))
    return total


def attention_weight_kernel(
    blocks, core_ref, normed_ref, q_ref, k_ref, v_ref, output_ref, weight_ref, q_rows, k_rows, v_rows, far_ref, own_ref, sent_ref
):
    step = pl.program_id(0)

    @pl.when(step < blocks)
    def _():
        low = low_lanes((normed_ref.shape[1], TILE))
        q, k, v = (dot(normed_ref[...], d[...], TN) for d in (q_ref, k_ref, v_ref))
        for n, part in enumerate((q, k, v)):
            own_ref[:, n * TILE : (n + 1) * TILE] = part[:, :TILE]
            far_ref[:, n * TILE : (n + 1) * TILE] = part[:, TILE : 2 * TILE].astype(BF)
        q, k, v = (part[:, 2 * TILE :] for part in (q, k, v))
        far_ref[:, 3 * TILE : 4 * TILE] = jnp.where(low, turned(q), k).astype(BF)
        far_ref[:, 4 * TILE : 5 * TILE] = jnp.where(low, turned(v), output_ref[:, TILE:].astype(F32)).astype(BF)
        far_ref[:, 5 * TILE :] = output_ref[:, :TILE]
        own_ref[:, 3 * TILE : 4 * TILE] = jnp.where(low, q, turned(k))
        own_ref[:, 4 * TILE :] = jnp.where(low, v, 0.0)

    @pl.when(step >= blocks)
    def _():
        sent_ref[...] = projected_back(weight_ref, (q_rows, k_rows, v_rows))


def attention_weight_grads(core, normed, q, k, v, output, weight):
    width = normed.shape[1]
    block = 256
    blocks = width // block
    at = lambda i: jnp.minimum(i, blocks - 1)
    later = lambda i: jnp.maximum(i, blocks) - blocks
    whole = lambda arr: pl.BlockSpec(arr.shape, lambda i, c: (0, 0))
    here = lambda n: pl.BlockSpec((block, n), lambda i, c: (at(i), 0))
    rows = pl.BlockSpec((block, q.shape[1]), lambda i, c: ((1 - c[0]) * 2 + later(i), 0))
    return pl.pallas_call(
        functools.partial(attention_weight_kernel, blocks),
        grid_spec=pltpu.PrefetchScalarGridSpec(
            num_scalar_prefetch=1,
            grid=(blocks + 2,),
            in_specs=[
                pl.BlockSpec((SEQ, block), lambda i, c: (0, at(i))),
                whole(q), whole(k), whole(v), here(2 * TILE), whole(weight), rows, rows, rows,
            ],
            out_specs=[here(6 * TILE), here(5 * TILE), pl.BlockSpec((block, width), lambda i, c: (later(i), 0))],
        ),
        out_shape=[
            jax.ShapeDtypeStruct((width, 6 * TILE), BF),
            jax.ShapeDtypeStruct((width, 5 * TILE), F32),
            jax.ShapeDtypeStruct((2 * block, width), F32),
        ],
        compiler_params=pltpu.CompilerParams(vmem_limit_bytes=40 * MIB),
        cost_estimate=SMALL_COST,
        name="attention_weight_grads",
    )(core, normed, q, k, v, output, weight, q, k, v)


def both_kernel(
    lane, micro_ref, core_ref, length_ref, weight_ref, q, k, v, got_ref, tokens_ref, gain_ref, grad_ref,
    info_ref, residual_ref, own_ref, far_ref, out_ref, extra_ref, acc_ref,
):
    block = residual_ref.shape[0]
    info = jnp.transpose(info_ref[...])
    place = lax.broadcasted_iota(jnp.int32, (block, 1), 0) + (core_ref[0] * 2 + pl.program_id(0)) * block
    rows = residual_ref[...] + picked_rows(info[:, 6:7], info[:, 7:8], (own_ref[...], far_ref[...]))
    out_ref[0] = jnp.where(place < length_ref[0], rows, 0.0).astype(BF)
    normed_grad = got_ref[...] + projected_back(weight_ref, (q, k, v))
    x = tokens_ref[0].astype(F32)
    inverse = lax.rsqrt(jnp.mean(x * x, axis=-1, keepdims=True) + 1e-06)
    plain = x * inverse
    scaled = normed_grad * gain_ref[...]
    mean = jnp.mean(scaled * plain, axis=-1, keepdims=True)
    out_ref[1] = (grad_ref[...] + inverse * (scaled - plain * mean)).astype(BF)
    wide = lax.broadcasted_iota(jnp.int32, (1, TILE), 1)
    part = folded(normed_grad * plain)

    @pl.when(pl.program_id(0) == 0)
    def _():
        acc_ref[...] = part

    @pl.when(pl.program_id(0) == 1)
    def _():
        extra_ref[...] = jnp.where(wide == lane, as_column(acc_ref[...] + part), 0.0)


def both_rows(lane, micro, core, length, weight, grads, got, layer_input, gain, residual_grad, info, residual, own, far):
    width = weight.shape[0]
    block = 256
    here = lambda n: pl.BlockSpec((block, n), lambda i, m, c, *_: (c[0] * 2 + i, 0))
    whole = lambda arr: pl.BlockSpec(arr.shape, lambda i, *_: (0, 0))
    return pl.pallas_call(
        functools.partial(both_kernel, lane),
        grid_spec=pltpu.PrefetchScalarGridSpec(
            num_scalar_prefetch=3,
            grid=(2,),
            in_specs=[whole(weight)]
            + [here(grads[0].shape[1])] * 3
            + [
                pl.BlockSpec((block, width), lambda i, *_: (i, 0)),
                pl.BlockSpec((1, block, width), lambda i, m, c, *_: (m[0], c[0] * 2 + i, 0)),
                whole(gain),
                here(width),
                pl.BlockSpec((8, block), lambda i, m, c, *_: (0, c[0] * 2 + i)),
                here(width),
                whole(own),
                whole(far),
            ],
            out_specs=[
                pl.BlockSpec((2, block, width), lambda i, *_: (0, i, 0)),
                pl.BlockSpec((width, TILE), lambda i, *_: (0, 0)),
            ],
            scratch_shapes=[pltpu.VMEM((8, width), F32)],
        ),
        out_shape=[jax.ShapeDtypeStruct((2, 2 * block, width), BF), jax.ShapeDtypeStruct((width, TILE), F32)],
        compiler_params=pltpu.CompilerParams(vmem_limit_bytes=40 * MIB),
        cost_estimate=SMALL_COST,
        name="both_rows",
    )(micro, core, length, weight, *grads, got, layer_input, gain, residual_grad, info, residual, own, far)


def sum_kernel(kept, own, got, out_own, early, late, late_far, table, sum_ref):
    low = low_lanes(early.shape)
    sum_ref[:, : 4 * TILE] = (own[:, : 4 * TILE] + got[:, : 4 * TILE].astype(F32)).astype(BF)
    mixed = jnp.where(low, own[:, 4 * TILE :], turned(out_own[:, TILE:]))
    sum_ref[:, 4 * TILE : 5 * TILE] = (mixed + got[:, 4 * TILE : 5 * TILE].astype(F32)).astype(BF)
    sum_ref[:, 5 * TILE : 6 * TILE] = (out_own[:, :TILE] + got[:, 5 * TILE :].astype(F32)).astype(BF)
    extra = early[...] + late[...] + late_far[...] + table[...]
    high = extra.astype(BF)
    rest = extra - high.astype(F32)
    if kept <= HEAD_DIM:
        sum_ref[:, 6 * TILE :] = jnp.where(low, high.astype(F32), turned(rest)).astype(BF)
    else:
        sum_ref[:, 6 * TILE : 7 * TILE] = high
        sum_ref[:, 7 * TILE :] = rest.astype(BF)


def packed_sums(kept, *parts):
    width = parts[0].shape[0]
    cols = (7 if kept <= HEAD_DIM else 8) * TILE
    block = 256
    here = lambda n: pl.BlockSpec((block, n), lambda i: (i, 0))
    return pl.pallas_call(
        functools.partial(sum_kernel, kept),
        grid=(width // block,),
        in_specs=[here(x.shape[1]) for x in parts],
        out_specs=here(cols),
        out_shape=jax.ShapeDtypeStruct((width, cols), BF),
        compiler_params=pltpu.CompilerParams(vmem_limit_bytes=40 * MIB),
        cost_estimate=SMALL_COST,
        name="packed_sums",
    )(*parts)


def final_kernel(kept, parts_ref, q_ref, k_ref, v_ref, o_ref, small_ref):
    total = parts_ref[0].astype(F32)
    for n in range(1, parts_ref.shape[0]):
        total = total + parts_ref[n].astype(F32)
    tile = lambda t: total[:, t * TILE : (t + 1) * TILE]
    q_ref[:, :TILE] = tile(0)
    q_ref[:, TILE:] = tile(3)[:, :HEAD_DIM]
    k_ref[:, :TILE] = tile(1)
    k_ref[:, TILE:] = turned(tile(3))[:, :HEAD_DIM]
    v_ref[:, :TILE] = tile(2)
    v_ref[:, TILE:] = tile(4)[:, :HEAD_DIM]
    o_ref[:, :TILE] = tile(5)
    o_ref[:, TILE:] = turned(tile(4))[:, :HEAD_DIM]
    small_ref[...] = tile(6) + (turned(tile(6)) if kept <= HEAD_DIM else tile(7))


def final_sums(kept, parts, shard):
    rows = parts.shape[1]
    return pl.pallas_call(
        functools.partial(final_kernel, kept),
        out_shape=[jax.ShapeDtypeStruct((rows, shard), F32)] * 4 + [jax.ShapeDtypeStruct((rows, TILE), F32)],
        compiler_params=pltpu.CompilerParams(vmem_limit_bytes=40 * MIB),
        cost_estimate=SMALL_COST,
        name="final_sums",
    )(parts)


def pair_gate(logits, own, other):
    lanes = lax.broadcasted_iota(jnp.int32, logits.shape, 1)
    gap = jnp.sum(
        jnp.where(lanes == own, logits, 0.0) - jnp.where(lanes == other, logits, 0.0), axis=1, keepdims=True
    )
    small = jnp.exp(-jnp.abs(gap))
    return jnp.where(gap >= 0.0, 1.0, small) / (1.0 + small)


def expert_kernel(lead, chunk, half, me_ref, partner_ref, rows_ref, grads_ref, router_ref, *refs):
    before, refs = (refs[0], refs[1:]) if lead is not None and lead > 0 else (None, refs)
    firsts, seconds = refs[:4], refs[4:8]
    back_ref, active_ref, slope_ref, gated_ref, gate_ref, mass_ref = refs[8:]
    rows = rows_ref[...]
    grads = grads_ref[...]
    gate = pair_gate(dot(rows, router_ref[...]), me_ref[0], partner_ref[...])
    gated_ref[...] = (gate * grads.astype(F32)).astype(BF)
    gate_ref[...] = jnp.broadcast_to(gate, gate_ref.shape)
    masses = [None] * (rows.shape[0] // STRIP)
    back = None
    width = firsts[0].shape[1]
    step = 256
    places = [(r, c) for r in range(4) for c in range(0, width, step)]

    def products(r, c):
        return dot(rows, firsts[r][:, c : c + step]), dot(grads, seconds[r][c : c + step, :], NT)

    ahead = products(*places[0])
    for n, (r, c) in enumerate(places):
        x, plain = ahead
        if n + 1 < len(places):
            ahead = products(*places[n + 1])
        place = slice(r * width + c, r * width + c + step)
        for at in range(0, rows.shape[0], STRIP):
            strip = slice(at, at + STRIP)
            value, flow = x[strip], plain[strip]
            square = value * value
            bent = jnp.tanh(value * (GELU_C + (GELU_C * GELU_A) * square))
            rise = 0.5 + 0.5 * bent
            active = value * rise
            slope = rise + active * (1.0 - bent) * (GELU_C + (3.0 * GELU_C * GELU_A) * square)
            low = active.astype(BF)
            active_ref[strip, place] = low
            slope_ref[strip, place] = (gate[strip] * flow * slope).astype(BF)
            part = low.astype(F32) * flow
            masses[at // STRIP] = put(masses[at // STRIP], part[:, :TILE] + part[:, TILE:])
        if c + step == width and r > 0:
            back = put(back, dot(slope_ref[:, (r - 1) * width : r * width], firsts[r - 1][...], NT))
    back = put(back, dot(slope_ref[:, 3 * width :], firsts[3][...], NT))
    back = back.astype(BF)
    mass = jnp.sum(jnp.concatenate(masses, 0), axis=1, keepdims=True)
    if lead is None:
        back_ref[...] = back
        mass_ref[...] = jnp.broadcast_to(mass, mass_ref.shape)
        return
    count = rows.shape[0] // chunk
    number = lax.broadcasted_iota(jnp.int32, (rows.shape[0], 1), 0)
    lanes = lax.broadcasted_iota(jnp.int32, (1, rows.shape[1]), 1)
    inside = lax.rem(number, chunk)
    spread = jnp.zeros(rows.shape, F32)
    for piece in range(3):
        high = mass.astype(BF).astype(F32)
        spread = jnp.where(lanes == piece * half + lead + inside, high, spread)
        mass = mass - high
    own = jnp.where(number // chunk == lax.broadcasted_iota(jnp.int32, (1, TILE), 1), 1.0, 0.0).astype(BF)
    line = dot(own, spread.astype(BF), TN)
    if before is None:
        back_ref[...] = back
        for e in range(count):
            mass_ref[e] = line[e : e + 1].astype(BF)
    else:
        back_ref[:, :chunk] = back.reshape(count, chunk, back.shape[1])
        row = lax.broadcasted_iota(jnp.int32, (16, 1), 0)
        for e in range(count):
            both = line[e : e + 1] + before[e].astype(F32)
            back_ref[e, chunk:] = jnp.where(row == 0, both, 0.0).astype(BF)


def row_block(total):
    return 320 if total % 320 == 0 else total


def expert_rows_pass(lead, chunk, half, me, partner, rows, grads, router, before, firsts, seconds):
    total, width = rows.shape
    block = row_block(total)
    experts = total // chunk
    hidden = sum(f.shape[1] for f in firsts)
    here = lambda cols: pl.BlockSpec((block, cols), lambda i: (i, 0))
    whole = lambda arr: pl.BlockSpec(arr.shape, lambda i: (0, 0))
    lines = pl.BlockSpec((block // chunk, 1, width), lambda i: (i, 0, 0))
    back_shape, back_spec = (total, width), here(width)
    mass_shape, mass_spec, mass_kind = (experts, 1, width), lines, BF
    if lead is None:
        mass_shape, mass_spec, mass_kind = (total, TILE), here(TILE), F32
    elif before is not None:
        back_shape = (experts, chunk + 16, width)
        back_spec = pl.BlockSpec((block // chunk, chunk + 16, width), lambda i: (i, 0, 0))
    return pl.pallas_call(
        functools.partial(expert_kernel, lead, chunk, half),
        grid=(total // block,),
        in_specs=[pl.BlockSpec(memory_space=pltpu.SMEM), here(1), here(width), here(width), whole(router)]
        + ([lines] if before is not None else [])
        + [whole(w) for w in firsts]
        + [whole(w) for w in seconds],
        out_specs=[back_spec, here(hidden), here(hidden), here(width), here(TILE), mass_spec],
        out_shape=[
            jax.ShapeDtypeStruct(back_shape, BF),
            jax.ShapeDtypeStruct((total, hidden), BF),
            jax.ShapeDtypeStruct((total, hidden), BF),
            jax.ShapeDtypeStruct((total, width), BF),
            jax.ShapeDtypeStruct((total, TILE), F32),
            jax.ShapeDtypeStruct(mass_shape, mass_kind),
        ],
        compiler_params=pltpu.CompilerParams(vmem_limit_bytes=56 * MIB),
        cost_estimate=SMALL_COST,
        name="expert_rows",
    )(me, partner, rows, grads, router, *([before] if before is not None else []), *firsts, *seconds)


def expert_weight_kernel(count, *refs):
    rows, slopes, active, gated = (refs[n * count : (n + 1) * count] for n in range(4))
    cross_ref, kept_ref = refs[4 * count :]
    step = pl.program_id(0)
    first, second = None, None
    for n in range(count):
        first = put(first, dot(rows[n][...], slopes[n][...], TN))
        second = put(second, dot(active[n][...], gated[n][...], TN))

    @pl.when(step < 2)
    def _():
        cross_ref[0, 0] = first.astype(BF)
        cross_ref[0, 1] = second.astype(BF)

    @pl.when(step >= 2)
    def _():
        kept_ref[0, 0] = first
        kept_ref[0, 1] = second


def expert_weight_grads(rows, slopes, active, gated):
    total, width = rows[0].shape
    hidden = slopes[0].shape[1] // 4
    count = len(rows)
    whole = pl.BlockSpec((total, width), lambda i: (0, 0))
    part = pl.BlockSpec((total, hidden), lambda i: (0, jnp.where(i < 2, 2 + i, 3 - i)))
    return pl.pallas_call(
        functools.partial(expert_weight_kernel, count),
        grid=(4,),
        in_specs=[whole] * count + [part] * (2 * count) + [whole] * count,
        out_specs=[
            pl.BlockSpec((1, 2, width, hidden), lambda i: (jnp.minimum(i, 1), 0, 0, 0)),
            pl.BlockSpec((1, 2, width, hidden), lambda i: (jnp.maximum(i, 2) - 2, 0, 0, 0)),
        ],
        out_shape=[
            jax.ShapeDtypeStruct((2, 2, width, hidden), BF),
            jax.ShapeDtypeStruct((2, 2, width, hidden), F32),
        ],
        compiler_params=pltpu.CompilerParams(vmem_limit_bytes=56 * MIB),
        cost_estimate=SMALL_COST,
        name="expert_weight_grads",
    )(*rows, *slopes, *active, *gated)


def result_kernel(chunks, *refs):
    active, gates, seconds, out_ref = refs[:chunks], refs[chunks : 2 * chunks], refs[2 * chunks : -1], refs[-1]
    for c in range(chunks):

        @pl.when(pl.program_id(0) == c)
        def _(c=c):
            width = seconds[0].shape[0]
            total = None
            for r, second in enumerate(seconds):
                total = put(total, dot(active[c][:, r * width : (r + 1) * width], second[...]))
            rows = (total * gates[c][:, :1]).astype(BF)
            if chunks > 1:
                out_ref[:, 0] = rows.reshape(out_ref.shape[0], out_ref.shape[2], out_ref.shape[3])
            else:
                out_ref[...] = rows


def expert_results(active, gates, seconds, experts):
    chunks = len(active)
    total, hidden = active[0].shape
    width = seconds[0].shape[1]
    block = row_block(total)
    steps = total // block

    def here(c, cols):
        return pl.BlockSpec((block, cols), lambda g, i: (jnp.where(g == c, i, jnp.where(g < c, 0, steps - 1)), 0))

    chunk = total // experts
    if chunks > 1:
        shape = (experts, chunks, chunk, width)
        out_spec = pl.BlockSpec((block // chunk, 1, chunk, width), lambda g, i: (i, g, 0, 0))
    else:
        shape = (total, width)
        out_spec = pl.BlockSpec((block, width), lambda g, i: (i, 0))
    out = pl.pallas_call(
        functools.partial(result_kernel, chunks),
        grid=(chunks, steps),
        in_specs=[here(c, hidden) for c in range(chunks)]
        + [here(c, TILE) for c in range(chunks)]
        + [pl.BlockSpec(w.shape, lambda g, i: (0, 0)) for w in seconds],
        out_specs=out_spec,
        out_shape=jax.ShapeDtypeStruct(shape, BF),
        compiler_params=pltpu.CompilerParams(vmem_limit_bytes=56 * MIB),
        cost_estimate=SMALL_COST,
        name="expert_results",
    )(*active, *gates, *seconds)
    return out.reshape(experts, chunks * chunk, width)


def cross_sum_kernel(kept_ref, got_ref, out_ref):
    out_ref[...] = (kept_ref[0] + got_ref[0].astype(F32)).astype(BF)


def cross_sums(kept, got):
    _, _, width, hidden = kept.shape
    block = 96
    return pl.pallas_call(
        cross_sum_kernel,
        grid=(width // block,),
        in_specs=[
            pl.BlockSpec((1, 2, block, hidden), lambda i: (0, 0, i, 0)),
            pl.BlockSpec((1, 2, block, hidden), lambda i: (1, 0, i, 0)),
        ],
        out_specs=pl.BlockSpec((2, block, hidden), lambda i: (0, i, 0)),
        out_shape=jax.ShapeDtypeStruct((2, width, hidden), BF),
        compiler_params=pltpu.CompilerParams(vmem_limit_bytes=40 * MIB),
        cost_estimate=SMALL_COST,
        name="cross_sums",
    )(kept, got)


def last_sum_kernel(kept_ref, core_ref, y_ref, out_first, out_second):
    for n, out in enumerate((out_first, out_second)):
        out[...] = kept_ref[0, n] + core_ref[0, n].astype(F32) + y_ref[n].astype(F32)


def last_sums(kept, got_core, got_y):
    _, _, width, hidden = kept.shape
    block = 96
    here = pl.BlockSpec((block, hidden), lambda i: (i, 0))
    return pl.pallas_call(
        last_sum_kernel,
        grid=(width // block,),
        in_specs=[
            pl.BlockSpec((1, 2, block, hidden), lambda i: (1, 0, i, 0)),
            pl.BlockSpec((1, 2, block, hidden), lambda i: (0, 0, i, 0)),
            pl.BlockSpec((2, block, hidden), lambda i: (0, i, 0)),
        ],
        out_specs=[here, here],
        out_shape=[jax.ShapeDtypeStruct((width, hidden), F32)] * 2,
        compiler_params=pltpu.CompilerParams(vmem_limit_bytes=40 * MIB),
        cost_estimate=SMALL_COST,
        name="last_sums",
    )(kept, got_core, got_y)


def send_kernel(micro_ref, code_ref, rows_ref, out_ref):
    block = out_ref.shape[0]
    ids = lax.broadcasted_iota(jnp.int32, (block, 1), 0) + pl.program_id(0) * block
    hot = jnp.where((ids == code_ref[:1]) | (ids == code_ref[1:2]), 1.0, 0.0).astype(BF)
    out_ref[...] = dot(hot, rows_ref[0]).astype(BF)


def send_rows(micro, code, rows, count):
    width = rows.shape[2]
    block = next(b for b in (336, 320, 384, count) if count % b == 0)
    return pl.pallas_call(
        send_kernel,
        grid_spec=pltpu.PrefetchScalarGridSpec(
            num_scalar_prefetch=1,
            grid=(count // block,),
            in_specs=[
                pl.BlockSpec(code.shape, lambda i, m: (0, 0)),
                pl.BlockSpec((1, SEQ, width), lambda i, m: (m[0], 0, 0)),
            ],
            out_specs=pl.BlockSpec((block, width), lambda i, m: (i, 0)),
        ),
        out_shape=jax.ShapeDtypeStruct((count, width), BF),
        compiler_params=pltpu.CompilerParams(vmem_limit_bytes=40 * MIB),
        cost_estimate=SMALL_COST,
        name="send_rows",
    )(micro, code, rows)


def place_kernel(place_ref, *refs):
    for n, piece in enumerate(refs[:4]):

        @pl.when(pl.program_id(0) == n)
        def _(piece=piece):
            for k, out_ref in enumerate(refs[4:]):
                out_ref[0] = piece[k]


def place_pieces(places, pieces):
    two, rows, width = pieces[0].shape
    whole = pl.BlockSpec(pieces[0].shape, lambda i, place_ref: (0, 0, 0))
    return pl.pallas_call(
        place_kernel,
        grid_spec=pltpu.PrefetchScalarGridSpec(
            num_scalar_prefetch=1,
            grid=(4,),
            in_specs=[whole] * 4,
            out_specs=[pl.BlockSpec((1, rows, width), lambda i, place_ref: (place_ref[i], 0, 0))] * two,
        ),
        out_shape=[jax.ShapeDtypeStruct((4, rows, width), pieces[0].dtype)] * two,
        compiler_params=pltpu.CompilerParams(vmem_limit_bytes=40 * MIB),
        cost_estimate=SMALL_COST,
        name="place_pieces",
    )(places, *pieces)


def swap(value, axis, count, bit):
    return lax.ppermute(value, axis, [(i, i ^ bit) for i in range(count)])


def all_to_all(value):
    return lax.all_to_all(value, "dp", split_axis=0, concat_axis=0, tiled=True)


def together(*values):
    return lax.optimization_barrier(values)


def local(
    layer_input, out_grad, first_gain, query_weight, key_weight, value_weight, output_weight,
    position_bias, second_gain, router_weight, expert_in, expert_out, seq_lengths, routes,
):
    micro_count, tok_rows, width = layer_input.shape
    dp_count = lax.axis_size("dp")
    expert_count = router_weight.shape[1]
    shard = query_weight.shape[1]
    heads_here = position_bias.shape[0]
    assert lax.axis_size("tensor") == 4 and micro_count == 2 and expert_count == dp_count
    assert tok_rows == SEQ and seq_lengths.shape[1] == 1
    capacity = max(8, 8 * (10 * tok_rows // (32 * expert_count)))
    half = capacity // 2
    stride = 8 * (half // 8 + 1)
    by_lines = dp_count == 8
    chunks = 2 if half % 32 == 0 else 1
    chunk = half // chunks
    chunk_rows = expert_count * chunk
    rows_here = query_weight.shape[0]
    me = lax.axis_index("dp")
    rank = lax.axis_index("tensor")
    micro = rank // 2
    core = rank % 2

    def swap_y(value):
        return swap(value, "tensor", 4, 2)

    def swap_core(value):
        return swap(value, "tensor", 4, 1)

    micro_arg = micro.reshape(1).astype(jnp.int32)
    core_arg = core.reshape(1).astype(jnp.int32)

    packed = pack_weights(query_weight, key_weight, value_weight, output_weight, first_gain, second_gain, router_weight)
    three = 3 * TILE

    def doubled(stacked, bit, axis=0):
        other = swap(stacked, "dp", dp_count, bit)
        high = (me & bit) != 0
        pair = jnp.where(high, jnp.stack([other, stacked], axis + 1), jnp.stack([stacked, other], axis + 1))
        return pair.reshape(stacked.shape[:axis] + (-1,) + stacked.shape[axis + 1 :])

    stacked = packed[None]
    bit = dp_count // 2
    while bit > 1:
        stacked = doubled(stacked, bit)
        bit //= 2
    length = lax.dynamic_index_in_dim(seq_lengths, micro, 0, keepdims=False)
    route = lax.dynamic_index_in_dim(routes, micro, 0, keepdims=False).T
    expert_ids = jnp.arange(expert_count, dtype=jnp.int32)
    named = (expert_ids[:, None, None] == route[None]).astype(jnp.int32)
    per_token = jnp.sum(named, axis=1, dtype=jnp.int32)
    earlier = jnp.cumsum(per_token, axis=1, dtype=jnp.int32) - per_token
    slot = jnp.sum(named * earlier[:, None, :], axis=0, dtype=jnp.int32)
    here = slot // half == core
    within = slot % half
    chunk_of = within // chunk
    inside = within % chunk
    spare = 16 * -(-chunk // 16)
    last_stride = spare + 16
    last = (chunks - 1) * chunk_rows
    code_back = jnp.where(
        chunk_of == chunks - 1, last + route * last_stride + inside, chunk_of * chunk_rows + route * chunk + inside
    )
    code_back = code_back + jnp.where(here, 0, last + expert_count * last_stride)
    code_result = route * half + within + jnp.where(here, 0, expert_count * half)
    info = jnp.concatenate([code_back, route, slot, code_result], 0)

    code_grads = jnp.where(here, route * stride + within, -1)
    valid = jnp.arange(SEQ, dtype=jnp.int32) < length[0]
    ids = jnp.arange(expert_count * stride, dtype=jnp.int32)[:, None]
    partner = jnp.sum(
        jnp.where(ids == code_grads[:1], route[1:], 0) + jnp.where(ids == code_grads[1:], route[:1], 0), axis=1, dtype=jnp.int32
    )
    grads_sent = send_rows(micro_arg, jnp.where(valid[None], code_grads, -1), out_grad, expert_count * stride)
    grads_sent = grads_sent.reshape(expert_count, stride, width)
    partner_row = jnp.pad(partner.reshape(expert_count, stride)[:, :half].astype(BF), ((0, 0), (0, width - half)))
    grads_sent = grads_sent.at[:, half].set(partner_row)
    stacked, grads_sent, position_bias = together(stacked, grads_sent, position_bias)
    if by_lines:
        lines = [list(range(x, dp_count, 2)) for x in range(2)]
        grads_z = lax.all_to_all(
            grads_sent.reshape(dp_count // 2, 2, stride, width), "dp", split_axis=0, concat_axis=0,
            axis_index_groups=lines, tiled=True,
        )

    first_own = expert_in[0]
    second_own = expert_out[0]
    part_b = stacked[:, :, :three]
    far_b = swap_y(part_b)
    part_a = doubled(stacked[:, :, three:], 1)
    part_a, far_b = together(part_a, far_b)
    pair_b = jnp.stack([part_b, far_b])
    a_own = part_a[:, :, :three]
    a_far = swap_y(a_own).reshape(width, three)
    a_own = a_own.reshape(width, three)
    pair_b = doubled(pair_b, 1, 1).reshape(2, width, three)
    if by_lines:
        a_far, pair_b, first_own = together(a_far, pair_b, first_own)
    else:
        a_far, pair_b, grads_sent, first_own = together(a_far, pair_b, grads_sent, first_own)
    first_y = swap_y(first_own)
    small_all = part_a[:, :, three:].reshape(width, TILE)
    gain_one = small_all[:, expert_count].astype(F32)[None]
    gain_two = small_all[:, expert_count + 1].astype(F32)[None]
    router_wide = small_all
    far_bias = swap_y(position_bias)
    bias = jnp.concatenate([position_bias[:2], far_bias[:2], position_bias[2:], far_bias[2:]], 0)
    head_total = bias.shape[0]
    hot_const = jnp.asarray(NEAR_HOT, dtype=BF)
    near = dot(bias, hot_const) - bias[:, NB - 1 :].astype(F32)
    near = near.reshape(head_total, 2, TILE, TILE)
    places = jnp.arange(TILE, dtype=jnp.int32)
    causal = jnp.stack([places[None, :] <= places[:, None], jnp.ones((TILE, TILE), bool)])
    near = jnp.where(causal[None], near, NEG)

    if by_lines:
        high = (me & 1) != 0
        kept_x = jnp.where(high, grads_z[:, 1], grads_z[:, 0])
        got_x = swap(jnp.where(high, grads_z[:, 0], grads_z[:, 1]), "dp", dp_count, 1)
    else:
        grads_here = all_to_all(grads_sent)

    qkv, normed_one, qkv_weight, output_own = norm_and_project(
        micro_arg, layer_input, gain_one, a_own, a_far, pair_b[0], pair_b[1]
    )
    output_far = swap_core(output_own)
    mixed, logs = attend(length, qkv, near)
    mixed, output_far = together(mixed, output_far)
    mixed_far = swap_core(mixed)
    code_chunks = jnp.where(here, chunk_of * chunk_rows + route * chunk + inside, -1)
    residual, parts = residual_and_rows(
        micro_arg, layer_input, mixed, mixed_far, output_own, output_far, gain_two, code_chunks, chunks * chunk_rows
    )

    if by_lines:
        parts, kept_x, first_y, second_own = together(parts, kept_x, first_y, second_own)
        pair_x = jnp.where(high, jnp.stack([got_x, kept_x], 1), jnp.stack([kept_x, got_x], 1))
        grads_here = pair_x.reshape(dp_count, stride, width)
    else:
        parts, grads_here, first_y, second_own = together(parts, grads_here, first_y, second_own)
    second_y = swap_y(second_own)
    parts = parts.reshape(chunks, expert_count, chunk, width)
    arrived = [all_to_all(parts[0])]
    partner_here = grads_here[:, half, :half].astype(jnp.int32)

    def chunk_grads(c):
        at = slice(c * chunk, (c + 1) * chunk)
        return grads_here[:, at].reshape(chunk_rows, width), partner_here[:, at].reshape(chunk_rows, 1)

    grads_parts = [chunk_grads(c) for c in range(chunks)]
    arrived[0], grads_parts, second_y = together(arrived[0], grads_parts, second_y)

    firsts = (first_own, first_y, swap_core(first_own), swap_core(first_y))
    seconds = (second_own, second_y, swap_core(second_own), swap_core(second_y))

    for c in range(1, chunks):
        sent, arrived[-1] = together(parts[c], arrived[-1])
        arrived.append(all_to_all(sent))

    me_arg = me.reshape(1).astype(jnp.int32)
    rows_all, slopes, active, gated, gates, backs = [], [], [], [], [], []
    line = None
    for c in range(chunks):
        grads_c, partner_c = grads_parts[c]
        rows_c = arrived[c].reshape(chunk_rows, width)
        back, act, slo, gat, gte, line = expert_rows_pass(
            c * chunk if chunks > 1 else None, chunk, half, me_arg, partner_c, rows_c, grads_c, router_wide, line, firsts, seconds
        )
        rows_all.append(rows_c)
        slopes.append(slo)
        active.append(act)
        gated.append(gat)
        gates.append(gte)
        if chunks == 1:
            gate_grad = line[:, 0].reshape(expert_count, chunk)
            pieces = []
            for _ in range(3):
                piece = gate_grad.astype(BF)
                pieces.append(piece)
                gate_grad = gate_grad - piece.astype(F32)
            gate_row = jnp.pad(jnp.concatenate(pieces, 1), ((0, 0), (0, width - 3 * half)))
            back = jnp.pad(back.reshape(expert_count, chunk, width), ((0, 0), (0, last_stride - chunk), (0, 0)))
            back = back.at[:, spare].set(gate_row)
        if c + 1 < chunks:
            back, arrived[c + 1] = together(back.reshape(expert_count, chunk, width), arrived[c + 1])
        else:
            back, rows_all[-1], backs = together(back, rows_all[-1], backs)
        backs.append(all_to_all(back))
    grads_cross, grads_kept = expert_weight_grads(rows_all, slopes, active, gated)
    gates, grads_cross = together(gates, grads_cross)
    grads_in = swap_core(grads_cross)
    results = expert_results(active, gates, seconds, expert_count)
    backs[-1], results = together(backs[-1], results)
    results_own = all_to_all(results).reshape(expert_count * half, width)

    across_y = swap_y(cross_sums(grads_kept, grads_in))

    backs_far = [swap_core(b) for b in backs]
    residual_grad, mixed_grad, extra_early, output_sent, output_kept = combine(
        micro_arg, core_arg, length, info, out_grad, residual, mixed, gain_two, router_wide, output_own,
        backs + backs_far, half, spare,
    )

    dq, dk, dv, tiles, sums = attend_back(length, qkv, near, mixed, logs, mixed_grad, 0, head_total // 2)
    far_sent, own_parts, sent = attention_weight_grads(core_arg, normed_one, dq, dk, dv, output_sent, qkv_weight)
    far_got = swap_y(far_sent)
    sent, results_own = together(sent, results_own)
    got = swap_core(sent)
    rows_both, extra_late = both_rows(
        expert_count, micro_arg, core_arg, length, qkv_weight, (dq, dk, dv), got, layer_input, gain_one, residual_grad,
        info, residual, results_own, swap_core(results_own),
    )
    rows_both, across_y, tiles = together(rows_both, across_y, tiles)
    late_far = swap_core(extra_late)
    corner = micro * 2 + core
    corners = jnp.stack([corner, corner ^ 1, corner ^ 2, corner ^ 3]).astype(jnp.int32)
    rows_y = swap_y(rows_both)
    layer_output, input_grad = place_pieces(corners, (rows_both, swap_core(rows_both), rows_y, swap_core(rows_y)))
    layer_output = layer_output.reshape(2, SEQ, width)
    input_grad = input_grad.reshape(2, SEQ, width)

    tiles = tiles.reshape(head_total, 2 * TILE * TILE)
    tiles_high = tiles.astype(BF)
    tiles_rest = (tiles - tiles_high.astype(F32)).astype(BF)
    table = dot(tiles_high, hot_const, NT) + dot(tiles_rest, hot_const, NT)
    far_sum = jnp.sum(sums[:, :, 0], axis=1) - jnp.sum(table[:, : NB - 1], axis=1)
    table = jnp.concatenate([table[:, : NB - 1], far_sum[:, None]], 1)
    table_own = jnp.concatenate([table[0:2], table[4:5]], 0)
    table_far = jnp.concatenate([table[2:4], table[5:6]], 0)
    table_cols = heads_here * NB // rows_here
    table_both = jnp.concatenate([table_own.reshape(rows_here, table_cols), table_far.reshape(rows_here, table_cols)], 1)
    base = expert_count + 2
    kept = base + 2 * table_cols
    table_tile = jnp.tile(jnp.pad(table_both, ((0, 0), (base, TILE - kept))), (dp_count, 1))

    grads = packed_sums(kept, own_parts, far_got, output_kept, extra_early, extra_late, late_far, table_tile)
    grads, across_y = together(grads, across_y)
    expert_in_grad, expert_out_grad = last_sums(grads_kept, grads_in, across_y)
    arrived_grads = all_to_all(grads.reshape(dp_count, rows_here, grads.shape[1]))
    arrived_grads, layer_output, input_grad = together(arrived_grads, layer_output, input_grad)
    query_grad, key_grad, value_grad, output_grad, small = final_sums(kept, arrived_grads, shard)
    small_y = swap_y(small)
    both = small + small_y
    table_sum = small[:, base : base + table_cols] + small_y[:, base + table_cols : kept]
    return (
        layer_output,
        input_grad,
        both[:, expert_count],
        query_grad,
        key_grad,
        value_grad,
        output_grad.T,
        table_sum.reshape(heads_here, NB),
        both[:, expert_count + 1],
        both[:, :expert_count],
        expert_in_grad[None],
        expert_out_grad[None],
    )


def solution(mesh):
    return jax.shard_map(
        local,
        mesh=mesh,
        in_specs=(
            P(None, "dp", None),
            P(None, "dp", None),
            P("dp"),
            P("dp", "tensor"),
            P("dp", "tensor"),
            P("dp", "tensor"),
            P("tensor", "dp"),
            P("tensor", None),
            P("dp"),
            P("dp", None),
            P("dp", None, "tensor"),
            P("dp", "tensor", None),
            P(None, "dp"),
            P(None, "dp", None),
        ),
        out_specs=(
            P(None, "dp", None),
            P(None, "dp", None),
            P("dp"),
            P("dp", "tensor"),
            P("dp", "tensor"),
            P("dp", "tensor"),
            P("tensor", "dp"),
            P("tensor", None),
            P("dp"),
            P("dp", None),
            P("dp", None, "tensor"),
            P("dp", "tensor", None),
        ),
        check_vma=False,
    )
```

```python
import functools

import jax
import jax.numpy as jnp
import numpy as np
from jax import lax
from jax.experimental import pallas as pl
from jax.experimental.pallas import tpu as pltpu
from jax.sharding import PartitionSpec as P

HEAD_DIM = 64
NB = 32
SEQ = 1024
TILE = 128
QROWS = 256
NEG = -1e30
GELU_C = 0.7978845608028654
GELU_A = 0.044715

BF = jnp.bfloat16
F32 = jnp.float32

bucket_edges = np.ceil(16.0 * 8.0 ** (np.arange(1, 16) / 16.0)).astype(np.int32)


def near_tables():
    rows = np.arange(TILE)[:, None]
    cols = np.arange(TILE)[None, :]
    hots = []
    for shift in (0, TILE):
        distance = rows - cols + shift
        clipped = np.maximum(distance, 0)
        reached = np.sum(clipped[..., None] >= bucket_edges, axis=-1)
        bucket = np.minimum(clipped, 16) + reached
        hots.append(bucket[..., None] == np.arange(NB))
    hot = np.stack(hots).reshape(2 * TILE * TILE, NB).T
    return hot


NEAR_HOT = near_tables()
assert bucket_edges[-1] <= TILE


def dot(a, b, dims=((1,), (0,))):
    return lax.dot_general(a, b, (dims, ((), ())), preferred_element_type=F32)


NT = ((1,), (1,))
TN = ((0,), (0,))


MIB = 2**20
SMALL_COST = pl.CostEstimate(flops=1_000_000, bytes_accessed=1_000_000, transcendentals=0)


STRIP = 32


def score_strip(s, block, j, start, near_ref, half, length):
    rows = slice(start, start + STRIP)
    part = s[rows]
    near = slice(start % TILE, start % TILE + STRIP)
    if j == block:
        if start < TILE:
            left = part[:, :TILE] + near_ref[half, 0, near, :]
            right = jnp.full((STRIP, TILE), NEG, F32)
        else:
            left = part[:, :TILE] + near_ref[half, 1, near, :]
            right = part[:, TILE:] + near_ref[half, 0, near, :]
        part = jnp.concatenate([left, right], 1)
    elif j == block - 1 and start < TILE:
        part = jnp.concatenate([part[:, :TILE], part[:, TILE:] + near_ref[half, 1, near, :]], 1)
    if (j + 1) * QROWS > SEQ // 2:
        place = lax.broadcasted_iota(jnp.int32, (1, QROWS), 1) + j * QROWS
        part = part + jnp.where(place < length, 0.0, NEG)
    return part


def lane_half(rows):
    return lax.broadcasted_iota(jnp.int32, (rows, 2 * HEAD_DIM), 1) < HEAD_DIM


def attend_kernel(length_ref, query_ref, key_ref, value_ref, near_ref, out_ref, log_ref):
    length = length_ref[0]
    lanes = lane_half(QROWS)
    ones = jnp.ones((SEQ, TILE), BF)
    value_ext = jnp.concatenate([value_ref[...], ones], 1)
    for i in range(SEQ // QROWS):
        q_rows = query_ref[i * QROWS : (i + 1) * QROWS, :] * BF(0.125)
        outs, logs = [], []
        for h in range(2):
            keep = lanes if h == 0 else ~lanes
            q_half = jnp.where(keep, q_rows, BF(0))
            tiles = [dot(q_half, key_ref[j * QROWS : (j + 1) * QROWS, :], NT) for j in range(i + 1)]
            tops = []
            weights = [[] for _ in tiles]
            for start in range(0, QROWS, STRIP):
                strips = [score_strip(s, i, j, start, near_ref, h, length) for j, s in enumerate(tiles)]
                top = strips[0]
                for s in strips[1:]:
                    top = jnp.maximum(top, s)
                top = jnp.max(top, axis=1, keepdims=True)
                tops.append(top)
                for j, s in enumerate(strips):
                    weights[j].append(jnp.exp(s - top).astype(BF))
            top = jnp.concatenate(tops, 0)
            total = None
            for j, strips in enumerate(weights):
                part = dot(jnp.concatenate(strips, 0), value_ext[j * QROWS : (j + 1) * QROWS, :])
                total = part if total is None else total + part
            row_sum = total[:, TILE:]
            outs.append(total[:, :TILE] / row_sum)
            logs.append(top + jnp.log(row_sum))
        out_ref[i * QROWS : (i + 1) * QROWS, :] = jnp.where(lanes, outs[0], outs[1]).astype(BF)
        log_ref[i * QROWS : (i + 1) * QROWS, :] = jnp.where(lanes, logs[0], logs[1])


def attend(length, qkv, near):
    pairs = qkv.shape[1] // (3 * TILE)
    cols = pairs * TILE
    return pl.pallas_call(
        attend_kernel,
        grid=(pairs,),
        in_specs=[
            pl.BlockSpec(memory_space=pltpu.SMEM),
            pl.BlockSpec((SEQ, TILE), lambda p: (0, p)),
            pl.BlockSpec((SEQ, TILE), lambda p: (0, pairs + p)),
            pl.BlockSpec((SEQ, TILE), lambda p: (0, 2 * pairs + p)),
            pl.BlockSpec((2, 2, TILE, TILE), lambda p: (p, 0, 0, 0)),
        ],
        out_specs=[
            pl.BlockSpec((SEQ, TILE), lambda p: (0, p)),
            pl.BlockSpec((SEQ, TILE), lambda p: (0, p)),
        ],
        out_shape=[
            jax.ShapeDtypeStruct((SEQ, cols), BF),
            jax.ShapeDtypeStruct((SEQ, cols), F32),
        ],
        compiler_params=pltpu.CompilerParams(vmem_limit_bytes=40 * MIB),
        cost_estimate=SMALL_COST,
        name="attend",
    )(length, qkv, qkv, qkv, near)


def attend_back_kernel(
    length_ref, query_ref, key_ref, value_ref, near_ref, out_ref, log_ref, grad_ref,
    dq_ref, dk_ref, dv_ref, tile_ref, sum_ref, dk_acc, dv_acc,
):
    length = length_ref[0]
    lanes = lane_half(QROWS)
    lanes_all = lane_half(SEQ)
    ones = jnp.ones((SEQ, TILE), BF)
    key_ext = [
        jnp.concatenate([jnp.where(lanes_all, key_ref[...], BF(0)), ones], 1),
        jnp.concatenate([jnp.where(lanes_all, BF(0), key_ref[...]), ones], 1),
    ]
    near_sums = [[None, None], [None, None]]
    all_sums = [None, None]

    for i in range(SEQ // QROWS):
        rows = slice(i * QROWS, (i + 1) * QROWS)
        q_rows = query_ref[rows, :] * BF(0.125)
        g_rows = grad_ref[rows, :]
        mass = g_rows.astype(F32) * out_ref[rows, :].astype(F32)
        dq = None
        for h in range(2):
            keep = lanes if h == 0 else ~lanes
            q_half = jnp.where(keep, q_rows, BF(0))
            g_half = jnp.where(keep, g_rows, BF(0))
            delta = jnp.sum(jnp.where(keep, mass, 0.0), axis=1, keepdims=True)
            log_col = log_ref[rows, h * HEAD_DIM : h * HEAD_DIM + 1]
            for j in range(i + 1):
                keys = slice(j * QROWS, (j + 1) * QROWS)
                s = dot(q_half, key_ref[keys, :], NT)
                dp = dot(g_half, value_ref[keys, :], NT)
                p_strips, d_strips = [], []
                for start in range(0, QROWS, STRIP):
                    strip = slice(start, start + STRIP)
                    p = jnp.exp(score_strip(s, i, j, start, near_ref, h, length) - log_col[strip])
                    p_strips.append(p.astype(BF))
                    d_strips.append((p * (dp[strip] - delta[strip])).astype(BF))
                p, ds = jnp.concatenate(p_strips, 0), jnp.concatenate(d_strips, 0)
                part = dot(ds, key_ext[h][keys, :])
                dq = put(dq, part[:, :TILE])
                all_sums[h] = put(all_sums[h], jnp.sum(part[:, TILE:].reshape(QROWS // 8, 8, TILE), axis=0))
                dk_part = dot(ds, q_half, TN)
                dv_part = dot(p, g_half, TN)
                if i == j and h == 0:
                    dk_acc[keys, :] = dk_part
                    dv_acc[keys, :] = dv_part
                else:
                    dk_acc[keys, :] += dk_part
                    dv_acc[keys, :] += dv_part
                if j == i:
                    wide = ds.astype(F32)
                    near_sums[h][0] = put(near_sums[h][0], wide[:TILE, :TILE] + wide[TILE:, TILE:])
                    near_sums[h][1] = put(near_sums[h][1], wide[TILE:, :TILE])
                elif j == i - 1:
                    near_sums[h][1] = put(near_sums[h][1], ds[:TILE, TILE:].astype(F32))
        dq_ref[rows, :] = (dq * 0.125).astype(BF)
    dk_ref[...] = dk_acc[...].astype(BF)
    dv_ref[...] = dv_acc[...].astype(BF)
    for h in range(2):
        tile_ref[h, 0] = near_sums[h][0]
        tile_ref[h, 1] = near_sums[h][1]
        sum_ref[h] = all_sums[h]


def attend_back(length, qkv, near, mixed, logs, grad, first, count):
    pairs = qkv.shape[1] // (3 * TILE)
    cols = count * TILE
    col = pl.BlockSpec((SEQ, TILE), lambda p: (0, first + p))
    out = pl.BlockSpec((SEQ, TILE), lambda p: (0, p))
    return pl.pallas_call(
        attend_back_kernel,
        grid=(count,),
        in_specs=[
            pl.BlockSpec(memory_space=pltpu.SMEM),
            col,
            pl.BlockSpec((SEQ, TILE), lambda p: (0, pairs + first + p)),
            pl.BlockSpec((SEQ, TILE), lambda p: (0, 2 * pairs + first + p)),
            pl.BlockSpec((2, 2, TILE, TILE), lambda p: (first + p, 0, 0, 0)),
            col,
            col,
            col,
        ],
        out_specs=[
            out,
            out,
            out,
            pl.BlockSpec((2, 2, TILE, TILE), lambda p: (p, 0, 0, 0)),
            pl.BlockSpec((2, 8, TILE), lambda p: (p, 0, 0)),
        ],
        out_shape=[
            jax.ShapeDtypeStruct((SEQ, cols), BF),
            jax.ShapeDtypeStruct((SEQ, cols), BF),
            jax.ShapeDtypeStruct((SEQ, cols), BF),
            jax.ShapeDtypeStruct((2 * count, 2, TILE, TILE), F32),
            jax.ShapeDtypeStruct((2 * count, 8, TILE), F32),
        ],
        scratch_shapes=[pltpu.VMEM((SEQ, TILE), F32), pltpu.VMEM((SEQ, TILE), F32)],
        compiler_params=pltpu.CompilerParams(vmem_limit_bytes=40 * MIB),
        cost_estimate=SMALL_COST,
        name="attend_back",
    )(length, qkv, qkv, qkv, near, mixed, logs, grad)


def low_lanes(shape):
    return lax.broadcasted_iota(jnp.int32, shape, 1) < HEAD_DIM


def turned(tile):
    return pltpu.roll(tile, HEAD_DIM, 1)


def pack_kernel(q_ref, k_ref, v_ref, o_ref, one_ref, two_ref, router_ref, out_ref):
    shard = q_ref.shape[1]
    rows = q_ref.shape[0]
    source = lax.broadcasted_iota(jnp.int32, (shard, 6 * TILE), 0)
    target = lax.broadcasted_iota(jnp.int32, (shard, 6 * TILE), 1)

    def moved(pair_base, last_base):
        want = jnp.where(source < TILE, source + pair_base, source - TILE + last_base)
        return jnp.where(target == want, 1.0, 0.0).astype(BF)

    total = dot(v_ref[...], moved(0, 2 * TILE)) + dot(o_ref[...], moved(TILE, 2 * TILE + HEAD_DIM), TN)
    total = total + dot(q_ref[...], moved(3 * TILE, 5 * TILE)) + dot(k_ref[...], moved(4 * TILE, 5 * TILE + HEAD_DIM))
    out_ref[:, : 6 * TILE] = total.astype(BF)
    experts = router_ref.shape[0]
    own_row = lax.broadcasted_iota(jnp.int32, (rows, rows), 0) == lax.broadcasted_iota(jnp.int32, (rows, rows), 1)

    def column(ref):
        return jnp.sum(jnp.where(own_row, ref[...].astype(F32), 0.0), axis=1, keepdims=True)

    lanes = lax.broadcasted_iota(jnp.int32, (experts, TILE), 1)
    spread = jnp.where(lanes == lax.broadcasted_iota(jnp.int32, (experts, TILE), 0), 1.0, 0.0).astype(BF)
    place = lax.broadcasted_iota(jnp.int32, (rows, TILE), 1)
    small = dot(router_ref[...], spread, TN)
    small = jnp.where(place == experts, column(one_ref), jnp.where(place == experts + 1, column(two_ref), small))
    out_ref[:, 6 * TILE :] = small.astype(BF)


def pack_weights(query, key, value, output, one, two, router):
    rows = query.shape[0]
    return pl.pallas_call(
        pack_kernel,
        out_shape=jax.ShapeDtypeStruct((rows, 7 * TILE), BF),
        compiler_params=pltpu.CompilerParams(vmem_limit_bytes=60 * MIB),
        cost_estimate=SMALL_COST,
        name="pack_weights",
    )(query, key, value, output, one[None], two[None], router.T)


def qkv_kernel(micro_ref, tokens_ref, gain_ref, a_own, a_far, b_own, b_far, qkv_ref, normed_ref, weight_ref, output_ref):
    width = tokens_ref.shape[2]

    @pl.when(pl.program_id(0) == 0)
    def _():
        low = low_lanes((width, TILE))

        def tiles(own, far, pair, low_half):
            at = slice(pair * TILE, (pair + 1) * TILE)
            one, two = own[:, 2 * TILE :].astype(F32), far[:, 2 * TILE :].astype(F32)
            last = jnp.where(low, one, turned(two)) if low_half else jnp.where(low, turned(one), two)
            return own[:, at], far[:, at], last.astype(BF)

        for n, (own, far, pair, low_half) in enumerate(
            ((a_own, a_far, 0, True), (a_own, a_far, 1, False), (b_own, b_far, 0, True))
        ):
            for t, tile in enumerate(tiles(own[...], far[...], pair, low_half)):
                at = 3 * n + t
                weight_ref[:, at * TILE : (at + 1) * TILE] = tile
        for t, tile in enumerate(tiles(b_own[...], b_far[...], 1, False)):
            output_ref[:, t * TILE : (t + 1) * TILE] = tile

    x = tokens_ref[0].astype(F32)
    inverse = lax.rsqrt(jnp.mean(x * x, axis=-1, keepdims=True) + 1e-06)
    normed = (x * inverse * gain_ref[...]).astype(BF)
    normed_ref[...] = normed
    qkv_ref[...] = dot(normed, weight_ref[...]).astype(BF)


def norm_and_project(micro, layer_input, gain, a_own, a_far, b_own, b_far):
    width = layer_input.shape[2]
    block = 256
    cols = 3 * TILE
    whole = lambda rows, n: pl.BlockSpec((rows, n), lambda i, m: (0, 0))
    here = lambda n: pl.BlockSpec((block, n), lambda i, m: (i, 0))
    return pl.pallas_call(
        qkv_kernel,
        grid_spec=pltpu.PrefetchScalarGridSpec(
            num_scalar_prefetch=1,
            grid=(SEQ // block,),
            in_specs=[pl.BlockSpec((1, block, width), lambda i, m: (m[0], i, 0)), whole(1, width)] + [whole(width, cols)] * 4,
            out_specs=[here(3 * cols), here(width), whole(width, 3 * cols), whole(width, cols)],
        ),
        out_shape=[
            jax.ShapeDtypeStruct((SEQ, 3 * cols), BF),
            jax.ShapeDtypeStruct((SEQ, width), BF),
            jax.ShapeDtypeStruct((width, 3 * cols), BF),
            jax.ShapeDtypeStruct((width, cols), BF),
        ],
        compiler_params=pltpu.CompilerParams(vmem_limit_bytes=40 * MIB),
        cost_estimate=SMALL_COST,
        name="norm_and_project",
    )(micro, layer_input, gain, a_own, a_far, b_own, b_far)


def middle_kernel(
    blocks, per, micro_ref, tokens_ref, mixed_ref, other_ref, own_ref, far_ref, gain_ref, code_ref, residual_ref, *refs
):
    sent_refs, normed = refs[:-1], refs[-1]
    step = pl.program_id(0)
    rows = tokens_ref.shape[1]

    @pl.when(step < blocks)
    def _():
        total = tokens_ref[0].astype(F32) + dot(mixed_ref[...], own_ref[...], NT) + dot(other_ref[...], far_ref[...], NT)
        residual_ref[...] = total
        inverse = lax.rsqrt(jnp.mean(total * total, axis=-1, keepdims=True) + 1e-06)
        normed[pl.ds(pl.multiple_of(step * rows, rows), rows), :] = (total * inverse * gain_ref[...]).astype(BF)

    for c, sent_ref in enumerate(sent_refs):

        @pl.when((step >= blocks + c * per) & (step < blocks + (c + 1) * per))
        def _(sent_ref=sent_ref):
            block = sent_ref.shape[0]
            ids = lax.broadcasted_iota(jnp.int32, (block, 1), 0) + (step - blocks) * block
            hot = jnp.where((ids == code_ref[:1]) | (ids == code_ref[1:2]), 1.0, 0.0).astype(BF)
            sent_ref[...] = dot(hot, normed[...]).astype(BF)


def residual_and_rows(micro, layer_input, mixed, other, output_own, output_far, gain, code, count, chunks):
    width = layer_input.shape[2]
    block = 256
    blocks = SEQ // block
    send = 320
    cols = mixed.shape[1]
    per = count // send
    at = lambda i: jnp.minimum(i, blocks - 1)
    whole = lambda arr: pl.BlockSpec(arr.shape, lambda i, m: (0, 0))
    here = lambda n: pl.BlockSpec((block, n), lambda i, m: (at(i), 0))

    def sent(c):
        return pl.BlockSpec((send, width), lambda i, m: (jnp.clip(i - blocks - c * per, 0, per - 1), 0))

    return pl.pallas_call(
        functools.partial(middle_kernel, blocks, per),
        grid_spec=pltpu.PrefetchScalarGridSpec(
            num_scalar_prefetch=1,
            grid=(blocks + chunks * per,),
            in_specs=[
                pl.BlockSpec((1, block, width), lambda i, m: (m[0], at(i), 0)),
                here(cols), here(cols), whole(output_own), whole(output_far), whole(gain), whole(code),
            ],
            out_specs=[here(width)] + [sent(c) for c in range(chunks)],
            scratch_shapes=[pltpu.VMEM((SEQ, width), BF)],
        ),
        out_shape=[jax.ShapeDtypeStruct((SEQ, width), F32)] + [jax.ShapeDtypeStruct((count, width), BF)] * chunks,
        compiler_params=pltpu.CompilerParams(vmem_limit_bytes=40 * MIB),
        cost_estimate=SMALL_COST,
        name="residual_and_rows",
    )(micro, layer_input, mixed, other, output_own, output_far, gain, code)


def picked_rows(first, second, segments):
    total = None
    start = 0
    for rows in segments:
        length = rows.shape[0]
        ids = lax.broadcasted_iota(jnp.int32, (1, length), 1) + start
        hot = []
        for at in range(0, first.shape[0], STRIP):
            one, two = first[at : at + STRIP], second[at : at + STRIP]
            hot.append(jnp.where((one == ids) | (two == ids), 1.0, 0.0).astype(BF))
        total = put(total, dot(jnp.concatenate(hot, 0), rows))
        start += length
    return total


def put(a, b):
    return b if a is None else a + b


def folded(product):
    return jnp.sum(product.reshape(product.shape[0] // 8, 8, product.shape[1]), axis=0)


def as_column(eight):
    ones = jnp.ones((16, TILE), BF)
    high = eight.astype(BF)
    rest = (eight - high.astype(F32)).astype(BF)
    return dot(jnp.concatenate([high, rest], 0), ones, TN)


def combine_kernel(experts, half, spare, micro_ref, core_ref, length_ref, *refs):
    info_ref, grad_ref, residual_ref, mixed_ref, gain_ref, router_ref, output_ref = refs[:7]
    backs = refs[7:-9]
    (total_ref, mixed_grad_ref, extra_ref, far_ref, own_ref, acc_ref, router_acc, gain_acc, tables) = refs[-9:]
    block = residual_ref.shape[0]
    step = pl.program_id(0)
    count = len(backs) // 2

    @pl.when(step == 0)
    def _():
        place = lax.broadcasted_iota(jnp.int32, (experts, 1), 0)
        for n, back in enumerate((backs[count - 1], backs[2 * count - 1])):
            table = jnp.zeros((experts, back.shape[2]), F32)
            for e in range(experts):
                row = back[e, spare : spare + 16, :].astype(F32)[:1]
                table = jnp.where(place == e, row, table)
            for piece in range(3):
                at = (3 * n + piece) * experts
                tables[at : at + experts] = table[:, piece * half : (piece + 1) * half]

    info = jnp.transpose(info_ref[...])
    number = lambda n: info[:, n : n + 1]
    columns = lax.broadcasted_iota(jnp.int32, (1, half), 1)
    lanes = lax.broadcasted_iota(jnp.int32, (1, 6 * experts), 1)
    table = tables[...].astype(BF)
    values = []
    for k in range(2):
        slot = number(4 + k)
        hot = jnp.where(columns == lax.rem(slot, half), 1.0, 0.0).astype(BF)
        found = dot(hot, table, NT)
        wanted = jnp.where(slot // half == core_ref[0], 0, 3 * experts) + number(2 + k)
        away = lanes - wanted
        hit = (away == 0) | (away == experts) | (away == 2 * experts)
        values.append(jnp.sum(jnp.where(hit, found, 0.0), axis=1, keepdims=True))
    wide = lax.broadcasted_iota(jnp.int32, (1, TILE), 1)
    is_first, is_second = wide == number(2), wide == number(3)
    residual = residual_ref[...]
    gain = gain_ref[...]
    inverse = lax.rsqrt(jnp.mean(residual * residual, axis=-1, keepdims=True) + 1e-06)
    plain = residual * inverse
    normed = (plain * gain).astype(BF)
    logits = dot(normed, router_ref[...])
    gap = jnp.sum(jnp.where(is_first, logits, 0.0) - jnp.where(is_second, logits, 0.0), axis=1, keepdims=True)
    small = jnp.exp(-jnp.abs(gap))
    logit = small / ((1.0 + small) * (1.0 + small)) * (values[0] - values[1])
    logit_grad = jnp.where(is_first, logit, jnp.where(is_second, -logit, 0.0)).astype(BF)
    segments = [b[...].reshape(b.shape[0] * b.shape[1], b.shape[2]) for b in backs]
    normed_grad = picked_rows(number(0), number(1), segments) + dot(logit_grad, router_ref[...], NT)
    scaled = normed_grad * gain
    mean = jnp.mean(scaled * plain, axis=-1, keepdims=True)
    place = lax.broadcasted_iota(jnp.int32, (block, 1), 0) + step * block
    grad_out = jnp.where(place < length_ref[0], grad_ref[0].astype(F32), 0.0)
    total = grad_out + inverse * (scaled - plain * mean)
    total_ref[...] = total
    branch = total.astype(BF)
    mixed_grad_ref[...] = dot(branch, output_ref[...]).astype(BF)
    router_part = dot(logit_grad, normed, TN)
    gain_part = folded(normed_grad * plain)
    output_part = dot(mixed_ref[...], branch, TN)

    @pl.when(step == 0)
    def _():
        router_acc[...] = router_part
        gain_acc[...] = gain_part
        acc_ref[...] = output_part

    @pl.when(step > 0)
    def _():
        router_acc[...] += router_part
        gain_acc[...] += gain_part
        acc_ref[...] += output_part

    @pl.when(step == pl.num_programs(0) - 1)
    def _():
        extra_ref[...] = jnp.transpose(router_acc[...]) + jnp.where(wide == experts + 1, as_column(gain_acc[...]), 0.0)
        parts = jnp.transpose(acc_ref[...])
        far_ref[...] = parts[:, TILE:].astype(BF)
        own_ref[:, :TILE] = parts[:, :TILE]
        own_ref[:, TILE:] = parts[:, 2 * TILE :]


def combine(micro, core, length, info, out_grad, residual, mixed, gain, router, output_own, backs, half, spare):
    width = residual.shape[1]
    block = 512
    cols = mixed.shape[1]
    whole = lambda arr: pl.BlockSpec(arr.shape, lambda i, *_: (0,) * arr.ndim)
    fixed = lambda rows, n: pl.BlockSpec((rows, n), lambda i, *_: (0, 0))
    here = lambda n: pl.BlockSpec((block, n), lambda i, *_: (i, 0))
    experts = backs[0].shape[0]
    return pl.pallas_call(
        functools.partial(combine_kernel, experts, half, spare),
        grid_spec=pltpu.PrefetchScalarGridSpec(
            num_scalar_prefetch=3,
            grid=(SEQ // block,),
            in_specs=[
                pl.BlockSpec((8, block), lambda i, *_: (0, i)),
                pl.BlockSpec((1, block, width), lambda i, m, *_: (m[0], i, 0)),
                here(width), here(cols), whole(gain), whole(router), whole(output_own),
            ]
            + [whole(x) for x in backs],
            out_specs=[here(width), here(cols), fixed(width, TILE), fixed(width, 2 * TILE), fixed(width, 2 * TILE)],
            scratch_shapes=[
                pltpu.VMEM((cols, width), F32),
                pltpu.VMEM((TILE, width), F32),
                pltpu.VMEM((8, width), F32),
                pltpu.VMEM((6 * experts, half), F32),
            ],
        ),
        out_shape=[
            jax.ShapeDtypeStruct((SEQ, width), F32),
            jax.ShapeDtypeStruct((SEQ, cols), BF),
            jax.ShapeDtypeStruct((width, TILE), F32),
            jax.ShapeDtypeStruct((width, 2 * TILE), BF),
            jax.ShapeDtypeStruct((width, 2 * TILE), F32),
        ],
        compiler_params=pltpu.CompilerParams(vmem_limit_bytes=40 * MIB),
        cost_estimate=SMALL_COST,
        name="combine",
    )(micro, core, length, info, out_grad, residual, mixed, gain, router, output_own, *backs)


def projected_back(weight_ref, grads):
    total = None
    for n, grad in enumerate(grads):
        cols = grad.shape[1]
        total = put(total, dot(grad[...], weight_ref[:, n * cols : (n + 1) * cols], NT))
    return total


def attention_weight_kernel(
    blocks, core_ref, normed_ref, q_ref, k_ref, v_ref, output_ref, weight_ref, q_rows, k_rows, v_rows, far_ref, own_ref, sent_ref
):
    step = pl.program_id(0)

    @pl.when(step < blocks)
    def _():
        low = low_lanes((normed_ref.shape[1], TILE))
        q, k, v = (dot(normed_ref[...], d[...], TN) for d in (q_ref, k_ref, v_ref))
        for n, part in enumerate((q, k, v)):
            own_ref[:, n * TILE : (n + 1) * TILE] = part[:, :TILE]
            far_ref[:, n * TILE : (n + 1) * TILE] = part[:, TILE : 2 * TILE].astype(BF)
        q, k, v = (part[:, 2 * TILE :] for part in (q, k, v))
        far_ref[:, 3 * TILE : 4 * TILE] = jnp.where(low, turned(q), k).astype(BF)
        far_ref[:, 4 * TILE : 5 * TILE] = jnp.where(low, turned(v), output_ref[:, TILE:].astype(F32)).astype(BF)
        far_ref[:, 5 * TILE :] = output_ref[:, :TILE]
        own_ref[:, 3 * TILE : 4 * TILE] = jnp.where(low, q, turned(k))
        own_ref[:, 4 * TILE :] = jnp.where(low, v, 0.0)

    @pl.when(step >= blocks)
    def _():
        sent_ref[...] = projected_back(weight_ref, (q_rows, k_rows, v_rows))


def attention_weight_grads(core, normed, q, k, v, output, weight):
    width = normed.shape[1]
    block = 256
    blocks = width // block
    at = lambda i: jnp.minimum(i, blocks - 1)
    later = lambda i: jnp.maximum(i, blocks) - blocks
    whole = lambda arr: pl.BlockSpec(arr.shape, lambda i, c: (0, 0))
    here = lambda n: pl.BlockSpec((block, n), lambda i, c: (at(i), 0))
    rows = pl.BlockSpec((block, q.shape[1]), lambda i, c: ((1 - c[0]) * 2 + later(i), 0))
    return pl.pallas_call(
        functools.partial(attention_weight_kernel, blocks),
        grid_spec=pltpu.PrefetchScalarGridSpec(
            num_scalar_prefetch=1,
            grid=(blocks + 2,),
            in_specs=[
                pl.BlockSpec((SEQ, block), lambda i, c: (0, at(i))),
                whole(q), whole(k), whole(v), here(2 * TILE), whole(weight), rows, rows, rows,
            ],
            out_specs=[here(6 * TILE), here(5 * TILE), pl.BlockSpec((block, width), lambda i, c: (later(i), 0))],
        ),
        out_shape=[
            jax.ShapeDtypeStruct((width, 6 * TILE), BF),
            jax.ShapeDtypeStruct((width, 5 * TILE), F32),
            jax.ShapeDtypeStruct((2 * block, width), F32),
        ],
        compiler_params=pltpu.CompilerParams(vmem_limit_bytes=60 * MIB),
        cost_estimate=SMALL_COST,
        name="attention_weight_grads",
    )(core, normed, q, k, v, output, weight, q, k, v)


def both_kernel(
    lane, micro_ref, core_ref, length_ref, weight_ref, q, k, v, got_ref, tokens_ref, gain_ref, grad_ref,
    info_ref, residual_ref, own_ref, far_ref, out_ref, extra_ref, acc_ref,
):
    block = residual_ref.shape[0]
    info = jnp.transpose(info_ref[...])
    place = lax.broadcasted_iota(jnp.int32, (block, 1), 0) + (core_ref[0] * 2 + pl.program_id(0)) * block
    rows = residual_ref[...] + picked_rows(info[:, 6:7], info[:, 7:8], (own_ref[...], far_ref[...]))
    out_ref[0] = jnp.where(place < length_ref[0], rows, 0.0).astype(BF)
    normed_grad = got_ref[...] + projected_back(weight_ref, (q, k, v))
    x = tokens_ref[0].astype(F32)
    inverse = lax.rsqrt(jnp.mean(x * x, axis=-1, keepdims=True) + 1e-06)
    plain = x * inverse
    scaled = normed_grad * gain_ref[...]
    mean = jnp.mean(scaled * plain, axis=-1, keepdims=True)
    out_ref[1] = (grad_ref[...] + inverse * (scaled - plain * mean)).astype(BF)
    wide = lax.broadcasted_iota(jnp.int32, (1, TILE), 1)
    part = folded(normed_grad * plain)

    @pl.when(pl.program_id(0) == 0)
    def _():
        acc_ref[...] = part

    @pl.when(pl.program_id(0) == 1)
    def _():
        extra_ref[...] = jnp.where(wide == lane, as_column(acc_ref[...] + part), 0.0)


def both_rows(lane, micro, core, length, weight, grads, got, layer_input, gain, residual_grad, info, residual, own, far):
    width = weight.shape[0]
    block = 256
    here = lambda n: pl.BlockSpec((block, n), lambda i, m, c, *_: (c[0] * 2 + i, 0))
    whole = lambda arr: pl.BlockSpec(arr.shape, lambda i, *_: (0, 0))
    return pl.pallas_call(
        functools.partial(both_kernel, lane),
        grid_spec=pltpu.PrefetchScalarGridSpec(
            num_scalar_prefetch=3,
            grid=(2,),
            in_specs=[whole(weight)]
            + [here(grads[0].shape[1])] * 3
            + [
                pl.BlockSpec((block, width), lambda i, *_: (i, 0)),
                pl.BlockSpec((1, block, width), lambda i, m, c, *_: (m[0], c[0] * 2 + i, 0)),
                whole(gain),
                here(width),
                pl.BlockSpec((8, block), lambda i, m, c, *_: (0, c[0] * 2 + i)),
                here(width),
                whole(own),
                whole(far),
            ],
            out_specs=[
                pl.BlockSpec((2, block, width), lambda i, *_: (0, i, 0)),
                pl.BlockSpec((width, TILE), lambda i, *_: (0, 0)),
            ],
            scratch_shapes=[pltpu.VMEM((8, width), F32)],
        ),
        out_shape=[jax.ShapeDtypeStruct((2, 2 * block, width), BF), jax.ShapeDtypeStruct((width, TILE), F32)],
        compiler_params=pltpu.CompilerParams(vmem_limit_bytes=60 * MIB),
        cost_estimate=SMALL_COST,
        name="both_rows",
    )(micro, core, length, weight, *grads, got, layer_input, gain, residual_grad, info, residual, own, far)


def sum_kernel(kept, own, got, out_own, early, late, late_far, table, sum_ref):
    low = low_lanes(early.shape)
    sum_ref[:, : 4 * TILE] = (own[:, : 4 * TILE] + got[:, : 4 * TILE].astype(F32)).astype(BF)
    mixed = jnp.where(low, own[:, 4 * TILE :], turned(out_own[:, TILE:]))
    sum_ref[:, 4 * TILE : 5 * TILE] = (mixed + got[:, 4 * TILE : 5 * TILE].astype(F32)).astype(BF)
    sum_ref[:, 5 * TILE : 6 * TILE] = (out_own[:, :TILE] + got[:, 5 * TILE :].astype(F32)).astype(BF)
    extra = early[...] + late[...] + late_far[...] + table[...]
    high = extra.astype(BF)
    rest = extra - high.astype(F32)
    if kept <= HEAD_DIM:
        sum_ref[:, 6 * TILE :] = jnp.where(low, high.astype(F32), turned(rest)).astype(BF)
    else:
        sum_ref[:, 6 * TILE : 7 * TILE] = high
        sum_ref[:, 7 * TILE :] = rest.astype(BF)


def packed_sums(kept, *parts):
    width = parts[0].shape[0]
    cols = (7 if kept <= HEAD_DIM else 8) * TILE
    block = 256
    here = lambda n: pl.BlockSpec((block, n), lambda i: (i, 0))
    return pl.pallas_call(
        functools.partial(sum_kernel, kept),
        grid=(width // block,),
        in_specs=[here(x.shape[1]) for x in parts],
        out_specs=here(cols),
        out_shape=jax.ShapeDtypeStruct((width, cols), BF),
        compiler_params=pltpu.CompilerParams(vmem_limit_bytes=40 * MIB),
        cost_estimate=SMALL_COST,
        name="packed_sums",
    )(*parts)


def final_kernel(kept, parts_ref, q_ref, k_ref, v_ref, o_ref, small_ref):
    total = parts_ref[0].astype(F32)
    for n in range(1, parts_ref.shape[0]):
        total = total + parts_ref[n].astype(F32)
    tile = lambda t: total[:, t * TILE : (t + 1) * TILE]
    q_ref[:, :TILE] = tile(0)
    q_ref[:, TILE:] = tile(3)[:, :HEAD_DIM]
    k_ref[:, :TILE] = tile(1)
    k_ref[:, TILE:] = turned(tile(3))[:, :HEAD_DIM]
    v_ref[:, :TILE] = tile(2)
    v_ref[:, TILE:] = tile(4)[:, :HEAD_DIM]
    o_ref[:, :TILE] = tile(5)
    o_ref[:, TILE:] = turned(tile(4))[:, :HEAD_DIM]
    small_ref[...] = tile(6) + (turned(tile(6)) if kept <= HEAD_DIM else tile(7))


def final_sums(kept, parts, shard):
    rows = parts.shape[1]
    return pl.pallas_call(
        functools.partial(final_kernel, kept),
        out_shape=[jax.ShapeDtypeStruct((rows, shard), F32)] * 4 + [jax.ShapeDtypeStruct((rows, TILE), F32)],
        compiler_params=pltpu.CompilerParams(vmem_limit_bytes=40 * MIB),
        cost_estimate=SMALL_COST,
        name="final_sums",
    )(parts)


def pair_gate(logits, own, other):
    lanes = lax.broadcasted_iota(jnp.int32, logits.shape, 1)
    gap = jnp.sum(
        jnp.where(lanes == own, logits, 0.0) - jnp.where(lanes == other, logits, 0.0), axis=1, keepdims=True
    )
    small = jnp.exp(-jnp.abs(gap))
    return jnp.where(gap >= 0.0, 1.0, small) / (1.0 + small)


def expert_kernel(lead, chunk, half, me_ref, partner_ref, rows_ref, grads_ref, router_ref, *refs):
    before, refs = (refs[0], refs[1:]) if lead is not None and lead > 0 else (None, refs)
    firsts, seconds = refs[:4], refs[4:8]
    back_ref, active_ref, slope_ref, gated_ref, gate_ref, mass_ref = refs[8:]
    rows = rows_ref[...]
    grads = grads_ref[...]
    gate = pair_gate(dot(rows, router_ref[...]), me_ref[0], partner_ref[...])
    gated_ref[...] = (gate * grads.astype(F32)).astype(BF)
    gate_ref[...] = jnp.broadcast_to(gate, gate_ref.shape)
    masses = [None] * (rows.shape[0] // STRIP)
    back = None
    width = firsts[0].shape[1]
    step = 256
    places = [(r, c) for r in range(4) for c in range(0, width, step)]

    def products(r, c):
        return dot(rows, firsts[r][:, c : c + step]), dot(grads, seconds[r][c : c + step, :], NT)

    ahead = products(*places[0])
    for n, (r, c) in enumerate(places):
        x, plain = ahead
        if n + 1 < len(places):
            ahead = products(*places[n + 1])
        place = slice(r * width + c, r * width + c + step)
        for at in range(0, rows.shape[0], STRIP):
            strip = slice(at, at + STRIP)
            value, flow = x[strip], plain[strip]
            square = value * value
            bent = jnp.tanh(value * (GELU_C + (GELU_C * GELU_A) * square))
            rise = 0.5 + 0.5 * bent
            active = value * rise
            slope = rise + active * (1.0 - bent) * (GELU_C + (3.0 * GELU_C * GELU_A) * square)
            low = active.astype(BF)
            active_ref[strip, place] = low
            slope_ref[strip, place] = (gate[strip] * flow * slope).astype(BF)
            part = low.astype(F32) * flow
            masses[at // STRIP] = put(masses[at // STRIP], part[:, :TILE] + part[:, TILE:])
        if c + step == width and r > 0:
            back = put(back, dot(slope_ref[:, (r - 1) * width : r * width], firsts[r - 1][...], NT))
    back = put(back, dot(slope_ref[:, 3 * width :], firsts[3][...], NT))
    back = back.astype(BF)
    mass = jnp.sum(jnp.concatenate(masses, 0), axis=1, keepdims=True)
    if lead is None:
        back_ref[...] = back
        mass_ref[...] = jnp.broadcast_to(mass, mass_ref.shape)
        return
    count = rows.shape[0] // chunk
    number = lax.broadcasted_iota(jnp.int32, (rows.shape[0], 1), 0)
    lanes = lax.broadcasted_iota(jnp.int32, (1, rows.shape[1]), 1)
    inside = lax.rem(number, chunk)
    spread = jnp.zeros(rows.shape, F32)
    for piece in range(3):
        high = mass.astype(BF).astype(F32)
        spread = jnp.where(lanes == piece * half + lead + inside, high, spread)
        mass = mass - high
    own = jnp.where(number // chunk == lax.broadcasted_iota(jnp.int32, (1, TILE), 1), 1.0, 0.0).astype(BF)
    line = dot(own, spread.astype(BF), TN)
    if before is None:
        back_ref[...] = back
        for e in range(count):
            mass_ref[e] = line[e : e + 1].astype(BF)
    else:
        back_ref[:, :chunk] = back.reshape(count, chunk, back.shape[1])
        row = lax.broadcasted_iota(jnp.int32, (16, 1), 0)
        for e in range(count):
            both = line[e : e + 1] + before[e].astype(F32)
            back_ref[e, chunk:] = jnp.where(row == 0, both, 0.0).astype(BF)


def row_block(total):
    return 320 if total % 320 == 0 else total


def expert_rows_pass(lead, chunk, half, me, partner, rows, grads, router, before, firsts, seconds):
    total, width = rows.shape
    block = row_block(total)
    experts = total // chunk
    hidden = sum(f.shape[1] for f in firsts)
    here = lambda cols: pl.BlockSpec((block, cols), lambda i: (i, 0))
    whole = lambda arr: pl.BlockSpec(arr.shape, lambda i: (0, 0))
    lines = pl.BlockSpec((block // chunk, 1, width), lambda i: (i, 0, 0))
    back_shape, back_spec = (total, width), here(width)
    mass_shape, mass_spec, mass_kind = (experts, 1, width), lines, BF
    if lead is None:
        mass_shape, mass_spec, mass_kind = (total, TILE), here(TILE), F32
    elif before is not None:
        back_shape = (experts, chunk + 16, width)
        back_spec = pl.BlockSpec((block // chunk, chunk + 16, width), lambda i: (i, 0, 0))
    return pl.pallas_call(
        functools.partial(expert_kernel, lead, chunk, half),
        grid=(total // block,),
        in_specs=[pl.BlockSpec(memory_space=pltpu.SMEM), here(1), here(width), here(width), whole(router)]
        + ([lines] if before is not None else [])
        + [whole(w) for w in firsts]
        + [whole(w) for w in seconds],
        out_specs=[back_spec, here(hidden), here(hidden), here(width), here(TILE), mass_spec],
        out_shape=[
            jax.ShapeDtypeStruct(back_shape, BF),
            jax.ShapeDtypeStruct((total, hidden), BF),
            jax.ShapeDtypeStruct((total, hidden), BF),
            jax.ShapeDtypeStruct((total, width), BF),
            jax.ShapeDtypeStruct((total, TILE), F32),
            jax.ShapeDtypeStruct(mass_shape, mass_kind),
        ],
        compiler_params=pltpu.CompilerParams(vmem_limit_bytes=56 * MIB),
        cost_estimate=SMALL_COST,
        name="expert_rows",
    )(me, partner, rows, grads, router, *([before] if before is not None else []), *firsts, *seconds)


def weight_parts(count, refs):
    rows, slopes, active, gated = (refs[n * count : (n + 1) * count] for n in range(4))
    first, second = None, None
    for n in range(count):
        first = put(first, dot(rows[n][...], slopes[n][...], TN))
        second = put(second, dot(active[n][...], gated[n][...], TN))
    return first, second


def cross_kernel(count, *refs):
    first, second = weight_parts(count, refs)
    refs[-1][0, 0] = first.astype(BF)
    refs[-1][0, 1] = second.astype(BF)


def kept_kernel(count, *refs):
    got_ref, far_ref, kept_ref = refs[-3:]
    first, second = weight_parts(count, refs)
    first = first + got_ref[0, 0].astype(F32)
    second = second + got_ref[0, 1].astype(F32)

    @pl.when(pl.program_id(0) == 0)
    def _():
        far_ref[0] = first.astype(BF)
        far_ref[1] = second.astype(BF)

    @pl.when(pl.program_id(0) == 1)
    def _():
        kept_ref[0] = first
        kept_ref[1] = second


def weight_specs(rows, slopes, quarter):
    total, width = rows[0].shape
    hidden = slopes[0].shape[1] // 4
    whole = pl.BlockSpec((total, width), lambda i: (0, 0))
    part = pl.BlockSpec((total, hidden), lambda i: (0, quarter(i)))
    count = len(rows)
    return width, hidden, [whole] * count + [part] * (2 * count) + [whole] * count


def cross_weight_grads(rows, slopes, active, gated):
    width, hidden, specs = weight_specs(rows, slopes, lambda i: 2 + i)
    return pl.pallas_call(
        functools.partial(cross_kernel, len(rows)),
        grid=(2,),
        in_specs=specs,
        out_specs=pl.BlockSpec((1, 2, width, hidden), lambda i: (i, 0, 0, 0)),
        out_shape=jax.ShapeDtypeStruct((2, 2, width, hidden), BF),
        compiler_params=pltpu.CompilerParams(vmem_limit_bytes=56 * MIB),
        cost_estimate=SMALL_COST,
        name="cross_weight_grads",
    )(*rows, *slopes, *active, *gated)


def kept_weight_grads(rows, slopes, active, gated, got):
    width, hidden, specs = weight_specs(rows, slopes, lambda i: 1 - i)
    fixed = pl.BlockSpec((2, width, hidden), lambda i: (0, 0, 0))
    return pl.pallas_call(
        functools.partial(kept_kernel, len(rows)),
        grid=(2,),
        in_specs=specs + [pl.BlockSpec((1, 2, width, hidden), lambda i: (1 - i, 0, 0, 0))],
        out_specs=[fixed, fixed],
        out_shape=[
            jax.ShapeDtypeStruct((2, width, hidden), BF),
            jax.ShapeDtypeStruct((2, width, hidden), F32),
        ],
        compiler_params=pltpu.CompilerParams(vmem_limit_bytes=56 * MIB),
        cost_estimate=SMALL_COST,
        name="kept_weight_grads",
    )(*rows, *slopes, *active, *gated, got)


def result_kernel(chunks, *refs):
    active, gates, seconds, out_ref = refs[:chunks], refs[chunks : 2 * chunks], refs[2 * chunks : -1], refs[-1]
    for c in range(chunks):

        @pl.when(pl.program_id(0) == c)
        def _(c=c):
            width = seconds[0].shape[0]
            total = None
            for r, second in enumerate(seconds):
                total = put(total, dot(active[c][:, r * width : (r + 1) * width], second[...]))
            rows = (total * gates[c][:, :1]).astype(BF)
            if chunks > 1:
                out_ref[:, 0] = rows.reshape(out_ref.shape[0], out_ref.shape[2], out_ref.shape[3])
            else:
                out_ref[...] = rows


def expert_results(active, gates, seconds, experts):
    chunks = len(active)
    total, hidden = active[0].shape
    width = seconds[0].shape[1]
    block = row_block(total)
    steps = total // block

    def here(c, cols):
        return pl.BlockSpec((block, cols), lambda g, i: (jnp.where(g == c, i, jnp.where(g < c, 0, steps - 1)), 0))

    chunk = total // experts
    if chunks > 1:
        shape = (experts, chunks, chunk, width)
        out_spec = pl.BlockSpec((block // chunk, 1, chunk, width), lambda g, i: (i, g, 0, 0))
    else:
        shape = (total, width)
        out_spec = pl.BlockSpec((block, width), lambda g, i: (i, 0))
    out = pl.pallas_call(
        functools.partial(result_kernel, chunks),
        grid=(chunks, steps),
        in_specs=[here(c, hidden) for c in range(chunks)]
        + [here(c, TILE) for c in range(chunks)]
        + [pl.BlockSpec(w.shape, lambda g, i: (0, 0)) for w in seconds],
        out_specs=out_spec,
        out_shape=jax.ShapeDtypeStruct(shape, BF),
        compiler_params=pltpu.CompilerParams(vmem_limit_bytes=56 * MIB),
        cost_estimate=SMALL_COST,
        name="expert_results",
    )(*active, *gates, *seconds)
    return out.reshape(experts, chunks * chunk, width)


def last_sum_kernel(kept_ref, y_ref, out_first, out_second):
    for n, out in enumerate((out_first, out_second)):
        out[...] = kept_ref[n] + y_ref[n].astype(F32)


def last_sums(kept, got_y):
    _, width, hidden = kept.shape
    block = 256
    here = pl.BlockSpec((block, hidden), lambda i: (i, 0))
    part = pl.BlockSpec((2, block, hidden), lambda i: (0, i, 0))
    return pl.pallas_call(
        last_sum_kernel,
        grid=(width // block,),
        in_specs=[part, part],
        out_specs=[here, here],
        out_shape=[jax.ShapeDtypeStruct((width, hidden), F32)] * 2,
        compiler_params=pltpu.CompilerParams(vmem_limit_bytes=40 * MIB),
        cost_estimate=SMALL_COST,
        name="last_sums",
    )(kept, got_y)


def send_kernel(micro_ref, code_ref, rows_ref, out_ref):
    block = out_ref.shape[0]
    ids = lax.broadcasted_iota(jnp.int32, (block, 1), 0) + pl.program_id(0) * block
    hot = jnp.where((ids == code_ref[:1]) | (ids == code_ref[1:2]), 1.0, 0.0).astype(BF)
    out_ref[...] = dot(hot, rows_ref[0]).astype(BF)


def send_rows(micro, code, rows, count):
    width = rows.shape[2]
    block = next(b for b in (336, 320, 384, count) if count % b == 0)
    return pl.pallas_call(
        send_kernel,
        grid_spec=pltpu.PrefetchScalarGridSpec(
            num_scalar_prefetch=1,
            grid=(count // block,),
            in_specs=[
                pl.BlockSpec(code.shape, lambda i, m: (0, 0)),
                pl.BlockSpec((1, SEQ, width), lambda i, m: (m[0], 0, 0)),
            ],
            out_specs=pl.BlockSpec((block, width), lambda i, m: (i, 0)),
        ),
        out_shape=jax.ShapeDtypeStruct((count, width), BF),
        compiler_params=pltpu.CompilerParams(vmem_limit_bytes=40 * MIB),
        cost_estimate=SMALL_COST,
        name="send_rows",
    )(micro, code, rows)


def place_kernel(place_ref, *refs):
    for n, piece in enumerate(refs[:4]):

        @pl.when(pl.program_id(0) == n)
        def _(piece=piece):
            for k, out_ref in enumerate(refs[4:]):
                out_ref[0] = piece[k]


def place_pieces(places, pieces):
    two, rows, width = pieces[0].shape
    whole = pl.BlockSpec(pieces[0].shape, lambda i, place_ref: (0, 0, 0))
    return pl.pallas_call(
        place_kernel,
        grid_spec=pltpu.PrefetchScalarGridSpec(
            num_scalar_prefetch=1,
            grid=(4,),
            in_specs=[whole] * 4,
            out_specs=[pl.BlockSpec((1, rows, width), lambda i, place_ref: (place_ref[i], 0, 0))] * two,
        ),
        out_shape=[jax.ShapeDtypeStruct((4, rows, width), pieces[0].dtype)] * two,
        compiler_params=pltpu.CompilerParams(vmem_limit_bytes=40 * MIB),
        cost_estimate=SMALL_COST,
        name="place_pieces",
    )(places, *pieces)


def swap(value, axis, count, bit):
    return lax.ppermute(value, axis, [(i, i ^ bit) for i in range(count)])


def all_to_all(value):
    return lax.all_to_all(value, "dp", split_axis=0, concat_axis=0, tiled=True)


def together(*values):
    return lax.optimization_barrier(values)


def local(
    layer_input, out_grad, first_gain, query_weight, key_weight, value_weight, output_weight,
    position_bias, second_gain, router_weight, expert_in, expert_out, seq_lengths, routes,
):
    micro_count, tok_rows, width = layer_input.shape
    dp_count = lax.axis_size("dp")
    expert_count = router_weight.shape[1]
    shard = query_weight.shape[1]
    heads_here = position_bias.shape[0]
    assert lax.axis_size("tensor") == 4 and micro_count == 2 and expert_count == dp_count
    assert tok_rows == SEQ and seq_lengths.shape[1] == 1
    capacity = max(8, 8 * (10 * tok_rows // (32 * expert_count)))
    half = capacity // 2
    stride = 8 * (half // 8 + 1)
    by_lines = dp_count == 8
    chunks = 2 if half % 32 == 0 else 1
    chunk = half // chunks
    chunk_rows = expert_count * chunk
    rows_here = query_weight.shape[0]
    me = lax.axis_index("dp")
    rank = lax.axis_index("tensor")
    micro = rank // 2
    core = rank % 2

    def swap_y(value):
        return swap(value, "tensor", 4, 2)

    def swap_core(value):
        return swap(value, "tensor", 4, 1)

    micro_arg = micro.reshape(1).astype(jnp.int32)
    core_arg = core.reshape(1).astype(jnp.int32)

    packed = pack_weights(query_weight, key_weight, value_weight, output_weight, first_gain, second_gain, router_weight)
    three = 3 * TILE

    def doubled(stacked, bit, axis=0):
        other = swap(stacked, "dp", dp_count, bit)
        high = (me & bit) != 0
        pair = jnp.where(high, jnp.stack([other, stacked], axis + 1), jnp.stack([stacked, other], axis + 1))
        return pair.reshape(stacked.shape[:axis] + (-1,) + stacked.shape[axis + 1 :])

    stacked = packed[None]
    bit = dp_count // 2
    while bit > 1:
        stacked = doubled(stacked, bit)
        bit //= 2
    length = lax.dynamic_index_in_dim(seq_lengths, micro, 0, keepdims=False)
    route = lax.dynamic_index_in_dim(routes, micro, 0, keepdims=False).T
    expert_ids = jnp.arange(expert_count, dtype=jnp.int32)
    named = (expert_ids[:, None, None] == route[None]).astype(jnp.int32)
    per_token = jnp.sum(named, axis=1, dtype=jnp.int32)
    earlier = jnp.cumsum(per_token, axis=1, dtype=jnp.int32) - per_token
    slot = jnp.sum(named * earlier[:, None, :], axis=0, dtype=jnp.int32)
    here = slot // half == core
    within = slot % half
    chunk_of = within // chunk
    inside = within % chunk
    spare = 16 * -(-chunk // 16)
    last_stride = spare + 16
    last = (chunks - 1) * chunk_rows
    code_back = jnp.where(
        chunk_of == chunks - 1, last + route * last_stride + inside, chunk_of * chunk_rows + route * chunk + inside
    )
    code_back = code_back + jnp.where(here, 0, last + expert_count * last_stride)
    code_result = route * half + within + jnp.where(here, 0, expert_count * half)
    info = jnp.concatenate([code_back, route, slot, code_result], 0)

    code_grads = jnp.where(here, route * stride + within, -1)
    valid = jnp.arange(SEQ, dtype=jnp.int32) < length[0]
    ids = jnp.arange(expert_count * stride, dtype=jnp.int32)[:, None]
    partner = jnp.sum(
        jnp.where(ids == code_grads[:1], route[1:], 0) + jnp.where(ids == code_grads[1:], route[:1], 0), axis=1, dtype=jnp.int32
    )
    grads_sent = send_rows(micro_arg, jnp.where(valid[None], code_grads, -1), out_grad, expert_count * stride)
    grads_sent = grads_sent.reshape(expert_count, stride, width)
    partner_row = jnp.pad(partner.reshape(expert_count, stride)[:, :half].astype(BF), ((0, 0), (0, width - half)))
    grads_sent = grads_sent.at[:, half].set(partner_row)
    stacked, grads_sent, position_bias = together(stacked, grads_sent, position_bias)
    if by_lines:
        lines = [list(range(x, dp_count, 2)) for x in range(2)]
        grads_z = lax.all_to_all(
            grads_sent.reshape(dp_count // 2, 2, stride, width), "dp", split_axis=0, concat_axis=0,
            axis_index_groups=lines, tiled=True,
        )

    first_own = expert_in[0]
    second_own = expert_out[0]
    part_b = stacked[:, :, :three]
    far_b = swap_y(part_b)
    part_a = doubled(stacked[:, :, three:], 1)
    part_a, far_b = together(part_a, far_b)
    pair_b = jnp.stack([part_b, far_b])
    a_own = part_a[:, :, :three]
    a_far = swap_y(a_own).reshape(width, three)
    a_own = a_own.reshape(width, three)
    pair_b = doubled(pair_b, 1, 1).reshape(2, width, three)
    if by_lines:
        a_far, pair_b, first_own = together(a_far, pair_b, first_own)
    else:
        a_far, pair_b, grads_sent, first_own = together(a_far, pair_b, grads_sent, first_own)
    first_y = swap_y(first_own)
    small_all = part_a[:, :, three:].reshape(width, TILE)
    gain_one = small_all[:, expert_count].astype(F32)[None]
    gain_two = small_all[:, expert_count + 1].astype(F32)[None]
    router_wide = small_all
    far_bias = swap_y(position_bias)
    bias = jnp.concatenate([position_bias[:2], far_bias[:2], position_bias[2:], far_bias[2:]], 0)
    head_total = bias.shape[0]
    hot_const = jnp.asarray(NEAR_HOT, dtype=BF)
    near = dot(bias, hot_const) - bias[:, NB - 1 :].astype(F32)
    near = near.reshape(head_total, 2, TILE, TILE)
    places = jnp.arange(TILE, dtype=jnp.int32)
    causal = jnp.stack([places[None, :] <= places[:, None], jnp.ones((TILE, TILE), bool)])
    near = jnp.where(causal[None], near, NEG)

    if by_lines:
        high = (me & 1) != 0
    else:
        grads_here = all_to_all(grads_sent)

    qkv, normed_one, qkv_weight, output_own = norm_and_project(
        micro_arg, layer_input, gain_one, a_own, a_far, pair_b[0], pair_b[1]
    )
    output_far = swap_core(output_own)
    mixed, logs = attend(length, qkv, near)
    mixed, output_far = together(mixed, output_far)
    mixed_far = swap_core(mixed)
    code_chunks = jnp.where(here, chunk_of * chunk_rows + route * chunk + inside, -1)
    if by_lines:
        sent_x = lax.dynamic_index_in_dim(grads_z, 1 - (me & 1), 1, keepdims=False)
        mixed_far, grads_z, sent_x = together(mixed_far, grads_z, sent_x)
        got_x = swap(sent_x, "dp", dp_count, 1)
    residual, *parts = residual_and_rows(
        micro_arg, layer_input, mixed, mixed_far, output_own, output_far, gain_two, code_chunks, chunk_rows, chunks
    )

    if by_lines:
        parts, first_y, second_own = together(parts, first_y, second_own)
        kept_x = jnp.where(high, grads_z[:, 1], grads_z[:, 0])
        pair_x = jnp.where(high, jnp.stack([got_x, kept_x], 1), jnp.stack([kept_x, got_x], 1))
        grads_here = pair_x.reshape(dp_count, stride, width)
    else:
        parts, grads_here, first_y, second_own = together(parts, grads_here, first_y, second_own)
    second_y = swap_y(second_own)
    parts = [part.reshape(expert_count, chunk, width) for part in parts]
    arrived = [all_to_all(parts[0])]
    partner_here = grads_here[:, half, :half].astype(jnp.int32)

    def chunk_grads(c):
        at = slice(c * chunk, (c + 1) * chunk)
        return grads_here[:, at].reshape(chunk_rows, width), partner_here[:, at].reshape(chunk_rows, 1)

    grads_parts = [chunk_grads(c) for c in range(chunks)]
    arrived[0], grads_parts, second_y = together(arrived[0], grads_parts, second_y)

    firsts = (first_own, first_y, swap_core(first_own), swap_core(first_y))
    seconds = (second_own, second_y, swap_core(second_own), swap_core(second_y))

    for c in range(1, chunks):
        sent, arrived[-1] = together(parts[c], arrived[-1])
        arrived.append(all_to_all(sent))

    me_arg = me.reshape(1).astype(jnp.int32)
    rows_all, slopes, active, gated, gates, backs = [], [], [], [], [], []
    line = None
    for c in range(chunks):
        grads_c, partner_c = grads_parts[c]
        rows_c = arrived[c].reshape(chunk_rows, width)
        back, act, slo, gat, gte, line = expert_rows_pass(
            c * chunk if chunks > 1 else None, chunk, half, me_arg, partner_c, rows_c, grads_c, router_wide, line, firsts, seconds
        )
        rows_all.append(rows_c)
        slopes.append(slo)
        active.append(act)
        gated.append(gat)
        gates.append(gte)
        if chunks == 1:
            gate_grad = line[:, 0].reshape(expert_count, chunk)
            pieces = []
            for _ in range(3):
                piece = gate_grad.astype(BF)
                pieces.append(piece)
                gate_grad = gate_grad - piece.astype(F32)
            gate_row = jnp.pad(jnp.concatenate(pieces, 1), ((0, 0), (0, width - 3 * half)))
            back = jnp.pad(back.reshape(expert_count, chunk, width), ((0, 0), (0, last_stride - chunk), (0, 0)))
            back = back.at[:, spare].set(gate_row)
        if c + 1 < chunks:
            back, arrived[c + 1] = together(back.reshape(expert_count, chunk, width), arrived[c + 1])
        else:
            back, rows_all[-1], backs = together(back, rows_all[-1], backs)
        backs.append(all_to_all(back))
    grads_cross = cross_weight_grads(rows_all, slopes, active, gated)
    gates, grads_cross = together(gates, grads_cross)
    grads_in = swap_core(grads_cross)
    results = expert_results(active, gates, seconds, expert_count)
    results, grads_in = together(results, grads_in)
    grads_far, grads_kept = kept_weight_grads(rows_all, slopes, active, gated, grads_in)
    backs[-1], results, grads_far = together(backs[-1], results, grads_far)

    across_y = swap_y(grads_far)
    results_own = all_to_all(results).reshape(expert_count * half, width)

    backs_far = [swap_core(b) for b in backs]
    residual_grad, mixed_grad, extra_early, output_sent, output_kept = combine(
        micro_arg, core_arg, length, info, out_grad, residual, mixed, gain_two, router_wide, output_own,
        backs + backs_far, half, spare,
    )

    dq, dk, dv, tiles, sums = attend_back(length, qkv, near, mixed, logs, mixed_grad, 0, head_total // 2)
    far_sent, own_parts, sent = attention_weight_grads(core_arg, normed_one, dq, dk, dv, output_sent, qkv_weight)
    far_got = swap_y(far_sent)
    sent, results_own = together(sent, results_own)
    got = swap_core(sent)
    rows_both, extra_late = both_rows(
        expert_count, micro_arg, core_arg, length, qkv_weight, (dq, dk, dv), got, layer_input, gain_one, residual_grad,
        info, residual, results_own, swap_core(results_own),
    )
    rows_both, across_y, tiles = together(rows_both, across_y, tiles)
    late_far = swap_core(extra_late)
    corner = micro * 2 + core
    corners = jnp.stack([corner, corner ^ 1, corner ^ 2, corner ^ 3]).astype(jnp.int32)
    rows_y = swap_y(rows_both)
    expert_in_grad, expert_out_grad = last_sums(grads_kept, across_y)
    rows_y, expert_in_grad, expert_out_grad = together(rows_y, expert_in_grad, expert_out_grad)
    layer_output, input_grad = place_pieces(corners, (rows_both, swap_core(rows_both), rows_y, swap_core(rows_y)))
    layer_output = layer_output.reshape(2, SEQ, width)
    input_grad = input_grad.reshape(2, SEQ, width)

    tiles = tiles.reshape(head_total, 2 * TILE * TILE)
    tiles_high = tiles.astype(BF)
    tiles_rest = (tiles - tiles_high.astype(F32)).astype(BF)
    table = dot(tiles_high, hot_const, NT) + dot(tiles_rest, hot_const, NT)
    far_sum = jnp.sum(sums[:, :, 0], axis=1) - jnp.sum(table[:, : NB - 1], axis=1)
    table = jnp.concatenate([table[:, : NB - 1], far_sum[:, None]], 1)
    table_own = jnp.concatenate([table[0:2], table[4:5]], 0)
    table_far = jnp.concatenate([table[2:4], table[5:6]], 0)
    table_cols = heads_here * NB // rows_here
    table_both = jnp.concatenate([table_own.reshape(rows_here, table_cols), table_far.reshape(rows_here, table_cols)], 1)
    base = expert_count + 2
    kept = base + 2 * table_cols
    table_tile = jnp.tile(jnp.pad(table_both, ((0, 0), (base, TILE - kept))), (dp_count, 1))

    grads = packed_sums(kept, own_parts, far_got, output_kept, extra_early, extra_late, late_far, table_tile)
    arrived_grads = all_to_all(grads.reshape(dp_count, rows_here, grads.shape[1]))
    arrived_grads, layer_output, input_grad = together(arrived_grads, layer_output, input_grad)
    query_grad, key_grad, value_grad, output_grad, small = final_sums(kept, arrived_grads, shard)
    small_y = swap_y(small)
    both = small + small_y
    table_sum = small[:, base : base + table_cols] + small_y[:, base + table_cols : kept]
    return (
        layer_output,
        input_grad,
        both[:, expert_count],
        query_grad,
        key_grad,
        value_grad,
        output_grad.T,
        table_sum.reshape(heads_here, NB),
        both[:, expert_count + 1],
        both[:, :expert_count],
        expert_in_grad[None],
        expert_out_grad[None],
    )


def solution(mesh):
    return jax.shard_map(
        local,
        mesh=mesh,
        in_specs=(
            P(None, "dp", None),
            P(None, "dp", None),
            P("dp"),
            P("dp", "tensor"),
            P("dp", "tensor"),
            P("dp", "tensor"),
            P("tensor", "dp"),
            P("tensor", None),
            P("dp"),
            P("dp", None),
            P("dp", None, "tensor"),
            P("dp", "tensor", None),
            P(None, "dp"),
            P(None, "dp", None),
        ),
        out_specs=(
            P(None, "dp", None),
            P(None, "dp", None),
            P("dp"),
            P("dp", "tensor"),
            P("dp", "tensor"),
            P("dp", "tensor"),
            P("tensor", "dp"),
            P("tensor", None),
            P("dp"),
            P("dp", None),
            P("dp", None, "tensor"),
            P("dp", "tensor", None),
        ),
        check_vma=False,
    )
```

```python
import functools

import jax
import jax.numpy as jnp
import numpy as np
from jax import lax
from jax.experimental import pallas as pl
from jax.experimental.pallas import tpu as pltpu
from jax.sharding import PartitionSpec as P

HEAD_DIM = 64
NB = 32
SEQ = 1024
TILE = 128
QROWS = 256
NEG = -1e30
GELU_C = 0.7978845608028654
GELU_A = 0.044715

BF = jnp.bfloat16
F32 = jnp.float32

bucket_edges = np.ceil(16.0 * 8.0 ** (np.arange(1, 16) / 16.0)).astype(np.int32)


def near_tables():
    rows = np.arange(TILE)[:, None]
    cols = np.arange(TILE)[None, :]
    hots = []
    for shift in (0, TILE):
        distance = rows - cols + shift
        clipped = np.maximum(distance, 0)
        reached = np.sum(clipped[..., None] >= bucket_edges, axis=-1)
        bucket = np.minimum(clipped, 16) + reached
        hots.append(bucket[..., None] == np.arange(NB))
    hot = np.stack(hots).reshape(2 * TILE * TILE, NB).T
    return hot


NEAR_HOT = near_tables()
assert bucket_edges[-1] <= TILE


def dot(a, b, dims=((1,), (0,))):
    return lax.dot_general(a, b, (dims, ((), ())), preferred_element_type=F32)


NT = ((1,), (1,))
TN = ((0,), (0,))


MIB = 2**20
SMALL_COST = pl.CostEstimate(flops=1_000_000, bytes_accessed=1_000_000, transcendentals=0)


STRIP = 32


def score_strip(s, at, block, j, start, near_ref, half, length):
    part = s[at : at + STRIP]
    near = slice(start % TILE, start % TILE + STRIP)
    if j == block:
        if start < TILE:
            left = part[:, :TILE] + near_ref[half, 0, near, :]
            right = jnp.full((STRIP, TILE), NEG, F32)
        else:
            left = part[:, :TILE] + near_ref[half, 1, near, :]
            right = part[:, TILE:] + near_ref[half, 0, near, :]
        part = jnp.concatenate([left, right], 1)
    elif j == block - 1 and start < TILE:
        part = jnp.concatenate([part[:, :TILE], part[:, TILE:] + near_ref[half, 1, near, :]], 1)
    if (j + 1) * QROWS > SEQ // 2:
        place = lax.broadcasted_iota(jnp.int32, (1, QROWS), 1) + j * QROWS
        part = part + jnp.where(place < length, 0.0, NEG)
    return part


def lane_half(rows):
    return lax.broadcasted_iota(jnp.int32, (rows, 2 * HEAD_DIM), 1) < HEAD_DIM


def attend_kernel(length_ref, query_ref, key_ref, value_ref, near_ref, out_ref, log_ref):
    length = length_ref[0]
    lanes = lane_half(QROWS)
    value_ext = jnp.concatenate([value_ref[...], jnp.ones((SEQ, TILE), BF)], 1)
    for i in range(SEQ // QROWS):
        q_rows = query_ref[i * QROWS : (i + 1) * QROWS, :] * BF(0.125)
        q_both = jnp.concatenate([jnp.where(lanes, q_rows, BF(0)), jnp.where(lanes, BF(0), q_rows)], 0)
        tiles = [dot(q_both, key_ref[j * QROWS : (j + 1) * QROWS, :], NT) for j in range(i + 1)]
        tops = []
        weights = [[] for _ in tiles]
        for h in range(2):
            for start in range(0, QROWS, STRIP):
                strips = [
                    score_strip(s, h * QROWS + start, i, j, start, near_ref, h, length) for j, s in enumerate(tiles)
                ]
                top = strips[0]
                for s in strips[1:]:
                    top = jnp.maximum(top, s)
                top = jnp.max(top, axis=1, keepdims=True)
                tops.append(top)
                for j, s in enumerate(strips):
                    weights[j].append(jnp.exp(s - top).astype(BF))
        total = None
        for j, strips in enumerate(weights):
            total = put(total, dot(jnp.concatenate(strips, 0), value_ext[j * QROWS : (j + 1) * QROWS, :]))
        row_sum = total[:, TILE:]
        out = total[:, :TILE] / row_sum
        logs = jnp.concatenate(tops, 0) + jnp.log(row_sum)
        out_ref[i * QROWS : (i + 1) * QROWS, :] = jnp.where(lanes, out[:QROWS], out[QROWS:]).astype(BF)
        log_ref[i * QROWS : (i + 1) * QROWS, :] = jnp.where(lanes, logs[:QROWS], logs[QROWS:])


def attend(length, qkv, near):
    pairs = qkv.shape[1] // (3 * TILE)
    cols = pairs * TILE
    return pl.pallas_call(
        attend_kernel,
        grid=(pairs,),
        in_specs=[
            pl.BlockSpec(memory_space=pltpu.SMEM),
            pl.BlockSpec((SEQ, TILE), lambda p: (0, p)),
            pl.BlockSpec((SEQ, TILE), lambda p: (0, pairs + p)),
            pl.BlockSpec((SEQ, TILE), lambda p: (0, 2 * pairs + p)),
            pl.BlockSpec((2, 2, TILE, TILE), lambda p: (p, 0, 0, 0)),
        ],
        out_specs=[
            pl.BlockSpec((SEQ, TILE), lambda p: (0, p)),
            pl.BlockSpec((SEQ, TILE), lambda p: (0, p)),
        ],
        out_shape=[
            jax.ShapeDtypeStruct((SEQ, cols), BF),
            jax.ShapeDtypeStruct((SEQ, cols), F32),
        ],
        compiler_params=pltpu.CompilerParams(vmem_limit_bytes=40 * MIB),
        cost_estimate=SMALL_COST,
        name="attend",
    )(length, qkv, qkv, qkv, near)


def attend_back_kernel(
    length_ref, query_ref, key_ref, value_ref, near_ref, out_ref, log_ref, grad_ref,
    dq_ref, dk_ref, dv_ref, tile_ref, sum_ref, dk_acc, dv_acc,
):
    length = length_ref[0]
    lanes = lane_half(QROWS)
    key_ext = jnp.concatenate([key_ref[...], jnp.ones((SEQ, TILE), BF)], 1)
    near_sums = [[None, None], [None, None]]
    all_sums = [None, None]

    def both(rows):
        return jnp.concatenate([jnp.where(lanes, rows, BF(0)), jnp.where(lanes, BF(0), rows)], 0)

    for i in range(SEQ // QROWS):
        rows = slice(i * QROWS, (i + 1) * QROWS)
        q_both = both(query_ref[rows, :] * BF(0.125))
        g_rows = grad_ref[rows, :]
        g_both = both(g_rows)
        mass = g_rows.astype(F32) * out_ref[rows, :].astype(F32)
        deltas = [
            jnp.sum(jnp.where(lanes, mass, 0.0), axis=1, keepdims=True),
            jnp.sum(jnp.where(lanes, 0.0, mass), axis=1, keepdims=True),
        ]
        logs = [log_ref[rows, h * HEAD_DIM : h * HEAD_DIM + 1] for h in range(2)]
        dq = None
        for j in range(i + 1):
            keys = slice(j * QROWS, (j + 1) * QROWS)
            s = dot(q_both, key_ref[keys, :], NT)
            dp = dot(g_both, value_ref[keys, :], NT)
            p_strips, d_strips = [], []
            for h in range(2):
                for start in range(0, QROWS, STRIP):
                    strip = slice(start, start + STRIP)
                    at = h * QROWS + start
                    p = jnp.exp(score_strip(s, at, i, j, start, near_ref, h, length) - logs[h][strip])
                    p_strips.append(p.astype(BF))
                    d_strips.append((p * (dp[at : at + STRIP] - deltas[h][strip])).astype(BF))
            p, ds = jnp.concatenate(p_strips, 0), jnp.concatenate(d_strips, 0)
            part = dot(ds, key_ext[keys, :])
            dq = put(dq, jnp.where(lanes, part[:QROWS, :TILE], part[QROWS:, :TILE]))
            for h in range(2):
                sums = part[h * QROWS : (h + 1) * QROWS, TILE:]
                all_sums[h] = put(all_sums[h], jnp.sum(sums.reshape(QROWS // 8, 8, TILE), axis=0))
            dk_part = dot(ds, q_both, TN)
            dv_part = dot(p, g_both, TN)
            if i == j:
                dk_acc[keys, :] = dk_part
                dv_acc[keys, :] = dv_part
            else:
                dk_acc[keys, :] += dk_part
                dv_acc[keys, :] += dv_part
            for h in range(2):
                mine = ds[h * QROWS : (h + 1) * QROWS]
                if j == i:
                    wide = mine.astype(F32)
                    near_sums[h][0] = put(near_sums[h][0], wide[:TILE, :TILE] + wide[TILE:, TILE:])
                    near_sums[h][1] = put(near_sums[h][1], wide[TILE:, :TILE])
                elif j == i - 1:
                    near_sums[h][1] = put(near_sums[h][1], mine[:TILE, TILE:].astype(F32))
        dq_ref[rows, :] = (dq * 0.125).astype(BF)
    dk_ref[...] = dk_acc[...].astype(BF)
    dv_ref[...] = dv_acc[...].astype(BF)
    for h in range(2):
        tile_ref[h, 0] = near_sums[h][0]
        tile_ref[h, 1] = near_sums[h][1]
        sum_ref[h] = all_sums[h]


def attend_back(length, qkv, near, mixed, logs, grad, first, count):
    pairs = qkv.shape[1] // (3 * TILE)
    cols = count * TILE
    col = pl.BlockSpec((SEQ, TILE), lambda p: (0, first + p))
    out = pl.BlockSpec((SEQ, TILE), lambda p: (0, p))
    return pl.pallas_call(
        attend_back_kernel,
        grid=(count,),
        in_specs=[
            pl.BlockSpec(memory_space=pltpu.SMEM),
            col,
            pl.BlockSpec((SEQ, TILE), lambda p: (0, pairs + first + p)),
            pl.BlockSpec((SEQ, TILE), lambda p: (0, 2 * pairs + first + p)),
            pl.BlockSpec((2, 2, TILE, TILE), lambda p: (first + p, 0, 0, 0)),
            col,
            col,
            col,
        ],
        out_specs=[
            out,
            out,
            out,
            pl.BlockSpec((2, 2, TILE, TILE), lambda p: (p, 0, 0, 0)),
            pl.BlockSpec((2, 8, TILE), lambda p: (p, 0, 0)),
        ],
        out_shape=[
            jax.ShapeDtypeStruct((SEQ, cols), BF),
            jax.ShapeDtypeStruct((SEQ, cols), BF),
            jax.ShapeDtypeStruct((SEQ, cols), BF),
            jax.ShapeDtypeStruct((2 * count, 2, TILE, TILE), F32),
            jax.ShapeDtypeStruct((2 * count, 8, TILE), F32),
        ],
        scratch_shapes=[pltpu.VMEM((SEQ, TILE), F32), pltpu.VMEM((SEQ, TILE), F32)],
        compiler_params=pltpu.CompilerParams(vmem_limit_bytes=40 * MIB),
        cost_estimate=SMALL_COST,
        name="attend_back",
    )(length, qkv, qkv, qkv, near, mixed, logs, grad)


def low_lanes(shape):
    return lax.broadcasted_iota(jnp.int32, shape, 1) < HEAD_DIM


def turned(tile):
    return pltpu.roll(tile, HEAD_DIM, 1)


def pack_kernel(q_ref, k_ref, v_ref, o_ref, one_ref, two_ref, router_ref, out_ref):
    shard = q_ref.shape[1]
    rows = q_ref.shape[0]
    source = lax.broadcasted_iota(jnp.int32, (shard, 6 * TILE), 0)
    target = lax.broadcasted_iota(jnp.int32, (shard, 6 * TILE), 1)

    def moved(pair_base, last_base):
        want = jnp.where(source < TILE, source + pair_base, source - TILE + last_base)
        return jnp.where(target == want, 1.0, 0.0).astype(BF)

    total = dot(v_ref[...], moved(0, 2 * TILE)) + dot(o_ref[...], moved(TILE, 2 * TILE + HEAD_DIM), TN)
    total = total + dot(q_ref[...], moved(3 * TILE, 5 * TILE)) + dot(k_ref[...], moved(4 * TILE, 5 * TILE + HEAD_DIM))
    out_ref[:, : 6 * TILE] = total.astype(BF)
    experts = router_ref.shape[0]
    own_row = lax.broadcasted_iota(jnp.int32, (rows, rows), 0) == lax.broadcasted_iota(jnp.int32, (rows, rows), 1)

    def column(ref):
        return jnp.sum(jnp.where(own_row, ref[...].astype(F32), 0.0), axis=1, keepdims=True)

    lanes = lax.broadcasted_iota(jnp.int32, (experts, TILE), 1)
    spread = jnp.where(lanes == lax.broadcasted_iota(jnp.int32, (experts, TILE), 0), 1.0, 0.0).astype(BF)
    place = lax.broadcasted_iota(jnp.int32, (rows, TILE), 1)
    small = dot(router_ref[...], spread, TN)
    small = jnp.where(place == experts, column(one_ref), jnp.where(place == experts + 1, column(two_ref), small))
    out_ref[:, 6 * TILE :] = small.astype(BF)


def pack_weights(query, key, value, output, one, two, router):
    rows = query.shape[0]
    return pl.pallas_call(
        pack_kernel,
        out_shape=jax.ShapeDtypeStruct((rows, 7 * TILE), BF),
        compiler_params=pltpu.CompilerParams(vmem_limit_bytes=60 * MIB),
        cost_estimate=SMALL_COST,
        name="pack_weights",
    )(query, key, value, output, one[None], two[None], router.T)


def qkv_kernel(micro_ref, tokens_ref, gain_ref, a_own, a_far, b_own, b_far, qkv_ref, normed_ref, weight_ref, output_ref):
    width = tokens_ref.shape[2]

    @pl.when(pl.program_id(0) == 0)
    def _():
        low = low_lanes((width, TILE))

        def tiles(own, far, pair, low_half):
            at = slice(pair * TILE, (pair + 1) * TILE)
            one, two = own[:, 2 * TILE :].astype(F32), far[:, 2 * TILE :].astype(F32)
            last = jnp.where(low, one, turned(two)) if low_half else jnp.where(low, turned(one), two)
            return own[:, at], far[:, at], last.astype(BF)

        for n, (own, far, pair, low_half) in enumerate(
            ((a_own, a_far, 0, True), (a_own, a_far, 1, False), (b_own, b_far, 0, True))
        ):
            for t, tile in enumerate(tiles(own[...], far[...], pair, low_half)):
                at = 3 * n + t
                weight_ref[:, at * TILE : (at + 1) * TILE] = tile
        for t, tile in enumerate(tiles(b_own[...], b_far[...], 1, False)):
            output_ref[:, t * TILE : (t + 1) * TILE] = tile

    x = tokens_ref[0].astype(F32)
    inverse = lax.rsqrt(jnp.mean(x * x, axis=-1, keepdims=True) + 1e-06)
    normed = (x * inverse * gain_ref[...]).astype(BF)
    normed_ref[...] = normed
    qkv_ref[...] = dot(normed, weight_ref[...]).astype(BF)


def norm_and_project(micro, layer_input, gain, a_own, a_far, b_own, b_far):
    width = layer_input.shape[2]
    block = 256
    cols = 3 * TILE
    whole = lambda rows, n: pl.BlockSpec((rows, n), lambda i, m: (0, 0))
    here = lambda n: pl.BlockSpec((block, n), lambda i, m: (i, 0))
    return pl.pallas_call(
        qkv_kernel,
        grid_spec=pltpu.PrefetchScalarGridSpec(
            num_scalar_prefetch=1,
            grid=(SEQ // block,),
            in_specs=[pl.BlockSpec((1, block, width), lambda i, m: (m[0], i, 0)), whole(1, width)] + [whole(width, cols)] * 4,
            out_specs=[here(3 * cols), here(width), whole(width, 3 * cols), whole(width, cols)],
        ),
        out_shape=[
            jax.ShapeDtypeStruct((SEQ, 3 * cols), BF),
            jax.ShapeDtypeStruct((SEQ, width), BF),
            jax.ShapeDtypeStruct((width, 3 * cols), BF),
            jax.ShapeDtypeStruct((width, cols), BF),
        ],
        compiler_params=pltpu.CompilerParams(vmem_limit_bytes=40 * MIB),
        cost_estimate=SMALL_COST,
        name="norm_and_project",
    )(micro, layer_input, gain, a_own, a_far, b_own, b_far)


def middle_kernel(
    blocks, per, micro_ref, tokens_ref, mixed_ref, other_ref, own_ref, far_ref, gain_ref, code_ref, residual_ref, *refs
):
    sent_refs, normed = refs[:-1], refs[-1]
    step = pl.program_id(0)
    rows = tokens_ref.shape[1]

    @pl.when(step < blocks)
    def _():
        total = tokens_ref[0].astype(F32) + dot(mixed_ref[...], own_ref[...], NT) + dot(other_ref[...], far_ref[...], NT)
        residual_ref[...] = total
        inverse = lax.rsqrt(jnp.mean(total * total, axis=-1, keepdims=True) + 1e-06)
        normed[pl.ds(pl.multiple_of(step * rows, rows), rows), :] = (total * inverse * gain_ref[...]).astype(BF)

    for c, sent_ref in enumerate(sent_refs):

        @pl.when((step >= blocks + c * per) & (step < blocks + (c + 1) * per))
        def _(sent_ref=sent_ref):
            block = sent_ref.shape[0]
            ids = lax.broadcasted_iota(jnp.int32, (block, 1), 0) + (step - blocks) * block
            hot = jnp.where((ids == code_ref[:1]) | (ids == code_ref[1:2]), 1.0, 0.0).astype(BF)
            sent_ref[...] = dot(hot, normed[...]).astype(BF)


def residual_and_rows(micro, layer_input, mixed, other, output_own, output_far, gain, code, count, chunks):
    width = layer_input.shape[2]
    block = 256
    blocks = SEQ // block
    send = 320
    cols = mixed.shape[1]
    per = count // send
    at = lambda i: jnp.minimum(i, blocks - 1)
    whole = lambda arr: pl.BlockSpec(arr.shape, lambda i, m: (0, 0))
    here = lambda n: pl.BlockSpec((block, n), lambda i, m: (at(i), 0))

    def sent(c):
        return pl.BlockSpec((send, width), lambda i, m: (jnp.clip(i - blocks - c * per, 0, per - 1), 0))

    return pl.pallas_call(
        functools.partial(middle_kernel, blocks, per),
        grid_spec=pltpu.PrefetchScalarGridSpec(
            num_scalar_prefetch=1,
            grid=(blocks + chunks * per,),
            in_specs=[
                pl.BlockSpec((1, block, width), lambda i, m: (m[0], at(i), 0)),
                here(cols), here(cols), whole(output_own), whole(output_far), whole(gain), whole(code),
            ],
            out_specs=[here(width)] + [sent(c) for c in range(chunks)],
            scratch_shapes=[pltpu.VMEM((SEQ, width), BF)],
        ),
        out_shape=[jax.ShapeDtypeStruct((SEQ, width), F32)] + [jax.ShapeDtypeStruct((count, width), BF)] * chunks,
        compiler_params=pltpu.CompilerParams(vmem_limit_bytes=40 * MIB),
        cost_estimate=SMALL_COST,
        name="residual_and_rows",
    )(micro, layer_input, mixed, other, output_own, output_far, gain, code)


def picked_rows(first, second, segments):
    total = None
    start = 0
    for rows in segments:
        length = rows.shape[0]
        ids = lax.broadcasted_iota(jnp.int32, (1, length), 1) + start
        hot = []
        for at in range(0, first.shape[0], STRIP):
            one, two = first[at : at + STRIP], second[at : at + STRIP]
            hot.append(jnp.where((one == ids) | (two == ids), 1.0, 0.0).astype(BF))
        total = put(total, dot(jnp.concatenate(hot, 0), rows))
        start += length
    return total


def put(a, b):
    return b if a is None else a + b


def folded(product):
    return jnp.sum(product.reshape(product.shape[0] // 8, 8, product.shape[1]), axis=0)


def as_column(eight):
    ones = jnp.ones((16, TILE), BF)
    high = eight.astype(BF)
    rest = (eight - high.astype(F32)).astype(BF)
    return dot(jnp.concatenate([high, rest], 0), ones, TN)


def combine_kernel(experts, half, spare, micro_ref, core_ref, length_ref, *refs):
    info_ref, grad_ref, residual_ref, mixed_ref, gain_ref, router_ref, output_ref = refs[:7]
    backs = refs[7:-9]
    (total_ref, mixed_grad_ref, extra_ref, far_ref, own_ref, acc_ref, router_acc, gain_acc, tables) = refs[-9:]
    block = residual_ref.shape[0]
    step = pl.program_id(0)
    count = len(backs) // 2

    @pl.when(step == 0)
    def _():
        place = lax.broadcasted_iota(jnp.int32, (experts, 1), 0)
        for n, back in enumerate((backs[count - 1], backs[2 * count - 1])):
            table = jnp.zeros((experts, back.shape[2]), F32)
            for e in range(experts):
                row = back[e, spare : spare + 16, :].astype(F32)[:1]
                table = jnp.where(place == e, row, table)
            for piece in range(3):
                at = (3 * n + piece) * experts
                tables[at : at + experts] = table[:, piece * half : (piece + 1) * half]

    info = jnp.transpose(info_ref[...])
    number = lambda n: info[:, n : n + 1]
    columns = lax.broadcasted_iota(jnp.int32, (1, half), 1)
    lanes = lax.broadcasted_iota(jnp.int32, (1, 6 * experts), 1)
    table = tables[...].astype(BF)
    values = []
    for k in range(2):
        slot = number(4 + k)
        hot = jnp.where(columns == lax.rem(slot, half), 1.0, 0.0).astype(BF)
        found = dot(hot, table, NT)
        wanted = jnp.where(slot // half == core_ref[0], 0, 3 * experts) + number(2 + k)
        away = lanes - wanted
        hit = (away == 0) | (away == experts) | (away == 2 * experts)
        values.append(jnp.sum(jnp.where(hit, found, 0.0), axis=1, keepdims=True))
    wide = lax.broadcasted_iota(jnp.int32, (1, TILE), 1)
    is_first, is_second = wide == number(2), wide == number(3)
    residual = residual_ref[...]
    gain = gain_ref[...]
    inverse = lax.rsqrt(jnp.mean(residual * residual, axis=-1, keepdims=True) + 1e-06)
    plain = residual * inverse
    normed = (plain * gain).astype(BF)
    logits = dot(normed, router_ref[...])
    gap = jnp.sum(jnp.where(is_first, logits, 0.0) - jnp.where(is_second, logits, 0.0), axis=1, keepdims=True)
    small = jnp.exp(-jnp.abs(gap))
    logit = small / ((1.0 + small) * (1.0 + small)) * (values[0] - values[1])
    logit_grad = jnp.where(is_first, logit, jnp.where(is_second, -logit, 0.0)).astype(BF)
    segments = [b[...].reshape(b.shape[0] * b.shape[1], b.shape[2]) for b in backs]
    normed_grad = picked_rows(number(0), number(1), segments) + dot(logit_grad, router_ref[...], NT)
    scaled = normed_grad * gain
    mean = jnp.mean(scaled * plain, axis=-1, keepdims=True)
    place = lax.broadcasted_iota(jnp.int32, (block, 1), 0) + step * block
    grad_out = jnp.where(place < length_ref[0], grad_ref[0].astype(F32), 0.0)
    total = grad_out + inverse * (scaled - plain * mean)
    total_ref[...] = total
    branch = total.astype(BF)
    mixed_grad_ref[...] = dot(branch, output_ref[...]).astype(BF)
    router_part = dot(logit_grad, normed, TN)
    gain_part = folded(normed_grad * plain)
    output_part = dot(mixed_ref[...], branch, TN)

    @pl.when(step == 0)
    def _():
        router_acc[...] = router_part
        gain_acc[...] = gain_part
        acc_ref[...] = output_part

    @pl.when(step > 0)
    def _():
        router_acc[...] += router_part
        gain_acc[...] += gain_part
        acc_ref[...] += output_part

    @pl.when(step == pl.num_programs(0) - 1)
    def _():
        extra_ref[...] = jnp.transpose(router_acc[...]) + jnp.where(wide == experts + 1, as_column(gain_acc[...]), 0.0)
        parts = jnp.transpose(acc_ref[...])
        far_ref[...] = parts[:, TILE:].astype(BF)
        own_ref[:, :TILE] = parts[:, :TILE]
        own_ref[:, TILE:] = parts[:, 2 * TILE :]


def combine(micro, core, length, info, out_grad, residual, mixed, gain, router, output_own, backs, half, spare):
    width = residual.shape[1]
    block = 512
    cols = mixed.shape[1]
    whole = lambda arr: pl.BlockSpec(arr.shape, lambda i, *_: (0,) * arr.ndim)
    fixed = lambda rows, n: pl.BlockSpec((rows, n), lambda i, *_: (0, 0))
    here = lambda n: pl.BlockSpec((block, n), lambda i, *_: (i, 0))
    experts = backs[0].shape[0]
    return pl.pallas_call(
        functools.partial(combine_kernel, experts, half, spare),
        grid_spec=pltpu.PrefetchScalarGridSpec(
            num_scalar_prefetch=3,
            grid=(SEQ // block,),
            in_specs=[
                pl.BlockSpec((8, block), lambda i, *_: (0, i)),
                pl.BlockSpec((1, block, width), lambda i, m, *_: (m[0], i, 0)),
                here(width), here(cols), whole(gain), whole(router), whole(output_own),
            ]
            + [whole(x) for x in backs],
            out_specs=[here(width), here(cols), fixed(width, TILE), fixed(width, 2 * TILE), fixed(width, 2 * TILE)],
            scratch_shapes=[
                pltpu.VMEM((cols, width), F32),
                pltpu.VMEM((TILE, width), F32),
                pltpu.VMEM((8, width), F32),
                pltpu.VMEM((6 * experts, half), F32),
            ],
        ),
        out_shape=[
            jax.ShapeDtypeStruct((SEQ, width), F32),
            jax.ShapeDtypeStruct((SEQ, cols), BF),
            jax.ShapeDtypeStruct((width, TILE), F32),
            jax.ShapeDtypeStruct((width, 2 * TILE), BF),
            jax.ShapeDtypeStruct((width, 2 * TILE), F32),
        ],
        compiler_params=pltpu.CompilerParams(vmem_limit_bytes=40 * MIB),
        cost_estimate=SMALL_COST,
        name="combine",
    )(micro, core, length, info, out_grad, residual, mixed, gain, router, output_own, *backs)


def projected_back(weight_ref, grads):
    total = None
    for n, grad in enumerate(grads):
        cols = grad.shape[1]
        total = put(total, dot(grad[...], weight_ref[:, n * cols : (n + 1) * cols], NT))
    return total


def attention_weight_kernel(
    blocks, core_ref, normed_ref, q_ref, k_ref, v_ref, output_ref, weight_ref, q_rows, k_rows, v_rows, far_ref, own_ref, sent_ref
):
    step = pl.program_id(0)

    @pl.when(step < blocks)
    def _():
        low = low_lanes((normed_ref.shape[1], TILE))
        q, k, v = (dot(normed_ref[...], d[...], TN) for d in (q_ref, k_ref, v_ref))
        for n, part in enumerate((q, k, v)):
            own_ref[:, n * TILE : (n + 1) * TILE] = part[:, :TILE]
            far_ref[:, n * TILE : (n + 1) * TILE] = part[:, TILE : 2 * TILE].astype(BF)
        q, k, v = (part[:, 2 * TILE :] for part in (q, k, v))
        far_ref[:, 3 * TILE : 4 * TILE] = jnp.where(low, turned(q), k).astype(BF)
        far_ref[:, 4 * TILE : 5 * TILE] = jnp.where(low, turned(v), output_ref[:, TILE:].astype(F32)).astype(BF)
        far_ref[:, 5 * TILE :] = output_ref[:, :TILE]
        own_ref[:, 3 * TILE : 4 * TILE] = jnp.where(low, q, turned(k))
        own_ref[:, 4 * TILE :] = jnp.where(low, v, 0.0)

    @pl.when(step >= blocks)
    def _():
        sent_ref[...] = projected_back(weight_ref, (q_rows, k_rows, v_rows))


def attention_weight_grads(core, normed, q, k, v, output, weight):
    width = normed.shape[1]
    block = 256
    blocks = width // block
    at = lambda i: jnp.minimum(i, blocks - 1)
    later = lambda i: jnp.maximum(i, blocks) - blocks
    whole = lambda arr: pl.BlockSpec(arr.shape, lambda i, c: (0, 0))
    here = lambda n: pl.BlockSpec((block, n), lambda i, c: (at(i), 0))
    rows = pl.BlockSpec((block, q.shape[1]), lambda i, c: ((1 - c[0]) * 2 + later(i), 0))
    return pl.pallas_call(
        functools.partial(attention_weight_kernel, blocks),
        grid_spec=pltpu.PrefetchScalarGridSpec(
            num_scalar_prefetch=1,
            grid=(blocks + 2,),
            in_specs=[
                pl.BlockSpec((SEQ, block), lambda i, c: (0, at(i))),
                whole(q), whole(k), whole(v), here(2 * TILE), whole(weight), rows, rows, rows,
            ],
            out_specs=[here(6 * TILE), here(5 * TILE), pl.BlockSpec((block, width), lambda i, c: (later(i), 0))],
        ),
        out_shape=[
            jax.ShapeDtypeStruct((width, 6 * TILE), BF),
            jax.ShapeDtypeStruct((width, 5 * TILE), F32),
            jax.ShapeDtypeStruct((2 * block, width), F32),
        ],
        compiler_params=pltpu.CompilerParams(vmem_limit_bytes=40 * MIB),
        cost_estimate=SMALL_COST,
        name="attention_weight_grads",
    )(core, normed, q, k, v, output, weight, q, k, v)


def both_kernel(
    lane, micro_ref, core_ref, length_ref, weight_ref, q, k, v, got_ref, tokens_ref, gain_ref, grad_ref,
    info_ref, residual_ref, own_ref, far_ref, out_ref, extra_ref, acc_ref,
):
    block = residual_ref.shape[0]
    info = jnp.transpose(info_ref[...])
    place = lax.broadcasted_iota(jnp.int32, (block, 1), 0) + (core_ref[0] * 2 + pl.program_id(0)) * block
    rows = residual_ref[...] + picked_rows(info[:, 6:7], info[:, 7:8], (own_ref[...], far_ref[...]))
    out_ref[0] = jnp.where(place < length_ref[0], rows, 0.0).astype(BF)
    normed_grad = got_ref[...] + projected_back(weight_ref, (q, k, v))
    x = tokens_ref[0].astype(F32)
    inverse = lax.rsqrt(jnp.mean(x * x, axis=-1, keepdims=True) + 1e-06)
    plain = x * inverse
    scaled = normed_grad * gain_ref[...]
    mean = jnp.mean(scaled * plain, axis=-1, keepdims=True)
    out_ref[1] = (grad_ref[...] + inverse * (scaled - plain * mean)).astype(BF)
    wide = lax.broadcasted_iota(jnp.int32, (1, TILE), 1)
    part = folded(normed_grad * plain)

    @pl.when(pl.program_id(0) == 0)
    def _():
        acc_ref[...] = part

    @pl.when(pl.program_id(0) == 1)
    def _():
        extra_ref[...] = jnp.where(wide == lane, as_column(acc_ref[...] + part), 0.0)


def both_rows(lane, micro, core, length, weight, grads, got, layer_input, gain, residual_grad, info, residual, own, far):
    width = weight.shape[0]
    block = 256
    here = lambda n: pl.BlockSpec((block, n), lambda i, m, c, *_: (c[0] * 2 + i, 0))
    whole = lambda arr: pl.BlockSpec(arr.shape, lambda i, *_: (0, 0))
    return pl.pallas_call(
        functools.partial(both_kernel, lane),
        grid_spec=pltpu.PrefetchScalarGridSpec(
            num_scalar_prefetch=3,
            grid=(2,),
            in_specs=[whole(weight)]
            + [here(grads[0].shape[1])] * 3
            + [
                pl.BlockSpec((block, width), lambda i, *_: (i, 0)),
                pl.BlockSpec((1, block, width), lambda i, m, c, *_: (m[0], c[0] * 2 + i, 0)),
                whole(gain),
                here(width),
                pl.BlockSpec((8, block), lambda i, m, c, *_: (0, c[0] * 2 + i)),
                here(width),
                whole(own),
                whole(far),
            ],
            out_specs=[
                pl.BlockSpec((2, block, width), lambda i, *_: (0, i, 0)),
                pl.BlockSpec((width, TILE), lambda i, *_: (0, 0)),
            ],
            scratch_shapes=[pltpu.VMEM((8, width), F32)],
        ),
        out_shape=[jax.ShapeDtypeStruct((2, 2 * block, width), BF), jax.ShapeDtypeStruct((width, TILE), F32)],
        compiler_params=pltpu.CompilerParams(vmem_limit_bytes=40 * MIB),
        cost_estimate=SMALL_COST,
        name="both_rows",
    )(micro, core, length, weight, *grads, got, layer_input, gain, residual_grad, info, residual, own, far)


def sum_kernel(kept, own, got, out_own, early, late, late_far, table, sum_ref):
    low = low_lanes(early.shape)
    sum_ref[:, : 4 * TILE] = (own[:, : 4 * TILE] + got[:, : 4 * TILE].astype(F32)).astype(BF)
    mixed = jnp.where(low, own[:, 4 * TILE :], turned(out_own[:, TILE:]))
    sum_ref[:, 4 * TILE : 5 * TILE] = (mixed + got[:, 4 * TILE : 5 * TILE].astype(F32)).astype(BF)
    sum_ref[:, 5 * TILE : 6 * TILE] = (out_own[:, :TILE] + got[:, 5 * TILE :].astype(F32)).astype(BF)
    extra = early[...] + late[...] + late_far[...] + table[...]
    high = extra.astype(BF)
    rest = extra - high.astype(F32)
    if kept <= HEAD_DIM:
        sum_ref[:, 6 * TILE :] = jnp.where(low, high.astype(F32), turned(rest)).astype(BF)
    else:
        sum_ref[:, 6 * TILE : 7 * TILE] = high
        sum_ref[:, 7 * TILE :] = rest.astype(BF)


def packed_sums(kept, *parts):
    width = parts[0].shape[0]
    cols = (7 if kept <= HEAD_DIM else 8) * TILE
    block = 256
    here = lambda n: pl.BlockSpec((block, n), lambda i: (i, 0))
    return pl.pallas_call(
        functools.partial(sum_kernel, kept),
        grid=(width // block,),
        in_specs=[here(x.shape[1]) for x in parts],
        out_specs=here(cols),
        out_shape=jax.ShapeDtypeStruct((width, cols), BF),
        compiler_params=pltpu.CompilerParams(vmem_limit_bytes=40 * MIB),
        cost_estimate=SMALL_COST,
        name="packed_sums",
    )(*parts)


def final_kernel(kept, parts_ref, q_ref, k_ref, v_ref, o_ref, small_ref):
    total = parts_ref[0].astype(F32)
    for n in range(1, parts_ref.shape[0]):
        total = total + parts_ref[n].astype(F32)
    tile = lambda t: total[:, t * TILE : (t + 1) * TILE]
    q_ref[:, :TILE] = tile(0)
    q_ref[:, TILE:] = tile(3)[:, :HEAD_DIM]
    k_ref[:, :TILE] = tile(1)
    k_ref[:, TILE:] = turned(tile(3))[:, :HEAD_DIM]
    v_ref[:, :TILE] = tile(2)
    v_ref[:, TILE:] = tile(4)[:, :HEAD_DIM]
    o_ref[:, :TILE] = tile(5)
    o_ref[:, TILE:] = turned(tile(4))[:, :HEAD_DIM]
    small_ref[...] = tile(6) + (turned(tile(6)) if kept <= HEAD_DIM else tile(7))


def final_sums(kept, parts, shard):
    rows = parts.shape[1]
    return pl.pallas_call(
        functools.partial(final_kernel, kept),
        out_shape=[jax.ShapeDtypeStruct((rows, shard), F32)] * 4 + [jax.ShapeDtypeStruct((rows, TILE), F32)],
        compiler_params=pltpu.CompilerParams(vmem_limit_bytes=40 * MIB),
        cost_estimate=SMALL_COST,
        name="final_sums",
    )(parts)


def pair_gate(logits, own, other):
    lanes = lax.broadcasted_iota(jnp.int32, logits.shape, 1)
    gap = jnp.sum(
        jnp.where(lanes == own, logits, 0.0) - jnp.where(lanes == other, logits, 0.0), axis=1, keepdims=True
    )
    small = jnp.exp(-jnp.abs(gap))
    return jnp.where(gap >= 0.0, 1.0, small) / (1.0 + small)


def expert_kernel(lead, chunk, half, me_ref, partner_ref, rows_ref, grads_ref, router_ref, *refs):
    before, refs = (refs[0], refs[1:]) if lead is not None and lead > 0 else (None, refs)
    firsts, seconds = refs[:4], refs[4:8]
    back_ref, active_ref, slope_ref, gated_ref, gate_ref, mass_ref = refs[8:]
    rows = rows_ref[...]
    grads = grads_ref[...]
    partner = jnp.transpose(jnp.broadcast_to(partner_ref[0], (8, rows.shape[0])))[:, :1]
    gate = pair_gate(dot(rows, router_ref[...]), me_ref[0], partner)
    gated_ref[...] = (gate * grads.astype(F32)).astype(BF)
    gate_ref[...] = jnp.broadcast_to(gate, gate_ref.shape)
    masses = [None] * (rows.shape[0] // STRIP)
    back = None
    width = firsts[0].shape[1]
    step = 256
    places = [(r, c) for r in range(4) for c in range(0, width, step)]

    def products(r, c):
        return dot(rows, firsts[r][:, c : c + step]), dot(grads, seconds[r][c : c + step, :], NT)

    ahead = products(*places[0])
    for n, (r, c) in enumerate(places):
        x, plain = ahead
        if n + 1 < len(places):
            ahead = products(*places[n + 1])
        place = slice(r * width + c, r * width + c + step)
        for at in range(0, rows.shape[0], STRIP):
            strip = slice(at, at + STRIP)
            value, flow = x[strip], plain[strip]
            square = value * value
            bent = jnp.tanh(value * (GELU_C + (GELU_C * GELU_A) * square))
            rise = 0.5 + 0.5 * bent
            active = value * rise
            slope = rise + active * (1.0 - bent) * (GELU_C + (3.0 * GELU_C * GELU_A) * square)
            low = active.astype(BF)
            active_ref[strip, place] = low
            slope_ref[strip, place] = (gate[strip] * flow * slope).astype(BF)
            part = low.astype(F32) * flow
            masses[at // STRIP] = put(masses[at // STRIP], part[:, :TILE] + part[:, TILE:])
        if c + step == width and r > 0:
            back = put(back, dot(slope_ref[:, (r - 1) * width : r * width], firsts[r - 1][...], NT))
    back = put(back, dot(slope_ref[:, 3 * width :], firsts[3][...], NT))
    back = back.astype(BF)
    mass = jnp.sum(jnp.concatenate(masses, 0), axis=1, keepdims=True)
    if lead is None:
        back_ref[...] = back
        mass_ref[...] = jnp.broadcast_to(mass, mass_ref.shape)
        return
    count = rows.shape[0] // chunk
    number = lax.broadcasted_iota(jnp.int32, (rows.shape[0], 1), 0)
    lanes = lax.broadcasted_iota(jnp.int32, (1, rows.shape[1]), 1)
    inside = lax.rem(number, chunk)
    spread = jnp.zeros(rows.shape, F32)
    for piece in range(3):
        high = mass.astype(BF).astype(F32)
        spread = jnp.where(lanes == piece * half + lead + inside, high, spread)
        mass = mass - high
    own = jnp.where(number // chunk == lax.broadcasted_iota(jnp.int32, (1, TILE), 1), 1.0, 0.0).astype(BF)
    line = dot(own, spread.astype(BF), TN)
    if before is None:
        back_ref[...] = back
        for e in range(count):
            mass_ref[e] = line[e : e + 1].astype(BF)
    else:
        back_ref[:, :chunk] = back.reshape(count, chunk, back.shape[1])
        row = lax.broadcasted_iota(jnp.int32, (16, 1), 0)
        for e in range(count):
            both = line[e : e + 1] + before[e].astype(F32)
            back_ref[e, chunk:] = jnp.where(row == 0, both, 0.0).astype(BF)


def row_block(total):
    return 320 if total % 320 == 0 else total


def expert_rows_pass(lead, chunk, half, me, partner, rows, grads, router, before, firsts, seconds):
    total, width = rows.shape
    block = row_block(total)
    experts = total // chunk
    hidden = sum(f.shape[1] for f in firsts)
    here = lambda cols: pl.BlockSpec((block, cols), lambda i: (i, 0))
    whole = lambda arr: pl.BlockSpec(arr.shape, lambda i: (0, 0))
    lines = pl.BlockSpec((block // chunk, 1, width), lambda i: (i, 0, 0))
    back_shape, back_spec = (total, width), here(width)
    mass_shape, mass_spec, mass_kind = (experts, 1, width), lines, BF
    if lead is None:
        mass_shape, mass_spec, mass_kind = (total, TILE), here(TILE), F32
    elif before is not None:
        back_shape = (experts, chunk + 16, width)
        back_spec = pl.BlockSpec((block // chunk, chunk + 16, width), lambda i: (i, 0, 0))
    return pl.pallas_call(
        functools.partial(expert_kernel, lead, chunk, half),
        grid=(total // block,),
        in_specs=[
            pl.BlockSpec(memory_space=pltpu.SMEM), pl.BlockSpec((1, 1, block), lambda i: (i, 0, 0)), here(width), here(width), whole(router),
        ]
        + ([lines] if before is not None else [])
        + [whole(w) for w in firsts]
        + [whole(w) for w in seconds],
        out_specs=[back_spec, here(hidden), here(hidden), here(width), here(TILE), mass_spec],
        out_shape=[
            jax.ShapeDtypeStruct(back_shape, BF),
            jax.ShapeDtypeStruct((total, hidden), BF),
            jax.ShapeDtypeStruct((total, hidden), BF),
            jax.ShapeDtypeStruct((total, width), BF),
            jax.ShapeDtypeStruct((total, TILE), F32),
            jax.ShapeDtypeStruct(mass_shape, mass_kind),
        ],
        compiler_params=pltpu.CompilerParams(vmem_limit_bytes=56 * MIB),
        cost_estimate=SMALL_COST,
        name="expert_rows",
    )(me, partner.reshape(total // block, 1, block), rows, grads, router, *([before] if before is not None else []), *firsts, *seconds)


def weight_parts(count, refs):
    rows, slopes, active, gated = (refs[n * count : (n + 1) * count] for n in range(4))
    first, second = None, None
    for n in range(count):
        first = put(first, dot(rows[n][...], slopes[n][...], TN))
        second = put(second, dot(active[n][...], gated[n][...], TN))
    return first, second


def cross_kernel(count, *refs):
    first, second = weight_parts(count, refs)
    refs[-1][0, 0] = first.astype(BF)
    refs[-1][0, 1] = second.astype(BF)


def kept_kernel(count, *refs):
    got_ref, far_ref, kept_ref = refs[-3:]
    first, second = weight_parts(count, refs)
    first = first + got_ref[0, 0].astype(F32)
    second = second + got_ref[0, 1].astype(F32)

    @pl.when(pl.program_id(0) == 0)
    def _():
        far_ref[0] = first.astype(BF)
        far_ref[1] = second.astype(BF)

    @pl.when(pl.program_id(0) == 1)
    def _():
        kept_ref[0] = first
        kept_ref[1] = second


def weight_specs(rows, slopes, quarter):
    total, width = rows[0].shape
    hidden = slopes[0].shape[1] // 4
    whole = pl.BlockSpec((total, width), lambda i: (0, 0))
    part = pl.BlockSpec((total, hidden), lambda i: (0, quarter(i)))
    count = len(rows)
    return width, hidden, [whole] * count + [part] * (2 * count) + [whole] * count


def cross_weight_grads(rows, slopes, active, gated):
    width, hidden, specs = weight_specs(rows, slopes, lambda i: 2 + i)
    return pl.pallas_call(
        functools.partial(cross_kernel, len(rows)),
        grid=(2,),
        in_specs=specs,
        out_specs=pl.BlockSpec((1, 2, width, hidden), lambda i: (i, 0, 0, 0)),
        out_shape=jax.ShapeDtypeStruct((2, 2, width, hidden), BF),
        compiler_params=pltpu.CompilerParams(vmem_limit_bytes=56 * MIB),
        cost_estimate=SMALL_COST,
        name="cross_weight_grads",
    )(*rows, *slopes, *active, *gated)


def kept_weight_grads(rows, slopes, active, gated, got):
    width, hidden, specs = weight_specs(rows, slopes, lambda i: 1 - i)
    fixed = pl.BlockSpec((2, width, hidden), lambda i: (0, 0, 0))
    return pl.pallas_call(
        functools.partial(kept_kernel, len(rows)),
        grid=(2,),
        in_specs=specs + [pl.BlockSpec((1, 2, width, hidden), lambda i: (1 - i, 0, 0, 0))],
        out_specs=[fixed, fixed],
        out_shape=[
            jax.ShapeDtypeStruct((2, width, hidden), BF),
            jax.ShapeDtypeStruct((2, width, hidden), F32),
        ],
        compiler_params=pltpu.CompilerParams(vmem_limit_bytes=56 * MIB),
        cost_estimate=SMALL_COST,
        name="kept_weight_grads",
    )(*rows, *slopes, *active, *gated, got)


def result_kernel(active_ref, gate_ref, b0, b1, b2, b3, *refs):
    out_ref = refs[-1]
    width = b0.shape[0]
    total = None
    for r, second in enumerate((b0, b1, b2, b3)):
        total = put(total, dot(active_ref[:, r * width : (r + 1) * width], second[...]))
    rows = (total * gate_ref[:, :1]).astype(BF)
    if len(out_ref.shape) > 2:
        out_ref[:, 0] = rows.reshape(out_ref.shape[0], out_ref.shape[2], out_ref.shape[3])
    else:
        out_ref[...] = rows


def expert_results(c, chunks, active, gates, seconds, experts, before):
    total, hidden = active.shape
    width = seconds[0].shape[1]
    block = row_block(total)
    here = lambda cols: pl.BlockSpec((block, cols), lambda i: (i, 0))
    chunk = total // experts
    if chunks > 1:
        shape = (experts, chunks, chunk, width)
        out_spec = pl.BlockSpec((block // chunk, 1, chunk, width), lambda i: (i, c, 0, 0))
    else:
        shape = (total, width)
        out_spec = here(width)
    more = [] if before is None else [before]
    return pl.pallas_call(
        result_kernel,
        grid=(total // block,),
        in_specs=[here(hidden), here(TILE)]
        + [pl.BlockSpec(w.shape, lambda i: (0, 0)) for w in seconds]
        + [pl.BlockSpec(memory_space=pl.ANY)] * len(more),
        out_specs=out_spec,
        out_shape=jax.ShapeDtypeStruct(shape, BF),
        input_output_aliases={6: 0} if more else {},
        compiler_params=pltpu.CompilerParams(vmem_limit_bytes=56 * MIB),
        cost_estimate=SMALL_COST,
        name="expert_results",
    )(active, gates, *seconds, *more)


def last_sum_kernel(kept_ref, y_ref, out_first, out_second):
    for n, out in enumerate((out_first, out_second)):
        out[...] = kept_ref[n] + y_ref[n].astype(F32)


def last_sums(kept, got_y):
    _, width, hidden = kept.shape
    block = 256
    here = pl.BlockSpec((block, hidden), lambda i: (i, 0))
    part = pl.BlockSpec((2, block, hidden), lambda i: (0, i, 0))
    return pl.pallas_call(
        last_sum_kernel,
        grid=(width // block,),
        in_specs=[part, part],
        out_specs=[here, here],
        out_shape=[jax.ShapeDtypeStruct((width, hidden), F32)] * 2,
        compiler_params=pltpu.CompilerParams(vmem_limit_bytes=40 * MIB),
        cost_estimate=SMALL_COST,
        name="last_sums",
    )(kept, got_y)


def send_kernel(micro_ref, code_ref, rows_ref, out_ref):
    block = out_ref.shape[0]
    ids = lax.broadcasted_iota(jnp.int32, (block, 1), 0) + pl.program_id(0) * block
    hot = jnp.where((ids == code_ref[:1]) | (ids == code_ref[1:2]), 1.0, 0.0).astype(BF)
    out_ref[...] = dot(hot, rows_ref[0]).astype(BF)


def send_rows(micro, code, rows, count):
    width = rows.shape[2]
    block = next(b for b in (336, 320, 384, count) if count % b == 0)
    return pl.pallas_call(
        send_kernel,
        grid_spec=pltpu.PrefetchScalarGridSpec(
            num_scalar_prefetch=1,
            grid=(count // block,),
            in_specs=[
                pl.BlockSpec(code.shape, lambda i, m: (0, 0)),
                pl.BlockSpec((1, SEQ, width), lambda i, m: (m[0], 0, 0)),
            ],
            out_specs=pl.BlockSpec((block, width), lambda i, m: (i, 0)),
        ),
        out_shape=jax.ShapeDtypeStruct((count, width), BF),
        compiler_params=pltpu.CompilerParams(vmem_limit_bytes=40 * MIB),
        cost_estimate=SMALL_COST,
        name="send_rows",
    )(micro, code, rows)


def place_kernel(place_ref, *refs):
    for n, piece in enumerate(refs[:4]):

        @pl.when(pl.program_id(0) == n)
        def _(piece=piece):
            for k, out_ref in enumerate(refs[4:]):
                out_ref[0] = piece[k]


def place_pieces(places, pieces):
    two, rows, width = pieces[0].shape
    whole = pl.BlockSpec(pieces[0].shape, lambda i, place_ref: (0, 0, 0))
    return pl.pallas_call(
        place_kernel,
        grid_spec=pltpu.PrefetchScalarGridSpec(
            num_scalar_prefetch=1,
            grid=(4,),
            in_specs=[whole] * 4,
            out_specs=[pl.BlockSpec((1, rows, width), lambda i, place_ref: (place_ref[i], 0, 0))] * two,
        ),
        out_shape=[jax.ShapeDtypeStruct((4, rows, width), pieces[0].dtype)] * two,
        compiler_params=pltpu.CompilerParams(vmem_limit_bytes=40 * MIB),
        cost_estimate=SMALL_COST,
        name="place_pieces",
    )(places, *pieces)


def swap(value, axis, count, bit):
    return lax.ppermute(value, axis, [(i, i ^ bit) for i in range(count)])


def all_to_all(value):
    return lax.all_to_all(value, "dp", split_axis=0, concat_axis=0, tiled=True)


def together(*values):
    return lax.optimization_barrier(values)


def local(
    layer_input, out_grad, first_gain, query_weight, key_weight, value_weight, output_weight,
    position_bias, second_gain, router_weight, expert_in, expert_out, seq_lengths, routes,
):
    micro_count, tok_rows, width = layer_input.shape
    dp_count = lax.axis_size("dp")
    expert_count = router_weight.shape[1]
    shard = query_weight.shape[1]
    heads_here = position_bias.shape[0]
    assert lax.axis_size("tensor") == 4 and micro_count == 2 and expert_count == dp_count
    assert tok_rows == SEQ and seq_lengths.shape[1] == 1
    capacity = max(8, 8 * (10 * tok_rows // (32 * expert_count)))
    half = capacity // 2
    stride = 8 * (half // 8 + 1)
    by_lines = dp_count == 8
    chunks = 2 if half % 32 == 0 else 1
    chunk = half // chunks
    chunk_rows = expert_count * chunk
    rows_here = query_weight.shape[0]
    me = lax.axis_index("dp")
    rank = lax.axis_index("tensor")
    micro = rank // 2
    core = rank % 2

    def swap_y(value):
        return swap(value, "tensor", 4, 2)

    def swap_core(value):
        return swap(value, "tensor", 4, 1)

    micro_arg = micro.reshape(1).astype(jnp.int32)
    core_arg = core.reshape(1).astype(jnp.int32)

    packed = pack_weights(query_weight, key_weight, value_weight, output_weight, first_gain, second_gain, router_weight)
    three = 3 * TILE

    def doubled(stacked, bit, axis=0):
        other = swap(stacked, "dp", dp_count, bit)
        high = (me & bit) != 0
        pair = jnp.where(high, jnp.stack([other, stacked], axis + 1), jnp.stack([stacked, other], axis + 1))
        return pair.reshape(stacked.shape[:axis] + (-1,) + stacked.shape[axis + 1 :])

    stacked = packed[None]
    bit = dp_count // 2
    while bit > 1:
        stacked = doubled(stacked, bit)
        bit //= 2
    length = lax.dynamic_index_in_dim(seq_lengths, micro, 0, keepdims=False)
    route = lax.dynamic_index_in_dim(routes, micro, 0, keepdims=False).T
    expert_ids = jnp.arange(expert_count, dtype=jnp.int32)
    named = (expert_ids[:, None, None] == route[None]).astype(jnp.int32)
    per_token = jnp.sum(named, axis=1, dtype=jnp.int32)
    earlier = jnp.cumsum(per_token, axis=1, dtype=jnp.int32) - per_token
    slot = jnp.sum(named * earlier[:, None, :], axis=0, dtype=jnp.int32)
    here = slot // half == core
    within = slot % half
    chunk_of = within // chunk
    inside = within % chunk
    spare = 16 * -(-chunk // 16)
    last_stride = spare + 16
    last = (chunks - 1) * chunk_rows
    code_back = jnp.where(
        chunk_of == chunks - 1, last + route * last_stride + inside, chunk_of * chunk_rows + route * chunk + inside
    )
    code_back = code_back + jnp.where(here, 0, last + expert_count * last_stride)
    code_result = route * half + within + jnp.where(here, 0, expert_count * half)
    info = jnp.concatenate([code_back, route, slot, code_result], 0)

    code_grads = jnp.where(here, route * stride + within, -1)
    valid = jnp.arange(SEQ, dtype=jnp.int32) < length[0]
    ids = jnp.arange(expert_count * stride, dtype=jnp.int32)[:, None]
    partner = jnp.sum(
        jnp.where(ids == code_grads[:1], route[1:], 0) + jnp.where(ids == code_grads[1:], route[:1], 0), axis=1, dtype=jnp.int32
    )
    grads_sent = send_rows(micro_arg, jnp.where(valid[None], code_grads, -1), out_grad, expert_count * stride)
    grads_sent = grads_sent.reshape(expert_count, stride, width)
    partner_row = jnp.pad(partner.reshape(expert_count, stride)[:, :half].astype(BF), ((0, 0), (0, width - half)))
    grads_sent = grads_sent.at[:, half].set(partner_row)
    stacked, grads_sent, position_bias = together(stacked, grads_sent, position_bias)
    if by_lines:
        lines = [list(range(x, dp_count, 2)) for x in range(2)]
        grads_z = lax.all_to_all(
            grads_sent.reshape(dp_count // 2, 2, stride, width), "dp", split_axis=0, concat_axis=0,
            axis_index_groups=lines, tiled=True,
        )

    first_own = expert_in[0]
    second_own = expert_out[0]
    part_b = stacked[:, :, :three]
    far_b = swap_y(part_b)
    part_a = doubled(stacked[:, :, three:], 1)
    part_a, far_b = together(part_a, far_b)
    pair_b = jnp.stack([part_b, far_b])
    a_own = part_a[:, :, :three]
    a_far = swap_y(a_own).reshape(width, three)
    a_own = a_own.reshape(width, three)
    pair_b = doubled(pair_b, 1, 1).reshape(2, width, three)
    if by_lines:
        a_far, pair_b, first_own = together(a_far, pair_b, first_own)
    else:
        a_far, pair_b, grads_sent, first_own = together(a_far, pair_b, grads_sent, first_own)
    first_y = swap_y(first_own)
    small_all = part_a[:, :, three:].reshape(width, TILE)
    gain_one = small_all[:, expert_count].astype(F32)[None]
    gain_two = small_all[:, expert_count + 1].astype(F32)[None]
    router_wide = small_all
    far_bias = swap_y(position_bias)
    bias = jnp.concatenate([position_bias[:2], far_bias[:2], position_bias[2:], far_bias[2:]], 0)
    head_total = bias.shape[0]
    hot_const = jnp.asarray(NEAR_HOT, dtype=BF)
    near = dot(bias, hot_const) - bias[:, NB - 1 :].astype(F32)
    near = near.reshape(head_total, 2, TILE, TILE)
    places = jnp.arange(TILE, dtype=jnp.int32)
    causal = jnp.stack([places[None, :] <= places[:, None], jnp.ones((TILE, TILE), bool)])
    near = jnp.where(causal[None], near, NEG)

    if by_lines:
        high = (me & 1) != 0
    else:
        grads_here = all_to_all(grads_sent)

    qkv, normed_one, qkv_weight, output_own = norm_and_project(
        micro_arg, layer_input, gain_one, a_own, a_far, pair_b[0], pair_b[1]
    )
    output_far = swap_core(output_own)
    mixed, logs = attend(length, qkv, near)
    mixed, output_far = together(mixed, output_far)
    mixed_far = swap_core(mixed)
    code_chunks = jnp.where(here, chunk_of * chunk_rows + route * chunk + inside, -1)
    if by_lines:
        sent_x = lax.dynamic_index_in_dim(grads_z, 1 - (me & 1), 1, keepdims=False)
        mixed_far, grads_z, sent_x, first_y, second_own = together(mixed_far, grads_z, sent_x, first_y, second_own)
        second_y = swap_y(second_own)
        got_x = swap(sent_x, "dp", dp_count, 1)
    residual, *parts = residual_and_rows(
        micro_arg, layer_input, mixed, mixed_far, output_own, output_far, gain_two, code_chunks, chunk_rows, chunks
    )

    if by_lines:
        parts, grads_z = together(parts, grads_z)
        kept_x = jnp.where(high, grads_z[:, 1], grads_z[:, 0])
        pair_x = jnp.where(high, jnp.stack([got_x, kept_x], 1), jnp.stack([kept_x, got_x], 1))
        grads_here = pair_x.reshape(dp_count, stride, width)
    else:
        parts, grads_here, first_y, second_own = together(parts, grads_here, first_y, second_own)
        second_y = swap_y(second_own)
    parts = [part.reshape(expert_count, chunk, width) for part in parts]
    arrived = [all_to_all(parts[0])]
    partner_here = grads_here[:, half, :half].astype(jnp.int32)

    def chunk_grads(c):
        at = slice(c * chunk, (c + 1) * chunk)
        return grads_here[:, at].reshape(chunk_rows, width), partner_here[:, at].reshape(chunk_rows)

    grads_parts = [chunk_grads(c) for c in range(chunks)]
    arrived[0], grads_parts, second_y = together(arrived[0], grads_parts, second_y)

    firsts = (first_own, first_y, swap_core(first_own), swap_core(first_y))
    seconds = (second_own, second_y, swap_core(second_own), swap_core(second_y))

    for c in range(1, chunks):
        sent, arrived[-1] = together(parts[c], arrived[-1])
        arrived.append(all_to_all(sent))

    me_arg = me.reshape(1).astype(jnp.int32)
    rows_all, slopes, active, gated, gates, backs = [], [], [], [], [], []
    line = None
    for c in range(chunks):
        grads_c, partner_c = grads_parts[c]
        rows_c = arrived[c].reshape(chunk_rows, width)
        back, act, slo, gat, gte, line = expert_rows_pass(
            c * chunk if chunks > 1 else None, chunk, half, me_arg, partner_c, rows_c, grads_c, router_wide, line, firsts, seconds
        )
        rows_all.append(rows_c)
        slopes.append(slo)
        active.append(act)
        gated.append(gat)
        gates.append(gte)
        if chunks == 1:
            gate_grad = line[:, 0].reshape(expert_count, chunk)
            pieces = []
            for _ in range(3):
                piece = gate_grad.astype(BF)
                pieces.append(piece)
                gate_grad = gate_grad - piece.astype(F32)
            gate_row = jnp.pad(jnp.concatenate(pieces, 1), ((0, 0), (0, width - 3 * half)))
            back = jnp.pad(back.reshape(expert_count, chunk, width), ((0, 0), (0, last_stride - chunk), (0, 0)))
            back = back.at[:, spare].set(gate_row)
        if c + 1 < chunks:
            back, arrived[c + 1] = together(back.reshape(expert_count, chunk, width), arrived[c + 1])
        else:
            if chunks > 1:
                results = None
                for k in range(chunks - 1):
                    results = expert_results(k, chunks, active[k], gates[k], seconds, expert_count, results)
                back, rows_all[-1], backs, results = together(back, rows_all[-1], backs, results)
            else:
                results = None
        backs.append(all_to_all(back))
    grads_cross = cross_weight_grads(rows_all, slopes, active, gated)
    gates, grads_cross = together(gates, grads_cross)
    grads_in = swap_core(grads_cross)
    results = expert_results(chunks - 1, chunks, active[-1], gates[-1], seconds, expert_count, results)
    results = results.reshape(expert_count, half, width)
    results, grads_in = together(results, grads_in)
    grads_far, grads_kept = kept_weight_grads(rows_all, slopes, active, gated, grads_in)
    backs[-1], results, grads_far = together(backs[-1], results, grads_far)

    across_y = swap_y(grads_far)
    results_own = all_to_all(results).reshape(expert_count * half, width)

    backs_far = [swap_core(b) for b in backs]
    residual_grad, mixed_grad, extra_early, output_sent, output_kept = combine(
        micro_arg, core_arg, length, info, out_grad, residual, mixed, gain_two, router_wide, output_own,
        backs + backs_far, half, spare,
    )

    dq, dk, dv, tiles, sums = attend_back(length, qkv, near, mixed, logs, mixed_grad, 0, head_total // 2)
    far_sent, own_parts, sent = attention_weight_grads(core_arg, normed_one, dq, dk, dv, output_sent, qkv_weight)
    far_got = swap_y(far_sent)
    sent, results_own = together(sent, results_own)
    got = swap_core(sent)
    rows_both, extra_late = both_rows(
        expert_count, micro_arg, core_arg, length, qkv_weight, (dq, dk, dv), got, layer_input, gain_one, residual_grad,
        info, residual, results_own, swap_core(results_own),
    )
    rows_both, across_y, tiles = together(rows_both, across_y, tiles)
    late_far = swap_core(extra_late)
    corner = micro * 2 + core
    corners = jnp.stack([corner, corner ^ 1, corner ^ 2, corner ^ 3]).astype(jnp.int32)
    rows_y = swap_y(rows_both)
    expert_in_grad, expert_out_grad = last_sums(grads_kept, across_y)
    rows_y, expert_in_grad, expert_out_grad = together(rows_y, expert_in_grad, expert_out_grad)
    pieces = (rows_both, swap_core(rows_both), rows_y, swap_core(rows_y))

    tiles = tiles.reshape(head_total, 2 * TILE * TILE)
    tiles_high = tiles.astype(BF)
    tiles_rest = (tiles - tiles_high.astype(F32)).astype(BF)
    table = dot(tiles_high, hot_const, NT) + dot(tiles_rest, hot_const, NT)
    far_sum = jnp.sum(sums[:, :, 0], axis=1) - jnp.sum(table[:, : NB - 1], axis=1)
    table = jnp.concatenate([table[:, : NB - 1], far_sum[:, None]], 1)
    table_own = jnp.concatenate([table[0:2], table[4:5]], 0)
    table_far = jnp.concatenate([table[2:4], table[5:6]], 0)
    table_cols = heads_here * NB // rows_here
    table_both = jnp.concatenate([table_own.reshape(rows_here, table_cols), table_far.reshape(rows_here, table_cols)], 1)
    base = expert_count + 2
    kept = base + 2 * table_cols
    table_tile = jnp.tile(jnp.pad(table_both, ((0, 0), (base, TILE - kept))), (dp_count, 1))

    grads = packed_sums(kept, own_parts, far_got, output_kept, extra_early, extra_late, late_far, table_tile)
    arrived_grads = all_to_all(grads.reshape(dp_count, rows_here, grads.shape[1]))
    query_grad, key_grad, value_grad, output_grad, small = final_sums(kept, arrived_grads, shard)
    pieces, small = together(pieces, small)
    small_y = swap_y(small)
    layer_output, input_grad = (out.reshape(2, SEQ, width) for out in place_pieces(corners, pieces))
    both = small + small_y
    table_sum = small[:, base : base + table_cols] + small_y[:, base + table_cols : kept]
    return (
        layer_output,
        input_grad,
        both[:, expert_count],
        query_grad,
        key_grad,
        value_grad,
        output_grad.T,
        table_sum.reshape(heads_here, NB),
        both[:, expert_count + 1],
        both[:, :expert_count],
        expert_in_grad[None],
        expert_out_grad[None],
    )


def solution(mesh):
    return jax.shard_map(
        local,
        mesh=mesh,
        in_specs=(
            P(None, "dp", None),
            P(None, "dp", None),
            P("dp"),
            P("dp", "tensor"),
            P("dp", "tensor"),
            P("dp", "tensor"),
            P("tensor", "dp"),
            P("tensor", None),
            P("dp"),
            P("dp", None),
            P("dp", None, "tensor"),
            P("dp", "tensor", None),
            P(None, "dp"),
            P(None, "dp", None),
        ),
        out_specs=(
            P(None, "dp", None),
            P(None, "dp", None),
            P("dp"),
            P("dp", "tensor"),
            P("dp", "tensor"),
            P("dp", "tensor"),
            P("tensor", "dp"),
            P("tensor", None),
            P("dp"),
            P("dp", None),
            P("dp", None, "tensor"),
            P("dp", "tensor", None),
        ),
        check_vma=False,
    )
```

```python
import functools

import jax
import jax.numpy as jnp
import numpy as np
from jax import lax
from jax.experimental import pallas as pl
from jax.experimental.pallas import tpu as pltpu
from jax.sharding import PartitionSpec as P

HEAD_DIM = 64
NB = 32
SEQ = 1024
TILE = 128
QROWS = 256
NEG = -1e30
GELU_C = 0.7978845608028654
GELU_A = 0.044715

BF = jnp.bfloat16
F32 = jnp.float32

bucket_edges = np.ceil(16.0 * 8.0 ** (np.arange(1, 16) / 16.0)).astype(np.int32)


def near_tables():
    rows = np.arange(TILE)[:, None]
    cols = np.arange(TILE)[None, :]
    hots = []
    for shift in (0, TILE):
        distance = rows - cols + shift
        clipped = np.maximum(distance, 0)
        reached = np.sum(clipped[..., None] >= bucket_edges, axis=-1)
        bucket = np.minimum(clipped, 16) + reached
        hots.append(bucket[..., None] == np.arange(NB))
    hot = np.stack(hots).reshape(2 * TILE * TILE, NB).T
    return hot


NEAR_HOT = near_tables()
assert bucket_edges[-1] <= TILE


def dot(a, b, dims=((1,), (0,))):
    return lax.dot_general(a, b, (dims, ((), ())), preferred_element_type=F32)


NT = ((1,), (1,))
TN = ((0,), (0,))


MIB = 2**20
SMALL_COST = pl.CostEstimate(flops=1_000_000, bytes_accessed=1_000_000, transcendentals=0)


STRIP = 32


def score_strip(s, at, block, j, start, near_ref, half, length):
    part = s[at : at + STRIP]
    near = slice(start % TILE, start % TILE + STRIP)
    if j == block:
        if start < TILE:
            left = part[:, :TILE] + near_ref[half, 0, near, :]
            right = jnp.full((STRIP, TILE), NEG, F32)
        else:
            left = part[:, :TILE] + near_ref[half, 1, near, :]
            right = part[:, TILE:] + near_ref[half, 0, near, :]
        part = jnp.concatenate([left, right], 1)
    elif j == block - 1 and start < TILE:
        part = jnp.concatenate([part[:, :TILE], part[:, TILE:] + near_ref[half, 1, near, :]], 1)
    if (j + 1) * QROWS > SEQ // 2:
        place = lax.broadcasted_iota(jnp.int32, (1, QROWS), 1) + j * QROWS
        part = part + jnp.where(place < length, 0.0, NEG)
    return part


def lane_half(rows):
    return lax.broadcasted_iota(jnp.int32, (rows, 2 * HEAD_DIM), 1) < HEAD_DIM


def attend_kernel(length_ref, query_ref, key_ref, value_ref, near_ref, out_ref, log_ref):
    length = length_ref[0]
    lanes = lane_half(QROWS)
    value_ext = jnp.concatenate([value_ref[...], jnp.ones((SEQ, TILE), BF)], 1)
    for i in range(SEQ // QROWS):
        q_rows = query_ref[i * QROWS : (i + 1) * QROWS, :] * BF(0.125)
        q_both = jnp.concatenate([jnp.where(lanes, q_rows, BF(0)), jnp.where(lanes, BF(0), q_rows)], 0)
        tiles = [dot(q_both, key_ref[j * QROWS : (j + 1) * QROWS, :], NT) for j in range(i + 1)]
        tops = []
        weights = [[] for _ in tiles]
        for h in range(2):
            for start in range(0, QROWS, STRIP):
                strips = [
                    score_strip(s, h * QROWS + start, i, j, start, near_ref, h, length) for j, s in enumerate(tiles)
                ]
                top = strips[0]
                for s in strips[1:]:
                    top = jnp.maximum(top, s)
                top = jnp.max(top, axis=1, keepdims=True)
                tops.append(top)
                for j, s in enumerate(strips):
                    weights[j].append(jnp.exp(s - top).astype(BF))
        total = None
        for j, strips in enumerate(weights):
            total = put(total, dot(jnp.concatenate(strips, 0), value_ext[j * QROWS : (j + 1) * QROWS, :]))
        row_sum = total[:, TILE:]
        out = total[:, :TILE] / row_sum
        logs = jnp.concatenate(tops, 0) + jnp.log(row_sum)
        out_ref[i * QROWS : (i + 1) * QROWS, :] = jnp.where(lanes, out[:QROWS], out[QROWS:]).astype(BF)
        log_ref[i * QROWS : (i + 1) * QROWS, :] = jnp.where(lanes, logs[:QROWS], logs[QROWS:])


def attend(length, qkv, near):
    pairs = qkv.shape[1] // (3 * TILE)
    cols = pairs * TILE
    return pl.pallas_call(
        attend_kernel,
        grid=(pairs,),
        in_specs=[
            pl.BlockSpec(memory_space=pltpu.SMEM),
            pl.BlockSpec((SEQ, TILE), lambda p: (0, p)),
            pl.BlockSpec((SEQ, TILE), lambda p: (0, pairs + p)),
            pl.BlockSpec((SEQ, TILE), lambda p: (0, 2 * pairs + p)),
            pl.BlockSpec((2, 2, TILE, TILE), lambda p: (p, 0, 0, 0)),
        ],
        out_specs=[
            pl.BlockSpec((SEQ, TILE), lambda p: (0, p)),
            pl.BlockSpec((SEQ, TILE), lambda p: (0, p)),
        ],
        out_shape=[
            jax.ShapeDtypeStruct((SEQ, cols), BF),
            jax.ShapeDtypeStruct((SEQ, cols), F32),
        ],
        compiler_params=pltpu.CompilerParams(vmem_limit_bytes=40 * MIB),
        cost_estimate=SMALL_COST,
        name="attend",
    )(length, qkv, qkv, qkv, near)


def attend_back_kernel(
    length_ref, query_ref, key_ref, value_ref, near_ref, out_ref, log_ref, grad_ref,
    dq_ref, dk_ref, dv_ref, tile_ref, sum_ref, dk_acc, dv_acc,
):
    length = length_ref[0]
    lanes = lane_half(QROWS)
    key_ext = jnp.concatenate([key_ref[...], jnp.ones((SEQ, TILE), BF)], 1)
    near_sums = [[None, None], [None, None]]
    all_sums = [None, None]

    def both(rows):
        return jnp.concatenate([jnp.where(lanes, rows, BF(0)), jnp.where(lanes, BF(0), rows)], 0)

    for i in range(SEQ // QROWS):
        rows = slice(i * QROWS, (i + 1) * QROWS)
        q_both = both(query_ref[rows, :] * BF(0.125))
        g_rows = grad_ref[rows, :]
        g_both = both(g_rows)
        mass = g_rows.astype(F32) * out_ref[rows, :].astype(F32)
        deltas = [
            jnp.sum(jnp.where(lanes, mass, 0.0), axis=1, keepdims=True),
            jnp.sum(jnp.where(lanes, 0.0, mass), axis=1, keepdims=True),
        ]
        logs = [log_ref[rows, h * HEAD_DIM : h * HEAD_DIM + 1] for h in range(2)]
        dq = None
        for j in range(i + 1):
            keys = slice(j * QROWS, (j + 1) * QROWS)
            s = dot(q_both, key_ref[keys, :], NT)
            dp = dot(g_both, value_ref[keys, :], NT)
            p_strips, d_strips = [], []
            for h in range(2):
                for start in range(0, QROWS, STRIP):
                    strip = slice(start, start + STRIP)
                    at = h * QROWS + start
                    p = jnp.exp(score_strip(s, at, i, j, start, near_ref, h, length) - logs[h][strip])
                    p_strips.append(p.astype(BF))
                    d_strips.append((p * (dp[at : at + STRIP] - deltas[h][strip])).astype(BF))
            p, ds = jnp.concatenate(p_strips, 0), jnp.concatenate(d_strips, 0)
            part = dot(ds, key_ext[keys, :])
            dq = put(dq, jnp.where(lanes, part[:QROWS, :TILE], part[QROWS:, :TILE]))
            for h in range(2):
                sums = part[h * QROWS : (h + 1) * QROWS, TILE:]
                all_sums[h] = put(all_sums[h], jnp.sum(sums.reshape(QROWS // 8, 8, TILE), axis=0))
            dk_part = dot(ds, q_both, TN)
            dv_part = dot(p, g_both, TN)
            if i == j:
                dk_acc[keys, :] = dk_part
                dv_acc[keys, :] = dv_part
            else:
                dk_acc[keys, :] += dk_part
                dv_acc[keys, :] += dv_part
            for h in range(2):
                mine = ds[h * QROWS : (h + 1) * QROWS]
                if j == i:
                    wide = mine.astype(F32)
                    near_sums[h][0] = put(near_sums[h][0], wide[:TILE, :TILE] + wide[TILE:, TILE:])
                    near_sums[h][1] = put(near_sums[h][1], wide[TILE:, :TILE])
                elif j == i - 1:
                    near_sums[h][1] = put(near_sums[h][1], mine[:TILE, TILE:].astype(F32))
        dq_ref[rows, :] = (dq * 0.125).astype(BF)
    dk_ref[...] = dk_acc[...].astype(BF)
    dv_ref[...] = dv_acc[...].astype(BF)
    for h in range(2):
        tile_ref[h, 0] = near_sums[h][0]
        tile_ref[h, 1] = near_sums[h][1]
        sum_ref[h] = all_sums[h]


def attend_back(length, qkv, near, mixed, logs, grad, first, count):
    pairs = qkv.shape[1] // (3 * TILE)
    cols = count * TILE
    col = pl.BlockSpec((SEQ, TILE), lambda p: (0, first + p))
    out = pl.BlockSpec((SEQ, TILE), lambda p: (0, p))
    return pl.pallas_call(
        attend_back_kernel,
        grid=(count,),
        in_specs=[
            pl.BlockSpec(memory_space=pltpu.SMEM),
            col,
            pl.BlockSpec((SEQ, TILE), lambda p: (0, pairs + first + p)),
            pl.BlockSpec((SEQ, TILE), lambda p: (0, 2 * pairs + first + p)),
            pl.BlockSpec((2, 2, TILE, TILE), lambda p: (first + p, 0, 0, 0)),
            col,
            col,
            col,
        ],
        out_specs=[
            out,
            out,
            out,
            pl.BlockSpec((2, 2, TILE, TILE), lambda p: (p, 0, 0, 0)),
            pl.BlockSpec((2, 8, TILE), lambda p: (p, 0, 0)),
        ],
        out_shape=[
            jax.ShapeDtypeStruct((SEQ, cols), BF),
            jax.ShapeDtypeStruct((SEQ, cols), BF),
            jax.ShapeDtypeStruct((SEQ, cols), BF),
            jax.ShapeDtypeStruct((2 * count, 2, TILE, TILE), F32),
            jax.ShapeDtypeStruct((2 * count, 8, TILE), F32),
        ],
        scratch_shapes=[pltpu.VMEM((SEQ, TILE), F32), pltpu.VMEM((SEQ, TILE), F32)],
        compiler_params=pltpu.CompilerParams(vmem_limit_bytes=40 * MIB),
        cost_estimate=SMALL_COST,
        name="attend_back",
    )(length, qkv, qkv, qkv, near, mixed, logs, grad)


def low_lanes(shape):
    return lax.broadcasted_iota(jnp.int32, shape, 1) < HEAD_DIM


def turned(tile):
    return pltpu.roll(tile, HEAD_DIM, 1)


def pack_kernel(q_ref, k_ref, v_ref, o_ref, one_ref, two_ref, router_ref, out_ref):
    shard = q_ref.shape[1]
    rows = q_ref.shape[0]
    source = lax.broadcasted_iota(jnp.int32, (shard, 6 * TILE), 0)
    target = lax.broadcasted_iota(jnp.int32, (shard, 6 * TILE), 1)

    def moved(pair_base, last_base):
        want = jnp.where(source < TILE, source + pair_base, source - TILE + last_base)
        return jnp.where(target == want, 1.0, 0.0).astype(BF)

    total = dot(v_ref[...], moved(0, 2 * TILE)) + dot(o_ref[...], moved(TILE, 2 * TILE + HEAD_DIM), TN)
    total = total + dot(q_ref[...], moved(3 * TILE, 5 * TILE)) + dot(k_ref[...], moved(4 * TILE, 5 * TILE + HEAD_DIM))
    out_ref[:, : 6 * TILE] = total.astype(BF)
    experts = router_ref.shape[0]
    own_row = lax.broadcasted_iota(jnp.int32, (rows, rows), 0) == lax.broadcasted_iota(jnp.int32, (rows, rows), 1)

    def column(ref):
        return jnp.sum(jnp.where(own_row, ref[...].astype(F32), 0.0), axis=1, keepdims=True)

    lanes = lax.broadcasted_iota(jnp.int32, (experts, TILE), 1)
    spread = jnp.where(lanes == lax.broadcasted_iota(jnp.int32, (experts, TILE), 0), 1.0, 0.0).astype(BF)
    place = lax.broadcasted_iota(jnp.int32, (rows, TILE), 1)
    small = dot(router_ref[...], spread, TN)
    small = jnp.where(place == experts, column(one_ref), jnp.where(place == experts + 1, column(two_ref), small))
    out_ref[:, 6 * TILE :] = small.astype(BF)


def pack_weights(query, key, value, output, one, two, router):
    rows = query.shape[0]
    return pl.pallas_call(
        pack_kernel,
        out_shape=jax.ShapeDtypeStruct((rows, 7 * TILE), BF),
        compiler_params=pltpu.CompilerParams(vmem_limit_bytes=60 * MIB),
        cost_estimate=SMALL_COST,
        name="pack_weights",
    )(query, key, value, output, one[None], two[None], router.T)


def qkv_kernel(micro_ref, tokens_ref, gain_ref, a_own, a_far, b_own, b_far, qkv_ref, normed_ref, weight_ref, output_ref):
    width = tokens_ref.shape[2]

    @pl.when(pl.program_id(0) == 0)
    def _():
        low = low_lanes((width, TILE))

        def tiles(own, far, pair, low_half):
            at = slice(pair * TILE, (pair + 1) * TILE)
            one, two = own[:, 2 * TILE :].astype(F32), far[:, 2 * TILE :].astype(F32)
            last = jnp.where(low, one, turned(two)) if low_half else jnp.where(low, turned(one), two)
            return own[:, at], far[:, at], last.astype(BF)

        for n, (own, far, pair, low_half) in enumerate(
            ((a_own, a_far, 0, True), (a_own, a_far, 1, False), (b_own, b_far, 0, True))
        ):
            for t, tile in enumerate(tiles(own[...], far[...], pair, low_half)):
                at = 3 * n + t
                weight_ref[:, at * TILE : (at + 1) * TILE] = tile
        for t, tile in enumerate(tiles(b_own[...], b_far[...], 1, False)):
            output_ref[:, t * TILE : (t + 1) * TILE] = tile

    x = tokens_ref[0].astype(F32)
    inverse = lax.rsqrt(jnp.mean(x * x, axis=-1, keepdims=True) + 1e-06)
    normed = (x * inverse * gain_ref[...]).astype(BF)
    normed_ref[...] = normed
    qkv_ref[...] = dot(normed, weight_ref[...]).astype(BF)


def norm_and_project(micro, layer_input, gain, a_own, a_far, b_own, b_far):
    width = layer_input.shape[2]
    block = 256
    cols = 3 * TILE
    whole = lambda rows, n: pl.BlockSpec((rows, n), lambda i, m: (0, 0))
    here = lambda n: pl.BlockSpec((block, n), lambda i, m: (i, 0))
    return pl.pallas_call(
        qkv_kernel,
        grid_spec=pltpu.PrefetchScalarGridSpec(
            num_scalar_prefetch=1,
            grid=(SEQ // block,),
            in_specs=[pl.BlockSpec((1, block, width), lambda i, m: (m[0], i, 0)), whole(1, width)] + [whole(width, cols)] * 4,
            out_specs=[here(3 * cols), here(width), whole(width, 3 * cols), whole(width, cols)],
        ),
        out_shape=[
            jax.ShapeDtypeStruct((SEQ, 3 * cols), BF),
            jax.ShapeDtypeStruct((SEQ, width), BF),
            jax.ShapeDtypeStruct((width, 3 * cols), BF),
            jax.ShapeDtypeStruct((width, cols), BF),
        ],
        compiler_params=pltpu.CompilerParams(vmem_limit_bytes=40 * MIB),
        cost_estimate=SMALL_COST,
        name="norm_and_project",
    )(micro, layer_input, gain, a_own, a_far, b_own, b_far)


def middle_kernel(
    blocks, per, micro_ref, tokens_ref, mixed_ref, other_ref, own_ref, far_ref, gain_ref, code_ref, residual_ref, *refs
):
    sent_refs, normed = refs[:-1], refs[-1]
    step = pl.program_id(0)
    rows = tokens_ref.shape[1]

    @pl.when(step < blocks)
    def _():
        total = tokens_ref[0].astype(F32) + dot(mixed_ref[...], own_ref[...], NT) + dot(other_ref[...], far_ref[...], NT)
        residual_ref[...] = total
        inverse = lax.rsqrt(jnp.mean(total * total, axis=-1, keepdims=True) + 1e-06)
        normed[pl.ds(pl.multiple_of(step * rows, rows), rows), :] = (total * inverse * gain_ref[...]).astype(BF)

    for c, sent_ref in enumerate(sent_refs):

        @pl.when((step >= blocks + c * per) & (step < blocks + (c + 1) * per))
        def _(sent_ref=sent_ref):
            block = sent_ref.shape[0]
            ids = lax.broadcasted_iota(jnp.int32, (block, 1), 0) + (step - blocks) * block
            hot = jnp.where((ids == code_ref[:1]) | (ids == code_ref[1:2]), 1.0, 0.0).astype(BF)
            sent_ref[...] = dot(hot, normed[...]).astype(BF)


def residual_and_rows(micro, layer_input, mixed, other, output_own, output_far, gain, code, count, chunks):
    width = layer_input.shape[2]
    block = 256
    blocks = SEQ // block
    send = 320
    cols = mixed.shape[1]
    per = count // send
    at = lambda i: jnp.minimum(i, blocks - 1)
    whole = lambda arr: pl.BlockSpec(arr.shape, lambda i, m: (0, 0))
    here = lambda n: pl.BlockSpec((block, n), lambda i, m: (at(i), 0))

    def sent(c):
        return pl.BlockSpec((send, width), lambda i, m: (jnp.clip(i - blocks - c * per, 0, per - 1), 0))

    return pl.pallas_call(
        functools.partial(middle_kernel, blocks, per),
        grid_spec=pltpu.PrefetchScalarGridSpec(
            num_scalar_prefetch=1,
            grid=(blocks + chunks * per,),
            in_specs=[
                pl.BlockSpec((1, block, width), lambda i, m: (m[0], at(i), 0)),
                here(cols), here(cols), whole(output_own), whole(output_far), whole(gain), whole(code),
            ],
            out_specs=[here(width)] + [sent(c) for c in range(chunks)],
            scratch_shapes=[pltpu.VMEM((SEQ, width), BF)],
        ),
        out_shape=[jax.ShapeDtypeStruct((SEQ, width), F32)] + [jax.ShapeDtypeStruct((count, width), BF)] * chunks,
        compiler_params=pltpu.CompilerParams(vmem_limit_bytes=40 * MIB),
        cost_estimate=SMALL_COST,
        name="residual_and_rows",
    )(micro, layer_input, mixed, other, output_own, output_far, gain, code)


def picked_rows(first, second, segments):
    total = None
    start = 0
    for rows in segments:
        length = rows.shape[0]
        ids = lax.broadcasted_iota(jnp.int32, (1, length), 1) + start
        hot = []
        for at in range(0, first.shape[0], STRIP):
            one, two = first[at : at + STRIP], second[at : at + STRIP]
            hot.append(jnp.where((one == ids) | (two == ids), 1.0, 0.0).astype(BF))
        total = put(total, dot(jnp.concatenate(hot, 0), rows))
        start += length
    return total


def put(a, b):
    return b if a is None else a + b


def folded(product):
    return jnp.sum(product.reshape(product.shape[0] // 8, 8, product.shape[1]), axis=0)


def as_column(eight):
    ones = jnp.ones((16, TILE), BF)
    high = eight.astype(BF)
    rest = (eight - high.astype(F32)).astype(BF)
    return dot(jnp.concatenate([high, rest], 0), ones, TN)


def combine_kernel(experts, half, spare, micro_ref, core_ref, length_ref, *refs):
    info_ref, grad_ref, residual_ref, mixed_ref, gain_ref, router_ref, output_ref = refs[:7]
    backs = refs[7:-9]
    (total_ref, mixed_grad_ref, extra_ref, far_ref, own_ref, acc_ref, router_acc, gain_acc, tables) = refs[-9:]
    block = residual_ref.shape[0]
    step = pl.program_id(0)
    count = len(backs) // 2

    @pl.when(step == 0)
    def _():
        place = lax.broadcasted_iota(jnp.int32, (experts, 1), 0)
        for n, back in enumerate((backs[count - 1], backs[2 * count - 1])):
            table = jnp.zeros((experts, back.shape[2]), F32)
            for e in range(experts):
                row = back[e, spare : spare + 16, :].astype(F32)[:1]
                table = jnp.where(place == e, row, table)
            for piece in range(3):
                at = (3 * n + piece) * experts
                tables[at : at + experts] = table[:, piece * half : (piece + 1) * half]

    info = jnp.transpose(info_ref[...])
    number = lambda n: info[:, n : n + 1]
    columns = lax.broadcasted_iota(jnp.int32, (1, half), 1)
    lanes = lax.broadcasted_iota(jnp.int32, (1, 6 * experts), 1)
    table = tables[...].astype(BF)
    values = []
    for k in range(2):
        slot = number(4 + k)
        hot = jnp.where(columns == lax.rem(slot, half), 1.0, 0.0).astype(BF)
        found = dot(hot, table, NT)
        wanted = jnp.where(slot // half == core_ref[0], 0, 3 * experts) + number(2 + k)
        away = lanes - wanted
        hit = (away == 0) | (away == experts) | (away == 2 * experts)
        values.append(jnp.sum(jnp.where(hit, found, 0.0), axis=1, keepdims=True))
    wide = lax.broadcasted_iota(jnp.int32, (1, TILE), 1)
    is_first, is_second = wide == number(2), wide == number(3)
    residual = residual_ref[...]
    gain = gain_ref[...]
    inverse = lax.rsqrt(jnp.mean(residual * residual, axis=-1, keepdims=True) + 1e-06)
    plain = residual * inverse
    normed = (plain * gain).astype(BF)
    logits = dot(normed, router_ref[...])
    gap = jnp.sum(jnp.where(is_first, logits, 0.0) - jnp.where(is_second, logits, 0.0), axis=1, keepdims=True)
    small = jnp.exp(-jnp.abs(gap))
    logit = small / ((1.0 + small) * (1.0 + small)) * (values[0] - values[1])
    logit_grad = jnp.where(is_first, logit, jnp.where(is_second, -logit, 0.0)).astype(BF)
    segments = [b[...].reshape(b.shape[0] * b.shape[1], b.shape[2]) for b in backs]
    normed_grad = picked_rows(number(0), number(1), segments) + dot(logit_grad, router_ref[...], NT)
    scaled = normed_grad * gain
    mean = jnp.mean(scaled * plain, axis=-1, keepdims=True)
    place = lax.broadcasted_iota(jnp.int32, (block, 1), 0) + step * block
    grad_out = jnp.where(place < length_ref[0], grad_ref[0].astype(F32), 0.0)
    total = grad_out + inverse * (scaled - plain * mean)
    total_ref[...] = total
    branch = total.astype(BF)
    mixed_grad_ref[...] = dot(branch, output_ref[...]).astype(BF)
    router_part = dot(logit_grad, normed, TN)
    gain_part = folded(normed_grad * plain)
    output_part = dot(mixed_ref[...], branch, TN)

    @pl.when(step == 0)
    def _():
        router_acc[...] = router_part
        gain_acc[...] = gain_part
        acc_ref[...] = output_part

    @pl.when(step > 0)
    def _():
        router_acc[...] += router_part
        gain_acc[...] += gain_part
        acc_ref[...] += output_part

    @pl.when(step == pl.num_programs(0) - 1)
    def _():
        extra_ref[...] = jnp.transpose(router_acc[...]) + jnp.where(wide == experts + 1, as_column(gain_acc[...]), 0.0)
        parts = jnp.transpose(acc_ref[...])
        far_ref[...] = parts[:, TILE:].astype(BF)
        own_ref[:, :TILE] = parts[:, :TILE]
        own_ref[:, TILE:] = parts[:, 2 * TILE :]


def combine(micro, core, length, info, out_grad, residual, mixed, gain, router, output_own, backs, half, spare):
    width = residual.shape[1]
    block = 512
    cols = mixed.shape[1]
    whole = lambda arr: pl.BlockSpec(arr.shape, lambda i, *_: (0,) * arr.ndim)
    fixed = lambda rows, n: pl.BlockSpec((rows, n), lambda i, *_: (0, 0))
    here = lambda n: pl.BlockSpec((block, n), lambda i, *_: (i, 0))
    experts = backs[0].shape[0]
    return pl.pallas_call(
        functools.partial(combine_kernel, experts, half, spare),
        grid_spec=pltpu.PrefetchScalarGridSpec(
            num_scalar_prefetch=3,
            grid=(SEQ // block,),
            in_specs=[
                pl.BlockSpec((8, block), lambda i, *_: (0, i)),
                pl.BlockSpec((1, block, width), lambda i, m, *_: (m[0], i, 0)),
                here(width), here(cols), whole(gain), whole(router), whole(output_own),
            ]
            + [whole(x) for x in backs],
            out_specs=[here(width), here(cols), fixed(width, TILE), fixed(width, 2 * TILE), fixed(width, 2 * TILE)],
            scratch_shapes=[
                pltpu.VMEM((cols, width), F32),
                pltpu.VMEM((TILE, width), F32),
                pltpu.VMEM((8, width), F32),
                pltpu.VMEM((6 * experts, half), F32),
            ],
        ),
        out_shape=[
            jax.ShapeDtypeStruct((SEQ, width), F32),
            jax.ShapeDtypeStruct((SEQ, cols), BF),
            jax.ShapeDtypeStruct((width, TILE), F32),
            jax.ShapeDtypeStruct((width, 2 * TILE), BF),
            jax.ShapeDtypeStruct((width, 2 * TILE), F32),
        ],
        compiler_params=pltpu.CompilerParams(vmem_limit_bytes=40 * MIB),
        cost_estimate=SMALL_COST,
        name="combine",
    )(micro, core, length, info, out_grad, residual, mixed, gain, router, output_own, *backs)


def projected_back(weight_ref, grads):
    total = None
    for n, grad in enumerate(grads):
        cols = grad.shape[1]
        total = put(total, dot(grad[...], weight_ref[:, n * cols : (n + 1) * cols], NT))
    return total


def attention_weight_kernel(
    blocks, core_ref, normed_ref, q_ref, k_ref, v_ref, output_ref, weight_ref, q_rows, k_rows, v_rows, far_ref, own_ref, sent_ref
):
    step = pl.program_id(0)

    @pl.when(step < blocks)
    def _():
        low = low_lanes((normed_ref.shape[1], TILE))
        q, k, v = (dot(normed_ref[...], d[...], TN) for d in (q_ref, k_ref, v_ref))
        for n, part in enumerate((q, k, v)):
            own_ref[:, n * TILE : (n + 1) * TILE] = part[:, :TILE]
            far_ref[:, n * TILE : (n + 1) * TILE] = part[:, TILE : 2 * TILE].astype(BF)
        q, k, v = (part[:, 2 * TILE :] for part in (q, k, v))
        far_ref[:, 3 * TILE : 4 * TILE] = jnp.where(low, turned(q), k).astype(BF)
        far_ref[:, 4 * TILE : 5 * TILE] = jnp.where(low, turned(v), output_ref[:, TILE:].astype(F32)).astype(BF)
        far_ref[:, 5 * TILE :] = output_ref[:, :TILE]
        own_ref[:, 3 * TILE : 4 * TILE] = jnp.where(low, q, turned(k))
        own_ref[:, 4 * TILE :] = jnp.where(low, v, 0.0)

    @pl.when(step >= blocks)
    def _():
        sent_ref[...] = projected_back(weight_ref, (q_rows, k_rows, v_rows))


def attention_weight_grads(core, normed, q, k, v, output, weight):
    width = normed.shape[1]
    block = 256
    blocks = width // block
    at = lambda i: jnp.minimum(i, blocks - 1)
    later = lambda i: jnp.maximum(i, blocks) - blocks
    whole = lambda arr: pl.BlockSpec(arr.shape, lambda i, c: (0, 0))
    here = lambda n: pl.BlockSpec((block, n), lambda i, c: (at(i), 0))
    rows = pl.BlockSpec((block, q.shape[1]), lambda i, c: ((1 - c[0]) * 2 + later(i), 0))
    return pl.pallas_call(
        functools.partial(attention_weight_kernel, blocks),
        grid_spec=pltpu.PrefetchScalarGridSpec(
            num_scalar_prefetch=1,
            grid=(blocks + 2,),
            in_specs=[
                pl.BlockSpec((SEQ, block), lambda i, c: (0, at(i))),
                whole(q), whole(k), whole(v), here(2 * TILE), whole(weight), rows, rows, rows,
            ],
            out_specs=[here(6 * TILE), here(5 * TILE), pl.BlockSpec((block, width), lambda i, c: (later(i), 0))],
        ),
        out_shape=[
            jax.ShapeDtypeStruct((width, 6 * TILE), BF),
            jax.ShapeDtypeStruct((width, 5 * TILE), F32),
            jax.ShapeDtypeStruct((2 * block, width), F32),
        ],
        compiler_params=pltpu.CompilerParams(vmem_limit_bytes=40 * MIB),
        cost_estimate=SMALL_COST,
        name="attention_weight_grads",
    )(core, normed, q, k, v, output, weight, q, k, v)


def both_kernel(
    lane, micro_ref, core_ref, length_ref, weight_ref, q, k, v, got_ref, tokens_ref, gain_ref, grad_ref,
    info_ref, residual_ref, own_ref, far_ref, out_ref, extra_ref, acc_ref,
):
    block = residual_ref.shape[0]
    info = jnp.transpose(info_ref[...])
    place = lax.broadcasted_iota(jnp.int32, (block, 1), 0) + (core_ref[0] * 2 + pl.program_id(0)) * block
    rows = residual_ref[...] + picked_rows(info[:, 6:7], info[:, 7:8], (own_ref[...], far_ref[...]))
    out_ref[0] = jnp.where(place < length_ref[0], rows, 0.0).astype(BF)
    normed_grad = got_ref[...] + projected_back(weight_ref, (q, k, v))
    x = tokens_ref[0].astype(F32)
    inverse = lax.rsqrt(jnp.mean(x * x, axis=-1, keepdims=True) + 1e-06)
    plain = x * inverse
    scaled = normed_grad * gain_ref[...]
    mean = jnp.mean(scaled * plain, axis=-1, keepdims=True)
    out_ref[1] = (grad_ref[...] + inverse * (scaled - plain * mean)).astype(BF)
    wide = lax.broadcasted_iota(jnp.int32, (1, TILE), 1)
    part = folded(normed_grad * plain)

    @pl.when(pl.program_id(0) == 0)
    def _():
        acc_ref[...] = part

    @pl.when(pl.program_id(0) == 1)
    def _():
        extra_ref[...] = jnp.where(wide == lane, as_column(acc_ref[...] + part), 0.0)


def both_rows(lane, micro, core, length, weight, grads, got, layer_input, gain, residual_grad, info, residual, own, far):
    width = weight.shape[0]
    block = 256
    here = lambda n: pl.BlockSpec((block, n), lambda i, m, c, *_: (c[0] * 2 + i, 0))
    whole = lambda arr: pl.BlockSpec(arr.shape, lambda i, *_: (0, 0))
    return pl.pallas_call(
        functools.partial(both_kernel, lane),
        grid_spec=pltpu.PrefetchScalarGridSpec(
            num_scalar_prefetch=3,
            grid=(2,),
            in_specs=[whole(weight)]
            + [here(grads[0].shape[1])] * 3
            + [
                pl.BlockSpec((block, width), lambda i, *_: (i, 0)),
                pl.BlockSpec((1, block, width), lambda i, m, c, *_: (m[0], c[0] * 2 + i, 0)),
                whole(gain),
                here(width),
                pl.BlockSpec((8, block), lambda i, m, c, *_: (0, c[0] * 2 + i)),
                here(width),
                whole(own),
                whole(far),
            ],
            out_specs=[
                pl.BlockSpec((2, block, width), lambda i, *_: (0, i, 0)),
                pl.BlockSpec((width, TILE), lambda i, *_: (0, 0)),
            ],
            scratch_shapes=[pltpu.VMEM((8, width), F32)],
        ),
        out_shape=[jax.ShapeDtypeStruct((2, 2 * block, width), BF), jax.ShapeDtypeStruct((width, TILE), F32)],
        compiler_params=pltpu.CompilerParams(vmem_limit_bytes=40 * MIB),
        cost_estimate=SMALL_COST,
        name="both_rows",
    )(micro, core, length, weight, *grads, got, layer_input, gain, residual_grad, info, residual, own, far)


def sum_kernel(kept, own, got, out_own, early, late, late_far, table, sum_ref):
    low = low_lanes(early.shape)
    sum_ref[:, : 4 * TILE] = (own[:, : 4 * TILE] + got[:, : 4 * TILE].astype(F32)).astype(BF)
    mixed = jnp.where(low, own[:, 4 * TILE :], turned(out_own[:, TILE:]))
    sum_ref[:, 4 * TILE : 5 * TILE] = (mixed + got[:, 4 * TILE : 5 * TILE].astype(F32)).astype(BF)
    sum_ref[:, 5 * TILE : 6 * TILE] = (out_own[:, :TILE] + got[:, 5 * TILE :].astype(F32)).astype(BF)
    extra = early[...] + late[...] + late_far[...] + table[...]
    high = extra.astype(BF)
    rest = extra - high.astype(F32)
    if kept <= HEAD_DIM:
        sum_ref[:, 6 * TILE :] = jnp.where(low, high.astype(F32), turned(rest)).astype(BF)
    else:
        sum_ref[:, 6 * TILE : 7 * TILE] = high
        sum_ref[:, 7 * TILE :] = rest.astype(BF)


def packed_sums(kept, *parts):
    width = parts[0].shape[0]
    cols = (7 if kept <= HEAD_DIM else 8) * TILE
    block = 256
    here = lambda n: pl.BlockSpec((block, n), lambda i: (i, 0))
    return pl.pallas_call(
        functools.partial(sum_kernel, kept),
        grid=(width // block,),
        in_specs=[here(x.shape[1]) for x in parts],
        out_specs=here(cols),
        out_shape=jax.ShapeDtypeStruct((width, cols), BF),
        compiler_params=pltpu.CompilerParams(vmem_limit_bytes=40 * MIB),
        cost_estimate=SMALL_COST,
        name="packed_sums",
    )(*parts)


def final_kernel(kept, parts_ref, q_ref, k_ref, v_ref, o_ref, small_ref):
    total = parts_ref[0].astype(F32)
    for n in range(1, parts_ref.shape[0]):
        total = total + parts_ref[n].astype(F32)
    tile = lambda t: total[:, t * TILE : (t + 1) * TILE]
    q_ref[:, :TILE] = tile(0)
    q_ref[:, TILE:] = tile(3)[:, :HEAD_DIM]
    k_ref[:, :TILE] = tile(1)
    k_ref[:, TILE:] = turned(tile(3))[:, :HEAD_DIM]
    v_ref[:, :TILE] = tile(2)
    v_ref[:, TILE:] = tile(4)[:, :HEAD_DIM]
    o_ref[:, :TILE] = tile(5)
    o_ref[:, TILE:] = turned(tile(4))[:, :HEAD_DIM]
    small_ref[...] = tile(6) + (turned(tile(6)) if kept <= HEAD_DIM else tile(7))


def final_sums(kept, parts, shard):
    rows = parts.shape[1]
    return pl.pallas_call(
        functools.partial(final_kernel, kept),
        out_shape=[jax.ShapeDtypeStruct((rows, shard), F32)] * 4 + [jax.ShapeDtypeStruct((rows, TILE), F32)],
        compiler_params=pltpu.CompilerParams(vmem_limit_bytes=40 * MIB),
        cost_estimate=SMALL_COST,
        name="final_sums",
    )(parts)


def pair_gate(logits, own, other):
    lanes = lax.broadcasted_iota(jnp.int32, logits.shape, 1)
    gap = jnp.sum(
        jnp.where(lanes == own, logits, 0.0) - jnp.where(lanes == other, logits, 0.0), axis=1, keepdims=True
    )
    small = jnp.exp(-jnp.abs(gap))
    return jnp.where(gap >= 0.0, 1.0, small) / (1.0 + small)


def expert_kernel(lead, chunk, half, me_ref, partner_ref, rows_ref, grads_ref, router_ref, *refs):
    before, refs = (refs[0], refs[1:]) if lead is not None and lead > 0 else (None, refs)
    plain_ref, firsts = refs[0], refs[1:5]
    back_ref, active_ref, slope_ref, gated_ref, gate_ref, mass_ref = refs[5:]
    rows = rows_ref[...]
    grads = grads_ref[...]
    partner = jnp.transpose(jnp.broadcast_to(partner_ref[0], (8, rows.shape[0])))[:, :1]
    gate = pair_gate(dot(rows, router_ref[...]), me_ref[0], partner)
    gated_ref[...] = (gate * grads.astype(F32)).astype(BF)
    gate_ref[...] = jnp.broadcast_to(gate, gate_ref.shape)
    masses = [None] * (rows.shape[0] // STRIP)
    back = None
    width = firsts[0].shape[1]
    step = 256
    places = [(r, c) for r in range(4) for c in range(0, width, step)]

    def products(r, c):
        return dot(rows, firsts[r][:, c : c + step])

    ahead = products(*places[0])
    for n, (r, c) in enumerate(places):
        x = ahead
        if n + 1 < len(places):
            ahead = products(*places[n + 1])
        place = slice(r * width + c, r * width + c + step)
        for at in range(0, rows.shape[0], STRIP):
            strip = slice(at, at + STRIP)
            value, flow = x[strip], plain_ref[strip, place].astype(F32)
            square = value * value
            bent = jnp.tanh(value * (GELU_C + (GELU_C * GELU_A) * square))
            rise = 0.5 + 0.5 * bent
            active = value * rise
            slope = rise + active * (1.0 - bent) * (GELU_C + (3.0 * GELU_C * GELU_A) * square)
            low = active.astype(BF)
            active_ref[strip, place] = low
            slope_ref[strip, place] = (gate[strip] * flow * slope).astype(BF)
            part = low.astype(F32) * flow
            masses[at // STRIP] = put(masses[at // STRIP], part[:, :TILE] + part[:, TILE:])
        if c + step == width and r > 0:
            back = put(back, dot(slope_ref[:, (r - 1) * width : r * width], firsts[r - 1][...], NT))
    back = put(back, dot(slope_ref[:, 3 * width :], firsts[3][...], NT))
    back = back.astype(BF)
    mass = jnp.sum(jnp.concatenate(masses, 0), axis=1, keepdims=True)
    if lead is None:
        back_ref[...] = back
        mass_ref[...] = jnp.broadcast_to(mass, mass_ref.shape)
        return
    count = rows.shape[0] // chunk
    number = lax.broadcasted_iota(jnp.int32, (rows.shape[0], 1), 0)
    lanes = lax.broadcasted_iota(jnp.int32, (1, rows.shape[1]), 1)
    inside = lax.rem(number, chunk)
    spread = jnp.zeros(rows.shape, F32)
    for piece in range(3):
        high = mass.astype(BF).astype(F32)
        spread = jnp.where(lanes == piece * half + lead + inside, high, spread)
        mass = mass - high
    own = jnp.where(number // chunk == lax.broadcasted_iota(jnp.int32, (1, TILE), 1), 1.0, 0.0).astype(BF)
    line = dot(own, spread.astype(BF), TN)
    if before is None:
        back_ref[...] = back
        for e in range(count):
            mass_ref[e] = line[e : e + 1].astype(BF)
    else:
        back_ref[:, :chunk] = back.reshape(count, chunk, back.shape[1])
        row = lax.broadcasted_iota(jnp.int32, (16, 1), 0)
        for e in range(count):
            both = line[e : e + 1] + before[e].astype(F32)
            back_ref[e, chunk:] = jnp.where(row == 0, both, 0.0).astype(BF)


def row_block(total):
    return 320 if total % 320 == 0 else total


def plain_kernel(grads_ref, b0, b1, b2, b3, out_ref):
    width = b0.shape[0]
    for r, second in enumerate((b0, b1, b2, b3)):
        out_ref[:, r * width : (r + 1) * width] = dot(grads_ref[...], second[...], NT).astype(BF)


def plain_grads(grads, seconds):
    total, width = grads.shape
    hidden = sum(w.shape[0] for w in seconds)
    block = row_block(total)
    here = lambda cols: pl.BlockSpec((block, cols), lambda i: (i, 0))
    return pl.pallas_call(
        plain_kernel,
        grid=(total // block,),
        in_specs=[here(width)] + [pl.BlockSpec(w.shape, lambda i: (0, 0)) for w in seconds],
        out_specs=here(hidden),
        out_shape=jax.ShapeDtypeStruct((total, hidden), BF),
        compiler_params=pltpu.CompilerParams(vmem_limit_bytes=56 * MIB),
        cost_estimate=SMALL_COST,
        name="plain_grads",
    )(grads, *seconds)


def expert_rows_pass(lead, chunk, half, me, partner, rows, grads, plain, router, before, firsts, number):
    total, width = rows.shape
    block = row_block(total)
    steps = total // block
    experts = total // chunk
    hidden = sum(f.shape[1] for f in firsts)
    here = lambda cols: pl.BlockSpec((block, cols), lambda i: (i, 0))
    there = lambda cols: pl.BlockSpec((block, cols), lambda i: (number * steps + i, 0))
    whole = lambda arr: pl.BlockSpec(arr.shape, lambda i: (0, 0))
    lines = pl.BlockSpec((block // chunk, 1, width), lambda i: (i, 0, 0))
    back_shape, back_spec = (total, width), here(width)
    mass_shape, mass_spec, mass_kind = (experts, 1, width), lines, BF
    if lead is None:
        mass_shape, mass_spec, mass_kind = (total, TILE), here(TILE), F32
    elif before is not None:
        back_shape = (experts, chunk + 16, width)
        back_spec = pl.BlockSpec((block // chunk, chunk + 16, width), lambda i: (i, 0, 0))
    return pl.pallas_call(
        functools.partial(expert_kernel, lead, chunk, half),
        grid=(steps,),
        in_specs=[
            pl.BlockSpec(memory_space=pltpu.SMEM),
            pl.BlockSpec((1, 1, block), lambda i: (number * steps + i, 0, 0)),
            here(width), there(width), whole(router),
        ]
        + ([lines] if before is not None else [])
        + [there(hidden)]
        + [whole(w) for w in firsts],
        out_specs=[back_spec, here(hidden), here(hidden), here(width), here(TILE), mass_spec],
        out_shape=[
            jax.ShapeDtypeStruct(back_shape, BF),
            jax.ShapeDtypeStruct((total, hidden), BF),
            jax.ShapeDtypeStruct((total, hidden), BF),
            jax.ShapeDtypeStruct((total, width), BF),
            jax.ShapeDtypeStruct((total, TILE), F32),
            jax.ShapeDtypeStruct(mass_shape, mass_kind),
        ],
        compiler_params=pltpu.CompilerParams(vmem_limit_bytes=56 * MIB),
        cost_estimate=SMALL_COST,
        name="expert_rows",
    )(me, partner, rows, grads, router, *([before] if before is not None else []), plain, *firsts)


def weight_parts(count, refs):
    rows, slopes, active, gated = (refs[n * count : (n + 1) * count] for n in range(4))
    first, second = None, None
    for n in range(count):
        first = put(first, dot(rows[n][...], slopes[n][...], TN))
        second = put(second, dot(active[n][...], gated[n][...], TN))
    return first, second


def cross_kernel(count, *refs):
    first, second = weight_parts(count, refs)
    refs[-1][0, 0] = first.astype(BF)
    refs[-1][0, 1] = second.astype(BF)


def kept_kernel(count, *refs):
    got_ref, far_ref, kept_ref = refs[-3:]
    first, second = weight_parts(count, refs)
    first = first + got_ref[0, 0].astype(F32)
    second = second + got_ref[0, 1].astype(F32)

    @pl.when(pl.program_id(0) == 0)
    def _():
        far_ref[0] = first.astype(BF)
        far_ref[1] = second.astype(BF)

    @pl.when(pl.program_id(0) == 1)
    def _():
        kept_ref[0] = first
        kept_ref[1] = second


def weight_specs(rows, slopes, quarter):
    total, width = rows[0].shape
    hidden = slopes[0].shape[1] // 4
    whole = pl.BlockSpec((total, width), lambda i: (0, 0))
    part = pl.BlockSpec((total, hidden), lambda i: (0, quarter(i)))
    count = len(rows)
    return width, hidden, [whole] * count + [part] * (2 * count) + [whole] * count


def cross_weight_grads(rows, slopes, active, gated):
    width, hidden, specs = weight_specs(rows, slopes, lambda i: 2 + i)
    return pl.pallas_call(
        functools.partial(cross_kernel, len(rows)),
        grid=(2,),
        in_specs=specs,
        out_specs=pl.BlockSpec((1, 2, width, hidden), lambda i: (i, 0, 0, 0)),
        out_shape=jax.ShapeDtypeStruct((2, 2, width, hidden), BF),
        compiler_params=pltpu.CompilerParams(vmem_limit_bytes=56 * MIB),
        cost_estimate=SMALL_COST,
        name="cross_weight_grads",
    )(*rows, *slopes, *active, *gated)


def kept_weight_grads(rows, slopes, active, gated, got):
    width, hidden, specs = weight_specs(rows, slopes, lambda i: 1 - i)
    fixed = pl.BlockSpec((2, width, hidden), lambda i: (0, 0, 0))
    return pl.pallas_call(
        functools.partial(kept_kernel, len(rows)),
        grid=(2,),
        in_specs=specs + [pl.BlockSpec((1, 2, width, hidden), lambda i: (1 - i, 0, 0, 0))],
        out_specs=[fixed, fixed],
        out_shape=[
            jax.ShapeDtypeStruct((2, width, hidden), BF),
            jax.ShapeDtypeStruct((2, width, hidden), F32),
        ],
        compiler_params=pltpu.CompilerParams(vmem_limit_bytes=56 * MIB),
        cost_estimate=SMALL_COST,
        name="kept_weight_grads",
    )(*rows, *slopes, *active, *gated, got)


def result_kernel(chunks, *refs):
    active, gates, seconds, out_ref = refs[:chunks], refs[chunks : 2 * chunks], refs[2 * chunks : -1], refs[-1]
    for c in range(chunks):

        @pl.when(pl.program_id(0) == c)
        def _(c=c):
            width = seconds[0].shape[0]
            total = None
            for r, second in enumerate(seconds):
                total = put(total, dot(active[c][:, r * width : (r + 1) * width], second[...]))
            rows = (total * gates[c][:, :1]).astype(BF)
            if chunks > 1:
                out_ref[:, 0] = rows.reshape(out_ref.shape[0], out_ref.shape[2], out_ref.shape[3])
            else:
                out_ref[...] = rows


def expert_results(active, gates, seconds, experts):
    chunks = len(active)
    total, hidden = active[0].shape
    width = seconds[0].shape[1]
    block = row_block(total)
    steps = total // block

    def here(c, cols):
        return pl.BlockSpec((block, cols), lambda g, i: (jnp.where(g == c, i, jnp.where(g < c, 0, steps - 1)), 0))

    chunk = total // experts
    if chunks > 1:
        shape = (experts, chunks, chunk, width)
        out_spec = pl.BlockSpec((block // chunk, 1, chunk, width), lambda g, i: (i, g, 0, 0))
    else:
        shape = (total, width)
        out_spec = pl.BlockSpec((block, width), lambda g, i: (i, 0))
    out = pl.pallas_call(
        functools.partial(result_kernel, chunks),
        grid=(chunks, steps),
        in_specs=[here(c, hidden) for c in range(chunks)]
        + [here(c, TILE) for c in range(chunks)]
        + [pl.BlockSpec(w.shape, lambda g, i: (0, 0)) for w in seconds],
        out_specs=out_spec,
        out_shape=jax.ShapeDtypeStruct(shape, BF),
        compiler_params=pltpu.CompilerParams(vmem_limit_bytes=56 * MIB),
        cost_estimate=SMALL_COST,
        name="expert_results",
    )(*active, *gates, *seconds)
    return out.reshape(experts, chunks * chunk, width)


def last_sum_kernel(kept_ref, y_ref, out_first, out_second):
    for n, out in enumerate((out_first, out_second)):
        out[...] = kept_ref[n] + y_ref[n].astype(F32)


def last_sums(kept, got_y):
    _, width, hidden = kept.shape
    block = 256
    here = pl.BlockSpec((block, hidden), lambda i: (i, 0))
    part = pl.BlockSpec((2, block, hidden), lambda i: (0, i, 0))
    return pl.pallas_call(
        last_sum_kernel,
        grid=(width // block,),
        in_specs=[part, part],
        out_specs=[here, here],
        out_shape=[jax.ShapeDtypeStruct((width, hidden), F32)] * 2,
        compiler_params=pltpu.CompilerParams(vmem_limit_bytes=40 * MIB),
        cost_estimate=SMALL_COST,
        name="last_sums",
    )(kept, got_y)


def send_kernel(micro_ref, code_ref, rows_ref, out_ref):
    block = out_ref.shape[0]
    ids = lax.broadcasted_iota(jnp.int32, (block, 1), 0) + pl.program_id(0) * block
    hot = jnp.where((ids == code_ref[:1]) | (ids == code_ref[1:2]), 1.0, 0.0).astype(BF)
    out_ref[...] = dot(hot, rows_ref[0]).astype(BF)


def send_rows(micro, code, rows, count):
    width = rows.shape[2]
    block = next(b for b in (336, 320, 384, count) if count % b == 0)
    return pl.pallas_call(
        send_kernel,
        grid_spec=pltpu.PrefetchScalarGridSpec(
            num_scalar_prefetch=1,
            grid=(count // block,),
            in_specs=[
                pl.BlockSpec(code.shape, lambda i, m: (0, 0)),
                pl.BlockSpec((1, SEQ, width), lambda i, m: (m[0], 0, 0)),
            ],
            out_specs=pl.BlockSpec((block, width), lambda i, m: (i, 0)),
        ),
        out_shape=jax.ShapeDtypeStruct((count, width), BF),
        compiler_params=pltpu.CompilerParams(vmem_limit_bytes=40 * MIB),
        cost_estimate=SMALL_COST,
        name="send_rows",
    )(micro, code, rows)


def place_kernel(place_ref, *refs):
    for n, piece in enumerate(refs[:4]):

        @pl.when(pl.program_id(0) == n)
        def _(piece=piece):
            for k, out_ref in enumerate(refs[4:]):
                out_ref[0] = piece[k]


def place_pieces(places, pieces):
    two, rows, width = pieces[0].shape
    whole = pl.BlockSpec(pieces[0].shape, lambda i, place_ref: (0, 0, 0))
    return pl.pallas_call(
        place_kernel,
        grid_spec=pltpu.PrefetchScalarGridSpec(
            num_scalar_prefetch=1,
            grid=(4,),
            in_specs=[whole] * 4,
            out_specs=[pl.BlockSpec((1, rows, width), lambda i, place_ref: (place_ref[i], 0, 0))] * two,
        ),
        out_shape=[jax.ShapeDtypeStruct((4, rows, width), pieces[0].dtype)] * two,
        compiler_params=pltpu.CompilerParams(vmem_limit_bytes=40 * MIB),
        cost_estimate=SMALL_COST,
        name="place_pieces",
    )(places, *pieces)


def swap(value, axis, count, bit):
    return lax.ppermute(value, axis, [(i, i ^ bit) for i in range(count)])


def all_to_all(value):
    return lax.all_to_all(value, "dp", split_axis=0, concat_axis=0, tiled=True)


def together(*values):
    return lax.optimization_barrier(values)


def local(
    layer_input, out_grad, first_gain, query_weight, key_weight, value_weight, output_weight,
    position_bias, second_gain, router_weight, expert_in, expert_out, seq_lengths, routes,
):
    micro_count, tok_rows, width = layer_input.shape
    dp_count = lax.axis_size("dp")
    expert_count = router_weight.shape[1]
    shard = query_weight.shape[1]
    heads_here = position_bias.shape[0]
    assert lax.axis_size("tensor") == 4 and micro_count == 2 and expert_count == dp_count
    assert tok_rows == SEQ and seq_lengths.shape[1] == 1
    capacity = max(8, 8 * (10 * tok_rows // (32 * expert_count)))
    half = capacity // 2
    stride = 8 * (half // 8 + 1)
    by_lines = dp_count == 8
    chunks = 2 if half % 32 == 0 else 1
    chunk = half // chunks
    chunk_rows = expert_count * chunk
    rows_here = query_weight.shape[0]
    me = lax.axis_index("dp")
    rank = lax.axis_index("tensor")
    micro = rank // 2
    core = rank % 2

    def swap_y(value):
        return swap(value, "tensor", 4, 2)

    def swap_core(value):
        return swap(value, "tensor", 4, 1)

    micro_arg = micro.reshape(1).astype(jnp.int32)
    core_arg = core.reshape(1).astype(jnp.int32)

    packed = pack_weights(query_weight, key_weight, value_weight, output_weight, first_gain, second_gain, router_weight)
    three = 3 * TILE

    def doubled(stacked, bit, axis=0):
        other = swap(stacked, "dp", dp_count, bit)
        high = (me & bit) != 0
        pair = jnp.where(high, jnp.stack([other, stacked], axis + 1), jnp.stack([stacked, other], axis + 1))
        return pair.reshape(stacked.shape[:axis] + (-1,) + stacked.shape[axis + 1 :])

    stacked = packed[None]
    bit = dp_count // 2
    while bit > 1:
        stacked = doubled(stacked, bit)
        bit //= 2
    length = lax.dynamic_index_in_dim(seq_lengths, micro, 0, keepdims=False)
    route = lax.dynamic_index_in_dim(routes, micro, 0, keepdims=False).T
    expert_ids = jnp.arange(expert_count, dtype=jnp.int32)
    named = (expert_ids[:, None, None] == route[None]).astype(jnp.int32)
    per_token = jnp.sum(named, axis=1, dtype=jnp.int32)
    earlier = jnp.cumsum(per_token, axis=1, dtype=jnp.int32) - per_token
    slot = jnp.sum(named * earlier[:, None, :], axis=0, dtype=jnp.int32)
    here = slot // half == core
    within = slot % half
    chunk_of = within // chunk
    inside = within % chunk
    spare = 16 * -(-chunk // 16)
    last_stride = spare + 16
    last = (chunks - 1) * chunk_rows
    code_back = jnp.where(
        chunk_of == chunks - 1, last + route * last_stride + inside, chunk_of * chunk_rows + route * chunk + inside
    )
    code_back = code_back + jnp.where(here, 0, last + expert_count * last_stride)
    code_result = route * half + within + jnp.where(here, 0, expert_count * half)
    info = jnp.concatenate([code_back, route, slot, code_result], 0)

    code_grads = jnp.where(here, route * stride + within, -1)
    valid = jnp.arange(SEQ, dtype=jnp.int32) < length[0]
    ids = jnp.arange(expert_count * stride, dtype=jnp.int32)[:, None]
    partner = jnp.sum(
        jnp.where(ids == code_grads[:1], route[1:], 0) + jnp.where(ids == code_grads[1:], route[:1], 0), axis=1, dtype=jnp.int32
    )
    grads_sent = send_rows(micro_arg, jnp.where(valid[None], code_grads, -1), out_grad, expert_count * stride)
    grads_sent = grads_sent.reshape(expert_count, stride, width)
    partner_row = jnp.pad(partner.reshape(expert_count, stride)[:, :half].astype(BF), ((0, 0), (0, width - half)))
    grads_sent = grads_sent.at[:, half].set(partner_row)
    stacked, grads_sent, position_bias = together(stacked, grads_sent, position_bias)
    if by_lines:
        lines = [list(range(x, dp_count, 2)) for x in range(2)]
        grads_z = lax.all_to_all(
            grads_sent.reshape(dp_count // 2, 2, stride, width), "dp", split_axis=0, concat_axis=0,
            axis_index_groups=lines, tiled=True,
        )

    first_own = expert_in[0]
    second_own = expert_out[0]
    part_b = stacked[:, :, :three]
    far_b = swap_y(part_b)
    part_a = doubled(stacked[:, :, three:], 1)
    part_a, far_b = together(part_a, far_b)
    pair_b = jnp.stack([part_b, far_b])
    a_own = part_a[:, :, :three]
    a_far = swap_y(a_own).reshape(width, three)
    a_own = a_own.reshape(width, three)
    pair_b = doubled(pair_b, 1, 1).reshape(2, width, three)
    if by_lines:
        a_far, pair_b, second_own = together(a_far, pair_b, second_own)
    else:
        a_far, pair_b, grads_sent, second_own = together(a_far, pair_b, grads_sent, second_own)
    second_y = swap_y(second_own)
    small_all = part_a[:, :, three:].reshape(width, TILE)
    gain_one = small_all[:, expert_count].astype(F32)[None]
    gain_two = small_all[:, expert_count + 1].astype(F32)[None]
    router_wide = small_all
    far_bias = swap_y(position_bias)
    bias = jnp.concatenate([position_bias[:2], far_bias[:2], position_bias[2:], far_bias[2:]], 0)
    head_total = bias.shape[0]
    hot_const = jnp.asarray(NEAR_HOT, dtype=BF)
    near = dot(bias, hot_const) - bias[:, NB - 1 :].astype(F32)
    near = near.reshape(head_total, 2, TILE, TILE)
    places = jnp.arange(TILE, dtype=jnp.int32)
    causal = jnp.stack([places[None, :] <= places[:, None], jnp.ones((TILE, TILE), bool)])
    near = jnp.where(causal[None], near, NEG)

    if by_lines:
        high = (me & 1) != 0
    else:
        grads_here = all_to_all(grads_sent)

    qkv, normed_one, qkv_weight, output_own = norm_and_project(
        micro_arg, layer_input, gain_one, a_own, a_far, pair_b[0], pair_b[1]
    )
    output_far = swap_core(output_own)
    mixed, logs = attend(length, qkv, near)
    mixed, output_far = together(mixed, output_far)
    mixed_far = swap_core(mixed)
    code_chunks = jnp.where(here, chunk_of * chunk_rows + route * chunk + inside, -1)
    if by_lines:
        sent_x = lax.dynamic_index_in_dim(grads_z, 1 - (me & 1), 1, keepdims=False)
        mixed_far, grads_z, sent_x = together(mixed_far, grads_z, sent_x)
        got_x = swap(sent_x, "dp", dp_count, 1)
    residual, *parts = residual_and_rows(
        micro_arg, layer_input, mixed, mixed_far, output_own, output_far, gain_two, code_chunks, chunk_rows, chunks
    )

    if by_lines:
        second_core = swap_core(second_own)
        parts, grads_z, second_y, first_own, second_core = together(parts, grads_z, second_y, first_own, second_core)
        kept_x = jnp.where(high, grads_z[:, 1], grads_z[:, 0])
        pair_x = jnp.where(high, jnp.stack([got_x, kept_x], 1), jnp.stack([kept_x, got_x], 1))
        grads_here = pair_x.reshape(dp_count, stride, width)
    else:
        second_core = swap_core(second_own)
        parts, grads_here, second_y, first_own, second_core = together(
            parts, grads_here, second_y, first_own, second_core
        )
    parts = [part.reshape(expert_count, chunk, width) for part in parts]
    arrived = [all_to_all(parts[0])]
    first_y = swap_y(first_own)
    first_core = swap_core(first_own)

    def by_chunk(rows):
        return jnp.swapaxes(rows.reshape((expert_count, chunks, chunk) + rows.shape[2:]), 0, 1)

    grads_all = by_chunk(grads_here[:, :half]).reshape(chunks * chunk_rows, width)
    block = row_block(chunk_rows)
    partner_all = by_chunk(grads_here[:, half, :half].astype(jnp.int32)).reshape(chunks * chunk_rows // block, 1, block)
    seconds = (second_own, second_y, second_core, swap_core(second_y))
    arrived[0], grads_all, partner_all, first_core = together(arrived[0], grads_all, partner_all, first_core)
    plain = plain_grads(grads_all, seconds)
    for c in range(1, chunks):
        sent, arrived[-1] = together(parts[c], arrived[-1])
        arrived.append(all_to_all(sent))

    firsts = (first_own, first_y, first_core, swap_core(first_y))
    me_arg = me.reshape(1).astype(jnp.int32)
    rows_all, slopes, active, gated, gates, backs = [], [], [], [], [], []
    line = None
    for c in range(chunks):
        rows_c = arrived[c].reshape(chunk_rows, width)
        back, act, slo, gat, gte, line = expert_rows_pass(
            c * chunk if chunks > 1 else None, chunk, half, me_arg, partner_all, rows_c, grads_all, plain, router_wide, line,
            firsts, c,
        )
        rows_all.append(rows_c)
        slopes.append(slo)
        active.append(act)
        gated.append(gat)
        gates.append(gte)
        if chunks == 1:
            gate_grad = line[:, 0].reshape(expert_count, chunk)
            pieces = []
            for _ in range(3):
                piece = gate_grad.astype(BF)
                pieces.append(piece)
                gate_grad = gate_grad - piece.astype(F32)
            gate_row = jnp.pad(jnp.concatenate(pieces, 1), ((0, 0), (0, width - 3 * half)))
            back = jnp.pad(back.reshape(expert_count, chunk, width), ((0, 0), (0, last_stride - chunk), (0, 0)))
            back = back.at[:, spare].set(gate_row)
        if c + 1 < chunks:
            back, arrived[c + 1] = together(back.reshape(expert_count, chunk, width), arrived[c + 1])
        else:
            back, rows_all[-1], backs = together(back, rows_all[-1], backs)
        backs.append(all_to_all(back))
    grads_cross = cross_weight_grads(rows_all, slopes, active, gated)
    gates, grads_cross = together(gates, grads_cross)
    grads_in = swap_core(grads_cross)
    results = expert_results(active, gates, seconds, expert_count)
    results, grads_in = together(results, grads_in)
    grads_far, grads_kept = kept_weight_grads(rows_all, slopes, active, gated, grads_in)
    backs[-1], results, grads_far = together(backs[-1], results, grads_far)

    across_y = swap_y(grads_far)
    results_own = all_to_all(results).reshape(expert_count * half, width)

    backs_far = [swap_core(b) for b in backs]
    residual_grad, mixed_grad, extra_early, output_sent, output_kept = combine(
        micro_arg, core_arg, length, info, out_grad, residual, mixed, gain_two, router_wide, output_own,
        backs + backs_far, half, spare,
    )

    dq, dk, dv, tiles, sums = attend_back(length, qkv, near, mixed, logs, mixed_grad, 0, head_total // 2)
    far_sent, own_parts, sent = attention_weight_grads(core_arg, normed_one, dq, dk, dv, output_sent, qkv_weight)
    far_got = swap_y(far_sent)
    sent, results_own = together(sent, results_own)
    got = swap_core(sent)
    rows_both, extra_late = both_rows(
        expert_count, micro_arg, core_arg, length, qkv_weight, (dq, dk, dv), got, layer_input, gain_one, residual_grad,
        info, residual, results_own, swap_core(results_own),
    )
    rows_both, across_y, tiles = together(rows_both, across_y, tiles)
    late_far = swap_core(extra_late)
    corner = micro * 2 + core
    corners = jnp.stack([corner, corner ^ 1, corner ^ 2, corner ^ 3]).astype(jnp.int32)
    rows_y = swap_y(rows_both)
    expert_in_grad, expert_out_grad = last_sums(grads_kept, across_y)
    rows_y, expert_in_grad, expert_out_grad = together(rows_y, expert_in_grad, expert_out_grad)
    pieces = (rows_both, swap_core(rows_both), rows_y, swap_core(rows_y))

    tiles = tiles.reshape(head_total, 2 * TILE * TILE)
    tiles_high = tiles.astype(BF)
    tiles_rest = (tiles - tiles_high.astype(F32)).astype(BF)
    table = dot(tiles_high, hot_const, NT) + dot(tiles_rest, hot_const, NT)
    far_sum = jnp.sum(sums[:, :, 0], axis=1) - jnp.sum(table[:, : NB - 1], axis=1)
    table = jnp.concatenate([table[:, : NB - 1], far_sum[:, None]], 1)
    table_own = jnp.concatenate([table[0:2], table[4:5]], 0)
    table_far = jnp.concatenate([table[2:4], table[5:6]], 0)
    table_cols = heads_here * NB // rows_here
    table_both = jnp.concatenate([table_own.reshape(rows_here, table_cols), table_far.reshape(rows_here, table_cols)], 1)
    base = expert_count + 2
    kept = base + 2 * table_cols
    table_tile = jnp.tile(jnp.pad(table_both, ((0, 0), (base, TILE - kept))), (dp_count, 1))

    grads = packed_sums(kept, own_parts, far_got, output_kept, extra_early, extra_late, late_far, table_tile)
    arrived_grads = all_to_all(grads.reshape(dp_count, rows_here, grads.shape[1]))
    layer_output, input_grad = (out.reshape(2, SEQ, width) for out in place_pieces(corners, pieces))
    arrived_grads, layer_output, input_grad = together(arrived_grads, layer_output, input_grad)
    query_grad, key_grad, value_grad, output_grad, small = final_sums(kept, arrived_grads, shard)
    small_y = swap_y(small)
    both = small + small_y
    table_sum = small[:, base : base + table_cols] + small_y[:, base + table_cols : kept]
    return (
        layer_output,
        input_grad,
        both[:, expert_count],
        query_grad,
        key_grad,
        value_grad,
        output_grad.T,
        table_sum.reshape(heads_here, NB),
        both[:, expert_count + 1],
        both[:, :expert_count],
        expert_in_grad[None],
        expert_out_grad[None],
    )


def solution(mesh):
    return jax.shard_map(
        local,
        mesh=mesh,
        in_specs=(
            P(None, "dp", None),
            P(None, "dp", None),
            P("dp"),
            P("dp", "tensor"),
            P("dp", "tensor"),
            P("dp", "tensor"),
            P("tensor", "dp"),
            P("tensor", None),
            P("dp"),
            P("dp", None),
            P("dp", None, "tensor"),
            P("dp", "tensor", None),
            P(None, "dp"),
            P(None, "dp", None),
        ),
        out_specs=(
            P(None, "dp", None),
            P(None, "dp", None),
            P("dp"),
            P("dp", "tensor"),
            P("dp", "tensor"),
            P("dp", "tensor"),
            P("tensor", "dp"),
            P("tensor", None),
            P("dp"),
            P("dp", None),
            P("dp", None, "tensor"),
            P("dp", "tensor", None),
        ),
        check_vma=False,
    )
```

```python
import functools

import jax
import jax.numpy as jnp
import numpy as np
from jax import lax
from jax.experimental import pallas as pl
from jax.experimental.pallas import tpu as pltpu
from jax.sharding import PartitionSpec as P

HEAD_DIM = 64
NB = 32
SEQ = 1024
TILE = 128
QROWS = 256
NEG = -1e30
GELU_C = 0.7978845608028654
GELU_A = 0.044715

BF = jnp.bfloat16
F32 = jnp.float32

bucket_edges = np.ceil(16.0 * 8.0 ** (np.arange(1, 16) / 16.0)).astype(np.int32)


def near_tables():
    rows = np.arange(TILE)[:, None]
    cols = np.arange(TILE)[None, :]
    hots = []
    for shift in (0, TILE):
        distance = rows - cols + shift
        clipped = np.maximum(distance, 0)
        reached = np.sum(clipped[..., None] >= bucket_edges, axis=-1)
        bucket = np.minimum(clipped, 16) + reached
        hots.append(bucket[..., None] == np.arange(NB))
    hot = np.stack(hots).reshape(2 * TILE * TILE, NB).T
    return hot


NEAR_HOT = near_tables()
assert bucket_edges[-1] <= TILE


def dot(a, b, dims=((1,), (0,))):
    return lax.dot_general(a, b, (dims, ((), ())), preferred_element_type=F32)


NT = ((1,), (1,))
TN = ((0,), (0,))


MIB = 2**20
SMALL_COST = pl.CostEstimate(flops=1_000_000, bytes_accessed=1_000_000, transcendentals=0)


STRIP = 32


def score_strip(s, at, block, j, start, near_ref, half, length):
    part = s[at : at + STRIP]
    near = slice(start % TILE, start % TILE + STRIP)
    if j == block:
        if start < TILE:
            left = part[:, :TILE] + near_ref[half, 0, near, :]
            right = jnp.full((STRIP, TILE), NEG, F32)
        else:
            left = part[:, :TILE] + near_ref[half, 1, near, :]
            right = part[:, TILE:] + near_ref[half, 0, near, :]
        part = jnp.concatenate([left, right], 1)
    elif j == block - 1 and start < TILE:
        part = jnp.concatenate([part[:, :TILE], part[:, TILE:] + near_ref[half, 1, near, :]], 1)
    if (j + 1) * QROWS > SEQ // 2:
        place = lax.broadcasted_iota(jnp.int32, (1, QROWS), 1) + j * QROWS
        part = part + jnp.where(place < length, 0.0, NEG)
    return part


def lane_half(rows):
    return lax.broadcasted_iota(jnp.int32, (rows, 2 * HEAD_DIM), 1) < HEAD_DIM


def attend_kernel(length_ref, query_ref, key_ref, value_ref, near_ref, out_ref, log_ref):
    length = length_ref[0]
    lanes = lane_half(QROWS)
    value_ext = jnp.concatenate([value_ref[...], jnp.ones((SEQ, TILE), BF)], 1)
    for i in range(SEQ // QROWS):
        q_rows = query_ref[i * QROWS : (i + 1) * QROWS, :] * BF(0.125)
        q_both = jnp.concatenate([jnp.where(lanes, q_rows, BF(0)), jnp.where(lanes, BF(0), q_rows)], 0)
        tiles = [dot(q_both, key_ref[j * QROWS : (j + 1) * QROWS, :], NT) for j in range(i + 1)]
        tops = []
        weights = [[] for _ in tiles]
        for h in range(2):
            for start in range(0, QROWS, STRIP):
                strips = [
                    score_strip(s, h * QROWS + start, i, j, start, near_ref, h, length) for j, s in enumerate(tiles)
                ]
                top = strips[0]
                for s in strips[1:]:
                    top = jnp.maximum(top, s)
                top = jnp.max(top, axis=1, keepdims=True)
                tops.append(top)
                for j, s in enumerate(strips):
                    weights[j].append(jnp.exp(s - top).astype(BF))
        total = None
        for j, strips in enumerate(weights):
            total = put(total, dot(jnp.concatenate(strips, 0), value_ext[j * QROWS : (j + 1) * QROWS, :]))
        row_sum = total[:, TILE:]
        out = total[:, :TILE] / row_sum
        logs = jnp.concatenate(tops, 0) + jnp.log(row_sum)
        out_ref[i * QROWS : (i + 1) * QROWS, :] = jnp.where(lanes, out[:QROWS], out[QROWS:]).astype(BF)
        log_ref[i * QROWS : (i + 1) * QROWS, :] = jnp.where(lanes, logs[:QROWS], logs[QROWS:])


def attend(length, qkv, near):
    pairs = qkv.shape[1] // (3 * TILE)
    cols = pairs * TILE
    return pl.pallas_call(
        attend_kernel,
        grid=(pairs,),
        in_specs=[
            pl.BlockSpec(memory_space=pltpu.SMEM),
            pl.BlockSpec((SEQ, TILE), lambda p: (0, p)),
            pl.BlockSpec((SEQ, TILE), lambda p: (0, pairs + p)),
            pl.BlockSpec((SEQ, TILE), lambda p: (0, 2 * pairs + p)),
            pl.BlockSpec((2, 2, TILE, TILE), lambda p: (p, 0, 0, 0)),
        ],
        out_specs=[
            pl.BlockSpec((SEQ, TILE), lambda p: (0, p)),
            pl.BlockSpec((SEQ, TILE), lambda p: (0, p)),
        ],
        out_shape=[
            jax.ShapeDtypeStruct((SEQ, cols), BF),
            jax.ShapeDtypeStruct((SEQ, cols), F32),
        ],
        compiler_params=pltpu.CompilerParams(vmem_limit_bytes=40 * MIB),
        cost_estimate=SMALL_COST,
        name="attend",
    )(length, qkv, qkv, qkv, near)


def attend_back_kernel(
    pairs, blocks, core_ref, length_ref, query_ref, key_ref, value_ref, near_ref, out_ref, log_ref, grad_ref,
    normed_ref, output_ref, weight_ref, tile_ref, sum_ref, far_ref, own_ref, sent_ref, kept_ref, grads, dk_acc, dv_acc,
):
    step = pl.program_id(0)

    @pl.when(step < pairs)
    def _():
        pair_grads(
            step, length_ref, query_ref, key_ref, value_ref, near_ref, out_ref, log_ref, grad_ref,
            tile_ref, sum_ref, grads, dk_acc, dv_acc,
        )

    @pl.when((step >= pairs) & (step < pairs + blocks))
    def _():
        low = low_lanes((normed_ref.shape[1], TILE))
        q, k, v = (
            dot(normed_ref[...], jnp.concatenate([grads[n, p] for p in range(pairs)], 1), TN) for n in range(3)
        )
        for n, part in enumerate((q, k, v)):
            own_ref[:, n * TILE : (n + 1) * TILE] = part[:, :TILE]
            far_ref[:, n * TILE : (n + 1) * TILE] = part[:, TILE : 2 * TILE].astype(BF)
        q, k, v = (part[:, 2 * TILE :] for part in (q, k, v))
        far_ref[:, 3 * TILE : 4 * TILE] = jnp.where(low, turned(q), k).astype(BF)
        far_ref[:, 4 * TILE : 5 * TILE] = jnp.where(low, turned(v), output_ref[:, TILE:].astype(F32)).astype(BF)
        far_ref[:, 5 * TILE :] = output_ref[:, :TILE]
        own_ref[:, 3 * TILE : 4 * TILE] = jnp.where(low, q, turned(k))
        own_ref[:, 4 * TILE :] = jnp.where(low, v, 0.0)

    for late, half_ref in enumerate((sent_ref, kept_ref)):
        first = pairs + blocks + 2 * late

        @pl.when((step >= first) & (step < first + 2))
        def _(half_ref=half_ref, first=first, late=late):
            rows = half_ref.shape[0]
            mine = core_ref[0] if late else 1 - core_ref[0]
            start = pl.multiple_of((2 * mine + step - first) * rows, rows)
            total = None
            for n in range(3):
                part = jnp.concatenate([grads[n, p, pl.ds(start, rows), :] for p in range(pairs)], 1)
                cols = part.shape[1]
                total = put(total, dot(part, weight_ref[:, n * cols : (n + 1) * cols], NT))
            half_ref[...] = total


def pair_grads(
    pair, length_ref, query_ref, key_ref, value_ref, near_ref, out_ref, log_ref, grad_ref, tile_ref, sum_ref, grads, dk_acc, dv_acc
):
    length = length_ref[0]
    lanes = lane_half(QROWS)
    key_ext = jnp.concatenate([key_ref[...], jnp.ones((SEQ, TILE), BF)], 1)
    near_sums = [[None, None], [None, None]]
    all_sums = [None, None]

    def both(rows):
        return jnp.concatenate([jnp.where(lanes, rows, BF(0)), jnp.where(lanes, BF(0), rows)], 0)

    for i in range(SEQ // QROWS):
        rows = slice(i * QROWS, (i + 1) * QROWS)
        q_both = both(query_ref[rows, :] * BF(0.125))
        g_rows = grad_ref[rows, :]
        g_both = both(g_rows)
        mass = g_rows.astype(F32) * out_ref[rows, :].astype(F32)
        deltas = [
            jnp.sum(jnp.where(lanes, mass, 0.0), axis=1, keepdims=True),
            jnp.sum(jnp.where(lanes, 0.0, mass), axis=1, keepdims=True),
        ]
        logs = [log_ref[rows, h * HEAD_DIM : h * HEAD_DIM + 1] for h in range(2)]
        dq = None
        for j in range(i + 1):
            keys = slice(j * QROWS, (j + 1) * QROWS)
            s = dot(q_both, key_ref[keys, :], NT)
            dp = dot(g_both, value_ref[keys, :], NT)
            p_strips, d_strips = [], []
            for h in range(2):
                for start in range(0, QROWS, STRIP):
                    strip = slice(start, start + STRIP)
                    at = h * QROWS + start
                    p = jnp.exp(score_strip(s, at, i, j, start, near_ref, h, length) - logs[h][strip])
                    p_strips.append(p.astype(BF))
                    d_strips.append((p * (dp[at : at + STRIP] - deltas[h][strip])).astype(BF))
            p, ds = jnp.concatenate(p_strips, 0), jnp.concatenate(d_strips, 0)
            part = dot(ds, key_ext[keys, :])
            dq = put(dq, jnp.where(lanes, part[:QROWS, :TILE], part[QROWS:, :TILE]))
            for h in range(2):
                sums = part[h * QROWS : (h + 1) * QROWS, TILE:]
                all_sums[h] = put(all_sums[h], jnp.sum(sums.reshape(QROWS // 8, 8, TILE), axis=0))
            dk_part = dot(ds, q_both, TN)
            dv_part = dot(p, g_both, TN)
            if i == j:
                dk_acc[keys, :] = dk_part
                dv_acc[keys, :] = dv_part
            else:
                dk_acc[keys, :] += dk_part
                dv_acc[keys, :] += dv_part
            for h in range(2):
                mine = ds[h * QROWS : (h + 1) * QROWS]
                if j == i:
                    wide = mine.astype(F32)
                    near_sums[h][0] = put(near_sums[h][0], wide[:TILE, :TILE] + wide[TILE:, TILE:])
                    near_sums[h][1] = put(near_sums[h][1], wide[TILE:, :TILE])
                elif j == i - 1:
                    near_sums[h][1] = put(near_sums[h][1], mine[:TILE, TILE:].astype(F32))
        grads[0, pair, rows, :] = (dq * 0.125).astype(BF)
    grads[1, pair] = dk_acc[...].astype(BF)
    grads[2, pair] = dv_acc[...].astype(BF)
    for h in range(2):
        tile_ref[h, 0] = near_sums[h][0]
        tile_ref[h, 1] = near_sums[h][1]
        sum_ref[h] = all_sums[h]


def attend_back(core, length, qkv, near, mixed, logs, grad, normed, output, weight):
    pairs = qkv.shape[1] // (3 * TILE)
    width = normed.shape[1]
    block = 256
    blocks = width // block
    at = lambda i: jnp.minimum(i, pairs - 1)
    then = lambda i: jnp.clip(i - pairs, 0, blocks - 1)
    return pl.pallas_call(
        functools.partial(attend_back_kernel, pairs, blocks),
        grid_spec=pltpu.PrefetchScalarGridSpec(
            num_scalar_prefetch=2,
            grid=(pairs + blocks + 4,),
            in_specs=[
                pl.BlockSpec((SEQ, TILE), lambda i, *_: (0, at(i))),
                pl.BlockSpec((SEQ, TILE), lambda i, *_: (0, pairs + at(i))),
                pl.BlockSpec((SEQ, TILE), lambda i, *_: (0, 2 * pairs + at(i))),
                pl.BlockSpec((2, 2, TILE, TILE), lambda i, *_: (at(i), 0, 0, 0)),
            ]
            + [pl.BlockSpec((SEQ, TILE), lambda i, *_: (0, at(i)))] * 3
            + [
                pl.BlockSpec((SEQ, block), lambda i, *_: (0, then(i))),
                pl.BlockSpec((block, 2 * TILE), lambda i, *_: (then(i), 0)),
                pl.BlockSpec(weight.shape, lambda i, *_: (0, 0)),
            ],
            out_specs=[
                pl.BlockSpec((2, 2, TILE, TILE), lambda i, *_: (at(i), 0, 0, 0)),
                pl.BlockSpec((2, 8, TILE), lambda i, *_: (at(i), 0, 0)),
                pl.BlockSpec((block, 6 * TILE), lambda i, *_: (then(i), 0)),
                pl.BlockSpec((block, 5 * TILE), lambda i, *_: (then(i), 0)),
                pl.BlockSpec((block, width), lambda i, *_: (jnp.clip(i - pairs - blocks, 0, 1), 0)),
                pl.BlockSpec((block, width), lambda i, *_: (jnp.clip(i - pairs - blocks - 2, 0, 1), 0)),
            ],
            scratch_shapes=[
                pltpu.VMEM((3, pairs, SEQ, TILE), BF), pltpu.VMEM((SEQ, TILE), F32), pltpu.VMEM((SEQ, TILE), F32),
            ],
        ),
        out_shape=[
            jax.ShapeDtypeStruct((2 * pairs, 2, TILE, TILE), F32),
            jax.ShapeDtypeStruct((2 * pairs, 8, TILE), F32),
            jax.ShapeDtypeStruct((width, 6 * TILE), BF),
            jax.ShapeDtypeStruct((width, 5 * TILE), F32),
            jax.ShapeDtypeStruct((2 * block, width), F32),
            jax.ShapeDtypeStruct((2 * block, width), F32),
        ],
        compiler_params=pltpu.CompilerParams(vmem_limit_bytes=40 * MIB),
        cost_estimate=SMALL_COST,
        name="attend_back",
    )(core, length, qkv, qkv, qkv, near, mixed, logs, grad, normed, output, weight)


def low_lanes(shape):
    return lax.broadcasted_iota(jnp.int32, shape, 1) < HEAD_DIM


def turned(tile):
    return pltpu.roll(tile, HEAD_DIM, 1)


def pack_kernel(q_ref, k_ref, v_ref, o_ref, one_ref, two_ref, router_ref, out_ref):
    shard = q_ref.shape[1]
    rows = q_ref.shape[0]
    source = lax.broadcasted_iota(jnp.int32, (shard, 6 * TILE), 0)
    target = lax.broadcasted_iota(jnp.int32, (shard, 6 * TILE), 1)

    def moved(pair_base, last_base):
        want = jnp.where(source < TILE, source + pair_base, source - TILE + last_base)
        return jnp.where(target == want, 1.0, 0.0).astype(BF)

    total = dot(v_ref[...], moved(0, 2 * TILE)) + dot(o_ref[...], moved(TILE, 2 * TILE + HEAD_DIM), TN)
    total = total + dot(q_ref[...], moved(3 * TILE, 5 * TILE)) + dot(k_ref[...], moved(4 * TILE, 5 * TILE + HEAD_DIM))
    out_ref[:, : 6 * TILE] = total.astype(BF)
    experts = router_ref.shape[0]
    own_row = lax.broadcasted_iota(jnp.int32, (rows, rows), 0) == lax.broadcasted_iota(jnp.int32, (rows, rows), 1)

    def column(ref):
        return jnp.sum(jnp.where(own_row, ref[...].astype(F32), 0.0), axis=1, keepdims=True)

    lanes = lax.broadcasted_iota(jnp.int32, (experts, TILE), 1)
    spread = jnp.where(lanes == lax.broadcasted_iota(jnp.int32, (experts, TILE), 0), 1.0, 0.0).astype(BF)
    place = lax.broadcasted_iota(jnp.int32, (rows, TILE), 1)
    small = dot(router_ref[...], spread, TN)
    small = jnp.where(place == experts, column(one_ref), jnp.where(place == experts + 1, column(two_ref), small))
    out_ref[:, 6 * TILE :] = small.astype(BF)


def pack_weights(query, key, value, output, one, two, router):
    rows = query.shape[0]
    return pl.pallas_call(
        pack_kernel,
        out_shape=jax.ShapeDtypeStruct((rows, 7 * TILE), BF),
        compiler_params=pltpu.CompilerParams(vmem_limit_bytes=60 * MIB),
        cost_estimate=SMALL_COST,
        name="pack_weights",
    )(query, key, value, output, one[None], two[None], router.T)


def qkv_kernel(micro_ref, tokens_ref, gain_ref, a_own, a_far, b_own, b_far, qkv_ref, normed_ref, weight_ref, output_ref):
    width = tokens_ref.shape[2]

    @pl.when(pl.program_id(0) == 0)
    def _():
        low = low_lanes((width, TILE))

        def tiles(own, far, pair, low_half):
            at = slice(pair * TILE, (pair + 1) * TILE)
            one, two = own[:, 2 * TILE :].astype(F32), far[:, 2 * TILE :].astype(F32)
            last = jnp.where(low, one, turned(two)) if low_half else jnp.where(low, turned(one), two)
            return own[:, at], far[:, at], last.astype(BF)

        for n, (own, far, pair, low_half) in enumerate(
            ((a_own, a_far, 0, True), (a_own, a_far, 1, False), (b_own, b_far, 0, True))
        ):
            for t, tile in enumerate(tiles(own[...], far[...], pair, low_half)):
                at = 3 * n + t
                weight_ref[:, at * TILE : (at + 1) * TILE] = tile
        for t, tile in enumerate(tiles(b_own[...], b_far[...], 1, False)):
            output_ref[:, t * TILE : (t + 1) * TILE] = tile

    x = tokens_ref[0].astype(F32)
    inverse = lax.rsqrt(jnp.mean(x * x, axis=-1, keepdims=True) + 1e-06)
    normed = (x * inverse * gain_ref[...]).astype(BF)
    normed_ref[...] = normed
    qkv_ref[...] = dot(normed, weight_ref[...]).astype(BF)


def norm_and_project(micro, layer_input, gain, a_own, a_far, b_own, b_far):
    width = layer_input.shape[2]
    block = 256
    cols = 3 * TILE
    whole = lambda rows, n: pl.BlockSpec((rows, n), lambda i, m: (0, 0))
    here = lambda n: pl.BlockSpec((block, n), lambda i, m: (i, 0))
    return pl.pallas_call(
        qkv_kernel,
        grid_spec=pltpu.PrefetchScalarGridSpec(
            num_scalar_prefetch=1,
            grid=(SEQ // block,),
            in_specs=[pl.BlockSpec((1, block, width), lambda i, m: (m[0], i, 0)), whole(1, width)] + [whole(width, cols)] * 4,
            out_specs=[here(3 * cols), here(width), whole(width, 3 * cols), whole(width, cols)],
        ),
        out_shape=[
            jax.ShapeDtypeStruct((SEQ, 3 * cols), BF),
            jax.ShapeDtypeStruct((SEQ, width), BF),
            jax.ShapeDtypeStruct((width, 3 * cols), BF),
            jax.ShapeDtypeStruct((width, cols), BF),
        ],
        compiler_params=pltpu.CompilerParams(vmem_limit_bytes=40 * MIB),
        cost_estimate=SMALL_COST,
        name="norm_and_project",
    )(micro, layer_input, gain, a_own, a_far, b_own, b_far)


def middle_kernel(
    blocks, per, micro_ref, tokens_ref, mixed_ref, other_ref, own_ref, far_ref, gain_ref, code_ref, residual_ref, *refs
):
    sent_refs, normed = refs[:-1], refs[-1]
    step = pl.program_id(0)
    rows = tokens_ref.shape[1]

    @pl.when(step < blocks)
    def _():
        total = tokens_ref[0].astype(F32) + dot(mixed_ref[...], own_ref[...], NT) + dot(other_ref[...], far_ref[...], NT)
        residual_ref[...] = total
        inverse = lax.rsqrt(jnp.mean(total * total, axis=-1, keepdims=True) + 1e-06)
        normed[pl.ds(pl.multiple_of(step * rows, rows), rows), :] = (total * inverse * gain_ref[...]).astype(BF)

    for c, sent_ref in enumerate(sent_refs):

        @pl.when((step >= blocks + c * per) & (step < blocks + (c + 1) * per))
        def _(sent_ref=sent_ref):
            block = sent_ref.shape[0]
            ids = lax.broadcasted_iota(jnp.int32, (block, 1), 0) + (step - blocks) * block
            hot = jnp.where((ids == code_ref[:1]) | (ids == code_ref[1:2]), 1.0, 0.0).astype(BF)
            sent_ref[...] = dot(hot, normed[...]).astype(BF)


def residual_and_rows(micro, layer_input, mixed, other, output_own, output_far, gain, code, count, chunks):
    width = layer_input.shape[2]
    block = 256
    blocks = SEQ // block
    send = 320
    cols = mixed.shape[1]
    per = count // send
    at = lambda i: jnp.minimum(i, blocks - 1)
    whole = lambda arr: pl.BlockSpec(arr.shape, lambda i, m: (0, 0))
    here = lambda n: pl.BlockSpec((block, n), lambda i, m: (at(i), 0))

    def sent(c):
        return pl.BlockSpec((send, width), lambda i, m: (jnp.clip(i - blocks - c * per, 0, per - 1), 0))

    return pl.pallas_call(
        functools.partial(middle_kernel, blocks, per),
        grid_spec=pltpu.PrefetchScalarGridSpec(
            num_scalar_prefetch=1,
            grid=(blocks + chunks * per,),
            in_specs=[
                pl.BlockSpec((1, block, width), lambda i, m: (m[0], at(i), 0)),
                here(cols), here(cols), whole(output_own), whole(output_far), whole(gain), whole(code),
            ],
            out_specs=[here(width)] + [sent(c) for c in range(chunks)],
            scratch_shapes=[pltpu.VMEM((SEQ, width), BF)],
        ),
        out_shape=[jax.ShapeDtypeStruct((SEQ, width), F32)] + [jax.ShapeDtypeStruct((count, width), BF)] * chunks,
        compiler_params=pltpu.CompilerParams(vmem_limit_bytes=40 * MIB),
        cost_estimate=SMALL_COST,
        name="residual_and_rows",
    )(micro, layer_input, mixed, other, output_own, output_far, gain, code)


def picked_rows(first, second, segments):
    total = None
    start = 0
    for rows in segments:
        length = rows.shape[0]
        ids = lax.broadcasted_iota(jnp.int32, (1, length), 1) + start
        hot = []
        for at in range(0, first.shape[0], STRIP):
            one, two = first[at : at + STRIP], second[at : at + STRIP]
            hot.append(jnp.where((one == ids) | (two == ids), 1.0, 0.0).astype(BF))
        total = put(total, dot(jnp.concatenate(hot, 0), rows))
        start += length
    return total


def put(a, b):
    return b if a is None else a + b


def folded(product):
    return jnp.sum(product.reshape(product.shape[0] // 8, 8, product.shape[1]), axis=0)


def as_column(eight):
    ones = jnp.ones((16, TILE), BF)
    high = eight.astype(BF)
    rest = (eight - high.astype(F32)).astype(BF)
    return dot(jnp.concatenate([high, rest], 0), ones, TN)


def combine_kernel(experts, half, spare, micro_ref, core_ref, length_ref, *refs):
    info_ref, grad_ref, residual_ref, mixed_ref, gain_ref, router_ref, output_ref = refs[:7]
    backs = refs[7:-9]
    (total_ref, mixed_grad_ref, extra_ref, far_ref, own_ref, acc_ref, router_acc, gain_acc, tables) = refs[-9:]
    block = residual_ref.shape[0]
    step = pl.program_id(0)
    count = len(backs) // 2

    @pl.when(step == 0)
    def _():
        place = lax.broadcasted_iota(jnp.int32, (experts, 1), 0)
        for n, back in enumerate((backs[count - 1], backs[2 * count - 1])):
            table = jnp.zeros((experts, back.shape[2]), F32)
            for e in range(experts):
                row = back[e, spare : spare + 16, :].astype(F32)[:1]
                table = jnp.where(place == e, row, table)
            for piece in range(3):
                at = (3 * n + piece) * experts
                tables[at : at + experts] = table[:, piece * half : (piece + 1) * half]

    info = jnp.transpose(info_ref[...])
    number = lambda n: info[:, n : n + 1]
    columns = lax.broadcasted_iota(jnp.int32, (1, half), 1)
    lanes = lax.broadcasted_iota(jnp.int32, (1, 6 * experts), 1)
    table = tables[...].astype(BF)
    values = []
    for k in range(2):
        slot = number(4 + k)
        hot = jnp.where(columns == lax.rem(slot, half), 1.0, 0.0).astype(BF)
        found = dot(hot, table, NT)
        wanted = jnp.where(slot // half == core_ref[0], 0, 3 * experts) + number(2 + k)
        away = lanes - wanted
        hit = (away == 0) | (away == experts) | (away == 2 * experts)
        values.append(jnp.sum(jnp.where(hit, found, 0.0), axis=1, keepdims=True))
    wide = lax.broadcasted_iota(jnp.int32, (1, TILE), 1)
    is_first, is_second = wide == number(2), wide == number(3)
    residual = residual_ref[...]
    gain = gain_ref[...]
    inverse = lax.rsqrt(jnp.mean(residual * residual, axis=-1, keepdims=True) + 1e-06)
    plain = residual * inverse
    normed = (plain * gain).astype(BF)
    logits = dot(normed, router_ref[...])
    gap = jnp.sum(jnp.where(is_first, logits, 0.0) - jnp.where(is_second, logits, 0.0), axis=1, keepdims=True)
    small = jnp.exp(-jnp.abs(gap))
    logit = small / ((1.0 + small) * (1.0 + small)) * (values[0] - values[1])
    logit_grad = jnp.where(is_first, logit, jnp.where(is_second, -logit, 0.0)).astype(BF)
    segments = [b[...].reshape(b.shape[0] * b.shape[1], b.shape[2]) for b in backs]
    normed_grad = picked_rows(number(0), number(1), segments) + dot(logit_grad, router_ref[...], NT)
    scaled = normed_grad * gain
    mean = jnp.mean(scaled * plain, axis=-1, keepdims=True)
    place = lax.broadcasted_iota(jnp.int32, (block, 1), 0) + step * block
    grad_out = jnp.where(place < length_ref[0], grad_ref[0].astype(F32), 0.0)
    total = grad_out + inverse * (scaled - plain * mean)

    @pl.when(step == core_ref[0])
    def _():
        total_ref[...] = total

    branch = total.astype(BF)
    mixed_grad_ref[...] = dot(branch, output_ref[...]).astype(BF)
    router_part = dot(logit_grad, normed, TN)
    gain_part = folded(normed_grad * plain)
    output_part = dot(mixed_ref[...], branch, TN)

    @pl.when(step == 0)
    def _():
        router_acc[...] = router_part
        gain_acc[...] = gain_part
        acc_ref[...] = output_part

    @pl.when(step > 0)
    def _():
        router_acc[...] += router_part
        gain_acc[...] += gain_part
        acc_ref[...] += output_part

    @pl.when(step == pl.num_programs(0) - 1)
    def _():
        extra_ref[...] = jnp.transpose(router_acc[...]) + jnp.where(wide == experts + 1, as_column(gain_acc[...]), 0.0)
        parts = jnp.transpose(acc_ref[...])
        far_ref[...] = parts[:, TILE:].astype(BF)
        own_ref[:, :TILE] = parts[:, :TILE]
        own_ref[:, TILE:] = parts[:, 2 * TILE :]


def combine(micro, core, length, info, out_grad, residual, mixed, gain, router, output_own, backs, half, spare):
    width = residual.shape[1]
    block = 512
    cols = mixed.shape[1]
    whole = lambda arr: pl.BlockSpec(arr.shape, lambda i, *_: (0,) * arr.ndim)
    fixed = lambda rows, n: pl.BlockSpec((rows, n), lambda i, *_: (0, 0))
    here = lambda n: pl.BlockSpec((block, n), lambda i, *_: (i, 0))
    experts = backs[0].shape[0]
    return pl.pallas_call(
        functools.partial(combine_kernel, experts, half, spare),
        grid_spec=pltpu.PrefetchScalarGridSpec(
            num_scalar_prefetch=3,
            grid=(SEQ // block,),
            in_specs=[
                pl.BlockSpec((8, block), lambda i, *_: (0, i)),
                pl.BlockSpec((1, block, width), lambda i, m, *_: (m[0], i, 0)),
                here(width), here(cols), whole(gain), whole(router), whole(output_own),
            ]
            + [whole(x) for x in backs],
            out_specs=[fixed(block, width), here(cols), fixed(width, TILE), fixed(width, 2 * TILE), fixed(width, 2 * TILE)],
            scratch_shapes=[
                pltpu.VMEM((cols, width), F32),
                pltpu.VMEM((TILE, width), F32),
                pltpu.VMEM((8, width), F32),
                pltpu.VMEM((6 * experts, half), F32),
            ],
        ),
        out_shape=[
            jax.ShapeDtypeStruct((block, width), F32),
            jax.ShapeDtypeStruct((SEQ, cols), BF),
            jax.ShapeDtypeStruct((width, TILE), F32),
            jax.ShapeDtypeStruct((width, 2 * TILE), BF),
            jax.ShapeDtypeStruct((width, 2 * TILE), F32),
        ],
        compiler_params=pltpu.CompilerParams(vmem_limit_bytes=40 * MIB),
        cost_estimate=SMALL_COST,
        name="combine",
    )(micro, core, length, info, out_grad, residual, mixed, gain, router, output_own, *backs)


def both_kernel(
    lane, micro_ref, core_ref, length_ref, part_ref, got_ref, tokens_ref, gain_ref, grad_ref,
    info_ref, residual_ref, own_ref, far_ref, out_ref, extra_ref, acc_ref,
):
    block = residual_ref.shape[0]
    info = jnp.transpose(info_ref[...])
    place = lax.broadcasted_iota(jnp.int32, (block, 1), 0) + (core_ref[0] * 2 + pl.program_id(0)) * block
    rows = residual_ref[...] + picked_rows(info[:, 6:7], info[:, 7:8], (own_ref[...], far_ref[...]))
    out_ref[0] = jnp.where(place < length_ref[0], rows, 0.0).astype(BF)
    normed_grad = got_ref[...] + part_ref[...]
    x = tokens_ref[0].astype(F32)
    inverse = lax.rsqrt(jnp.mean(x * x, axis=-1, keepdims=True) + 1e-06)
    plain = x * inverse
    scaled = normed_grad * gain_ref[...]
    mean = jnp.mean(scaled * plain, axis=-1, keepdims=True)
    out_ref[1] = (grad_ref[...] + inverse * (scaled - plain * mean)).astype(BF)
    wide = lax.broadcasted_iota(jnp.int32, (1, TILE), 1)
    part = folded(normed_grad * plain)

    @pl.when(pl.program_id(0) == 0)
    def _():
        acc_ref[...] = part

    @pl.when(pl.program_id(0) == 1)
    def _():
        extra_ref[...] = jnp.where(wide == lane, as_column(acc_ref[...] + part), 0.0)


def both_rows(lane, micro, core, length, part, got, layer_input, gain, residual_grad, info, residual, own, far):
    width = part.shape[1]
    plain = pl.BlockSpec((256, width), lambda i, *_: (i, 0))
    block = 256
    here = lambda n: pl.BlockSpec((block, n), lambda i, m, c, *_: (c[0] * 2 + i, 0))
    whole = lambda arr: pl.BlockSpec(arr.shape, lambda i, *_: (0, 0))
    return pl.pallas_call(
        functools.partial(both_kernel, lane),
        grid_spec=pltpu.PrefetchScalarGridSpec(
            num_scalar_prefetch=3,
            grid=(2,),
            in_specs=[
                plain,
                plain,
                pl.BlockSpec((1, block, width), lambda i, m, c, *_: (m[0], c[0] * 2 + i, 0)),
                whole(gain),
                plain,
                pl.BlockSpec((8, block), lambda i, m, c, *_: (0, c[0] * 2 + i)),
                here(width),
                whole(own),
                whole(far),
            ],
            out_specs=[
                pl.BlockSpec((2, block, width), lambda i, *_: (0, i, 0)),
                pl.BlockSpec((width, TILE), lambda i, *_: (0, 0)),
            ],
            scratch_shapes=[pltpu.VMEM((8, width), F32)],
        ),
        out_shape=[jax.ShapeDtypeStruct((2, 2 * block, width), BF), jax.ShapeDtypeStruct((width, TILE), F32)],
        compiler_params=pltpu.CompilerParams(vmem_limit_bytes=40 * MIB),
        cost_estimate=SMALL_COST,
        name="both_rows",
    )(micro, core, length, part, got, layer_input, gain, residual_grad, info, residual, own, far)


def sum_kernel(kept, own, got, out_own, early, late, late_far, table, sum_ref):
    low = low_lanes(early.shape)
    sum_ref[:, : 4 * TILE] = (own[:, : 4 * TILE] + got[:, : 4 * TILE].astype(F32)).astype(BF)
    mixed = jnp.where(low, own[:, 4 * TILE :], turned(out_own[:, TILE:]))
    sum_ref[:, 4 * TILE : 5 * TILE] = (mixed + got[:, 4 * TILE : 5 * TILE].astype(F32)).astype(BF)
    sum_ref[:, 5 * TILE : 6 * TILE] = (out_own[:, :TILE] + got[:, 5 * TILE :].astype(F32)).astype(BF)
    extra = early[...] + late[...] + late_far[...] + table[...]
    high = extra.astype(BF)
    rest = extra - high.astype(F32)
    if kept <= HEAD_DIM:
        sum_ref[:, 6 * TILE :] = jnp.where(low, high.astype(F32), turned(rest)).astype(BF)
    else:
        sum_ref[:, 6 * TILE : 7 * TILE] = high
        sum_ref[:, 7 * TILE :] = rest.astype(BF)


def packed_sums(kept, *parts):
    width = parts[0].shape[0]
    cols = (7 if kept <= HEAD_DIM else 8) * TILE
    block = 256
    here = lambda n: pl.BlockSpec((block, n), lambda i: (i, 0))
    return pl.pallas_call(
        functools.partial(sum_kernel, kept),
        grid=(width // block,),
        in_specs=[here(x.shape[1]) for x in parts],
        out_specs=here(cols),
        out_shape=jax.ShapeDtypeStruct((width, cols), BF),
        compiler_params=pltpu.CompilerParams(vmem_limit_bytes=40 * MIB),
        cost_estimate=SMALL_COST,
        name="packed_sums",
    )(*parts)


def final_kernel(kept, parts_ref, q_ref, k_ref, v_ref, o_ref, small_ref):
    total = parts_ref[0].astype(F32)
    for n in range(1, parts_ref.shape[0]):
        total = total + parts_ref[n].astype(F32)
    tile = lambda t: total[:, t * TILE : (t + 1) * TILE]
    q_ref[:, :TILE] = tile(0)
    q_ref[:, TILE:] = tile(3)[:, :HEAD_DIM]
    k_ref[:, :TILE] = tile(1)
    k_ref[:, TILE:] = turned(tile(3))[:, :HEAD_DIM]
    v_ref[:, :TILE] = tile(2)
    v_ref[:, TILE:] = tile(4)[:, :HEAD_DIM]
    o_ref[:, :TILE] = tile(5)
    o_ref[:, TILE:] = turned(tile(4))[:, :HEAD_DIM]
    small_ref[...] = tile(6) + (turned(tile(6)) if kept <= HEAD_DIM else tile(7))


def final_sums(kept, parts, shard):
    rows = parts.shape[1]
    return pl.pallas_call(
        functools.partial(final_kernel, kept),
        out_shape=[jax.ShapeDtypeStruct((rows, shard), F32)] * 4 + [jax.ShapeDtypeStruct((rows, TILE), F32)],
        compiler_params=pltpu.CompilerParams(vmem_limit_bytes=40 * MIB),
        cost_estimate=SMALL_COST,
        name="final_sums",
    )(parts)


def pair_gate(logits, own, other):
    lanes = lax.broadcasted_iota(jnp.int32, logits.shape, 1)
    gap = jnp.sum(
        jnp.where(lanes == own, logits, 0.0) - jnp.where(lanes == other, logits, 0.0), axis=1, keepdims=True
    )
    small = jnp.exp(-jnp.abs(gap))
    return jnp.where(gap >= 0.0, 1.0, small) / (1.0 + small)


def expert_kernel(lead, chunk, half, me_ref, partner_ref, rows_ref, grads_ref, router_ref, *refs):
    before, refs = (refs[0], refs[1:]) if lead is not None and lead > 0 else (None, refs)
    plain_ref, firsts = refs[0], refs[1:5]
    back_ref, active_ref, slope_ref, gated_ref, gate_ref, mass_ref = refs[5:]
    rows = rows_ref[...]
    grads = grads_ref[...]
    partner = jnp.transpose(jnp.broadcast_to(partner_ref[0], (8, rows.shape[0])))[:, :1]
    gate = pair_gate(dot(rows, router_ref[...]), me_ref[0], partner)
    gated_ref[...] = (gate * grads.astype(F32)).astype(BF)
    gate_ref[...] = jnp.broadcast_to(gate, gate_ref.shape)
    masses = [None] * (rows.shape[0] // STRIP)
    back = None
    width = firsts[0].shape[1]
    step = 256
    places = [(r, c) for r in range(4) for c in range(0, width, step)]

    def products(r, c):
        return dot(rows, firsts[r][:, c : c + step])

    ahead = products(*places[0])
    for n, (r, c) in enumerate(places):
        x = ahead
        if n + 1 < len(places):
            ahead = products(*places[n + 1])
        place = slice(r * width + c, r * width + c + step)
        for at in range(0, rows.shape[0], STRIP):
            strip = slice(at, at + STRIP)
            value, flow = x[strip], plain_ref[strip, place].astype(F32)
            square = value * value
            bent = jnp.tanh(value * (GELU_C + (GELU_C * GELU_A) * square))
            rise = 0.5 + 0.5 * bent
            active = value * rise
            slope = rise + active * (1.0 - bent) * (GELU_C + (3.0 * GELU_C * GELU_A) * square)
            low = active.astype(BF)
            active_ref[strip, place] = low
            slope_ref[strip, place] = (gate[strip] * flow * slope).astype(BF)
            part = low.astype(F32) * flow
            masses[at // STRIP] = put(masses[at // STRIP], part[:, :TILE] + part[:, TILE:])
        if c + step == width and r > 0:
            back = put(back, dot(slope_ref[:, (r - 1) * width : r * width], firsts[r - 1][...], NT))
    back = put(back, dot(slope_ref[:, 3 * width :], firsts[3][...], NT))
    back = back.astype(BF)
    mass = jnp.sum(jnp.concatenate(masses, 0), axis=1, keepdims=True)
    if lead is None:
        back_ref[...] = back
        mass_ref[...] = jnp.broadcast_to(mass, mass_ref.shape)
        return
    count = rows.shape[0] // chunk
    number = lax.broadcasted_iota(jnp.int32, (rows.shape[0], 1), 0)
    lanes = lax.broadcasted_iota(jnp.int32, (1, rows.shape[1]), 1)
    inside = lax.rem(number, chunk)
    spread = jnp.zeros(rows.shape, F32)
    for piece in range(3):
        high = mass.astype(BF).astype(F32)
        spread = jnp.where(lanes == piece * half + lead + inside, high, spread)
        mass = mass - high
    own = jnp.where(number // chunk == lax.broadcasted_iota(jnp.int32, (1, TILE), 1), 1.0, 0.0).astype(BF)
    line = dot(own, spread.astype(BF), TN)
    if before is None:
        back_ref[...] = back
        for e in range(count):
            mass_ref[e] = line[e : e + 1].astype(BF)
    else:
        back_ref[:, :chunk] = back.reshape(count, chunk, back.shape[1])
        row = lax.broadcasted_iota(jnp.int32, (16, 1), 0)
        for e in range(count):
            both = line[e : e + 1] + before[e].astype(F32)
            back_ref[e, chunk:] = jnp.where(row == 0, both, 0.0).astype(BF)


def row_block(total):
    return 320 if total % 320 == 0 else total


def plain_kernel(grads_ref, b0, b1, b2, b3, out_ref):
    width = b0.shape[0]
    for r, second in enumerate((b0, b1, b2, b3)):
        out_ref[:, r * width : (r + 1) * width] = dot(grads_ref[...], second[...], NT).astype(BF)


def plain_grads(grads, seconds):
    total, width = grads.shape
    hidden = sum(w.shape[0] for w in seconds)
    block = row_block(total)
    here = lambda cols: pl.BlockSpec((block, cols), lambda i: (i, 0))
    return pl.pallas_call(
        plain_kernel,
        grid=(total // block,),
        in_specs=[here(width)] + [pl.BlockSpec(w.shape, lambda i: (0, 0)) for w in seconds],
        out_specs=here(hidden),
        out_shape=jax.ShapeDtypeStruct((total, hidden), BF),
        compiler_params=pltpu.CompilerParams(vmem_limit_bytes=56 * MIB),
        cost_estimate=SMALL_COST,
        name="plain_grads",
    )(grads, *seconds)


def expert_rows_pass(lead, chunk, half, me, partner, rows, grads, plain, router, before, firsts, number):
    total, width = rows.shape
    block = row_block(total)
    steps = total // block
    experts = total // chunk
    hidden = sum(f.shape[1] for f in firsts)
    here = lambda cols: pl.BlockSpec((block, cols), lambda i: (i, 0))
    there = lambda cols: pl.BlockSpec((block, cols), lambda i: (number * steps + i, 0))
    whole = lambda arr: pl.BlockSpec(arr.shape, lambda i: (0, 0))
    lines = pl.BlockSpec((block // chunk, 1, width), lambda i: (i, 0, 0))
    back_shape, back_spec = (total, width), here(width)
    mass_shape, mass_spec, mass_kind = (experts, 1, width), lines, BF
    if lead is None:
        mass_shape, mass_spec, mass_kind = (total, TILE), here(TILE), F32
    elif before is not None:
        back_shape = (experts, chunk + 16, width)
        back_spec = pl.BlockSpec((block // chunk, chunk + 16, width), lambda i: (i, 0, 0))
    return pl.pallas_call(
        functools.partial(expert_kernel, lead, chunk, half),
        grid=(steps,),
        in_specs=[
            pl.BlockSpec(memory_space=pltpu.SMEM),
            pl.BlockSpec((1, 1, block), lambda i: (number * steps + i, 0, 0)),
            here(width), there(width), whole(router),
        ]
        + ([lines] if before is not None else [])
        + [there(hidden)]
        + [whole(w) for w in firsts],
        out_specs=[back_spec, here(hidden), here(hidden), here(width), here(TILE), mass_spec],
        out_shape=[
            jax.ShapeDtypeStruct(back_shape, BF),
            jax.ShapeDtypeStruct((total, hidden), BF),
            jax.ShapeDtypeStruct((total, hidden), BF),
            jax.ShapeDtypeStruct((total, width), BF),
            jax.ShapeDtypeStruct((total, TILE), F32),
            jax.ShapeDtypeStruct(mass_shape, mass_kind),
        ],
        compiler_params=pltpu.CompilerParams(vmem_limit_bytes=56 * MIB),
        cost_estimate=SMALL_COST,
        name="expert_rows",
    )(me, partner, rows, grads, router, *([before] if before is not None else []), plain, *firsts)


def weight_parts(count, refs):
    rows, slopes, active, gated = (refs[n * count : (n + 1) * count] for n in range(4))
    first, second = None, None
    for n in range(count):
        first = put(first, dot(rows[n][...], slopes[n][...], TN))
        second = put(second, dot(active[n][...], gated[n][...], TN))
    return first, second


def cross_kernel(count, *refs):
    first, second = weight_parts(count, refs)
    refs[-1][0, 0] = first.astype(BF)
    refs[-1][0, 1] = second.astype(BF)


def kept_kernel(count, *refs):
    got_ref, far_ref, kept_ref = refs[-3:]
    first, second = weight_parts(count, refs)
    first = first + got_ref[0, 0].astype(F32)
    second = second + got_ref[0, 1].astype(F32)

    @pl.when(pl.program_id(0) == 0)
    def _():
        far_ref[0] = first.astype(BF)
        far_ref[1] = second.astype(BF)

    @pl.when(pl.program_id(0) == 1)
    def _():
        kept_ref[0] = first
        kept_ref[1] = second


def weight_specs(rows, slopes, quarter):
    total, width = rows[0].shape
    hidden = slopes[0].shape[1] // 4
    whole = pl.BlockSpec((total, width), lambda i: (0, 0))
    part = pl.BlockSpec((total, hidden), lambda i: (0, quarter(i)))
    count = len(rows)
    return width, hidden, [whole] * count + [part] * (2 * count) + [whole] * count


def cross_weight_grads(rows, slopes, active, gated):
    width, hidden, specs = weight_specs(rows, slopes, lambda i: 2 + i)
    return pl.pallas_call(
        functools.partial(cross_kernel, len(rows)),
        grid=(2,),
        in_specs=specs,
        out_specs=pl.BlockSpec((1, 2, width, hidden), lambda i: (i, 0, 0, 0)),
        out_shape=jax.ShapeDtypeStruct((2, 2, width, hidden), BF),
        compiler_params=pltpu.CompilerParams(vmem_limit_bytes=56 * MIB),
        cost_estimate=SMALL_COST,
        name="cross_weight_grads",
    )(*rows, *slopes, *active, *gated)


def kept_weight_grads(rows, slopes, active, gated, got):
    width, hidden, specs = weight_specs(rows, slopes, lambda i: 1 - i)
    fixed = pl.BlockSpec((2, width, hidden), lambda i: (0, 0, 0))
    return pl.pallas_call(
        functools.partial(kept_kernel, len(rows)),
        grid=(2,),
        in_specs=specs + [pl.BlockSpec((1, 2, width, hidden), lambda i: (1 - i, 0, 0, 0))],
        out_specs=[fixed, fixed],
        out_shape=[
            jax.ShapeDtypeStruct((2, width, hidden), BF),
            jax.ShapeDtypeStruct((2, width, hidden), F32),
        ],
        compiler_params=pltpu.CompilerParams(vmem_limit_bytes=56 * MIB),
        cost_estimate=SMALL_COST,
        name="kept_weight_grads",
    )(*rows, *slopes, *active, *gated, got)


def result_kernel(chunks, *refs):
    active, gates, seconds, out_ref = refs[:chunks], refs[chunks : 2 * chunks], refs[2 * chunks : -1], refs[-1]
    for c in range(chunks):

        @pl.when(pl.program_id(0) == c)
        def _(c=c):
            width = seconds[0].shape[0]
            total = None
            for r, second in enumerate(seconds):
                total = put(total, dot(active[c][:, r * width : (r + 1) * width], second[...]))
            rows = (total * gates[c][:, :1]).astype(BF)
            if chunks > 1:
                out_ref[:, 0] = rows.reshape(out_ref.shape[0], out_ref.shape[2], out_ref.shape[3])
            else:
                out_ref[...] = rows


def expert_results(active, gates, seconds, experts):
    chunks = len(active)
    total, hidden = active[0].shape
    width = seconds[0].shape[1]
    block = row_block(total)
    steps = total // block

    def here(c, cols):
        return pl.BlockSpec((block, cols), lambda g, i: (jnp.where(g == c, i, jnp.where(g < c, 0, steps - 1)), 0))

    chunk = total // experts
    if chunks > 1:
        shape = (experts, chunks, chunk, width)
        out_spec = pl.BlockSpec((block // chunk, 1, chunk, width), lambda g, i: (i, g, 0, 0))
    else:
        shape = (total, width)
        out_spec = pl.BlockSpec((block, width), lambda g, i: (i, 0))
    out = pl.pallas_call(
        functools.partial(result_kernel, chunks),
        grid=(chunks, steps),
        in_specs=[here(c, hidden) for c in range(chunks)]
        + [here(c, TILE) for c in range(chunks)]
        + [pl.BlockSpec(w.shape, lambda g, i: (0, 0)) for w in seconds],
        out_specs=out_spec,
        out_shape=jax.ShapeDtypeStruct(shape, BF),
        compiler_params=pltpu.CompilerParams(vmem_limit_bytes=56 * MIB),
        cost_estimate=SMALL_COST,
        name="expert_results",
    )(*active, *gates, *seconds)
    return out.reshape(experts, chunks * chunk, width)


def last_sum_kernel(kept_ref, y_ref, out_first, out_second):
    for n, out in enumerate((out_first, out_second)):
        out[...] = kept_ref[n] + y_ref[n].astype(F32)


def last_sums(kept, got_y):
    _, width, hidden = kept.shape
    block = 256
    here = pl.BlockSpec((block, hidden), lambda i: (i, 0))
    part = pl.BlockSpec((2, block, hidden), lambda i: (0, i, 0))
    return pl.pallas_call(
        last_sum_kernel,
        grid=(width // block,),
        in_specs=[part, part],
        out_specs=[here, here],
        out_shape=[jax.ShapeDtypeStruct((width, hidden), F32)] * 2,
        compiler_params=pltpu.CompilerParams(vmem_limit_bytes=40 * MIB),
        cost_estimate=SMALL_COST,
        name="last_sums",
    )(kept, got_y)


def send_kernel(micro_ref, code_ref, rows_ref, out_ref):
    block = out_ref.shape[0]
    ids = lax.broadcasted_iota(jnp.int32, (block, 1), 0) + pl.program_id(0) * block
    hot = jnp.where((ids == code_ref[:1]) | (ids == code_ref[1:2]), 1.0, 0.0).astype(BF)
    out_ref[...] = dot(hot, rows_ref[0]).astype(BF)


def send_rows(micro, code, rows, count):
    width = rows.shape[2]
    block = next(b for b in (336, 320, 384, count) if count % b == 0)
    return pl.pallas_call(
        send_kernel,
        grid_spec=pltpu.PrefetchScalarGridSpec(
            num_scalar_prefetch=1,
            grid=(count // block,),
            in_specs=[
                pl.BlockSpec(code.shape, lambda i, m: (0, 0)),
                pl.BlockSpec((1, SEQ, width), lambda i, m: (m[0], 0, 0)),
            ],
            out_specs=pl.BlockSpec((block, width), lambda i, m: (i, 0)),
        ),
        out_shape=jax.ShapeDtypeStruct((count, width), BF),
        compiler_params=pltpu.CompilerParams(vmem_limit_bytes=40 * MIB),
        cost_estimate=SMALL_COST,
        name="send_rows",
    )(micro, code, rows)


def place_kernel(place_ref, *refs):
    for n, piece in enumerate(refs[:4]):

        @pl.when(pl.program_id(0) == n)
        def _(piece=piece):
            for k, out_ref in enumerate(refs[4:]):
                out_ref[0] = piece[k]


def place_pieces(places, pieces):
    two, rows, width = pieces[0].shape
    whole = pl.BlockSpec(pieces[0].shape, lambda i, place_ref: (0, 0, 0))
    return pl.pallas_call(
        place_kernel,
        grid_spec=pltpu.PrefetchScalarGridSpec(
            num_scalar_prefetch=1,
            grid=(4,),
            in_specs=[whole] * 4,
            out_specs=[pl.BlockSpec((1, rows, width), lambda i, place_ref: (place_ref[i], 0, 0))] * two,
        ),
        out_shape=[jax.ShapeDtypeStruct((4, rows, width), pieces[0].dtype)] * two,
        compiler_params=pltpu.CompilerParams(vmem_limit_bytes=40 * MIB),
        cost_estimate=SMALL_COST,
        name="place_pieces",
    )(places, *pieces)


def swap(value, axis, count, bit):
    return lax.ppermute(value, axis, [(i, i ^ bit) for i in range(count)])


def all_to_all(value):
    return lax.all_to_all(value, "dp", split_axis=0, concat_axis=0, tiled=True)


def together(*values):
    return lax.optimization_barrier(values)


def local(
    layer_input, out_grad, first_gain, query_weight, key_weight, value_weight, output_weight,
    position_bias, second_gain, router_weight, expert_in, expert_out, seq_lengths, routes,
):
    micro_count, tok_rows, width = layer_input.shape
    dp_count = lax.axis_size("dp")
    expert_count = router_weight.shape[1]
    shard = query_weight.shape[1]
    heads_here = position_bias.shape[0]
    assert lax.axis_size("tensor") == 4 and micro_count == 2 and expert_count == dp_count
    assert tok_rows == SEQ and seq_lengths.shape[1] == 1
    capacity = max(8, 8 * (10 * tok_rows // (32 * expert_count)))
    half = capacity // 2
    stride = 8 * (half // 8 + 1)
    by_lines = dp_count == 8
    chunks = 2 if half % 32 == 0 else 1
    chunk = half // chunks
    chunk_rows = expert_count * chunk
    rows_here = query_weight.shape[0]
    me = lax.axis_index("dp")
    rank = lax.axis_index("tensor")
    micro = rank // 2
    core = rank % 2

    def swap_y(value):
        return swap(value, "tensor", 4, 2)

    def swap_core(value):
        return swap(value, "tensor", 4, 1)

    micro_arg = micro.reshape(1).astype(jnp.int32)
    core_arg = core.reshape(1).astype(jnp.int32)

    packed = pack_weights(query_weight, key_weight, value_weight, output_weight, first_gain, second_gain, router_weight)
    three = 3 * TILE

    def doubled(stacked, bit, axis=0):
        other = swap(stacked, "dp", dp_count, bit)
        high = (me & bit) != 0
        pair = jnp.where(high, jnp.stack([other, stacked], axis + 1), jnp.stack([stacked, other], axis + 1))
        return pair.reshape(stacked.shape[:axis] + (-1,) + stacked.shape[axis + 1 :])

    stacked = packed[None]
    bit = dp_count // 2
    while bit > 1:
        stacked = doubled(stacked, bit)
        bit //= 2
    length = lax.dynamic_index_in_dim(seq_lengths, micro, 0, keepdims=False)
    route = lax.dynamic_index_in_dim(routes, micro, 0, keepdims=False).T
    expert_ids = jnp.arange(expert_count, dtype=jnp.int32)
    named = (expert_ids[:, None, None] == route[None]).astype(jnp.int32)
    per_token = jnp.sum(named, axis=1, dtype=jnp.int32)
    earlier = jnp.cumsum(per_token, axis=1, dtype=jnp.int32) - per_token
    slot = jnp.sum(named * earlier[:, None, :], axis=0, dtype=jnp.int32)
    here = slot // half == core
    within = slot % half
    chunk_of = within // chunk
    inside = within % chunk
    spare = 16 * -(-chunk // 16)
    last_stride = spare + 16
    last = (chunks - 1) * chunk_rows
    code_back = jnp.where(
        chunk_of == chunks - 1, last + route * last_stride + inside, chunk_of * chunk_rows + route * chunk + inside
    )
    code_back = code_back + jnp.where(here, 0, last + expert_count * last_stride)
    code_result = route * half + within + jnp.where(here, 0, expert_count * half)
    info = jnp.concatenate([code_back, route, slot, code_result], 0)

    code_grads = jnp.where(here, route * stride + within, -1)
    valid = jnp.arange(SEQ, dtype=jnp.int32) < length[0]
    ids = jnp.arange(expert_count * stride, dtype=jnp.int32)[:, None]
    partner = jnp.sum(
        jnp.where(ids == code_grads[:1], route[1:], 0) + jnp.where(ids == code_grads[1:], route[:1], 0), axis=1, dtype=jnp.int32
    )
    grads_sent = send_rows(micro_arg, jnp.where(valid[None], code_grads, -1), out_grad, expert_count * stride)
    grads_sent = grads_sent.reshape(expert_count, stride, width)
    partner_row = jnp.pad(partner.reshape(expert_count, stride)[:, :half].astype(BF), ((0, 0), (0, width - half)))
    grads_sent = grads_sent.at[:, half].set(partner_row)
    stacked, grads_sent, position_bias = together(stacked, grads_sent, position_bias)
    if by_lines:
        lines = [list(range(x, dp_count, 2)) for x in range(2)]
        grads_z = lax.all_to_all(
            grads_sent.reshape(dp_count // 2, 2, stride, width), "dp", split_axis=0, concat_axis=0,
            axis_index_groups=lines, tiled=True,
        )

    first_own = expert_in[0]
    second_own = expert_out[0]
    part_b = stacked[:, :, :three]
    far_b = swap_y(part_b)
    part_a = doubled(stacked[:, :, three:], 1)
    part_a, far_b = together(part_a, far_b)
    pair_b = jnp.stack([part_b, far_b])
    a_own = part_a[:, :, :three]
    a_far = swap_y(a_own).reshape(width, three)
    a_own = a_own.reshape(width, three)
    pair_b = doubled(pair_b, 1, 1).reshape(2, width, three)
    if by_lines:
        a_far, pair_b, second_own = together(a_far, pair_b, second_own)
    else:
        a_far, pair_b, grads_sent, second_own = together(a_far, pair_b, grads_sent, second_own)
    second_y = swap_y(second_own)
    small_all = part_a[:, :, three:].reshape(width, TILE)
    gain_one = small_all[:, expert_count].astype(F32)[None]
    gain_two = small_all[:, expert_count + 1].astype(F32)[None]
    router_wide = small_all
    far_bias = swap_y(position_bias)
    bias = jnp.concatenate([position_bias[:2], far_bias[:2], position_bias[2:], far_bias[2:]], 0)
    head_total = bias.shape[0]
    hot_const = jnp.asarray(NEAR_HOT, dtype=BF)
    near = dot(bias, hot_const) - bias[:, NB - 1 :].astype(F32)
    near = near.reshape(head_total, 2, TILE, TILE)
    places = jnp.arange(TILE, dtype=jnp.int32)
    causal = jnp.stack([places[None, :] <= places[:, None], jnp.ones((TILE, TILE), bool)])
    near = jnp.where(causal[None], near, NEG)

    if by_lines:
        high = (me & 1) != 0
    else:
        grads_here = all_to_all(grads_sent)

    qkv, normed_one, qkv_weight, output_own = norm_and_project(
        micro_arg, layer_input, gain_one, a_own, a_far, pair_b[0], pair_b[1]
    )
    output_far = swap_core(output_own)
    mixed, logs = attend(length, qkv, near)
    mixed, output_far = together(mixed, output_far)
    mixed_far = swap_core(mixed)
    code_chunks = jnp.where(here, chunk_of * chunk_rows + route * chunk + inside, -1)
    if by_lines:
        sent_x = lax.dynamic_index_in_dim(grads_z, 1 - (me & 1), 1, keepdims=False)
        mixed_far, grads_z, sent_x = together(mixed_far, grads_z, sent_x)
        got_x = swap(sent_x, "dp", dp_count, 1)
    residual, *parts = residual_and_rows(
        micro_arg, layer_input, mixed, mixed_far, output_own, output_far, gain_two, code_chunks, chunk_rows, chunks
    )

    if by_lines:
        parts, grads_z, second_y, first_own = together(parts, grads_z, second_y, first_own)
        kept_x = jnp.where(high, grads_z[:, 1], grads_z[:, 0])
        pair_x = jnp.where(high, jnp.stack([got_x, kept_x], 1), jnp.stack([kept_x, got_x], 1))
        grads_here = pair_x.reshape(dp_count, stride, width)
    else:
        parts, grads_here, second_y, first_own = together(parts, grads_here, second_y, first_own)
    parts = [part.reshape(expert_count, chunk, width) for part in parts]
    arrived = [all_to_all(parts[0])]
    first_y = swap_y(first_own)

    def by_chunk(rows):
        return jnp.swapaxes(rows.reshape((expert_count, chunks, chunk) + rows.shape[2:]), 0, 1)

    grads_all = by_chunk(grads_here[:, :half]).reshape(chunks * chunk_rows, width)
    block = row_block(chunk_rows)
    partner_all = by_chunk(grads_here[:, half, :half].astype(jnp.int32)).reshape(chunks * chunk_rows // block, 1, block)
    seconds = (second_own, second_y, swap_core(second_own), swap_core(second_y))
    arrived[0], grads_all, partner_all = together(arrived[0], grads_all, partner_all)
    plain = plain_grads(grads_all, seconds)
    for c in range(1, chunks):
        sent, arrived[-1] = together(parts[c], arrived[-1])
        arrived.append(all_to_all(sent))

    firsts = (first_own, first_y, swap_core(first_own), swap_core(first_y))
    me_arg = me.reshape(1).astype(jnp.int32)
    rows_all, slopes, active, gated, gates, backs = [], [], [], [], [], []
    line = None
    for c in range(chunks):
        rows_c = arrived[c].reshape(chunk_rows, width)
        back, act, slo, gat, gte, line = expert_rows_pass(
            c * chunk if chunks > 1 else None, chunk, half, me_arg, partner_all, rows_c, grads_all, plain, router_wide, line,
            firsts, c,
        )
        rows_all.append(rows_c)
        slopes.append(slo)
        active.append(act)
        gated.append(gat)
        gates.append(gte)
        if chunks == 1:
            gate_grad = line[:, 0].reshape(expert_count, chunk)
            pieces = []
            for _ in range(3):
                piece = gate_grad.astype(BF)
                pieces.append(piece)
                gate_grad = gate_grad - piece.astype(F32)
            gate_row = jnp.pad(jnp.concatenate(pieces, 1), ((0, 0), (0, width - 3 * half)))
            back = jnp.pad(back.reshape(expert_count, chunk, width), ((0, 0), (0, last_stride - chunk), (0, 0)))
            back = back.at[:, spare].set(gate_row)
        if c + 1 < chunks:
            back, arrived[c + 1] = together(back.reshape(expert_count, chunk, width), arrived[c + 1])
        else:
            back, rows_all[-1], backs = together(back, rows_all[-1], backs)
        backs.append(all_to_all(back))
    grads_cross = cross_weight_grads(rows_all, slopes, active, gated)
    gates, grads_cross = together(gates, grads_cross)
    grads_in = swap_core(grads_cross)
    results = expert_results(active, gates, seconds, expert_count)
    results, grads_in = together(results, grads_in)
    grads_far, grads_kept = kept_weight_grads(rows_all, slopes, active, gated, grads_in)
    backs[-1], results, grads_far = together(backs[-1], results, grads_far)

    across_y = swap_y(grads_far)
    results_own = all_to_all(results).reshape(expert_count * half, width)

    backs_far = [swap_core(b) for b in backs]
    residual_grad, mixed_grad, extra_early, output_sent, output_kept = combine(
        micro_arg, core_arg, length, info, out_grad, residual, mixed, gain_two, router_wide, output_own,
        backs + backs_far, half, spare,
    )

    tiles, sums, far_sent, own_parts, sent, kept_part = attend_back(
        core_arg, length, qkv, near, mixed, logs, mixed_grad, normed_one, output_sent, qkv_weight
    )
    far_got = swap_y(far_sent)
    sent, results_own = together(sent, results_own)
    got = swap_core(sent)
    rows_both, extra_late = both_rows(
        expert_count, micro_arg, core_arg, length, kept_part, got, layer_input, gain_one, residual_grad,
        info, residual, results_own, swap_core(results_own),
    )
    rows_both, across_y, tiles = together(rows_both, across_y, tiles)
    late_far = swap_core(extra_late)
    corner = micro * 2 + core
    corners = jnp.stack([corner, corner ^ 1, corner ^ 2, corner ^ 3]).astype(jnp.int32)
    rows_y = swap_y(rows_both)
    expert_in_grad, expert_out_grad = last_sums(grads_kept, across_y)
    rows_y, expert_in_grad, expert_out_grad = together(rows_y, expert_in_grad, expert_out_grad)
    pieces = (rows_both, swap_core(rows_both), rows_y, swap_core(rows_y))

    tiles = tiles.reshape(head_total, 2 * TILE * TILE)
    tiles_high = tiles.astype(BF)
    tiles_rest = (tiles - tiles_high.astype(F32)).astype(BF)
    table = dot(tiles_high, hot_const, NT) + dot(tiles_rest, hot_const, NT)
    far_sum = jnp.sum(sums[:, :, 0], axis=1) - jnp.sum(table[:, : NB - 1], axis=1)
    table = jnp.concatenate([table[:, : NB - 1], far_sum[:, None]], 1)
    table_own = jnp.concatenate([table[0:2], table[4:5]], 0)
    table_far = jnp.concatenate([table[2:4], table[5:6]], 0)
    table_cols = heads_here * NB // rows_here
    table_both = jnp.concatenate([table_own.reshape(rows_here, table_cols), table_far.reshape(rows_here, table_cols)], 1)
    base = expert_count + 2
    kept = base + 2 * table_cols
    table_tile = jnp.tile(jnp.pad(table_both, ((0, 0), (base, TILE - kept))), (dp_count, 1))

    grads = packed_sums(kept, own_parts, far_got, output_kept, extra_early, extra_late, late_far, table_tile)
    arrived_grads = all_to_all(grads.reshape(dp_count, rows_here, grads.shape[1]))
    layer_output, input_grad = (out.reshape(2, SEQ, width) for out in place_pieces(corners, pieces))
    arrived_grads, layer_output, input_grad = together(arrived_grads, layer_output, input_grad)
    query_grad, key_grad, value_grad, output_grad, small = final_sums(kept, arrived_grads, shard)
    small_y = swap_y(small)
    both = small + small_y
    table_sum = small[:, base : base + table_cols] + small_y[:, base + table_cols : kept]
    return (
        layer_output,
        input_grad,
        both[:, expert_count],
        query_grad,
        key_grad,
        value_grad,
        output_grad.T,
        table_sum.reshape(heads_here, NB),
        both[:, expert_count + 1],
        both[:, :expert_count],
        expert_in_grad[None],
        expert_out_grad[None],
    )


def solution(mesh):
    return jax.shard_map(
        local,
        mesh=mesh,
        in_specs=(
            P(None, "dp", None),
            P(None, "dp", None),
            P("dp"),
            P("dp", "tensor"),
            P("dp", "tensor"),
            P("dp", "tensor"),
            P("tensor", "dp"),
            P("tensor", None),
            P("dp"),
            P("dp", None),
            P("dp", None, "tensor"),
            P("dp", "tensor", None),
            P(None, "dp"),
            P(None, "dp", None),
        ),
        out_specs=(
            P(None, "dp", None),
            P(None, "dp", None),
            P("dp"),
            P("dp", "tensor"),
            P("dp", "tensor"),
            P("dp", "tensor"),
            P("tensor", "dp"),
            P("tensor", None),
            P("dp"),
            P("dp", None),
            P("dp", None, "tensor"),
            P("dp", "tensor", None),
        ),
        check_vma=False,
    )
```

```python
import functools

import jax
import jax.numpy as jnp
import numpy as np
from jax import lax
from jax.experimental import pallas as pl
from jax.experimental.pallas import tpu as pltpu
from jax.sharding import PartitionSpec as P

HEAD_DIM = 64
NB = 32
SEQ = 1024
TILE = 128
QROWS = 256
NEG = -1e30
GELU_C = 0.7978845608028654
GELU_A = 0.044715

BF = jnp.bfloat16
F32 = jnp.float32

bucket_edges = np.ceil(16.0 * 8.0 ** (np.arange(1, 16) / 16.0)).astype(np.int32)


def near_tables():
    rows = np.arange(TILE)[:, None]
    cols = np.arange(TILE)[None, :]
    hots = []
    for shift in (0, TILE):
        distance = rows - cols + shift
        clipped = np.maximum(distance, 0)
        reached = np.sum(clipped[..., None] >= bucket_edges, axis=-1)
        bucket = np.minimum(clipped, 16) + reached
        hots.append(bucket[..., None] == np.arange(NB))
    hot = np.stack(hots).reshape(2 * TILE * TILE, NB).T
    return hot


NEAR_HOT = near_tables()
assert bucket_edges[-1] <= TILE


def dot(a, b, dims=((1,), (0,))):
    return lax.dot_general(a, b, (dims, ((), ())), preferred_element_type=F32)


NT = ((1,), (1,))
TN = ((0,), (0,))


MIB = 2**20
SMALL_COST = pl.CostEstimate(flops=1_000_000, bytes_accessed=1_000_000, transcendentals=0)


STRIP = 32


def score_strip(s, at, block, j, start, near_ref, half, length):
    part = s[at : at + STRIP]
    near = slice(start % TILE, start % TILE + STRIP)
    if j == block:
        if start < TILE:
            left = part[:, :TILE] + near_ref[half, 0, near, :]
            right = jnp.full((STRIP, TILE), NEG, F32)
        else:
            left = part[:, :TILE] + near_ref[half, 1, near, :]
            right = part[:, TILE:] + near_ref[half, 0, near, :]
        part = jnp.concatenate([left, right], 1)
    elif j == block - 1 and start < TILE:
        part = jnp.concatenate([part[:, :TILE], part[:, TILE:] + near_ref[half, 1, near, :]], 1)
    if (j + 1) * QROWS > SEQ // 2:
        place = lax.broadcasted_iota(jnp.int32, (1, QROWS), 1) + j * QROWS
        part = part + jnp.where(place < length, 0.0, NEG)
    return part


def lane_half(rows):
    return lax.broadcasted_iota(jnp.int32, (rows, 2 * HEAD_DIM), 1) < HEAD_DIM


def attend_kernel(length_ref, query_ref, key_ref, value_ref, near_ref, out_ref, log_ref):
    length = length_ref[0]
    lanes = lane_half(QROWS)
    value_ext = jnp.concatenate([value_ref[...], jnp.ones((SEQ, TILE), BF)], 1)
    for i in range(SEQ // QROWS):
        q_rows = query_ref[i * QROWS : (i + 1) * QROWS, :] * BF(0.125)
        q_both = jnp.concatenate([jnp.where(lanes, q_rows, BF(0)), jnp.where(lanes, BF(0), q_rows)], 0)
        tiles = [dot(q_both, key_ref[j * QROWS : (j + 1) * QROWS, :], NT) for j in range(i + 1)]
        tops = []
        weights = [[] for _ in tiles]
        for h in range(2):
            for start in range(0, QROWS, STRIP):
                strips = [
                    score_strip(s, h * QROWS + start, i, j, start, near_ref, h, length) for j, s in enumerate(tiles)
                ]
                top = strips[0]
                for s in strips[1:]:
                    top = jnp.maximum(top, s)
                top = jnp.max(top, axis=1, keepdims=True)
                tops.append(top)
                for j, s in enumerate(strips):
                    weights[j].append(jnp.exp(s - top).astype(BF))
        total = None
        for j, strips in enumerate(weights):
            total = put(total, dot(jnp.concatenate(strips, 0), value_ext[j * QROWS : (j + 1) * QROWS, :]))
        row_sum = total[:, TILE:]
        out = total[:, :TILE] / row_sum
        logs = jnp.concatenate(tops, 0) + jnp.log(row_sum)
        out_ref[i * QROWS : (i + 1) * QROWS, :] = jnp.where(lanes, out[:QROWS], out[QROWS:]).astype(BF)
        log_ref[i * QROWS : (i + 1) * QROWS, :] = jnp.where(lanes, logs[:QROWS], logs[QROWS:])


def attend(length, qkv, near):
    pairs = qkv.shape[1] // (3 * TILE)
    cols = pairs * TILE
    return pl.pallas_call(
        attend_kernel,
        grid=(pairs,),
        in_specs=[
            pl.BlockSpec(memory_space=pltpu.SMEM),
            pl.BlockSpec((SEQ, TILE), lambda p: (0, p)),
            pl.BlockSpec((SEQ, TILE), lambda p: (0, pairs + p)),
            pl.BlockSpec((SEQ, TILE), lambda p: (0, 2 * pairs + p)),
            pl.BlockSpec((2, 2, TILE, TILE), lambda p: (p, 0, 0, 0)),
        ],
        out_specs=[
            pl.BlockSpec((SEQ, TILE), lambda p: (0, p)),
            pl.BlockSpec((SEQ, TILE), lambda p: (0, p)),
        ],
        out_shape=[
            jax.ShapeDtypeStruct((SEQ, cols), BF),
            jax.ShapeDtypeStruct((SEQ, cols), F32),
        ],
        compiler_params=pltpu.CompilerParams(vmem_limit_bytes=40 * MIB),
        cost_estimate=SMALL_COST,
        name="attend",
    )(length, qkv, qkv, qkv, near)


def attend_back_kernel(
    pairs, blocks, core_ref, length_ref, query_ref, key_ref, value_ref, near_ref, out_ref, log_ref, grad_ref,
    normed_ref, output_ref, weight_ref, tile_ref, sum_ref, far_ref, own_ref, sent_ref, kept_ref, grads, dk_acc, dv_acc,
):
    step = pl.program_id(0)

    @pl.when(step < pairs)
    def _():
        pair_grads(
            step, length_ref, query_ref, key_ref, value_ref, near_ref, out_ref, log_ref, grad_ref,
            tile_ref, sum_ref, grads, dk_acc, dv_acc,
        )

    @pl.when((step >= pairs) & (step < pairs + blocks))
    def _():
        low = low_lanes((normed_ref.shape[1], TILE))
        q, k, v = (
            dot(normed_ref[...], jnp.concatenate([grads[n, p] for p in range(pairs)], 1), TN) for n in range(3)
        )
        for n, part in enumerate((q, k, v)):
            own_ref[:, n * TILE : (n + 1) * TILE] = part[:, :TILE]
            far_ref[:, n * TILE : (n + 1) * TILE] = part[:, TILE : 2 * TILE].astype(BF)
        q, k, v = (part[:, 2 * TILE :] for part in (q, k, v))
        far_ref[:, 3 * TILE : 4 * TILE] = jnp.where(low, turned(q), k).astype(BF)
        far_ref[:, 4 * TILE : 5 * TILE] = jnp.where(low, turned(v), output_ref[:, TILE:].astype(F32)).astype(BF)
        far_ref[:, 5 * TILE :] = output_ref[:, :TILE]
        own_ref[:, 3 * TILE : 4 * TILE] = jnp.where(low, q, turned(k))
        own_ref[:, 4 * TILE :] = jnp.where(low, v, 0.0)

    for late, half_ref in enumerate((sent_ref, kept_ref)):
        first = pairs + blocks + 2 * late

        @pl.when((step >= first) & (step < first + 2))
        def _(half_ref=half_ref, first=first, late=late):
            rows = half_ref.shape[0]
            mine = core_ref[0] if late else 1 - core_ref[0]
            start = pl.multiple_of((2 * mine + step - first) * rows, rows)
            total = None
            for n in range(3):
                part = jnp.concatenate([grads[n, p, pl.ds(start, rows), :] for p in range(pairs)], 1)
                cols = part.shape[1]
                total = put(total, dot(part, weight_ref[:, n * cols : (n + 1) * cols], NT))
            half_ref[...] = total


def pair_grads(
    pair, length_ref, query_ref, key_ref, value_ref, near_ref, out_ref, log_ref, grad_ref, tile_ref, sum_ref, grads, dk_acc, dv_acc
):
    length = length_ref[0]
    lanes = lane_half(QROWS)
    key_ext = jnp.concatenate([key_ref[...], jnp.ones((SEQ, TILE), BF)], 1)
    near_sums = [[None, None], [None, None]]
    all_sums = [None, None]

    def both(rows):
        return jnp.concatenate([jnp.where(lanes, rows, BF(0)), jnp.where(lanes, BF(0), rows)], 0)

    for i in range(SEQ // QROWS):
        rows = slice(i * QROWS, (i + 1) * QROWS)
        q_both = both(query_ref[rows, :] * BF(0.125))
        g_rows = grad_ref[rows, :]
        g_both = both(g_rows)
        mass = g_rows.astype(F32) * out_ref[rows, :].astype(F32)
        deltas = [
            jnp.sum(jnp.where(lanes, mass, 0.0), axis=1, keepdims=True),
            jnp.sum(jnp.where(lanes, 0.0, mass), axis=1, keepdims=True),
        ]
        logs = [log_ref[rows, h * HEAD_DIM : h * HEAD_DIM + 1] for h in range(2)]
        dq = None
        for j in range(i + 1):
            keys = slice(j * QROWS, (j + 1) * QROWS)
            s = dot(q_both, key_ref[keys, :], NT)
            dp = dot(g_both, value_ref[keys, :], NT)
            p_strips, d_strips = [], []
            for h in range(2):
                for start in range(0, QROWS, STRIP):
                    strip = slice(start, start + STRIP)
                    at = h * QROWS + start
                    p = jnp.exp(score_strip(s, at, i, j, start, near_ref, h, length) - logs[h][strip])
                    p_strips.append(p.astype(BF))
                    d_strips.append((p * (dp[at : at + STRIP] - deltas[h][strip])).astype(BF))
            p, ds = jnp.concatenate(p_strips, 0), jnp.concatenate(d_strips, 0)
            part = dot(ds, key_ext[keys, :])
            dq = put(dq, jnp.where(lanes, part[:QROWS, :TILE], part[QROWS:, :TILE]))
            for h in range(2):
                sums = part[h * QROWS : (h + 1) * QROWS, TILE:]
                all_sums[h] = put(all_sums[h], jnp.sum(sums.reshape(QROWS // 8, 8, TILE), axis=0))
            dk_part = dot(ds, q_both, TN)
            dv_part = dot(p, g_both, TN)
            if i == j:
                dk_acc[keys, :] = dk_part
                dv_acc[keys, :] = dv_part
            else:
                dk_acc[keys, :] += dk_part
                dv_acc[keys, :] += dv_part
            for h in range(2):
                mine = ds[h * QROWS : (h + 1) * QROWS]
                if j == i:
                    wide = mine.astype(F32)
                    near_sums[h][0] = put(near_sums[h][0], wide[:TILE, :TILE] + wide[TILE:, TILE:])
                    near_sums[h][1] = put(near_sums[h][1], wide[TILE:, :TILE])
                elif j == i - 1:
                    near_sums[h][1] = put(near_sums[h][1], mine[:TILE, TILE:].astype(F32))
        grads[0, pair, rows, :] = (dq * 0.125).astype(BF)
    grads[1, pair] = dk_acc[...].astype(BF)
    grads[2, pair] = dv_acc[...].astype(BF)
    for h in range(2):
        tile_ref[h, 0] = near_sums[h][0]
        tile_ref[h, 1] = near_sums[h][1]
        sum_ref[h] = all_sums[h]


def attend_back(core, length, qkv, near, mixed, logs, grad, normed, output, weight):
    pairs = qkv.shape[1] // (3 * TILE)
    width = normed.shape[1]
    block = 256
    blocks = width // block
    at = lambda i: jnp.minimum(i, pairs - 1)
    then = lambda i: jnp.clip(i - pairs, 0, blocks - 1)
    return pl.pallas_call(
        functools.partial(attend_back_kernel, pairs, blocks),
        grid_spec=pltpu.PrefetchScalarGridSpec(
            num_scalar_prefetch=2,
            grid=(pairs + blocks + 4,),
            in_specs=[
                pl.BlockSpec((SEQ, TILE), lambda i, *_: (0, at(i))),
                pl.BlockSpec((SEQ, TILE), lambda i, *_: (0, pairs + at(i))),
                pl.BlockSpec((SEQ, TILE), lambda i, *_: (0, 2 * pairs + at(i))),
                pl.BlockSpec((2, 2, TILE, TILE), lambda i, *_: (at(i), 0, 0, 0)),
            ]
            + [pl.BlockSpec((SEQ, TILE), lambda i, *_: (0, at(i)))] * 3
            + [
                pl.BlockSpec((SEQ, block), lambda i, *_: (0, then(i))),
                pl.BlockSpec((block, 2 * TILE), lambda i, *_: (then(i), 0)),
                pl.BlockSpec(weight.shape, lambda i, *_: (0, 0)),
            ],
            out_specs=[
                pl.BlockSpec((2, 2, TILE, TILE), lambda i, *_: (at(i), 0, 0, 0)),
                pl.BlockSpec((2, 8, TILE), lambda i, *_: (at(i), 0, 0)),
                pl.BlockSpec((block, 6 * TILE), lambda i, *_: (then(i), 0)),
                pl.BlockSpec((block, 5 * TILE), lambda i, *_: (then(i), 0)),
                pl.BlockSpec((block, width), lambda i, *_: (jnp.clip(i - pairs - blocks, 0, 1), 0)),
                pl.BlockSpec((block, width), lambda i, *_: (jnp.clip(i - pairs - blocks - 2, 0, 1), 0)),
            ],
            scratch_shapes=[
                pltpu.VMEM((3, pairs, SEQ, TILE), BF), pltpu.VMEM((SEQ, TILE), F32), pltpu.VMEM((SEQ, TILE), F32),
            ],
        ),
        out_shape=[
            jax.ShapeDtypeStruct((2 * pairs, 2, TILE, TILE), F32),
            jax.ShapeDtypeStruct((2 * pairs, 8, TILE), F32),
            jax.ShapeDtypeStruct((width, 6 * TILE), BF),
            jax.ShapeDtypeStruct((width, 5 * TILE), F32),
            jax.ShapeDtypeStruct((2 * block, width), F32),
            jax.ShapeDtypeStruct((2 * block, width), F32),
        ],
        compiler_params=pltpu.CompilerParams(vmem_limit_bytes=40 * MIB),
        cost_estimate=SMALL_COST,
        name="attend_back",
    )(core, length, qkv, qkv, qkv, near, mixed, logs, grad, normed, output, weight)


def low_lanes(shape):
    return lax.broadcasted_iota(jnp.int32, shape, 1) < HEAD_DIM


def turned(tile):
    return pltpu.roll(tile, HEAD_DIM, 1)


def pack_kernel(q_ref, k_ref, v_ref, o_ref, one_ref, two_ref, router_ref, out_ref):
    shard = q_ref.shape[1]
    rows = q_ref.shape[0]
    source = lax.broadcasted_iota(jnp.int32, (shard, 6 * TILE), 0)
    target = lax.broadcasted_iota(jnp.int32, (shard, 6 * TILE), 1)

    def moved(pair_base, last_base):
        want = jnp.where(source < TILE, source + pair_base, source - TILE + last_base)
        return jnp.where(target == want, 1.0, 0.0).astype(BF)

    total = dot(v_ref[...], moved(0, 2 * TILE)) + dot(o_ref[...], moved(TILE, 2 * TILE + HEAD_DIM), TN)
    total = total + dot(q_ref[...], moved(3 * TILE, 5 * TILE)) + dot(k_ref[...], moved(4 * TILE, 5 * TILE + HEAD_DIM))
    out_ref[:, : 6 * TILE] = total.astype(BF)
    experts = router_ref.shape[0]
    own_row = lax.broadcasted_iota(jnp.int32, (rows, rows), 0) == lax.broadcasted_iota(jnp.int32, (rows, rows), 1)

    def column(ref):
        return jnp.sum(jnp.where(own_row, ref[...].astype(F32), 0.0), axis=1, keepdims=True)

    lanes = lax.broadcasted_iota(jnp.int32, (experts, TILE), 1)
    spread = jnp.where(lanes == lax.broadcasted_iota(jnp.int32, (experts, TILE), 0), 1.0, 0.0).astype(BF)
    place = lax.broadcasted_iota(jnp.int32, (rows, TILE), 1)
    small = dot(router_ref[...], spread, TN)
    small = jnp.where(place == experts, column(one_ref), jnp.where(place == experts + 1, column(two_ref), small))
    out_ref[:, 6 * TILE :] = small.astype(BF)


def pack_weights(query, key, value, output, one, two, router):
    rows = query.shape[0]
    return pl.pallas_call(
        pack_kernel,
        out_shape=jax.ShapeDtypeStruct((rows, 7 * TILE), BF),
        compiler_params=pltpu.CompilerParams(vmem_limit_bytes=60 * MIB),
        cost_estimate=SMALL_COST,
        name="pack_weights",
    )(query, key, value, output, one[None], two[None], router.T)


def qkv_kernel(micro_ref, tokens_ref, gain_ref, a_own, a_far, b_own, b_far, qkv_ref, normed_ref, weight_ref, output_ref):
    width = tokens_ref.shape[2]

    @pl.when(pl.program_id(0) == 0)
    def _():
        low = low_lanes((width, TILE))

        def tiles(own, far, pair, low_half):
            at = slice(pair * TILE, (pair + 1) * TILE)
            one, two = own[:, 2 * TILE :].astype(F32), far[:, 2 * TILE :].astype(F32)
            last = jnp.where(low, one, turned(two)) if low_half else jnp.where(low, turned(one), two)
            return own[:, at], far[:, at], last.astype(BF)

        for n, (own, far, pair, low_half) in enumerate(
            ((a_own, a_far, 0, True), (a_own, a_far, 1, False), (b_own, b_far, 0, True))
        ):
            for t, tile in enumerate(tiles(own[...], far[...], pair, low_half)):
                at = 3 * n + t
                weight_ref[:, at * TILE : (at + 1) * TILE] = tile
        for t, tile in enumerate(tiles(b_own[...], b_far[...], 1, False)):
            output_ref[:, t * TILE : (t + 1) * TILE] = tile

    x = tokens_ref[0].astype(F32)
    inverse = lax.rsqrt(jnp.mean(x * x, axis=-1, keepdims=True) + 1e-06)
    normed = (x * inverse * gain_ref[...]).astype(BF)
    normed_ref[...] = normed
    qkv_ref[...] = dot(normed, weight_ref[...]).astype(BF)


def norm_and_project(micro, layer_input, gain, a_own, a_far, b_own, b_far):
    width = layer_input.shape[2]
    block = 256
    cols = 3 * TILE
    whole = lambda rows, n: pl.BlockSpec((rows, n), lambda i, m: (0, 0))
    here = lambda n: pl.BlockSpec((block, n), lambda i, m: (i, 0))
    return pl.pallas_call(
        qkv_kernel,
        grid_spec=pltpu.PrefetchScalarGridSpec(
            num_scalar_prefetch=1,
            grid=(SEQ // block,),
            in_specs=[pl.BlockSpec((1, block, width), lambda i, m: (m[0], i, 0)), whole(1, width)] + [whole(width, cols)] * 4,
            out_specs=[here(3 * cols), here(width), whole(width, 3 * cols), whole(width, cols)],
        ),
        out_shape=[
            jax.ShapeDtypeStruct((SEQ, 3 * cols), BF),
            jax.ShapeDtypeStruct((SEQ, width), BF),
            jax.ShapeDtypeStruct((width, 3 * cols), BF),
            jax.ShapeDtypeStruct((width, cols), BF),
        ],
        compiler_params=pltpu.CompilerParams(vmem_limit_bytes=40 * MIB),
        cost_estimate=SMALL_COST,
        name="norm_and_project",
    )(micro, layer_input, gain, a_own, a_far, b_own, b_far)


def middle_kernel(
    blocks, per, micro_ref, tokens_ref, mixed_ref, other_ref, own_ref, far_ref, gain_ref, code_ref, residual_ref, *refs
):
    sent_refs, normed = refs[:-1], refs[-1]
    step = pl.program_id(0)
    rows = tokens_ref.shape[1]

    @pl.when(step < blocks)
    def _():
        total = tokens_ref[0].astype(F32) + dot(mixed_ref[...], own_ref[...], NT) + dot(other_ref[...], far_ref[...], NT)
        residual_ref[...] = total
        inverse = lax.rsqrt(jnp.mean(total * total, axis=-1, keepdims=True) + 1e-06)
        normed[pl.ds(pl.multiple_of(step * rows, rows), rows), :] = (total * inverse * gain_ref[...]).astype(BF)

    for c, sent_ref in enumerate(sent_refs):

        @pl.when((step >= blocks + c * per) & (step < blocks + (c + 1) * per))
        def _(sent_ref=sent_ref):
            block = sent_ref.shape[0]
            ids = lax.broadcasted_iota(jnp.int32, (block, 1), 0) + (step - blocks) * block
            hot = jnp.where((ids == code_ref[:1]) | (ids == code_ref[1:2]), 1.0, 0.0).astype(BF)
            sent_ref[...] = dot(hot, normed[...]).astype(BF)


def residual_and_rows(micro, layer_input, mixed, other, output_own, output_far, gain, code, count, chunks):
    width = layer_input.shape[2]
    block = 256
    blocks = SEQ // block
    send = 320
    cols = mixed.shape[1]
    per = count // send
    at = lambda i: jnp.minimum(i, blocks - 1)
    whole = lambda arr: pl.BlockSpec(arr.shape, lambda i, m: (0, 0))
    here = lambda n: pl.BlockSpec((block, n), lambda i, m: (at(i), 0))

    def sent(c):
        return pl.BlockSpec((send, width), lambda i, m: (jnp.clip(i - blocks - c * per, 0, per - 1), 0))

    return pl.pallas_call(
        functools.partial(middle_kernel, blocks, per),
        grid_spec=pltpu.PrefetchScalarGridSpec(
            num_scalar_prefetch=1,
            grid=(blocks + chunks * per,),
            in_specs=[
                pl.BlockSpec((1, block, width), lambda i, m: (m[0], at(i), 0)),
                here(cols), here(cols), whole(output_own), whole(output_far), whole(gain), whole(code),
            ],
            out_specs=[here(width)] + [sent(c) for c in range(chunks)],
            scratch_shapes=[pltpu.VMEM((SEQ, width), BF)],
        ),
        out_shape=[jax.ShapeDtypeStruct((SEQ, width), F32)] + [jax.ShapeDtypeStruct((count, width), BF)] * chunks,
        compiler_params=pltpu.CompilerParams(vmem_limit_bytes=40 * MIB),
        cost_estimate=SMALL_COST,
        name="residual_and_rows",
    )(micro, layer_input, mixed, other, output_own, output_far, gain, code)


def picked_rows(first, second, segments):
    total = None
    start = 0
    for rows in segments:
        length = rows.shape[0]
        ids = lax.broadcasted_iota(jnp.int32, (1, length), 1) + start
        hot = []
        for at in range(0, first.shape[0], STRIP):
            one, two = first[at : at + STRIP], second[at : at + STRIP]
            hot.append(jnp.where((one == ids) | (two == ids), 1.0, 0.0).astype(BF))
        total = put(total, dot(jnp.concatenate(hot, 0), rows))
        start += length
    return total


def put(a, b):
    return b if a is None else a + b


def folded(product):
    return jnp.sum(product.reshape(product.shape[0] // 8, 8, product.shape[1]), axis=0)


def as_column(eight):
    ones = jnp.ones((16, TILE), BF)
    high = eight.astype(BF)
    rest = (eight - high.astype(F32)).astype(BF)
    return dot(jnp.concatenate([high, rest], 0), ones, TN)


def combine_kernel(experts, half, spare, micro_ref, core_ref, length_ref, *refs):
    info_ref, grad_ref, residual_ref, mixed_ref, gain_ref, router_ref, output_ref = refs[:7]
    backs = refs[7:-9]
    (total_ref, mixed_grad_ref, extra_ref, far_ref, own_ref, acc_ref, router_acc, gain_acc, tables) = refs[-9:]
    block = residual_ref.shape[0]
    step = pl.program_id(0)
    count = len(backs) // 2

    @pl.when(step == 0)
    def _():
        place = lax.broadcasted_iota(jnp.int32, (experts, 1), 0)
        for n, back in enumerate((backs[count - 1], backs[2 * count - 1])):
            table = jnp.zeros((experts, back.shape[2]), F32)
            for e in range(experts):
                row = back[e, spare : spare + 16, :].astype(F32)[:1]
                table = jnp.where(place == e, row, table)
            for piece in range(3):
                at = (3 * n + piece) * experts
                tables[at : at + experts] = table[:, piece * half : (piece + 1) * half]

    info = jnp.transpose(info_ref[...])
    number = lambda n: info[:, n : n + 1]
    columns = lax.broadcasted_iota(jnp.int32, (1, half), 1)
    lanes = lax.broadcasted_iota(jnp.int32, (1, 6 * experts), 1)
    table = tables[...].astype(BF)
    values = []
    for k in range(2):
        slot = number(4 + k)
        hot = jnp.where(columns == lax.rem(slot, half), 1.0, 0.0).astype(BF)
        found = dot(hot, table, NT)
        wanted = jnp.where(slot // half == core_ref[0], 0, 3 * experts) + number(2 + k)
        away = lanes - wanted
        hit = (away == 0) | (away == experts) | (away == 2 * experts)
        values.append(jnp.sum(jnp.where(hit, found, 0.0), axis=1, keepdims=True))
    wide = lax.broadcasted_iota(jnp.int32, (1, TILE), 1)
    is_first, is_second = wide == number(2), wide == number(3)
    residual = residual_ref[...]
    gain = gain_ref[...]
    inverse = lax.rsqrt(jnp.mean(residual * residual, axis=-1, keepdims=True) + 1e-06)
    plain = residual * inverse
    normed = (plain * gain).astype(BF)
    logits = dot(normed, router_ref[...])
    gap = jnp.sum(jnp.where(is_first, logits, 0.0) - jnp.where(is_second, logits, 0.0), axis=1, keepdims=True)
    small = jnp.exp(-jnp.abs(gap))
    logit = small / ((1.0 + small) * (1.0 + small)) * (values[0] - values[1])
    logit_grad = jnp.where(is_first, logit, jnp.where(is_second, -logit, 0.0)).astype(BF)
    segments = [b[...].reshape(b.shape[0] * b.shape[1], b.shape[2]) for b in backs]
    normed_grad = picked_rows(number(0), number(1), segments) + dot(logit_grad, router_ref[...], NT)
    scaled = normed_grad * gain
    mean = jnp.mean(scaled * plain, axis=-1, keepdims=True)
    place = lax.broadcasted_iota(jnp.int32, (block, 1), 0) + step * block
    grad_out = jnp.where(place < length_ref[0], grad_ref[0].astype(F32), 0.0)
    total = grad_out + inverse * (scaled - plain * mean)

    @pl.when(step == core_ref[0])
    def _():
        total_ref[...] = total

    branch = total.astype(BF)
    mixed_grad_ref[...] = dot(branch, output_ref[...]).astype(BF)
    router_part = dot(logit_grad, normed, TN)
    gain_part = folded(normed_grad * plain)
    output_part = dot(mixed_ref[...], branch, TN)

    @pl.when(step == 0)
    def _():
        router_acc[...] = router_part
        gain_acc[...] = gain_part
        acc_ref[...] = output_part

    @pl.when(step > 0)
    def _():
        router_acc[...] += router_part
        gain_acc[...] += gain_part
        acc_ref[...] += output_part

    @pl.when(step == pl.num_programs(0) - 1)
    def _():
        extra_ref[...] = jnp.transpose(router_acc[...]) + jnp.where(wide == experts + 1, as_column(gain_acc[...]), 0.0)
        parts = jnp.transpose(acc_ref[...])
        far_ref[...] = parts[:, TILE:].astype(BF)
        own_ref[:, :TILE] = parts[:, :TILE]
        own_ref[:, TILE:] = parts[:, 2 * TILE :]


def combine(micro, core, length, info, out_grad, residual, mixed, gain, router, output_own, backs, half, spare):
    width = residual.shape[1]
    block = 512
    cols = mixed.shape[1]
    whole = lambda arr: pl.BlockSpec(arr.shape, lambda i, *_: (0,) * arr.ndim)
    fixed = lambda rows, n: pl.BlockSpec((rows, n), lambda i, *_: (0, 0))
    here = lambda n: pl.BlockSpec((block, n), lambda i, *_: (i, 0))
    experts = backs[0].shape[0]
    return pl.pallas_call(
        functools.partial(combine_kernel, experts, half, spare),
        grid_spec=pltpu.PrefetchScalarGridSpec(
            num_scalar_prefetch=3,
            grid=(SEQ // block,),
            in_specs=[
                pl.BlockSpec((8, block), lambda i, *_: (0, i)),
                pl.BlockSpec((1, block, width), lambda i, m, *_: (m[0], i, 0)),
                here(width), here(cols), whole(gain), whole(router), whole(output_own),
            ]
            + [whole(x) for x in backs],
            out_specs=[fixed(block, width), here(cols), fixed(width, TILE), fixed(width, 2 * TILE), fixed(width, 2 * TILE)],
            scratch_shapes=[
                pltpu.VMEM((cols, width), F32),
                pltpu.VMEM((TILE, width), F32),
                pltpu.VMEM((8, width), F32),
                pltpu.VMEM((6 * experts, half), F32),
            ],
        ),
        out_shape=[
            jax.ShapeDtypeStruct((block, width), F32),
            jax.ShapeDtypeStruct((SEQ, cols), BF),
            jax.ShapeDtypeStruct((width, TILE), F32),
            jax.ShapeDtypeStruct((width, 2 * TILE), BF),
            jax.ShapeDtypeStruct((width, 2 * TILE), F32),
        ],
        compiler_params=pltpu.CompilerParams(vmem_limit_bytes=40 * MIB),
        cost_estimate=SMALL_COST,
        name="combine",
    )(micro, core, length, info, out_grad, residual, mixed, gain, router, output_own, *backs)


def both_kernel(
    lane, micro_ref, core_ref, length_ref, part_ref, got_ref, tokens_ref, gain_ref, grad_ref,
    info_ref, residual_ref, own_ref, far_ref, out_ref, extra_ref, acc_ref,
):
    block = residual_ref.shape[0]
    info = jnp.transpose(info_ref[...])
    place = lax.broadcasted_iota(jnp.int32, (block, 1), 0) + (core_ref[0] * 2 + pl.program_id(0)) * block
    rows = residual_ref[...] + picked_rows(info[:, 6:7], info[:, 7:8], (own_ref[...], far_ref[...]))
    out_ref[0] = jnp.where(place < length_ref[0], rows, 0.0).astype(BF)
    normed_grad = got_ref[...] + part_ref[...]
    x = tokens_ref[0].astype(F32)
    inverse = lax.rsqrt(jnp.mean(x * x, axis=-1, keepdims=True) + 1e-06)
    plain = x * inverse
    scaled = normed_grad * gain_ref[...]
    mean = jnp.mean(scaled * plain, axis=-1, keepdims=True)
    out_ref[1] = (grad_ref[...] + inverse * (scaled - plain * mean)).astype(BF)
    wide = lax.broadcasted_iota(jnp.int32, (1, TILE), 1)
    part = folded(normed_grad * plain)

    @pl.when(pl.program_id(0) == 0)
    def _():
        acc_ref[...] = part

    @pl.when(pl.program_id(0) == 1)
    def _():
        extra_ref[...] = jnp.where(wide == lane, as_column(acc_ref[...] + part), 0.0)


def both_rows(lane, micro, core, length, part, got, layer_input, gain, residual_grad, info, residual, own, far):
    width = part.shape[1]
    plain = pl.BlockSpec((256, width), lambda i, *_: (i, 0))
    block = 256
    here = lambda n: pl.BlockSpec((block, n), lambda i, m, c, *_: (c[0] * 2 + i, 0))
    whole = lambda arr: pl.BlockSpec(arr.shape, lambda i, *_: (0, 0))
    return pl.pallas_call(
        functools.partial(both_kernel, lane),
        grid_spec=pltpu.PrefetchScalarGridSpec(
            num_scalar_prefetch=3,
            grid=(2,),
            in_specs=[
                plain,
                plain,
                pl.BlockSpec((1, block, width), lambda i, m, c, *_: (m[0], c[0] * 2 + i, 0)),
                whole(gain),
                plain,
                pl.BlockSpec((8, block), lambda i, m, c, *_: (0, c[0] * 2 + i)),
                here(width),
                whole(own),
                whole(far),
            ],
            out_specs=[
                pl.BlockSpec((2, block, width), lambda i, *_: (0, i, 0)),
                pl.BlockSpec((width, TILE), lambda i, *_: (0, 0)),
            ],
            scratch_shapes=[pltpu.VMEM((8, width), F32)],
        ),
        out_shape=[jax.ShapeDtypeStruct((2, 2 * block, width), BF), jax.ShapeDtypeStruct((width, TILE), F32)],
        compiler_params=pltpu.CompilerParams(vmem_limit_bytes=40 * MIB),
        cost_estimate=SMALL_COST,
        name="both_rows",
    )(micro, core, length, part, got, layer_input, gain, residual_grad, info, residual, own, far)


def sum_kernel(kept, own, got, out_own, early, late, late_far, table, sum_ref):
    low = low_lanes(early.shape)
    sum_ref[:, : 4 * TILE] = (own[:, : 4 * TILE] + got[:, : 4 * TILE].astype(F32)).astype(BF)
    mixed = jnp.where(low, own[:, 4 * TILE :], turned(out_own[:, TILE:]))
    sum_ref[:, 4 * TILE : 5 * TILE] = (mixed + got[:, 4 * TILE : 5 * TILE].astype(F32)).astype(BF)
    sum_ref[:, 5 * TILE : 6 * TILE] = (out_own[:, :TILE] + got[:, 5 * TILE :].astype(F32)).astype(BF)
    extra = early[...] + late[...] + late_far[...] + table[...]
    high = extra.astype(BF)
    rest = extra - high.astype(F32)
    if kept <= HEAD_DIM:
        sum_ref[:, 6 * TILE :] = jnp.where(low, high.astype(F32), turned(rest)).astype(BF)
    else:
        sum_ref[:, 6 * TILE : 7 * TILE] = high
        sum_ref[:, 7 * TILE :] = rest.astype(BF)


def packed_sums(kept, *parts):
    width = parts[0].shape[0]
    cols = (7 if kept <= HEAD_DIM else 8) * TILE
    block = 256
    here = lambda n: pl.BlockSpec((block, n), lambda i: (i, 0))
    return pl.pallas_call(
        functools.partial(sum_kernel, kept),
        grid=(width // block,),
        in_specs=[here(x.shape[1]) for x in parts],
        out_specs=here(cols),
        out_shape=jax.ShapeDtypeStruct((width, cols), BF),
        compiler_params=pltpu.CompilerParams(vmem_limit_bytes=40 * MIB),
        cost_estimate=SMALL_COST,
        name="packed_sums",
    )(*parts)


def final_kernel(kept, parts_ref, q_ref, k_ref, v_ref, o_ref, small_ref):
    total = parts_ref[0].astype(F32)
    for n in range(1, parts_ref.shape[0]):
        total = total + parts_ref[n].astype(F32)
    tile = lambda t: total[:, t * TILE : (t + 1) * TILE]
    q_ref[:, :TILE] = tile(0)
    q_ref[:, TILE:] = tile(3)[:, :HEAD_DIM]
    k_ref[:, :TILE] = tile(1)
    k_ref[:, TILE:] = turned(tile(3))[:, :HEAD_DIM]
    v_ref[:, :TILE] = tile(2)
    v_ref[:, TILE:] = tile(4)[:, :HEAD_DIM]
    o_ref[:, :TILE] = tile(5)
    o_ref[:, TILE:] = turned(tile(4))[:, :HEAD_DIM]
    small_ref[...] = tile(6) + (turned(tile(6)) if kept <= HEAD_DIM else tile(7))


def final_sums(kept, parts, shard):
    rows = parts.shape[1]
    return pl.pallas_call(
        functools.partial(final_kernel, kept),
        out_shape=[jax.ShapeDtypeStruct((rows, shard), F32)] * 4 + [jax.ShapeDtypeStruct((rows, TILE), F32)],
        compiler_params=pltpu.CompilerParams(vmem_limit_bytes=40 * MIB),
        cost_estimate=SMALL_COST,
        name="final_sums",
    )(parts)


def pair_gate(logits, own, other):
    lanes = lax.broadcasted_iota(jnp.int32, logits.shape, 1)
    gap = jnp.sum(
        jnp.where(lanes == own, logits, 0.0) - jnp.where(lanes == other, logits, 0.0), axis=1, keepdims=True
    )
    small = jnp.exp(-jnp.abs(gap))
    return jnp.where(gap >= 0.0, 1.0, small) / (1.0 + small)


def expert_kernel(lead, chunk, half, me_ref, partner_ref, rows_ref, grads_ref, router_ref, *refs):
    before, refs = (refs[0], refs[1:]) if lead is not None and lead > 0 else (None, refs)
    plain_ref, firsts = refs[0], refs[1:5]
    back_ref, active_ref, slope_ref, gated_ref, gate_ref, mass_ref = refs[5:]
    rows = rows_ref[...]
    grads = grads_ref[...]
    partner = jnp.transpose(jnp.broadcast_to(partner_ref[0], (8, rows.shape[0])))[:, :1]
    gate = pair_gate(dot(rows, router_ref[...]), me_ref[0], partner)
    gated_ref[...] = (gate * grads.astype(F32)).astype(BF)
    gate_ref[...] = jnp.broadcast_to(gate, gate_ref.shape)
    masses = [None] * (rows.shape[0] // STRIP)
    back = None
    width = firsts[0].shape[1]
    step = 256
    places = [(r, c) for r in range(4) for c in range(0, width, step)]

    def products(r, c):
        return dot(rows, firsts[r][:, c : c + step])

    ahead = products(*places[0])
    for n, (r, c) in enumerate(places):
        x = ahead
        if n + 1 < len(places):
            ahead = products(*places[n + 1])
        place = slice(r * width + c, r * width + c + step)
        for at in range(0, rows.shape[0], STRIP):
            strip = slice(at, at + STRIP)
            value, flow = x[strip], plain_ref[strip, place].astype(F32)
            square = value * value
            bent = jnp.tanh(value * (GELU_C + (GELU_C * GELU_A) * square))
            rise = 0.5 + 0.5 * bent
            active = value * rise
            slope = rise + active * (1.0 - bent) * (GELU_C + (3.0 * GELU_C * GELU_A) * square)
            low = active.astype(BF)
            active_ref[strip, place] = low
            slope_ref[strip, place] = (gate[strip] * flow * slope).astype(BF)
            part = low.astype(F32) * flow
            masses[at // STRIP] = put(masses[at // STRIP], part[:, :TILE] + part[:, TILE:])
        if c + step == width and r > 0:
            back = put(back, dot(slope_ref[:, (r - 1) * width : r * width], firsts[r - 1][...], NT))
    back = put(back, dot(slope_ref[:, 3 * width :], firsts[3][...], NT))
    back = back.astype(BF)
    mass = jnp.sum(jnp.concatenate(masses, 0), axis=1, keepdims=True)
    if lead is None:
        back_ref[...] = back
        mass_ref[...] = jnp.broadcast_to(mass, mass_ref.shape)
        return
    count = rows.shape[0] // chunk
    number = lax.broadcasted_iota(jnp.int32, (rows.shape[0], 1), 0)
    lanes = lax.broadcasted_iota(jnp.int32, (1, rows.shape[1]), 1)
    inside = lax.rem(number, chunk)
    spread = jnp.zeros(rows.shape, F32)
    for piece in range(3):
        high = mass.astype(BF).astype(F32)
        spread = jnp.where(lanes == piece * half + lead + inside, high, spread)
        mass = mass - high
    own = jnp.where(number // chunk == lax.broadcasted_iota(jnp.int32, (1, TILE), 1), 1.0, 0.0).astype(BF)
    line = dot(own, spread.astype(BF), TN)
    if before is None:
        back_ref[...] = back
        for e in range(count):
            mass_ref[e] = line[e : e + 1].astype(BF)
    else:
        back_ref[:, :chunk] = back.reshape(count, chunk, back.shape[1])
        row = lax.broadcasted_iota(jnp.int32, (16, 1), 0)
        for e in range(count):
            both = line[e : e + 1] + before[e].astype(F32)
            back_ref[e, chunk:] = jnp.where(row == 0, both, 0.0).astype(BF)


def row_block(total):
    return 320 if total % 320 == 0 else total


def plain_kernel(grads_ref, b0, b1, b2, b3, out_ref):
    width = b0.shape[0]
    for r, second in enumerate((b0, b1, b2, b3)):
        out_ref[:, r * width : (r + 1) * width] = dot(grads_ref[...], second[...], NT).astype(BF)


def plain_grads(grads, seconds):
    total, width = grads.shape
    hidden = sum(w.shape[0] for w in seconds)
    block = row_block(total)
    here = lambda cols: pl.BlockSpec((block, cols), lambda i: (i, 0))
    return pl.pallas_call(
        plain_kernel,
        grid=(total // block,),
        in_specs=[here(width)] + [pl.BlockSpec(w.shape, lambda i: (0, 0)) for w in seconds],
        out_specs=here(hidden),
        out_shape=jax.ShapeDtypeStruct((total, hidden), BF),
        compiler_params=pltpu.CompilerParams(vmem_limit_bytes=56 * MIB),
        cost_estimate=SMALL_COST,
        name="plain_grads",
    )(grads, *seconds)


def expert_rows_pass(lead, chunk, half, me, partner, rows, grads, plain, router, before, firsts, number):
    total, width = rows.shape
    block = row_block(total)
    steps = total // block
    experts = total // chunk
    hidden = sum(f.shape[1] for f in firsts)
    here = lambda cols: pl.BlockSpec((block, cols), lambda i: (i, 0))
    there = lambda cols: pl.BlockSpec((block, cols), lambda i: (number * steps + i, 0))
    whole = lambda arr: pl.BlockSpec(arr.shape, lambda i: (0, 0))
    lines = pl.BlockSpec((block // chunk, 1, width), lambda i: (i, 0, 0))
    back_shape, back_spec = (total, width), here(width)
    mass_shape, mass_spec, mass_kind = (experts, 1, width), lines, BF
    if lead is None:
        mass_shape, mass_spec, mass_kind = (total, TILE), here(TILE), F32
    elif before is not None:
        back_shape = (experts, chunk + 16, width)
        back_spec = pl.BlockSpec((block // chunk, chunk + 16, width), lambda i: (i, 0, 0))
    return pl.pallas_call(
        functools.partial(expert_kernel, lead, chunk, half),
        grid=(steps,),
        in_specs=[
            pl.BlockSpec(memory_space=pltpu.SMEM),
            pl.BlockSpec((1, 1, block), lambda i: (number * steps + i, 0, 0)),
            here(width), there(width), whole(router),
        ]
        + ([lines] if before is not None else [])
        + [there(hidden)]
        + [whole(w) for w in firsts],
        out_specs=[back_spec, here(hidden), here(hidden), here(width), here(TILE), mass_spec],
        out_shape=[
            jax.ShapeDtypeStruct(back_shape, BF),
            jax.ShapeDtypeStruct((total, hidden), BF),
            jax.ShapeDtypeStruct((total, hidden), BF),
            jax.ShapeDtypeStruct((total, width), BF),
            jax.ShapeDtypeStruct((total, TILE), F32),
            jax.ShapeDtypeStruct(mass_shape, mass_kind),
        ],
        compiler_params=pltpu.CompilerParams(vmem_limit_bytes=56 * MIB),
        cost_estimate=SMALL_COST,
        name="expert_rows",
    )(me, partner, rows, grads, router, *([before] if before is not None else []), plain, *firsts)


def weight_parts(count, refs):
    rows, slopes, active, gated = (refs[n * count : (n + 1) * count] for n in range(4))
    first, second = None, None
    for n in range(count):
        first = put(first, dot(rows[n][...], slopes[n][...], TN))
        second = put(second, dot(active[n][...], gated[n][...], TN))
    return first, second


def cross_kernel(count, *refs):
    first, second = weight_parts(count, refs)
    refs[-1][0, 0] = first.astype(BF)
    refs[-1][0, 1] = second.astype(BF)


def kept_kernel(count, *refs):
    got_ref, far_ref, kept_ref = refs[-3:]
    first, second = weight_parts(count, refs)
    first = first + got_ref[0, 0].astype(F32)
    second = second + got_ref[0, 1].astype(F32)

    @pl.when(pl.program_id(0) == 0)
    def _():
        far_ref[0] = first.astype(BF)
        far_ref[1] = second.astype(BF)

    @pl.when(pl.program_id(0) == 1)
    def _():
        kept_ref[0] = first
        kept_ref[1] = second


def weight_specs(rows, slopes, quarter):
    total, width = rows[0].shape
    hidden = slopes[0].shape[1] // 4
    whole = pl.BlockSpec((total, width), lambda i: (0, 0))
    part = pl.BlockSpec((total, hidden), lambda i: (0, quarter(i)))
    count = len(rows)
    return width, hidden, [whole] * count + [part] * (2 * count) + [whole] * count


def cross_weight_grads(rows, slopes, active, gated):
    width, hidden, specs = weight_specs(rows, slopes, lambda i: 2 + i)
    return pl.pallas_call(
        functools.partial(cross_kernel, len(rows)),
        grid=(2,),
        in_specs=specs,
        out_specs=pl.BlockSpec((1, 2, width, hidden), lambda i: (i, 0, 0, 0)),
        out_shape=jax.ShapeDtypeStruct((2, 2, width, hidden), BF),
        compiler_params=pltpu.CompilerParams(vmem_limit_bytes=56 * MIB),
        cost_estimate=SMALL_COST,
        name="cross_weight_grads",
    )(*rows, *slopes, *active, *gated)


def kept_weight_grads(rows, slopes, active, gated, got):
    width, hidden, specs = weight_specs(rows, slopes, lambda i: 1 - i)
    fixed = pl.BlockSpec((2, width, hidden), lambda i: (0, 0, 0))
    return pl.pallas_call(
        functools.partial(kept_kernel, len(rows)),
        grid=(2,),
        in_specs=specs + [pl.BlockSpec((1, 2, width, hidden), lambda i: (1 - i, 0, 0, 0))],
        out_specs=[fixed, fixed],
        out_shape=[
            jax.ShapeDtypeStruct((2, width, hidden), BF),
            jax.ShapeDtypeStruct((2, width, hidden), F32),
        ],
        compiler_params=pltpu.CompilerParams(vmem_limit_bytes=56 * MIB),
        cost_estimate=SMALL_COST,
        name="kept_weight_grads",
    )(*rows, *slopes, *active, *gated, got)


def result_kernel(chunks, *refs):
    active, gates, seconds, out_ref = refs[:chunks], refs[chunks : 2 * chunks], refs[2 * chunks : -1], refs[-1]
    for c in range(chunks):

        @pl.when(pl.program_id(0) == c)
        def _(c=c):
            width = seconds[0].shape[0]
            total = None
            for r, second in enumerate(seconds):
                total = put(total, dot(active[c][:, r * width : (r + 1) * width], second[...]))
            rows = (total * gates[c][:, :1]).astype(BF)
            if chunks > 1:
                out_ref[:, 0] = rows.reshape(out_ref.shape[0], out_ref.shape[2], out_ref.shape[3])
            else:
                out_ref[...] = rows


def expert_results(active, gates, seconds, experts):
    chunks = len(active)
    total, hidden = active[0].shape
    width = seconds[0].shape[1]
    block = row_block(total)
    steps = total // block

    def here(c, cols):
        return pl.BlockSpec((block, cols), lambda g, i: (jnp.where(g == c, i, jnp.where(g < c, 0, steps - 1)), 0))

    chunk = total // experts
    if chunks > 1:
        shape = (experts, chunks, chunk, width)
        out_spec = pl.BlockSpec((block // chunk, 1, chunk, width), lambda g, i: (i, g, 0, 0))
    else:
        shape = (total, width)
        out_spec = pl.BlockSpec((block, width), lambda g, i: (i, 0))
    out = pl.pallas_call(
        functools.partial(result_kernel, chunks),
        grid=(chunks, steps),
        in_specs=[here(c, hidden) for c in range(chunks)]
        + [here(c, TILE) for c in range(chunks)]
        + [pl.BlockSpec(w.shape, lambda g, i: (0, 0)) for w in seconds],
        out_specs=out_spec,
        out_shape=jax.ShapeDtypeStruct(shape, BF),
        compiler_params=pltpu.CompilerParams(vmem_limit_bytes=56 * MIB),
        cost_estimate=SMALL_COST,
        name="expert_results",
    )(*active, *gates, *seconds)
    return out.reshape(experts, chunks * chunk, width)


def last_sum_kernel(kept_ref, y_ref, out_first, out_second):
    for n, out in enumerate((out_first, out_second)):
        out[...] = kept_ref[n] + y_ref[n].astype(F32)


def last_sums(kept, got_y):
    _, width, hidden = kept.shape
    block = 256
    here = pl.BlockSpec((block, hidden), lambda i: (i, 0))
    part = pl.BlockSpec((2, block, hidden), lambda i: (0, i, 0))
    return pl.pallas_call(
        last_sum_kernel,
        grid=(width // block,),
        in_specs=[part, part],
        out_specs=[here, here],
        out_shape=[jax.ShapeDtypeStruct((width, hidden), F32)] * 2,
        compiler_params=pltpu.CompilerParams(vmem_limit_bytes=40 * MIB),
        cost_estimate=SMALL_COST,
        name="last_sums",
    )(kept, got_y)


def send_kernel(micro_ref, code_ref, rows_ref, out_ref):
    block = out_ref.shape[0]
    ids = lax.broadcasted_iota(jnp.int32, (block, 1), 0) + pl.program_id(0) * block
    hot = jnp.where((ids == code_ref[:1]) | (ids == code_ref[1:2]), 1.0, 0.0).astype(BF)
    out_ref[...] = dot(hot, rows_ref[0]).astype(BF)


def send_rows(micro, code, rows, count):
    width = rows.shape[2]
    block = next(b for b in (336, 320, 384, count) if count % b == 0)
    return pl.pallas_call(
        send_kernel,
        grid_spec=pltpu.PrefetchScalarGridSpec(
            num_scalar_prefetch=1,
            grid=(count // block,),
            in_specs=[
                pl.BlockSpec(code.shape, lambda i, m: (0, 0)),
                pl.BlockSpec((1, SEQ, width), lambda i, m: (m[0], 0, 0)),
            ],
            out_specs=pl.BlockSpec((block, width), lambda i, m: (i, 0)),
        ),
        out_shape=jax.ShapeDtypeStruct((count, width), BF),
        compiler_params=pltpu.CompilerParams(vmem_limit_bytes=40 * MIB),
        cost_estimate=SMALL_COST,
        name="send_rows",
    )(micro, code, rows)


def place_kernel(place_ref, *refs):
    for n, piece in enumerate(refs[:4]):

        @pl.when(pl.program_id(0) == n)
        def _(piece=piece):
            for k, out_ref in enumerate(refs[4:]):
                out_ref[0] = piece[k]


def place_pieces(places, pieces):
    two, rows, width = pieces[0].shape
    whole = pl.BlockSpec(pieces[0].shape, lambda i, place_ref: (0, 0, 0))
    return pl.pallas_call(
        place_kernel,
        grid_spec=pltpu.PrefetchScalarGridSpec(
            num_scalar_prefetch=1,
            grid=(4,),
            in_specs=[whole] * 4,
            out_specs=[pl.BlockSpec((1, rows, width), lambda i, place_ref: (place_ref[i], 0, 0))] * two,
        ),
        out_shape=[jax.ShapeDtypeStruct((4, rows, width), pieces[0].dtype)] * two,
        compiler_params=pltpu.CompilerParams(vmem_limit_bytes=40 * MIB),
        cost_estimate=SMALL_COST,
        name="place_pieces",
    )(places, *pieces)


def swap(value, axis, count, bit):
    return lax.ppermute(value, axis, [(i, i ^ bit) for i in range(count)])


def all_to_all(value):
    return lax.all_to_all(value, "dp", split_axis=0, concat_axis=0, tiled=True)


def together(*values):
    return lax.optimization_barrier(values)


def local(
    layer_input, out_grad, first_gain, query_weight, key_weight, value_weight, output_weight,
    position_bias, second_gain, router_weight, expert_in, expert_out, seq_lengths, routes,
):
    micro_count, tok_rows, width = layer_input.shape
    dp_count = lax.axis_size("dp")
    expert_count = router_weight.shape[1]
    shard = query_weight.shape[1]
    heads_here = position_bias.shape[0]
    assert lax.axis_size("tensor") == 4 and micro_count == 2 and expert_count == dp_count
    assert tok_rows == SEQ and seq_lengths.shape[1] == 1
    capacity = max(8, 8 * (10 * tok_rows // (32 * expert_count)))
    half = capacity // 2
    stride = 8 * (half // 8 + 1)
    by_lines = dp_count == 8
    chunks = 2 if half % 32 == 0 else 1
    chunk = half // chunks
    chunk_rows = expert_count * chunk
    rows_here = query_weight.shape[0]
    me = lax.axis_index("dp")
    rank = lax.axis_index("tensor")
    micro = rank // 2
    core = rank % 2

    def swap_y(value):
        return swap(value, "tensor", 4, 2)

    def swap_core(value):
        return swap(value, "tensor", 4, 1)

    micro_arg = micro.reshape(1).astype(jnp.int32)
    core_arg = core.reshape(1).astype(jnp.int32)

    packed = pack_weights(query_weight, key_weight, value_weight, output_weight, first_gain, second_gain, router_weight)
    three = 3 * TILE

    def doubled(stacked, bit, axis=0):
        other = swap(stacked, "dp", dp_count, bit)
        high = (me & bit) != 0
        pair = jnp.where(high, jnp.stack([other, stacked], axis + 1), jnp.stack([stacked, other], axis + 1))
        return pair.reshape(stacked.shape[:axis] + (-1,) + stacked.shape[axis + 1 :])

    stacked = packed[None]
    bit = dp_count // 2
    while bit > 1:
        stacked = doubled(stacked, bit)
        bit //= 2
    length = lax.dynamic_index_in_dim(seq_lengths, micro, 0, keepdims=False)
    route = lax.dynamic_index_in_dim(routes, micro, 0, keepdims=False).T
    expert_ids = jnp.arange(expert_count, dtype=jnp.int32)
    named = (expert_ids[:, None, None] == route[None]).astype(jnp.int32)
    per_token = jnp.sum(named, axis=1, dtype=jnp.int32)
    earlier = jnp.cumsum(per_token, axis=1, dtype=jnp.int32) - per_token
    slot = jnp.sum(named * earlier[:, None, :], axis=0, dtype=jnp.int32)
    here = slot // half == core
    within = slot % half
    chunk_of = within // chunk
    inside = within % chunk
    spare = 16 * -(-chunk // 16)
    last_stride = spare + 16
    last = (chunks - 1) * chunk_rows
    code_back = jnp.where(
        chunk_of == chunks - 1, last + route * last_stride + inside, chunk_of * chunk_rows + route * chunk + inside
    )
    code_back = code_back + jnp.where(here, 0, last + expert_count * last_stride)
    code_result = route * half + within + jnp.where(here, 0, expert_count * half)
    info = jnp.concatenate([code_back, route, slot, code_result], 0)

    code_grads = jnp.where(here, route * stride + within, -1)
    valid = jnp.arange(SEQ, dtype=jnp.int32) < length[0]
    ids = jnp.arange(expert_count * stride, dtype=jnp.int32)[:, None]
    partner = jnp.sum(
        jnp.where(ids == code_grads[:1], route[1:], 0) + jnp.where(ids == code_grads[1:], route[:1], 0), axis=1, dtype=jnp.int32
    )
    grads_sent = send_rows(micro_arg, jnp.where(valid[None], code_grads, -1), out_grad, expert_count * stride)
    grads_sent = grads_sent.reshape(expert_count, stride, width)
    partner_row = jnp.pad(partner.reshape(expert_count, stride)[:, :half].astype(BF), ((0, 0), (0, width - half)))
    grads_sent = grads_sent.at[:, half].set(partner_row)
    stacked, grads_sent, position_bias = together(stacked, grads_sent, position_bias)
    if by_lines:
        lines = [list(range(x, dp_count, 2)) for x in range(2)]
        grads_z = lax.all_to_all(
            grads_sent.reshape(dp_count // 2, 2, stride, width), "dp", split_axis=0, concat_axis=0,
            axis_index_groups=lines, tiled=True,
        )

    first_own = expert_in[0]
    second_own = expert_out[0]
    part_b = stacked[:, :, :three]
    far_b = swap_y(part_b)
    part_a = doubled(stacked[:, :, three:], 1)
    part_a, far_b = together(part_a, far_b)
    pair_b = jnp.stack([part_b, far_b])
    a_own = part_a[:, :, :three]
    a_far = swap_y(a_own).reshape(width, three)
    a_own = a_own.reshape(width, three)
    pair_b = doubled(pair_b, 1, 1).reshape(2, width, three)
    if by_lines:
        a_far, pair_b, second_own = together(a_far, pair_b, second_own)
    else:
        a_far, pair_b, grads_sent, second_own = together(a_far, pair_b, grads_sent, second_own)
    second_y = swap_y(second_own)
    small_all = part_a[:, :, three:].reshape(width, TILE)
    gain_one = small_all[:, expert_count].astype(F32)[None]
    gain_two = small_all[:, expert_count + 1].astype(F32)[None]
    router_wide = small_all
    far_bias = swap_y(position_bias)
    bias = jnp.concatenate([position_bias[:2], far_bias[:2], position_bias[2:], far_bias[2:]], 0)
    head_total = bias.shape[0]
    hot_const = jnp.asarray(NEAR_HOT, dtype=BF)
    near = dot(bias, hot_const) - bias[:, NB - 1 :].astype(F32)
    near = near.reshape(head_total, 2, TILE, TILE)
    places = jnp.arange(TILE, dtype=jnp.int32)
    causal = jnp.stack([places[None, :] <= places[:, None], jnp.ones((TILE, TILE), bool)])
    near = jnp.where(causal[None], near, NEG)

    if by_lines:
        high = (me & 1) != 0
    else:
        grads_here = all_to_all(grads_sent)

    qkv, normed_one, qkv_weight, output_own = norm_and_project(
        micro_arg, layer_input, gain_one, a_own, a_far, pair_b[0], pair_b[1]
    )
    output_far = swap_core(output_own)
    mixed, logs = attend(length, qkv, near)
    mixed, output_far = together(mixed, output_far)
    mixed_far = swap_core(mixed)
    code_chunks = jnp.where(here, chunk_of * chunk_rows + route * chunk + inside, -1)
    if by_lines:
        sent_x = lax.dynamic_index_in_dim(grads_z, 1 - (me & 1), 1, keepdims=False)
        middle = dp_count // 4
        sent_x = (sent_x[:middle], sent_x[middle:])
        mixed_far, grads_z, sent_x = together(mixed_far, grads_z, sent_x)
        got_first = swap(sent_x[0], "dp", dp_count, 1)
    residual, *parts = residual_and_rows(
        micro_arg, layer_input, mixed, mixed_far, output_own, output_far, gain_two, code_chunks, chunk_rows, chunks
    )

    if by_lines:
        parts, grads_z, second_y, first_own, got_first, sent_last = together(
            parts, grads_z, second_y, first_own, got_first, sent_x[1]
        )
        got_x = jnp.concatenate([got_first, swap(sent_last, "dp", dp_count, 1)], 0)
        kept_x = jnp.where(high, grads_z[:, 1], grads_z[:, 0])
        pair_x = jnp.where(high, jnp.stack([got_x, kept_x], 1), jnp.stack([kept_x, got_x], 1))
        grads_here = pair_x.reshape(dp_count, stride, width)
    else:
        parts, grads_here, second_y, first_own = together(parts, grads_here, second_y, first_own)
    parts = [part.reshape(expert_count, chunk, width) for part in parts]
    arrived = [all_to_all(parts[0])]
    first_y = swap_y(first_own)

    def by_chunk(rows):
        return jnp.swapaxes(rows.reshape((expert_count, chunks, chunk) + rows.shape[2:]), 0, 1)

    grads_all = by_chunk(grads_here[:, :half]).reshape(chunks * chunk_rows, width)
    block = row_block(chunk_rows)
    partner_all = by_chunk(grads_here[:, half, :half].astype(jnp.int32)).reshape(chunks * chunk_rows // block, 1, block)
    seconds = (second_own, second_y, swap_core(second_own), swap_core(second_y))
    arrived[0], grads_all, partner_all, seconds = together(arrived[0], grads_all, partner_all, seconds)
    plain = plain_grads(grads_all, seconds)
    for c in range(1, chunks):
        sent, arrived[-1] = together(parts[c], arrived[-1])
        arrived.append(all_to_all(sent))

    firsts = (first_own, first_y, swap_core(first_own), swap_core(first_y))
    me_arg = me.reshape(1).astype(jnp.int32)
    rows_all, slopes, active, gated, gates, backs = [], [], [], [], [], []
    line = None
    for c in range(chunks):
        rows_c = arrived[c].reshape(chunk_rows, width)
        back, act, slo, gat, gte, line = expert_rows_pass(
            c * chunk if chunks > 1 else None, chunk, half, me_arg, partner_all, rows_c, grads_all, plain, router_wide, line,
            firsts, c,
        )
        rows_all.append(rows_c)
        slopes.append(slo)
        active.append(act)
        gated.append(gat)
        gates.append(gte)
        if chunks == 1:
            gate_grad = line[:, 0].reshape(expert_count, chunk)
            pieces = []
            for _ in range(3):
                piece = gate_grad.astype(BF)
                pieces.append(piece)
                gate_grad = gate_grad - piece.astype(F32)
            gate_row = jnp.pad(jnp.concatenate(pieces, 1), ((0, 0), (0, width - 3 * half)))
            back = jnp.pad(back.reshape(expert_count, chunk, width), ((0, 0), (0, last_stride - chunk), (0, 0)))
            back = back.at[:, spare].set(gate_row)
        if c + 1 < chunks:
            back, arrived[c + 1] = together(back.reshape(expert_count, chunk, width), arrived[c + 1])
        else:
            back, rows_all[-1], backs = together(back, rows_all[-1], backs)
        backs.append(all_to_all(back))
    grads_cross = cross_weight_grads(rows_all, slopes, active, gated)
    gates, grads_cross = together(gates, grads_cross)
    grads_in = swap_core(grads_cross)
    results = expert_results(active, gates, seconds, expert_count)
    results, grads_in = together(results, grads_in)
    grads_far, grads_kept = kept_weight_grads(rows_all, slopes, active, gated, grads_in)
    backs[-1], results, grads_far = together(backs[-1], results, grads_far)

    across_y = swap_y(grads_far)
    results_own = all_to_all(results).reshape(expert_count * half, width)

    backs_far = [swap_core(b) for b in backs]
    residual_grad, mixed_grad, extra_early, output_sent, output_kept = combine(
        micro_arg, core_arg, length, info, out_grad, residual, mixed, gain_two, router_wide, output_own,
        backs + backs_far, half, spare,
    )

    tiles, sums, far_sent, own_parts, sent, kept_part = attend_back(
        core_arg, length, qkv, near, mixed, logs, mixed_grad, normed_one, output_sent, qkv_weight
    )
    far_got = swap_y(far_sent)
    sent, results_own = together(sent, results_own)
    got = swap_core(sent)
    rows_both, extra_late = both_rows(
        expert_count, micro_arg, core_arg, length, kept_part, got, layer_input, gain_one, residual_grad,
        info, residual, results_own, swap_core(results_own),
    )
    rows_both, across_y, tiles = together(rows_both, across_y, tiles)
    late_far = swap_core(extra_late)
    corner = micro * 2 + core
    corners = jnp.stack([corner, corner ^ 1, corner ^ 2, corner ^ 3]).astype(jnp.int32)
    rows_y = swap_y(rows_both)
    expert_in_grad, expert_out_grad = last_sums(grads_kept, across_y)
    rows_y, expert_in_grad, expert_out_grad = together(rows_y, expert_in_grad, expert_out_grad)
    pieces = (rows_both, swap_core(rows_both), rows_y, swap_core(rows_y))

    tiles = tiles.reshape(head_total, 2 * TILE * TILE)
    tiles_high = tiles.astype(BF)
    tiles_rest = (tiles - tiles_high.astype(F32)).astype(BF)
    table = dot(tiles_high, hot_const, NT) + dot(tiles_rest, hot_const, NT)
    far_sum = jnp.sum(sums[:, :, 0], axis=1) - jnp.sum(table[:, : NB - 1], axis=1)
    table = jnp.concatenate([table[:, : NB - 1], far_sum[:, None]], 1)
    table_own = jnp.concatenate([table[0:2], table[4:5]], 0)
    table_far = jnp.concatenate([table[2:4], table[5:6]], 0)
    table_cols = heads_here * NB // rows_here
    table_both = jnp.concatenate([table_own.reshape(rows_here, table_cols), table_far.reshape(rows_here, table_cols)], 1)
    base = expert_count + 2
    kept = base + 2 * table_cols
    table_tile = jnp.tile(jnp.pad(table_both, ((0, 0), (base, TILE - kept))), (dp_count, 1))

    grads = packed_sums(kept, own_parts, far_got, output_kept, extra_early, extra_late, late_far, table_tile)
    arrived_grads = all_to_all(grads.reshape(dp_count, rows_here, grads.shape[1]))
    layer_output, input_grad = (out.reshape(2, SEQ, width) for out in place_pieces(corners, pieces))
    arrived_grads, layer_output, input_grad = together(arrived_grads, layer_output, input_grad)
    query_grad, key_grad, value_grad, output_grad, small = final_sums(kept, arrived_grads, shard)
    small_y = swap_y(small)
    both = small + small_y
    table_sum = small[:, base : base + table_cols] + small_y[:, base + table_cols : kept]
    return (
        layer_output,
        input_grad,
        both[:, expert_count],
        query_grad,
        key_grad,
        value_grad,
        output_grad.T,
        table_sum.reshape(heads_here, NB),
        both[:, expert_count + 1],
        both[:, :expert_count],
        expert_in_grad[None],
        expert_out_grad[None],
    )


def solution(mesh):
    return jax.shard_map(
        local,
        mesh=mesh,
        in_specs=(
            P(None, "dp", None),
            P(None, "dp", None),
            P("dp"),
            P("dp", "tensor"),
            P("dp", "tensor"),
            P("dp", "tensor"),
            P("tensor", "dp"),
            P("tensor", None),
            P("dp"),
            P("dp", None),
            P("dp", None, "tensor"),
            P("dp", "tensor", None),
            P(None, "dp"),
            P(None, "dp", None),
        ),
        out_specs=(
            P(None, "dp", None),
            P(None, "dp", None),
            P("dp"),
            P("dp", "tensor"),
            P("dp", "tensor"),
            P("dp", "tensor"),
            P("tensor", "dp"),
            P("tensor", None),
            P("dp"),
            P("dp", None),
            P("dp", None, "tensor"),
            P("dp", "tensor", None),
        ),
        check_vma=False,
    )
```

```python
import functools

import jax
import jax.numpy as jnp
import numpy as np
from jax import lax
from jax.experimental import pallas as pl
from jax.experimental.pallas import tpu as pltpu
from jax.sharding import PartitionSpec as P

HEAD_DIM = 64
NB = 32
SEQ = 1024
TILE = 128
QROWS = 256
NEG = -1e30
GELU_C = 0.7978845608028654
GELU_A = 0.044715

BF = jnp.bfloat16
F32 = jnp.float32

bucket_edges = np.ceil(16.0 * 8.0 ** (np.arange(1, 16) / 16.0)).astype(np.int32)


def near_tables():
    rows = np.arange(TILE)[:, None]
    cols = np.arange(TILE)[None, :]
    hots = []
    for shift in (0, TILE):
        distance = rows - cols + shift
        clipped = np.maximum(distance, 0)
        reached = np.sum(clipped[..., None] >= bucket_edges, axis=-1)
        bucket = np.minimum(clipped, 16) + reached
        hots.append(bucket[..., None] == np.arange(NB))
    hot = np.stack(hots).reshape(2 * TILE * TILE, NB).T
    return hot


NEAR_HOT = near_tables()
assert bucket_edges[-1] <= TILE


def dot(a, b, dims=((1,), (0,))):
    return lax.dot_general(a, b, (dims, ((), ())), preferred_element_type=F32)


NT = ((1,), (1,))
TN = ((0,), (0,))


MIB = 2**20
SMALL_COST = pl.CostEstimate(flops=1_000_000, bytes_accessed=1_000_000, transcendentals=0)


STRIP = 32


def score_strip(s, at, block, j, start, near_ref, half, length):
    part = s[at : at + STRIP]
    near = slice(start % TILE, start % TILE + STRIP)
    if j == block:
        if start < TILE:
            left = part[:, :TILE] + near_ref[half, 0, near, :]
            right = jnp.full((STRIP, TILE), NEG, F32)
        else:
            left = part[:, :TILE] + near_ref[half, 1, near, :]
            right = part[:, TILE:] + near_ref[half, 0, near, :]
        part = jnp.concatenate([left, right], 1)
    elif j == block - 1 and start < TILE:
        part = jnp.concatenate([part[:, :TILE], part[:, TILE:] + near_ref[half, 1, near, :]], 1)
    if (j + 1) * QROWS > SEQ // 2:
        place = lax.broadcasted_iota(jnp.int32, (1, QROWS), 1) + j * QROWS
        part = part + jnp.where(place < length, 0.0, NEG)
    return part


def lane_half(rows):
    return lax.broadcasted_iota(jnp.int32, (rows, 2 * HEAD_DIM), 1) < HEAD_DIM


def attend_kernel(length_ref, query_ref, key_ref, value_ref, near_ref, out_ref, log_ref):
    length = length_ref[0]
    lanes = lane_half(QROWS)
    value_ext = jnp.concatenate([value_ref[...], jnp.ones((SEQ, TILE), BF)], 1)
    for i in range(SEQ // QROWS):
        q_rows = query_ref[i * QROWS : (i + 1) * QROWS, :] * BF(0.125)
        q_both = jnp.concatenate([jnp.where(lanes, q_rows, BF(0)), jnp.where(lanes, BF(0), q_rows)], 0)
        tiles = [dot(q_both, key_ref[j * QROWS : (j + 1) * QROWS, :], NT) for j in range(i + 1)]
        tops = []
        weights = [[] for _ in tiles]
        for h in range(2):
            for start in range(0, QROWS, STRIP):
                strips = [
                    score_strip(s, h * QROWS + start, i, j, start, near_ref, h, length) for j, s in enumerate(tiles)
                ]
                top = strips[0]
                for s in strips[1:]:
                    top = jnp.maximum(top, s)
                top = jnp.max(top, axis=1, keepdims=True)
                tops.append(top)
                for j, s in enumerate(strips):
                    weights[j].append(jnp.exp(s - top).astype(BF))
        total = None
        for j, strips in enumerate(weights):
            total = put(total, dot(jnp.concatenate(strips, 0), value_ext[j * QROWS : (j + 1) * QROWS, :]))
        row_sum = total[:, TILE:]
        out = total[:, :TILE] / row_sum
        logs = jnp.concatenate(tops, 0) + jnp.log(row_sum)
        out_ref[i * QROWS : (i + 1) * QROWS, :] = jnp.where(lanes, out[:QROWS], out[QROWS:]).astype(BF)
        log_ref[i * QROWS : (i + 1) * QROWS, :] = jnp.where(lanes, logs[:QROWS], logs[QROWS:])


def attend(length, qkv, near):
    pairs = qkv.shape[1] // (3 * TILE)
    cols = pairs * TILE
    return pl.pallas_call(
        attend_kernel,
        grid=(pairs,),
        in_specs=[
            pl.BlockSpec(memory_space=pltpu.SMEM),
            pl.BlockSpec((SEQ, TILE), lambda p: (0, p)),
            pl.BlockSpec((SEQ, TILE), lambda p: (0, pairs + p)),
            pl.BlockSpec((SEQ, TILE), lambda p: (0, 2 * pairs + p)),
            pl.BlockSpec((2, 2, TILE, TILE), lambda p: (p, 0, 0, 0)),
        ],
        out_specs=[
            pl.BlockSpec((SEQ, TILE), lambda p: (0, p)),
            pl.BlockSpec((SEQ, TILE), lambda p: (0, p)),
        ],
        out_shape=[
            jax.ShapeDtypeStruct((SEQ, cols), BF),
            jax.ShapeDtypeStruct((SEQ, cols), F32),
        ],
        compiler_params=pltpu.CompilerParams(vmem_limit_bytes=40 * MIB),
        cost_estimate=SMALL_COST,
        name="attend",
    )(length, qkv, qkv, qkv, near)


def attend_back_kernel(
    pairs, blocks, core_ref, length_ref, query_ref, key_ref, value_ref, near_ref, out_ref, log_ref, grad_ref,
    normed_ref, output_ref, weight_ref, tile_ref, sum_ref, far_ref, own_ref, sent_ref, kept_ref, grads, dk_acc, dv_acc,
):
    step = pl.program_id(0)

    @pl.when(step < pairs)
    def _():
        pair_grads(
            step, length_ref, query_ref, key_ref, value_ref, near_ref, out_ref, log_ref, grad_ref,
            tile_ref, sum_ref, grads, dk_acc, dv_acc,
        )

    @pl.when((step >= pairs) & (step < pairs + blocks))
    def _():
        low = low_lanes((normed_ref.shape[1], TILE))
        q, k, v = (
            dot(normed_ref[...], jnp.concatenate([grads[n, p] for p in range(pairs)], 1), TN) for n in range(3)
        )
        for n, part in enumerate((q, k, v)):
            own_ref[:, n * TILE : (n + 1) * TILE] = part[:, :TILE]
            far_ref[:, n * TILE : (n + 1) * TILE] = part[:, TILE : 2 * TILE].astype(BF)
        q, k, v = (part[:, 2 * TILE :] for part in (q, k, v))
        far_ref[:, 3 * TILE : 4 * TILE] = jnp.where(low, turned(q), k).astype(BF)
        far_ref[:, 4 * TILE : 5 * TILE] = jnp.where(low, turned(v), output_ref[:, TILE:].astype(F32)).astype(BF)
        far_ref[:, 5 * TILE :] = output_ref[:, :TILE]
        own_ref[:, 3 * TILE : 4 * TILE] = jnp.where(low, q, turned(k))
        own_ref[:, 4 * TILE :] = jnp.where(low, v, 0.0)

    for late, half_ref in enumerate((sent_ref, kept_ref)):
        first = pairs + blocks + 2 * late

        @pl.when((step >= first) & (step < first + 2))
        def _(half_ref=half_ref, first=first, late=late):
            rows = half_ref.shape[0]
            mine = core_ref[0] if late else 1 - core_ref[0]
            start = pl.multiple_of((2 * mine + step - first) * rows, rows)
            total = None
            for n in range(3):
                part = jnp.concatenate([grads[n, p, pl.ds(start, rows), :] for p in range(pairs)], 1)
                cols = part.shape[1]
                total = put(total, dot(part, weight_ref[:, n * cols : (n + 1) * cols], NT))
            half_ref[...] = total


def pair_grads(
    pair, length_ref, query_ref, key_ref, value_ref, near_ref, out_ref, log_ref, grad_ref, tile_ref, sum_ref, grads, dk_acc, dv_acc
):
    length = length_ref[0]
    lanes = lane_half(QROWS)
    key_ext = jnp.concatenate([key_ref[...], jnp.ones((SEQ, TILE), BF)], 1)
    near_sums = [[None, None], [None, None]]
    all_sums = [None, None]

    def both(rows):
        return jnp.concatenate([jnp.where(lanes, rows, BF(0)), jnp.where(lanes, BF(0), rows)], 0)

    for i in range(SEQ // QROWS):
        rows = slice(i * QROWS, (i + 1) * QROWS)
        q_both = both(query_ref[rows, :] * BF(0.125))
        g_rows = grad_ref[rows, :]
        g_both = both(g_rows)
        mass = g_rows.astype(F32) * out_ref[rows, :].astype(F32)
        deltas = [
            jnp.sum(jnp.where(lanes, mass, 0.0), axis=1, keepdims=True),
            jnp.sum(jnp.where(lanes, 0.0, mass), axis=1, keepdims=True),
        ]
        logs = [log_ref[rows, h * HEAD_DIM : h * HEAD_DIM + 1] for h in range(2)]
        dq = None
        for j in range(i + 1):
            keys = slice(j * QROWS, (j + 1) * QROWS)
            s = dot(q_both, key_ref[keys, :], NT)
            dp = dot(g_both, value_ref[keys, :], NT)
            p_strips, d_strips = [], []
            for h in range(2):
                for start in range(0, QROWS, STRIP):
                    strip = slice(start, start + STRIP)
                    at = h * QROWS + start
                    p = jnp.exp(score_strip(s, at, i, j, start, near_ref, h, length) - logs[h][strip])
                    p_strips.append(p.astype(BF))
                    d_strips.append((p * (dp[at : at + STRIP] - deltas[h][strip])).astype(BF))
            p, ds = jnp.concatenate(p_strips, 0), jnp.concatenate(d_strips, 0)
            part = dot(ds, key_ext[keys, :])
            dq = put(dq, jnp.where(lanes, part[:QROWS, :TILE], part[QROWS:, :TILE]))
            for h in range(2):
                sums = part[h * QROWS : (h + 1) * QROWS, TILE:]
                all_sums[h] = put(all_sums[h], jnp.sum(sums.reshape(QROWS // 8, 8, TILE), axis=0))
            dk_part = dot(ds, q_both, TN)
            dv_part = dot(p, g_both, TN)
            if i == j:
                dk_acc[keys, :] = dk_part
                dv_acc[keys, :] = dv_part
            else:
                dk_acc[keys, :] += dk_part
                dv_acc[keys, :] += dv_part
            for h in range(2):
                mine = ds[h * QROWS : (h + 1) * QROWS]
                if j == i:
                    wide = mine.astype(F32)
                    near_sums[h][0] = put(near_sums[h][0], wide[:TILE, :TILE] + wide[TILE:, TILE:])
                    near_sums[h][1] = put(near_sums[h][1], wide[TILE:, :TILE])
                elif j == i - 1:
                    near_sums[h][1] = put(near_sums[h][1], mine[:TILE, TILE:].astype(F32))
        grads[0, pair, rows, :] = (dq * 0.125).astype(BF)
    grads[1, pair] = dk_acc[...].astype(BF)
    grads[2, pair] = dv_acc[...].astype(BF)
    for h in range(2):
        tile_ref[h, 0] = near_sums[h][0]
        tile_ref[h, 1] = near_sums[h][1]
        sum_ref[h] = all_sums[h]


def attend_back(core, length, qkv, near, mixed, logs, grad, normed, output, weight):
    pairs = qkv.shape[1] // (3 * TILE)
    width = normed.shape[1]
    block = 256
    blocks = width // block
    at = lambda i: jnp.minimum(i, pairs - 1)
    then = lambda i: jnp.clip(i - pairs, 0, blocks - 1)
    return pl.pallas_call(
        functools.partial(attend_back_kernel, pairs, blocks),
        grid_spec=pltpu.PrefetchScalarGridSpec(
            num_scalar_prefetch=2,
            grid=(pairs + blocks + 4,),
            in_specs=[
                pl.BlockSpec((SEQ, TILE), lambda i, *_: (0, at(i))),
                pl.BlockSpec((SEQ, TILE), lambda i, *_: (0, pairs + at(i))),
                pl.BlockSpec((SEQ, TILE), lambda i, *_: (0, 2 * pairs + at(i))),
                pl.BlockSpec((2, 2, TILE, TILE), lambda i, *_: (at(i), 0, 0, 0)),
            ]
            + [pl.BlockSpec((SEQ, TILE), lambda i, *_: (0, at(i)))] * 3
            + [
                pl.BlockSpec((SEQ, block), lambda i, *_: (0, then(i))),
                pl.BlockSpec((block, 2 * TILE), lambda i, *_: (then(i), 0)),
                pl.BlockSpec(weight.shape, lambda i, *_: (0, 0)),
            ],
            out_specs=[
                pl.BlockSpec((2, 2, TILE, TILE), lambda i, *_: (at(i), 0, 0, 0)),
                pl.BlockSpec((2, 8, TILE), lambda i, *_: (at(i), 0, 0)),
                pl.BlockSpec((block, 6 * TILE), lambda i, *_: (then(i), 0)),
                pl.BlockSpec((block, 5 * TILE), lambda i, *_: (then(i), 0)),
                pl.BlockSpec((block, width), lambda i, *_: (jnp.clip(i - pairs - blocks, 0, 1), 0)),
                pl.BlockSpec((block, width), lambda i, *_: (jnp.clip(i - pairs - blocks - 2, 0, 1), 0)),
            ],
            scratch_shapes=[
                pltpu.VMEM((3, pairs, SEQ, TILE), BF), pltpu.VMEM((SEQ, TILE), F32), pltpu.VMEM((SEQ, TILE), F32),
            ],
        ),
        out_shape=[
            jax.ShapeDtypeStruct((2 * pairs, 2, TILE, TILE), F32),
            jax.ShapeDtypeStruct((2 * pairs, 8, TILE), F32),
            jax.ShapeDtypeStruct((width, 6 * TILE), BF),
            jax.ShapeDtypeStruct((width, 5 * TILE), F32),
            jax.ShapeDtypeStruct((2 * block, width), F32),
            jax.ShapeDtypeStruct((2 * block, width), F32),
        ],
        compiler_params=pltpu.CompilerParams(vmem_limit_bytes=60 * MIB),
        cost_estimate=SMALL_COST,
        name="attend_back",
    )(core, length, qkv, qkv, qkv, near, mixed, logs, grad, normed, output, weight)


def low_lanes(shape):
    return lax.broadcasted_iota(jnp.int32, shape, 1) < HEAD_DIM


def turned(tile):
    return pltpu.roll(tile, HEAD_DIM, 1)


def pack_kernel(q_ref, k_ref, v_ref, o_ref, one_ref, two_ref, router_ref, out_ref):
    shard = q_ref.shape[1]
    rows = q_ref.shape[0]
    source = lax.broadcasted_iota(jnp.int32, (shard, 6 * TILE), 0)
    target = lax.broadcasted_iota(jnp.int32, (shard, 6 * TILE), 1)

    def moved(pair_base, last_base):
        want = jnp.where(source < TILE, source + pair_base, source - TILE + last_base)
        return jnp.where(target == want, 1.0, 0.0).astype(BF)

    total = dot(v_ref[...], moved(0, 2 * TILE)) + dot(o_ref[...], moved(TILE, 2 * TILE + HEAD_DIM), TN)
    total = total + dot(q_ref[...], moved(3 * TILE, 5 * TILE)) + dot(k_ref[...], moved(4 * TILE, 5 * TILE + HEAD_DIM))
    out_ref[:, : 6 * TILE] = total.astype(BF)
    experts = router_ref.shape[0]
    own_row = lax.broadcasted_iota(jnp.int32, (rows, rows), 0) == lax.broadcasted_iota(jnp.int32, (rows, rows), 1)

    def column(ref):
        return jnp.sum(jnp.where(own_row, ref[...].astype(F32), 0.0), axis=1, keepdims=True)

    lanes = lax.broadcasted_iota(jnp.int32, (experts, TILE), 1)
    spread = jnp.where(lanes == lax.broadcasted_iota(jnp.int32, (experts, TILE), 0), 1.0, 0.0).astype(BF)
    place = lax.broadcasted_iota(jnp.int32, (rows, TILE), 1)
    small = dot(router_ref[...], spread, TN)
    small = jnp.where(place == experts, column(one_ref), jnp.where(place == experts + 1, column(two_ref), small))
    out_ref[:, 6 * TILE :] = small.astype(BF)


def pack_weights(query, key, value, output, one, two, router):
    rows = query.shape[0]
    return pl.pallas_call(
        pack_kernel,
        out_shape=jax.ShapeDtypeStruct((rows, 7 * TILE), BF),
        compiler_params=pltpu.CompilerParams(vmem_limit_bytes=60 * MIB),
        cost_estimate=SMALL_COST,
        name="pack_weights",
    )(query, key, value, output, one[None], two[None], router.T)


def qkv_kernel(micro_ref, tokens_ref, gain_ref, a_own, a_far, b_own, b_far, qkv_ref, normed_ref, weight_ref, output_ref):
    width = tokens_ref.shape[2]

    @pl.when(pl.program_id(0) == 0)
    def _():
        low = low_lanes((width, TILE))

        def tiles(own, far, pair, low_half):
            at = slice(pair * TILE, (pair + 1) * TILE)
            one, two = own[:, 2 * TILE :].astype(F32), far[:, 2 * TILE :].astype(F32)
            last = jnp.where(low, one, turned(two)) if low_half else jnp.where(low, turned(one), two)
            return own[:, at], far[:, at], last.astype(BF)

        for n, (own, far, pair, low_half) in enumerate(
            ((a_own, a_far, 0, True), (a_own, a_far, 1, False), (b_own, b_far, 0, True))
        ):
            for t, tile in enumerate(tiles(own[...], far[...], pair, low_half)):
                at = 3 * n + t
                weight_ref[:, at * TILE : (at + 1) * TILE] = tile
        for t, tile in enumerate(tiles(b_own[...], b_far[...], 1, False)):
            output_ref[:, t * TILE : (t + 1) * TILE] = tile

    x = tokens_ref[0].astype(F32)
    inverse = lax.rsqrt(jnp.mean(x * x, axis=-1, keepdims=True) + 1e-06)
    normed = (x * inverse * gain_ref[...]).astype(BF)
    normed_ref[...] = normed
    qkv_ref[...] = dot(normed, weight_ref[...]).astype(BF)


def norm_and_project(micro, layer_input, gain, a_own, a_far, b_own, b_far):
    width = layer_input.shape[2]
    block = 256
    cols = 3 * TILE
    whole = lambda rows, n: pl.BlockSpec((rows, n), lambda i, m: (0, 0))
    here = lambda n: pl.BlockSpec((block, n), lambda i, m: (i, 0))
    return pl.pallas_call(
        qkv_kernel,
        grid_spec=pltpu.PrefetchScalarGridSpec(
            num_scalar_prefetch=1,
            grid=(SEQ // block,),
            in_specs=[pl.BlockSpec((1, block, width), lambda i, m: (m[0], i, 0)), whole(1, width)] + [whole(width, cols)] * 4,
            out_specs=[here(3 * cols), here(width), whole(width, 3 * cols), whole(width, cols)],
        ),
        out_shape=[
            jax.ShapeDtypeStruct((SEQ, 3 * cols), BF),
            jax.ShapeDtypeStruct((SEQ, width), BF),
            jax.ShapeDtypeStruct((width, 3 * cols), BF),
            jax.ShapeDtypeStruct((width, cols), BF),
        ],
        compiler_params=pltpu.CompilerParams(vmem_limit_bytes=40 * MIB),
        cost_estimate=SMALL_COST,
        name="norm_and_project",
    )(micro, layer_input, gain, a_own, a_far, b_own, b_far)


def middle_kernel(
    blocks, per, micro_ref, tokens_ref, mixed_ref, other_ref, own_ref, far_ref, gain_ref, code_ref, residual_ref, *refs
):
    sent_refs, normed = refs[:-1], refs[-1]
    step = pl.program_id(0)
    rows = tokens_ref.shape[1]

    @pl.when(step < blocks)
    def _():
        total = tokens_ref[0].astype(F32) + dot(mixed_ref[...], own_ref[...], NT) + dot(other_ref[...], far_ref[...], NT)
        residual_ref[...] = total
        inverse = lax.rsqrt(jnp.mean(total * total, axis=-1, keepdims=True) + 1e-06)
        normed[pl.ds(pl.multiple_of(step * rows, rows), rows), :] = (total * inverse * gain_ref[...]).astype(BF)

    for c, sent_ref in enumerate(sent_refs):

        @pl.when((step >= blocks + c * per) & (step < blocks + (c + 1) * per))
        def _(sent_ref=sent_ref):
            block = sent_ref.shape[0]
            ids = lax.broadcasted_iota(jnp.int32, (block, 1), 0) + (step - blocks) * block
            hot = jnp.where((ids == code_ref[:1]) | (ids == code_ref[1:2]), 1.0, 0.0).astype(BF)
            sent_ref[...] = dot(hot, normed[...]).astype(BF)


def residual_and_rows(micro, layer_input, mixed, other, output_own, output_far, gain, code, count, chunks):
    width = layer_input.shape[2]
    block = 256
    blocks = SEQ // block
    send = 320
    cols = mixed.shape[1]
    per = count // send
    at = lambda i: jnp.minimum(i, blocks - 1)
    whole = lambda arr: pl.BlockSpec(arr.shape, lambda i, m: (0, 0))
    here = lambda n: pl.BlockSpec((block, n), lambda i, m: (at(i), 0))

    def sent(c):
        return pl.BlockSpec((send, width), lambda i, m: (jnp.clip(i - blocks - c * per, 0, per - 1), 0))

    return pl.pallas_call(
        functools.partial(middle_kernel, blocks, per),
        grid_spec=pltpu.PrefetchScalarGridSpec(
            num_scalar_prefetch=1,
            grid=(blocks + chunks * per,),
            in_specs=[
                pl.BlockSpec((1, block, width), lambda i, m: (m[0], at(i), 0)),
                here(cols), here(cols), whole(output_own), whole(output_far), whole(gain), whole(code),
            ],
            out_specs=[here(width)] + [sent(c) for c in range(chunks)],
            scratch_shapes=[pltpu.VMEM((SEQ, width), BF)],
        ),
        out_shape=[jax.ShapeDtypeStruct((SEQ, width), F32)] + [jax.ShapeDtypeStruct((count, width), BF)] * chunks,
        compiler_params=pltpu.CompilerParams(vmem_limit_bytes=40 * MIB),
        cost_estimate=SMALL_COST,
        name="residual_and_rows",
    )(micro, layer_input, mixed, other, output_own, output_far, gain, code)


def picked_rows(first, second, segments):
    total = None
    start = 0
    for rows in segments:
        length = rows.shape[0]
        ids = lax.broadcasted_iota(jnp.int32, (1, length), 1) + start
        hot = []
        for at in range(0, first.shape[0], STRIP):
            one, two = first[at : at + STRIP], second[at : at + STRIP]
            hot.append(jnp.where((one == ids) | (two == ids), 1.0, 0.0).astype(BF))
        total = put(total, dot(jnp.concatenate(hot, 0), rows))
        start += length
    return total


def put(a, b):
    return b if a is None else a + b


def folded(product):
    return jnp.sum(product.reshape(product.shape[0] // 8, 8, product.shape[1]), axis=0)


def as_column(eight):
    ones = jnp.ones((16, TILE), BF)
    high = eight.astype(BF)
    rest = (eight - high.astype(F32)).astype(BF)
    return dot(jnp.concatenate([high, rest], 0), ones, TN)


def combine_kernel(experts, half, spare, micro_ref, core_ref, length_ref, *refs):
    info_ref, grad_ref, residual_ref, mixed_ref, gain_ref, router_ref, output_ref = refs[:7]
    backs = refs[7:-9]
    (total_ref, mixed_grad_ref, extra_ref, far_ref, own_ref, acc_ref, router_acc, gain_acc, tables) = refs[-9:]
    block = residual_ref.shape[0]
    step = pl.program_id(0)
    count = len(backs) // 2

    @pl.when(step == 0)
    def _():
        place = lax.broadcasted_iota(jnp.int32, (experts, 1), 0)
        for n, back in enumerate((backs[count - 1], backs[2 * count - 1])):
            table = jnp.zeros((experts, back.shape[2]), F32)
            for e in range(experts):
                row = back[e, spare : spare + 16, :].astype(F32)[:1]
                table = jnp.where(place == e, row, table)
            for piece in range(3):
                at = (3 * n + piece) * experts
                tables[at : at + experts] = table[:, piece * half : (piece + 1) * half]

    info = jnp.transpose(info_ref[...])
    number = lambda n: info[:, n : n + 1]
    columns = lax.broadcasted_iota(jnp.int32, (1, half), 1)
    lanes = lax.broadcasted_iota(jnp.int32, (1, 6 * experts), 1)
    table = tables[...].astype(BF)
    values = []
    for k in range(2):
        slot = number(4 + k)
        hot = jnp.where(columns == lax.rem(slot, half), 1.0, 0.0).astype(BF)
        found = dot(hot, table, NT)
        wanted = jnp.where(slot // half == core_ref[0], 0, 3 * experts) + number(2 + k)
        away = lanes - wanted
        hit = (away == 0) | (away == experts) | (away == 2 * experts)
        values.append(jnp.sum(jnp.where(hit, found, 0.0), axis=1, keepdims=True))
    wide = lax.broadcasted_iota(jnp.int32, (1, TILE), 1)
    is_first, is_second = wide == number(2), wide == number(3)
    residual = residual_ref[...]
    gain = gain_ref[...]
    inverse = lax.rsqrt(jnp.mean(residual * residual, axis=-1, keepdims=True) + 1e-06)
    plain = residual * inverse
    normed = (plain * gain).astype(BF)
    logits = dot(normed, router_ref[...])
    gap = jnp.sum(jnp.where(is_first, logits, 0.0) - jnp.where(is_second, logits, 0.0), axis=1, keepdims=True)
    small = jnp.exp(-jnp.abs(gap))
    logit = small / ((1.0 + small) * (1.0 + small)) * (values[0] - values[1])
    logit_grad = jnp.where(is_first, logit, jnp.where(is_second, -logit, 0.0)).astype(BF)
    segments = [b[...].reshape(b.shape[0] * b.shape[1], b.shape[2]) for b in backs]
    normed_grad = picked_rows(number(0), number(1), segments) + dot(logit_grad, router_ref[...], NT)
    scaled = normed_grad * gain
    mean = jnp.mean(scaled * plain, axis=-1, keepdims=True)
    place = lax.broadcasted_iota(jnp.int32, (block, 1), 0) + step * block
    grad_out = jnp.where(place < length_ref[0], grad_ref[0].astype(F32), 0.0)
    total = grad_out + inverse * (scaled - plain * mean)

    @pl.when(step == core_ref[0])
    def _():
        total_ref[...] = total

    branch = total.astype(BF)
    mixed_grad_ref[...] = dot(branch, output_ref[...]).astype(BF)
    router_part = dot(logit_grad, normed, TN)
    gain_part = folded(normed_grad * plain)
    output_part = dot(mixed_ref[...], branch, TN)

    @pl.when(step == 0)
    def _():
        router_acc[...] = router_part
        gain_acc[...] = gain_part
        acc_ref[...] = output_part

    @pl.when(step > 0)
    def _():
        router_acc[...] += router_part
        gain_acc[...] += gain_part
        acc_ref[...] += output_part

    @pl.when(step == pl.num_programs(0) - 1)
    def _():
        extra_ref[...] = jnp.transpose(router_acc[...]) + jnp.where(wide == experts + 1, as_column(gain_acc[...]), 0.0)
        parts = jnp.transpose(acc_ref[...])
        far_ref[...] = parts[:, TILE:].astype(BF)
        own_ref[:, :TILE] = parts[:, :TILE]
        own_ref[:, TILE:] = parts[:, 2 * TILE :]


def combine(micro, core, length, info, out_grad, residual, mixed, gain, router, output_own, backs, half, spare):
    width = residual.shape[1]
    block = 512
    cols = mixed.shape[1]
    whole = lambda arr: pl.BlockSpec(arr.shape, lambda i, *_: (0,) * arr.ndim)
    fixed = lambda rows, n: pl.BlockSpec((rows, n), lambda i, *_: (0, 0))
    here = lambda n: pl.BlockSpec((block, n), lambda i, *_: (i, 0))
    experts = backs[0].shape[0]
    return pl.pallas_call(
        functools.partial(combine_kernel, experts, half, spare),
        grid_spec=pltpu.PrefetchScalarGridSpec(
            num_scalar_prefetch=3,
            grid=(SEQ // block,),
            in_specs=[
                pl.BlockSpec((8, block), lambda i, *_: (0, i)),
                pl.BlockSpec((1, block, width), lambda i, m, *_: (m[0], i, 0)),
                here(width), here(cols), whole(gain), whole(router), whole(output_own),
            ]
            + [whole(x) for x in backs],
            out_specs=[fixed(block, width), here(cols), fixed(width, TILE), fixed(width, 2 * TILE), fixed(width, 2 * TILE)],
            scratch_shapes=[
                pltpu.VMEM((cols, width), F32),
                pltpu.VMEM((TILE, width), F32),
                pltpu.VMEM((8, width), F32),
                pltpu.VMEM((6 * experts, half), F32),
            ],
        ),
        out_shape=[
            jax.ShapeDtypeStruct((block, width), F32),
            jax.ShapeDtypeStruct((SEQ, cols), BF),
            jax.ShapeDtypeStruct((width, TILE), F32),
            jax.ShapeDtypeStruct((width, 2 * TILE), BF),
            jax.ShapeDtypeStruct((width, 2 * TILE), F32),
        ],
        compiler_params=pltpu.CompilerParams(vmem_limit_bytes=60 * MIB),
        cost_estimate=SMALL_COST,
        name="combine",
    )(micro, core, length, info, out_grad, residual, mixed, gain, router, output_own, *backs)


def both_kernel(
    lane, micro_ref, core_ref, length_ref, part_ref, got_ref, tokens_ref, gain_ref, grad_ref,
    info_ref, residual_ref, own_ref, far_ref, out_ref, extra_ref, acc_ref,
):
    block = residual_ref.shape[0]
    info = jnp.transpose(info_ref[...])
    place = lax.broadcasted_iota(jnp.int32, (block, 1), 0) + (core_ref[0] * 2 + pl.program_id(0)) * block
    rows = residual_ref[...] + picked_rows(info[:, 6:7], info[:, 7:8], (own_ref[...], far_ref[...]))
    out_ref[0] = jnp.where(place < length_ref[0], rows, 0.0).astype(BF)
    normed_grad = got_ref[...] + part_ref[...]
    x = tokens_ref[0].astype(F32)
    inverse = lax.rsqrt(jnp.mean(x * x, axis=-1, keepdims=True) + 1e-06)
    plain = x * inverse
    scaled = normed_grad * gain_ref[...]
    mean = jnp.mean(scaled * plain, axis=-1, keepdims=True)
    out_ref[1] = (grad_ref[...] + inverse * (scaled - plain * mean)).astype(BF)
    wide = lax.broadcasted_iota(jnp.int32, (1, TILE), 1)
    part = folded(normed_grad * plain)

    @pl.when(pl.program_id(0) == 0)
    def _():
        acc_ref[...] = part

    @pl.when(pl.program_id(0) == 1)
    def _():
        extra_ref[...] = jnp.where(wide == lane, as_column(acc_ref[...] + part), 0.0)


def both_rows(lane, micro, core, length, part, got, layer_input, gain, residual_grad, info, residual, own, far):
    width = part.shape[1]
    plain = pl.BlockSpec((256, width), lambda i, *_: (i, 0))
    block = 256
    here = lambda n: pl.BlockSpec((block, n), lambda i, m, c, *_: (c[0] * 2 + i, 0))
    whole = lambda arr: pl.BlockSpec(arr.shape, lambda i, *_: (0, 0))
    return pl.pallas_call(
        functools.partial(both_kernel, lane),
        grid_spec=pltpu.PrefetchScalarGridSpec(
            num_scalar_prefetch=3,
            grid=(2,),
            in_specs=[
                plain,
                plain,
                pl.BlockSpec((1, block, width), lambda i, m, c, *_: (m[0], c[0] * 2 + i, 0)),
                whole(gain),
                plain,
                pl.BlockSpec((8, block), lambda i, m, c, *_: (0, c[0] * 2 + i)),
                here(width),
                whole(own),
                whole(far),
            ],
            out_specs=[
                pl.BlockSpec((2, block, width), lambda i, *_: (0, i, 0)),
                pl.BlockSpec((width, TILE), lambda i, *_: (0, 0)),
            ],
            scratch_shapes=[pltpu.VMEM((8, width), F32)],
        ),
        out_shape=[jax.ShapeDtypeStruct((2, 2 * block, width), BF), jax.ShapeDtypeStruct((width, TILE), F32)],
        compiler_params=pltpu.CompilerParams(vmem_limit_bytes=40 * MIB),
        cost_estimate=SMALL_COST,
        name="both_rows",
    )(micro, core, length, part, got, layer_input, gain, residual_grad, info, residual, own, far)


def sum_kernel(kept, own, got, out_own, early, late, late_far, table, sum_ref):
    low = low_lanes(early.shape)
    sum_ref[:, : 4 * TILE] = (own[:, : 4 * TILE] + got[:, : 4 * TILE].astype(F32)).astype(BF)
    mixed = jnp.where(low, own[:, 4 * TILE :], turned(out_own[:, TILE:]))
    sum_ref[:, 4 * TILE : 5 * TILE] = (mixed + got[:, 4 * TILE : 5 * TILE].astype(F32)).astype(BF)
    sum_ref[:, 5 * TILE : 6 * TILE] = (out_own[:, :TILE] + got[:, 5 * TILE :].astype(F32)).astype(BF)
    extra = early[...] + late[...] + late_far[...] + table[...]
    high = extra.astype(BF)
    rest = extra - high.astype(F32)
    if kept <= HEAD_DIM:
        sum_ref[:, 6 * TILE :] = jnp.where(low, high.astype(F32), turned(rest)).astype(BF)
    else:
        sum_ref[:, 6 * TILE : 7 * TILE] = high
        sum_ref[:, 7 * TILE :] = rest.astype(BF)


def packed_sums(kept, *parts):
    width = parts[0].shape[0]
    cols = (7 if kept <= HEAD_DIM else 8) * TILE
    block = 256
    here = lambda n: pl.BlockSpec((block, n), lambda i: (i, 0))
    return pl.pallas_call(
        functools.partial(sum_kernel, kept),
        grid=(width // block,),
        in_specs=[here(x.shape[1]) for x in parts],
        out_specs=here(cols),
        out_shape=jax.ShapeDtypeStruct((width, cols), BF),
        compiler_params=pltpu.CompilerParams(vmem_limit_bytes=40 * MIB),
        cost_estimate=SMALL_COST,
        name="packed_sums",
    )(*parts)


def final_kernel(kept, parts_ref, q_ref, k_ref, v_ref, o_ref, small_ref):
    total = parts_ref[0].astype(F32)
    for n in range(1, parts_ref.shape[0]):
        total = total + parts_ref[n].astype(F32)
    tile = lambda t: total[:, t * TILE : (t + 1) * TILE]
    q_ref[:, :TILE] = tile(0)
    q_ref[:, TILE:] = tile(3)[:, :HEAD_DIM]
    k_ref[:, :TILE] = tile(1)
    k_ref[:, TILE:] = turned(tile(3))[:, :HEAD_DIM]
    v_ref[:, :TILE] = tile(2)
    v_ref[:, TILE:] = tile(4)[:, :HEAD_DIM]
    o_ref[:, :TILE] = tile(5)
    o_ref[:, TILE:] = turned(tile(4))[:, :HEAD_DIM]
    small_ref[...] = tile(6) + (turned(tile(6)) if kept <= HEAD_DIM else tile(7))


def final_sums(kept, parts, shard):
    rows = parts.shape[1]
    return pl.pallas_call(
        functools.partial(final_kernel, kept),
        out_shape=[jax.ShapeDtypeStruct((rows, shard), F32)] * 4 + [jax.ShapeDtypeStruct((rows, TILE), F32)],
        compiler_params=pltpu.CompilerParams(vmem_limit_bytes=40 * MIB),
        cost_estimate=SMALL_COST,
        name="final_sums",
    )(parts)


def pair_gate(logits, own, other):
    lanes = lax.broadcasted_iota(jnp.int32, logits.shape, 1)
    gap = jnp.sum(
        jnp.where(lanes == own, logits, 0.0) - jnp.where(lanes == other, logits, 0.0), axis=1, keepdims=True
    )
    small = jnp.exp(-jnp.abs(gap))
    return jnp.where(gap >= 0.0, 1.0, small) / (1.0 + small)


def expert_kernel(lead, chunk, half, me_ref, partner_ref, rows_ref, grads_ref, router_ref, *refs):
    before, refs = (refs[0], refs[1:]) if lead is not None and lead > 0 else (None, refs)
    plain_ref, firsts = refs[0], refs[1:5]
    back_ref, active_ref, slope_ref, gated_ref, gate_ref, mass_ref = refs[5:]
    rows = rows_ref[...]
    grads = grads_ref[...]
    partner = jnp.transpose(jnp.broadcast_to(partner_ref[0], (8, rows.shape[0])))[:, :1]
    gate = pair_gate(dot(rows, router_ref[...]), me_ref[0], partner)
    gated_ref[...] = (gate * grads.astype(F32)).astype(BF)
    gate_ref[...] = jnp.broadcast_to(gate, gate_ref.shape)
    masses = [None] * (rows.shape[0] // STRIP)
    back = None
    width = firsts[0].shape[1]
    step = 256
    places = [(r, c) for r in range(4) for c in range(0, width, step)]

    def products(r, c):
        return dot(rows, firsts[r][:, c : c + step])

    ahead = products(*places[0])
    for n, (r, c) in enumerate(places):
        x = ahead
        if n + 1 < len(places):
            ahead = products(*places[n + 1])
        place = slice(r * width + c, r * width + c + step)
        for at in range(0, rows.shape[0], STRIP):
            strip = slice(at, at + STRIP)
            value, flow = x[strip], plain_ref[strip, place].astype(F32)
            square = value * value
            bent = jnp.tanh(value * (GELU_C + (GELU_C * GELU_A) * square))
            rise = 0.5 + 0.5 * bent
            active = value * rise
            slope = rise + active * (1.0 - bent) * (GELU_C + (3.0 * GELU_C * GELU_A) * square)
            low = active.astype(BF)
            active_ref[strip, place] = low
            slope_ref[strip, place] = (gate[strip] * flow * slope).astype(BF)
            part = low.astype(F32) * flow
            masses[at // STRIP] = put(masses[at // STRIP], part[:, :TILE] + part[:, TILE:])
        if c + step == width and r > 0:
            back = put(back, dot(slope_ref[:, (r - 1) * width : r * width], firsts[r - 1][...], NT))
    back = put(back, dot(slope_ref[:, 3 * width :], firsts[3][...], NT))
    back = back.astype(BF)
    mass = jnp.sum(jnp.concatenate(masses, 0), axis=1, keepdims=True)
    if lead is None:
        back_ref[...] = back
        mass_ref[...] = jnp.broadcast_to(mass, mass_ref.shape)
        return
    count = rows.shape[0] // chunk
    number = lax.broadcasted_iota(jnp.int32, (rows.shape[0], 1), 0)
    lanes = lax.broadcasted_iota(jnp.int32, (1, rows.shape[1]), 1)
    inside = lax.rem(number, chunk)
    spread = jnp.zeros(rows.shape, F32)
    for piece in range(3):
        high = mass.astype(BF).astype(F32)
        spread = jnp.where(lanes == piece * half + lead + inside, high, spread)
        mass = mass - high
    own = jnp.where(number // chunk == lax.broadcasted_iota(jnp.int32, (1, TILE), 1), 1.0, 0.0).astype(BF)
    line = dot(own, spread.astype(BF), TN)
    if before is None:
        back_ref[...] = back
        for e in range(count):
            mass_ref[e] = line[e : e + 1].astype(BF)
    else:
        back_ref[:, :chunk] = back.reshape(count, chunk, back.shape[1])
        row = lax.broadcasted_iota(jnp.int32, (16, 1), 0)
        for e in range(count):
            both = line[e : e + 1] + before[e].astype(F32)
            back_ref[e, chunk:] = jnp.where(row == 0, both, 0.0).astype(BF)


def row_block(total):
    return 320 if total % 320 == 0 else total


def plain_kernel(grads_ref, *refs):
    seconds, out_ref = refs[:-1], refs[-1]
    rows = seconds[0].shape[0]
    for n, second in enumerate(seconds):
        out_ref[:, n * rows : (n + 1) * rows] = dot(grads_ref[...], second[...], NT).astype(BF)


def piece_specs(seconds, rows):
    width = seconds[0][0].shape[1]
    return [pl.BlockSpec((rows, width), lambda *_, n=n: (n, 0)) for _, n in seconds]


def plain_grads(grads, seconds):
    total, width = grads.shape
    rows = min(w.shape[0] for w, _ in seconds)
    hidden = rows * len(seconds)
    block = row_block(total)
    here = lambda cols: pl.BlockSpec((block, cols), lambda i: (i, 0))
    return pl.pallas_call(
        plain_kernel,
        grid=(total // block,),
        in_specs=[here(width)] + piece_specs(seconds, rows),
        out_specs=here(hidden),
        out_shape=jax.ShapeDtypeStruct((total, hidden), BF),
        compiler_params=pltpu.CompilerParams(vmem_limit_bytes=56 * MIB),
        cost_estimate=SMALL_COST,
        name="plain_grads",
    )(grads, *[w for w, _ in seconds])


def expert_rows_pass(lead, chunk, half, me, partner, rows, grads, plain, router, before, firsts):
    total, width = rows.shape
    block = row_block(total)
    steps = total // block
    experts = total // chunk
    hidden = sum(f.shape[1] for f in firsts)
    here = lambda cols: pl.BlockSpec((block, cols), lambda i: (i, 0))
    whole = lambda arr: pl.BlockSpec(arr.shape, lambda i: (0, 0))
    lines = pl.BlockSpec((block // chunk, 1, width), lambda i: (i, 0, 0))
    back_shape, back_spec = (total, width), here(width)
    mass_shape, mass_spec, mass_kind = (experts, 1, width), lines, BF
    if lead is None:
        mass_shape, mass_spec, mass_kind = (total, TILE), here(TILE), F32
    elif before is not None:
        back_shape = (experts, chunk + 16, width)
        back_spec = pl.BlockSpec((block // chunk, chunk + 16, width), lambda i: (i, 0, 0))
    return pl.pallas_call(
        functools.partial(expert_kernel, lead, chunk, half),
        grid=(steps,),
        in_specs=[
            pl.BlockSpec(memory_space=pltpu.SMEM),
            pl.BlockSpec((1, 1, block), lambda i: (i, 0, 0)),
            here(width), here(width), whole(router),
        ]
        + ([lines] if before is not None else [])
        + [here(hidden)]
        + [whole(w) for w in firsts],
        out_specs=[back_spec, here(hidden), here(hidden), here(width), here(TILE), mass_spec],
        out_shape=[
            jax.ShapeDtypeStruct(back_shape, BF),
            jax.ShapeDtypeStruct((total, hidden), BF),
            jax.ShapeDtypeStruct((total, hidden), BF),
            jax.ShapeDtypeStruct((total, width), BF),
            jax.ShapeDtypeStruct((total, TILE), F32),
            jax.ShapeDtypeStruct(mass_shape, mass_kind),
        ],
        compiler_params=pltpu.CompilerParams(vmem_limit_bytes=56 * MIB),
        cost_estimate=SMALL_COST,
        name="expert_rows",
    )(me, partner, rows, grads, router, *([before] if before is not None else []), plain, *firsts)


def weight_parts(count, refs):
    rows, slopes, active, gated = (refs[n * count : (n + 1) * count] for n in range(4))
    first, second = None, None
    for n in range(count):
        first = put(first, dot(rows[n][...], slopes[n][...], TN))
        second = put(second, dot(active[n][...], gated[n][...], TN))
    return first, second


def cross_kernel(count, *refs):
    first, second = weight_parts(count, refs)
    refs[-1][0, 0] = first.astype(BF)
    refs[-1][0, 1] = second.astype(BF)


def kept_kernel(count, *refs):
    got_ref, far_ref, kept_ref = refs[-3:]
    first, second = weight_parts(count, refs)
    first = first + got_ref[0, 0].astype(F32)
    second = second + got_ref[0, 1].astype(F32)

    @pl.when(pl.program_id(0) == 0)
    def _():
        far_ref[0] = first.astype(BF)
        far_ref[1] = second.astype(BF)

    @pl.when(pl.program_id(0) == 1)
    def _():
        kept_ref[0] = first
        kept_ref[1] = second


def weight_specs(rows, slopes, quarter):
    total, width = rows[0].shape
    hidden = slopes[0].shape[1] // 4
    whole = pl.BlockSpec((total, width), lambda i: (0, 0))
    part = pl.BlockSpec((total, hidden), lambda i: (0, quarter(i)))
    count = len(rows)
    return width, hidden, [whole] * count + [part] * (2 * count) + [whole] * count


def cross_weight_grads(rows, slopes, active, gated):
    width, hidden, specs = weight_specs(rows, slopes, lambda i: 2 + i)
    return pl.pallas_call(
        functools.partial(cross_kernel, len(rows)),
        grid=(2,),
        in_specs=specs,
        out_specs=pl.BlockSpec((1, 2, width, hidden), lambda i: (i, 0, 0, 0)),
        out_shape=jax.ShapeDtypeStruct((2, 2, width, hidden), BF),
        compiler_params=pltpu.CompilerParams(vmem_limit_bytes=56 * MIB),
        cost_estimate=SMALL_COST,
        name="cross_weight_grads",
    )(*rows, *slopes, *active, *gated)


def kept_weight_grads(rows, slopes, active, gated, got):
    width, hidden, specs = weight_specs(rows, slopes, lambda i: 1 - i)
    fixed = pl.BlockSpec((2, width, hidden), lambda i: (0, 0, 0))
    return pl.pallas_call(
        functools.partial(kept_kernel, len(rows)),
        grid=(2,),
        in_specs=specs + [pl.BlockSpec((1, 2, width, hidden), lambda i: (1 - i, 0, 0, 0))],
        out_specs=[fixed, fixed],
        out_shape=[
            jax.ShapeDtypeStruct((2, width, hidden), BF),
            jax.ShapeDtypeStruct((2, width, hidden), F32),
        ],
        compiler_params=pltpu.CompilerParams(vmem_limit_bytes=56 * MIB),
        cost_estimate=SMALL_COST,
        name="kept_weight_grads",
    )(*rows, *slopes, *active, *gated, got)


def result_kernel(chunks, *refs):
    active, gates, seconds, out_ref = refs[:chunks], refs[chunks : 2 * chunks], refs[2 * chunks : -1], refs[-1]
    for c in range(chunks):

        @pl.when(pl.program_id(0) == c)
        def _(c=c):
            width = seconds[0].shape[0]
            total = None
            for r, second in enumerate(seconds):
                total = put(total, dot(active[c][:, r * width : (r + 1) * width], second[...]))
            rows = (total * gates[c][:, :1]).astype(BF)
            if chunks > 1:
                out_ref[:, 0] = rows.reshape(out_ref.shape[0], out_ref.shape[2], out_ref.shape[3])
            else:
                out_ref[...] = rows


def expert_results(active, gates, seconds, experts):
    chunks = len(active)
    total, hidden = active[0].shape
    width = seconds[0][0].shape[1]
    rows = min(w.shape[0] for w, _ in seconds)
    block = row_block(total)
    steps = total // block

    def here(c, cols):
        return pl.BlockSpec((block, cols), lambda g, i: (jnp.where(g == c, i, jnp.where(g < c, 0, steps - 1)), 0))

    chunk = total // experts
    if chunks > 1:
        shape = (experts, chunks, chunk, width)
        out_spec = pl.BlockSpec((block // chunk, 1, chunk, width), lambda g, i: (i, g, 0, 0))
    else:
        shape = (total, width)
        out_spec = pl.BlockSpec((block, width), lambda g, i: (i, 0))
    out = pl.pallas_call(
        functools.partial(result_kernel, chunks),
        grid=(chunks, steps),
        in_specs=[here(c, hidden) for c in range(chunks)]
        + [here(c, TILE) for c in range(chunks)]
        + piece_specs(seconds, rows),
        out_specs=out_spec,
        out_shape=jax.ShapeDtypeStruct(shape, BF),
        compiler_params=pltpu.CompilerParams(vmem_limit_bytes=56 * MIB),
        cost_estimate=SMALL_COST,
        name="expert_results",
    )(*active, *gates, *[w for w, _ in seconds])
    return out.reshape(experts, chunks * chunk, width)


def last_sum_kernel(kept_ref, y_ref, out_first, out_second):
    for n, out in enumerate((out_first, out_second)):
        out[...] = kept_ref[n] + y_ref[n].astype(F32)


def last_sums(kept, got_y):
    _, width, hidden = kept.shape
    block = 256
    here = pl.BlockSpec((block, hidden), lambda i: (i, 0))
    part = pl.BlockSpec((2, block, hidden), lambda i: (0, i, 0))
    return pl.pallas_call(
        last_sum_kernel,
        grid=(width // block,),
        in_specs=[part, part],
        out_specs=[here, here],
        out_shape=[jax.ShapeDtypeStruct((width, hidden), F32)] * 2,
        compiler_params=pltpu.CompilerParams(vmem_limit_bytes=40 * MIB),
        cost_estimate=SMALL_COST,
        name="last_sums",
    )(kept, got_y)


def send_kernel(micro_ref, code_ref, rows_ref, out_ref):
    block = out_ref.shape[0]
    ids = lax.broadcasted_iota(jnp.int32, (block, 1), 0) + pl.program_id(0) * block
    hot = jnp.where((ids == code_ref[:1]) | (ids == code_ref[1:2]), 1.0, 0.0).astype(BF)
    out_ref[...] = dot(hot, rows_ref[0]).astype(BF)


def send_rows(micro, code, rows, count):
    width = rows.shape[2]
    block = next(b for b in (336, 320, 384, count) if count % b == 0)
    return pl.pallas_call(
        send_kernel,
        grid_spec=pltpu.PrefetchScalarGridSpec(
            num_scalar_prefetch=1,
            grid=(count // block,),
            in_specs=[
                pl.BlockSpec(code.shape, lambda i, m: (0, 0)),
                pl.BlockSpec((1, SEQ, width), lambda i, m: (m[0], 0, 0)),
            ],
            out_specs=pl.BlockSpec((block, width), lambda i, m: (i, 0)),
        ),
        out_shape=jax.ShapeDtypeStruct((count, width), BF),
        compiler_params=pltpu.CompilerParams(vmem_limit_bytes=40 * MIB),
        cost_estimate=SMALL_COST,
        name="send_rows",
    )(micro, code, rows)


def place_kernel(place_ref, *refs):
    for n, piece in enumerate(refs[:4]):

        @pl.when(pl.program_id(0) == n)
        def _(piece=piece):
            for k, out_ref in enumerate(refs[4:]):
                out_ref[0] = piece[k]


def place_pieces(places, pieces):
    two, rows, width = pieces[0].shape
    whole = pl.BlockSpec(pieces[0].shape, lambda i, place_ref: (0, 0, 0))
    return pl.pallas_call(
        place_kernel,
        grid_spec=pltpu.PrefetchScalarGridSpec(
            num_scalar_prefetch=1,
            grid=(4,),
            in_specs=[whole] * 4,
            out_specs=[pl.BlockSpec((1, rows, width), lambda i, place_ref: (place_ref[i], 0, 0))] * two,
        ),
        out_shape=[jax.ShapeDtypeStruct((4, rows, width), pieces[0].dtype)] * two,
        compiler_params=pltpu.CompilerParams(vmem_limit_bytes=40 * MIB),
        cost_estimate=SMALL_COST,
        name="place_pieces",
    )(places, *pieces)


def swap(value, axis, count, bit):
    return lax.ppermute(value, axis, [(i, i ^ bit) for i in range(count)])


def all_to_all(value):
    return lax.all_to_all(value, "dp", split_axis=0, concat_axis=0, tiled=True)


def together(*values):
    return lax.optimization_barrier(values)


def local(
    layer_input, out_grad, first_gain, query_weight, key_weight, value_weight, output_weight,
    position_bias, second_gain, router_weight, expert_in, expert_out, seq_lengths, routes,
):
    micro_count, tok_rows, width = layer_input.shape
    dp_count = lax.axis_size("dp")
    expert_count = router_weight.shape[1]
    shard = query_weight.shape[1]
    heads_here = position_bias.shape[0]
    assert lax.axis_size("tensor") == 4 and micro_count == 2 and expert_count == dp_count
    assert tok_rows == SEQ and seq_lengths.shape[1] == 1
    capacity = max(8, 8 * (10 * tok_rows // (32 * expert_count)))
    half = capacity // 2
    stride = 8 * (half // 8 + 1)
    by_lines = dp_count == 8
    chunks = 2 if half % 32 == 0 else 1
    chunk = half // chunks
    chunk_rows = expert_count * chunk
    rows_here = query_weight.shape[0]
    me = lax.axis_index("dp")
    rank = lax.axis_index("tensor")
    micro = rank // 2
    core = rank % 2

    def swap_y(value):
        return swap(value, "tensor", 4, 2)

    def swap_core(value):
        return swap(value, "tensor", 4, 1)

    micro_arg = micro.reshape(1).astype(jnp.int32)
    core_arg = core.reshape(1).astype(jnp.int32)

    packed = pack_weights(query_weight, key_weight, value_weight, output_weight, first_gain, second_gain, router_weight)
    three = 3 * TILE

    def doubled(stacked, bit, axis=0):
        other = swap(stacked, "dp", dp_count, bit)
        high = (me & bit) != 0
        pair = jnp.where(high, jnp.stack([other, stacked], axis + 1), jnp.stack([stacked, other], axis + 1))
        return pair.reshape(stacked.shape[:axis] + (-1,) + stacked.shape[axis + 1 :])

    stacked = packed[None]
    bit = dp_count // 2
    while bit > 1:
        stacked = doubled(stacked, bit)
        bit //= 2
    length = lax.dynamic_index_in_dim(seq_lengths, micro, 0, keepdims=False)
    route = lax.dynamic_index_in_dim(routes, micro, 0, keepdims=False).T
    expert_ids = jnp.arange(expert_count, dtype=jnp.int32)
    named = (expert_ids[:, None, None] == route[None]).astype(jnp.int32)
    per_token = jnp.sum(named, axis=1, dtype=jnp.int32)
    earlier = jnp.cumsum(per_token, axis=1, dtype=jnp.int32) - per_token
    slot = jnp.sum(named * earlier[:, None, :], axis=0, dtype=jnp.int32)
    here = slot // half == core
    within = slot % half
    chunk_of = within // chunk
    inside = within % chunk
    spare = 16 * -(-chunk // 16)
    last_stride = spare + 16
    last = (chunks - 1) * chunk_rows
    code_back = jnp.where(
        chunk_of == chunks - 1, last + route * last_stride + inside, chunk_of * chunk_rows + route * chunk + inside
    )
    code_back = code_back + jnp.where(here, 0, last + expert_count * last_stride)
    code_result = route * half + within + jnp.where(here, 0, expert_count * half)
    info = jnp.concatenate([code_back, route, slot, code_result], 0)

    code_grads = jnp.where(here, route * stride + within + jnp.where(chunk_of > 0, stride - half, 0), -1)
    valid = jnp.arange(SEQ, dtype=jnp.int32) < length[0]
    ids = jnp.arange(expert_count * stride, dtype=jnp.int32)[:, None]
    partner = jnp.sum(
        jnp.where(ids == code_grads[:1], route[1:], 0) + jnp.where(ids == code_grads[1:], route[:1], 0), axis=1, dtype=jnp.int32
    )
    grads_sent = send_rows(micro_arg, jnp.where(valid[None], code_grads, -1), out_grad, expert_count * stride)
    grads_sent = grads_sent.reshape(expert_count, stride, width)
    partner = partner.reshape(expert_count, stride)
    numbers = [partner[:, :chunk]] + [partner[:, chunk + stride - half :]] * (chunks - 1)
    partner_row = jnp.pad(jnp.concatenate(numbers, 1).astype(BF), ((0, 0), (0, width - half)))
    grads_sent = grads_sent.at[:, chunk].set(partner_row)
    stacked, grads_sent, position_bias = together(stacked, grads_sent, position_bias)
    if by_lines:
        lines = [list(range(x, dp_count, 2)) for x in range(2)]
        grads_z = lax.all_to_all(
            grads_sent.reshape(dp_count // 2, 2, stride, width), "dp", split_axis=0, concat_axis=0,
            axis_index_groups=lines, tiled=True,
        )

    first_own = expert_in[0]
    second_own = expert_out[0]
    part_b = stacked[:, :, :three]
    far_b = swap_y(part_b)
    part_a = doubled(stacked[:, :, three:], 1)
    part_a, far_b = together(part_a, far_b)
    pair_b = jnp.stack([part_b, far_b])
    a_own = part_a[:, :, :three]
    a_far = swap_y(a_own).reshape(width, three)
    a_own = a_own.reshape(width, three)
    pair_b = doubled(pair_b, 1, 1).reshape(2, width, three)
    if by_lines:
        a_far, pair_b, second_own = together(a_far, pair_b, second_own)
        second_parts = jnp.split(second_own, 2)
        second_y = [swap_y(second_parts[0])]
    else:
        a_far, pair_b, grads_sent, second_own = together(a_far, pair_b, grads_sent, second_own)
        second_y = [swap_y(second_own)]
    small_all = part_a[:, :, three:].reshape(width, TILE)
    gain_one = small_all[:, expert_count].astype(F32)[None]
    gain_two = small_all[:, expert_count + 1].astype(F32)[None]
    router_wide = small_all
    far_bias = swap_y(position_bias)
    bias = jnp.concatenate([position_bias[:2], far_bias[:2], position_bias[2:], far_bias[2:]], 0)
    head_total = bias.shape[0]
    hot_const = jnp.asarray(NEAR_HOT, dtype=BF)
    near = dot(bias, hot_const) - bias[:, NB - 1 :].astype(F32)
    near = near.reshape(head_total, 2, TILE, TILE)
    places = jnp.arange(TILE, dtype=jnp.int32)
    causal = jnp.stack([places[None, :] <= places[:, None], jnp.ones((TILE, TILE), bool)])
    near = jnp.where(causal[None], near, NEG)

    if by_lines:
        high = (me & 1) != 0
    else:
        grads_here = all_to_all(grads_sent)

    qkv, normed_one, qkv_weight, output_own = norm_and_project(
        micro_arg, layer_input, gain_one, a_own, a_far, pair_b[0], pair_b[1]
    )
    output_far = swap_core(output_own)
    mixed, logs = attend(length, qkv, near)
    mixed, output_far = together(mixed, output_far)
    mixed_far = swap_core(mixed)
    code_chunks = jnp.where(here, chunk_of * chunk_rows + route * chunk + inside, -1)
    if by_lines:
        sent_x = lax.dynamic_index_in_dim(grads_z, 1 - (me & 1), 1, keepdims=False)
        first_rows = chunk + stride - half
        sent_x = (sent_x[:, :first_rows], sent_x[:, first_rows:])
        mixed_far, grads_z, sent_x, second_y, second_parts = together(mixed_far, grads_z, sent_x, second_y, second_parts)
        second_y.append(swap_y(second_parts[1]))
        got_first = swap(sent_x[0], "dp", dp_count, 1)
    residual, *parts = residual_and_rows(
        micro_arg, layer_input, mixed, mixed_far, output_own, output_far, gain_two, code_chunks, chunk_rows, chunks
    )

    if by_lines:
        parts, grads_z, second_y, first_own, got_first, sent_last = together(
            parts, grads_z, second_y, first_own, got_first, sent_x[1]
        )
        got_last = swap(sent_last, "dp", dp_count, 1)
        kept_x = jnp.where(high, grads_z[:, 1], grads_z[:, 0])

        def in_order(kept, got):
            pair = jnp.where(high, jnp.stack([got, kept], 1), jnp.stack([kept, got], 1))
            return pair.reshape((dp_count,) + kept.shape[1:])

        grads_parts = [in_order(kept_x[:, :chunk], got_first[:, :chunk]), in_order(kept_x[:, first_rows:], got_last)]
        partner_all = in_order(kept_x[:, chunk, :half], got_first[:, chunk, :half])
    else:
        parts, grads_here, second_y, first_own = together(parts, grads_here, second_y, first_own)
        grads_parts = [grads_here[:, :chunk]] + [grads_here[:, chunk + stride - half :]] * (chunks - 1)
        partner_all = grads_here[:, chunk, :half]
    parts = [part.reshape(expert_count, chunk, width) for part in parts]
    arrived = [all_to_all(parts[0])]
    first_y = swap_y(first_own)

    block = row_block(chunk_rows)
    partner_all = partner_all.astype(jnp.int32)
    partners = [
        partner_all[:, c * chunk : (c + 1) * chunk].reshape(chunk_rows // block, 1, block) for c in range(chunks)
    ]
    grads_parts = [part.reshape(chunk_rows, width) for part in grads_parts]
    pieces = len(second_y)
    own_pieces = lambda arr: [(arr, n) for n in range(pieces)]
    seconds = own_pieces(second_own) + [(part, 0) for part in second_y]
    seconds = seconds + own_pieces(swap_core(second_own)) + [(swap_core(part), 0) for part in second_y]
    plains = [plain_grads(grads_parts[0], seconds)]
    arrived[0], plains[0], partners = together(arrived[0], plains[0], partners)
    plains = plains + [plain_grads(part, seconds) for part in grads_parts[1:]]
    for c in range(1, chunks):
        sent, arrived[-1] = together(parts[c], arrived[-1])
        arrived.append(all_to_all(sent))

    firsts = (first_own, first_y, swap_core(first_own), swap_core(first_y))
    me_arg = me.reshape(1).astype(jnp.int32)
    rows_all, slopes, active, gated, gates, backs = [], [], [], [], [], []
    line = None
    for c in range(chunks):
        rows_c = arrived[c].reshape(chunk_rows, width)
        back, act, slo, gat, gte, line = expert_rows_pass(
            c * chunk if chunks > 1 else None, chunk, half, me_arg, partners[c], rows_c, grads_parts[c], plains[c],
            router_wide, line, firsts,
        )
        rows_all.append(rows_c)
        slopes.append(slo)
        active.append(act)
        gated.append(gat)
        gates.append(gte)
        if chunks == 1:
            gate_grad = line[:, 0].reshape(expert_count, chunk)
            pieces = []
            for _ in range(3):
                piece = gate_grad.astype(BF)
                pieces.append(piece)
                gate_grad = gate_grad - piece.astype(F32)
            gate_row = jnp.pad(jnp.concatenate(pieces, 1), ((0, 0), (0, width - 3 * half)))
            back = jnp.pad(back.reshape(expert_count, chunk, width), ((0, 0), (0, last_stride - chunk), (0, 0)))
            back = back.at[:, spare].set(gate_row)
        if c + 1 < chunks:
            back, arrived[c + 1] = together(back.reshape(expert_count, chunk, width), arrived[c + 1])
        else:
            back, rows_all[-1], backs = together(back, rows_all[-1], backs)
        backs.append(all_to_all(back))
    grads_cross = cross_weight_grads(rows_all, slopes, active, gated)
    gates, grads_cross = together(gates, grads_cross)
    grads_in = swap_core(grads_cross)
    results = expert_results(active, gates, seconds, expert_count)
    results, grads_in = together(results, grads_in)
    grads_far, grads_kept = kept_weight_grads(rows_all, slopes, active, gated, grads_in)
    backs[-1], results, grads_far = together(backs[-1], results, grads_far)

    across_y = swap_y(grads_far)
    results_own = all_to_all(results).reshape(expert_count * half, width)

    backs_far = [swap_core(b) for b in backs]
    residual_grad, mixed_grad, extra_early, output_sent, output_kept = combine(
        micro_arg, core_arg, length, info, out_grad, residual, mixed, gain_two, router_wide, output_own,
        backs + backs_far, half, spare,
    )

    tiles, sums, far_sent, own_parts, sent, kept_part = attend_back(
        core_arg, length, qkv, near, mixed, logs, mixed_grad, normed_one, output_sent, qkv_weight
    )
    far_got = swap_y(far_sent)
    sent, results_own = together(sent, results_own)
    got = swap_core(sent)
    rows_both, extra_late = both_rows(
        expert_count, micro_arg, core_arg, length, kept_part, got, layer_input, gain_one, residual_grad,
        info, residual, results_own, swap_core(results_own),
    )
    rows_both, across_y, tiles = together(rows_both, across_y, tiles)
    late_far = swap_core(extra_late)
    corner = micro * 2 + core
    corners = jnp.stack([corner, corner ^ 1, corner ^ 2, corner ^ 3]).astype(jnp.int32)
    rows_y = swap_y(rows_both)
    expert_in_grad, expert_out_grad = last_sums(grads_kept, across_y)
    rows_y, expert_in_grad, expert_out_grad = together(rows_y, expert_in_grad, expert_out_grad)
    pieces = (rows_both, swap_core(rows_both), rows_y, swap_core(rows_y))

    tiles = tiles.reshape(head_total, 2 * TILE * TILE)
    tiles_high = tiles.astype(BF)
    tiles_rest = (tiles - tiles_high.astype(F32)).astype(BF)
    table = dot(tiles_high, hot_const, NT) + dot(tiles_rest, hot_const, NT)
    far_sum = jnp.sum(sums[:, :, 0], axis=1) - jnp.sum(table[:, : NB - 1], axis=1)
    table = jnp.concatenate([table[:, : NB - 1], far_sum[:, None]], 1)
    table_own = jnp.concatenate([table[0:2], table[4:5]], 0)
    table_far = jnp.concatenate([table[2:4], table[5:6]], 0)
    table_cols = heads_here * NB // rows_here
    table_both = jnp.concatenate([table_own.reshape(rows_here, table_cols), table_far.reshape(rows_here, table_cols)], 1)
    base = expert_count + 2
    kept = base + 2 * table_cols
    table_tile = jnp.tile(jnp.pad(table_both, ((0, 0), (base, TILE - kept))), (dp_count, 1))

    grads = packed_sums(kept, own_parts, far_got, output_kept, extra_early, extra_late, late_far, table_tile)
    arrived_grads = all_to_all(grads.reshape(dp_count, rows_here, grads.shape[1]))
    layer_output, input_grad = (out.reshape(2, SEQ, width) for out in place_pieces(corners, pieces))
    arrived_grads, layer_output, input_grad = together(arrived_grads, layer_output, input_grad)
    query_grad, key_grad, value_grad, output_grad, small = final_sums(kept, arrived_grads, shard)
    small_y = swap_y(small)
    both = small + small_y
    table_sum = small[:, base : base + table_cols] + small_y[:, base + table_cols : kept]
    return (
        layer_output,
        input_grad,
        both[:, expert_count],
        query_grad,
        key_grad,
        value_grad,
        output_grad.T,
        table_sum.reshape(heads_here, NB),
        both[:, expert_count + 1],
        both[:, :expert_count],
        expert_in_grad[None],
        expert_out_grad[None],
    )


def solution(mesh):
    return jax.shard_map(
        local,
        mesh=mesh,
        in_specs=(
            P(None, "dp", None),
            P(None, "dp", None),
            P("dp"),
            P("dp", "tensor"),
            P("dp", "tensor"),
            P("dp", "tensor"),
            P("tensor", "dp"),
            P("tensor", None),
            P("dp"),
            P("dp", None),
            P("dp", None, "tensor"),
            P("dp", "tensor", None),
            P(None, "dp"),
            P(None, "dp", None),
        ),
        out_specs=(
            P(None, "dp", None),
            P(None, "dp", None),
            P("dp"),
            P("dp", "tensor"),
            P("dp", "tensor"),
            P("dp", "tensor"),
            P("tensor", "dp"),
            P("tensor", None),
            P("dp"),
            P("dp", None),
            P("dp", None, "tensor"),
            P("dp", "tensor", None),
        ),
        check_vma=False,
    )
```

```python
import functools

import jax
import jax.numpy as jnp
import numpy as np
from jax import lax
from jax.experimental import pallas as pl
from jax.experimental.pallas import tpu as pltpu
from jax.sharding import PartitionSpec as P

HEAD_DIM = 64
NB = 32
SEQ = 1024
TILE = 128
QROWS = 256
NEG = -1e30
GELU_C = 0.7978845608028654
GELU_A = 0.044715

BF = jnp.bfloat16
F32 = jnp.float32

bucket_edges = np.ceil(16.0 * 8.0 ** (np.arange(1, 16) / 16.0)).astype(np.int32)


def near_tables():
    rows = np.arange(TILE)[:, None]
    cols = np.arange(TILE)[None, :]
    hots = []
    for shift in (0, TILE):
        distance = rows - cols + shift
        clipped = np.maximum(distance, 0)
        reached = np.sum(clipped[..., None] >= bucket_edges, axis=-1)
        bucket = np.minimum(clipped, 16) + reached
        hots.append(bucket[..., None] == np.arange(NB))
    hot = np.stack(hots).reshape(2 * TILE * TILE, NB).T
    return hot


NEAR_HOT = near_tables()
assert bucket_edges[-1] <= TILE


def dot(a, b, dims=((1,), (0,))):
    return lax.dot_general(a, b, (dims, ((), ())), preferred_element_type=F32)


NT = ((1,), (1,))
TN = ((0,), (0,))


MIB = 2**20
SMALL_COST = pl.CostEstimate(flops=1_000_000, bytes_accessed=1_000_000, transcendentals=0)


STRIP = 32


def score_strip(s, at, block, j, start, near_ref, half, length):
    part = s[at : at + STRIP]
    near = slice(start % TILE, start % TILE + STRIP)
    if j == block:
        if start < TILE:
            left = part[:, :TILE] + near_ref[half, 0, near, :]
            right = jnp.full((STRIP, TILE), NEG, F32)
        else:
            left = part[:, :TILE] + near_ref[half, 1, near, :]
            right = part[:, TILE:] + near_ref[half, 0, near, :]
        part = jnp.concatenate([left, right], 1)
    elif j == block - 1 and start < TILE:
        part = jnp.concatenate([part[:, :TILE], part[:, TILE:] + near_ref[half, 1, near, :]], 1)
    if (j + 1) * QROWS > SEQ // 2:
        place = lax.broadcasted_iota(jnp.int32, (1, QROWS), 1) + j * QROWS
        part = part + jnp.where(place < length, 0.0, NEG)
    return part


def lane_half(rows):
    return lax.broadcasted_iota(jnp.int32, (rows, 2 * HEAD_DIM), 1) < HEAD_DIM


def attend_kernel(length_ref, query_ref, key_ref, value_ref, near_ref, out_ref, log_ref):
    length = length_ref[0]
    lanes = lane_half(QROWS)
    value_ext = jnp.concatenate([value_ref[...], jnp.ones((SEQ, TILE), BF)], 1)
    for i in range(SEQ // QROWS):
        q_rows = query_ref[i * QROWS : (i + 1) * QROWS, :] * BF(0.125)
        q_both = jnp.concatenate([jnp.where(lanes, q_rows, BF(0)), jnp.where(lanes, BF(0), q_rows)], 0)
        tiles = [dot(q_both, key_ref[j * QROWS : (j + 1) * QROWS, :], NT) for j in range(i + 1)]
        tops = []
        weights = [[] for _ in tiles]
        for h in range(2):
            for start in range(0, QROWS, STRIP):
                strips = [
                    score_strip(s, h * QROWS + start, i, j, start, near_ref, h, length) for j, s in enumerate(tiles)
                ]
                top = strips[0]
                for s in strips[1:]:
                    top = jnp.maximum(top, s)
                top = jnp.max(top, axis=1, keepdims=True)
                tops.append(top)
                for j, s in enumerate(strips):
                    weights[j].append(jnp.exp(s - top).astype(BF))
        total = None
        for j, strips in enumerate(weights):
            total = put(total, dot(jnp.concatenate(strips, 0), value_ext[j * QROWS : (j + 1) * QROWS, :]))
        row_sum = total[:, TILE:]
        out = total[:, :TILE] / row_sum
        logs = jnp.concatenate(tops, 0) + jnp.log(row_sum)
        out_ref[i * QROWS : (i + 1) * QROWS, :] = jnp.where(lanes, out[:QROWS], out[QROWS:]).astype(BF)
        log_ref[i * QROWS : (i + 1) * QROWS, :] = jnp.where(lanes, logs[:QROWS], logs[QROWS:])


def attend(length, qkv, near):
    pairs = qkv.shape[1] // (3 * TILE)
    cols = pairs * TILE
    return pl.pallas_call(
        attend_kernel,
        grid=(pairs,),
        in_specs=[
            pl.BlockSpec(memory_space=pltpu.SMEM),
            pl.BlockSpec((SEQ, TILE), lambda p: (0, p)),
            pl.BlockSpec((SEQ, TILE), lambda p: (0, pairs + p)),
            pl.BlockSpec((SEQ, TILE), lambda p: (0, 2 * pairs + p)),
            pl.BlockSpec((2, 2, TILE, TILE), lambda p: (p, 0, 0, 0)),
        ],
        out_specs=[
            pl.BlockSpec((SEQ, TILE), lambda p: (0, p)),
            pl.BlockSpec((SEQ, TILE), lambda p: (0, p)),
        ],
        out_shape=[
            jax.ShapeDtypeStruct((SEQ, cols), BF),
            jax.ShapeDtypeStruct((SEQ, cols), F32),
        ],
        compiler_params=pltpu.CompilerParams(vmem_limit_bytes=40 * MIB),
        cost_estimate=SMALL_COST,
        name="attend",
    )(length, qkv, qkv, qkv, near)


def attend_back_kernel(
    pairs, blocks, core_ref, length_ref, query_ref, key_ref, value_ref, near_ref, out_ref, log_ref, grad_ref,
    normed_ref, output_ref, weight_ref, tile_ref, sum_ref, far_ref, own_ref, sent_ref, kept_ref, grads, dk_acc, dv_acc,
):
    step = pl.program_id(0)

    @pl.when(step < pairs)
    def _():
        pair_grads(
            step, length_ref, query_ref, key_ref, value_ref, near_ref, out_ref, log_ref, grad_ref,
            tile_ref, sum_ref, grads, dk_acc, dv_acc,
        )

    @pl.when((step >= pairs) & (step < pairs + blocks))
    def _():
        low = low_lanes((normed_ref.shape[1], TILE))
        q, k, v = (
            dot(normed_ref[...], jnp.concatenate([grads[n, p] for p in range(pairs)], 1), TN) for n in range(3)
        )
        for n, part in enumerate((q, k, v)):
            own_ref[:, n * TILE : (n + 1) * TILE] = part[:, :TILE]
            far_ref[:, n * TILE : (n + 1) * TILE] = part[:, TILE : 2 * TILE].astype(BF)
        q, k, v = (part[:, 2 * TILE :] for part in (q, k, v))
        far_ref[:, 3 * TILE : 4 * TILE] = jnp.where(low, turned(q), k).astype(BF)
        far_ref[:, 4 * TILE : 5 * TILE] = jnp.where(low, turned(v), output_ref[:, TILE:].astype(F32)).astype(BF)
        far_ref[:, 5 * TILE :] = output_ref[:, :TILE]
        own_ref[:, 3 * TILE : 4 * TILE] = jnp.where(low, q, turned(k))
        own_ref[:, 4 * TILE :] = jnp.where(low, v, 0.0)

    for late, half_ref in enumerate((sent_ref, kept_ref)):
        first = pairs + blocks + 2 * late

        @pl.when((step >= first) & (step < first + 2))
        def _(half_ref=half_ref, first=first, late=late):
            rows = half_ref.shape[0]
            mine = core_ref[0] if late else 1 - core_ref[0]
            start = pl.multiple_of((2 * mine + step - first) * rows, rows)
            total = None
            for n in range(3):
                part = jnp.concatenate([grads[n, p, pl.ds(start, rows), :] for p in range(pairs)], 1)
                cols = part.shape[1]
                total = put(total, dot(part, weight_ref[:, n * cols : (n + 1) * cols], NT))
            half_ref[...] = total


def pair_grads(
    pair, length_ref, query_ref, key_ref, value_ref, near_ref, out_ref, log_ref, grad_ref, tile_ref, sum_ref, grads, dk_acc, dv_acc
):
    length = length_ref[0]
    lanes = lane_half(QROWS)
    key_ext = jnp.concatenate([key_ref[...], jnp.ones((SEQ, TILE), BF)], 1)
    near_sums = [[None, None], [None, None]]
    all_sums = [None, None]

    def both(rows):
        return jnp.concatenate([jnp.where(lanes, rows, BF(0)), jnp.where(lanes, BF(0), rows)], 0)

    for i in range(SEQ // QROWS):
        rows = slice(i * QROWS, (i + 1) * QROWS)
        q_both = both(query_ref[rows, :] * BF(0.125))
        g_rows = grad_ref[rows, :]
        g_both = both(g_rows)
        mass = g_rows.astype(F32) * out_ref[rows, :].astype(F32)
        deltas = [
            jnp.sum(jnp.where(lanes, mass, 0.0), axis=1, keepdims=True),
            jnp.sum(jnp.where(lanes, 0.0, mass), axis=1, keepdims=True),
        ]
        logs = [log_ref[rows, h * HEAD_DIM : h * HEAD_DIM + 1] for h in range(2)]
        dq = None
        for j in range(i + 1):
            keys = slice(j * QROWS, (j + 1) * QROWS)
            s = dot(q_both, key_ref[keys, :], NT)
            dp = dot(g_both, value_ref[keys, :], NT)
            p_strips, d_strips = [], []
            for h in range(2):
                for start in range(0, QROWS, STRIP):
                    strip = slice(start, start + STRIP)
                    at = h * QROWS + start
                    p = jnp.exp(score_strip(s, at, i, j, start, near_ref, h, length) - logs[h][strip])
                    p_strips.append(p.astype(BF))
                    d_strips.append((p * (dp[at : at + STRIP] - deltas[h][strip])).astype(BF))
            p, ds = jnp.concatenate(p_strips, 0), jnp.concatenate(d_strips, 0)
            part = dot(ds, key_ext[keys, :])
            dq = put(dq, jnp.where(lanes, part[:QROWS, :TILE], part[QROWS:, :TILE]))
            for h in range(2):
                sums = part[h * QROWS : (h + 1) * QROWS, TILE:]
                all_sums[h] = put(all_sums[h], jnp.sum(sums.reshape(QROWS // 8, 8, TILE), axis=0))
            dk_part = dot(ds, q_both, TN)
            dv_part = dot(p, g_both, TN)
            if i == j:
                dk_acc[keys, :] = dk_part
                dv_acc[keys, :] = dv_part
            else:
                dk_acc[keys, :] += dk_part
                dv_acc[keys, :] += dv_part
            for h in range(2):
                mine = ds[h * QROWS : (h + 1) * QROWS]
                if j == i:
                    wide = mine.astype(F32)
                    near_sums[h][0] = put(near_sums[h][0], wide[:TILE, :TILE] + wide[TILE:, TILE:])
                    near_sums[h][1] = put(near_sums[h][1], wide[TILE:, :TILE])
                elif j == i - 1:
                    near_sums[h][1] = put(near_sums[h][1], mine[:TILE, TILE:].astype(F32))
        grads[0, pair, rows, :] = (dq * 0.125).astype(BF)
    grads[1, pair] = dk_acc[...].astype(BF)
    grads[2, pair] = dv_acc[...].astype(BF)
    for h in range(2):
        tile_ref[h, 0] = near_sums[h][0]
        tile_ref[h, 1] = near_sums[h][1]
        sum_ref[h] = all_sums[h]


def attend_back(core, length, qkv, near, mixed, logs, grad, normed, output, weight):
    pairs = qkv.shape[1] // (3 * TILE)
    width = normed.shape[1]
    block = 256
    blocks = width // block
    at = lambda i: jnp.minimum(i, pairs - 1)
    then = lambda i: jnp.clip(i - pairs, 0, blocks - 1)
    return pl.pallas_call(
        functools.partial(attend_back_kernel, pairs, blocks),
        grid_spec=pltpu.PrefetchScalarGridSpec(
            num_scalar_prefetch=2,
            grid=(pairs + blocks + 4,),
            in_specs=[
                pl.BlockSpec((SEQ, TILE), lambda i, *_: (0, at(i))),
                pl.BlockSpec((SEQ, TILE), lambda i, *_: (0, pairs + at(i))),
                pl.BlockSpec((SEQ, TILE), lambda i, *_: (0, 2 * pairs + at(i))),
                pl.BlockSpec((2, 2, TILE, TILE), lambda i, *_: (at(i), 0, 0, 0)),
            ]
            + [pl.BlockSpec((SEQ, TILE), lambda i, *_: (0, at(i)))] * 3
            + [
                pl.BlockSpec((SEQ, block), lambda i, *_: (0, then(i))),
                pl.BlockSpec((block, 2 * TILE), lambda i, *_: (then(i), 0)),
                pl.BlockSpec(weight.shape, lambda i, *_: (0, 0)),
            ],
            out_specs=[
                pl.BlockSpec((2, 2, TILE, TILE), lambda i, *_: (at(i), 0, 0, 0)),
                pl.BlockSpec((2, 8, TILE), lambda i, *_: (at(i), 0, 0)),
                pl.BlockSpec((block, 6 * TILE), lambda i, *_: (then(i), 0)),
                pl.BlockSpec((block, 5 * TILE), lambda i, *_: (then(i), 0)),
                pl.BlockSpec((block, width), lambda i, *_: (jnp.clip(i - pairs - blocks, 0, 1), 0)),
                pl.BlockSpec((block, width), lambda i, *_: (jnp.clip(i - pairs - blocks - 2, 0, 1), 0)),
            ],
            scratch_shapes=[
                pltpu.VMEM((3, pairs, SEQ, TILE), BF), pltpu.VMEM((SEQ, TILE), F32), pltpu.VMEM((SEQ, TILE), F32),
            ],
        ),
        out_shape=[
            jax.ShapeDtypeStruct((2 * pairs, 2, TILE, TILE), F32),
            jax.ShapeDtypeStruct((2 * pairs, 8, TILE), F32),
            jax.ShapeDtypeStruct((width, 6 * TILE), BF),
            jax.ShapeDtypeStruct((width, 5 * TILE), F32),
            jax.ShapeDtypeStruct((2 * block, width), F32),
            jax.ShapeDtypeStruct((2 * block, width), F32),
        ],
        compiler_params=pltpu.CompilerParams(vmem_limit_bytes=60 * MIB),
        cost_estimate=SMALL_COST,
        name="attend_back",
    )(core, length, qkv, qkv, qkv, near, mixed, logs, grad, normed, output, weight)


def low_lanes(shape):
    return lax.broadcasted_iota(jnp.int32, shape, 1) < HEAD_DIM


def turned(tile):
    return pltpu.roll(tile, HEAD_DIM, 1)


def pack_kernel(q_ref, k_ref, v_ref, o_ref, one_ref, two_ref, router_ref, out_ref):
    shard = q_ref.shape[1]
    rows = q_ref.shape[0]
    source = lax.broadcasted_iota(jnp.int32, (shard, 6 * TILE), 0)
    target = lax.broadcasted_iota(jnp.int32, (shard, 6 * TILE), 1)

    def moved(pair_base, last_base):
        want = jnp.where(source < TILE, source + pair_base, source - TILE + last_base)
        return jnp.where(target == want, 1.0, 0.0).astype(BF)

    total = dot(v_ref[...], moved(0, 2 * TILE)) + dot(o_ref[...], moved(TILE, 2 * TILE + HEAD_DIM), TN)
    total = total + dot(q_ref[...], moved(3 * TILE, 5 * TILE)) + dot(k_ref[...], moved(4 * TILE, 5 * TILE + HEAD_DIM))
    out_ref[:, : 6 * TILE] = total.astype(BF)
    experts = router_ref.shape[0]
    own_row = lax.broadcasted_iota(jnp.int32, (rows, rows), 0) == lax.broadcasted_iota(jnp.int32, (rows, rows), 1)

    def column(ref):
        return jnp.sum(jnp.where(own_row, ref[...].astype(F32), 0.0), axis=1, keepdims=True)

    lanes = lax.broadcasted_iota(jnp.int32, (experts, TILE), 1)
    spread = jnp.where(lanes == lax.broadcasted_iota(jnp.int32, (experts, TILE), 0), 1.0, 0.0).astype(BF)
    place = lax.broadcasted_iota(jnp.int32, (rows, TILE), 1)
    small = dot(router_ref[...], spread, TN)
    small = jnp.where(place == experts, column(one_ref), jnp.where(place == experts + 1, column(two_ref), small))
    out_ref[:, 6 * TILE :] = small.astype(BF)


def pack_weights(query, key, value, output, one, two, router):
    rows = query.shape[0]
    return pl.pallas_call(
        pack_kernel,
        out_shape=jax.ShapeDtypeStruct((rows, 7 * TILE), BF),
        compiler_params=pltpu.CompilerParams(vmem_limit_bytes=60 * MIB),
        cost_estimate=SMALL_COST,
        name="pack_weights",
    )(query, key, value, output, one[None], two[None], router.T)


def qkv_kernel(micro_ref, tokens_ref, gain_ref, a_own, a_far, b_own, b_far, qkv_ref, normed_ref, weight_ref, output_ref):
    width = tokens_ref.shape[2]

    @pl.when(pl.program_id(0) == 0)
    def _():
        low = low_lanes((width, TILE))

        def tiles(own, far, pair, low_half):
            at = slice(pair * TILE, (pair + 1) * TILE)
            one, two = own[:, 2 * TILE :].astype(F32), far[:, 2 * TILE :].astype(F32)
            last = jnp.where(low, one, turned(two)) if low_half else jnp.where(low, turned(one), two)
            return own[:, at], far[:, at], last.astype(BF)

        for n, (own, far, pair, low_half) in enumerate(
            ((a_own, a_far, 0, True), (a_own, a_far, 1, False), (b_own, b_far, 0, True))
        ):
            for t, tile in enumerate(tiles(own[...], far[...], pair, low_half)):
                at = 3 * n + t
                weight_ref[:, at * TILE : (at + 1) * TILE] = tile
        for t, tile in enumerate(tiles(b_own[...], b_far[...], 1, False)):
            output_ref[:, t * TILE : (t + 1) * TILE] = tile

    x = tokens_ref[0].astype(F32)
    inverse = lax.rsqrt(jnp.mean(x * x, axis=-1, keepdims=True) + 1e-06)
    normed = (x * inverse * gain_ref[...]).astype(BF)
    normed_ref[...] = normed
    qkv_ref[...] = dot(normed, weight_ref[...]).astype(BF)


def norm_and_project(micro, layer_input, gain, a_own, a_far, b_own, b_far):
    width = layer_input.shape[2]
    block = 256
    cols = 3 * TILE
    whole = lambda rows, n: pl.BlockSpec((rows, n), lambda i, m: (0, 0))
    here = lambda n: pl.BlockSpec((block, n), lambda i, m: (i, 0))
    return pl.pallas_call(
        qkv_kernel,
        grid_spec=pltpu.PrefetchScalarGridSpec(
            num_scalar_prefetch=1,
            grid=(SEQ // block,),
            in_specs=[pl.BlockSpec((1, block, width), lambda i, m: (m[0], i, 0)), whole(1, width)] + [whole(width, cols)] * 4,
            out_specs=[here(3 * cols), here(width), whole(width, 3 * cols), whole(width, cols)],
        ),
        out_shape=[
            jax.ShapeDtypeStruct((SEQ, 3 * cols), BF),
            jax.ShapeDtypeStruct((SEQ, width), BF),
            jax.ShapeDtypeStruct((width, 3 * cols), BF),
            jax.ShapeDtypeStruct((width, cols), BF),
        ],
        compiler_params=pltpu.CompilerParams(vmem_limit_bytes=40 * MIB),
        cost_estimate=SMALL_COST,
        name="norm_and_project",
    )(micro, layer_input, gain, a_own, a_far, b_own, b_far)


def middle_kernel(
    blocks, per, micro_ref, tokens_ref, mixed_ref, other_ref, own_ref, far_ref, gain_ref, code_ref, residual_ref, *refs
):
    sent_refs, normed = refs[:-1], refs[-1]
    step = pl.program_id(0)
    rows = tokens_ref.shape[1]

    @pl.when(step < blocks)
    def _():
        total = tokens_ref[0].astype(F32) + dot(mixed_ref[...], own_ref[...], NT) + dot(other_ref[...], far_ref[...], NT)
        residual_ref[...] = total
        inverse = lax.rsqrt(jnp.mean(total * total, axis=-1, keepdims=True) + 1e-06)
        normed[pl.ds(pl.multiple_of(step * rows, rows), rows), :] = (total * inverse * gain_ref[...]).astype(BF)

    for c, sent_ref in enumerate(sent_refs):

        @pl.when((step >= blocks + c * per) & (step < blocks + (c + 1) * per))
        def _(sent_ref=sent_ref):
            block = sent_ref.shape[0]
            ids = lax.broadcasted_iota(jnp.int32, (block, 1), 0) + (step - blocks) * block
            hot = jnp.where((ids == code_ref[:1]) | (ids == code_ref[1:2]), 1.0, 0.0).astype(BF)
            sent_ref[...] = dot(hot, normed[...]).astype(BF)


def residual_and_rows(micro, layer_input, mixed, other, output_own, output_far, gain, code, count, chunks):
    width = layer_input.shape[2]
    block = 256
    blocks = SEQ // block
    send = 320
    cols = mixed.shape[1]
    per = count // send
    at = lambda i: jnp.minimum(i, blocks - 1)
    whole = lambda arr: pl.BlockSpec(arr.shape, lambda i, m: (0, 0))
    here = lambda n: pl.BlockSpec((block, n), lambda i, m: (at(i), 0))

    def sent(c):
        return pl.BlockSpec((send, width), lambda i, m: (jnp.clip(i - blocks - c * per, 0, per - 1), 0))

    return pl.pallas_call(
        functools.partial(middle_kernel, blocks, per),
        grid_spec=pltpu.PrefetchScalarGridSpec(
            num_scalar_prefetch=1,
            grid=(blocks + chunks * per,),
            in_specs=[
                pl.BlockSpec((1, block, width), lambda i, m: (m[0], at(i), 0)),
                here(cols), here(cols), whole(output_own), whole(output_far), whole(gain), whole(code),
            ],
            out_specs=[here(width)] + [sent(c) for c in range(chunks)],
            scratch_shapes=[pltpu.VMEM((SEQ, width), BF)],
        ),
        out_shape=[jax.ShapeDtypeStruct((SEQ, width), F32)] + [jax.ShapeDtypeStruct((count, width), BF)] * chunks,
        compiler_params=pltpu.CompilerParams(vmem_limit_bytes=40 * MIB),
        cost_estimate=SMALL_COST,
        name="residual_and_rows",
    )(micro, layer_input, mixed, other, output_own, output_far, gain, code)


def picked_rows(first, second, segments):
    total = None
    start = 0
    for rows in segments:
        length = rows.shape[0]
        ids = lax.broadcasted_iota(jnp.int32, (1, length), 1) + start
        hot = []
        for at in range(0, first.shape[0], STRIP):
            one, two = first[at : at + STRIP], second[at : at + STRIP]
            hot.append(jnp.where((one == ids) | (two == ids), 1.0, 0.0).astype(BF))
        total = put(total, dot(jnp.concatenate(hot, 0), rows))
        start += length
    return total


def put(a, b):
    return b if a is None else a + b


def folded(product):
    return jnp.sum(product.reshape(product.shape[0] // 8, 8, product.shape[1]), axis=0)


def as_column(eight):
    ones = jnp.ones((16, TILE), BF)
    high = eight.astype(BF)
    rest = (eight - high.astype(F32)).astype(BF)
    return dot(jnp.concatenate([high, rest], 0), ones, TN)


def combine_kernel(experts, half, spare, micro_ref, core_ref, length_ref, *refs):
    info_ref, grad_ref, residual_ref, mixed_ref, gain_ref, router_ref, output_ref = refs[:7]
    backs = refs[7:-9]
    (total_ref, mixed_grad_ref, extra_ref, far_ref, own_ref, acc_ref, router_acc, gain_acc, tables) = refs[-9:]
    block = residual_ref.shape[0]
    step = pl.program_id(0)
    count = len(backs) // 2

    @pl.when(step == 0)
    def _():
        place = lax.broadcasted_iota(jnp.int32, (experts, 1), 0)
        for n, back in enumerate((backs[count - 1], backs[2 * count - 1])):
            table = jnp.zeros((experts, back.shape[2]), F32)
            for e in range(experts):
                row = back[e, spare : spare + 16, :].astype(F32)[:1]
                table = jnp.where(place == e, row, table)
            for piece in range(3):
                at = (3 * n + piece) * experts
                tables[at : at + experts] = table[:, piece * half : (piece + 1) * half]

    info = jnp.transpose(info_ref[...])
    number = lambda n: info[:, n : n + 1]
    columns = lax.broadcasted_iota(jnp.int32, (1, half), 1)
    lanes = lax.broadcasted_iota(jnp.int32, (1, 6 * experts), 1)
    table = tables[...].astype(BF)
    values = []
    for k in range(2):
        slot = number(4 + k)
        hot = jnp.where(columns == lax.rem(slot, half), 1.0, 0.0).astype(BF)
        found = dot(hot, table, NT)
        wanted = jnp.where(slot // half == core_ref[0], 0, 3 * experts) + number(2 + k)
        away = lanes - wanted
        hit = (away == 0) | (away == experts) | (away == 2 * experts)
        values.append(jnp.sum(jnp.where(hit, found, 0.0), axis=1, keepdims=True))
    wide = lax.broadcasted_iota(jnp.int32, (1, TILE), 1)
    is_first, is_second = wide == number(2), wide == number(3)
    residual = residual_ref[...]
    gain = gain_ref[...]
    inverse = lax.rsqrt(jnp.mean(residual * residual, axis=-1, keepdims=True) + 1e-06)
    plain = residual * inverse
    normed = (plain * gain).astype(BF)
    logits = dot(normed, router_ref[...])
    gap = jnp.sum(jnp.where(is_first, logits, 0.0) - jnp.where(is_second, logits, 0.0), axis=1, keepdims=True)
    small = jnp.exp(-jnp.abs(gap))
    logit = small / ((1.0 + small) * (1.0 + small)) * (values[0] - values[1])
    logit_grad = jnp.where(is_first, logit, jnp.where(is_second, -logit, 0.0)).astype(BF)
    segments = [b[...].reshape(b.shape[0] * b.shape[1], b.shape[2]) for b in backs]
    normed_grad = picked_rows(number(0), number(1), segments) + dot(logit_grad, router_ref[...], NT)
    scaled = normed_grad * gain
    mean = jnp.mean(scaled * plain, axis=-1, keepdims=True)
    place = lax.broadcasted_iota(jnp.int32, (block, 1), 0) + step * block
    grad_out = jnp.where(place < length_ref[0], grad_ref[0].astype(F32), 0.0)
    total = grad_out + inverse * (scaled - plain * mean)

    @pl.when(step == core_ref[0])
    def _():
        total_ref[...] = total

    branch = total.astype(BF)
    mixed_grad_ref[...] = dot(branch, output_ref[...]).astype(BF)
    router_part = dot(logit_grad, normed, TN)
    gain_part = folded(normed_grad * plain)
    output_part = dot(mixed_ref[...], branch, TN)

    @pl.when(step == 0)
    def _():
        router_acc[...] = router_part
        gain_acc[...] = gain_part
        acc_ref[...] = output_part

    @pl.when(step > 0)
    def _():
        router_acc[...] += router_part
        gain_acc[...] += gain_part
        acc_ref[...] += output_part

    @pl.when(step == pl.num_programs(0) - 1)
    def _():
        extra_ref[...] = jnp.transpose(router_acc[...]) + jnp.where(wide == experts + 1, as_column(gain_acc[...]), 0.0)
        parts = jnp.transpose(acc_ref[...])
        far_ref[...] = parts[:, TILE:].astype(BF)
        own_ref[:, :TILE] = parts[:, :TILE]
        own_ref[:, TILE:] = parts[:, 2 * TILE :]


def combine(micro, core, length, info, out_grad, residual, mixed, gain, router, output_own, backs, half, spare):
    width = residual.shape[1]
    block = 512
    cols = mixed.shape[1]
    whole = lambda arr: pl.BlockSpec(arr.shape, lambda i, *_: (0,) * arr.ndim)
    fixed = lambda rows, n: pl.BlockSpec((rows, n), lambda i, *_: (0, 0))
    here = lambda n: pl.BlockSpec((block, n), lambda i, *_: (i, 0))
    experts = backs[0].shape[0]
    return pl.pallas_call(
        functools.partial(combine_kernel, experts, half, spare),
        grid_spec=pltpu.PrefetchScalarGridSpec(
            num_scalar_prefetch=3,
            grid=(SEQ // block,),
            in_specs=[
                pl.BlockSpec((8, block), lambda i, *_: (0, i)),
                pl.BlockSpec((1, block, width), lambda i, m, *_: (m[0], i, 0)),
                here(width), here(cols), whole(gain), whole(router), whole(output_own),
            ]
            + [whole(x) for x in backs],
            out_specs=[fixed(block, width), here(cols), fixed(width, TILE), fixed(width, 2 * TILE), fixed(width, 2 * TILE)],
            scratch_shapes=[
                pltpu.VMEM((cols, width), F32),
                pltpu.VMEM((TILE, width), F32),
                pltpu.VMEM((8, width), F32),
                pltpu.VMEM((6 * experts, half), F32),
            ],
        ),
        out_shape=[
            jax.ShapeDtypeStruct((block, width), F32),
            jax.ShapeDtypeStruct((SEQ, cols), BF),
            jax.ShapeDtypeStruct((width, TILE), F32),
            jax.ShapeDtypeStruct((width, 2 * TILE), BF),
            jax.ShapeDtypeStruct((width, 2 * TILE), F32),
        ],
        compiler_params=pltpu.CompilerParams(vmem_limit_bytes=60 * MIB),
        cost_estimate=SMALL_COST,
        name="combine",
    )(micro, core, length, info, out_grad, residual, mixed, gain, router, output_own, *backs)


def both_kernel(
    lane, micro_ref, core_ref, length_ref, part_ref, got_ref, tokens_ref, gain_ref, grad_ref,
    info_ref, residual_ref, own_ref, far_ref, out_ref, extra_ref, acc_ref,
):
    block = residual_ref.shape[0]
    info = jnp.transpose(info_ref[...])
    place = lax.broadcasted_iota(jnp.int32, (block, 1), 0) + (core_ref[0] * 2 + pl.program_id(0)) * block
    rows = residual_ref[...] + picked_rows(info[:, 6:7], info[:, 7:8], (own_ref[...], far_ref[...]))
    out_ref[0] = jnp.where(place < length_ref[0], rows, 0.0).astype(BF)
    normed_grad = got_ref[...] + part_ref[...]
    x = tokens_ref[0].astype(F32)
    inverse = lax.rsqrt(jnp.mean(x * x, axis=-1, keepdims=True) + 1e-06)
    plain = x * inverse
    scaled = normed_grad * gain_ref[...]
    mean = jnp.mean(scaled * plain, axis=-1, keepdims=True)
    out_ref[1] = (grad_ref[...] + inverse * (scaled - plain * mean)).astype(BF)
    wide = lax.broadcasted_iota(jnp.int32, (1, TILE), 1)
    part = folded(normed_grad * plain)

    @pl.when(pl.program_id(0) == 0)
    def _():
        acc_ref[...] = part

    @pl.when(pl.program_id(0) == 1)
    def _():
        extra_ref[...] = jnp.where(wide == lane, as_column(acc_ref[...] + part), 0.0)


def both_rows(lane, micro, core, length, part, got, layer_input, gain, residual_grad, info, residual, own, far):
    width = part.shape[1]
    plain = pl.BlockSpec((256, width), lambda i, *_: (i, 0))
    block = 256
    here = lambda n: pl.BlockSpec((block, n), lambda i, m, c, *_: (c[0] * 2 + i, 0))
    whole = lambda arr: pl.BlockSpec(arr.shape, lambda i, *_: (0, 0))
    return pl.pallas_call(
        functools.partial(both_kernel, lane),
        grid_spec=pltpu.PrefetchScalarGridSpec(
            num_scalar_prefetch=3,
            grid=(2,),
            in_specs=[
                plain,
                plain,
                pl.BlockSpec((1, block, width), lambda i, m, c, *_: (m[0], c[0] * 2 + i, 0)),
                whole(gain),
                plain,
                pl.BlockSpec((8, block), lambda i, m, c, *_: (0, c[0] * 2 + i)),
                here(width),
                whole(own),
                whole(far),
            ],
            out_specs=[
                pl.BlockSpec((2, block, width), lambda i, *_: (0, i, 0)),
                pl.BlockSpec((width, TILE), lambda i, *_: (0, 0)),
            ],
            scratch_shapes=[pltpu.VMEM((8, width), F32)],
        ),
        out_shape=[jax.ShapeDtypeStruct((2, 2 * block, width), BF), jax.ShapeDtypeStruct((width, TILE), F32)],
        compiler_params=pltpu.CompilerParams(vmem_limit_bytes=40 * MIB),
        cost_estimate=SMALL_COST,
        name="both_rows",
    )(micro, core, length, part, got, layer_input, gain, residual_grad, info, residual, own, far)


def sum_kernel(kept, own, got, out_own, early, late, late_far, table, sum_ref):
    low = low_lanes(early.shape)
    sum_ref[:, : 4 * TILE] = (own[:, : 4 * TILE] + got[:, : 4 * TILE].astype(F32)).astype(BF)
    mixed = jnp.where(low, own[:, 4 * TILE :], turned(out_own[:, TILE:]))
    sum_ref[:, 4 * TILE : 5 * TILE] = (mixed + got[:, 4 * TILE : 5 * TILE].astype(F32)).astype(BF)
    sum_ref[:, 5 * TILE : 6 * TILE] = (out_own[:, :TILE] + got[:, 5 * TILE :].astype(F32)).astype(BF)
    extra = early[...] + late[...] + late_far[...] + table[...]
    high = extra.astype(BF)
    rest = extra - high.astype(F32)
    if kept <= HEAD_DIM:
        sum_ref[:, 6 * TILE :] = jnp.where(low, high.astype(F32), turned(rest)).astype(BF)
    else:
        sum_ref[:, 6 * TILE : 7 * TILE] = high
        sum_ref[:, 7 * TILE :] = rest.astype(BF)


def packed_sums(kept, *parts):
    width = parts[0].shape[0]
    cols = (7 if kept <= HEAD_DIM else 8) * TILE
    block = 256
    here = lambda n: pl.BlockSpec((block, n), lambda i: (i, 0))
    return pl.pallas_call(
        functools.partial(sum_kernel, kept),
        grid=(width // block,),
        in_specs=[here(x.shape[1]) for x in parts],
        out_specs=here(cols),
        out_shape=jax.ShapeDtypeStruct((width, cols), BF),
        compiler_params=pltpu.CompilerParams(vmem_limit_bytes=40 * MIB),
        cost_estimate=SMALL_COST,
        name="packed_sums",
    )(*parts)


def final_kernel(kept, parts_ref, q_ref, k_ref, v_ref, o_ref, small_ref):
    total = parts_ref[0].astype(F32)
    for n in range(1, parts_ref.shape[0]):
        total = total + parts_ref[n].astype(F32)
    tile = lambda t: total[:, t * TILE : (t + 1) * TILE]
    q_ref[:, :TILE] = tile(0)
    q_ref[:, TILE:] = tile(3)[:, :HEAD_DIM]
    k_ref[:, :TILE] = tile(1)
    k_ref[:, TILE:] = turned(tile(3))[:, :HEAD_DIM]
    v_ref[:, :TILE] = tile(2)
    v_ref[:, TILE:] = tile(4)[:, :HEAD_DIM]
    o_ref[:, :TILE] = tile(5)
    o_ref[:, TILE:] = turned(tile(4))[:, :HEAD_DIM]
    small_ref[...] = tile(6) + (turned(tile(6)) if kept <= HEAD_DIM else tile(7))


def final_sums(kept, parts, shard):
    rows = parts.shape[1]
    return pl.pallas_call(
        functools.partial(final_kernel, kept),
        out_shape=[jax.ShapeDtypeStruct((rows, shard), F32)] * 4 + [jax.ShapeDtypeStruct((rows, TILE), F32)],
        compiler_params=pltpu.CompilerParams(vmem_limit_bytes=40 * MIB),
        cost_estimate=SMALL_COST,
        name="final_sums",
    )(parts)


def pair_gate(logits, own, other):
    lanes = lax.broadcasted_iota(jnp.int32, logits.shape, 1)
    gap = jnp.sum(
        jnp.where(lanes == own, logits, 0.0) - jnp.where(lanes == other, logits, 0.0), axis=1, keepdims=True
    )
    small = jnp.exp(-jnp.abs(gap))
    return jnp.where(gap >= 0.0, 1.0, small) / (1.0 + small)


def expert_kernel(lead, chunk, half, me_ref, partner_ref, rows_ref, grads_ref, router_ref, *refs):
    before, refs = (refs[0], refs[1:]) if lead is not None and lead > 0 else (None, refs)
    firsts, seconds = refs[:4], refs[4:8]
    back_ref, active_ref, slope_ref, gated_ref, gate_ref, mass_ref = refs[8:]
    rows = rows_ref[...]
    grads = grads_ref[...]
    gate = pair_gate(dot(rows, router_ref[...]), me_ref[0], partner_ref[...])
    gated_ref[...] = (gate * grads.astype(F32)).astype(BF)
    gate_ref[...] = jnp.broadcast_to(gate, gate_ref.shape)
    masses = [None] * (rows.shape[0] // STRIP)
    back = None
    width = firsts[0].shape[1]
    step = 256
    places = [(r, c) for r in range(4) for c in range(0, width, step)]

    def products(r, c):
        return dot(rows, firsts[r][:, c : c + step]), dot(grads, seconds[r][c : c + step, :], NT)

    ahead = products(*places[0])
    for n, (r, c) in enumerate(places):
        x, plain = ahead
        if n + 1 < len(places):
            ahead = products(*places[n + 1])
        place = slice(r * width + c, r * width + c + step)
        for at in range(0, rows.shape[0], STRIP):
            strip = slice(at, at + STRIP)
            value, flow = x[strip], plain[strip]
            square = value * value
            bent = jnp.tanh(value * (GELU_C + (GELU_C * GELU_A) * square))
            rise = 0.5 + 0.5 * bent
            active = value * rise
            slope = rise + active * (1.0 - bent) * (GELU_C + (3.0 * GELU_C * GELU_A) * square)
            low = active.astype(BF)
            active_ref[strip, place] = low
            slope_ref[strip, place] = (gate[strip] * flow * slope).astype(BF)
            part = low.astype(F32) * flow
            masses[at // STRIP] = put(masses[at // STRIP], part[:, :TILE] + part[:, TILE:])
        if c + step == width and r > 0:
            back = put(back, dot(slope_ref[:, (r - 1) * width : r * width], firsts[r - 1][...], NT))
    back = put(back, dot(slope_ref[:, 3 * width :], firsts[3][...], NT))
    back = back.astype(BF)
    mass = jnp.sum(jnp.concatenate(masses, 0), axis=1, keepdims=True)
    if lead is None:
        back_ref[...] = back
        mass_ref[...] = jnp.broadcast_to(mass, mass_ref.shape)
        return
    count = rows.shape[0] // chunk
    number = lax.broadcasted_iota(jnp.int32, (rows.shape[0], 1), 0)
    lanes = lax.broadcasted_iota(jnp.int32, (1, rows.shape[1]), 1)
    inside = lax.rem(number, chunk)
    spread = jnp.zeros(rows.shape, F32)
    for piece in range(3):
        high = mass.astype(BF).astype(F32)
        spread = jnp.where(lanes == piece * half + lead + inside, high, spread)
        mass = mass - high
    own = jnp.where(number // chunk == lax.broadcasted_iota(jnp.int32, (1, TILE), 1), 1.0, 0.0).astype(BF)
    line = dot(own, spread.astype(BF), TN)
    if before is None:
        back_ref[...] = back
        for e in range(count):
            mass_ref[e] = line[e : e + 1].astype(BF)
    else:
        back_ref[:, :chunk] = back.reshape(count, chunk, back.shape[1])
        row = lax.broadcasted_iota(jnp.int32, (16, 1), 0)
        for e in range(count):
            both = line[e : e + 1] + before[e].astype(F32)
            back_ref[e, chunk:] = jnp.where(row == 0, both, 0.0).astype(BF)


def row_block(total):
    return 320 if total % 320 == 0 else total


def expert_rows_pass(lead, chunk, half, me, partner, rows, grads, router, before, firsts, seconds):
    total, width = rows.shape
    block = row_block(total)
    experts = total // chunk
    hidden = sum(f.shape[1] for f in firsts)
    here = lambda cols: pl.BlockSpec((block, cols), lambda i: (i, 0))
    whole = lambda arr: pl.BlockSpec(arr.shape, lambda i: (0, 0))
    lines = pl.BlockSpec((block // chunk, 1, width), lambda i: (i, 0, 0))
    back_shape, back_spec = (total, width), here(width)
    mass_shape, mass_spec, mass_kind = (experts, 1, width), lines, BF
    if lead is None:
        mass_shape, mass_spec, mass_kind = (total, TILE), here(TILE), F32
    elif before is not None:
        back_shape = (experts, chunk + 16, width)
        back_spec = pl.BlockSpec((block // chunk, chunk + 16, width), lambda i: (i, 0, 0))
    return pl.pallas_call(
        functools.partial(expert_kernel, lead, chunk, half),
        grid=(total // block,),
        in_specs=[pl.BlockSpec(memory_space=pltpu.SMEM), here(1), here(width), here(width), whole(router)]
        + ([lines] if before is not None else [])
        + [whole(w) for w in firsts]
        + [whole(w) for w in seconds],
        out_specs=[back_spec, here(hidden), here(hidden), here(width), here(TILE), mass_spec],
        out_shape=[
            jax.ShapeDtypeStruct(back_shape, BF),
            jax.ShapeDtypeStruct((total, hidden), BF),
            jax.ShapeDtypeStruct((total, hidden), BF),
            jax.ShapeDtypeStruct((total, width), BF),
            jax.ShapeDtypeStruct((total, TILE), F32),
            jax.ShapeDtypeStruct(mass_shape, mass_kind),
        ],
        compiler_params=pltpu.CompilerParams(vmem_limit_bytes=56 * MIB),
        cost_estimate=SMALL_COST,
        name="expert_rows",
    )(me, partner, rows, grads, router, *([before] if before is not None else []), *firsts, *seconds)


def weight_parts(count, refs):
    rows, slopes, active, gated = (refs[n * count : (n + 1) * count] for n in range(4))
    first, second = None, None
    for n in range(count):
        first = put(first, dot(rows[n][...], slopes[n][...], TN))
        second = put(second, dot(active[n][...], gated[n][...], TN))
    return first, second


def cross_kernel(count, *refs):
    first, second = weight_parts(count, refs)
    refs[-1][0, 0] = first.astype(BF)
    refs[-1][0, 1] = second.astype(BF)


def kept_kernel(count, *refs):
    got_ref, far_ref, kept_ref = refs[-3:]
    first, second = weight_parts(count, refs)
    first = first + got_ref[0, 0].astype(F32)
    second = second + got_ref[0, 1].astype(F32)

    @pl.when(pl.program_id(0) == 0)
    def _():
        far_ref[0] = first.astype(BF)
        far_ref[1] = second.astype(BF)

    @pl.when(pl.program_id(0) == 1)
    def _():
        kept_ref[0] = first
        kept_ref[1] = second


def weight_specs(rows, slopes, quarter):
    total, width = rows[0].shape
    hidden = slopes[0].shape[1] // 4
    whole = pl.BlockSpec((total, width), lambda i: (0, 0))
    part = pl.BlockSpec((total, hidden), lambda i: (0, quarter(i)))
    count = len(rows)
    return width, hidden, [whole] * count + [part] * (2 * count) + [whole] * count


def cross_weight_grads(rows, slopes, active, gated):
    width, hidden, specs = weight_specs(rows, slopes, lambda i: 2 + i)
    return pl.pallas_call(
        functools.partial(cross_kernel, len(rows)),
        grid=(2,),
        in_specs=specs,
        out_specs=pl.BlockSpec((1, 2, width, hidden), lambda i: (i, 0, 0, 0)),
        out_shape=jax.ShapeDtypeStruct((2, 2, width, hidden), BF),
        compiler_params=pltpu.CompilerParams(vmem_limit_bytes=56 * MIB),
        cost_estimate=SMALL_COST,
        name="cross_weight_grads",
    )(*rows, *slopes, *active, *gated)


def kept_weight_grads(rows, slopes, active, gated, got):
    width, hidden, specs = weight_specs(rows, slopes, lambda i: 1 - i)
    fixed = pl.BlockSpec((2, width, hidden), lambda i: (0, 0, 0))
    return pl.pallas_call(
        functools.partial(kept_kernel, len(rows)),
        grid=(2,),
        in_specs=specs + [pl.BlockSpec((1, 2, width, hidden), lambda i: (1 - i, 0, 0, 0))],
        out_specs=[fixed, fixed],
        out_shape=[
            jax.ShapeDtypeStruct((2, width, hidden), BF),
            jax.ShapeDtypeStruct((2, width, hidden), F32),
        ],
        compiler_params=pltpu.CompilerParams(vmem_limit_bytes=56 * MIB),
        cost_estimate=SMALL_COST,
        name="kept_weight_grads",
    )(*rows, *slopes, *active, *gated, got)


def result_kernel(chunks, *refs):
    active, gates, seconds, out_ref = refs[:chunks], refs[chunks : 2 * chunks], refs[2 * chunks : -1], refs[-1]
    for c in range(chunks):

        @pl.when(pl.program_id(0) == c)
        def _(c=c):
            width = seconds[0].shape[0]
            total = None
            for r, second in enumerate(seconds):
                total = put(total, dot(active[c][:, r * width : (r + 1) * width], second[...]))
            rows = (total * gates[c][:, :1]).astype(BF)
            if chunks > 1:
                out_ref[:, 0] = rows.reshape(out_ref.shape[0], out_ref.shape[2], out_ref.shape[3])
            else:
                out_ref[...] = rows


def expert_results(active, gates, seconds, experts):
    chunks = len(active)
    total, hidden = active[0].shape
    width = seconds[0].shape[1]
    block = row_block(total)
    steps = total // block

    def here(c, cols):
        return pl.BlockSpec((block, cols), lambda g, i: (jnp.where(g == c, i, jnp.where(g < c, 0, steps - 1)), 0))

    chunk = total // experts
    if chunks > 1:
        shape = (experts, chunks, chunk, width)
        out_spec = pl.BlockSpec((block // chunk, 1, chunk, width), lambda g, i: (i, g, 0, 0))
    else:
        shape = (total, width)
        out_spec = pl.BlockSpec((block, width), lambda g, i: (i, 0))
    out = pl.pallas_call(
        functools.partial(result_kernel, chunks),
        grid=(chunks, steps),
        in_specs=[here(c, hidden) for c in range(chunks)]
        + [here(c, TILE) for c in range(chunks)]
        + [pl.BlockSpec(w.shape, lambda g, i: (0, 0)) for w in seconds],
        out_specs=out_spec,
        out_shape=jax.ShapeDtypeStruct(shape, BF),
        compiler_params=pltpu.CompilerParams(vmem_limit_bytes=56 * MIB),
        cost_estimate=SMALL_COST,
        name="expert_results",
    )(*active, *gates, *seconds)
    return out.reshape(experts, chunks * chunk, width)


def last_sum_kernel(kept_ref, y_ref, out_first, out_second):
    for n, out in enumerate((out_first, out_second)):
        out[...] = kept_ref[n] + y_ref[n].astype(F32)


def last_sums(kept, got_y):
    _, width, hidden = kept.shape
    block = 256
    here = pl.BlockSpec((block, hidden), lambda i: (i, 0))
    part = pl.BlockSpec((2, block, hidden), lambda i: (0, i, 0))
    return pl.pallas_call(
        last_sum_kernel,
        grid=(width // block,),
        in_specs=[part, part],
        out_specs=[here, here],
        out_shape=[jax.ShapeDtypeStruct((width, hidden), F32)] * 2,
        compiler_params=pltpu.CompilerParams(vmem_limit_bytes=40 * MIB),
        cost_estimate=SMALL_COST,
        name="last_sums",
    )(kept, got_y)


def send_kernel(micro_ref, code_ref, rows_ref, out_ref):
    block = out_ref.shape[0]
    ids = lax.broadcasted_iota(jnp.int32, (block, 1), 0) + pl.program_id(0) * block
    hot = jnp.where((ids == code_ref[:1]) | (ids == code_ref[1:2]), 1.0, 0.0).astype(BF)
    out_ref[...] = dot(hot, rows_ref[0]).astype(BF)


def send_rows(micro, code, rows, count):
    width = rows.shape[2]
    block = next(b for b in (336, 320, 384, count) if count % b == 0)
    return pl.pallas_call(
        send_kernel,
        grid_spec=pltpu.PrefetchScalarGridSpec(
            num_scalar_prefetch=1,
            grid=(count // block,),
            in_specs=[
                pl.BlockSpec(code.shape, lambda i, m: (0, 0)),
                pl.BlockSpec((1, SEQ, width), lambda i, m: (m[0], 0, 0)),
            ],
            out_specs=pl.BlockSpec((block, width), lambda i, m: (i, 0)),
        ),
        out_shape=jax.ShapeDtypeStruct((count, width), BF),
        compiler_params=pltpu.CompilerParams(vmem_limit_bytes=40 * MIB),
        cost_estimate=SMALL_COST,
        name="send_rows",
    )(micro, code, rows)


def place_kernel(place_ref, *refs):
    for n, piece in enumerate(refs[:4]):

        @pl.when(pl.program_id(0) == n)
        def _(piece=piece):
            for k, out_ref in enumerate(refs[4:]):
                out_ref[0] = piece[k]


def place_pieces(places, pieces):
    two, rows, width = pieces[0].shape
    whole = pl.BlockSpec(pieces[0].shape, lambda i, place_ref: (0, 0, 0))
    return pl.pallas_call(
        place_kernel,
        grid_spec=pltpu.PrefetchScalarGridSpec(
            num_scalar_prefetch=1,
            grid=(4,),
            in_specs=[whole] * 4,
            out_specs=[pl.BlockSpec((1, rows, width), lambda i, place_ref: (place_ref[i], 0, 0))] * two,
        ),
        out_shape=[jax.ShapeDtypeStruct((4, rows, width), pieces[0].dtype)] * two,
        compiler_params=pltpu.CompilerParams(vmem_limit_bytes=40 * MIB),
        cost_estimate=SMALL_COST,
        name="place_pieces",
    )(places, *pieces)


def swap(value, axis, count, bit):
    return lax.ppermute(value, axis, [(i, i ^ bit) for i in range(count)])


def all_to_all(value):
    return lax.all_to_all(value, "dp", split_axis=0, concat_axis=0, tiled=True)


def together(*values):
    return lax.optimization_barrier(values)


def local(
    layer_input, out_grad, first_gain, query_weight, key_weight, value_weight, output_weight,
    position_bias, second_gain, router_weight, expert_in, expert_out, seq_lengths, routes,
):
    micro_count, tok_rows, width = layer_input.shape
    dp_count = lax.axis_size("dp")
    expert_count = router_weight.shape[1]
    shard = query_weight.shape[1]
    heads_here = position_bias.shape[0]
    assert lax.axis_size("tensor") == 4 and micro_count == 2 and expert_count == dp_count
    assert tok_rows == SEQ and seq_lengths.shape[1] == 1
    capacity = max(8, 8 * (10 * tok_rows // (32 * expert_count)))
    half = capacity // 2
    stride = 8 * (half // 8 + 1)
    by_lines = dp_count == 8
    chunks = 2 if half % 32 == 0 else 1
    chunk = half // chunks
    chunk_rows = expert_count * chunk
    rows_here = query_weight.shape[0]
    me = lax.axis_index("dp")
    rank = lax.axis_index("tensor")
    micro = rank // 2
    core = rank % 2

    def swap_y(value):
        return swap(value, "tensor", 4, 2)

    def swap_core(value):
        return swap(value, "tensor", 4, 1)

    micro_arg = micro.reshape(1).astype(jnp.int32)
    core_arg = core.reshape(1).astype(jnp.int32)

    packed = pack_weights(query_weight, key_weight, value_weight, output_weight, first_gain, second_gain, router_weight)
    three = 3 * TILE

    def doubled(stacked, bit, axis=0):
        other = swap(stacked, "dp", dp_count, bit)
        high = (me & bit) != 0
        pair = jnp.where(high, jnp.stack([other, stacked], axis + 1), jnp.stack([stacked, other], axis + 1))
        return pair.reshape(stacked.shape[:axis] + (-1,) + stacked.shape[axis + 1 :])

    stacked = packed[None]
    bit = dp_count // 2
    while bit > 1:
        stacked = doubled(stacked, bit)
        bit //= 2
    length = lax.dynamic_index_in_dim(seq_lengths, micro, 0, keepdims=False)
    route = lax.dynamic_index_in_dim(routes, micro, 0, keepdims=False).T
    expert_ids = jnp.arange(expert_count, dtype=jnp.int32)
    named = (expert_ids[:, None, None] == route[None]).astype(jnp.int32)
    per_token = jnp.sum(named, axis=1, dtype=jnp.int32)
    earlier = jnp.cumsum(per_token, axis=1, dtype=jnp.int32) - per_token
    slot = jnp.sum(named * earlier[:, None, :], axis=0, dtype=jnp.int32)
    here = slot // half == core
    within = slot % half
    chunk_of = within // chunk
    inside = within % chunk
    spare = 16 * -(-chunk // 16)
    last_stride = spare + 16
    last = (chunks - 1) * chunk_rows
    code_back = jnp.where(
        chunk_of == chunks - 1, last + route * last_stride + inside, chunk_of * chunk_rows + route * chunk + inside
    )
    code_back = code_back + jnp.where(here, 0, last + expert_count * last_stride)
    code_result = route * half + within + jnp.where(here, 0, expert_count * half)
    info = jnp.concatenate([code_back, route, slot, code_result], 0)

    code_grads = jnp.where(here, route * stride + within, -1)
    valid = jnp.arange(SEQ, dtype=jnp.int32) < length[0]
    ids = jnp.arange(expert_count * stride, dtype=jnp.int32)[:, None]
    partner = jnp.sum(
        jnp.where(ids == code_grads[:1], route[1:], 0) + jnp.where(ids == code_grads[1:], route[:1], 0), axis=1, dtype=jnp.int32
    )
    grads_sent = send_rows(micro_arg, jnp.where(valid[None], code_grads, -1), out_grad, expert_count * stride)
    grads_sent = grads_sent.reshape(expert_count, stride, width)
    partner_row = jnp.pad(partner.reshape(expert_count, stride)[:, :half].astype(BF), ((0, 0), (0, width - half)))
    grads_sent = grads_sent.at[:, half].set(partner_row)
    stacked, grads_sent, position_bias = together(stacked, grads_sent, position_bias)
    if by_lines:
        lines = [list(range(x, dp_count, 2)) for x in range(2)]
        grads_z = lax.all_to_all(
            grads_sent.reshape(dp_count // 2, 2, stride, width), "dp", split_axis=0, concat_axis=0,
            axis_index_groups=lines, tiled=True,
        )

    first_own = expert_in[0]
    second_own = expert_out[0]
    part_b = stacked[:, :, :three]
    far_b = swap_y(part_b)
    part_a = doubled(stacked[:, :, three:], 1)
    part_a, far_b = together(part_a, far_b)
    pair_b = jnp.stack([part_b, far_b])
    a_own = part_a[:, :, :three]
    a_far = swap_y(a_own).reshape(width, three)
    a_own = a_own.reshape(width, three)
    pair_b = doubled(pair_b, 1, 1).reshape(2, width, three)
    if by_lines:
        a_far, pair_b, first_own = together(a_far, pair_b, first_own)
    else:
        a_far, pair_b, grads_sent, first_own = together(a_far, pair_b, grads_sent, first_own)
    first_y = swap_y(first_own)
    small_all = part_a[:, :, three:].reshape(width, TILE)
    gain_one = small_all[:, expert_count].astype(F32)[None]
    gain_two = small_all[:, expert_count + 1].astype(F32)[None]
    router_wide = small_all
    far_bias = swap_y(position_bias)
    bias = jnp.concatenate([position_bias[:2], far_bias[:2], position_bias[2:], far_bias[2:]], 0)
    head_total = bias.shape[0]
    hot_const = jnp.asarray(NEAR_HOT, dtype=BF)
    near = dot(bias, hot_const) - bias[:, NB - 1 :].astype(F32)
    near = near.reshape(head_total, 2, TILE, TILE)
    places = jnp.arange(TILE, dtype=jnp.int32)
    causal = jnp.stack([places[None, :] <= places[:, None], jnp.ones((TILE, TILE), bool)])
    near = jnp.where(causal[None], near, NEG)

    if by_lines:
        high = (me & 1) != 0
    else:
        grads_here = all_to_all(grads_sent)

    qkv, normed_one, qkv_weight, output_own = norm_and_project(
        micro_arg, layer_input, gain_one, a_own, a_far, pair_b[0], pair_b[1]
    )
    output_far = swap_core(output_own)
    mixed, logs = attend(length, qkv, near)
    mixed, output_far = together(mixed, output_far)
    mixed_far = swap_core(mixed)
    code_chunks = jnp.where(here, chunk_of * chunk_rows + route * chunk + inside, -1)
    if by_lines:
        sent_x = lax.dynamic_index_in_dim(grads_z, 1 - (me & 1), 1, keepdims=False)
        mixed_far, grads_z, sent_x = together(mixed_far, grads_z, sent_x)
        got_x = swap(sent_x, "dp", dp_count, 1)
    residual, *parts = residual_and_rows(
        micro_arg, layer_input, mixed, mixed_far, output_own, output_far, gain_two, code_chunks, chunk_rows, chunks
    )

    if by_lines:
        parts, first_y, second_own = together(parts, first_y, second_own)
        kept_x = jnp.where(high, grads_z[:, 1], grads_z[:, 0])
        pair_x = jnp.where(high, jnp.stack([got_x, kept_x], 1), jnp.stack([kept_x, got_x], 1))
        grads_here = pair_x.reshape(dp_count, stride, width)
    else:
        parts, grads_here, first_y, second_own = together(parts, grads_here, first_y, second_own)
    second_y = swap_y(second_own)
    parts = [part.reshape(expert_count, chunk, width) for part in parts]
    arrived = [all_to_all(parts[0])]
    partner_here = grads_here[:, half, :half].astype(jnp.int32)

    def chunk_grads(c):
        at = slice(c * chunk, (c + 1) * chunk)
        return grads_here[:, at].reshape(chunk_rows, width), partner_here[:, at].reshape(chunk_rows, 1)

    grads_parts = [chunk_grads(c) for c in range(chunks)]
    arrived[0], grads_parts, second_y = together(arrived[0], grads_parts, second_y)

    firsts = (first_own, first_y, swap_core(first_own), swap_core(first_y))
    seconds = (second_own, second_y, swap_core(second_own), swap_core(second_y))

    for c in range(1, chunks):
        sent, arrived[-1] = together(parts[c], arrived[-1])
        arrived.append(all_to_all(sent))

    me_arg = me.reshape(1).astype(jnp.int32)
    rows_all, slopes, active, gated, gates, backs = [], [], [], [], [], []
    line = None
    for c in range(chunks):
        grads_c, partner_c = grads_parts[c]
        rows_c = arrived[c].reshape(chunk_rows, width)
        back, act, slo, gat, gte, line = expert_rows_pass(
            c * chunk if chunks > 1 else None, chunk, half, me_arg, partner_c, rows_c, grads_c, router_wide, line, firsts, seconds
        )
        rows_all.append(rows_c)
        slopes.append(slo)
        active.append(act)
        gated.append(gat)
        gates.append(gte)
        if chunks == 1:
            gate_grad = line[:, 0].reshape(expert_count, chunk)
            pieces = []
            for _ in range(3):
                piece = gate_grad.astype(BF)
                pieces.append(piece)
                gate_grad = gate_grad - piece.astype(F32)
            gate_row = jnp.pad(jnp.concatenate(pieces, 1), ((0, 0), (0, width - 3 * half)))
            back = jnp.pad(back.reshape(expert_count, chunk, width), ((0, 0), (0, last_stride - chunk), (0, 0)))
            back = back.at[:, spare].set(gate_row)
        if c + 1 < chunks:
            back, arrived[c + 1] = together(back.reshape(expert_count, chunk, width), arrived[c + 1])
        else:
            back, rows_all[-1], backs = together(back, rows_all[-1], backs)
        backs.append(all_to_all(back))
    grads_cross = cross_weight_grads(rows_all, slopes, active, gated)
    gates, grads_cross = together(gates, grads_cross)
    grads_in = swap_core(grads_cross)
    results = expert_results(active, gates, seconds, expert_count)
    results, grads_in = together(results, grads_in)
    grads_far, grads_kept = kept_weight_grads(rows_all, slopes, active, gated, grads_in)
    backs[-1], results, grads_far = together(backs[-1], results, grads_far)

    across_y = swap_y(grads_far)
    results_own = all_to_all(results).reshape(expert_count * half, width)

    backs_far = [swap_core(b) for b in backs]
    residual_grad, mixed_grad, extra_early, output_sent, output_kept = combine(
        micro_arg, core_arg, length, info, out_grad, residual, mixed, gain_two, router_wide, output_own,
        backs + backs_far, half, spare,
    )

    tiles, sums, far_sent, own_parts, sent, kept_part = attend_back(
        core_arg, length, qkv, near, mixed, logs, mixed_grad, normed_one, output_sent, qkv_weight
    )
    far_got = swap_y(far_sent)
    sent, results_own = together(sent, results_own)
    got = swap_core(sent)
    rows_both, extra_late = both_rows(
        expert_count, micro_arg, core_arg, length, kept_part, got, layer_input, gain_one, residual_grad,
        info, residual, results_own, swap_core(results_own),
    )
    rows_both, across_y, tiles = together(rows_both, across_y, tiles)
    late_far = swap_core(extra_late)
    corner = micro * 2 + core
    corners = jnp.stack([corner, corner ^ 1, corner ^ 2, corner ^ 3]).astype(jnp.int32)
    rows_y = swap_y(rows_both)
    expert_in_grad, expert_out_grad = last_sums(grads_kept, across_y)
    rows_y, expert_in_grad, expert_out_grad = together(rows_y, expert_in_grad, expert_out_grad)
    pieces = (rows_both, swap_core(rows_both), rows_y, swap_core(rows_y))

    tiles = tiles.reshape(head_total, 2 * TILE * TILE)
    tiles_high = tiles.astype(BF)
    tiles_rest = (tiles - tiles_high.astype(F32)).astype(BF)
    table = dot(tiles_high, hot_const, NT) + dot(tiles_rest, hot_const, NT)
    far_sum = jnp.sum(sums[:, :, 0], axis=1) - jnp.sum(table[:, : NB - 1], axis=1)
    table = jnp.concatenate([table[:, : NB - 1], far_sum[:, None]], 1)
    table_own = jnp.concatenate([table[0:2], table[4:5]], 0)
    table_far = jnp.concatenate([table[2:4], table[5:6]], 0)
    table_cols = heads_here * NB // rows_here
    table_both = jnp.concatenate([table_own.reshape(rows_here, table_cols), table_far.reshape(rows_here, table_cols)], 1)
    base = expert_count + 2
    kept = base + 2 * table_cols
    table_tile = jnp.tile(jnp.pad(table_both, ((0, 0), (base, TILE - kept))), (dp_count, 1))

    grads = packed_sums(kept, own_parts, far_got, output_kept, extra_early, extra_late, late_far, table_tile)
    arrived_grads = all_to_all(grads.reshape(dp_count, rows_here, grads.shape[1]))
    layer_output, input_grad = (out.reshape(2, SEQ, width) for out in place_pieces(corners, pieces))
    arrived_grads, layer_output, input_grad = together(arrived_grads, layer_output, input_grad)
    query_grad, key_grad, value_grad, output_grad, small = final_sums(kept, arrived_grads, shard)
    small_y = swap_y(small)
    both = small + small_y
    table_sum = small[:, base : base + table_cols] + small_y[:, base + table_cols : kept]
    return (
        layer_output,
        input_grad,
        both[:, expert_count],
        query_grad,
        key_grad,
        value_grad,
        output_grad.T,
        table_sum.reshape(heads_here, NB),
        both[:, expert_count + 1],
        both[:, :expert_count],
        expert_in_grad[None],
        expert_out_grad[None],
    )


def solution(mesh):
    return jax.shard_map(
        local,
        mesh=mesh,
        in_specs=(
            P(None, "dp", None),
            P(None, "dp", None),
            P("dp"),
            P("dp", "tensor"),
            P("dp", "tensor"),
            P("dp", "tensor"),
            P("tensor", "dp"),
            P("tensor", None),
            P("dp"),
            P("dp", None),
            P("dp", None, "tensor"),
            P("dp", "tensor", None),
            P(None, "dp"),
            P(None, "dp", None),
        ),
        out_specs=(
            P(None, "dp", None),
            P(None, "dp", None),
            P("dp"),
            P("dp", "tensor"),
            P("dp", "tensor"),
            P("dp", "tensor"),
            P("tensor", "dp"),
            P("tensor", None),
            P("dp"),
            P("dp", None),
            P("dp", None, "tensor"),
            P("dp", "tensor", None),
        ),
        check_vma=False,
    )
```

```python
import functools

import jax
import jax.numpy as jnp
import numpy as np
from jax import lax
from jax.experimental import pallas as pl
from jax.experimental.pallas import tpu as pltpu
from jax.sharding import PartitionSpec as P

HEAD_DIM = 64
NB = 32
SEQ = 1024
TILE = 128
QROWS = 256
NEG = -1e30
GELU_C = 0.7978845608028654
GELU_A = 0.044715

BF = jnp.bfloat16
F32 = jnp.float32

bucket_edges = np.ceil(16.0 * 8.0 ** (np.arange(1, 16) / 16.0)).astype(np.int32)


def near_tables():
    rows = np.arange(TILE)[:, None]
    cols = np.arange(TILE)[None, :]
    hots = []
    for shift in (0, TILE):
        distance = rows - cols + shift
        clipped = np.maximum(distance, 0)
        reached = np.sum(clipped[..., None] >= bucket_edges, axis=-1)
        bucket = np.minimum(clipped, 16) + reached
        hots.append(bucket[..., None] == np.arange(NB))
    hot = np.stack(hots).reshape(2 * TILE * TILE, NB).T
    return hot


NEAR_HOT = near_tables()
assert bucket_edges[-1] <= TILE


def dot(a, b, dims=((1,), (0,))):
    return lax.dot_general(a, b, (dims, ((), ())), preferred_element_type=F32)


NT = ((1,), (1,))
TN = ((0,), (0,))


MIB = 2**20
SMALL_COST = pl.CostEstimate(flops=1_000_000, bytes_accessed=1_000_000, transcendentals=0)


STRIP = 32


def score_strip(s, at, block, j, start, near_ref, half, length):
    part = s[at : at + STRIP]
    near = slice(start % TILE, start % TILE + STRIP)
    if j == block:
        if start < TILE:
            left = part[:, :TILE] + near_ref[half, 0, near, :]
            right = jnp.full((STRIP, TILE), NEG, F32)
        else:
            left = part[:, :TILE] + near_ref[half, 1, near, :]
            right = part[:, TILE:] + near_ref[half, 0, near, :]
        part = jnp.concatenate([left, right], 1)
    elif j == block - 1 and start < TILE:
        part = jnp.concatenate([part[:, :TILE], part[:, TILE:] + near_ref[half, 1, near, :]], 1)
    if (j + 1) * QROWS > SEQ // 2:
        place = lax.broadcasted_iota(jnp.int32, (1, QROWS), 1) + j * QROWS
        part = part + jnp.where(place < length, 0.0, NEG)
    return part


def lane_half(rows):
    return lax.broadcasted_iota(jnp.int32, (rows, 2 * HEAD_DIM), 1) < HEAD_DIM


def attend_kernel(length_ref, query_ref, key_ref, value_ref, near_ref, out_ref, log_ref):
    length = length_ref[0]
    lanes = lane_half(QROWS)
    value_ext = jnp.concatenate([value_ref[...], jnp.ones((SEQ, TILE), BF)], 1)
    for i in range(SEQ // QROWS):
        q_rows = query_ref[i * QROWS : (i + 1) * QROWS, :] * BF(0.125)
        q_both = jnp.concatenate([jnp.where(lanes, q_rows, BF(0)), jnp.where(lanes, BF(0), q_rows)], 0)
        tiles = [dot(q_both, key_ref[j * QROWS : (j + 1) * QROWS, :], NT) for j in range(i + 1)]
        tops = []
        weights = [[] for _ in tiles]
        for h in range(2):
            for start in range(0, QROWS, STRIP):
                strips = [
                    score_strip(s, h * QROWS + start, i, j, start, near_ref, h, length) for j, s in enumerate(tiles)
                ]
                top = strips[0]
                for s in strips[1:]:
                    top = jnp.maximum(top, s)
                top = jnp.max(top, axis=1, keepdims=True)
                tops.append(top)
                for j, s in enumerate(strips):
                    weights[j].append(jnp.exp(s - top).astype(BF))
        total = None
        for j, strips in enumerate(weights):
            total = put(total, dot(jnp.concatenate(strips, 0), value_ext[j * QROWS : (j + 1) * QROWS, :]))
        row_sum = total[:, TILE:]
        out = total[:, :TILE] / row_sum
        logs = jnp.concatenate(tops, 0) + jnp.log(row_sum)
        out_ref[i * QROWS : (i + 1) * QROWS, :] = jnp.where(lanes, out[:QROWS], out[QROWS:]).astype(BF)
        log_ref[i * QROWS : (i + 1) * QROWS, :] = jnp.where(lanes, logs[:QROWS], logs[QROWS:])


def attend(length, qkv, near):
    pairs = qkv.shape[1] // (3 * TILE)
    cols = pairs * TILE
    return pl.pallas_call(
        attend_kernel,
        grid=(pairs,),
        in_specs=[
            pl.BlockSpec(memory_space=pltpu.SMEM),
            pl.BlockSpec((SEQ, TILE), lambda p: (0, p)),
            pl.BlockSpec((SEQ, TILE), lambda p: (0, pairs + p)),
            pl.BlockSpec((SEQ, TILE), lambda p: (0, 2 * pairs + p)),
            pl.BlockSpec((2, 2, TILE, TILE), lambda p: (p, 0, 0, 0)),
        ],
        out_specs=[
            pl.BlockSpec((SEQ, TILE), lambda p: (0, p)),
            pl.BlockSpec((SEQ, TILE), lambda p: (0, p)),
        ],
        out_shape=[
            jax.ShapeDtypeStruct((SEQ, cols), BF),
            jax.ShapeDtypeStruct((SEQ, cols), F32),
        ],
        compiler_params=pltpu.CompilerParams(vmem_limit_bytes=40 * MIB),
        cost_estimate=SMALL_COST,
        name="attend",
    )(length, qkv, qkv, qkv, near)


def attend_back_kernel(
    pairs, blocks, core_ref, length_ref, query_ref, key_ref, value_ref, near_ref, out_ref, log_ref, grad_ref,
    normed_ref, output_ref, weight_ref, tile_ref, sum_ref, far_ref, own_ref, sent_ref, kept_ref, grads, dk_acc, dv_acc,
):
    step = pl.program_id(0)

    @pl.when(step < pairs)
    def _():
        pair_grads(
            step, length_ref, query_ref, key_ref, value_ref, near_ref, out_ref, log_ref, grad_ref,
            tile_ref, sum_ref, grads, dk_acc, dv_acc,
        )

    @pl.when((step >= pairs) & (step < pairs + blocks))
    def _():
        low = low_lanes((normed_ref.shape[1], TILE))
        q, k, v = (
            dot(normed_ref[...], jnp.concatenate([grads[n, p] for p in range(pairs)], 1), TN) for n in range(3)
        )
        for n, part in enumerate((q, k, v)):
            own_ref[:, n * TILE : (n + 1) * TILE] = part[:, :TILE]
            far_ref[:, n * TILE : (n + 1) * TILE] = part[:, TILE : 2 * TILE].astype(BF)
        q, k, v = (part[:, 2 * TILE :] for part in (q, k, v))
        far_ref[:, 3 * TILE : 4 * TILE] = jnp.where(low, turned(q), k).astype(BF)
        far_ref[:, 4 * TILE : 5 * TILE] = jnp.where(low, turned(v), output_ref[:, TILE:].astype(F32)).astype(BF)
        far_ref[:, 5 * TILE :] = output_ref[:, :TILE]
        own_ref[:, 3 * TILE : 4 * TILE] = jnp.where(low, q, turned(k))
        own_ref[:, 4 * TILE :] = jnp.where(low, v, 0.0)

    for late, half_ref in enumerate((sent_ref, kept_ref)):
        first = pairs + blocks + 2 * late

        @pl.when((step >= first) & (step < first + 2))
        def _(half_ref=half_ref, first=first, late=late):
            rows = half_ref.shape[0]
            mine = core_ref[0] if late else 1 - core_ref[0]
            start = pl.multiple_of((2 * mine + step - first) * rows, rows)
            total = None
            for n in range(3):
                part = jnp.concatenate([grads[n, p, pl.ds(start, rows), :] for p in range(pairs)], 1)
                cols = part.shape[1]
                total = put(total, dot(part, weight_ref[:, n * cols : (n + 1) * cols], NT))
            half_ref[...] = total


def pair_grads(
    pair, length_ref, query_ref, key_ref, value_ref, near_ref, out_ref, log_ref, grad_ref, tile_ref, sum_ref, grads, dk_acc, dv_acc
):
    length = length_ref[0]
    lanes = lane_half(QROWS)
    key_ext = jnp.concatenate([key_ref[...], jnp.ones((SEQ, TILE), BF)], 1)
    near_sums = [[None, None], [None, None]]
    all_sums = [None, None]

    def both(rows):
        return jnp.concatenate([jnp.where(lanes, rows, BF(0)), jnp.where(lanes, BF(0), rows)], 0)

    for i in range(SEQ // QROWS):
        rows = slice(i * QROWS, (i + 1) * QROWS)
        q_both = both(query_ref[rows, :] * BF(0.125))
        g_rows = grad_ref[rows, :]
        g_both = both(g_rows)
        mass = g_rows.astype(F32) * out_ref[rows, :].astype(F32)
        deltas = [
            jnp.sum(jnp.where(lanes, mass, 0.0), axis=1, keepdims=True),
            jnp.sum(jnp.where(lanes, 0.0, mass), axis=1, keepdims=True),
        ]
        logs = [log_ref[rows, h * HEAD_DIM : h * HEAD_DIM + 1] for h in range(2)]
        dq = None
        for j in range(i + 1):
            keys = slice(j * QROWS, (j + 1) * QROWS)
            s = dot(q_both, key_ref[keys, :], NT)
            dp = dot(g_both, value_ref[keys, :], NT)
            p_strips, d_strips = [], []
            for h in range(2):
                for start in range(0, QROWS, STRIP):
                    strip = slice(start, start + STRIP)
                    at = h * QROWS + start
                    p = jnp.exp(score_strip(s, at, i, j, start, near_ref, h, length) - logs[h][strip])
                    p_strips.append(p.astype(BF))
                    d_strips.append((p * (dp[at : at + STRIP] - deltas[h][strip])).astype(BF))
            p, ds = jnp.concatenate(p_strips, 0), jnp.concatenate(d_strips, 0)
            part = dot(ds, key_ext[keys, :])
            dq = put(dq, jnp.where(lanes, part[:QROWS, :TILE], part[QROWS:, :TILE]))
            for h in range(2):
                sums = part[h * QROWS : (h + 1) * QROWS, TILE:]
                all_sums[h] = put(all_sums[h], jnp.sum(sums.reshape(QROWS // 8, 8, TILE), axis=0))
            dk_part = dot(ds, q_both, TN)
            dv_part = dot(p, g_both, TN)
            if i == j:
                dk_acc[keys, :] = dk_part
                dv_acc[keys, :] = dv_part
            else:
                dk_acc[keys, :] += dk_part
                dv_acc[keys, :] += dv_part
            for h in range(2):
                mine = ds[h * QROWS : (h + 1) * QROWS]
                if j == i:
                    wide = mine.astype(F32)
                    near_sums[h][0] = put(near_sums[h][0], wide[:TILE, :TILE] + wide[TILE:, TILE:])
                    near_sums[h][1] = put(near_sums[h][1], wide[TILE:, :TILE])
                elif j == i - 1:
                    near_sums[h][1] = put(near_sums[h][1], mine[:TILE, TILE:].astype(F32))
        grads[0, pair, rows, :] = (dq * 0.125).astype(BF)
    grads[1, pair] = dk_acc[...].astype(BF)
    grads[2, pair] = dv_acc[...].astype(BF)
    for h in range(2):
        tile_ref[h, 0] = near_sums[h][0]
        tile_ref[h, 1] = near_sums[h][1]
        sum_ref[h] = all_sums[h]


def attend_back(core, length, qkv, near, mixed, logs, grad, normed, output, weight):
    pairs = qkv.shape[1] // (3 * TILE)
    width = normed.shape[1]
    block = 256
    blocks = width // block
    at = lambda i: jnp.minimum(i, pairs - 1)
    then = lambda i: jnp.clip(i - pairs, 0, blocks - 1)
    return pl.pallas_call(
        functools.partial(attend_back_kernel, pairs, blocks),
        grid_spec=pltpu.PrefetchScalarGridSpec(
            num_scalar_prefetch=2,
            grid=(pairs + blocks + 4,),
            in_specs=[
                pl.BlockSpec((SEQ, TILE), lambda i, *_: (0, at(i))),
                pl.BlockSpec((SEQ, TILE), lambda i, *_: (0, pairs + at(i))),
                pl.BlockSpec((SEQ, TILE), lambda i, *_: (0, 2 * pairs + at(i))),
                pl.BlockSpec((2, 2, TILE, TILE), lambda i, *_: (at(i), 0, 0, 0)),
            ]
            + [pl.BlockSpec((SEQ, TILE), lambda i, *_: (0, at(i)))] * 3
            + [
                pl.BlockSpec((SEQ, block), lambda i, *_: (0, then(i))),
                pl.BlockSpec((block, 2 * TILE), lambda i, *_: (then(i), 0)),
                pl.BlockSpec(weight.shape, lambda i, *_: (0, 0)),
            ],
            out_specs=[
                pl.BlockSpec((2, 2, TILE, TILE), lambda i, *_: (at(i), 0, 0, 0)),
                pl.BlockSpec((2, 8, TILE), lambda i, *_: (at(i), 0, 0)),
                pl.BlockSpec((block, 6 * TILE), lambda i, *_: (then(i), 0)),
                pl.BlockSpec((block, 5 * TILE), lambda i, *_: (then(i), 0)),
                pl.BlockSpec((block, width), lambda i, *_: (jnp.clip(i - pairs - blocks, 0, 1), 0)),
                pl.BlockSpec((block, width), lambda i, *_: (jnp.clip(i - pairs - blocks - 2, 0, 1), 0)),
            ],
            scratch_shapes=[
                pltpu.VMEM((3, pairs, SEQ, TILE), BF), pltpu.VMEM((SEQ, TILE), F32), pltpu.VMEM((SEQ, TILE), F32),
            ],
        ),
        out_shape=[
            jax.ShapeDtypeStruct((2 * pairs, 2, TILE, TILE), F32),
            jax.ShapeDtypeStruct((2 * pairs, 8, TILE), F32),
            jax.ShapeDtypeStruct((width, 6 * TILE), BF),
            jax.ShapeDtypeStruct((width, 5 * TILE), F32),
            jax.ShapeDtypeStruct((2 * block, width), F32),
            jax.ShapeDtypeStruct((2 * block, width), F32),
        ],
        compiler_params=pltpu.CompilerParams(vmem_limit_bytes=60 * MIB),
        cost_estimate=SMALL_COST,
        name="attend_back",
    )(core, length, qkv, qkv, qkv, near, mixed, logs, grad, normed, output, weight)


def low_lanes(shape):
    return lax.broadcasted_iota(jnp.int32, shape, 1) < HEAD_DIM


def turned(tile):
    return pltpu.roll(tile, HEAD_DIM, 1)


def pack_kernel(q_ref, k_ref, v_ref, o_ref, one_ref, two_ref, router_ref, out_ref):
    shard = q_ref.shape[1]
    rows = q_ref.shape[0]
    source = lax.broadcasted_iota(jnp.int32, (shard, 6 * TILE), 0)
    target = lax.broadcasted_iota(jnp.int32, (shard, 6 * TILE), 1)

    def moved(pair_base, last_base):
        want = jnp.where(source < TILE, source + pair_base, source - TILE + last_base)
        return jnp.where(target == want, 1.0, 0.0).astype(BF)

    total = dot(v_ref[...], moved(0, 2 * TILE)) + dot(o_ref[...], moved(TILE, 2 * TILE + HEAD_DIM), TN)
    total = total + dot(q_ref[...], moved(3 * TILE, 5 * TILE)) + dot(k_ref[...], moved(4 * TILE, 5 * TILE + HEAD_DIM))
    out_ref[:, : 6 * TILE] = total.astype(BF)
    experts = router_ref.shape[0]
    own_row = lax.broadcasted_iota(jnp.int32, (rows, rows), 0) == lax.broadcasted_iota(jnp.int32, (rows, rows), 1)

    def column(ref):
        return jnp.sum(jnp.where(own_row, ref[...].astype(F32), 0.0), axis=1, keepdims=True)

    lanes = lax.broadcasted_iota(jnp.int32, (experts, TILE), 1)
    spread = jnp.where(lanes == lax.broadcasted_iota(jnp.int32, (experts, TILE), 0), 1.0, 0.0).astype(BF)
    place = lax.broadcasted_iota(jnp.int32, (rows, TILE), 1)
    small = dot(router_ref[...], spread, TN)
    small = jnp.where(place == experts, column(one_ref), jnp.where(place == experts + 1, column(two_ref), small))
    out_ref[:, 6 * TILE :] = small.astype(BF)


def pack_weights(query, key, value, output, one, two, router):
    rows = query.shape[0]
    return pl.pallas_call(
        pack_kernel,
        out_shape=jax.ShapeDtypeStruct((rows, 7 * TILE), BF),
        compiler_params=pltpu.CompilerParams(vmem_limit_bytes=60 * MIB),
        cost_estimate=SMALL_COST,
        name="pack_weights",
    )(query, key, value, output, one[None], two[None], router.T)


def qkv_kernel(micro_ref, tokens_ref, gain_ref, a_own, a_far, b_own, b_far, qkv_ref, normed_ref, weight_ref, output_ref):
    width = tokens_ref.shape[2]

    @pl.when(pl.program_id(0) == 0)
    def _():
        low = low_lanes((width, TILE))

        def tiles(own, far, pair, low_half):
            at = slice(pair * TILE, (pair + 1) * TILE)
            one, two = own[:, 2 * TILE :].astype(F32), far[:, 2 * TILE :].astype(F32)
            last = jnp.where(low, one, turned(two)) if low_half else jnp.where(low, turned(one), two)
            return own[:, at], far[:, at], last.astype(BF)

        for n, (own, far, pair, low_half) in enumerate(
            ((a_own, a_far, 0, True), (a_own, a_far, 1, False), (b_own, b_far, 0, True))
        ):
            for t, tile in enumerate(tiles(own[...], far[...], pair, low_half)):
                at = 3 * n + t
                weight_ref[:, at * TILE : (at + 1) * TILE] = tile
        for t, tile in enumerate(tiles(b_own[...], b_far[...], 1, False)):
            output_ref[:, t * TILE : (t + 1) * TILE] = tile

    x = tokens_ref[0].astype(F32)
    inverse = lax.rsqrt(jnp.mean(x * x, axis=-1, keepdims=True) + 1e-06)
    normed = (x * inverse * gain_ref[...]).astype(BF)
    normed_ref[...] = normed
    qkv_ref[...] = dot(normed, weight_ref[...]).astype(BF)


def norm_and_project(micro, layer_input, gain, a_own, a_far, b_own, b_far):
    width = layer_input.shape[2]
    block = 256
    cols = 3 * TILE
    whole = lambda rows, n: pl.BlockSpec((rows, n), lambda i, m: (0, 0))
    here = lambda n: pl.BlockSpec((block, n), lambda i, m: (i, 0))
    return pl.pallas_call(
        qkv_kernel,
        grid_spec=pltpu.PrefetchScalarGridSpec(
            num_scalar_prefetch=1,
            grid=(SEQ // block,),
            in_specs=[pl.BlockSpec((1, block, width), lambda i, m: (m[0], i, 0)), whole(1, width)] + [whole(width, cols)] * 4,
            out_specs=[here(3 * cols), here(width), whole(width, 3 * cols), whole(width, cols)],
        ),
        out_shape=[
            jax.ShapeDtypeStruct((SEQ, 3 * cols), BF),
            jax.ShapeDtypeStruct((SEQ, width), BF),
            jax.ShapeDtypeStruct((width, 3 * cols), BF),
            jax.ShapeDtypeStruct((width, cols), BF),
        ],
        compiler_params=pltpu.CompilerParams(vmem_limit_bytes=40 * MIB),
        cost_estimate=SMALL_COST,
        name="norm_and_project",
    )(micro, layer_input, gain, a_own, a_far, b_own, b_far)


def middle_kernel(
    blocks, per, micro_ref, tokens_ref, mixed_ref, other_ref, own_ref, far_ref, gain_ref, code_ref, residual_ref, *refs
):
    sent_refs, normed = refs[:-1], refs[-1]
    step = pl.program_id(0)
    rows = tokens_ref.shape[1]

    @pl.when(step < blocks)
    def _():
        total = tokens_ref[0].astype(F32) + dot(mixed_ref[...], own_ref[...], NT) + dot(other_ref[...], far_ref[...], NT)
        residual_ref[...] = total
        inverse = lax.rsqrt(jnp.mean(total * total, axis=-1, keepdims=True) + 1e-06)
        normed[pl.ds(pl.multiple_of(step * rows, rows), rows), :] = (total * inverse * gain_ref[...]).astype(BF)

    for c, sent_ref in enumerate(sent_refs):

        @pl.when((step >= blocks + c * per) & (step < blocks + (c + 1) * per))
        def _(sent_ref=sent_ref):
            block = sent_ref.shape[0]
            ids = lax.broadcasted_iota(jnp.int32, (block, 1), 0) + (step - blocks) * block
            hot = jnp.where((ids == code_ref[:1]) | (ids == code_ref[1:2]), 1.0, 0.0).astype(BF)
            sent_ref[...] = dot(hot, normed[...]).astype(BF)


def residual_and_rows(micro, layer_input, mixed, other, output_own, output_far, gain, code, count, chunks):
    width = layer_input.shape[2]
    block = 256
    blocks = SEQ // block
    send = 320
    cols = mixed.shape[1]
    per = count // send
    at = lambda i: jnp.minimum(i, blocks - 1)
    whole = lambda arr: pl.BlockSpec(arr.shape, lambda i, m: (0, 0))
    here = lambda n: pl.BlockSpec((block, n), lambda i, m: (at(i), 0))

    def sent(c):
        return pl.BlockSpec((send, width), lambda i, m: (jnp.clip(i - blocks - c * per, 0, per - 1), 0))

    return pl.pallas_call(
        functools.partial(middle_kernel, blocks, per),
        grid_spec=pltpu.PrefetchScalarGridSpec(
            num_scalar_prefetch=1,
            grid=(blocks + chunks * per,),
            in_specs=[
                pl.BlockSpec((1, block, width), lambda i, m: (m[0], at(i), 0)),
                here(cols), here(cols), whole(output_own), whole(output_far), whole(gain), whole(code),
            ],
            out_specs=[here(width)] + [sent(c) for c in range(chunks)],
            scratch_shapes=[pltpu.VMEM((SEQ, width), BF)],
        ),
        out_shape=[jax.ShapeDtypeStruct((SEQ, width), F32)] + [jax.ShapeDtypeStruct((count, width), BF)] * chunks,
        compiler_params=pltpu.CompilerParams(vmem_limit_bytes=40 * MIB),
        cost_estimate=SMALL_COST,
        name="residual_and_rows",
    )(micro, layer_input, mixed, other, output_own, output_far, gain, code)


def picked_rows(first, second, segments):
    total = None
    start = 0
    for rows in segments:
        length = rows.shape[0]
        ids = lax.broadcasted_iota(jnp.int32, (1, length), 1) + start
        hot = []
        for at in range(0, first.shape[0], STRIP):
            one, two = first[at : at + STRIP], second[at : at + STRIP]
            hot.append(jnp.where((one == ids) | (two == ids), 1.0, 0.0).astype(BF))
        total = put(total, dot(jnp.concatenate(hot, 0), rows))
        start += length
    return total


def put(a, b):
    return b if a is None else a + b


def folded(product):
    return jnp.sum(product.reshape(product.shape[0] // 8, 8, product.shape[1]), axis=0)


def as_column(eight):
    ones = jnp.ones((16, TILE), BF)
    high = eight.astype(BF)
    rest = (eight - high.astype(F32)).astype(BF)
    return dot(jnp.concatenate([high, rest], 0), ones, TN)


def combine_kernel(experts, half, spare, micro_ref, core_ref, length_ref, *refs):
    info_ref, grad_ref, residual_ref, mixed_ref, gain_ref, router_ref, output_ref = refs[:7]
    backs = refs[7:-9]
    (total_ref, mixed_grad_ref, extra_ref, far_ref, own_ref, acc_ref, router_acc, gain_acc, tables) = refs[-9:]
    block = residual_ref.shape[0]
    step = pl.program_id(0)
    count = len(backs) // 2

    @pl.when(step == 0)
    def _():
        place = lax.broadcasted_iota(jnp.int32, (experts, 1), 0)
        for n, back in enumerate((backs[count - 1], backs[2 * count - 1])):
            table = jnp.zeros((experts, back.shape[2]), F32)
            for e in range(experts):
                row = back[e, spare : spare + 16, :].astype(F32)[:1]
                table = jnp.where(place == e, row, table)
            for piece in range(3):
                at = (3 * n + piece) * experts
                tables[at : at + experts] = table[:, piece * half : (piece + 1) * half]

    info = jnp.transpose(info_ref[...])
    number = lambda n: info[:, n : n + 1]
    columns = lax.broadcasted_iota(jnp.int32, (1, half), 1)
    lanes = lax.broadcasted_iota(jnp.int32, (1, 6 * experts), 1)
    table = tables[...].astype(BF)
    values = []
    for k in range(2):
        slot = number(4 + k)
        hot = jnp.where(columns == lax.rem(slot, half), 1.0, 0.0).astype(BF)
        found = dot(hot, table, NT)
        wanted = jnp.where(slot // half == core_ref[0], 0, 3 * experts) + number(2 + k)
        away = lanes - wanted
        hit = (away == 0) | (away == experts) | (away == 2 * experts)
        values.append(jnp.sum(jnp.where(hit, found, 0.0), axis=1, keepdims=True))
    wide = lax.broadcasted_iota(jnp.int32, (1, TILE), 1)
    is_first, is_second = wide == number(2), wide == number(3)
    residual = residual_ref[...]
    gain = gain_ref[...]
    inverse = lax.rsqrt(jnp.mean(residual * residual, axis=-1, keepdims=True) + 1e-06)
    plain = residual * inverse
    normed = (plain * gain).astype(BF)
    logits = dot(normed, router_ref[...])
    gap = jnp.sum(jnp.where(is_first, logits, 0.0) - jnp.where(is_second, logits, 0.0), axis=1, keepdims=True)
    small = jnp.exp(-jnp.abs(gap))
    logit = small / ((1.0 + small) * (1.0 + small)) * (values[0] - values[1])
    logit_grad = jnp.where(is_first, logit, jnp.where(is_second, -logit, 0.0)).astype(BF)
    segments = [b[...].reshape(b.shape[0] * b.shape[1], b.shape[2]) for b in backs]
    normed_grad = picked_rows(number(0), number(1), segments) + dot(logit_grad, router_ref[...], NT)
    scaled = normed_grad * gain
    mean = jnp.mean(scaled * plain, axis=-1, keepdims=True)
    place = lax.broadcasted_iota(jnp.int32, (block, 1), 0) + step * block
    grad_out = jnp.where(place < length_ref[0], grad_ref[0].astype(F32), 0.0)
    total = grad_out + inverse * (scaled - plain * mean)

    @pl.when(step == core_ref[0])
    def _():
        total_ref[...] = total

    branch = total.astype(BF)
    mixed_grad_ref[...] = dot(branch, output_ref[...]).astype(BF)
    router_part = dot(logit_grad, normed, TN)
    gain_part = folded(normed_grad * plain)
    output_part = dot(mixed_ref[...], branch, TN)

    @pl.when(step == 0)
    def _():
        router_acc[...] = router_part
        gain_acc[...] = gain_part
        acc_ref[...] = output_part

    @pl.when(step > 0)
    def _():
        router_acc[...] += router_part
        gain_acc[...] += gain_part
        acc_ref[...] += output_part

    @pl.when(step == pl.num_programs(0) - 1)
    def _():
        extra_ref[...] = jnp.transpose(router_acc[...]) + jnp.where(wide == experts + 1, as_column(gain_acc[...]), 0.0)
        parts = jnp.transpose(acc_ref[...])
        far_ref[...] = parts[:, TILE:].astype(BF)
        own_ref[:, :TILE] = parts[:, :TILE]
        own_ref[:, TILE:] = parts[:, 2 * TILE :]


def combine(micro, core, length, info, out_grad, residual, mixed, gain, router, output_own, backs, half, spare):
    width = residual.shape[1]
    block = 512
    cols = mixed.shape[1]
    whole = lambda arr: pl.BlockSpec(arr.shape, lambda i, *_: (0,) * arr.ndim)
    fixed = lambda rows, n: pl.BlockSpec((rows, n), lambda i, *_: (0, 0))
    here = lambda n: pl.BlockSpec((block, n), lambda i, *_: (i, 0))
    experts = backs[0].shape[0]
    return pl.pallas_call(
        functools.partial(combine_kernel, experts, half, spare),
        grid_spec=pltpu.PrefetchScalarGridSpec(
            num_scalar_prefetch=3,
            grid=(SEQ // block,),
            in_specs=[
                pl.BlockSpec((8, block), lambda i, *_: (0, i)),
                pl.BlockSpec((1, block, width), lambda i, m, *_: (m[0], i, 0)),
                here(width), here(cols), whole(gain), whole(router), whole(output_own),
            ]
            + [whole(x) for x in backs],
            out_specs=[fixed(block, width), here(cols), fixed(width, TILE), fixed(width, 2 * TILE), fixed(width, 2 * TILE)],
            scratch_shapes=[
                pltpu.VMEM((cols, width), F32),
                pltpu.VMEM((TILE, width), F32),
                pltpu.VMEM((8, width), F32),
                pltpu.VMEM((6 * experts, half), F32),
            ],
        ),
        out_shape=[
            jax.ShapeDtypeStruct((block, width), F32),
            jax.ShapeDtypeStruct((SEQ, cols), BF),
            jax.ShapeDtypeStruct((width, TILE), F32),
            jax.ShapeDtypeStruct((width, 2 * TILE), BF),
            jax.ShapeDtypeStruct((width, 2 * TILE), F32),
        ],
        compiler_params=pltpu.CompilerParams(vmem_limit_bytes=60 * MIB),
        cost_estimate=SMALL_COST,
        name="combine",
    )(micro, core, length, info, out_grad, residual, mixed, gain, router, output_own, *backs)


def both_kernel(
    lane, micro_ref, core_ref, length_ref, part_ref, got_ref, tokens_ref, gain_ref, grad_ref,
    info_ref, residual_ref, own_ref, far_ref, out_ref, extra_ref, acc_ref,
):
    block = residual_ref.shape[0]
    info = jnp.transpose(info_ref[...])
    place = lax.broadcasted_iota(jnp.int32, (block, 1), 0) + (core_ref[0] * 2 + pl.program_id(0)) * block
    rows = residual_ref[...] + picked_rows(info[:, 6:7], info[:, 7:8], (own_ref[...], far_ref[...]))
    out_ref[0] = jnp.where(place < length_ref[0], rows, 0.0).astype(BF)
    normed_grad = got_ref[...] + part_ref[...]
    x = tokens_ref[0].astype(F32)
    inverse = lax.rsqrt(jnp.mean(x * x, axis=-1, keepdims=True) + 1e-06)
    plain = x * inverse
    scaled = normed_grad * gain_ref[...]
    mean = jnp.mean(scaled * plain, axis=-1, keepdims=True)
    out_ref[1] = (grad_ref[...] + inverse * (scaled - plain * mean)).astype(BF)
    wide = lax.broadcasted_iota(jnp.int32, (1, TILE), 1)
    part = folded(normed_grad * plain)

    @pl.when(pl.program_id(0) == 0)
    def _():
        acc_ref[...] = part

    @pl.when(pl.program_id(0) == 1)
    def _():
        extra_ref[...] = jnp.where(wide == lane, as_column(acc_ref[...] + part), 0.0)


def both_rows(lane, micro, core, length, part, got, layer_input, gain, residual_grad, info, residual, own, far):
    width = part.shape[1]
    plain = pl.BlockSpec((256, width), lambda i, *_: (i, 0))
    block = 256
    here = lambda n: pl.BlockSpec((block, n), lambda i, m, c, *_: (c[0] * 2 + i, 0))
    whole = lambda arr: pl.BlockSpec(arr.shape, lambda i, *_: (0, 0))
    return pl.pallas_call(
        functools.partial(both_kernel, lane),
        grid_spec=pltpu.PrefetchScalarGridSpec(
            num_scalar_prefetch=3,
            grid=(2,),
            in_specs=[
                plain,
                plain,
                pl.BlockSpec((1, block, width), lambda i, m, c, *_: (m[0], c[0] * 2 + i, 0)),
                whole(gain),
                plain,
                pl.BlockSpec((8, block), lambda i, m, c, *_: (0, c[0] * 2 + i)),
                here(width),
                whole(own),
                whole(far),
            ],
            out_specs=[
                pl.BlockSpec((2, block, width), lambda i, *_: (0, i, 0)),
                pl.BlockSpec((width, TILE), lambda i, *_: (0, 0)),
            ],
            scratch_shapes=[pltpu.VMEM((8, width), F32)],
        ),
        out_shape=[jax.ShapeDtypeStruct((2, 2 * block, width), BF), jax.ShapeDtypeStruct((width, TILE), F32)],
        compiler_params=pltpu.CompilerParams(vmem_limit_bytes=40 * MIB),
        cost_estimate=SMALL_COST,
        name="both_rows",
    )(micro, core, length, part, got, layer_input, gain, residual_grad, info, residual, own, far)


def sum_kernel(kept, own, got, out_own, early, late, late_far, table, sum_ref):
    low = low_lanes(early.shape)
    sum_ref[:, : 4 * TILE] = (own[:, : 4 * TILE] + got[:, : 4 * TILE].astype(F32)).astype(BF)
    mixed = jnp.where(low, own[:, 4 * TILE :], turned(out_own[:, TILE:]))
    sum_ref[:, 4 * TILE : 5 * TILE] = (mixed + got[:, 4 * TILE : 5 * TILE].astype(F32)).astype(BF)
    sum_ref[:, 5 * TILE : 6 * TILE] = (out_own[:, :TILE] + got[:, 5 * TILE :].astype(F32)).astype(BF)
    extra = early[...] + late[...] + late_far[...] + table[...]
    high = extra.astype(BF)
    rest = extra - high.astype(F32)
    if kept <= HEAD_DIM:
        sum_ref[:, 6 * TILE :] = jnp.where(low, high.astype(F32), turned(rest)).astype(BF)
    else:
        sum_ref[:, 6 * TILE : 7 * TILE] = high
        sum_ref[:, 7 * TILE :] = rest.astype(BF)


def packed_sums(kept, *parts):
    width = parts[0].shape[0]
    cols = (7 if kept <= HEAD_DIM else 8) * TILE
    block = 256
    here = lambda n: pl.BlockSpec((block, n), lambda i: (i, 0))
    return pl.pallas_call(
        functools.partial(sum_kernel, kept),
        grid=(width // block,),
        in_specs=[here(x.shape[1]) for x in parts],
        out_specs=here(cols),
        out_shape=jax.ShapeDtypeStruct((width, cols), BF),
        compiler_params=pltpu.CompilerParams(vmem_limit_bytes=40 * MIB),
        cost_estimate=SMALL_COST,
        name="packed_sums",
    )(*parts)


def final_kernel(kept, parts_ref, q_ref, k_ref, v_ref, o_ref, small_ref):
    total = parts_ref[0].astype(F32)
    for n in range(1, parts_ref.shape[0]):
        total = total + parts_ref[n].astype(F32)
    tile = lambda t: total[:, t * TILE : (t + 1) * TILE]
    q_ref[:, :TILE] = tile(0)
    q_ref[:, TILE:] = tile(3)[:, :HEAD_DIM]
    k_ref[:, :TILE] = tile(1)
    k_ref[:, TILE:] = turned(tile(3))[:, :HEAD_DIM]
    v_ref[:, :TILE] = tile(2)
    v_ref[:, TILE:] = tile(4)[:, :HEAD_DIM]
    o_ref[:, :TILE] = tile(5)
    o_ref[:, TILE:] = turned(tile(4))[:, :HEAD_DIM]
    small_ref[...] = tile(6) + (turned(tile(6)) if kept <= HEAD_DIM else tile(7))


def final_sums(kept, parts, shard):
    rows = parts.shape[1]
    return pl.pallas_call(
        functools.partial(final_kernel, kept),
        out_shape=[jax.ShapeDtypeStruct((rows, shard), F32)] * 4 + [jax.ShapeDtypeStruct((rows, TILE), F32)],
        compiler_params=pltpu.CompilerParams(vmem_limit_bytes=40 * MIB),
        cost_estimate=SMALL_COST,
        name="final_sums",
    )(parts)


def pair_gate(logits, own, other):
    lanes = lax.broadcasted_iota(jnp.int32, logits.shape, 1)
    gap = jnp.sum(
        jnp.where(lanes == own, logits, 0.0) - jnp.where(lanes == other, logits, 0.0), axis=1, keepdims=True
    )
    small = jnp.exp(-jnp.abs(gap))
    return jnp.where(gap >= 0.0, 1.0, small) / (1.0 + small)


def expert_kernel(lead, chunk, half, me_ref, partner_ref, rows_ref, grads_ref, router_ref, *refs):
    before, refs = (refs[0], refs[1:]) if lead is not None and lead > 0 else (None, refs)
    firsts, seconds = refs[:4], refs[4:8]
    back_ref, active_ref, slope_ref, gated_ref, gate_ref, mass_ref = refs[8:]
    rows = rows_ref[...]
    grads = grads_ref[...]
    gate = pair_gate(dot(rows, router_ref[...]), me_ref[0], partner_ref[...])
    gated_ref[...] = (gate * grads.astype(F32)).astype(BF)
    gate_ref[...] = jnp.broadcast_to(gate, gate_ref.shape)
    masses = [None] * (rows.shape[0] // STRIP)
    back = None
    width = firsts[0].shape[1]
    step = 256
    places = [(r, c) for r in range(4) for c in range(0, width, step)]

    def products(r, c):
        return dot(rows, firsts[r][:, c : c + step]), dot(grads, seconds[r][c : c + step, :], NT)

    ahead = products(*places[0])
    for n, (r, c) in enumerate(places):
        x, plain = ahead
        if n + 1 < len(places):
            ahead = products(*places[n + 1])
        place = slice(r * width + c, r * width + c + step)
        for at in range(0, rows.shape[0], STRIP):
            strip = slice(at, at + STRIP)
            value, flow = x[strip], plain[strip]
            square = value * value
            bent = jnp.tanh(value * (GELU_C + (GELU_C * GELU_A) * square))
            rise = 0.5 + 0.5 * bent
            active = value * rise
            slope = rise + active * (1.0 - bent) * (GELU_C + (3.0 * GELU_C * GELU_A) * square)
            low = active.astype(BF)
            active_ref[strip, place] = low
            slope_ref[strip, place] = (gate[strip] * flow * slope).astype(BF)
            part = low.astype(F32) * flow
            masses[at // STRIP] = put(masses[at // STRIP], part[:, :TILE] + part[:, TILE:])
        if c + step == width and r > 0:
            back = put(back, dot(slope_ref[:, (r - 1) * width : r * width], firsts[r - 1][...], NT))
    back = put(back, dot(slope_ref[:, 3 * width :], firsts[3][...], NT))
    back = back.astype(BF)
    mass = jnp.sum(jnp.concatenate(masses, 0), axis=1, keepdims=True)
    if lead is None:
        back_ref[...] = back
        mass_ref[...] = jnp.broadcast_to(mass, mass_ref.shape)
        return
    count = rows.shape[0] // chunk
    number = lax.broadcasted_iota(jnp.int32, (rows.shape[0], 1), 0)
    lanes = lax.broadcasted_iota(jnp.int32, (1, rows.shape[1]), 1)
    inside = lax.rem(number, chunk)
    spread = jnp.zeros(rows.shape, F32)
    for piece in range(3):
        high = mass.astype(BF).astype(F32)
        spread = jnp.where(lanes == piece * half + lead + inside, high, spread)
        mass = mass - high
    own = jnp.where(number // chunk == lax.broadcasted_iota(jnp.int32, (1, TILE), 1), 1.0, 0.0).astype(BF)
    line = dot(own, spread.astype(BF), TN)
    if before is None:
        back_ref[...] = back
        for e in range(count):
            mass_ref[e] = line[e : e + 1].astype(BF)
    else:
        back_ref[:, :chunk] = back.reshape(count, chunk, back.shape[1])
        row = lax.broadcasted_iota(jnp.int32, (16, 1), 0)
        for e in range(count):
            both = line[e : e + 1] + before[e].astype(F32)
            back_ref[e, chunk:] = jnp.where(row == 0, both, 0.0).astype(BF)


def row_block(total):
    return 320 if total % 320 == 0 else total


def expert_rows_pass(lead, chunk, half, me, partner, rows, grads, router, before, firsts, seconds):
    total, width = rows.shape
    block = row_block(total)
    experts = total // chunk
    hidden = sum(f.shape[1] for f in firsts)
    here = lambda cols: pl.BlockSpec((block, cols), lambda i: (i, 0))
    whole = lambda arr: pl.BlockSpec(arr.shape, lambda i: (0, 0))
    lines = pl.BlockSpec((block // chunk, 1, width), lambda i: (i, 0, 0))
    back_shape, back_spec = (total, width), here(width)
    mass_shape, mass_spec, mass_kind = (experts, 1, width), lines, BF
    if lead is None:
        mass_shape, mass_spec, mass_kind = (total, TILE), here(TILE), F32
    elif before is not None:
        back_shape = (experts, chunk + 16, width)
        back_spec = pl.BlockSpec((block // chunk, chunk + 16, width), lambda i: (i, 0, 0))
    return pl.pallas_call(
        functools.partial(expert_kernel, lead, chunk, half),
        grid=(total // block,),
        in_specs=[pl.BlockSpec(memory_space=pltpu.SMEM), here(1), here(width), here(width), whole(router)]
        + ([lines] if before is not None else [])
        + [whole(w) for w in firsts]
        + [whole(w) for w in seconds],
        out_specs=[back_spec, here(hidden), here(hidden), here(width), here(TILE), mass_spec],
        out_shape=[
            jax.ShapeDtypeStruct(back_shape, BF),
            jax.ShapeDtypeStruct((total, hidden), BF),
            jax.ShapeDtypeStruct((total, hidden), BF),
            jax.ShapeDtypeStruct((total, width), BF),
            jax.ShapeDtypeStruct((total, TILE), F32),
            jax.ShapeDtypeStruct(mass_shape, mass_kind),
        ],
        compiler_params=pltpu.CompilerParams(vmem_limit_bytes=56 * MIB),
        cost_estimate=SMALL_COST,
        name="expert_rows",
    )(me, partner, rows, grads, router, *([before] if before is not None else []), *firsts, *seconds)


def weight_parts(count, refs):
    rows, slopes, active, gated = (refs[n * count : (n + 1) * count] for n in range(4))
    first, second = None, None
    for n in range(count):
        first = put(first, dot(rows[n][...], slopes[n][...], TN))
        second = put(second, dot(active[n][...], gated[n][...], TN))
    return first, second


def cross_kernel(count, *refs):
    first, second = weight_parts(count, refs)
    refs[-1][0, 0] = first.astype(BF)
    refs[-1][0, 1] = second.astype(BF)


def kept_kernel(count, *refs):
    got_ref, far_ref, kept_ref = refs[-3:]
    first, second = weight_parts(count, refs)
    first = first + got_ref[0, 0].astype(F32)
    second = second + got_ref[0, 1].astype(F32)

    @pl.when(pl.program_id(0) == 0)
    def _():
        far_ref[0] = first.astype(BF)
        far_ref[1] = second.astype(BF)

    @pl.when(pl.program_id(0) == 1)
    def _():
        kept_ref[0] = first
        kept_ref[1] = second


def weight_specs(rows, slopes, quarter):
    total, width = rows[0].shape
    hidden = slopes[0].shape[1] // 4
    whole = pl.BlockSpec((total, width), lambda i: (0, 0))
    part = pl.BlockSpec((total, hidden), lambda i: (0, quarter(i)))
    count = len(rows)
    return width, hidden, [whole] * count + [part] * (2 * count) + [whole] * count


def cross_weight_grads(rows, slopes, active, gated):
    width, hidden, specs = weight_specs(rows, slopes, lambda i: 2 + i)
    return pl.pallas_call(
        functools.partial(cross_kernel, len(rows)),
        grid=(2,),
        in_specs=specs,
        out_specs=pl.BlockSpec((1, 2, width, hidden), lambda i: (i, 0, 0, 0)),
        out_shape=jax.ShapeDtypeStruct((2, 2, width, hidden), BF),
        compiler_params=pltpu.CompilerParams(vmem_limit_bytes=56 * MIB),
        cost_estimate=SMALL_COST,
        name="cross_weight_grads",
    )(*rows, *slopes, *active, *gated)


def kept_weight_grads(rows, slopes, active, gated, got):
    width, hidden, specs = weight_specs(rows, slopes, lambda i: 1 - i)
    fixed = pl.BlockSpec((2, width, hidden), lambda i: (0, 0, 0))
    return pl.pallas_call(
        functools.partial(kept_kernel, len(rows)),
        grid=(2,),
        in_specs=specs + [pl.BlockSpec((1, 2, width, hidden), lambda i: (1 - i, 0, 0, 0))],
        out_specs=[fixed, fixed],
        out_shape=[
            jax.ShapeDtypeStruct((2, width, hidden), BF),
            jax.ShapeDtypeStruct((2, width, hidden), F32),
        ],
        compiler_params=pltpu.CompilerParams(vmem_limit_bytes=56 * MIB),
        cost_estimate=SMALL_COST,
        name="kept_weight_grads",
    )(*rows, *slopes, *active, *gated, got)


def result_kernel(chunks, *refs):
    active, gates, seconds, out_ref = refs[:chunks], refs[chunks : 2 * chunks], refs[2 * chunks : -1], refs[-1]
    for c in range(chunks):

        @pl.when(pl.program_id(0) == c)
        def _(c=c):
            width = seconds[0].shape[0]
            total = None
            for r, second in enumerate(seconds):
                total = put(total, dot(active[c][:, r * width : (r + 1) * width], second[...]))
            rows = (total * gates[c][:, :1]).astype(BF)
            if chunks > 1:
                out_ref[:, 0] = rows.reshape(out_ref.shape[0], out_ref.shape[2], out_ref.shape[3])
            else:
                out_ref[...] = rows


def expert_results(active, gates, seconds, experts):
    chunks = len(active)
    total, hidden = active[0].shape
    width = seconds[0].shape[1]
    block = row_block(total)
    steps = total // block

    def here(c, cols):
        return pl.BlockSpec((block, cols), lambda g, i: (jnp.where(g == c, i, jnp.where(g < c, 0, steps - 1)), 0))

    chunk = total // experts
    if chunks > 1:
        shape = (experts, chunks, chunk, width)
        out_spec = pl.BlockSpec((block // chunk, 1, chunk, width), lambda g, i: (i, g, 0, 0))
    else:
        shape = (total, width)
        out_spec = pl.BlockSpec((block, width), lambda g, i: (i, 0))
    out = pl.pallas_call(
        functools.partial(result_kernel, chunks),
        grid=(chunks, steps),
        in_specs=[here(c, hidden) for c in range(chunks)]
        + [here(c, TILE) for c in range(chunks)]
        + [pl.BlockSpec(w.shape, lambda g, i: (0, 0)) for w in seconds],
        out_specs=out_spec,
        out_shape=jax.ShapeDtypeStruct(shape, BF),
        compiler_params=pltpu.CompilerParams(vmem_limit_bytes=56 * MIB),
        cost_estimate=SMALL_COST,
        name="expert_results",
    )(*active, *gates, *seconds)
    return out.reshape(experts, chunks * chunk, width)


def last_sum_kernel(kept_ref, y_ref, out_first, out_second):
    for n, out in enumerate((out_first, out_second)):
        out[...] = kept_ref[n] + y_ref[n].astype(F32)


def last_sums(kept, got_y):
    _, width, hidden = kept.shape
    block = 256
    here = pl.BlockSpec((block, hidden), lambda i: (i, 0))
    part = pl.BlockSpec((2, block, hidden), lambda i: (0, i, 0))
    return pl.pallas_call(
        last_sum_kernel,
        grid=(width // block,),
        in_specs=[part, part],
        out_specs=[here, here],
        out_shape=[jax.ShapeDtypeStruct((width, hidden), F32)] * 2,
        compiler_params=pltpu.CompilerParams(vmem_limit_bytes=40 * MIB),
        cost_estimate=SMALL_COST,
        name="last_sums",
    )(kept, got_y)


def send_kernel(micro_ref, code_ref, rows_ref, out_ref):
    block = out_ref.shape[0]
    ids = lax.broadcasted_iota(jnp.int32, (block, 1), 0) + pl.program_id(0) * block
    hot = jnp.where((ids == code_ref[:1]) | (ids == code_ref[1:2]), 1.0, 0.0).astype(BF)
    out_ref[...] = dot(hot, rows_ref[0]).astype(BF)


def send_rows(micro, code, rows, count):
    width = rows.shape[2]
    block = next(b for b in (336, 320, 384, count) if count % b == 0)
    return pl.pallas_call(
        send_kernel,
        grid_spec=pltpu.PrefetchScalarGridSpec(
            num_scalar_prefetch=1,
            grid=(count // block,),
            in_specs=[
                pl.BlockSpec(code.shape, lambda i, m: (0, 0)),
                pl.BlockSpec((1, SEQ, width), lambda i, m: (m[0], 0, 0)),
            ],
            out_specs=pl.BlockSpec((block, width), lambda i, m: (i, 0)),
        ),
        out_shape=jax.ShapeDtypeStruct((count, width), BF),
        compiler_params=pltpu.CompilerParams(vmem_limit_bytes=40 * MIB),
        cost_estimate=SMALL_COST,
        name="send_rows",
    )(micro, code, rows)


def place_kernel(place_ref, one_ref, two_ref, *refs):
    for n, piece in enumerate((one_ref, two_ref)):

        @pl.when(pl.program_id(0) == n)
        def _(piece=piece):
            for k, out_ref in enumerate(refs[-2:]):
                out_ref[0] = piece[k]


def place_pieces(places, pieces, before=()):
    two, rows, width = pieces[0].shape
    whole = pl.BlockSpec(pieces[0].shape, lambda i, place_ref: (0, 0, 0))
    return pl.pallas_call(
        place_kernel,
        grid_spec=pltpu.PrefetchScalarGridSpec(
            num_scalar_prefetch=1,
            grid=(2,),
            in_specs=[whole] * 2 + [pl.BlockSpec(memory_space=pl.ANY)] * len(before),
            out_specs=[pl.BlockSpec((1, rows, width), lambda i, place_ref: (place_ref[i], 0, 0))] * two,
        ),
        out_shape=[jax.ShapeDtypeStruct((4, rows, width), pieces[0].dtype)] * two,
        input_output_aliases={3: 0, 4: 1} if before else {},
        compiler_params=pltpu.CompilerParams(vmem_limit_bytes=40 * MIB),
        cost_estimate=SMALL_COST,
        name="place_pieces",
    )(places, *pieces, *before)


def swap(value, axis, count, bit):
    return lax.ppermute(value, axis, [(i, i ^ bit) for i in range(count)])


def all_to_all(value):
    return lax.all_to_all(value, "dp", split_axis=0, concat_axis=0, tiled=True)


def together(*values):
    return lax.optimization_barrier(values)


def local(
    layer_input, out_grad, first_gain, query_weight, key_weight, value_weight, output_weight,
    position_bias, second_gain, router_weight, expert_in, expert_out, seq_lengths, routes,
):
    micro_count, tok_rows, width = layer_input.shape
    dp_count = lax.axis_size("dp")
    expert_count = router_weight.shape[1]
    shard = query_weight.shape[1]
    heads_here = position_bias.shape[0]
    assert lax.axis_size("tensor") == 4 and micro_count == 2 and expert_count == dp_count
    assert tok_rows == SEQ and seq_lengths.shape[1] == 1
    capacity = max(8, 8 * (10 * tok_rows // (32 * expert_count)))
    half = capacity // 2
    stride = 8 * (half // 8 + 1)
    by_lines = dp_count == 8
    chunks = 2 if half % 32 == 0 else 1
    chunk = half // chunks
    chunk_rows = expert_count * chunk
    rows_here = query_weight.shape[0]
    me = lax.axis_index("dp")
    rank = lax.axis_index("tensor")
    micro = rank // 2
    core = rank % 2

    def swap_y(value):
        return swap(value, "tensor", 4, 2)

    def swap_core(value):
        return swap(value, "tensor", 4, 1)

    micro_arg = micro.reshape(1).astype(jnp.int32)
    core_arg = core.reshape(1).astype(jnp.int32)

    packed = pack_weights(query_weight, key_weight, value_weight, output_weight, first_gain, second_gain, router_weight)
    three = 3 * TILE

    def doubled(stacked, bit, axis=0):
        other = swap(stacked, "dp", dp_count, bit)
        high = (me & bit) != 0
        pair = jnp.where(high, jnp.stack([other, stacked], axis + 1), jnp.stack([stacked, other], axis + 1))
        return pair.reshape(stacked.shape[:axis] + (-1,) + stacked.shape[axis + 1 :])

    stacked = packed[None]
    bit = dp_count // 2
    while bit > 1:
        stacked = doubled(stacked, bit)
        bit //= 2
    length = lax.dynamic_index_in_dim(seq_lengths, micro, 0, keepdims=False)
    route = lax.dynamic_index_in_dim(routes, micro, 0, keepdims=False).T
    expert_ids = jnp.arange(expert_count, dtype=jnp.int32)
    named = (expert_ids[:, None, None] == route[None]).astype(jnp.int32)
    per_token = jnp.sum(named, axis=1, dtype=jnp.int32)
    earlier = jnp.cumsum(per_token, axis=1, dtype=jnp.int32) - per_token
    slot = jnp.sum(named * earlier[:, None, :], axis=0, dtype=jnp.int32)
    here = slot // half == core
    within = slot % half
    chunk_of = within // chunk
    inside = within % chunk
    spare = 16 * -(-chunk // 16)
    last_stride = spare + 16
    last = (chunks - 1) * chunk_rows
    code_back = jnp.where(
        chunk_of == chunks - 1, last + route * last_stride + inside, chunk_of * chunk_rows + route * chunk + inside
    )
    code_back = code_back + jnp.where(here, 0, last + expert_count * last_stride)
    code_result = route * half + within + jnp.where(here, 0, expert_count * half)
    info = jnp.concatenate([code_back, route, slot, code_result], 0)

    code_grads = jnp.where(here, route * stride + within, -1)
    valid = jnp.arange(SEQ, dtype=jnp.int32) < length[0]
    ids = jnp.arange(expert_count * stride, dtype=jnp.int32)[:, None]
    partner = jnp.sum(
        jnp.where(ids == code_grads[:1], route[1:], 0) + jnp.where(ids == code_grads[1:], route[:1], 0), axis=1, dtype=jnp.int32
    )
    grads_sent = send_rows(micro_arg, jnp.where(valid[None], code_grads, -1), out_grad, expert_count * stride)
    grads_sent = grads_sent.reshape(expert_count, stride, width)
    partner_row = jnp.pad(partner.reshape(expert_count, stride)[:, :half].astype(BF), ((0, 0), (0, width - half)))
    grads_sent = grads_sent.at[:, half].set(partner_row)
    stacked, grads_sent, position_bias = together(stacked, grads_sent, position_bias)
    if by_lines:
        lines = [list(range(x, dp_count, 2)) for x in range(2)]
        grads_z = lax.all_to_all(
            grads_sent.reshape(dp_count // 2, 2, stride, width), "dp", split_axis=0, concat_axis=0,
            axis_index_groups=lines, tiled=True,
        )

    first_own = expert_in[0]
    second_own = expert_out[0]
    part_b = stacked[:, :, :three]
    far_b = swap_y(part_b)
    part_a = doubled(stacked[:, :, three:], 1)
    part_a, far_b = together(part_a, far_b)
    pair_b = jnp.stack([part_b, far_b])
    a_own = part_a[:, :, :three]
    a_far = swap_y(a_own).reshape(width, three)
    a_own = a_own.reshape(width, three)
    pair_b = doubled(pair_b, 1, 1).reshape(2, width, three)
    if by_lines:
        a_far, pair_b, first_own = together(a_far, pair_b, first_own)
    else:
        a_far, pair_b, grads_sent, first_own = together(a_far, pair_b, grads_sent, first_own)
    first_y = swap_y(first_own)
    small_all = part_a[:, :, three:].reshape(width, TILE)
    gain_one = small_all[:, expert_count].astype(F32)[None]
    gain_two = small_all[:, expert_count + 1].astype(F32)[None]
    router_wide = small_all
    far_bias = swap_y(position_bias)
    bias = jnp.concatenate([position_bias[:2], far_bias[:2], position_bias[2:], far_bias[2:]], 0)
    head_total = bias.shape[0]
    hot_const = jnp.asarray(NEAR_HOT, dtype=BF)
    near = dot(bias, hot_const) - bias[:, NB - 1 :].astype(F32)
    near = near.reshape(head_total, 2, TILE, TILE)
    places = jnp.arange(TILE, dtype=jnp.int32)
    causal = jnp.stack([places[None, :] <= places[:, None], jnp.ones((TILE, TILE), bool)])
    near = jnp.where(causal[None], near, NEG)

    if by_lines:
        high = (me & 1) != 0
    else:
        grads_here = all_to_all(grads_sent)

    qkv, normed_one, qkv_weight, output_own = norm_and_project(
        micro_arg, layer_input, gain_one, a_own, a_far, pair_b[0], pair_b[1]
    )
    output_far = swap_core(output_own)
    mixed, logs = attend(length, qkv, near)
    mixed, output_far = together(mixed, output_far)
    mixed_far = swap_core(mixed)
    code_chunks = jnp.where(here, chunk_of * chunk_rows + route * chunk + inside, -1)
    if by_lines:
        sent_x = lax.dynamic_index_in_dim(grads_z, 1 - (me & 1), 1, keepdims=False)
        mixed_far, grads_z, sent_x = together(mixed_far, grads_z, sent_x)
        got_x = swap(sent_x, "dp", dp_count, 1)
    residual, *parts = residual_and_rows(
        micro_arg, layer_input, mixed, mixed_far, output_own, output_far, gain_two, code_chunks, chunk_rows, chunks
    )

    if by_lines:
        parts, first_y, second_own = together(parts, first_y, second_own)
        kept_x = jnp.where(high, grads_z[:, 1], grads_z[:, 0])
        pair_x = jnp.where(high, jnp.stack([got_x, kept_x], 1), jnp.stack([kept_x, got_x], 1))
        grads_here = pair_x.reshape(dp_count, stride, width)
    else:
        parts, grads_here, first_y, second_own = together(parts, grads_here, first_y, second_own)
    second_y = swap_y(second_own)
    parts = [part.reshape(expert_count, chunk, width) for part in parts]
    arrived = [all_to_all(parts[0])]
    partner_here = grads_here[:, half, :half].astype(jnp.int32)

    def chunk_grads(c):
        at = slice(c * chunk, (c + 1) * chunk)
        return grads_here[:, at].reshape(chunk_rows, width), partner_here[:, at].reshape(chunk_rows, 1)

    grads_parts = [chunk_grads(c) for c in range(chunks)]
    grads_parts, second_y = together(grads_parts, second_y)

    firsts = (first_own, first_y, swap_core(first_own), swap_core(first_y))
    seconds = (second_own, second_y, swap_core(second_own), swap_core(second_y))

    for c in range(1, chunks):
        sent, arrived[-1] = together(parts[c], arrived[-1])
        arrived.append(all_to_all(sent))

    me_arg = me.reshape(1).astype(jnp.int32)
    rows_all, slopes, active, gated, gates, backs = [], [], [], [], [], []
    line = None
    for c in range(chunks):
        grads_c, partner_c = grads_parts[c]
        rows_c = arrived[c].reshape(chunk_rows, width)
        back, act, slo, gat, gte, line = expert_rows_pass(
            c * chunk if chunks > 1 else None, chunk, half, me_arg, partner_c, rows_c, grads_c, router_wide, line, firsts, seconds
        )
        rows_all.append(rows_c)
        slopes.append(slo)
        active.append(act)
        gated.append(gat)
        gates.append(gte)
        if chunks == 1:
            gate_grad = line[:, 0].reshape(expert_count, chunk)
            pieces = []
            for _ in range(3):
                piece = gate_grad.astype(BF)
                pieces.append(piece)
                gate_grad = gate_grad - piece.astype(F32)
            gate_row = jnp.pad(jnp.concatenate(pieces, 1), ((0, 0), (0, width - 3 * half)))
            back = jnp.pad(back.reshape(expert_count, chunk, width), ((0, 0), (0, last_stride - chunk), (0, 0)))
            back = back.at[:, spare].set(gate_row)
        if c + 1 < chunks:
            back, arrived[c + 1] = together(back.reshape(expert_count, chunk, width), arrived[c + 1])
        else:
            back, rows_all[-1], backs = together(back, rows_all[-1], backs)
        backs.append(all_to_all(back))
    grads_cross = cross_weight_grads(rows_all, slopes, active, gated)
    gates, grads_cross = together(gates, grads_cross)
    grads_in = swap_core(grads_cross)
    results = expert_results(active, gates, seconds, expert_count)
    results, grads_in = together(results, grads_in)
    grads_far, grads_kept = kept_weight_grads(rows_all, slopes, active, gated, grads_in)
    backs[-1], results, grads_far = together(backs[-1], results, grads_far)

    across_y = swap_y(grads_far)
    results_own = all_to_all(results).reshape(expert_count * half, width)

    backs_far = [swap_core(b) for b in backs]
    residual_grad, mixed_grad, extra_early, output_sent, output_kept = combine(
        micro_arg, core_arg, length, info, out_grad, residual, mixed, gain_two, router_wide, output_own,
        backs + backs_far, half, spare,
    )

    tiles, sums, far_sent, own_parts, sent, kept_part = attend_back(
        core_arg, length, qkv, near, mixed, logs, mixed_grad, normed_one, output_sent, qkv_weight
    )
    far_got = swap_y(far_sent)
    sent, results_own = together(sent, results_own)
    got = swap_core(sent)
    rows_both, extra_late = both_rows(
        expert_count, micro_arg, core_arg, length, kept_part, got, layer_input, gain_one, residual_grad,
        info, residual, results_own, swap_core(results_own),
    )
    rows_both, across_y, tiles = together(rows_both, across_y, tiles)
    late_far = swap_core(extra_late)
    corner = micro * 2 + core
    corners = jnp.stack([corner, corner ^ 1, corner ^ 2, corner ^ 3]).astype(jnp.int32)
    rows_y = swap_y(rows_both)
    expert_in_grad, expert_out_grad = last_sums(grads_kept, across_y)
    placed = place_pieces(corners[:2], (rows_both, swap_core(rows_both)))
    rows_y, expert_in_grad, expert_out_grad, placed = together(rows_y, expert_in_grad, expert_out_grad, placed)
    placed = place_pieces(corners[2:], (rows_y, swap_core(rows_y)), placed)

    tiles = tiles.reshape(head_total, 2 * TILE * TILE)
    tiles_high = tiles.astype(BF)
    tiles_rest = (tiles - tiles_high.astype(F32)).astype(BF)
    table = dot(tiles_high, hot_const, NT) + dot(tiles_rest, hot_const, NT)
    far_sum = jnp.sum(sums[:, :, 0], axis=1) - jnp.sum(table[:, : NB - 1], axis=1)
    table = jnp.concatenate([table[:, : NB - 1], far_sum[:, None]], 1)
    table_own = jnp.concatenate([table[0:2], table[4:5]], 0)
    table_far = jnp.concatenate([table[2:4], table[5:6]], 0)
    table_cols = heads_here * NB // rows_here
    table_both = jnp.concatenate([table_own.reshape(rows_here, table_cols), table_far.reshape(rows_here, table_cols)], 1)
    base = expert_count + 2
    kept = base + 2 * table_cols
    table_tile = jnp.tile(jnp.pad(table_both, ((0, 0), (base, TILE - kept))), (dp_count, 1))

    grads = packed_sums(kept, own_parts, far_got, output_kept, extra_early, extra_late, late_far, table_tile)
    arrived_grads = all_to_all(grads.reshape(dp_count, rows_here, grads.shape[1]))
    layer_output, input_grad = (out.reshape(2, SEQ, width) for out in placed)
    arrived_grads, layer_output, input_grad = together(arrived_grads, layer_output, input_grad)
    query_grad, key_grad, value_grad, output_grad, small = final_sums(kept, arrived_grads, shard)
    small_y = swap_y(small)
    both = small + small_y
    table_sum = small[:, base : base + table_cols] + small_y[:, base + table_cols : kept]
    return (
        layer_output,
        input_grad,
        both[:, expert_count],
        query_grad,
        key_grad,
        value_grad,
        output_grad.T,
        table_sum.reshape(heads_here, NB),
        both[:, expert_count + 1],
        both[:, :expert_count],
        expert_in_grad[None],
        expert_out_grad[None],
    )


def solution(mesh):
    return jax.shard_map(
        local,
        mesh=mesh,
        in_specs=(
            P(None, "dp", None),
            P(None, "dp", None),
            P("dp"),
            P("dp", "tensor"),
            P("dp", "tensor"),
            P("dp", "tensor"),
            P("tensor", "dp"),
            P("tensor", None),
            P("dp"),
            P("dp", None),
            P("dp", None, "tensor"),
            P("dp", "tensor", None),
            P(None, "dp"),
            P(None, "dp", None),
        ),
        out_specs=(
            P(None, "dp", None),
            P(None, "dp", None),
            P("dp"),
            P("dp", "tensor"),
            P("dp", "tensor"),
            P("dp", "tensor"),
            P("tensor", "dp"),
            P("tensor", None),
            P("dp"),
            P("dp", None),
            P("dp", None, "tensor"),
            P("dp", "tensor", None),
        ),
        check_vma=False,
    )
```

```python
import functools

import jax
import jax.numpy as jnp
import numpy as np
from jax import lax
from jax.experimental import pallas as pl
from jax.experimental.pallas import tpu as pltpu
from jax.sharding import PartitionSpec as P

HEAD_DIM = 64
NB = 32
SEQ = 1024
TILE = 128
QROWS = 256
NEG = -1e30
GELU_C = 0.7978845608028654
GELU_A = 0.044715

BF = jnp.bfloat16
F32 = jnp.float32

bucket_edges = np.ceil(16.0 * 8.0 ** (np.arange(1, 16) / 16.0)).astype(np.int32)


def near_tables():
    rows = np.arange(TILE)[:, None]
    cols = np.arange(TILE)[None, :]
    hots = []
    for shift in (0, TILE):
        distance = rows - cols + shift
        clipped = np.maximum(distance, 0)
        reached = np.sum(clipped[..., None] >= bucket_edges, axis=-1)
        bucket = np.minimum(clipped, 16) + reached
        hots.append(bucket[..., None] == np.arange(NB))
    hot = np.stack(hots).reshape(2 * TILE * TILE, NB).T
    return hot


NEAR_HOT = near_tables()
assert bucket_edges[-1] <= TILE


def dot(a, b, dims=((1,), (0,))):
    return lax.dot_general(a, b, (dims, ((), ())), preferred_element_type=F32)


NT = ((1,), (1,))
TN = ((0,), (0,))


MIB = 2**20
SMALL_COST = pl.CostEstimate(flops=1_000_000, bytes_accessed=1_000_000, transcendentals=0)


STRIP = 32


def score_strip(s, at, block, j, start, near_ref, half, length):
    part = s[at : at + STRIP]
    near = slice(start % TILE, start % TILE + STRIP)
    if j == block:
        if start < TILE:
            left = part[:, :TILE] + near_ref[half, 0, near, :]
            right = jnp.full((STRIP, TILE), NEG, F32)
        else:
            left = part[:, :TILE] + near_ref[half, 1, near, :]
            right = part[:, TILE:] + near_ref[half, 0, near, :]
        part = jnp.concatenate([left, right], 1)
    elif j == block - 1 and start < TILE:
        part = jnp.concatenate([part[:, :TILE], part[:, TILE:] + near_ref[half, 1, near, :]], 1)
    if (j + 1) * QROWS > SEQ // 2:
        place = lax.broadcasted_iota(jnp.int32, (1, QROWS), 1) + j * QROWS
        part = part + jnp.where(place < length, 0.0, NEG)
    return part


def lane_half(rows):
    return lax.broadcasted_iota(jnp.int32, (rows, 2 * HEAD_DIM), 1) < HEAD_DIM


def attend_kernel(length_ref, query_ref, key_ref, value_ref, near_ref, out_ref, log_ref):
    length = length_ref[0]
    lanes = lane_half(QROWS)
    value_ext = jnp.concatenate([value_ref[...], jnp.ones((SEQ, TILE), BF)], 1)
    for i in range(SEQ // QROWS):
        q_rows = query_ref[i * QROWS : (i + 1) * QROWS, :] * BF(0.125)
        q_both = jnp.concatenate([jnp.where(lanes, q_rows, BF(0)), jnp.where(lanes, BF(0), q_rows)], 0)
        tiles = [dot(q_both, key_ref[j * QROWS : (j + 1) * QROWS, :], NT) for j in range(i + 1)]
        tops = []
        weights = [[] for _ in tiles]
        for h in range(2):
            for start in range(0, QROWS, STRIP):
                strips = [
                    score_strip(s, h * QROWS + start, i, j, start, near_ref, h, length) for j, s in enumerate(tiles)
                ]
                top = strips[0]
                for s in strips[1:]:
                    top = jnp.maximum(top, s)
                top = jnp.max(top, axis=1, keepdims=True)
                tops.append(top)
                for j, s in enumerate(strips):
                    weights[j].append(jnp.exp(s - top).astype(BF))
        total = None
        for j, strips in enumerate(weights):
            total = put(total, dot(jnp.concatenate(strips, 0), value_ext[j * QROWS : (j + 1) * QROWS, :]))
        row_sum = total[:, TILE:]
        out = total[:, :TILE] / row_sum
        logs = jnp.concatenate(tops, 0) + jnp.log(row_sum)
        out_ref[i * QROWS : (i + 1) * QROWS, :] = jnp.where(lanes, out[:QROWS], out[QROWS:]).astype(BF)
        log_ref[i * QROWS : (i + 1) * QROWS, :] = jnp.where(lanes, logs[:QROWS], logs[QROWS:])


def attend(length, qkv, near):
    pairs = qkv.shape[1] // (3 * TILE)
    cols = pairs * TILE
    return pl.pallas_call(
        attend_kernel,
        grid=(pairs,),
        in_specs=[
            pl.BlockSpec(memory_space=pltpu.SMEM),
            pl.BlockSpec((SEQ, TILE), lambda p: (0, p)),
            pl.BlockSpec((SEQ, TILE), lambda p: (0, pairs + p)),
            pl.BlockSpec((SEQ, TILE), lambda p: (0, 2 * pairs + p)),
            pl.BlockSpec((2, 2, TILE, TILE), lambda p: (p, 0, 0, 0)),
        ],
        out_specs=[
            pl.BlockSpec((SEQ, TILE), lambda p: (0, p)),
            pl.BlockSpec((SEQ, TILE), lambda p: (0, p)),
        ],
        out_shape=[
            jax.ShapeDtypeStruct((SEQ, cols), BF),
            jax.ShapeDtypeStruct((SEQ, cols), F32),
        ],
        compiler_params=pltpu.CompilerParams(vmem_limit_bytes=40 * MIB),
        cost_estimate=SMALL_COST,
        name="attend",
    )(length, qkv, qkv, qkv, near)


def attend_back_kernel(
    pairs, blocks, core_ref, length_ref, query_ref, key_ref, value_ref, near_ref, out_ref, log_ref, grad_ref,
    normed_ref, output_ref, output_own, weight_ref, tile_ref, sum_ref, far_ref, own_ref, cross_ref, sent_ref, kept_ref,
    grads, dk_acc, dv_acc,
):
    step = pl.program_id(0)

    @pl.when(step < pairs)
    def _():
        pair_grads(
            step, length_ref, query_ref, key_ref, value_ref, near_ref, out_ref, log_ref, grad_ref,
            tile_ref, sum_ref, grads, dk_acc, dv_acc,
        )

    @pl.when((step >= pairs) & (step < pairs + blocks))
    def _():
        low = low_lanes((normed_ref.shape[1], TILE))
        q, k, v = (
            dot(normed_ref[...], jnp.concatenate([grads[n, p] for p in range(pairs)], 1), TN) for n in range(3)
        )
        for n, part in enumerate((q, k, v)):
            own_ref[:, n * TILE : (n + 1) * TILE] = part[:, :TILE]
            far_ref[:, n * TILE : (n + 1) * TILE] = part[:, TILE : 2 * TILE].astype(BF)
        q, k, v = (part[:, 2 * TILE :] for part in (q, k, v))
        tiles = (
            jnp.where(low, q, turned(k)),
            jnp.where(low, v, turned(output_own[:, TILE:])),
            output_own[:, :TILE],
            jnp.where(low, turned(q), k),
            jnp.where(low, turned(v), output_ref[:, TILE:].astype(F32)),
            output_ref[:, :TILE],
        )
        for n, tile in enumerate(tiles):
            cross_ref[:, n * TILE : (n + 1) * TILE] = tile.astype(BF)

    for late, half_ref in enumerate((sent_ref, kept_ref)):
        first = pairs + blocks + 2 * late

        @pl.when((step >= first) & (step < first + 2))
        def _(half_ref=half_ref, first=first, late=late):
            rows = half_ref.shape[0]
            mine = core_ref[0] if late else 1 - core_ref[0]
            start = pl.multiple_of((2 * mine + step - first) * rows, rows)
            total = None
            for n in range(3):
                part = jnp.concatenate([grads[n, p, pl.ds(start, rows), :] for p in range(pairs)], 1)
                cols = part.shape[1]
                total = put(total, dot(part, weight_ref[:, n * cols : (n + 1) * cols], NT))
            half_ref[...] = total


def pair_grads(
    pair, length_ref, query_ref, key_ref, value_ref, near_ref, out_ref, log_ref, grad_ref, tile_ref, sum_ref, grads, dk_acc, dv_acc
):
    length = length_ref[0]
    lanes = lane_half(QROWS)
    key_ext = jnp.concatenate([key_ref[...], jnp.ones((SEQ, TILE), BF)], 1)
    near_sums = [[None, None], [None, None]]
    all_sums = [None, None]

    def both(rows):
        return jnp.concatenate([jnp.where(lanes, rows, BF(0)), jnp.where(lanes, BF(0), rows)], 0)

    for i in range(SEQ // QROWS):
        rows = slice(i * QROWS, (i + 1) * QROWS)
        q_both = both(query_ref[rows, :] * BF(0.125))
        g_rows = grad_ref[rows, :]
        g_both = both(g_rows)
        mass = g_rows.astype(F32) * out_ref[rows, :].astype(F32)
        deltas = [
            jnp.sum(jnp.where(lanes, mass, 0.0), axis=1, keepdims=True),
            jnp.sum(jnp.where(lanes, 0.0, mass), axis=1, keepdims=True),
        ]
        logs = [log_ref[rows, h * HEAD_DIM : h * HEAD_DIM + 1] for h in range(2)]
        dq = None
        for j in range(i + 1):
            keys = slice(j * QROWS, (j + 1) * QROWS)
            s = dot(q_both, key_ref[keys, :], NT)
            dp = dot(g_both, value_ref[keys, :], NT)
            p_strips, d_strips = [], []
            for h in range(2):
                for start in range(0, QROWS, STRIP):
                    strip = slice(start, start + STRIP)
                    at = h * QROWS + start
                    p = jnp.exp(score_strip(s, at, i, j, start, near_ref, h, length) - logs[h][strip])
                    p_strips.append(p.astype(BF))
                    d_strips.append((p * (dp[at : at + STRIP] - deltas[h][strip])).astype(BF))
            p, ds = jnp.concatenate(p_strips, 0), jnp.concatenate(d_strips, 0)
            part = dot(ds, key_ext[keys, :])
            dq = put(dq, jnp.where(lanes, part[:QROWS, :TILE], part[QROWS:, :TILE]))
            for h in range(2):
                sums = part[h * QROWS : (h + 1) * QROWS, TILE:]
                all_sums[h] = put(all_sums[h], jnp.sum(sums.reshape(QROWS // 8, 8, TILE), axis=0))
            dk_part = dot(ds, q_both, TN)
            dv_part = dot(p, g_both, TN)
            if i == j:
                dk_acc[keys, :] = dk_part
                dv_acc[keys, :] = dv_part
            else:
                dk_acc[keys, :] += dk_part
                dv_acc[keys, :] += dv_part
            for h in range(2):
                mine = ds[h * QROWS : (h + 1) * QROWS]
                if j == i:
                    wide = mine.astype(F32)
                    near_sums[h][0] = put(near_sums[h][0], wide[:TILE, :TILE] + wide[TILE:, TILE:])
                    near_sums[h][1] = put(near_sums[h][1], wide[TILE:, :TILE])
                elif j == i - 1:
                    near_sums[h][1] = put(near_sums[h][1], mine[:TILE, TILE:].astype(F32))
        grads[0, pair, rows, :] = (dq * 0.125).astype(BF)
    grads[1, pair] = dk_acc[...].astype(BF)
    grads[2, pair] = dv_acc[...].astype(BF)
    for h in range(2):
        tile_ref[h, 0] = near_sums[h][0]
        tile_ref[h, 1] = near_sums[h][1]
        sum_ref[h] = all_sums[h]


def attend_back(core, length, qkv, near, mixed, logs, grad, normed, output, output_own, weight):
    pairs = qkv.shape[1] // (3 * TILE)
    width = normed.shape[1]
    block = 256
    blocks = width // block
    at = lambda i: jnp.minimum(i, pairs - 1)
    then = lambda i: jnp.clip(i - pairs, 0, blocks - 1)
    return pl.pallas_call(
        functools.partial(attend_back_kernel, pairs, blocks),
        grid_spec=pltpu.PrefetchScalarGridSpec(
            num_scalar_prefetch=2,
            grid=(pairs + blocks + 4,),
            in_specs=[
                pl.BlockSpec((SEQ, TILE), lambda i, *_: (0, at(i))),
                pl.BlockSpec((SEQ, TILE), lambda i, *_: (0, pairs + at(i))),
                pl.BlockSpec((SEQ, TILE), lambda i, *_: (0, 2 * pairs + at(i))),
                pl.BlockSpec((2, 2, TILE, TILE), lambda i, *_: (at(i), 0, 0, 0)),
            ]
            + [pl.BlockSpec((SEQ, TILE), lambda i, *_: (0, at(i)))] * 3
            + [
                pl.BlockSpec((SEQ, block), lambda i, *_: (0, then(i))),
                pl.BlockSpec((block, 2 * TILE), lambda i, *_: (then(i), 0)),
                pl.BlockSpec((block, 2 * TILE), lambda i, *_: (then(i), 0)),
                pl.BlockSpec(weight.shape, lambda i, *_: (0, 0)),
            ],
            out_specs=[
                pl.BlockSpec((2, 2, TILE, TILE), lambda i, *_: (at(i), 0, 0, 0)),
                pl.BlockSpec((2, 8, TILE), lambda i, *_: (at(i), 0, 0)),
                pl.BlockSpec((block, 3 * TILE), lambda i, *_: (then(i), 0)),
                pl.BlockSpec((block, 3 * TILE), lambda i, *_: (then(i), 0)),
                pl.BlockSpec((block, 6 * TILE), lambda i, *_: (then(i), 0)),
                pl.BlockSpec((block, width), lambda i, *_: (jnp.clip(i - pairs - blocks, 0, 1), 0)),
                pl.BlockSpec((block, width), lambda i, *_: (jnp.clip(i - pairs - blocks - 2, 0, 1), 0)),
            ],
            scratch_shapes=[
                pltpu.VMEM((3, pairs, SEQ, TILE), BF), pltpu.VMEM((SEQ, TILE), F32), pltpu.VMEM((SEQ, TILE), F32),
            ],
        ),
        out_shape=[
            jax.ShapeDtypeStruct((2 * pairs, 2, TILE, TILE), F32),
            jax.ShapeDtypeStruct((2 * pairs, 8, TILE), F32),
            jax.ShapeDtypeStruct((width, 3 * TILE), BF),
            jax.ShapeDtypeStruct((width, 3 * TILE), F32),
            jax.ShapeDtypeStruct((width, 6 * TILE), BF),
            jax.ShapeDtypeStruct((2 * block, width), F32),
            jax.ShapeDtypeStruct((2 * block, width), F32),
        ],
        compiler_params=pltpu.CompilerParams(vmem_limit_bytes=60 * MIB),
        cost_estimate=SMALL_COST,
        name="attend_back",
    )(core, length, qkv, qkv, qkv, near, mixed, logs, grad, normed, output, output_own, weight)


def low_lanes(shape):
    return lax.broadcasted_iota(jnp.int32, shape, 1) < HEAD_DIM


def turned(tile):
    return pltpu.roll(tile, HEAD_DIM, 1)


def pack_kernel(q_ref, k_ref, v_ref, o_ref, one_ref, two_ref, router_ref, out_ref):
    shard = q_ref.shape[1]
    rows = q_ref.shape[0]
    source = lax.broadcasted_iota(jnp.int32, (shard, 6 * TILE), 0)
    target = lax.broadcasted_iota(jnp.int32, (shard, 6 * TILE), 1)

    def moved(pair_base, last_base):
        want = jnp.where(source < TILE, source + pair_base, source - TILE + last_base)
        return jnp.where(target == want, 1.0, 0.0).astype(BF)

    total = dot(v_ref[...], moved(0, 2 * TILE)) + dot(o_ref[...], moved(TILE, 2 * TILE + HEAD_DIM), TN)
    total = total + dot(q_ref[...], moved(3 * TILE, 5 * TILE)) + dot(k_ref[...], moved(4 * TILE, 5 * TILE + HEAD_DIM))
    out_ref[:, : 6 * TILE] = total.astype(BF)
    experts = router_ref.shape[0]
    own_row = lax.broadcasted_iota(jnp.int32, (rows, rows), 0) == lax.broadcasted_iota(jnp.int32, (rows, rows), 1)

    def column(ref):
        return jnp.sum(jnp.where(own_row, ref[...].astype(F32), 0.0), axis=1, keepdims=True)

    lanes = lax.broadcasted_iota(jnp.int32, (experts, TILE), 1)
    spread = jnp.where(lanes == lax.broadcasted_iota(jnp.int32, (experts, TILE), 0), 1.0, 0.0).astype(BF)
    place = lax.broadcasted_iota(jnp.int32, (rows, TILE), 1)
    small = dot(router_ref[...], spread, TN)
    small = jnp.where(place == experts, column(one_ref), jnp.where(place == experts + 1, column(two_ref), small))
    out_ref[:, 6 * TILE :] = small.astype(BF)


def pack_weights(query, key, value, output, one, two, router):
    rows = query.shape[0]
    return pl.pallas_call(
        pack_kernel,
        out_shape=jax.ShapeDtypeStruct((rows, 7 * TILE), BF),
        compiler_params=pltpu.CompilerParams(vmem_limit_bytes=60 * MIB),
        cost_estimate=SMALL_COST,
        name="pack_weights",
    )(query, key, value, output, one[None], two[None], router.T)


def qkv_kernel(micro_ref, tokens_ref, gain_ref, a_own, a_far, b_own, b_far, qkv_ref, normed_ref, weight_ref, output_ref):
    width = tokens_ref.shape[2]

    @pl.when(pl.program_id(0) == 0)
    def _():
        low = low_lanes((width, TILE))

        def tiles(own, far, pair, low_half):
            at = slice(pair * TILE, (pair + 1) * TILE)
            one, two = own[:, 2 * TILE :].astype(F32), far[:, 2 * TILE :].astype(F32)
            last = jnp.where(low, one, turned(two)) if low_half else jnp.where(low, turned(one), two)
            return own[:, at], far[:, at], last.astype(BF)

        for n, (own, far, pair, low_half) in enumerate(
            ((a_own, a_far, 0, True), (a_own, a_far, 1, False), (b_own, b_far, 0, True))
        ):
            for t, tile in enumerate(tiles(own[...], far[...], pair, low_half)):
                at = 3 * n + t
                weight_ref[:, at * TILE : (at + 1) * TILE] = tile
        for t, tile in enumerate(tiles(b_own[...], b_far[...], 1, False)):
            output_ref[:, t * TILE : (t + 1) * TILE] = tile

    x = tokens_ref[0].astype(F32)
    inverse = lax.rsqrt(jnp.mean(x * x, axis=-1, keepdims=True) + 1e-06)
    normed = (x * inverse * gain_ref[...]).astype(BF)
    normed_ref[...] = normed
    qkv_ref[...] = dot(normed, weight_ref[...]).astype(BF)


def norm_and_project(micro, layer_input, gain, a_own, a_far, b_own, b_far):
    width = layer_input.shape[2]
    block = 256
    cols = 3 * TILE
    whole = lambda rows, n: pl.BlockSpec((rows, n), lambda i, m: (0, 0))
    here = lambda n: pl.BlockSpec((block, n), lambda i, m: (i, 0))
    return pl.pallas_call(
        qkv_kernel,
        grid_spec=pltpu.PrefetchScalarGridSpec(
            num_scalar_prefetch=1,
            grid=(SEQ // block,),
            in_specs=[pl.BlockSpec((1, block, width), lambda i, m: (m[0], i, 0)), whole(1, width)] + [whole(width, cols)] * 4,
            out_specs=[here(3 * cols), here(width), whole(width, 3 * cols), whole(width, cols)],
        ),
        out_shape=[
            jax.ShapeDtypeStruct((SEQ, 3 * cols), BF),
            jax.ShapeDtypeStruct((SEQ, width), BF),
            jax.ShapeDtypeStruct((width, 3 * cols), BF),
            jax.ShapeDtypeStruct((width, cols), BF),
        ],
        compiler_params=pltpu.CompilerParams(vmem_limit_bytes=40 * MIB),
        cost_estimate=SMALL_COST,
        name="norm_and_project",
    )(micro, layer_input, gain, a_own, a_far, b_own, b_far)


def middle_kernel(
    blocks, per, micro_ref, tokens_ref, mixed_ref, other_ref, own_ref, far_ref, gain_ref, code_ref, residual_ref, *refs
):
    sent_refs, normed = refs[:-1], refs[-1]
    step = pl.program_id(0)
    rows = tokens_ref.shape[1]

    @pl.when(step < blocks)
    def _():
        total = tokens_ref[0].astype(F32) + dot(mixed_ref[...], own_ref[...], NT) + dot(other_ref[...], far_ref[...], NT)
        residual_ref[...] = total
        inverse = lax.rsqrt(jnp.mean(total * total, axis=-1, keepdims=True) + 1e-06)
        normed[pl.ds(pl.multiple_of(step * rows, rows), rows), :] = (total * inverse * gain_ref[...]).astype(BF)

    for c, sent_ref in enumerate(sent_refs):

        @pl.when((step >= blocks + c * per) & (step < blocks + (c + 1) * per))
        def _(sent_ref=sent_ref):
            block = sent_ref.shape[0]
            ids = lax.broadcasted_iota(jnp.int32, (block, 1), 0) + (step - blocks) * block
            hot = jnp.where((ids == code_ref[:1]) | (ids == code_ref[1:2]), 1.0, 0.0).astype(BF)
            sent_ref[...] = dot(hot, normed[...]).astype(BF)


def residual_and_rows(micro, layer_input, mixed, other, output_own, output_far, gain, code, count, chunks):
    width = layer_input.shape[2]
    block = 256
    blocks = SEQ // block
    send = 320
    cols = mixed.shape[1]
    per = count // send
    at = lambda i: jnp.minimum(i, blocks - 1)
    whole = lambda arr: pl.BlockSpec(arr.shape, lambda i, m: (0, 0))
    here = lambda n: pl.BlockSpec((block, n), lambda i, m: (at(i), 0))

    def sent(c):
        return pl.BlockSpec((send, width), lambda i, m: (jnp.clip(i - blocks - c * per, 0, per - 1), 0))

    return pl.pallas_call(
        functools.partial(middle_kernel, blocks, per),
        grid_spec=pltpu.PrefetchScalarGridSpec(
            num_scalar_prefetch=1,
            grid=(blocks + chunks * per,),
            in_specs=[
                pl.BlockSpec((1, block, width), lambda i, m: (m[0], at(i), 0)),
                here(cols), here(cols), whole(output_own), whole(output_far), whole(gain), whole(code),
            ],
            out_specs=[here(width)] + [sent(c) for c in range(chunks)],
            scratch_shapes=[pltpu.VMEM((SEQ, width), BF)],
        ),
        out_shape=[jax.ShapeDtypeStruct((SEQ, width), F32)] + [jax.ShapeDtypeStruct((count, width), BF)] * chunks,
        compiler_params=pltpu.CompilerParams(vmem_limit_bytes=40 * MIB),
        cost_estimate=SMALL_COST,
        name="residual_and_rows",
    )(micro, layer_input, mixed, other, output_own, output_far, gain, code)


def picked_rows(first, second, segments):
    total = None
    start = 0
    for rows in segments:
        length = rows.shape[0]
        ids = lax.broadcasted_iota(jnp.int32, (1, length), 1) + start
        hot = []
        for at in range(0, first.shape[0], STRIP):
            one, two = first[at : at + STRIP], second[at : at + STRIP]
            hot.append(jnp.where((one == ids) | (two == ids), 1.0, 0.0).astype(BF))
        total = put(total, dot(jnp.concatenate(hot, 0), rows))
        start += length
    return total


def put(a, b):
    return b if a is None else a + b


def folded(product):
    return jnp.sum(product.reshape(product.shape[0] // 8, 8, product.shape[1]), axis=0)


def as_column(eight):
    ones = jnp.ones((16, TILE), BF)
    high = eight.astype(BF)
    rest = (eight - high.astype(F32)).astype(BF)
    return dot(jnp.concatenate([high, rest], 0), ones, TN)


def combine_kernel(experts, half, spare, micro_ref, core_ref, length_ref, *refs):
    info_ref, grad_ref, residual_ref, mixed_ref, gain_ref, router_ref, output_ref = refs[:7]
    backs = refs[7:-9]
    (total_ref, mixed_grad_ref, extra_ref, far_ref, own_ref, acc_ref, router_acc, gain_acc, tables) = refs[-9:]
    block = residual_ref.shape[0]
    step = pl.program_id(0)
    count = len(backs) // 2

    @pl.when(step == 0)
    def _():
        place = lax.broadcasted_iota(jnp.int32, (experts, 1), 0)
        for n, back in enumerate((backs[count - 1], backs[2 * count - 1])):
            table = jnp.zeros((experts, back.shape[2]), F32)
            for e in range(experts):
                row = back[e, spare : spare + 16, :].astype(F32)[:1]
                table = jnp.where(place == e, row, table)
            for piece in range(3):
                at = (3 * n + piece) * experts
                tables[at : at + experts] = table[:, piece * half : (piece + 1) * half]

    info = jnp.transpose(info_ref[...])
    number = lambda n: info[:, n : n + 1]
    columns = lax.broadcasted_iota(jnp.int32, (1, half), 1)
    lanes = lax.broadcasted_iota(jnp.int32, (1, 6 * experts), 1)
    table = tables[...].astype(BF)
    values = []
    for k in range(2):
        slot = number(4 + k)
        hot = jnp.where(columns == lax.rem(slot, half), 1.0, 0.0).astype(BF)
        found = dot(hot, table, NT)
        wanted = jnp.where(slot // half == core_ref[0], 0, 3 * experts) + number(2 + k)
        away = lanes - wanted
        hit = (away == 0) | (away == experts) | (away == 2 * experts)
        values.append(jnp.sum(jnp.where(hit, found, 0.0), axis=1, keepdims=True))
    wide = lax.broadcasted_iota(jnp.int32, (1, TILE), 1)
    is_first, is_second = wide == number(2), wide == number(3)
    residual = residual_ref[...]
    gain = gain_ref[...]
    inverse = lax.rsqrt(jnp.mean(residual * residual, axis=-1, keepdims=True) + 1e-06)
    plain = residual * inverse
    normed = (plain * gain).astype(BF)
    logits = dot(normed, router_ref[...])
    gap = jnp.sum(jnp.where(is_first, logits, 0.0) - jnp.where(is_second, logits, 0.0), axis=1, keepdims=True)
    small = jnp.exp(-jnp.abs(gap))
    logit = small / ((1.0 + small) * (1.0 + small)) * (values[0] - values[1])
    logit_grad = jnp.where(is_first, logit, jnp.where(is_second, -logit, 0.0)).astype(BF)
    segments = [b[...].reshape(b.shape[0] * b.shape[1], b.shape[2]) for b in backs]
    normed_grad = picked_rows(number(0), number(1), segments) + dot(logit_grad, router_ref[...], NT)
    scaled = normed_grad * gain
    mean = jnp.mean(scaled * plain, axis=-1, keepdims=True)
    place = lax.broadcasted_iota(jnp.int32, (block, 1), 0) + step * block
    grad_out = jnp.where(place < length_ref[0], grad_ref[0].astype(F32), 0.0)
    total = grad_out + inverse * (scaled - plain * mean)

    @pl.when(step == core_ref[0])
    def _():
        total_ref[...] = total

    branch = total.astype(BF)
    mixed_grad_ref[...] = dot(branch, output_ref[...]).astype(BF)
    router_part = dot(logit_grad, normed, TN)
    gain_part = folded(normed_grad * plain)
    output_part = dot(mixed_ref[...], branch, TN)

    @pl.when(step == 0)
    def _():
        router_acc[...] = router_part
        gain_acc[...] = gain_part
        acc_ref[...] = output_part

    @pl.when(step > 0)
    def _():
        router_acc[...] += router_part
        gain_acc[...] += gain_part
        acc_ref[...] += output_part

    @pl.when(step == pl.num_programs(0) - 1)
    def _():
        extra_ref[...] = jnp.transpose(router_acc[...]) + jnp.where(wide == experts + 1, as_column(gain_acc[...]), 0.0)
        parts = jnp.transpose(acc_ref[...])
        far_ref[...] = parts[:, TILE:].astype(BF)
        own_ref[:, :TILE] = parts[:, :TILE]
        own_ref[:, TILE:] = parts[:, 2 * TILE :]


def combine(micro, core, length, info, out_grad, residual, mixed, gain, router, output_own, backs, half, spare):
    width = residual.shape[1]
    block = 512
    cols = mixed.shape[1]
    whole = lambda arr: pl.BlockSpec(arr.shape, lambda i, *_: (0,) * arr.ndim)
    fixed = lambda rows, n: pl.BlockSpec((rows, n), lambda i, *_: (0, 0))
    here = lambda n: pl.BlockSpec((block, n), lambda i, *_: (i, 0))
    experts = backs[0].shape[0]
    return pl.pallas_call(
        functools.partial(combine_kernel, experts, half, spare),
        grid_spec=pltpu.PrefetchScalarGridSpec(
            num_scalar_prefetch=3,
            grid=(SEQ // block,),
            in_specs=[
                pl.BlockSpec((8, block), lambda i, *_: (0, i)),
                pl.BlockSpec((1, block, width), lambda i, m, *_: (m[0], i, 0)),
                here(width), here(cols), whole(gain), whole(router), whole(output_own),
            ]
            + [whole(x) for x in backs],
            out_specs=[fixed(block, width), here(cols), fixed(width, TILE), fixed(width, 2 * TILE), fixed(width, 2 * TILE)],
            scratch_shapes=[
                pltpu.VMEM((cols, width), F32),
                pltpu.VMEM((TILE, width), F32),
                pltpu.VMEM((8, width), F32),
                pltpu.VMEM((6 * experts, half), F32),
            ],
        ),
        out_shape=[
            jax.ShapeDtypeStruct((block, width), F32),
            jax.ShapeDtypeStruct((SEQ, cols), BF),
            jax.ShapeDtypeStruct((width, TILE), F32),
            jax.ShapeDtypeStruct((width, 2 * TILE), BF),
            jax.ShapeDtypeStruct((width, 2 * TILE), F32),
        ],
        compiler_params=pltpu.CompilerParams(vmem_limit_bytes=60 * MIB),
        cost_estimate=SMALL_COST,
        name="combine",
    )(micro, core, length, info, out_grad, residual, mixed, gain, router, output_own, *backs)


def both_kernel(
    lane, micro_ref, core_ref, length_ref, part_ref, got_ref, tokens_ref, gain_ref, grad_ref,
    info_ref, residual_ref, own_ref, far_ref, out_ref, extra_ref, acc_ref,
):
    block = residual_ref.shape[0]
    info = jnp.transpose(info_ref[...])
    place = lax.broadcasted_iota(jnp.int32, (block, 1), 0) + (core_ref[0] * 2 + pl.program_id(0)) * block
    rows = residual_ref[...] + picked_rows(info[:, 6:7], info[:, 7:8], (own_ref[...], far_ref[...]))
    out_ref[0] = jnp.where(place < length_ref[0], rows, 0.0).astype(BF)
    normed_grad = got_ref[...] + part_ref[...]
    x = tokens_ref[0].astype(F32)
    inverse = lax.rsqrt(jnp.mean(x * x, axis=-1, keepdims=True) + 1e-06)
    plain = x * inverse
    scaled = normed_grad * gain_ref[...]
    mean = jnp.mean(scaled * plain, axis=-1, keepdims=True)
    out_ref[1] = (grad_ref[...] + inverse * (scaled - plain * mean)).astype(BF)
    wide = lax.broadcasted_iota(jnp.int32, (1, TILE), 1)
    part = folded(normed_grad * plain)

    @pl.when(pl.program_id(0) == 0)
    def _():
        acc_ref[...] = part

    @pl.when(pl.program_id(0) == 1)
    def _():
        extra_ref[...] = jnp.where(wide == lane, as_column(acc_ref[...] + part), 0.0)


def both_rows(lane, micro, core, length, part, got, layer_input, gain, residual_grad, info, residual, own, far):
    width = part.shape[1]
    plain = pl.BlockSpec((256, width), lambda i, *_: (i, 0))
    block = 256
    here = lambda n: pl.BlockSpec((block, n), lambda i, m, c, *_: (c[0] * 2 + i, 0))
    whole = lambda arr: pl.BlockSpec(arr.shape, lambda i, *_: (0, 0))
    return pl.pallas_call(
        functools.partial(both_kernel, lane),
        grid_spec=pltpu.PrefetchScalarGridSpec(
            num_scalar_prefetch=3,
            grid=(2,),
            in_specs=[
                plain,
                plain,
                pl.BlockSpec((1, block, width), lambda i, m, c, *_: (m[0], c[0] * 2 + i, 0)),
                whole(gain),
                plain,
                pl.BlockSpec((8, block), lambda i, m, c, *_: (0, c[0] * 2 + i)),
                here(width),
                whole(own),
                whole(far),
            ],
            out_specs=[
                pl.BlockSpec((2, block, width), lambda i, *_: (0, i, 0)),
                pl.BlockSpec((width, TILE), lambda i, *_: (0, 0)),
            ],
            scratch_shapes=[pltpu.VMEM((8, width), F32)],
        ),
        out_shape=[jax.ShapeDtypeStruct((2, 2 * block, width), BF), jax.ShapeDtypeStruct((width, TILE), F32)],
        compiler_params=pltpu.CompilerParams(vmem_limit_bytes=40 * MIB),
        cost_estimate=SMALL_COST,
        name="both_rows",
    )(micro, core, length, part, got, layer_input, gain, residual_grad, info, residual, own, far)


def sum_kernel(kept, own, got, early, late, late_far, table, sum_ref):
    low = low_lanes(early.shape)
    sum_ref[:, : 3 * TILE] = (own[...] + got[...].astype(F32)).astype(BF)
    extra = early[...] + late[...] + late_far[...] + table[...]
    high = extra.astype(BF)
    rest = extra - high.astype(F32)
    if kept <= HEAD_DIM:
        sum_ref[:, 3 * TILE :] = jnp.where(low, high.astype(F32), turned(rest)).astype(BF)
    else:
        sum_ref[:, 3 * TILE : 4 * TILE] = high
        sum_ref[:, 4 * TILE :] = rest.astype(BF)


def packed_sums(kept, *parts):
    width = parts[0].shape[0]
    cols = (4 if kept <= HEAD_DIM else 5) * TILE
    block = 256
    here = lambda n: pl.BlockSpec((block, n), lambda i: (i, 0))
    return pl.pallas_call(
        functools.partial(sum_kernel, kept),
        grid=(width // block,),
        in_specs=[here(x.shape[1]) for x in parts],
        out_specs=here(cols),
        out_shape=jax.ShapeDtypeStruct((width, cols), BF),
        compiler_params=pltpu.CompilerParams(vmem_limit_bytes=40 * MIB),
        cost_estimate=SMALL_COST,
        name="packed_sums",
    )(*parts)


def added(parts_ref):
    total = parts_ref[0].astype(F32)
    for n in range(1, parts_ref.shape[0]):
        total = total + parts_ref[n].astype(F32)
    return total


def first_kernel(parts_ref, own_ref, far_ref):
    total = added(parts_ref)
    own_ref[...] = total[:, : 3 * TILE]
    far_ref[...] = total[:, 3 * TILE :]


def first_sums(parts):
    rows = parts.shape[1]
    return pl.pallas_call(
        first_kernel,
        out_shape=[jax.ShapeDtypeStruct((rows, 3 * TILE), F32)] * 2,
        compiler_params=pltpu.CompilerParams(vmem_limit_bytes=40 * MIB),
        cost_estimate=SMALL_COST,
        name="first_sums",
    )(parts)


def final_kernel(kept, parts_ref, own_ref, got_ref, q_ref, k_ref, v_ref, o_ref, small_ref):
    total = added(parts_ref)
    other = own_ref[...] + got_ref[...]
    tile = lambda arr, t: arr[:, t * TILE : (t + 1) * TILE]
    q_ref[:, :TILE] = tile(total, 0)
    q_ref[:, TILE:] = tile(other, 0)[:, :HEAD_DIM]
    k_ref[:, :TILE] = tile(total, 1)
    k_ref[:, TILE:] = turned(tile(other, 0))[:, :HEAD_DIM]
    v_ref[:, :TILE] = tile(total, 2)
    v_ref[:, TILE:] = tile(other, 1)[:, :HEAD_DIM]
    o_ref[:, :TILE] = tile(other, 2)
    o_ref[:, TILE:] = turned(tile(other, 1))[:, :HEAD_DIM]
    small_ref[...] = tile(total, 3) + (turned(tile(total, 3)) if kept <= HEAD_DIM else tile(total, 4))


def final_sums(kept, parts, own, got, shard):
    rows = parts.shape[1]
    return pl.pallas_call(
        functools.partial(final_kernel, kept),
        out_shape=[jax.ShapeDtypeStruct((rows, shard), F32)] * 4 + [jax.ShapeDtypeStruct((rows, TILE), F32)],
        compiler_params=pltpu.CompilerParams(vmem_limit_bytes=40 * MIB),
        cost_estimate=SMALL_COST,
        name="final_sums",
    )(parts, own, got)


def pair_gate(logits, own, other):
    lanes = lax.broadcasted_iota(jnp.int32, logits.shape, 1)
    gap = jnp.sum(
        jnp.where(lanes == own, logits, 0.0) - jnp.where(lanes == other, logits, 0.0), axis=1, keepdims=True
    )
    small = jnp.exp(-jnp.abs(gap))
    return jnp.where(gap >= 0.0, 1.0, small) / (1.0 + small)


def expert_kernel(lead, chunk, half, me_ref, partner_ref, rows_ref, grads_ref, router_ref, *refs):
    before, refs = (refs[0], refs[1:]) if lead is not None and lead > 0 else (None, refs)
    firsts, seconds = refs[:4], refs[4:8]
    back_ref, active_ref, slope_ref, gated_ref, gate_ref, mass_ref = refs[8:]
    rows = rows_ref[...]
    grads = grads_ref[...]
    gate = pair_gate(dot(rows, router_ref[...]), me_ref[0], partner_ref[...])
    gated_ref[...] = (gate * grads.astype(F32)).astype(BF)
    gate_ref[...] = jnp.broadcast_to(gate, gate_ref.shape)
    masses = [None] * (rows.shape[0] // STRIP)
    back = None
    width = firsts[0].shape[1]
    step = 256
    places = [(r, c) for r in range(4) for c in range(0, width, step)]

    def products(r, c):
        return dot(rows, firsts[r][:, c : c + step]), dot(grads, seconds[r][c : c + step, :], NT)

    ahead = products(*places[0])
    for n, (r, c) in enumerate(places):
        x, plain = ahead
        if n + 1 < len(places):
            ahead = products(*places[n + 1])
        place = slice(r * width + c, r * width + c + step)
        for at in range(0, rows.shape[0], STRIP):
            strip = slice(at, at + STRIP)
            value, flow = x[strip], plain[strip]
            square = value * value
            bent = jnp.tanh(value * (GELU_C + (GELU_C * GELU_A) * square))
            rise = 0.5 + 0.5 * bent
            active = value * rise
            slope = rise + active * (1.0 - bent) * (GELU_C + (3.0 * GELU_C * GELU_A) * square)
            low = active.astype(BF)
            active_ref[strip, place] = low
            slope_ref[strip, place] = (gate[strip] * flow * slope).astype(BF)
            part = low.astype(F32) * flow
            masses[at // STRIP] = put(masses[at // STRIP], part[:, :TILE] + part[:, TILE:])
        if c + step == width and r > 0:
            back = put(back, dot(slope_ref[:, (r - 1) * width : r * width], firsts[r - 1][...], NT))
    back = put(back, dot(slope_ref[:, 3 * width :], firsts[3][...], NT))
    back = back.astype(BF)
    mass = jnp.sum(jnp.concatenate(masses, 0), axis=1, keepdims=True)
    if lead is None:
        back_ref[...] = back
        mass_ref[...] = jnp.broadcast_to(mass, mass_ref.shape)
        return
    count = rows.shape[0] // chunk
    number = lax.broadcasted_iota(jnp.int32, (rows.shape[0], 1), 0)
    lanes = lax.broadcasted_iota(jnp.int32, (1, rows.shape[1]), 1)
    inside = lax.rem(number, chunk)
    spread = jnp.zeros(rows.shape, F32)
    for piece in range(3):
        high = mass.astype(BF).astype(F32)
        spread = jnp.where(lanes == piece * half + lead + inside, high, spread)
        mass = mass - high
    own = jnp.where(number // chunk == lax.broadcasted_iota(jnp.int32, (1, TILE), 1), 1.0, 0.0).astype(BF)
    line = dot(own, spread.astype(BF), TN)
    if before is None:
        back_ref[...] = back
        for e in range(count):
            mass_ref[e] = line[e : e + 1].astype(BF)
    else:
        back_ref[:, :chunk] = back.reshape(count, chunk, back.shape[1])
        row = lax.broadcasted_iota(jnp.int32, (16, 1), 0)
        for e in range(count):
            both = line[e : e + 1] + before[e].astype(F32)
            back_ref[e, chunk:] = jnp.where(row == 0, both, 0.0).astype(BF)


def row_block(total):
    return 320 if total % 320 == 0 else total


def expert_rows_pass(lead, chunk, half, me, partner, rows, grads, router, before, firsts, seconds):
    total, width = rows.shape
    block = row_block(total)
    experts = total // chunk
    hidden = sum(f.shape[1] for f in firsts)
    here = lambda cols: pl.BlockSpec((block, cols), lambda i: (i, 0))
    whole = lambda arr: pl.BlockSpec(arr.shape, lambda i: (0, 0))
    lines = pl.BlockSpec((block // chunk, 1, width), lambda i: (i, 0, 0))
    back_shape, back_spec = (total, width), here(width)
    mass_shape, mass_spec, mass_kind = (experts, 1, width), lines, BF
    if lead is None:
        mass_shape, mass_spec, mass_kind = (total, TILE), here(TILE), F32
    elif before is not None:
        back_shape = (experts, chunk + 16, width)
        back_spec = pl.BlockSpec((block // chunk, chunk + 16, width), lambda i: (i, 0, 0))
    return pl.pallas_call(
        functools.partial(expert_kernel, lead, chunk, half),
        grid=(total // block,),
        in_specs=[pl.BlockSpec(memory_space=pltpu.SMEM), here(1), here(width), here(width), whole(router)]
        + ([lines] if before is not None else [])
        + [whole(w) for w in firsts]
        + [whole(w) for w in seconds],
        out_specs=[back_spec, here(hidden), here(hidden), here(width), here(TILE), mass_spec],
        out_shape=[
            jax.ShapeDtypeStruct(back_shape, BF),
            jax.ShapeDtypeStruct((total, hidden), BF),
            jax.ShapeDtypeStruct((total, hidden), BF),
            jax.ShapeDtypeStruct((total, width), BF),
            jax.ShapeDtypeStruct((total, TILE), F32),
            jax.ShapeDtypeStruct(mass_shape, mass_kind),
        ],
        compiler_params=pltpu.CompilerParams(vmem_limit_bytes=56 * MIB),
        cost_estimate=SMALL_COST,
        name="expert_rows",
    )(me, partner, rows, grads, router, *([before] if before is not None else []), *firsts, *seconds)


def weight_parts(count, refs):
    rows, slopes, active, gated = (refs[n * count : (n + 1) * count] for n in range(4))
    first, second = None, None
    for n in range(count):
        first = put(first, dot(rows[n][...], slopes[n][...], TN))
        second = put(second, dot(active[n][...], gated[n][...], TN))
    return first, second


def cross_kernel(count, *refs):
    first, second = weight_parts(count, refs)
    refs[-1][0, 0] = first.astype(BF)
    refs[-1][0, 1] = second.astype(BF)


def kept_kernel(count, *refs):
    got_ref, far_ref, kept_ref = refs[-3:]
    first, second = weight_parts(count, refs)
    first = first + got_ref[0, 0].astype(F32)
    second = second + got_ref[0, 1].astype(F32)

    @pl.when(pl.program_id(0) == 0)
    def _():
        far_ref[0] = first.astype(BF)
        far_ref[1] = second.astype(BF)

    @pl.when(pl.program_id(0) == 1)
    def _():
        kept_ref[0] = first
        kept_ref[1] = second


def weight_specs(rows, slopes, quarter):
    total, width = rows[0].shape
    hidden = slopes[0].shape[1] // 4
    whole = pl.BlockSpec((total, width), lambda i: (0, 0))
    part = pl.BlockSpec((total, hidden), lambda i: (0, quarter(i)))
    count = len(rows)
    return width, hidden, [whole] * count + [part] * (2 * count) + [whole] * count


def cross_weight_grads(rows, slopes, active, gated):
    width, hidden, specs = weight_specs(rows, slopes, lambda i: 2 + i)
    return pl.pallas_call(
        functools.partial(cross_kernel, len(rows)),
        grid=(2,),
        in_specs=specs,
        out_specs=pl.BlockSpec((1, 2, width, hidden), lambda i: (i, 0, 0, 0)),
        out_shape=jax.ShapeDtypeStruct((2, 2, width, hidden), BF),
        compiler_params=pltpu.CompilerParams(vmem_limit_bytes=56 * MIB),
        cost_estimate=SMALL_COST,
        name="cross_weight_grads",
    )(*rows, *slopes, *active, *gated)


def kept_weight_grads(rows, slopes, active, gated, got):
    width, hidden, specs = weight_specs(rows, slopes, lambda i: 1 - i)
    fixed = pl.BlockSpec((2, width, hidden), lambda i: (0, 0, 0))
    return pl.pallas_call(
        functools.partial(kept_kernel, len(rows)),
        grid=(2,),
        in_specs=specs + [pl.BlockSpec((1, 2, width, hidden), lambda i: (1 - i, 0, 0, 0))],
        out_specs=[fixed, fixed],
        out_shape=[
            jax.ShapeDtypeStruct((2, width, hidden), BF),
            jax.ShapeDtypeStruct((2, width, hidden), F32),
        ],
        compiler_params=pltpu.CompilerParams(vmem_limit_bytes=56 * MIB),
        cost_estimate=SMALL_COST,
        name="kept_weight_grads",
    )(*rows, *slopes, *active, *gated, got)


def result_kernel(chunks, *refs):
    active, gates, seconds, out_ref = refs[:chunks], refs[chunks : 2 * chunks], refs[2 * chunks : -1], refs[-1]
    for c in range(chunks):

        @pl.when(pl.program_id(0) == c)
        def _(c=c):
            width = seconds[0].shape[0]
            total = None
            for r, second in enumerate(seconds):
                total = put(total, dot(active[c][:, r * width : (r + 1) * width], second[...]))
            rows = (total * gates[c][:, :1]).astype(BF)
            if chunks > 1:
                out_ref[:, 0] = rows.reshape(out_ref.shape[0], out_ref.shape[2], out_ref.shape[3])
            else:
                out_ref[...] = rows


def expert_results(active, gates, seconds, experts):
    chunks = len(active)
    total, hidden = active[0].shape
    width = seconds[0].shape[1]
    block = row_block(total)
    steps = total // block

    def here(c, cols):
        return pl.BlockSpec((block, cols), lambda g, i: (jnp.where(g == c, i, jnp.where(g < c, 0, steps - 1)), 0))

    chunk = total // experts
    if chunks > 1:
        shape = (experts, chunks, chunk, width)
        out_spec = pl.BlockSpec((block // chunk, 1, chunk, width), lambda g, i: (i, g, 0, 0))
    else:
        shape = (total, width)
        out_spec = pl.BlockSpec((block, width), lambda g, i: (i, 0))
    out = pl.pallas_call(
        functools.partial(result_kernel, chunks),
        grid=(chunks, steps),
        in_specs=[here(c, hidden) for c in range(chunks)]
        + [here(c, TILE) for c in range(chunks)]
        + [pl.BlockSpec(w.shape, lambda g, i: (0, 0)) for w in seconds],
        out_specs=out_spec,
        out_shape=jax.ShapeDtypeStruct(shape, BF),
        compiler_params=pltpu.CompilerParams(vmem_limit_bytes=56 * MIB),
        cost_estimate=SMALL_COST,
        name="expert_results",
    )(*active, *gates, *seconds)
    return out.reshape(experts, chunks * chunk, width)


def last_sum_kernel(kept_ref, y_ref, out_first, out_second):
    for n, out in enumerate((out_first, out_second)):
        out[...] = kept_ref[n] + y_ref[n].astype(F32)


def last_sums(kept, got_y):
    _, width, hidden = kept.shape
    block = 256
    here = pl.BlockSpec((block, hidden), lambda i: (i, 0))
    part = pl.BlockSpec((2, block, hidden), lambda i: (0, i, 0))
    return pl.pallas_call(
        last_sum_kernel,
        grid=(width // block,),
        in_specs=[part, part],
        out_specs=[here, here],
        out_shape=[jax.ShapeDtypeStruct((width, hidden), F32)] * 2,
        compiler_params=pltpu.CompilerParams(vmem_limit_bytes=40 * MIB),
        cost_estimate=SMALL_COST,
        name="last_sums",
    )(kept, got_y)


def send_kernel(micro_ref, code_ref, rows_ref, out_ref):
    block = out_ref.shape[0]
    ids = lax.broadcasted_iota(jnp.int32, (block, 1), 0) + pl.program_id(0) * block
    hot = jnp.where((ids == code_ref[:1]) | (ids == code_ref[1:2]), 1.0, 0.0).astype(BF)
    out_ref[...] = dot(hot, rows_ref[0]).astype(BF)


def send_rows(micro, code, rows, count):
    width = rows.shape[2]
    block = next(b for b in (336, 320, 384, count) if count % b == 0)
    return pl.pallas_call(
        send_kernel,
        grid_spec=pltpu.PrefetchScalarGridSpec(
            num_scalar_prefetch=1,
            grid=(count // block,),
            in_specs=[
                pl.BlockSpec(code.shape, lambda i, m: (0, 0)),
                pl.BlockSpec((1, SEQ, width), lambda i, m: (m[0], 0, 0)),
            ],
            out_specs=pl.BlockSpec((block, width), lambda i, m: (i, 0)),
        ),
        out_shape=jax.ShapeDtypeStruct((count, width), BF),
        compiler_params=pltpu.CompilerParams(vmem_limit_bytes=40 * MIB),
        cost_estimate=SMALL_COST,
        name="send_rows",
    )(micro, code, rows)


def place_kernel(place_ref, one_ref, two_ref, *refs):
    for n, piece in enumerate((one_ref, two_ref)):

        @pl.when(pl.program_id(0) == n)
        def _(piece=piece):
            for k, out_ref in enumerate(refs[-2:]):
                out_ref[0] = piece[k]


def place_pieces(places, pieces, before=()):
    two, rows, width = pieces[0].shape
    whole = pl.BlockSpec(pieces[0].shape, lambda i, place_ref: (0, 0, 0))
    return pl.pallas_call(
        place_kernel,
        grid_spec=pltpu.PrefetchScalarGridSpec(
            num_scalar_prefetch=1,
            grid=(2,),
            in_specs=[whole] * 2 + [pl.BlockSpec(memory_space=pl.ANY)] * len(before),
            out_specs=[pl.BlockSpec((1, rows, width), lambda i, place_ref: (place_ref[i], 0, 0))] * two,
        ),
        out_shape=[jax.ShapeDtypeStruct((4, rows, width), pieces[0].dtype)] * two,
        input_output_aliases={3: 0, 4: 1} if before else {},
        compiler_params=pltpu.CompilerParams(vmem_limit_bytes=40 * MIB),
        cost_estimate=SMALL_COST,
        name="place_pieces",
    )(places, *pieces, *before)


def swap(value, axis, count, bit):
    return lax.ppermute(value, axis, [(i, i ^ bit) for i in range(count)])


def all_to_all(value):
    return lax.all_to_all(value, "dp", split_axis=0, concat_axis=0, tiled=True)


def together(*values):
    return lax.optimization_barrier(values)


def local(
    layer_input, out_grad, first_gain, query_weight, key_weight, value_weight, output_weight,
    position_bias, second_gain, router_weight, expert_in, expert_out, seq_lengths, routes,
):
    micro_count, tok_rows, width = layer_input.shape
    dp_count = lax.axis_size("dp")
    expert_count = router_weight.shape[1]
    shard = query_weight.shape[1]
    heads_here = position_bias.shape[0]
    assert lax.axis_size("tensor") == 4 and micro_count == 2 and expert_count == dp_count
    assert tok_rows == SEQ and seq_lengths.shape[1] == 1
    capacity = max(8, 8 * (10 * tok_rows // (32 * expert_count)))
    half = capacity // 2
    stride = 8 * (half // 8 + 1)
    by_lines = dp_count == 8
    chunks = 2 if half % 32 == 0 else 1
    chunk = half // chunks
    chunk_rows = expert_count * chunk
    rows_here = query_weight.shape[0]
    me = lax.axis_index("dp")
    rank = lax.axis_index("tensor")
    micro = rank // 2
    core = rank % 2

    def swap_y(value):
        return swap(value, "tensor", 4, 2)

    def swap_core(value):
        return swap(value, "tensor", 4, 1)

    micro_arg = micro.reshape(1).astype(jnp.int32)
    core_arg = core.reshape(1).astype(jnp.int32)

    packed = pack_weights(query_weight, key_weight, value_weight, output_weight, first_gain, second_gain, router_weight)
    three = 3 * TILE

    def doubled(stacked, bit, axis=0):
        other = swap(stacked, "dp", dp_count, bit)
        high = (me & bit) != 0
        pair = jnp.where(high, jnp.stack([other, stacked], axis + 1), jnp.stack([stacked, other], axis + 1))
        return pair.reshape(stacked.shape[:axis] + (-1,) + stacked.shape[axis + 1 :])

    stacked = packed[None]
    bit = dp_count // 2
    while bit > 1:
        stacked = doubled(stacked, bit)
        bit //= 2
    length = lax.dynamic_index_in_dim(seq_lengths, micro, 0, keepdims=False)
    route = lax.dynamic_index_in_dim(routes, micro, 0, keepdims=False).T
    expert_ids = jnp.arange(expert_count, dtype=jnp.int32)
    named = (expert_ids[:, None, None] == route[None]).astype(jnp.int32)
    per_token = jnp.sum(named, axis=1, dtype=jnp.int32)
    earlier = jnp.cumsum(per_token, axis=1, dtype=jnp.int32) - per_token
    slot = jnp.sum(named * earlier[:, None, :], axis=0, dtype=jnp.int32)
    here = slot // half == core
    within = slot % half
    chunk_of = within // chunk
    inside = within % chunk
    spare = 16 * -(-chunk // 16)
    last_stride = spare + 16
    last = (chunks - 1) * chunk_rows
    code_back = jnp.where(
        chunk_of == chunks - 1, last + route * last_stride + inside, chunk_of * chunk_rows + route * chunk + inside
    )
    code_back = code_back + jnp.where(here, 0, last + expert_count * last_stride)
    code_result = route * half + within + jnp.where(here, 0, expert_count * half)
    info = jnp.concatenate([code_back, route, slot, code_result], 0)

    code_grads = jnp.where(here, route * stride + within, -1)
    valid = jnp.arange(SEQ, dtype=jnp.int32) < length[0]
    ids = jnp.arange(expert_count * stride, dtype=jnp.int32)[:, None]
    partner = jnp.sum(
        jnp.where(ids == code_grads[:1], route[1:], 0) + jnp.where(ids == code_grads[1:], route[:1], 0), axis=1, dtype=jnp.int32
    )
    grads_sent = send_rows(micro_arg, jnp.where(valid[None], code_grads, -1), out_grad, expert_count * stride)
    grads_sent = grads_sent.reshape(expert_count, stride, width)
    partner_row = jnp.pad(partner.reshape(expert_count, stride)[:, :half].astype(BF), ((0, 0), (0, width - half)))
    grads_sent = grads_sent.at[:, half].set(partner_row)
    stacked, grads_sent, position_bias = together(stacked, grads_sent, position_bias)
    if by_lines:
        lines = [list(range(x, dp_count, 2)) for x in range(2)]
        grads_z = lax.all_to_all(
            grads_sent.reshape(dp_count // 2, 2, stride, width), "dp", split_axis=0, concat_axis=0,
            axis_index_groups=lines, tiled=True,
        )

    first_own = expert_in[0]
    second_own = expert_out[0]
    part_b = stacked[:, :, :three]
    far_b = swap_y(part_b)
    part_a = doubled(stacked[:, :, three:], 1)
    part_a, far_b = together(part_a, far_b)
    pair_b = jnp.stack([part_b, far_b])
    a_own = part_a[:, :, :three]
    a_far = swap_y(a_own).reshape(width, three)
    a_own = a_own.reshape(width, three)
    pair_b = doubled(pair_b, 1, 1).reshape(2, width, three)
    if by_lines:
        a_far, pair_b, first_own = together(a_far, pair_b, first_own)
    else:
        a_far, pair_b, grads_sent, first_own = together(a_far, pair_b, grads_sent, first_own)
    first_y = swap_y(first_own)
    small_all = part_a[:, :, three:].reshape(width, TILE)
    gain_one = small_all[:, expert_count].astype(F32)[None]
    gain_two = small_all[:, expert_count + 1].astype(F32)[None]
    router_wide = small_all
    far_bias = swap_y(position_bias)
    bias = jnp.concatenate([position_bias[:2], far_bias[:2], position_bias[2:], far_bias[2:]], 0)
    head_total = bias.shape[0]
    hot_const = jnp.asarray(NEAR_HOT, dtype=BF)
    near = dot(bias, hot_const) - bias[:, NB - 1 :].astype(F32)
    near = near.reshape(head_total, 2, TILE, TILE)
    places = jnp.arange(TILE, dtype=jnp.int32)
    causal = jnp.stack([places[None, :] <= places[:, None], jnp.ones((TILE, TILE), bool)])
    near = jnp.where(causal[None], near, NEG)

    if by_lines:
        high = (me & 1) != 0
    else:
        grads_here = all_to_all(grads_sent)

    qkv, normed_one, qkv_weight, output_own = norm_and_project(
        micro_arg, layer_input, gain_one, a_own, a_far, pair_b[0], pair_b[1]
    )
    output_far = swap_core(output_own)
    mixed, logs = attend(length, qkv, near)
    mixed, output_far = together(mixed, output_far)
    mixed_far = swap_core(mixed)
    code_chunks = jnp.where(here, chunk_of * chunk_rows + route * chunk + inside, -1)
    if by_lines:
        sent_x = lax.dynamic_index_in_dim(grads_z, 1 - (me & 1), 1, keepdims=False)
        mixed_far, grads_z, sent_x = together(mixed_far, grads_z, sent_x)
        got_x = swap(sent_x, "dp", dp_count, 1)
    residual, *parts = residual_and_rows(
        micro_arg, layer_input, mixed, mixed_far, output_own, output_far, gain_two, code_chunks, chunk_rows, chunks
    )

    if by_lines:
        parts, first_y, second_own = together(parts, first_y, second_own)
        kept_x = jnp.where(high, grads_z[:, 1], grads_z[:, 0])
        pair_x = jnp.where(high, jnp.stack([got_x, kept_x], 1), jnp.stack([kept_x, got_x], 1))
        grads_here = pair_x.reshape(dp_count, stride, width)
    else:
        parts, grads_here, first_y, second_own = together(parts, grads_here, first_y, second_own)
    second_y = swap_y(second_own)
    parts = [part.reshape(expert_count, chunk, width) for part in parts]
    arrived = [all_to_all(parts[0])]
    partner_here = grads_here[:, half, :half].astype(jnp.int32)

    def chunk_grads(c):
        at = slice(c * chunk, (c + 1) * chunk)
        return grads_here[:, at].reshape(chunk_rows, width), partner_here[:, at].reshape(chunk_rows, 1)

    grads_parts = [chunk_grads(c) for c in range(chunks)]
    arrived[0], grads_parts, second_y = together(arrived[0], grads_parts, second_y)

    firsts = (first_own, first_y, swap_core(first_own), swap_core(first_y))
    seconds = (second_own, second_y, swap_core(second_own), swap_core(second_y))

    for c in range(1, chunks):
        sent, arrived[-1] = together(parts[c], arrived[-1])
        arrived.append(all_to_all(sent))

    me_arg = me.reshape(1).astype(jnp.int32)
    rows_all, slopes, active, gated, gates, backs = [], [], [], [], [], []
    line = None
    for c in range(chunks):
        grads_c, partner_c = grads_parts[c]
        rows_c = arrived[c].reshape(chunk_rows, width)
        back, act, slo, gat, gte, line = expert_rows_pass(
            c * chunk if chunks > 1 else None, chunk, half, me_arg, partner_c, rows_c, grads_c, router_wide, line, firsts, seconds
        )
        rows_all.append(rows_c)
        slopes.append(slo)
        active.append(act)
        gated.append(gat)
        gates.append(gte)
        if chunks == 1:
            gate_grad = line[:, 0].reshape(expert_count, chunk)
            pieces = []
            for _ in range(3):
                piece = gate_grad.astype(BF)
                pieces.append(piece)
                gate_grad = gate_grad - piece.astype(F32)
            gate_row = jnp.pad(jnp.concatenate(pieces, 1), ((0, 0), (0, width - 3 * half)))
            back = jnp.pad(back.reshape(expert_count, chunk, width), ((0, 0), (0, last_stride - chunk), (0, 0)))
            back = back.at[:, spare].set(gate_row)
        if c + 1 < chunks:
            back, arrived[c + 1] = together(back.reshape(expert_count, chunk, width), arrived[c + 1])
        else:
            back, rows_all[-1], backs = together(back, rows_all[-1], backs)
        backs.append(all_to_all(back))
    grads_cross = cross_weight_grads(rows_all, slopes, active, gated)
    gates, grads_cross = together(gates, grads_cross)
    grads_in = swap_core(grads_cross)
    results = expert_results(active, gates, seconds, expert_count)
    results, grads_in = together(results, grads_in)
    grads_far, grads_kept = kept_weight_grads(rows_all, slopes, active, gated, grads_in)
    backs[-1], results, grads_far = together(backs[-1], results, grads_far)

    across_y = swap_y(grads_far)
    results_own = all_to_all(results).reshape(expert_count * half, width)

    backs_far = [swap_core(b) for b in backs]
    residual_grad, mixed_grad, extra_early, output_sent, output_kept = combine(
        micro_arg, core_arg, length, info, out_grad, residual, mixed, gain_two, router_wide, output_own,
        backs + backs_far, half, spare,
    )

    tiles, sums, far_sent, own_parts, cross_parts, sent, kept_part = attend_back(
        core_arg, length, qkv, near, mixed, logs, mixed_grad, normed_one, output_sent, output_kept, qkv_weight
    )
    arrived_cross = all_to_all(cross_parts.reshape(dp_count, rows_here, cross_parts.shape[1]))
    far_got = swap_y(far_sent)
    sent, results_own = together(sent, results_own)
    got = swap_core(sent)
    rows_both, extra_late = both_rows(
        expert_count, micro_arg, core_arg, length, kept_part, got, layer_input, gain_one, residual_grad,
        info, residual, results_own, swap_core(results_own),
    )
    rows_both, across_y, tiles = together(rows_both, across_y, tiles)
    late_far = swap_core(extra_late)
    corner = micro * 2 + core
    corners = jnp.stack([corner, corner ^ 1, corner ^ 2, corner ^ 3]).astype(jnp.int32)
    rows_y = swap_y(rows_both)
    expert_in_grad, expert_out_grad = last_sums(grads_kept, across_y)
    placed = place_pieces(corners[:2], (rows_both, swap_core(rows_both)))
    rows_y, expert_in_grad, expert_out_grad, placed = together(rows_y, expert_in_grad, expert_out_grad, placed)
    placed = place_pieces(corners[2:], (rows_y, swap_core(rows_y)), placed)

    tiles = tiles.reshape(head_total, 2 * TILE * TILE)
    tiles_high = tiles.astype(BF)
    tiles_rest = (tiles - tiles_high.astype(F32)).astype(BF)
    table = dot(tiles_high, hot_const, NT) + dot(tiles_rest, hot_const, NT)
    far_sum = jnp.sum(sums[:, :, 0], axis=1) - jnp.sum(table[:, : NB - 1], axis=1)
    table = jnp.concatenate([table[:, : NB - 1], far_sum[:, None]], 1)
    table_own = jnp.concatenate([table[0:2], table[4:5]], 0)
    table_far = jnp.concatenate([table[2:4], table[5:6]], 0)
    table_cols = heads_here * NB // rows_here
    table_both = jnp.concatenate([table_own.reshape(rows_here, table_cols), table_far.reshape(rows_here, table_cols)], 1)
    base = expert_count + 2
    kept = base + 2 * table_cols
    table_tile = jnp.tile(jnp.pad(table_both, ((0, 0), (base, TILE - kept))), (dp_count, 1))

    grads = packed_sums(kept, own_parts, far_got, extra_early, extra_late, late_far, table_tile)
    grads, arrived_cross = together(grads, arrived_cross)
    cross_own, cross_far = first_sums(arrived_cross)
    cross_got = swap_y(cross_far)
    arrived_grads = all_to_all(grads.reshape(dp_count, rows_here, grads.shape[1]))
    layer_output, input_grad = (out.reshape(2, SEQ, width) for out in placed)
    arrived_grads, layer_output, input_grad = together(arrived_grads, layer_output, input_grad)
    query_grad, key_grad, value_grad, output_grad, small = final_sums(
        kept, arrived_grads, cross_own, cross_got, shard
    )
    small_y = swap_y(small)
    both = small + small_y
    table_sum = small[:, base : base + table_cols] + small_y[:, base + table_cols : kept]
    return (
        layer_output,
        input_grad,
        both[:, expert_count],
        query_grad,
        key_grad,
        value_grad,
        output_grad.T,
        table_sum.reshape(heads_here, NB),
        both[:, expert_count + 1],
        both[:, :expert_count],
        expert_in_grad[None],
        expert_out_grad[None],
    )


def solution(mesh):
    return jax.shard_map(
        local,
        mesh=mesh,
        in_specs=(
            P(None, "dp", None),
            P(None, "dp", None),
            P("dp"),
            P("dp", "tensor"),
            P("dp", "tensor"),
            P("dp", "tensor"),
            P("tensor", "dp"),
            P("tensor", None),
            P("dp"),
            P("dp", None),
            P("dp", None, "tensor"),
            P("dp", "tensor", None),
            P(None, "dp"),
            P(None, "dp", None),
        ),
        out_specs=(
            P(None, "dp", None),
            P(None, "dp", None),
            P("dp"),
            P("dp", "tensor"),
            P("dp", "tensor"),
            P("dp", "tensor"),
            P("tensor", "dp"),
            P("tensor", None),
            P("dp"),
            P("dp", None),
            P("dp", None, "tensor"),
            P("dp", "tensor", None),
        ),
        check_vma=False,
    )
```

```python
import functools

import jax
import jax.numpy as jnp
import numpy as np
from jax import lax
from jax.experimental import pallas as pl
from jax.experimental.pallas import tpu as pltpu
from jax.sharding import PartitionSpec as P

HEAD_DIM = 64
NB = 32
SEQ = 1024
TILE = 128
QROWS = 256
NEG = -1e30
GELU_C = 0.7978845608028654
GELU_A = 0.044715

BF = jnp.bfloat16
F32 = jnp.float32

bucket_edges = np.ceil(16.0 * 8.0 ** (np.arange(1, 16) / 16.0)).astype(np.int32)


def near_tables():
    rows = np.arange(TILE)[:, None]
    cols = np.arange(TILE)[None, :]
    hots = []
    for shift in (0, TILE):
        distance = rows - cols + shift
        clipped = np.maximum(distance, 0)
        reached = np.sum(clipped[..., None] >= bucket_edges, axis=-1)
        bucket = np.minimum(clipped, 16) + reached
        hots.append(bucket[..., None] == np.arange(NB))
    hot = np.stack(hots).reshape(2 * TILE * TILE, NB).T
    return hot


NEAR_HOT = near_tables()
assert bucket_edges[-1] <= TILE


def dot(a, b, dims=((1,), (0,))):
    return lax.dot_general(a, b, (dims, ((), ())), preferred_element_type=F32)


NT = ((1,), (1,))
TN = ((0,), (0,))


MIB = 2**20
SMALL_COST = pl.CostEstimate(flops=1_000_000, bytes_accessed=1_000_000, transcendentals=0)


STRIP = 32


def score_strip(s, at, block, j, start, near_ref, half, length):
    part = s[at : at + STRIP]
    near = slice(start % TILE, start % TILE + STRIP)
    if j == block:
        if start < TILE:
            left = part[:, :TILE] + near_ref[half, 0, near, :]
            right = jnp.full((STRIP, TILE), NEG, F32)
        else:
            left = part[:, :TILE] + near_ref[half, 1, near, :]
            right = part[:, TILE:] + near_ref[half, 0, near, :]
        part = jnp.concatenate([left, right], 1)
    elif j == block - 1 and start < TILE:
        part = jnp.concatenate([part[:, :TILE], part[:, TILE:] + near_ref[half, 1, near, :]], 1)
    if (j + 1) * QROWS > SEQ // 2:
        place = lax.broadcasted_iota(jnp.int32, (1, QROWS), 1) + j * QROWS
        part = part + jnp.where(place < length, 0.0, NEG)
    return part


def lane_half(rows):
    return lax.broadcasted_iota(jnp.int32, (rows, 2 * HEAD_DIM), 1) < HEAD_DIM


def attend_kernel(length_ref, query_ref, key_ref, value_ref, near_ref, out_ref, log_ref):
    length = length_ref[0]
    lanes = lane_half(QROWS)
    value_ext = jnp.concatenate([value_ref[...], jnp.ones((SEQ, TILE), BF)], 1)
    for i in range(SEQ // QROWS):
        q_rows = query_ref[i * QROWS : (i + 1) * QROWS, :] * BF(0.125)
        q_both = jnp.concatenate([jnp.where(lanes, q_rows, BF(0)), jnp.where(lanes, BF(0), q_rows)], 0)
        tiles = [dot(q_both, key_ref[j * QROWS : (j + 1) * QROWS, :], NT) for j in range(i + 1)]
        tops = []
        weights = [[] for _ in tiles]
        for h in range(2):
            for start in range(0, QROWS, STRIP):
                strips = [
                    score_strip(s, h * QROWS + start, i, j, start, near_ref, h, length) for j, s in enumerate(tiles)
                ]
                top = strips[0]
                for s in strips[1:]:
                    top = jnp.maximum(top, s)
                top = jnp.max(top, axis=1, keepdims=True)
                tops.append(top)
                for j, s in enumerate(strips):
                    weights[j].append(jnp.exp(s - top).astype(BF))
        total = None
        for j, strips in enumerate(weights):
            total = put(total, dot(jnp.concatenate(strips, 0), value_ext[j * QROWS : (j + 1) * QROWS, :]))
        row_sum = total[:, TILE:]
        out = total[:, :TILE] / row_sum
        logs = jnp.concatenate(tops, 0) + jnp.log(row_sum)
        out_ref[i * QROWS : (i + 1) * QROWS, :] = jnp.where(lanes, out[:QROWS], out[QROWS:]).astype(BF)
        log_ref[i * QROWS : (i + 1) * QROWS, :] = jnp.where(lanes, logs[:QROWS], logs[QROWS:])


def attend(length, qkv, near):
    pairs = qkv.shape[1] // (3 * TILE)
    cols = pairs * TILE
    return pl.pallas_call(
        attend_kernel,
        grid=(pairs,),
        in_specs=[
            pl.BlockSpec(memory_space=pltpu.SMEM),
            pl.BlockSpec((SEQ, TILE), lambda p: (0, p)),
            pl.BlockSpec((SEQ, TILE), lambda p: (0, pairs + p)),
            pl.BlockSpec((SEQ, TILE), lambda p: (0, 2 * pairs + p)),
            pl.BlockSpec((2, 2, TILE, TILE), lambda p: (p, 0, 0, 0)),
        ],
        out_specs=[
            pl.BlockSpec((SEQ, TILE), lambda p: (0, p)),
            pl.BlockSpec((SEQ, TILE), lambda p: (0, p)),
        ],
        out_shape=[
            jax.ShapeDtypeStruct((SEQ, cols), BF),
            jax.ShapeDtypeStruct((SEQ, cols), F32),
        ],
        compiler_params=pltpu.CompilerParams(vmem_limit_bytes=40 * MIB),
        cost_estimate=SMALL_COST,
        name="attend",
    )(length, qkv, qkv, qkv, near)


def attend_back_kernel(
    pairs, blocks, core_ref, length_ref, query_ref, key_ref, value_ref, near_ref, out_ref, log_ref, grad_ref,
    normed_ref, output_ref, output_own, weight_ref, tile_ref, sum_ref, far_ref, own_ref, cross_ref, sent_ref, kept_ref,
    grads, dk_acc, dv_acc,
):
    step = pl.program_id(0)

    @pl.when(step < pairs)
    def _():
        pair_grads(
            step, length_ref, query_ref, key_ref, value_ref, near_ref, out_ref, log_ref, grad_ref,
            tile_ref, sum_ref, grads, dk_acc, dv_acc,
        )

    @pl.when((step >= pairs) & (step < pairs + blocks))
    def _():
        low = low_lanes((normed_ref.shape[1], TILE))
        q, k, v = (
            dot(normed_ref[...], jnp.concatenate([grads[n, p] for p in range(pairs)], 1), TN) for n in range(3)
        )
        for n, part in enumerate((q, k, v)):
            own_ref[:, n * TILE : (n + 1) * TILE] = part[:, :TILE]
            far_ref[:, n * TILE : (n + 1) * TILE] = part[:, TILE : 2 * TILE].astype(BF)
        q, k, v = (part[:, 2 * TILE :] for part in (q, k, v))
        tiles = (
            jnp.where(low, q, turned(k)),
            jnp.where(low, v, turned(output_own[:, TILE:])),
            output_own[:, :TILE],
            jnp.where(low, turned(q), k),
            jnp.where(low, turned(v), output_ref[:, TILE:].astype(F32)),
            output_ref[:, :TILE],
        )
        for n, tile in enumerate(tiles):
            cross_ref[:, n * TILE : (n + 1) * TILE] = tile.astype(BF)

    for late, half_ref in enumerate((sent_ref, kept_ref)):
        first = pairs + blocks + 2 * late

        @pl.when((step >= first) & (step < first + 2))
        def _(half_ref=half_ref, first=first, late=late):
            rows = half_ref.shape[0]
            mine = core_ref[0] if late else 1 - core_ref[0]
            start = pl.multiple_of((2 * mine + step - first) * rows, rows)
            total = None
            for n in range(3):
                part = jnp.concatenate([grads[n, p, pl.ds(start, rows), :] for p in range(pairs)], 1)
                cols = part.shape[1]
                total = put(total, dot(part, weight_ref[:, n * cols : (n + 1) * cols], NT))
            half_ref[...] = total


def pair_grads(
    pair, length_ref, query_ref, key_ref, value_ref, near_ref, out_ref, log_ref, grad_ref, tile_ref, sum_ref, grads, dk_acc, dv_acc
):
    length = length_ref[0]
    lanes = lane_half(QROWS)
    key_ext = jnp.concatenate([key_ref[...], jnp.ones((SEQ, TILE), BF)], 1)
    near_sums = [[None, None], [None, None]]
    all_sums = [None, None]

    def both(rows):
        return jnp.concatenate([jnp.where(lanes, rows, BF(0)), jnp.where(lanes, BF(0), rows)], 0)

    for i in range(SEQ // QROWS):
        rows = slice(i * QROWS, (i + 1) * QROWS)
        q_both = both(query_ref[rows, :] * BF(0.125))
        g_rows = grad_ref[rows, :]
        g_both = both(g_rows)
        mass = g_rows.astype(F32) * out_ref[rows, :].astype(F32)
        deltas = [
            jnp.sum(jnp.where(lanes, mass, 0.0), axis=1, keepdims=True),
            jnp.sum(jnp.where(lanes, 0.0, mass), axis=1, keepdims=True),
        ]
        logs = [log_ref[rows, h * HEAD_DIM : h * HEAD_DIM + 1] for h in range(2)]
        dq = None
        for j in range(i + 1):
            keys = slice(j * QROWS, (j + 1) * QROWS)
            s = dot(q_both, key_ref[keys, :], NT)
            dp = dot(g_both, value_ref[keys, :], NT)
            p_strips, d_strips = [], []
            for h in range(2):
                for start in range(0, QROWS, STRIP):
                    strip = slice(start, start + STRIP)
                    at = h * QROWS + start
                    p = jnp.exp(score_strip(s, at, i, j, start, near_ref, h, length) - logs[h][strip])
                    p_strips.append(p.astype(BF))
                    d_strips.append((p * (dp[at : at + STRIP] - deltas[h][strip])).astype(BF))
            p, ds = jnp.concatenate(p_strips, 0), jnp.concatenate(d_strips, 0)
            part = dot(ds, key_ext[keys, :])
            dq = put(dq, jnp.where(lanes, part[:QROWS, :TILE], part[QROWS:, :TILE]))
            for h in range(2):
                sums = part[h * QROWS : (h + 1) * QROWS, TILE:]
                all_sums[h] = put(all_sums[h], jnp.sum(sums.reshape(QROWS // 8, 8, TILE), axis=0))
            dk_part = dot(ds, q_both, TN)
            dv_part = dot(p, g_both, TN)
            if i == j:
                dk_acc[keys, :] = dk_part
                dv_acc[keys, :] = dv_part
            else:
                dk_acc[keys, :] += dk_part
                dv_acc[keys, :] += dv_part
            for h in range(2):
                mine = ds[h * QROWS : (h + 1) * QROWS]
                if j == i:
                    wide = mine.astype(F32)
                    near_sums[h][0] = put(near_sums[h][0], wide[:TILE, :TILE] + wide[TILE:, TILE:])
                    near_sums[h][1] = put(near_sums[h][1], wide[TILE:, :TILE])
                elif j == i - 1:
                    near_sums[h][1] = put(near_sums[h][1], mine[:TILE, TILE:].astype(F32))
        grads[0, pair, rows, :] = (dq * 0.125).astype(BF)
    grads[1, pair] = dk_acc[...].astype(BF)
    grads[2, pair] = dv_acc[...].astype(BF)
    for h in range(2):
        tile_ref[h, 0] = near_sums[h][0]
        tile_ref[h, 1] = near_sums[h][1]
        sum_ref[h] = all_sums[h]


def attend_back(core, length, qkv, near, mixed, logs, grad, normed, output, output_own, weight):
    pairs = qkv.shape[1] // (3 * TILE)
    width = normed.shape[1]
    block = 256
    blocks = width // block
    at = lambda i: jnp.minimum(i, pairs - 1)
    then = lambda i: jnp.clip(i - pairs, 0, blocks - 1)
    return pl.pallas_call(
        functools.partial(attend_back_kernel, pairs, blocks),
        grid_spec=pltpu.PrefetchScalarGridSpec(
            num_scalar_prefetch=2,
            grid=(pairs + blocks + 4,),
            in_specs=[
                pl.BlockSpec((SEQ, TILE), lambda i, *_: (0, at(i))),
                pl.BlockSpec((SEQ, TILE), lambda i, *_: (0, pairs + at(i))),
                pl.BlockSpec((SEQ, TILE), lambda i, *_: (0, 2 * pairs + at(i))),
                pl.BlockSpec((2, 2, TILE, TILE), lambda i, *_: (at(i), 0, 0, 0)),
            ]
            + [pl.BlockSpec((SEQ, TILE), lambda i, *_: (0, at(i)))] * 3
            + [
                pl.BlockSpec((SEQ, block), lambda i, *_: (0, then(i))),
                pl.BlockSpec((block, 2 * TILE), lambda i, *_: (then(i), 0)),
                pl.BlockSpec((block, 2 * TILE), lambda i, *_: (then(i), 0)),
                pl.BlockSpec(weight.shape, lambda i, *_: (0, 0)),
            ],
            out_specs=[
                pl.BlockSpec((2, 2, TILE, TILE), lambda i, *_: (at(i), 0, 0, 0)),
                pl.BlockSpec((2, 8, TILE), lambda i, *_: (at(i), 0, 0)),
                pl.BlockSpec((block, 3 * TILE), lambda i, *_: (then(i), 0)),
                pl.BlockSpec((block, 3 * TILE), lambda i, *_: (then(i), 0)),
                pl.BlockSpec((block, 6 * TILE), lambda i, *_: (then(i), 0)),
                pl.BlockSpec((block, width), lambda i, *_: (jnp.clip(i - pairs - blocks, 0, 1), 0)),
                pl.BlockSpec((block, width), lambda i, *_: (jnp.clip(i - pairs - blocks - 2, 0, 1), 0)),
            ],
            scratch_shapes=[
                pltpu.VMEM((3, pairs, SEQ, TILE), BF), pltpu.VMEM((SEQ, TILE), F32), pltpu.VMEM((SEQ, TILE), F32),
            ],
        ),
        out_shape=[
            jax.ShapeDtypeStruct((2 * pairs, 2, TILE, TILE), F32),
            jax.ShapeDtypeStruct((2 * pairs, 8, TILE), F32),
            jax.ShapeDtypeStruct((width, 3 * TILE), BF),
            jax.ShapeDtypeStruct((width, 3 * TILE), F32),
            jax.ShapeDtypeStruct((width, 6 * TILE), BF),
            jax.ShapeDtypeStruct((2 * block, width), F32),
            jax.ShapeDtypeStruct((2 * block, width), F32),
        ],
        compiler_params=pltpu.CompilerParams(vmem_limit_bytes=60 * MIB),
        cost_estimate=SMALL_COST,
        name="attend_back",
    )(core, length, qkv, qkv, qkv, near, mixed, logs, grad, normed, output, output_own, weight)


def low_lanes(shape):
    return lax.broadcasted_iota(jnp.int32, shape, 1) < HEAD_DIM


def turned(tile):
    return pltpu.roll(tile, HEAD_DIM, 1)


def pack_kernel(q_ref, k_ref, v_ref, o_ref, one_ref, two_ref, router_ref, out_ref):
    shard = q_ref.shape[1]
    rows = q_ref.shape[0]
    source = lax.broadcasted_iota(jnp.int32, (shard, 6 * TILE), 0)
    target = lax.broadcasted_iota(jnp.int32, (shard, 6 * TILE), 1)

    def moved(pair_base, last_base):
        want = jnp.where(source < TILE, source + pair_base, source - TILE + last_base)
        return jnp.where(target == want, 1.0, 0.0).astype(BF)

    total = dot(v_ref[...], moved(0, 2 * TILE)) + dot(o_ref[...], moved(TILE, 2 * TILE + HEAD_DIM), TN)
    total = total + dot(q_ref[...], moved(3 * TILE, 5 * TILE)) + dot(k_ref[...], moved(4 * TILE, 5 * TILE + HEAD_DIM))
    out_ref[:, : 6 * TILE] = total.astype(BF)
    experts = router_ref.shape[0]
    own_row = lax.broadcasted_iota(jnp.int32, (rows, rows), 0) == lax.broadcasted_iota(jnp.int32, (rows, rows), 1)

    def column(ref):
        return jnp.sum(jnp.where(own_row, ref[...].astype(F32), 0.0), axis=1, keepdims=True)

    lanes = lax.broadcasted_iota(jnp.int32, (experts, TILE), 1)
    spread = jnp.where(lanes == lax.broadcasted_iota(jnp.int32, (experts, TILE), 0), 1.0, 0.0).astype(BF)
    place = lax.broadcasted_iota(jnp.int32, (rows, TILE), 1)
    small = dot(router_ref[...], spread, TN)
    small = jnp.where(place == experts, column(one_ref), jnp.where(place == experts + 1, column(two_ref), small))
    out_ref[:, 6 * TILE :] = small.astype(BF)


def pack_weights(query, key, value, output, one, two, router):
    rows = query.shape[0]
    return pl.pallas_call(
        pack_kernel,
        out_shape=jax.ShapeDtypeStruct((rows, 7 * TILE), BF),
        compiler_params=pltpu.CompilerParams(vmem_limit_bytes=60 * MIB),
        cost_estimate=SMALL_COST,
        name="pack_weights",
    )(query, key, value, output, one[None], two[None], router.T)


def qkv_kernel(micro_ref, tokens_ref, gain_ref, a_own, a_far, b_own, b_far, qkv_ref, normed_ref, weight_ref, output_ref):
    width = tokens_ref.shape[2]

    @pl.when(pl.program_id(0) == 0)
    def _():
        low = low_lanes((width, TILE))

        def tiles(own, far, pair, low_half):
            at = slice(pair * TILE, (pair + 1) * TILE)
            one, two = own[:, 2 * TILE :].astype(F32), far[:, 2 * TILE :].astype(F32)
            last = jnp.where(low, one, turned(two)) if low_half else jnp.where(low, turned(one), two)
            return own[:, at], far[:, at], last.astype(BF)

        for n, (own, far, pair, low_half) in enumerate(
            ((a_own, a_far, 0, True), (a_own, a_far, 1, False), (b_own, b_far, 0, True))
        ):
            for t, tile in enumerate(tiles(own[...], far[...], pair, low_half)):
                at = 3 * n + t
                weight_ref[:, at * TILE : (at + 1) * TILE] = tile
        for t, tile in enumerate(tiles(b_own[...], b_far[...], 1, False)):
            output_ref[:, t * TILE : (t + 1) * TILE] = tile

    x = tokens_ref[0].astype(F32)
    inverse = lax.rsqrt(jnp.mean(x * x, axis=-1, keepdims=True) + 1e-06)
    normed = (x * inverse * gain_ref[...]).astype(BF)
    normed_ref[...] = normed
    qkv_ref[...] = dot(normed, weight_ref[...]).astype(BF)


def norm_and_project(micro, layer_input, gain, a_own, a_far, b_own, b_far):
    width = layer_input.shape[2]
    block = 256
    cols = 3 * TILE
    whole = lambda rows, n: pl.BlockSpec((rows, n), lambda i, m: (0, 0))
    here = lambda n: pl.BlockSpec((block, n), lambda i, m: (i, 0))
    return pl.pallas_call(
        qkv_kernel,
        grid_spec=pltpu.PrefetchScalarGridSpec(
            num_scalar_prefetch=1,
            grid=(SEQ // block,),
            in_specs=[pl.BlockSpec((1, block, width), lambda i, m: (m[0], i, 0)), whole(1, width)] + [whole(width, cols)] * 4,
            out_specs=[here(3 * cols), here(width), whole(width, 3 * cols), whole(width, cols)],
        ),
        out_shape=[
            jax.ShapeDtypeStruct((SEQ, 3 * cols), BF),
            jax.ShapeDtypeStruct((SEQ, width), BF),
            jax.ShapeDtypeStruct((width, 3 * cols), BF),
            jax.ShapeDtypeStruct((width, cols), BF),
        ],
        compiler_params=pltpu.CompilerParams(vmem_limit_bytes=40 * MIB),
        cost_estimate=SMALL_COST,
        name="norm_and_project",
    )(micro, layer_input, gain, a_own, a_far, b_own, b_far)


def middle_kernel(
    blocks, per, micro_ref, tokens_ref, mixed_ref, other_ref, own_ref, far_ref, gain_ref, code_ref, residual_ref, *refs
):
    sent_refs, normed = refs[:-1], refs[-1]
    step = pl.program_id(0)
    rows = tokens_ref.shape[1]

    @pl.when(step < blocks)
    def _():
        total = tokens_ref[0].astype(F32) + dot(mixed_ref[...], own_ref[...], NT) + dot(other_ref[...], far_ref[...], NT)
        residual_ref[...] = total
        inverse = lax.rsqrt(jnp.mean(total * total, axis=-1, keepdims=True) + 1e-06)
        normed[pl.ds(pl.multiple_of(step * rows, rows), rows), :] = (total * inverse * gain_ref[...]).astype(BF)

    for c, sent_ref in enumerate(sent_refs):

        @pl.when((step >= blocks + c * per) & (step < blocks + (c + 1) * per))
        def _(sent_ref=sent_ref):
            block = sent_ref.shape[0]
            ids = lax.broadcasted_iota(jnp.int32, (block, 1), 0) + (step - blocks) * block
            hot = jnp.where((ids == code_ref[:1]) | (ids == code_ref[1:2]), 1.0, 0.0).astype(BF)
            sent_ref[...] = dot(hot, normed[...]).astype(BF)


def residual_and_rows(micro, layer_input, mixed, other, output_own, output_far, gain, code, count, chunks):
    width = layer_input.shape[2]
    block = 256
    blocks = SEQ // block
    send = 320
    cols = mixed.shape[1]
    per = count // send
    at = lambda i: jnp.minimum(i, blocks - 1)
    whole = lambda arr: pl.BlockSpec(arr.shape, lambda i, m: (0, 0))
    here = lambda n: pl.BlockSpec((block, n), lambda i, m: (at(i), 0))

    def sent(c):
        return pl.BlockSpec((send, width), lambda i, m: (jnp.clip(i - blocks - c * per, 0, per - 1), 0))

    return pl.pallas_call(
        functools.partial(middle_kernel, blocks, per),
        grid_spec=pltpu.PrefetchScalarGridSpec(
            num_scalar_prefetch=1,
            grid=(blocks + chunks * per,),
            in_specs=[
                pl.BlockSpec((1, block, width), lambda i, m: (m[0], at(i), 0)),
                here(cols), here(cols), whole(output_own), whole(output_far), whole(gain), whole(code),
            ],
            out_specs=[here(width)] + [sent(c) for c in range(chunks)],
            scratch_shapes=[pltpu.VMEM((SEQ, width), BF)],
        ),
        out_shape=[jax.ShapeDtypeStruct((SEQ, width), F32)] + [jax.ShapeDtypeStruct((count, width), BF)] * chunks,
        compiler_params=pltpu.CompilerParams(vmem_limit_bytes=40 * MIB),
        cost_estimate=SMALL_COST,
        name="residual_and_rows",
    )(micro, layer_input, mixed, other, output_own, output_far, gain, code)


def picked_rows(first, second, segments):
    total = None
    start = 0
    for rows in segments:
        length = rows.shape[0]
        ids = lax.broadcasted_iota(jnp.int32, (1, length), 1) + start
        hot = []
        for at in range(0, first.shape[0], STRIP):
            one, two = first[at : at + STRIP], second[at : at + STRIP]
            hot.append(jnp.where((one == ids) | (two == ids), 1.0, 0.0).astype(BF))
        total = put(total, dot(jnp.concatenate(hot, 0), rows))
        start += length
    return total


def put(a, b):
    return b if a is None else a + b


def folded(product):
    return jnp.sum(product.reshape(product.shape[0] // 8, 8, product.shape[1]), axis=0)


def as_column(eight):
    ones = jnp.ones((16, TILE), BF)
    high = eight.astype(BF)
    rest = (eight - high.astype(F32)).astype(BF)
    return dot(jnp.concatenate([high, rest], 0), ones, TN)


def combine_kernel(experts, half, spare, micro_ref, core_ref, length_ref, *refs):
    info_ref, grad_ref, residual_ref, mixed_ref, gain_ref, router_ref, output_ref = refs[:7]
    backs = refs[7:-9]
    (total_ref, mixed_grad_ref, extra_ref, far_ref, own_ref, acc_ref, router_acc, gain_acc, tables) = refs[-9:]
    block = residual_ref.shape[0]
    step = pl.program_id(0)
    count = len(backs) // 2

    @pl.when(step == 0)
    def _():
        place = lax.broadcasted_iota(jnp.int32, (experts, 1), 0)
        for n, back in enumerate((backs[count - 1], backs[2 * count - 1])):
            table = jnp.zeros((experts, back.shape[2]), F32)
            for e in range(experts):
                row = back[e, spare : spare + 16, :].astype(F32)[:1]
                table = jnp.where(place == e, row, table)
            for piece in range(3):
                at = (3 * n + piece) * experts
                tables[at : at + experts] = table[:, piece * half : (piece + 1) * half]

    info = jnp.transpose(info_ref[...])
    number = lambda n: info[:, n : n + 1]
    columns = lax.broadcasted_iota(jnp.int32, (1, half), 1)
    lanes = lax.broadcasted_iota(jnp.int32, (1, 6 * experts), 1)
    table = tables[...].astype(BF)
    values = []
    for k in range(2):
        slot = number(4 + k)
        hot = jnp.where(columns == lax.rem(slot, half), 1.0, 0.0).astype(BF)
        found = dot(hot, table, NT)
        wanted = jnp.where(slot // half == core_ref[0], 0, 3 * experts) + number(2 + k)
        away = lanes - wanted
        hit = (away == 0) | (away == experts) | (away == 2 * experts)
        values.append(jnp.sum(jnp.where(hit, found, 0.0), axis=1, keepdims=True))
    wide = lax.broadcasted_iota(jnp.int32, (1, TILE), 1)
    is_first, is_second = wide == number(2), wide == number(3)
    residual = residual_ref[...]
    gain = gain_ref[...]
    inverse = lax.rsqrt(jnp.mean(residual * residual, axis=-1, keepdims=True) + 1e-06)
    plain = residual * inverse
    normed = (plain * gain).astype(BF)
    logits = dot(normed, router_ref[...])
    gap = jnp.sum(jnp.where(is_first, logits, 0.0) - jnp.where(is_second, logits, 0.0), axis=1, keepdims=True)
    small = jnp.exp(-jnp.abs(gap))
    logit = small / ((1.0 + small) * (1.0 + small)) * (values[0] - values[1])
    logit_grad = jnp.where(is_first, logit, jnp.where(is_second, -logit, 0.0)).astype(BF)
    segments = [b[...].reshape(b.shape[0] * b.shape[1], b.shape[2]) for b in backs]
    normed_grad = picked_rows(number(0), number(1), segments) + dot(logit_grad, router_ref[...], NT)
    scaled = normed_grad * gain
    mean = jnp.mean(scaled * plain, axis=-1, keepdims=True)
    place = lax.broadcasted_iota(jnp.int32, (block, 1), 0) + step * block
    grad_out = jnp.where(place < length_ref[0], grad_ref[0].astype(F32), 0.0)
    total = grad_out + inverse * (scaled - plain * mean)

    @pl.when(step == core_ref[0])
    def _():
        total_ref[...] = total

    branch = total.astype(BF)
    mixed_grad_ref[...] = dot(branch, output_ref[...]).astype(BF)
    router_part = dot(logit_grad, normed, TN)
    gain_part = folded(normed_grad * plain)
    output_part = dot(mixed_ref[...], branch, TN)

    @pl.when(step == 0)
    def _():
        router_acc[...] = router_part
        gain_acc[...] = gain_part
        acc_ref[...] = output_part

    @pl.when(step > 0)
    def _():
        router_acc[...] += router_part
        gain_acc[...] += gain_part
        acc_ref[...] += output_part

    @pl.when(step == pl.num_programs(0) - 1)
    def _():
        extra_ref[...] = jnp.transpose(router_acc[...]) + jnp.where(wide == experts + 1, as_column(gain_acc[...]), 0.0)
        parts = jnp.transpose(acc_ref[...])
        far_ref[...] = parts[:, TILE:].astype(BF)
        own_ref[:, :TILE] = parts[:, :TILE]
        own_ref[:, TILE:] = parts[:, 2 * TILE :]


def combine(micro, core, length, info, out_grad, residual, mixed, gain, router, output_own, backs, half, spare):
    width = residual.shape[1]
    block = 512
    cols = mixed.shape[1]
    whole = lambda arr: pl.BlockSpec(arr.shape, lambda i, *_: (0,) * arr.ndim)
    fixed = lambda rows, n: pl.BlockSpec((rows, n), lambda i, *_: (0, 0))
    here = lambda n: pl.BlockSpec((block, n), lambda i, *_: (i, 0))
    experts = backs[0].shape[0]
    return pl.pallas_call(
        functools.partial(combine_kernel, experts, half, spare),
        grid_spec=pltpu.PrefetchScalarGridSpec(
            num_scalar_prefetch=3,
            grid=(SEQ // block,),
            in_specs=[
                pl.BlockSpec((8, block), lambda i, *_: (0, i)),
                pl.BlockSpec((1, block, width), lambda i, m, *_: (m[0], i, 0)),
                here(width), here(cols), whole(gain), whole(router), whole(output_own),
            ]
            + [whole(x) for x in backs],
            out_specs=[fixed(block, width), here(cols), fixed(width, TILE), fixed(width, 2 * TILE), fixed(width, 2 * TILE)],
            scratch_shapes=[
                pltpu.VMEM((cols, width), F32),
                pltpu.VMEM((TILE, width), F32),
                pltpu.VMEM((8, width), F32),
                pltpu.VMEM((6 * experts, half), F32),
            ],
        ),
        out_shape=[
            jax.ShapeDtypeStruct((block, width), F32),
            jax.ShapeDtypeStruct((SEQ, cols), BF),
            jax.ShapeDtypeStruct((width, TILE), F32),
            jax.ShapeDtypeStruct((width, 2 * TILE), BF),
            jax.ShapeDtypeStruct((width, 2 * TILE), F32),
        ],
        compiler_params=pltpu.CompilerParams(vmem_limit_bytes=60 * MIB),
        cost_estimate=SMALL_COST,
        name="combine",
    )(micro, core, length, info, out_grad, residual, mixed, gain, router, output_own, *backs)


def both_kernel(
    lane, micro_ref, core_ref, length_ref, part_ref, got_ref, tokens_ref, gain_ref, grad_ref,
    info_ref, residual_ref, own_ref, far_ref, out_ref, extra_ref, acc_ref,
):
    block = residual_ref.shape[0]
    info = jnp.transpose(info_ref[...])
    place = lax.broadcasted_iota(jnp.int32, (block, 1), 0) + (core_ref[0] * 2 + pl.program_id(0)) * block
    rows = residual_ref[...] + picked_rows(info[:, 6:7], info[:, 7:8], (own_ref[...], far_ref[...]))
    out_ref[0] = jnp.where(place < length_ref[0], rows, 0.0).astype(BF)
    normed_grad = got_ref[...] + part_ref[...]
    x = tokens_ref[0].astype(F32)
    inverse = lax.rsqrt(jnp.mean(x * x, axis=-1, keepdims=True) + 1e-06)
    plain = x * inverse
    scaled = normed_grad * gain_ref[...]
    mean = jnp.mean(scaled * plain, axis=-1, keepdims=True)
    out_ref[1] = (grad_ref[...] + inverse * (scaled - plain * mean)).astype(BF)
    wide = lax.broadcasted_iota(jnp.int32, (1, TILE), 1)
    part = folded(normed_grad * plain)

    @pl.when(pl.program_id(0) == 0)
    def _():
        acc_ref[...] = part

    @pl.when(pl.program_id(0) == 1)
    def _():
        extra_ref[...] = jnp.where(wide == lane, as_column(acc_ref[...] + part), 0.0)


def both_rows(lane, micro, core, length, part, got, layer_input, gain, residual_grad, info, residual, own, far):
    width = part.shape[1]
    plain = pl.BlockSpec((256, width), lambda i, *_: (i, 0))
    block = 256
    here = lambda n: pl.BlockSpec((block, n), lambda i, m, c, *_: (c[0] * 2 + i, 0))
    whole = lambda arr: pl.BlockSpec(arr.shape, lambda i, *_: (0, 0))
    return pl.pallas_call(
        functools.partial(both_kernel, lane),
        grid_spec=pltpu.PrefetchScalarGridSpec(
            num_scalar_prefetch=3,
            grid=(2,),
            in_specs=[
                plain,
                plain,
                pl.BlockSpec((1, block, width), lambda i, m, c, *_: (m[0], c[0] * 2 + i, 0)),
                whole(gain),
                plain,
                pl.BlockSpec((8, block), lambda i, m, c, *_: (0, c[0] * 2 + i)),
                here(width),
                whole(own),
                whole(far),
            ],
            out_specs=[
                pl.BlockSpec((2, block, width), lambda i, *_: (0, i, 0)),
                pl.BlockSpec((width, TILE), lambda i, *_: (0, 0)),
            ],
            scratch_shapes=[pltpu.VMEM((8, width), F32)],
        ),
        out_shape=[jax.ShapeDtypeStruct((2, 2 * block, width), BF), jax.ShapeDtypeStruct((width, TILE), F32)],
        compiler_params=pltpu.CompilerParams(vmem_limit_bytes=40 * MIB),
        cost_estimate=SMALL_COST,
        name="both_rows",
    )(micro, core, length, part, got, layer_input, gain, residual_grad, info, residual, own, far)


def sum_kernel(kept, own, got, early, late, late_far, table, sum_ref):
    low = low_lanes(early.shape)
    sum_ref[:, : 3 * TILE] = (own[...] + got[...].astype(F32)).astype(BF)
    extra = early[...] + late[...] + late_far[...] + table[...]
    high = extra.astype(BF)
    rest = extra - high.astype(F32)
    if kept <= HEAD_DIM:
        sum_ref[:, 3 * TILE :] = jnp.where(low, high.astype(F32), turned(rest)).astype(BF)
    else:
        sum_ref[:, 3 * TILE : 4 * TILE] = high
        sum_ref[:, 4 * TILE :] = rest.astype(BF)


def packed_sums(kept, *parts):
    width = parts[0].shape[0]
    cols = (4 if kept <= HEAD_DIM else 5) * TILE
    block = 256
    here = lambda n: pl.BlockSpec((block, n), lambda i: (i, 0))
    return pl.pallas_call(
        functools.partial(sum_kernel, kept),
        grid=(width // block,),
        in_specs=[here(x.shape[1]) for x in parts],
        out_specs=here(cols),
        out_shape=jax.ShapeDtypeStruct((width, cols), BF),
        compiler_params=pltpu.CompilerParams(vmem_limit_bytes=40 * MIB),
        cost_estimate=SMALL_COST,
        name="packed_sums",
    )(*parts)


def added(parts_ref):
    total = parts_ref[0].astype(F32)
    for n in range(1, parts_ref.shape[0]):
        total = total + parts_ref[n].astype(F32)
    return total


def first_kernel(parts_ref, own_ref, far_ref):
    total = added(parts_ref)
    own_ref[...] = total[:, : 3 * TILE]
    far_ref[...] = total[:, 3 * TILE :]


def first_sums(parts):
    rows = parts.shape[1]
    return pl.pallas_call(
        first_kernel,
        out_shape=[jax.ShapeDtypeStruct((rows, 3 * TILE), F32)] * 2,
        compiler_params=pltpu.CompilerParams(vmem_limit_bytes=40 * MIB),
        cost_estimate=SMALL_COST,
        name="first_sums",
    )(parts)


def final_kernel(kept, parts_ref, own_ref, got_ref, q_ref, k_ref, v_ref, o_ref, small_ref):
    total = added(parts_ref)
    other = own_ref[...] + got_ref[...]
    tile = lambda arr, t: arr[:, t * TILE : (t + 1) * TILE]
    q_ref[:, :TILE] = tile(total, 0)
    q_ref[:, TILE:] = tile(other, 0)[:, :HEAD_DIM]
    k_ref[:, :TILE] = tile(total, 1)
    k_ref[:, TILE:] = turned(tile(other, 0))[:, :HEAD_DIM]
    v_ref[:, :TILE] = tile(total, 2)
    v_ref[:, TILE:] = tile(other, 1)[:, :HEAD_DIM]
    o_ref[:, :TILE] = tile(other, 2)
    o_ref[:, TILE:] = turned(tile(other, 1))[:, :HEAD_DIM]
    small_ref[...] = tile(total, 3) + (turned(tile(total, 3)) if kept <= HEAD_DIM else tile(total, 4))


def final_sums(kept, parts, own, got, shard):
    rows = parts.shape[1]
    return pl.pallas_call(
        functools.partial(final_kernel, kept),
        out_shape=[jax.ShapeDtypeStruct((rows, shard), F32)] * 4 + [jax.ShapeDtypeStruct((rows, TILE), F32)],
        compiler_params=pltpu.CompilerParams(vmem_limit_bytes=40 * MIB),
        cost_estimate=SMALL_COST,
        name="final_sums",
    )(parts, own, got)


def pair_gate(logits, own, other):
    lanes = lax.broadcasted_iota(jnp.int32, logits.shape, 1)
    gap = jnp.sum(
        jnp.where(lanes == own, logits, 0.0) - jnp.where(lanes == other, logits, 0.0), axis=1, keepdims=True
    )
    small = jnp.exp(-jnp.abs(gap))
    return jnp.where(gap >= 0.0, 1.0, small) / (1.0 + small)


def expert_kernel(lead, chunk, half, me_ref, partner_ref, rows_ref, grads_ref, router_ref, *refs):
    before, refs = (refs[0], refs[1:]) if lead is not None and lead > 0 else (None, refs)
    firsts, seconds = refs[:4], refs[4:8]
    back_ref, active_ref, slope_ref, gated_ref, gate_ref, mass_ref = refs[8:]
    rows = rows_ref[...]
    grads = grads_ref[...]
    gate = pair_gate(dot(rows, router_ref[...]), me_ref[0], partner_ref[...])
    gated_ref[...] = (gate * grads.astype(F32)).astype(BF)
    gate_ref[...] = jnp.broadcast_to(gate, gate_ref.shape)
    masses = [None] * (rows.shape[0] // STRIP)
    back = None
    width = firsts[0].shape[1]
    step = 256
    places = [(r, c) for r in range(4) for c in range(0, width, step)]

    def products(r, c):
        return dot(rows, firsts[r][:, c : c + step]), dot(grads, seconds[r][c : c + step, :], NT)

    ahead = products(*places[0])
    for n, (r, c) in enumerate(places):
        x, plain = ahead
        if n + 1 < len(places):
            ahead = products(*places[n + 1])
        place = slice(r * width + c, r * width + c + step)
        for at in range(0, rows.shape[0], STRIP):
            strip = slice(at, at + STRIP)
            value, flow = x[strip], plain[strip]
            square = value * value
            bent = jnp.tanh(value * (GELU_C + (GELU_C * GELU_A) * square))
            rise = 0.5 + 0.5 * bent
            active = value * rise
            slope = rise + active * (1.0 - bent) * (GELU_C + (3.0 * GELU_C * GELU_A) * square)
            low = active.astype(BF)
            active_ref[strip, place] = low
            slope_ref[strip, place] = (gate[strip] * flow * slope).astype(BF)
            part = low.astype(F32) * flow
            masses[at // STRIP] = put(masses[at // STRIP], part[:, :TILE] + part[:, TILE:])
        if c + step == width and r > 0:
            back = put(back, dot(slope_ref[:, (r - 1) * width : r * width], firsts[r - 1][...], NT))
    back = put(back, dot(slope_ref[:, 3 * width :], firsts[3][...], NT))
    back = back.astype(BF)
    mass = jnp.sum(jnp.concatenate(masses, 0), axis=1, keepdims=True)
    if lead is None:
        back_ref[...] = back
        mass_ref[...] = jnp.broadcast_to(mass, mass_ref.shape)
        return
    count = rows.shape[0] // chunk
    number = lax.broadcasted_iota(jnp.int32, (rows.shape[0], 1), 0)
    lanes = lax.broadcasted_iota(jnp.int32, (1, rows.shape[1]), 1)
    inside = lax.rem(number, chunk)
    spread = jnp.zeros(rows.shape, F32)
    for piece in range(3):
        high = mass.astype(BF).astype(F32)
        spread = jnp.where(lanes == piece * half + lead + inside, high, spread)
        mass = mass - high
    own = jnp.where(number // chunk == lax.broadcasted_iota(jnp.int32, (1, TILE), 1), 1.0, 0.0).astype(BF)
    line = dot(own, spread.astype(BF), TN)
    if before is None:
        back_ref[...] = back
        for e in range(count):
            mass_ref[e] = line[e : e + 1].astype(BF)
    else:
        back_ref[:, :chunk] = back.reshape(count, chunk, back.shape[1])
        row = lax.broadcasted_iota(jnp.int32, (16, 1), 0)
        for e in range(count):
            both = line[e : e + 1] + before[e].astype(F32)
            back_ref[e, chunk:] = jnp.where(row == 0, both, 0.0).astype(BF)


def row_block(total):
    return 320 if total % 320 == 0 else total


def expert_rows_pass(lead, chunk, half, me, partner, rows, grads, router, before, firsts, seconds):
    total, width = rows.shape
    block = row_block(total)
    experts = total // chunk
    hidden = sum(f.shape[1] for f in firsts)
    here = lambda cols: pl.BlockSpec((block, cols), lambda i: (i, 0))
    whole = lambda arr: pl.BlockSpec(arr.shape, lambda i: (0, 0))
    lines = pl.BlockSpec((block // chunk, 1, width), lambda i: (i, 0, 0))
    back_shape, back_spec = (total, width), here(width)
    mass_shape, mass_spec, mass_kind = (experts, 1, width), lines, BF
    if lead is None:
        mass_shape, mass_spec, mass_kind = (total, TILE), here(TILE), F32
    elif before is not None:
        back_shape = (experts, chunk + 16, width)
        back_spec = pl.BlockSpec((block // chunk, chunk + 16, width), lambda i: (i, 0, 0))
    return pl.pallas_call(
        functools.partial(expert_kernel, lead, chunk, half),
        grid=(total // block,),
        in_specs=[pl.BlockSpec(memory_space=pltpu.SMEM), here(1), here(width), here(width), whole(router)]
        + ([lines] if before is not None else [])
        + [whole(w) for w in firsts]
        + [whole(w) for w in seconds],
        out_specs=[back_spec, here(hidden), here(hidden), here(width), here(TILE), mass_spec],
        out_shape=[
            jax.ShapeDtypeStruct(back_shape, BF),
            jax.ShapeDtypeStruct((total, hidden), BF),
            jax.ShapeDtypeStruct((total, hidden), BF),
            jax.ShapeDtypeStruct((total, width), BF),
            jax.ShapeDtypeStruct((total, TILE), F32),
            jax.ShapeDtypeStruct(mass_shape, mass_kind),
        ],
        compiler_params=pltpu.CompilerParams(vmem_limit_bytes=56 * MIB),
        cost_estimate=SMALL_COST,
        name="expert_rows",
    )(me, partner, rows, grads, router, *([before] if before is not None else []), *firsts, *seconds)


def weight_parts(count, refs):
    rows, slopes, active, gated = (refs[n * count : (n + 1) * count] for n in range(4))
    first, second = None, None
    for n in range(count):
        first = put(first, dot(rows[n][...], slopes[n][...], TN))
        second = put(second, dot(active[n][...], gated[n][...], TN))
    return first, second


def cross_kernel(count, *refs):
    first, second = weight_parts(count, refs)
    refs[-1][0, 0] = first.astype(BF)
    refs[-1][0, 1] = second.astype(BF)


def kept_kernel(count, *refs):
    got_ref, far_ref, kept_ref = refs[-3:]
    first, second = weight_parts(count, refs)
    first = first + got_ref[0, 0].astype(F32)
    second = second + got_ref[0, 1].astype(F32)

    @pl.when(pl.program_id(0) == 0)
    def _():
        far_ref[0] = first.astype(BF)
        far_ref[1] = second.astype(BF)

    @pl.when(pl.program_id(0) == 1)
    def _():
        kept_ref[0] = first
        kept_ref[1] = second


def weight_specs(rows, slopes, quarter):
    total, width = rows[0].shape
    hidden = slopes[0].shape[1] // 4
    whole = pl.BlockSpec((total, width), lambda i: (0, 0))
    part = pl.BlockSpec((total, hidden), lambda i: (0, quarter(i)))
    count = len(rows)
    return width, hidden, [whole] * count + [part] * (2 * count) + [whole] * count


def cross_weight_grads(rows, slopes, active, gated):
    width, hidden, specs = weight_specs(rows, slopes, lambda i: 2 + i)
    return pl.pallas_call(
        functools.partial(cross_kernel, len(rows)),
        grid=(2,),
        in_specs=specs,
        out_specs=pl.BlockSpec((1, 2, width, hidden), lambda i: (i, 0, 0, 0)),
        out_shape=jax.ShapeDtypeStruct((2, 2, width, hidden), BF),
        compiler_params=pltpu.CompilerParams(vmem_limit_bytes=56 * MIB),
        cost_estimate=SMALL_COST,
        name="cross_weight_grads",
    )(*rows, *slopes, *active, *gated)


def kept_weight_grads(rows, slopes, active, gated, got):
    width, hidden, specs = weight_specs(rows, slopes, lambda i: 1 - i)
    fixed = pl.BlockSpec((2, width, hidden), lambda i: (0, 0, 0))
    return pl.pallas_call(
        functools.partial(kept_kernel, len(rows)),
        grid=(2,),
        in_specs=specs + [pl.BlockSpec((1, 2, width, hidden), lambda i: (1 - i, 0, 0, 0))],
        out_specs=[fixed, fixed],
        out_shape=[
            jax.ShapeDtypeStruct((2, width, hidden), BF),
            jax.ShapeDtypeStruct((2, width, hidden), F32),
        ],
        compiler_params=pltpu.CompilerParams(vmem_limit_bytes=56 * MIB),
        cost_estimate=SMALL_COST,
        name="kept_weight_grads",
    )(*rows, *slopes, *active, *gated, got)


def result_kernel(chunks, *refs):
    active, gates, seconds, out_ref = refs[:chunks], refs[chunks : 2 * chunks], refs[2 * chunks : -1], refs[-1]
    for c in range(chunks):

        @pl.when(pl.program_id(0) == c)
        def _(c=c):
            width = seconds[0].shape[0]
            total = None
            for r, second in enumerate(seconds):
                total = put(total, dot(active[c][:, r * width : (r + 1) * width], second[...]))
            rows = (total * gates[c][:, :1]).astype(BF)
            if chunks > 1:
                out_ref[:, 0] = rows.reshape(out_ref.shape[0], out_ref.shape[2], out_ref.shape[3])
            else:
                out_ref[...] = rows


def expert_results(active, gates, seconds, experts):
    chunks = len(active)
    total, hidden = active[0].shape
    width = seconds[0].shape[1]
    block = row_block(total)
    steps = total // block

    def here(c, cols):
        return pl.BlockSpec((block, cols), lambda g, i: (jnp.where(g == c, i, jnp.where(g < c, 0, steps - 1)), 0))

    chunk = total // experts
    if chunks > 1:
        shape = (experts, chunks, chunk, width)
        out_spec = pl.BlockSpec((block // chunk, 1, chunk, width), lambda g, i: (i, g, 0, 0))
    else:
        shape = (total, width)
        out_spec = pl.BlockSpec((block, width), lambda g, i: (i, 0))
    out = pl.pallas_call(
        functools.partial(result_kernel, chunks),
        grid=(chunks, steps),
        in_specs=[here(c, hidden) for c in range(chunks)]
        + [here(c, TILE) for c in range(chunks)]
        + [pl.BlockSpec(w.shape, lambda g, i: (0, 0)) for w in seconds],
        out_specs=out_spec,
        out_shape=jax.ShapeDtypeStruct(shape, BF),
        compiler_params=pltpu.CompilerParams(vmem_limit_bytes=56 * MIB),
        cost_estimate=SMALL_COST,
        name="expert_results",
    )(*active, *gates, *seconds)
    return out.reshape(experts, chunks * chunk, width)


def last_sum_kernel(kept_ref, y_ref, out_first, out_second):
    for n, out in enumerate((out_first, out_second)):
        out[...] = kept_ref[n] + y_ref[n].astype(F32)


def last_sums(kept, got_y):
    _, width, hidden = kept.shape
    block = 256
    here = pl.BlockSpec((block, hidden), lambda i: (i, 0))
    part = pl.BlockSpec((2, block, hidden), lambda i: (0, i, 0))
    return pl.pallas_call(
        last_sum_kernel,
        grid=(width // block,),
        in_specs=[part, part],
        out_specs=[here, here],
        out_shape=[jax.ShapeDtypeStruct((width, hidden), F32)] * 2,
        compiler_params=pltpu.CompilerParams(vmem_limit_bytes=40 * MIB),
        cost_estimate=SMALL_COST,
        name="last_sums",
    )(kept, got_y)


def send_kernel(micro_ref, code_ref, rows_ref, out_ref):
    block = out_ref.shape[0]
    ids = lax.broadcasted_iota(jnp.int32, (block, 1), 0) + pl.program_id(0) * block
    hot = jnp.where((ids == code_ref[:1]) | (ids == code_ref[1:2]), 1.0, 0.0).astype(BF)
    out_ref[...] = dot(hot, rows_ref[0]).astype(BF)


def send_rows(micro, code, rows, count):
    width = rows.shape[2]
    block = next(b for b in (336, 320, 384, count) if count % b == 0)
    return pl.pallas_call(
        send_kernel,
        grid_spec=pltpu.PrefetchScalarGridSpec(
            num_scalar_prefetch=1,
            grid=(count // block,),
            in_specs=[
                pl.BlockSpec(code.shape, lambda i, m: (0, 0)),
                pl.BlockSpec((1, SEQ, width), lambda i, m: (m[0], 0, 0)),
            ],
            out_specs=pl.BlockSpec((block, width), lambda i, m: (i, 0)),
        ),
        out_shape=jax.ShapeDtypeStruct((count, width), BF),
        compiler_params=pltpu.CompilerParams(vmem_limit_bytes=40 * MIB),
        cost_estimate=SMALL_COST,
        name="send_rows",
    )(micro, code, rows)


def place_kernel(place_ref, one_ref, two_ref, *refs):
    for n, piece in enumerate((one_ref, two_ref)):

        @pl.when(pl.program_id(0) == n)
        def _(piece=piece):
            for k, out_ref in enumerate(refs[-2:]):
                out_ref[0] = piece[k]


def place_pieces(places, pieces, before=()):
    two, rows, width = pieces[0].shape
    whole = pl.BlockSpec(pieces[0].shape, lambda i, place_ref: (0, 0, 0))
    return pl.pallas_call(
        place_kernel,
        grid_spec=pltpu.PrefetchScalarGridSpec(
            num_scalar_prefetch=1,
            grid=(2,),
            in_specs=[whole] * 2 + [pl.BlockSpec(memory_space=pl.ANY)] * len(before),
            out_specs=[pl.BlockSpec((1, rows, width), lambda i, place_ref: (place_ref[i], 0, 0))] * two,
        ),
        out_shape=[jax.ShapeDtypeStruct((4, rows, width), pieces[0].dtype)] * two,
        input_output_aliases={3: 0, 4: 1} if before else {},
        compiler_params=pltpu.CompilerParams(vmem_limit_bytes=40 * MIB),
        cost_estimate=SMALL_COST,
        name="place_pieces",
    )(places, *pieces, *before)


def swap(value, axis, count, bit):
    return lax.ppermute(value, axis, [(i, i ^ bit) for i in range(count)])


def all_to_all(value):
    return lax.all_to_all(value, "dp", split_axis=0, concat_axis=0, tiled=True)


def together(*values):
    return lax.optimization_barrier(values)


def local(
    layer_input, out_grad, first_gain, query_weight, key_weight, value_weight, output_weight,
    position_bias, second_gain, router_weight, expert_in, expert_out, seq_lengths, routes,
):
    micro_count, tok_rows, width = layer_input.shape
    dp_count = lax.axis_size("dp")
    expert_count = router_weight.shape[1]
    shard = query_weight.shape[1]
    heads_here = position_bias.shape[0]
    assert lax.axis_size("tensor") == 4 and micro_count == 2 and expert_count == dp_count
    assert tok_rows == SEQ and seq_lengths.shape[1] == 1
    capacity = max(8, 8 * (10 * tok_rows // (32 * expert_count)))
    half = capacity // 2
    stride = 8 * (half // 8 + 1)
    by_lines = dp_count == 8
    chunks = 2 if half % 32 == 0 else 1
    chunk = half // chunks
    chunk_rows = expert_count * chunk
    rows_here = query_weight.shape[0]
    me = lax.axis_index("dp")
    rank = lax.axis_index("tensor")
    micro = rank // 2
    core = rank % 2

    def swap_y(value):
        return swap(value, "tensor", 4, 2)

    def swap_core(value):
        return swap(value, "tensor", 4, 1)

    micro_arg = micro.reshape(1).astype(jnp.int32)
    core_arg = core.reshape(1).astype(jnp.int32)

    packed = pack_weights(query_weight, key_weight, value_weight, output_weight, first_gain, second_gain, router_weight)
    three = 3 * TILE

    def doubled(stacked, bit, axis=0):
        other = swap(stacked, "dp", dp_count, bit)
        high = (me & bit) != 0
        pair = jnp.where(high, jnp.stack([other, stacked], axis + 1), jnp.stack([stacked, other], axis + 1))
        return pair.reshape(stacked.shape[:axis] + (-1,) + stacked.shape[axis + 1 :])

    stacked = packed[None]
    bit = dp_count // 2
    while bit > 1:
        stacked = doubled(stacked, bit)
        bit //= 2
    length = lax.dynamic_index_in_dim(seq_lengths, micro, 0, keepdims=False)
    route = lax.dynamic_index_in_dim(routes, micro, 0, keepdims=False).T
    expert_ids = jnp.arange(expert_count, dtype=jnp.int32)
    named = (expert_ids[:, None, None] == route[None]).astype(jnp.int32)
    per_token = jnp.sum(named, axis=1, dtype=jnp.int32)
    earlier = jnp.cumsum(per_token, axis=1, dtype=jnp.int32) - per_token
    slot = jnp.sum(named * earlier[:, None, :], axis=0, dtype=jnp.int32)
    here = slot // half == core
    within = slot % half
    chunk_of = within // chunk
    inside = within % chunk
    spare = 16 * -(-chunk // 16)
    last_stride = spare + 16
    last = (chunks - 1) * chunk_rows
    code_back = jnp.where(
        chunk_of == chunks - 1, last + route * last_stride + inside, chunk_of * chunk_rows + route * chunk + inside
    )
    code_back = code_back + jnp.where(here, 0, last + expert_count * last_stride)
    code_result = route * half + within + jnp.where(here, 0, expert_count * half)
    info = jnp.concatenate([code_back, route, slot, code_result], 0)

    code_grads = jnp.where(here, route * stride + within, -1)
    valid = jnp.arange(SEQ, dtype=jnp.int32) < length[0]
    ids = jnp.arange(expert_count * stride, dtype=jnp.int32)[:, None]
    partner = jnp.sum(
        jnp.where(ids == code_grads[:1], route[1:], 0) + jnp.where(ids == code_grads[1:], route[:1], 0), axis=1, dtype=jnp.int32
    )
    grads_sent = send_rows(micro_arg, jnp.where(valid[None], code_grads, -1), out_grad, expert_count * stride)
    grads_sent = grads_sent.reshape(expert_count, stride, width)
    partner_row = jnp.pad(partner.reshape(expert_count, stride)[:, :half].astype(BF), ((0, 0), (0, width - half)))
    grads_sent = grads_sent.at[:, half].set(partner_row)
    stacked, grads_sent, position_bias = together(stacked, grads_sent, position_bias)
    if by_lines:
        lines = [list(range(x, dp_count, 2)) for x in range(2)]
        grads_z = lax.all_to_all(
            grads_sent.reshape(dp_count // 2, 2, stride, width), "dp", split_axis=0, concat_axis=0,
            axis_index_groups=lines, tiled=True,
        )

    first_own = expert_in[0]
    second_own = expert_out[0]
    part_b = stacked[:, :, :three]
    far_b = swap_y(part_b)
    part_a = doubled(stacked[:, :, three:], 1)
    part_a, far_b = together(part_a, far_b)
    pair_b = jnp.stack([part_b, far_b])
    a_own = part_a[:, :, :three]
    a_far = swap_y(a_own).reshape(width, three)
    a_own = a_own.reshape(width, three)
    pair_b = doubled(pair_b, 1, 1).reshape(2, width, three)
    if by_lines:
        a_far, pair_b, first_own = together(a_far, pair_b, first_own)
    else:
        a_far, pair_b, grads_sent, first_own = together(a_far, pair_b, grads_sent, first_own)
    first_y = swap_y(first_own)
    small_all = part_a[:, :, three:].reshape(width, TILE)
    gain_one = small_all[:, expert_count].astype(F32)[None]
    gain_two = small_all[:, expert_count + 1].astype(F32)[None]
    router_wide = small_all
    far_bias = swap_y(position_bias)
    bias = jnp.concatenate([position_bias[:2], far_bias[:2], position_bias[2:], far_bias[2:]], 0)
    head_total = bias.shape[0]
    hot_const = jnp.asarray(NEAR_HOT, dtype=BF)
    near = dot(bias, hot_const) - bias[:, NB - 1 :].astype(F32)
    near = near.reshape(head_total, 2, TILE, TILE)
    places = jnp.arange(TILE, dtype=jnp.int32)
    causal = jnp.stack([places[None, :] <= places[:, None], jnp.ones((TILE, TILE), bool)])
    near = jnp.where(causal[None], near, NEG)

    if by_lines:
        high = (me & 1) != 0
    else:
        grads_here = all_to_all(grads_sent)

    qkv, normed_one, qkv_weight, output_own = norm_and_project(
        micro_arg, layer_input, gain_one, a_own, a_far, pair_b[0], pair_b[1]
    )
    output_far = swap_core(output_own)
    mixed, logs = attend(length, qkv, near)
    mixed, output_far = together(mixed, output_far)
    mixed_far = swap_core(mixed)
    code_chunks = jnp.where(here, chunk_of * chunk_rows + route * chunk + inside, -1)
    if by_lines:
        sent_x = lax.dynamic_index_in_dim(grads_z, 1 - (me & 1), 1, keepdims=False)
        mixed_far, grads_z, sent_x = together(mixed_far, grads_z, sent_x)
        got_x = swap(sent_x, "dp", dp_count, 1)
    residual, *parts = residual_and_rows(
        micro_arg, layer_input, mixed, mixed_far, output_own, output_far, gain_two, code_chunks, chunk_rows, chunks
    )

    if by_lines:
        parts, first_y, second_own = together(parts, first_y, second_own)
        kept_x = jnp.where(high, grads_z[:, 1], grads_z[:, 0])
        pair_x = jnp.where(high, jnp.stack([got_x, kept_x], 1), jnp.stack([kept_x, got_x], 1))
        grads_here = pair_x.reshape(dp_count, stride, width)
    else:
        parts, grads_here, first_y, second_own = together(parts, grads_here, first_y, second_own)
    second_y = swap_y(second_own)
    parts = [part.reshape(expert_count, chunk, width) for part in parts]
    arrived = [all_to_all(parts[0])]
    partner_here = grads_here[:, half, :half].astype(jnp.int32)

    def chunk_grads(c):
        at = slice(c * chunk, (c + 1) * chunk)
        return grads_here[:, at].reshape(chunk_rows, width), partner_here[:, at].reshape(chunk_rows, 1)

    grads_parts = [chunk_grads(c) for c in range(chunks)]
    arrived[0], grads_parts, second_y = together(arrived[0], grads_parts, second_y)

    firsts = (first_own, first_y, swap_core(first_own), swap_core(first_y))
    seconds = (second_own, second_y, swap_core(second_own), swap_core(second_y))

    for c in range(1, chunks):
        sent, arrived[-1] = together(parts[c], arrived[-1])
        arrived.append(all_to_all(sent))

    me_arg = me.reshape(1).astype(jnp.int32)
    rows_all, slopes, active, gated, gates, backs = [], [], [], [], [], []
    line = None
    for c in range(chunks):
        grads_c, partner_c = grads_parts[c]
        rows_c = arrived[c].reshape(chunk_rows, width)
        back, act, slo, gat, gte, line = expert_rows_pass(
            c * chunk if chunks > 1 else None, chunk, half, me_arg, partner_c, rows_c, grads_c, router_wide, line, firsts, seconds
        )
        rows_all.append(rows_c)
        slopes.append(slo)
        active.append(act)
        gated.append(gat)
        gates.append(gte)
        if chunks == 1:
            gate_grad = line[:, 0].reshape(expert_count, chunk)
            pieces = []
            for _ in range(3):
                piece = gate_grad.astype(BF)
                pieces.append(piece)
                gate_grad = gate_grad - piece.astype(F32)
            gate_row = jnp.pad(jnp.concatenate(pieces, 1), ((0, 0), (0, width - 3 * half)))
            back = jnp.pad(back.reshape(expert_count, chunk, width), ((0, 0), (0, last_stride - chunk), (0, 0)))
            back = back.at[:, spare].set(gate_row)
        if c + 1 < chunks:
            back, arrived[c + 1] = together(back.reshape(expert_count, chunk, width), arrived[c + 1])
        else:
            back, rows_all[-1], backs = together(back, rows_all[-1], backs)
        backs.append(all_to_all(back))
    grads_cross = cross_weight_grads(rows_all, slopes, active, gated)
    gates, grads_cross = together(gates, grads_cross)
    grads_in = swap_core(grads_cross)
    results = expert_results(active, gates, seconds, expert_count)
    results, grads_in = together(results, grads_in)
    grads_far, grads_kept = kept_weight_grads(rows_all, slopes, active, gated, grads_in)
    backs[-1], results, grads_far = together(backs[-1], results, grads_far)

    across_y = swap_y(grads_far)
    results_own = all_to_all(results).reshape(expert_count * half, width)

    backs_far = [swap_core(b) for b in backs]
    residual_grad, mixed_grad, extra_early, output_sent, output_kept = combine(
        micro_arg, core_arg, length, info, out_grad, residual, mixed, gain_two, router_wide, output_own,
        backs + backs_far, half, spare,
    )

    tiles, sums, far_sent, own_parts, cross_parts, sent, kept_part = attend_back(
        core_arg, length, qkv, near, mixed, logs, mixed_grad, normed_one, output_sent, output_kept, qkv_weight
    )
    arrived_cross = all_to_all(cross_parts.reshape(dp_count, rows_here, cross_parts.shape[1]))
    far_got = swap_y(far_sent)
    sent, results_own = together(sent, results_own)
    got = swap_core(sent)
    rows_both, extra_late = both_rows(
        expert_count, micro_arg, core_arg, length, kept_part, got, layer_input, gain_one, residual_grad,
        info, residual, results_own, swap_core(results_own),
    )
    rows_both, across_y, tiles = together(rows_both, across_y, tiles)
    late_far = swap_core(extra_late)
    corner = micro * 2 + core
    corners = jnp.stack([corner, corner ^ 1, corner ^ 2, corner ^ 3]).astype(jnp.int32)
    rows_y = swap_y(rows_both)
    expert_in_grad, expert_out_grad = last_sums(grads_kept, across_y)
    placed = place_pieces(corners[:2], (rows_both, swap_core(rows_both)))

    tiles = tiles.reshape(head_total, 2 * TILE * TILE)
    tiles_high = tiles.astype(BF)
    tiles_rest = (tiles - tiles_high.astype(F32)).astype(BF)
    table = dot(tiles_high, hot_const, NT) + dot(tiles_rest, hot_const, NT)
    far_sum = jnp.sum(sums[:, :, 0], axis=1) - jnp.sum(table[:, : NB - 1], axis=1)
    table = jnp.concatenate([table[:, : NB - 1], far_sum[:, None]], 1)
    table_own = jnp.concatenate([table[0:2], table[4:5]], 0)
    table_far = jnp.concatenate([table[2:4], table[5:6]], 0)
    table_cols = heads_here * NB // rows_here
    table_both = jnp.concatenate([table_own.reshape(rows_here, table_cols), table_far.reshape(rows_here, table_cols)], 1)
    base = expert_count + 2
    kept = base + 2 * table_cols
    table_tile = jnp.tile(jnp.pad(table_both, ((0, 0), (base, TILE - kept))), (dp_count, 1))

    grads = packed_sums(kept, own_parts, far_got, extra_early, extra_late, late_far, table_tile)
    grads, arrived_cross = together(grads, arrived_cross)
    cross_own, cross_far = first_sums(arrived_cross)
    arrived_grads = all_to_all(grads.reshape(dp_count, rows_here, grads.shape[1]))
    rows_y, expert_in_grad, expert_out_grad, placed, cross_own, cross_far = together(
        rows_y, expert_in_grad, expert_out_grad, placed, cross_own, cross_far
    )
    placed = place_pieces(corners[2:], (rows_y, swap_core(rows_y)), placed)
    cross_got = swap_y(cross_far)
    layer_output, input_grad = (out.reshape(2, SEQ, width) for out in placed)
    arrived_grads, layer_output, input_grad = together(arrived_grads, layer_output, input_grad)
    query_grad, key_grad, value_grad, output_grad, small = final_sums(
        kept, arrived_grads, cross_own, cross_got, shard
    )
    small_y = swap_y(small)
    both = small + small_y
    table_sum = small[:, base : base + table_cols] + small_y[:, base + table_cols : kept]
    return (
        layer_output,
        input_grad,
        both[:, expert_count],
        query_grad,
        key_grad,
        value_grad,
        output_grad.T,
        table_sum.reshape(heads_here, NB),
        both[:, expert_count + 1],
        both[:, :expert_count],
        expert_in_grad[None],
        expert_out_grad[None],
    )


def solution(mesh):
    return jax.shard_map(
        local,
        mesh=mesh,
        in_specs=(
            P(None, "dp", None),
            P(None, "dp", None),
            P("dp"),
            P("dp", "tensor"),
            P("dp", "tensor"),
            P("dp", "tensor"),
            P("tensor", "dp"),
            P("tensor", None),
            P("dp"),
            P("dp", None),
            P("dp", None, "tensor"),
            P("dp", "tensor", None),
            P(None, "dp"),
            P(None, "dp", None),
        ),
        out_specs=(
            P(None, "dp", None),
            P(None, "dp", None),
            P("dp"),
            P("dp", "tensor"),
            P("dp", "tensor"),
            P("dp", "tensor"),
            P("tensor", "dp"),
            P("tensor", None),
            P("dp"),
            P("dp", None),
            P("dp", None, "tensor"),
            P("dp", "tensor", None),
        ),
        check_vma=False,
    )
```

```python
import functools

import jax
import jax.numpy as jnp
import numpy as np
from jax import lax
from jax.experimental import pallas as pl
from jax.experimental.pallas import tpu as pltpu
from jax.sharding import PartitionSpec as P

HEAD_DIM = 64
NB = 32
SEQ = 1024
TILE = 128
QROWS = 256
NEG = -1e30
GELU_C = 0.7978845608028654
GELU_A = 0.044715

BF = jnp.bfloat16
F32 = jnp.float32

bucket_edges = np.ceil(16.0 * 8.0 ** (np.arange(1, 16) / 16.0)).astype(np.int32)


def near_tables():
    rows = np.arange(TILE)[:, None]
    cols = np.arange(TILE)[None, :]
    hots = []
    for shift in (0, TILE):
        distance = rows - cols + shift
        clipped = np.maximum(distance, 0)
        reached = np.sum(clipped[..., None] >= bucket_edges, axis=-1)
        bucket = np.minimum(clipped, 16) + reached
        hots.append(bucket[..., None] == np.arange(NB))
    hot = np.stack(hots).reshape(2 * TILE * TILE, NB).T
    return hot


NEAR_HOT = near_tables()
assert bucket_edges[-1] <= TILE


def dot(a, b, dims=((1,), (0,))):
    return lax.dot_general(a, b, (dims, ((), ())), preferred_element_type=F32)


NT = ((1,), (1,))
TN = ((0,), (0,))


MIB = 2**20
SMALL_COST = pl.CostEstimate(flops=1_000_000, bytes_accessed=1_000_000, transcendentals=0)


STRIP = 32


def score_strip(s, at, block, j, start, near_ref, half, length):
    part = s[at : at + STRIP]
    near = slice(start % TILE, start % TILE + STRIP)
    if j == block:
        if start < TILE:
            left = part[:, :TILE] + near_ref[half, 0, near, :]
            right = jnp.full((STRIP, TILE), NEG, F32)
        else:
            left = part[:, :TILE] + near_ref[half, 1, near, :]
            right = part[:, TILE:] + near_ref[half, 0, near, :]
        part = jnp.concatenate([left, right], 1)
    elif j == block - 1 and start < TILE:
        part = jnp.concatenate([part[:, :TILE], part[:, TILE:] + near_ref[half, 1, near, :]], 1)
    if (j + 1) * QROWS > SEQ // 2:
        place = lax.broadcasted_iota(jnp.int32, (1, QROWS), 1) + j * QROWS
        part = part + jnp.where(place < length, 0.0, NEG)
    return part


def lane_half(rows):
    return lax.broadcasted_iota(jnp.int32, (rows, 2 * HEAD_DIM), 1) < HEAD_DIM


def attend_kernel(length_ref, query_ref, key_ref, value_ref, near_ref, out_ref, log_ref):
    length = length_ref[0]
    lanes = lane_half(QROWS)
    value_ext = jnp.concatenate([value_ref[...], jnp.ones((SEQ, TILE), BF)], 1)
    for i in range(SEQ // QROWS):
        q_rows = query_ref[i * QROWS : (i + 1) * QROWS, :] * BF(0.125)
        q_both = jnp.concatenate([jnp.where(lanes, q_rows, BF(0)), jnp.where(lanes, BF(0), q_rows)], 0)
        tiles = [dot(q_both, key_ref[j * QROWS : (j + 1) * QROWS, :], NT) for j in range(i + 1)]
        tops = []
        weights = [[] for _ in tiles]
        for h in range(2):
            for start in range(0, QROWS, STRIP):
                strips = [
                    score_strip(s, h * QROWS + start, i, j, start, near_ref, h, length) for j, s in enumerate(tiles)
                ]
                top = strips[0]
                for s in strips[1:]:
                    top = jnp.maximum(top, s)
                top = jnp.max(top, axis=1, keepdims=True)
                tops.append(top)
                for j, s in enumerate(strips):
                    weights[j].append(jnp.exp(s - top).astype(BF))
        total = None
        for j, strips in enumerate(weights):
            total = put(total, dot(jnp.concatenate(strips, 0), value_ext[j * QROWS : (j + 1) * QROWS, :]))
        row_sum = total[:, TILE:]
        out = total[:, :TILE] / row_sum
        logs = jnp.concatenate(tops, 0) + jnp.log(row_sum)
        out_ref[i * QROWS : (i + 1) * QROWS, :] = jnp.where(lanes, out[:QROWS], out[QROWS:]).astype(BF)
        log_ref[i * QROWS : (i + 1) * QROWS, :] = jnp.where(lanes, logs[:QROWS], logs[QROWS:])


def attend(length, qkv, near):
    pairs = qkv.shape[1] // (3 * TILE)
    cols = pairs * TILE
    return pl.pallas_call(
        attend_kernel,
        grid=(pairs,),
        in_specs=[
            pl.BlockSpec(memory_space=pltpu.SMEM),
            pl.BlockSpec((SEQ, TILE), lambda p: (0, p)),
            pl.BlockSpec((SEQ, TILE), lambda p: (0, pairs + p)),
            pl.BlockSpec((SEQ, TILE), lambda p: (0, 2 * pairs + p)),
            pl.BlockSpec((2, 2, TILE, TILE), lambda p: (p, 0, 0, 0)),
        ],
        out_specs=[
            pl.BlockSpec((SEQ, TILE), lambda p: (0, p)),
            pl.BlockSpec((SEQ, TILE), lambda p: (0, p)),
        ],
        out_shape=[
            jax.ShapeDtypeStruct((SEQ, cols), BF),
            jax.ShapeDtypeStruct((SEQ, cols), F32),
        ],
        compiler_params=pltpu.CompilerParams(vmem_limit_bytes=40 * MIB),
        cost_estimate=SMALL_COST,
        name="attend",
    )(length, qkv, qkv, qkv, near)


def attend_back_kernel(
    pairs, blocks, core_ref, length_ref, query_ref, key_ref, value_ref, near_ref, out_ref, log_ref, grad_ref,
    normed_ref, output_ref, output_own, weight_ref, tile_ref, sum_ref, far_ref, own_ref, cross_ref, sent_ref, kept_ref,
    grads, dk_acc, dv_acc,
):
    step = pl.program_id(0)

    @pl.when(step < pairs)
    def _():
        pair_grads(
            step, length_ref, query_ref, key_ref, value_ref, near_ref, out_ref, log_ref, grad_ref,
            tile_ref, sum_ref, grads, dk_acc, dv_acc,
        )

    @pl.when((step >= pairs) & (step < pairs + blocks))
    def _():
        low = low_lanes((normed_ref.shape[1], TILE))
        q, k, v = (
            dot(normed_ref[...], jnp.concatenate([grads[n, p] for p in range(pairs)], 1), TN) for n in range(3)
        )
        for n, part in enumerate((q, k, v)):
            own_ref[:, n * TILE : (n + 1) * TILE] = part[:, :TILE]
            far_ref[:, n * TILE : (n + 1) * TILE] = part[:, TILE : 2 * TILE].astype(BF)
        q, k, v = (part[:, 2 * TILE :] for part in (q, k, v))
        tiles = (
            jnp.where(low, q, turned(k)),
            jnp.where(low, v, turned(output_own[:, TILE:])),
            output_own[:, :TILE],
            jnp.where(low, turned(q), k),
            jnp.where(low, turned(v), output_ref[:, TILE:].astype(F32)),
            output_ref[:, :TILE],
        )
        for n, tile in enumerate(tiles):
            cross_ref[:, n * TILE : (n + 1) * TILE] = tile.astype(BF)

    for late, half_ref in enumerate((sent_ref, kept_ref)):
        first = pairs + blocks + 2 * late

        @pl.when((step >= first) & (step < first + 2))
        def _(half_ref=half_ref, first=first, late=late):
            rows = half_ref.shape[0]
            mine = core_ref[0] if late else 1 - core_ref[0]
            start = pl.multiple_of((2 * mine + step - first) * rows, rows)
            total = None
            for n in range(3):
                part = jnp.concatenate([grads[n, p, pl.ds(start, rows), :] for p in range(pairs)], 1)
                cols = part.shape[1]
                total = put(total, dot(part, weight_ref[:, n * cols : (n + 1) * cols], NT))
            half_ref[...] = total


def pair_grads(
    pair, length_ref, query_ref, key_ref, value_ref, near_ref, out_ref, log_ref, grad_ref, tile_ref, sum_ref, grads, dk_acc, dv_acc
):
    length = length_ref[0]
    lanes = lane_half(QROWS)
    key_ext = jnp.concatenate([key_ref[...], jnp.ones((SEQ, TILE), BF)], 1)
    near_sums = [[None, None], [None, None]]
    all_sums = [None, None]

    def both(rows):
        return jnp.concatenate([jnp.where(lanes, rows, BF(0)), jnp.where(lanes, BF(0), rows)], 0)

    for i in range(SEQ // QROWS):
        rows = slice(i * QROWS, (i + 1) * QROWS)
        q_both = both(query_ref[rows, :] * BF(0.125))
        g_rows = grad_ref[rows, :]
        g_both = both(g_rows)
        mass = g_rows.astype(F32) * out_ref[rows, :].astype(F32)
        deltas = [
            jnp.sum(jnp.where(lanes, mass, 0.0), axis=1, keepdims=True),
            jnp.sum(jnp.where(lanes, 0.0, mass), axis=1, keepdims=True),
        ]
        logs = [log_ref[rows, h * HEAD_DIM : h * HEAD_DIM + 1] for h in range(2)]
        dq = None
        for j in range(i + 1):
            keys = slice(j * QROWS, (j + 1) * QROWS)
            s = dot(q_both, key_ref[keys, :], NT)
            dp = dot(g_both, value_ref[keys, :], NT)
            p_strips, d_strips = [], []
            for h in range(2):
                for start in range(0, QROWS, STRIP):
                    strip = slice(start, start + STRIP)
                    at = h * QROWS + start
                    p = jnp.exp(score_strip(s, at, i, j, start, near_ref, h, length) - logs[h][strip])
                    p_strips.append(p.astype(BF))
                    d_strips.append((p * (dp[at : at + STRIP] - deltas[h][strip])).astype(BF))
            p, ds = jnp.concatenate(p_strips, 0), jnp.concatenate(d_strips, 0)
            part = dot(ds, key_ext[keys, :])
            dq = put(dq, jnp.where(lanes, part[:QROWS, :TILE], part[QROWS:, :TILE]))
            for h in range(2):
                sums = part[h * QROWS : (h + 1) * QROWS, TILE:]
                all_sums[h] = put(all_sums[h], jnp.sum(sums.reshape(QROWS // 8, 8, TILE), axis=0))
            dk_part = dot(ds, q_both, TN)
            dv_part = dot(p, g_both, TN)
            if i == j:
                dk_acc[keys, :] = dk_part
                dv_acc[keys, :] = dv_part
            else:
                dk_acc[keys, :] += dk_part
                dv_acc[keys, :] += dv_part
            for h in range(2):
                mine = ds[h * QROWS : (h + 1) * QROWS]
                if j == i:
                    wide = mine.astype(F32)
                    near_sums[h][0] = put(near_sums[h][0], wide[:TILE, :TILE] + wide[TILE:, TILE:])
                    near_sums[h][1] = put(near_sums[h][1], wide[TILE:, :TILE])
                elif j == i - 1:
                    near_sums[h][1] = put(near_sums[h][1], mine[:TILE, TILE:].astype(F32))
        grads[0, pair, rows, :] = (dq * 0.125).astype(BF)
    grads[1, pair] = dk_acc[...].astype(BF)
    grads[2, pair] = dv_acc[...].astype(BF)
    for h in range(2):
        tile_ref[h, 0] = near_sums[h][0]
        tile_ref[h, 1] = near_sums[h][1]
        sum_ref[h] = all_sums[h]


def attend_back(core, length, qkv, near, mixed, logs, grad, normed, output, output_own, weight):
    pairs = qkv.shape[1] // (3 * TILE)
    width = normed.shape[1]
    block = 256
    blocks = width // block
    at = lambda i: jnp.minimum(i, pairs - 1)
    then = lambda i: jnp.clip(i - pairs, 0, blocks - 1)
    return pl.pallas_call(
        functools.partial(attend_back_kernel, pairs, blocks),
        grid_spec=pltpu.PrefetchScalarGridSpec(
            num_scalar_prefetch=2,
            grid=(pairs + blocks + 4,),
            in_specs=[
                pl.BlockSpec((SEQ, TILE), lambda i, *_: (0, at(i))),
                pl.BlockSpec((SEQ, TILE), lambda i, *_: (0, pairs + at(i))),
                pl.BlockSpec((SEQ, TILE), lambda i, *_: (0, 2 * pairs + at(i))),
                pl.BlockSpec((2, 2, TILE, TILE), lambda i, *_: (at(i), 0, 0, 0)),
            ]
            + [pl.BlockSpec((SEQ, TILE), lambda i, *_: (0, at(i)))] * 3
            + [
                pl.BlockSpec((SEQ, block), lambda i, *_: (0, then(i))),
                pl.BlockSpec((block, 2 * TILE), lambda i, *_: (then(i), 0)),
                pl.BlockSpec((block, 2 * TILE), lambda i, *_: (then(i), 0)),
                pl.BlockSpec(weight.shape, lambda i, *_: (0, 0)),
            ],
            out_specs=[
                pl.BlockSpec((2, 2, TILE, TILE), lambda i, *_: (at(i), 0, 0, 0)),
                pl.BlockSpec((2, 8, TILE), lambda i, *_: (at(i), 0, 0)),
                pl.BlockSpec((block, 3 * TILE), lambda i, *_: (then(i), 0)),
                pl.BlockSpec((block, 3 * TILE), lambda i, *_: (then(i), 0)),
                pl.BlockSpec((block, 6 * TILE), lambda i, *_: (then(i), 0)),
                pl.BlockSpec((block, width), lambda i, *_: (jnp.clip(i - pairs - blocks, 0, 1), 0)),
                pl.BlockSpec((block, width), lambda i, *_: (jnp.clip(i - pairs - blocks - 2, 0, 1), 0)),
            ],
            scratch_shapes=[
                pltpu.VMEM((3, pairs, SEQ, TILE), BF), pltpu.VMEM((SEQ, TILE), F32), pltpu.VMEM((SEQ, TILE), F32),
            ],
        ),
        out_shape=[
            jax.ShapeDtypeStruct((2 * pairs, 2, TILE, TILE), F32),
            jax.ShapeDtypeStruct((2 * pairs, 8, TILE), F32),
            jax.ShapeDtypeStruct((width, 3 * TILE), BF),
            jax.ShapeDtypeStruct((width, 3 * TILE), F32),
            jax.ShapeDtypeStruct((width, 6 * TILE), BF),
            jax.ShapeDtypeStruct((2 * block, width), F32),
            jax.ShapeDtypeStruct((2 * block, width), F32),
        ],
        compiler_params=pltpu.CompilerParams(vmem_limit_bytes=60 * MIB),
        cost_estimate=SMALL_COST,
        name="attend_back",
    )(core, length, qkv, qkv, qkv, near, mixed, logs, grad, normed, output, output_own, weight)


def low_lanes(shape):
    return lax.broadcasted_iota(jnp.int32, shape, 1) < HEAD_DIM


def turned(tile):
    return pltpu.roll(tile, HEAD_DIM, 1)


def pack_kernel(q_ref, k_ref, v_ref, o_ref, one_ref, two_ref, router_ref, out_ref):
    shard = q_ref.shape[1]
    rows = q_ref.shape[0]
    source = lax.broadcasted_iota(jnp.int32, (shard, 6 * TILE), 0)
    target = lax.broadcasted_iota(jnp.int32, (shard, 6 * TILE), 1)

    def moved(pair_base, last_base):
        want = jnp.where(source < TILE, source + pair_base, source - TILE + last_base)
        return jnp.where(target == want, 1.0, 0.0).astype(BF)

    total = dot(v_ref[...], moved(0, 2 * TILE)) + dot(o_ref[...], moved(TILE, 2 * TILE + HEAD_DIM), TN)
    total = total + dot(q_ref[...], moved(3 * TILE, 5 * TILE)) + dot(k_ref[...], moved(4 * TILE, 5 * TILE + HEAD_DIM))
    out_ref[:, : 6 * TILE] = total.astype(BF)
    experts = router_ref.shape[0]
    own_row = lax.broadcasted_iota(jnp.int32, (rows, rows), 0) == lax.broadcasted_iota(jnp.int32, (rows, rows), 1)

    def column(ref):
        return jnp.sum(jnp.where(own_row, ref[...].astype(F32), 0.0), axis=1, keepdims=True)

    lanes = lax.broadcasted_iota(jnp.int32, (experts, TILE), 1)
    spread = jnp.where(lanes == lax.broadcasted_iota(jnp.int32, (experts, TILE), 0), 1.0, 0.0).astype(BF)
    place = lax.broadcasted_iota(jnp.int32, (rows, TILE), 1)
    small = dot(router_ref[...], spread, TN)
    small = jnp.where(place == experts, column(one_ref), jnp.where(place == experts + 1, column(two_ref), small))
    out_ref[:, 6 * TILE :] = small.astype(BF)


def pack_weights(query, key, value, output, one, two, router):
    rows = query.shape[0]
    return pl.pallas_call(
        pack_kernel,
        out_shape=jax.ShapeDtypeStruct((rows, 7 * TILE), BF),
        compiler_params=pltpu.CompilerParams(vmem_limit_bytes=60 * MIB),
        cost_estimate=SMALL_COST,
        name="pack_weights",
    )(query, key, value, output, one[None], two[None], router.T)


def qkv_kernel(micro_ref, tokens_ref, gain_ref, a_own, a_far, b_own, b_far, qkv_ref, normed_ref, weight_ref, output_ref):
    width = tokens_ref.shape[2]

    @pl.when(pl.program_id(0) == 0)
    def _():
        low = low_lanes((width, TILE))

        def tiles(own, far, pair, low_half):
            at = slice(pair * TILE, (pair + 1) * TILE)
            one, two = own[:, 2 * TILE :].astype(F32), far[:, 2 * TILE :].astype(F32)
            last = jnp.where(low, one, turned(two)) if low_half else jnp.where(low, turned(one), two)
            return own[:, at], far[:, at], last.astype(BF)

        for n, (own, far, pair, low_half) in enumerate(
            ((a_own, a_far, 0, True), (a_own, a_far, 1, False), (b_own, b_far, 0, True))
        ):
            for t, tile in enumerate(tiles(own[...], far[...], pair, low_half)):
                at = 3 * n + t
                weight_ref[:, at * TILE : (at + 1) * TILE] = tile
        for t, tile in enumerate(tiles(b_own[...], b_far[...], 1, False)):
            output_ref[:, t * TILE : (t + 1) * TILE] = tile

    x = tokens_ref[0].astype(F32)
    inverse = lax.rsqrt(jnp.mean(x * x, axis=-1, keepdims=True) + 1e-06)
    normed = (x * inverse * gain_ref[...]).astype(BF)
    normed_ref[...] = normed
    qkv_ref[...] = dot(normed, weight_ref[...]).astype(BF)


def norm_and_project(micro, layer_input, gain, a_own, a_far, b_own, b_far):
    width = layer_input.shape[2]
    block = 256
    cols = 3 * TILE
    whole = lambda rows, n: pl.BlockSpec((rows, n), lambda i, m: (0, 0))
    here = lambda n: pl.BlockSpec((block, n), lambda i, m: (i, 0))
    return pl.pallas_call(
        qkv_kernel,
        grid_spec=pltpu.PrefetchScalarGridSpec(
            num_scalar_prefetch=1,
            grid=(SEQ // block,),
            in_specs=[pl.BlockSpec((1, block, width), lambda i, m: (m[0], i, 0)), whole(1, width)] + [whole(width, cols)] * 4,
            out_specs=[here(3 * cols), here(width), whole(width, 3 * cols), whole(width, cols)],
        ),
        out_shape=[
            jax.ShapeDtypeStruct((SEQ, 3 * cols), BF),
            jax.ShapeDtypeStruct((SEQ, width), BF),
            jax.ShapeDtypeStruct((width, 3 * cols), BF),
            jax.ShapeDtypeStruct((width, cols), BF),
        ],
        compiler_params=pltpu.CompilerParams(vmem_limit_bytes=40 * MIB),
        cost_estimate=SMALL_COST,
        name="norm_and_project",
    )(micro, layer_input, gain, a_own, a_far, b_own, b_far)


def middle_kernel(
    blocks, per, micro_ref, tokens_ref, mixed_ref, other_ref, own_ref, far_ref, gain_ref, code_ref, residual_ref, *refs
):
    sent_refs, normed = refs[:-1], refs[-1]
    step = pl.program_id(0)
    rows = tokens_ref.shape[1]

    @pl.when(step < blocks)
    def _():
        total = tokens_ref[0].astype(F32) + dot(mixed_ref[...], own_ref[...], NT) + dot(other_ref[...], far_ref[...], NT)
        residual_ref[...] = total
        inverse = lax.rsqrt(jnp.mean(total * total, axis=-1, keepdims=True) + 1e-06)
        normed[pl.ds(pl.multiple_of(step * rows, rows), rows), :] = (total * inverse * gain_ref[...]).astype(BF)

    for c, sent_ref in enumerate(sent_refs):

        @pl.when((step >= blocks + c * per) & (step < blocks + (c + 1) * per))
        def _(sent_ref=sent_ref):
            block = sent_ref.shape[0]
            ids = lax.broadcasted_iota(jnp.int32, (block, 1), 0) + (step - blocks) * block
            hot = jnp.where((ids == code_ref[:1]) | (ids == code_ref[1:2]), 1.0, 0.0).astype(BF)
            sent_ref[...] = dot(hot, normed[...]).astype(BF)


def residual_and_rows(micro, layer_input, mixed, other, output_own, output_far, gain, code, count, chunks):
    width = layer_input.shape[2]
    block = 256
    blocks = SEQ // block
    send = 320
    cols = mixed.shape[1]
    per = count // send
    at = lambda i: jnp.minimum(i, blocks - 1)
    whole = lambda arr: pl.BlockSpec(arr.shape, lambda i, m: (0, 0))
    here = lambda n: pl.BlockSpec((block, n), lambda i, m: (at(i), 0))

    def sent(c):
        return pl.BlockSpec((send, width), lambda i, m: (jnp.clip(i - blocks - c * per, 0, per - 1), 0))

    return pl.pallas_call(
        functools.partial(middle_kernel, blocks, per),
        grid_spec=pltpu.PrefetchScalarGridSpec(
            num_scalar_prefetch=1,
            grid=(blocks + chunks * per,),
            in_specs=[
                pl.BlockSpec((1, block, width), lambda i, m: (m[0], at(i), 0)),
                here(cols), here(cols), whole(output_own), whole(output_far), whole(gain), whole(code),
            ],
            out_specs=[here(width)] + [sent(c) for c in range(chunks)],
            scratch_shapes=[pltpu.VMEM((SEQ, width), BF)],
        ),
        out_shape=[jax.ShapeDtypeStruct((SEQ, width), F32)] + [jax.ShapeDtypeStruct((count, width), BF)] * chunks,
        compiler_params=pltpu.CompilerParams(vmem_limit_bytes=40 * MIB),
        cost_estimate=SMALL_COST,
        name="residual_and_rows",
    )(micro, layer_input, mixed, other, output_own, output_far, gain, code)


def picked_rows(first, second, segments):
    total = None
    start = 0
    for rows in segments:
        length = rows.shape[0]
        ids = lax.broadcasted_iota(jnp.int32, (1, length), 1) + start
        hot = []
        for at in range(0, first.shape[0], STRIP):
            one, two = first[at : at + STRIP], second[at : at + STRIP]
            hot.append(jnp.where((one == ids) | (two == ids), 1.0, 0.0).astype(BF))
        total = put(total, dot(jnp.concatenate(hot, 0), rows))
        start += length
    return total


def put(a, b):
    return b if a is None else a + b


def folded(product):
    return jnp.sum(product.reshape(product.shape[0] // 8, 8, product.shape[1]), axis=0)


def as_column(eight):
    ones = jnp.ones((16, TILE), BF)
    high = eight.astype(BF)
    rest = (eight - high.astype(F32)).astype(BF)
    return dot(jnp.concatenate([high, rest], 0), ones, TN)


def combine_kernel(experts, half, spare, micro_ref, core_ref, length_ref, *refs):
    info_ref, grad_ref, residual_ref, mixed_ref, gain_ref, router_ref, output_ref = refs[:7]
    backs = refs[7:-9]
    (total_ref, mixed_grad_ref, extra_ref, far_ref, own_ref, acc_ref, router_acc, gain_acc, tables) = refs[-9:]
    block = residual_ref.shape[0]
    step = pl.program_id(0)
    count = len(backs) // 2

    @pl.when(step == 0)
    def _():
        place = lax.broadcasted_iota(jnp.int32, (experts, 1), 0)
        for n, back in enumerate((backs[count - 1], backs[2 * count - 1])):
            table = jnp.zeros((experts, back.shape[2]), F32)
            for e in range(experts):
                row = back[e, spare : spare + 16, :].astype(F32)[:1]
                table = jnp.where(place == e, row, table)
            for piece in range(3):
                at = (3 * n + piece) * experts
                tables[at : at + experts] = table[:, piece * half : (piece + 1) * half]

    info = jnp.transpose(info_ref[...])
    number = lambda n: info[:, n : n + 1]
    columns = lax.broadcasted_iota(jnp.int32, (1, half), 1)
    lanes = lax.broadcasted_iota(jnp.int32, (1, 6 * experts), 1)
    table = tables[...].astype(BF)
    values = []
    for k in range(2):
        slot = number(4 + k)
        hot = jnp.where(columns == lax.rem(slot, half), 1.0, 0.0).astype(BF)
        found = dot(hot, table, NT)
        wanted = jnp.where(slot // half == core_ref[0], 0, 3 * experts) + number(2 + k)
        away = lanes - wanted
        hit = (away == 0) | (away == experts) | (away == 2 * experts)
        values.append(jnp.sum(jnp.where(hit, found, 0.0), axis=1, keepdims=True))
    wide = lax.broadcasted_iota(jnp.int32, (1, TILE), 1)
    is_first, is_second = wide == number(2), wide == number(3)
    residual = residual_ref[...]
    gain = gain_ref[...]
    inverse = lax.rsqrt(jnp.mean(residual * residual, axis=-1, keepdims=True) + 1e-06)
    plain = residual * inverse
    normed = (plain * gain).astype(BF)
    logits = dot(normed, router_ref[...])
    gap = jnp.sum(jnp.where(is_first, logits, 0.0) - jnp.where(is_second, logits, 0.0), axis=1, keepdims=True)
    small = jnp.exp(-jnp.abs(gap))
    logit = small / ((1.0 + small) * (1.0 + small)) * (values[0] - values[1])
    logit_grad = jnp.where(is_first, logit, jnp.where(is_second, -logit, 0.0)).astype(BF)
    segments = [b[...].reshape(b.shape[0] * b.shape[1], b.shape[2]) for b in backs]
    normed_grad = picked_rows(number(0), number(1), segments) + dot(logit_grad, router_ref[...], NT)
    scaled = normed_grad * gain
    mean = jnp.mean(scaled * plain, axis=-1, keepdims=True)
    place = lax.broadcasted_iota(jnp.int32, (block, 1), 0) + step * block
    grad_out = jnp.where(place < length_ref[0], grad_ref[0].astype(F32), 0.0)
    total = grad_out + inverse * (scaled - plain * mean)

    @pl.when(step == core_ref[0])
    def _():
        total_ref[...] = total

    branch = total.astype(BF)
    mixed_grad_ref[...] = dot(branch, output_ref[...]).astype(BF)
    router_part = dot(logit_grad, normed, TN)
    gain_part = folded(normed_grad * plain)
    output_part = dot(mixed_ref[...], branch, TN)

    @pl.when(step == 0)
    def _():
        router_acc[...] = router_part
        gain_acc[...] = gain_part
        acc_ref[...] = output_part

    @pl.when(step > 0)
    def _():
        router_acc[...] += router_part
        gain_acc[...] += gain_part
        acc_ref[...] += output_part

    @pl.when(step == pl.num_programs(0) - 1)
    def _():
        extra_ref[...] = jnp.transpose(router_acc[...]) + jnp.where(wide == experts + 1, as_column(gain_acc[...]), 0.0)
        parts = jnp.transpose(acc_ref[...])
        far_ref[...] = parts[:, TILE:].astype(BF)
        own_ref[:, :TILE] = parts[:, :TILE]
        own_ref[:, TILE:] = parts[:, 2 * TILE :]


def combine(micro, core, length, info, out_grad, residual, mixed, gain, router, output_own, backs, half, spare):
    width = residual.shape[1]
    block = 512
    cols = mixed.shape[1]
    whole = lambda arr: pl.BlockSpec(arr.shape, lambda i, *_: (0,) * arr.ndim)
    fixed = lambda rows, n: pl.BlockSpec((rows, n), lambda i, *_: (0, 0))
    here = lambda n: pl.BlockSpec((block, n), lambda i, *_: (i, 0))
    experts = backs[0].shape[0]
    return pl.pallas_call(
        functools.partial(combine_kernel, experts, half, spare),
        grid_spec=pltpu.PrefetchScalarGridSpec(
            num_scalar_prefetch=3,
            grid=(SEQ // block,),
            in_specs=[
                pl.BlockSpec((8, block), lambda i, *_: (0, i)),
                pl.BlockSpec((1, block, width), lambda i, m, *_: (m[0], i, 0)),
                here(width), here(cols), whole(gain), whole(router), whole(output_own),
            ]
            + [whole(x) for x in backs],
            out_specs=[fixed(block, width), here(cols), fixed(width, TILE), fixed(width, 2 * TILE), fixed(width, 2 * TILE)],
            scratch_shapes=[
                pltpu.VMEM((cols, width), F32),
                pltpu.VMEM((TILE, width), F32),
                pltpu.VMEM((8, width), F32),
                pltpu.VMEM((6 * experts, half), F32),
            ],
        ),
        out_shape=[
            jax.ShapeDtypeStruct((block, width), F32),
            jax.ShapeDtypeStruct((SEQ, cols), BF),
            jax.ShapeDtypeStruct((width, TILE), F32),
            jax.ShapeDtypeStruct((width, 2 * TILE), BF),
            jax.ShapeDtypeStruct((width, 2 * TILE), F32),
        ],
        compiler_params=pltpu.CompilerParams(vmem_limit_bytes=60 * MIB),
        cost_estimate=SMALL_COST,
        name="combine",
    )(micro, core, length, info, out_grad, residual, mixed, gain, router, output_own, *backs)


def both_kernel(
    lane, micro_ref, core_ref, length_ref, part_ref, got_ref, tokens_ref, gain_ref, grad_ref,
    info_ref, residual_ref, own_ref, far_ref, out_ref, extra_ref, acc_ref,
):
    block = residual_ref.shape[0]
    info = jnp.transpose(info_ref[...])
    place = lax.broadcasted_iota(jnp.int32, (block, 1), 0) + (core_ref[0] * 2 + pl.program_id(0)) * block
    rows = residual_ref[...] + picked_rows(info[:, 6:7], info[:, 7:8], (own_ref[...], far_ref[...]))
    out_ref[0] = jnp.where(place < length_ref[0], rows, 0.0).astype(BF)
    normed_grad = got_ref[...] + part_ref[...]
    x = tokens_ref[0].astype(F32)
    inverse = lax.rsqrt(jnp.mean(x * x, axis=-1, keepdims=True) + 1e-06)
    plain = x * inverse
    scaled = normed_grad * gain_ref[...]
    mean = jnp.mean(scaled * plain, axis=-1, keepdims=True)
    out_ref[1] = (grad_ref[...] + inverse * (scaled - plain * mean)).astype(BF)
    wide = lax.broadcasted_iota(jnp.int32, (1, TILE), 1)
    part = folded(normed_grad * plain)

    @pl.when(pl.program_id(0) == 0)
    def _():
        acc_ref[...] = part

    @pl.when(pl.program_id(0) == 1)
    def _():
        extra_ref[...] = jnp.where(wide == lane, as_column(acc_ref[...] + part), 0.0)


def both_rows(lane, micro, core, length, part, got, layer_input, gain, residual_grad, info, residual, own, far):
    width = part.shape[1]
    plain = pl.BlockSpec((256, width), lambda i, *_: (i, 0))
    block = 256
    here = lambda n: pl.BlockSpec((block, n), lambda i, m, c, *_: (c[0] * 2 + i, 0))
    whole = lambda arr: pl.BlockSpec(arr.shape, lambda i, *_: (0, 0))
    return pl.pallas_call(
        functools.partial(both_kernel, lane),
        grid_spec=pltpu.PrefetchScalarGridSpec(
            num_scalar_prefetch=3,
            grid=(2,),
            in_specs=[
                plain,
                plain,
                pl.BlockSpec((1, block, width), lambda i, m, c, *_: (m[0], c[0] * 2 + i, 0)),
                whole(gain),
                plain,
                pl.BlockSpec((8, block), lambda i, m, c, *_: (0, c[0] * 2 + i)),
                here(width),
                whole(own),
                whole(far),
            ],
            out_specs=[
                pl.BlockSpec((2, block, width), lambda i, *_: (0, i, 0)),
                pl.BlockSpec((width, TILE), lambda i, *_: (0, 0)),
            ],
            scratch_shapes=[pltpu.VMEM((8, width), F32)],
        ),
        out_shape=[jax.ShapeDtypeStruct((2, 2 * block, width), BF), jax.ShapeDtypeStruct((width, TILE), F32)],
        compiler_params=pltpu.CompilerParams(vmem_limit_bytes=40 * MIB),
        cost_estimate=SMALL_COST,
        name="both_rows",
    )(micro, core, length, part, got, layer_input, gain, residual_grad, info, residual, own, far)


def sum_kernel(kept, own, got, early, late, late_far, table, sum_ref):
    low = low_lanes(early.shape)
    sum_ref[:, : 3 * TILE] = (own[...] + got[...].astype(F32)).astype(BF)
    extra = early[...] + late[...] + late_far[...] + table[...]
    high = extra.astype(BF)
    rest = extra - high.astype(F32)
    if kept <= HEAD_DIM:
        sum_ref[:, 3 * TILE :] = jnp.where(low, high.astype(F32), turned(rest)).astype(BF)
    else:
        sum_ref[:, 3 * TILE : 4 * TILE] = high
        sum_ref[:, 4 * TILE :] = rest.astype(BF)


def packed_sums(kept, *parts):
    width = parts[0].shape[0]
    cols = (4 if kept <= HEAD_DIM else 5) * TILE
    block = 256
    here = lambda n: pl.BlockSpec((block, n), lambda i: (i, 0))
    return pl.pallas_call(
        functools.partial(sum_kernel, kept),
        grid=(width // block,),
        in_specs=[here(x.shape[1]) for x in parts],
        out_specs=here(cols),
        out_shape=jax.ShapeDtypeStruct((width, cols), BF),
        compiler_params=pltpu.CompilerParams(vmem_limit_bytes=40 * MIB),
        cost_estimate=SMALL_COST,
        name="packed_sums",
    )(*parts)


def added(parts_ref):
    total = parts_ref[0].astype(F32)
    for n in range(1, parts_ref.shape[0]):
        total = total + parts_ref[n].astype(F32)
    return total


def first_kernel(parts_ref, own_ref, far_ref):
    total = added(parts_ref)
    own_ref[...] = total[:, : 3 * TILE]
    far_ref[...] = total[:, 3 * TILE :]


def first_sums(parts):
    rows = parts.shape[1]
    return pl.pallas_call(
        first_kernel,
        out_shape=[jax.ShapeDtypeStruct((rows, 3 * TILE), F32)] * 2,
        compiler_params=pltpu.CompilerParams(vmem_limit_bytes=40 * MIB),
        cost_estimate=SMALL_COST,
        name="first_sums",
    )(parts)


def final_kernel(kept, parts_ref, own_ref, got_ref, q_ref, k_ref, v_ref, o_ref, small_ref):
    total = added(parts_ref)
    other = own_ref[...] + got_ref[...]
    tile = lambda arr, t: arr[:, t * TILE : (t + 1) * TILE]
    q_ref[:, :TILE] = tile(total, 0)
    q_ref[:, TILE:] = tile(other, 0)[:, :HEAD_DIM]
    k_ref[:, :TILE] = tile(total, 1)
    k_ref[:, TILE:] = turned(tile(other, 0))[:, :HEAD_DIM]
    v_ref[:, :TILE] = tile(total, 2)
    v_ref[:, TILE:] = tile(other, 1)[:, :HEAD_DIM]
    o_ref[:, :TILE] = tile(other, 2)
    o_ref[:, TILE:] = turned(tile(other, 1))[:, :HEAD_DIM]
    small_ref[...] = tile(total, 3) + (turned(tile(total, 3)) if kept <= HEAD_DIM else tile(total, 4))


def final_sums(kept, parts, own, got, shard):
    rows = parts.shape[1]
    return pl.pallas_call(
        functools.partial(final_kernel, kept),
        out_shape=[jax.ShapeDtypeStruct((rows, shard), F32)] * 4 + [jax.ShapeDtypeStruct((rows, TILE), F32)],
        compiler_params=pltpu.CompilerParams(vmem_limit_bytes=40 * MIB),
        cost_estimate=SMALL_COST,
        name="final_sums",
    )(parts, own, got)


def pair_gate(logits, own, other):
    lanes = lax.broadcasted_iota(jnp.int32, logits.shape, 1)
    gap = jnp.sum(
        jnp.where(lanes == own, logits, 0.0) - jnp.where(lanes == other, logits, 0.0), axis=1, keepdims=True
    )
    small = jnp.exp(-jnp.abs(gap))
    return jnp.where(gap >= 0.0, 1.0, small) / (1.0 + small)


def expert_kernel(lead, chunk, half, me_ref, partner_ref, rows_ref, grads_ref, router_ref, *refs):
    before, refs = (refs[0], refs[1:]) if lead is not None and lead > 0 else (None, refs)
    firsts, seconds = refs[:4], refs[4:8]
    back_ref, active_ref, slope_ref, gated_ref, gate_ref, mass_ref = refs[8:]
    rows = rows_ref[...]
    grads = grads_ref[...]
    gate = pair_gate(dot(rows, router_ref[...]), me_ref[0], partner_ref[...])
    gated_ref[...] = (gate * grads.astype(F32)).astype(BF)
    gate_ref[...] = jnp.broadcast_to(gate, gate_ref.shape)
    masses = [None] * (rows.shape[0] // STRIP)
    back = None
    width = firsts[0].shape[1]
    step = 256
    places = [(r, c) for r in range(4) for c in range(0, width, step)]

    def products(r, c):
        return dot(rows, firsts[r][:, c : c + step]), dot(grads, seconds[r][c : c + step, :], NT)

    ahead = products(*places[0])
    for n, (r, c) in enumerate(places):
        x, plain = ahead
        if n + 1 < len(places):
            ahead = products(*places[n + 1])
        place = slice(r * width + c, r * width + c + step)
        for at in range(0, rows.shape[0], STRIP):
            strip = slice(at, at + STRIP)
            value, flow = x[strip], plain[strip]
            square = value * value
            bent = jnp.tanh(value * (GELU_C + (GELU_C * GELU_A) * square))
            rise = 0.5 + 0.5 * bent
            active = value * rise
            slope = rise + active * (1.0 - bent) * (GELU_C + (3.0 * GELU_C * GELU_A) * square)
            low = active.astype(BF)
            active_ref[strip, place] = low
            slope_ref[strip, place] = (gate[strip] * flow * slope).astype(BF)
            part = low.astype(F32) * flow
            masses[at // STRIP] = put(masses[at // STRIP], part[:, :TILE] + part[:, TILE:])
        if c + step == width and r > 0:
            back = put(back, dot(slope_ref[:, (r - 1) * width : r * width], firsts[r - 1][...], NT))
    back = put(back, dot(slope_ref[:, 3 * width :], firsts[3][...], NT))
    back = back.astype(BF)
    mass = jnp.sum(jnp.concatenate(masses, 0), axis=1, keepdims=True)
    if lead is None:
        back_ref[...] = back
        mass_ref[...] = jnp.broadcast_to(mass, mass_ref.shape)
        return
    count = rows.shape[0] // chunk
    number = lax.broadcasted_iota(jnp.int32, (rows.shape[0], 1), 0)
    lanes = lax.broadcasted_iota(jnp.int32, (1, rows.shape[1]), 1)
    inside = lax.rem(number, chunk)
    spread = jnp.zeros(rows.shape, F32)
    for piece in range(3):
        high = mass.astype(BF).astype(F32)
        spread = jnp.where(lanes == piece * half + lead + inside, high, spread)
        mass = mass - high
    own = jnp.where(number // chunk == lax.broadcasted_iota(jnp.int32, (1, TILE), 1), 1.0, 0.0).astype(BF)
    line = dot(own, spread.astype(BF), TN)
    if before is None:
        back_ref[...] = back
        for e in range(count):
            mass_ref[e] = line[e : e + 1].astype(BF)
    else:
        back_ref[:, :chunk] = back.reshape(count, chunk, back.shape[1])
        row = lax.broadcasted_iota(jnp.int32, (16, 1), 0)
        for e in range(count):
            both = line[e : e + 1] + before[e].astype(F32)
            back_ref[e, chunk:] = jnp.where(row == 0, both, 0.0).astype(BF)


def row_block(total):
    return 320 if total % 320 == 0 else total


def expert_rows_pass(lead, chunk, half, me, partner, rows, grads, router, before, firsts, seconds):
    total, width = rows.shape
    block = row_block(total)
    experts = total // chunk
    hidden = sum(f.shape[1] for f in firsts)
    here = lambda cols: pl.BlockSpec((block, cols), lambda i: (i, 0))
    whole = lambda arr: pl.BlockSpec(arr.shape, lambda i: (0, 0))
    lines = pl.BlockSpec((block // chunk, 1, width), lambda i: (i, 0, 0))
    back_shape, back_spec = (total, width), here(width)
    mass_shape, mass_spec, mass_kind = (experts, 1, width), lines, BF
    if lead is None:
        mass_shape, mass_spec, mass_kind = (total, TILE), here(TILE), F32
    elif before is not None:
        back_shape = (experts, chunk + 16, width)
        back_spec = pl.BlockSpec((block // chunk, chunk + 16, width), lambda i: (i, 0, 0))
    return pl.pallas_call(
        functools.partial(expert_kernel, lead, chunk, half),
        grid=(total // block,),
        in_specs=[pl.BlockSpec(memory_space=pltpu.SMEM), here(1), here(width), here(width), whole(router)]
        + ([lines] if before is not None else [])
        + [whole(w) for w in firsts]
        + [whole(w) for w in seconds],
        out_specs=[back_spec, here(hidden), here(hidden), here(width), here(TILE), mass_spec],
        out_shape=[
            jax.ShapeDtypeStruct(back_shape, BF),
            jax.ShapeDtypeStruct((total, hidden), BF),
            jax.ShapeDtypeStruct((total, hidden), BF),
            jax.ShapeDtypeStruct((total, width), BF),
            jax.ShapeDtypeStruct((total, TILE), F32),
            jax.ShapeDtypeStruct(mass_shape, mass_kind),
        ],
        compiler_params=pltpu.CompilerParams(vmem_limit_bytes=56 * MIB),
        cost_estimate=SMALL_COST,
        name="expert_rows",
    )(me, partner, rows, grads, router, *([before] if before is not None else []), *firsts, *seconds)


def weight_parts(count, refs):
    rows, slopes, active, gated = (refs[n * count : (n + 1) * count] for n in range(4))
    first, second = None, None
    for n in range(count):
        first = put(first, dot(rows[n][...], slopes[n][...], TN))
        second = put(second, dot(active[n][...], gated[n][...], TN))
    return first, second


def cross_kernel(count, *refs):
    first, second = weight_parts(count, refs)
    refs[-1][0, 0] = first.astype(BF)
    refs[-1][0, 1] = second.astype(BF)


def kept_kernel(count, *refs):
    got_ref, far_ref, kept_ref = refs[-3:]
    first, second = weight_parts(count, refs)
    first = first + got_ref[0, 0].astype(F32)
    second = second + got_ref[0, 1].astype(F32)

    @pl.when(pl.program_id(0) == 0)
    def _():
        far_ref[0] = first.astype(BF)
        far_ref[1] = second.astype(BF)

    @pl.when(pl.program_id(0) == 1)
    def _():
        kept_ref[0] = first
        kept_ref[1] = second


def weight_specs(rows, slopes, quarter):
    total, width = rows[0].shape
    hidden = slopes[0].shape[1] // 4
    whole = pl.BlockSpec((total, width), lambda i: (0, 0))
    part = pl.BlockSpec((total, hidden), lambda i: (0, quarter(i)))
    count = len(rows)
    return width, hidden, [whole] * count + [part] * (2 * count) + [whole] * count


def cross_weight_grads(rows, slopes, active, gated):
    width, hidden, specs = weight_specs(rows, slopes, lambda i: 2 + i)
    return pl.pallas_call(
        functools.partial(cross_kernel, len(rows)),
        grid=(2,),
        in_specs=specs,
        out_specs=pl.BlockSpec((1, 2, width, hidden), lambda i: (i, 0, 0, 0)),
        out_shape=jax.ShapeDtypeStruct((2, 2, width, hidden), BF),
        compiler_params=pltpu.CompilerParams(vmem_limit_bytes=56 * MIB),
        cost_estimate=SMALL_COST,
        name="cross_weight_grads",
    )(*rows, *slopes, *active, *gated)


def kept_weight_grads(rows, slopes, active, gated, got):
    width, hidden, specs = weight_specs(rows, slopes, lambda i: 1 - i)
    fixed = pl.BlockSpec((2, width, hidden), lambda i: (0, 0, 0))
    return pl.pallas_call(
        functools.partial(kept_kernel, len(rows)),
        grid=(2,),
        in_specs=specs + [pl.BlockSpec((1, 2, width, hidden), lambda i: (1 - i, 0, 0, 0))],
        out_specs=[fixed, fixed],
        out_shape=[
            jax.ShapeDtypeStruct((2, width, hidden), BF),
            jax.ShapeDtypeStruct((2, width, hidden), F32),
        ],
        compiler_params=pltpu.CompilerParams(vmem_limit_bytes=56 * MIB),
        cost_estimate=SMALL_COST,
        name="kept_weight_grads",
    )(*rows, *slopes, *active, *gated, got)


def result_kernel(chunks, *refs):
    active, gates, seconds, out_ref = refs[:chunks], refs[chunks : 2 * chunks], refs[2 * chunks : -1], refs[-1]
    for c in range(chunks):

        @pl.when(pl.program_id(0) == c)
        def _(c=c):
            width = seconds[0].shape[0]
            total = None
            for r, second in enumerate(seconds):
                total = put(total, dot(active[c][:, r * width : (r + 1) * width], second[...]))
            rows = (total * gates[c][:, :1]).astype(BF)
            if chunks > 1:
                out_ref[:, 0] = rows.reshape(out_ref.shape[0], out_ref.shape[2], out_ref.shape[3])
            else:
                out_ref[...] = rows


def expert_results(active, gates, seconds, experts):
    chunks = len(active)
    total, hidden = active[0].shape
    width = seconds[0].shape[1]
    block = row_block(total)
    steps = total // block

    def here(c, cols):
        return pl.BlockSpec((block, cols), lambda g, i: (jnp.where(g == c, i, jnp.where(g < c, 0, steps - 1)), 0))

    chunk = total // experts
    if chunks > 1:
        shape = (experts, chunks, chunk, width)
        out_spec = pl.BlockSpec((block // chunk, 1, chunk, width), lambda g, i: (i, g, 0, 0))
    else:
        shape = (total, width)
        out_spec = pl.BlockSpec((block, width), lambda g, i: (i, 0))
    out = pl.pallas_call(
        functools.partial(result_kernel, chunks),
        grid=(chunks, steps),
        in_specs=[here(c, hidden) for c in range(chunks)]
        + [here(c, TILE) for c in range(chunks)]
        + [pl.BlockSpec(w.shape, lambda g, i: (0, 0)) for w in seconds],
        out_specs=out_spec,
        out_shape=jax.ShapeDtypeStruct(shape, BF),
        compiler_params=pltpu.CompilerParams(vmem_limit_bytes=56 * MIB),
        cost_estimate=SMALL_COST,
        name="expert_results",
    )(*active, *gates, *seconds)
    return out.reshape(experts, chunks * chunk, width)


def last_sum_kernel(kept_ref, y_ref, out_first, out_second):
    for n, out in enumerate((out_first, out_second)):
        out[...] = kept_ref[n] + y_ref[n].astype(F32)


def last_sums(kept, got_y):
    _, width, hidden = kept.shape
    block = 256
    here = pl.BlockSpec((block, hidden), lambda i: (i, 0))
    part = pl.BlockSpec((2, block, hidden), lambda i: (0, i, 0))
    return pl.pallas_call(
        last_sum_kernel,
        grid=(width // block,),
        in_specs=[part, part],
        out_specs=[here, here],
        out_shape=[jax.ShapeDtypeStruct((width, hidden), F32)] * 2,
        compiler_params=pltpu.CompilerParams(vmem_limit_bytes=40 * MIB),
        cost_estimate=SMALL_COST,
        name="last_sums",
    )(kept, got_y)


def send_kernel(micro_ref, code_ref, rows_ref, out_ref):
    block = out_ref.shape[0]
    ids = lax.broadcasted_iota(jnp.int32, (block, 1), 0) + pl.program_id(0) * block
    hot = jnp.where((ids == code_ref[:1]) | (ids == code_ref[1:2]), 1.0, 0.0).astype(BF)
    out_ref[...] = dot(hot, rows_ref[0]).astype(BF)


def send_rows(micro, code, rows, count):
    width = rows.shape[2]
    block = next(b for b in (336, 320, 384, count) if count % b == 0)
    return pl.pallas_call(
        send_kernel,
        grid_spec=pltpu.PrefetchScalarGridSpec(
            num_scalar_prefetch=1,
            grid=(count // block,),
            in_specs=[
                pl.BlockSpec(code.shape, lambda i, m: (0, 0)),
                pl.BlockSpec((1, SEQ, width), lambda i, m: (m[0], 0, 0)),
            ],
            out_specs=pl.BlockSpec((block, width), lambda i, m: (i, 0)),
        ),
        out_shape=jax.ShapeDtypeStruct((count, width), BF),
        compiler_params=pltpu.CompilerParams(vmem_limit_bytes=40 * MIB),
        cost_estimate=SMALL_COST,
        name="send_rows",
    )(micro, code, rows)


def place_kernel(place_ref, one_ref, two_ref, *refs):
    for n, piece in enumerate((one_ref, two_ref)):

        @pl.when(pl.program_id(0) == n)
        def _(piece=piece):
            for k, out_ref in enumerate(refs[-2:]):
                out_ref[0] = piece[k]


def place_pieces(places, pieces, before=()):
    two, rows, width = pieces[0].shape
    whole = pl.BlockSpec(pieces[0].shape, lambda i, place_ref: (0, 0, 0))
    return pl.pallas_call(
        place_kernel,
        grid_spec=pltpu.PrefetchScalarGridSpec(
            num_scalar_prefetch=1,
            grid=(2,),
            in_specs=[whole] * 2 + [pl.BlockSpec(memory_space=pl.ANY)] * len(before),
            out_specs=[pl.BlockSpec((1, rows, width), lambda i, place_ref: (place_ref[i], 0, 0))] * two,
        ),
        out_shape=[jax.ShapeDtypeStruct((4, rows, width), pieces[0].dtype)] * two,
        input_output_aliases={3: 0, 4: 1} if before else {},
        compiler_params=pltpu.CompilerParams(vmem_limit_bytes=40 * MIB),
        cost_estimate=SMALL_COST,
        name="place_pieces",
    )(places, *pieces, *before)


def swap(value, axis, count, bit):
    return lax.ppermute(value, axis, [(i, i ^ bit) for i in range(count)])


def all_to_all(value):
    return lax.all_to_all(value, "dp", split_axis=0, concat_axis=0, tiled=True)


def together(*values):
    return lax.optimization_barrier(values)


def local(
    layer_input, out_grad, first_gain, query_weight, key_weight, value_weight, output_weight,
    position_bias, second_gain, router_weight, expert_in, expert_out, seq_lengths, routes,
):
    micro_count, tok_rows, width = layer_input.shape
    dp_count = lax.axis_size("dp")
    expert_count = router_weight.shape[1]
    shard = query_weight.shape[1]
    heads_here = position_bias.shape[0]
    assert lax.axis_size("tensor") == 4 and micro_count == 2 and expert_count == dp_count
    assert tok_rows == SEQ and seq_lengths.shape[1] == 1
    capacity = max(8, 8 * (10 * tok_rows // (32 * expert_count)))
    half = capacity // 2
    stride = 8 * (half // 8 + 1)
    by_lines = dp_count == 8
    chunks = 2 if half % 32 == 0 else 1
    chunk = half // chunks
    chunk_rows = expert_count * chunk
    rows_here = query_weight.shape[0]
    me = lax.axis_index("dp")
    rank = lax.axis_index("tensor")
    micro = rank // 2
    core = rank % 2

    def swap_y(value):
        return swap(value, "tensor", 4, 2)

    def swap_core(value):
        return swap(value, "tensor", 4, 1)

    micro_arg = micro.reshape(1).astype(jnp.int32)
    core_arg = core.reshape(1).astype(jnp.int32)

    packed = pack_weights(query_weight, key_weight, value_weight, output_weight, first_gain, second_gain, router_weight)
    three = 3 * TILE

    def doubled(stacked, bit, axis=0):
        other = swap(stacked, "dp", dp_count, bit)
        high = (me & bit) != 0
        pair = jnp.where(high, jnp.stack([other, stacked], axis + 1), jnp.stack([stacked, other], axis + 1))
        return pair.reshape(stacked.shape[:axis] + (-1,) + stacked.shape[axis + 1 :])

    stacked = packed[None]
    bit = dp_count // 2
    while bit > 1:
        stacked = doubled(stacked, bit)
        bit //= 2
    length = lax.dynamic_index_in_dim(seq_lengths, micro, 0, keepdims=False)
    route = lax.dynamic_index_in_dim(routes, micro, 0, keepdims=False).T
    expert_ids = jnp.arange(expert_count, dtype=jnp.int32)
    named = (expert_ids[:, None, None] == route[None]).astype(jnp.int32)
    per_token = jnp.sum(named, axis=1, dtype=jnp.int32)
    earlier = jnp.cumsum(per_token, axis=1, dtype=jnp.int32) - per_token
    slot = jnp.sum(named * earlier[:, None, :], axis=0, dtype=jnp.int32)
    here = slot // half == core
    within = slot % half
    chunk_of = within // chunk
    inside = within % chunk
    spare = 16 * -(-chunk // 16)
    last_stride = spare + 16
    last = (chunks - 1) * chunk_rows
    code_back = jnp.where(
        chunk_of == chunks - 1, last + route * last_stride + inside, chunk_of * chunk_rows + route * chunk + inside
    )
    code_back = code_back + jnp.where(here, 0, last + expert_count * last_stride)
    code_result = route * half + within + jnp.where(here, 0, expert_count * half)
    info = jnp.concatenate([code_back, route, slot, code_result], 0)

    code_grads = jnp.where(here, route * stride + within, -1)
    valid = jnp.arange(SEQ, dtype=jnp.int32) < length[0]
    ids = jnp.arange(expert_count * stride, dtype=jnp.int32)[:, None]
    partner = jnp.sum(
        jnp.where(ids == code_grads[:1], route[1:], 0) + jnp.where(ids == code_grads[1:], route[:1], 0), axis=1, dtype=jnp.int32
    )
    grads_sent = send_rows(micro_arg, jnp.where(valid[None], code_grads, -1), out_grad, expert_count * stride)
    grads_sent = grads_sent.reshape(expert_count, stride, width)
    partner_row = jnp.pad(partner.reshape(expert_count, stride)[:, :half].astype(BF), ((0, 0), (0, width - half)))
    grads_sent = grads_sent.at[:, half].set(partner_row)
    stacked, grads_sent, position_bias = together(stacked, grads_sent, position_bias)
    if by_lines:
        lines = [list(range(x, dp_count, 2)) for x in range(2)]
        grads_z = lax.all_to_all(
            grads_sent.reshape(dp_count // 2, 2, stride, width), "dp", split_axis=0, concat_axis=0,
            axis_index_groups=lines, tiled=True,
        )

    first_own = expert_in[0]
    second_own = expert_out[0]
    part_b = stacked[:, :, :three]
    far_b = swap_y(part_b)
    part_a = doubled(stacked[:, :, three:], 1)
    part_a, far_b = together(part_a, far_b)
    pair_b = jnp.stack([part_b, far_b])
    a_own = part_a[:, :, :three]
    a_far = swap_y(a_own).reshape(width, three)
    a_own = a_own.reshape(width, three)
    pair_b = doubled(pair_b, 1, 1).reshape(2, width, three)
    if by_lines:
        a_far, pair_b, first_own = together(a_far, pair_b, first_own)
    else:
        a_far, pair_b, grads_sent, first_own = together(a_far, pair_b, grads_sent, first_own)
    first_y = swap_y(first_own)
    small_all = part_a[:, :, three:].reshape(width, TILE)
    gain_one = small_all[:, expert_count].astype(F32)[None]
    gain_two = small_all[:, expert_count + 1].astype(F32)[None]
    router_wide = small_all
    far_bias = swap_y(position_bias)
    bias = jnp.concatenate([position_bias[:2], far_bias[:2], position_bias[2:], far_bias[2:]], 0)
    head_total = bias.shape[0]
    hot_const = jnp.asarray(NEAR_HOT, dtype=BF)
    near = dot(bias, hot_const) - bias[:, NB - 1 :].astype(F32)
    near = near.reshape(head_total, 2, TILE, TILE)
    places = jnp.arange(TILE, dtype=jnp.int32)
    causal = jnp.stack([places[None, :] <= places[:, None], jnp.ones((TILE, TILE), bool)])
    near = jnp.where(causal[None], near, NEG)

    if by_lines:
        high = (me & 1) != 0
    else:
        grads_here = all_to_all(grads_sent)

    qkv, normed_one, qkv_weight, output_own = norm_and_project(
        micro_arg, layer_input, gain_one, a_own, a_far, pair_b[0], pair_b[1]
    )
    output_far = swap_core(output_own)
    mixed, logs = attend(length, qkv, near)
    mixed, output_far = together(mixed, output_far)
    mixed_far = swap_core(mixed)
    code_chunks = jnp.where(here, chunk_of * chunk_rows + route * chunk + inside, -1)
    if by_lines:
        sent_x = lax.dynamic_index_in_dim(grads_z, 1 - (me & 1), 1, keepdims=False)
        mixed_far, grads_z, sent_x = together(mixed_far, grads_z, sent_x)
        got_x = swap(sent_x, "dp", dp_count, 1)
    residual, *parts = residual_and_rows(
        micro_arg, layer_input, mixed, mixed_far, output_own, output_far, gain_two, code_chunks, chunk_rows, chunks
    )

    if by_lines:
        parts, first_y, second_own = together(parts, first_y, second_own)
        kept_x = jnp.where(high, grads_z[:, 1], grads_z[:, 0])
        pair_x = jnp.where(high, jnp.stack([got_x, kept_x], 1), jnp.stack([kept_x, got_x], 1))
        grads_here = pair_x.reshape(dp_count, stride, width)
    else:
        parts, grads_here, first_y, second_own = together(parts, grads_here, first_y, second_own)
    second_y = swap_y(second_own)
    parts = [part.reshape(expert_count, chunk, width) for part in parts]
    arrived = [all_to_all(parts[0])]
    partner_here = grads_here[:, half, :half].astype(jnp.int32)

    def chunk_grads(c):
        at = slice(c * chunk, (c + 1) * chunk)
        return grads_here[:, at].reshape(chunk_rows, width), partner_here[:, at].reshape(chunk_rows, 1)

    grads_parts = [chunk_grads(c) for c in range(chunks)]
    arrived[0], grads_parts, second_y = together(arrived[0], grads_parts, second_y)

    firsts = (first_own, first_y, swap_core(first_own), swap_core(first_y))
    seconds = (second_own, second_y, swap_core(second_own), swap_core(second_y))

    for c in range(1, chunks):
        sent, arrived[-1] = together(parts[c], arrived[-1])
        arrived.append(all_to_all(sent))

    me_arg = me.reshape(1).astype(jnp.int32)
    rows_all, slopes, active, gated, gates, backs = [], [], [], [], [], []
    line = None
    for c in range(chunks):
        grads_c, partner_c = grads_parts[c]
        rows_c = arrived[c].reshape(chunk_rows, width)
        back, act, slo, gat, gte, line = expert_rows_pass(
            c * chunk if chunks > 1 else None, chunk, half, me_arg, partner_c, rows_c, grads_c, router_wide, line, firsts, seconds
        )
        rows_all.append(rows_c)
        slopes.append(slo)
        active.append(act)
        gated.append(gat)
        gates.append(gte)
        if chunks == 1:
            gate_grad = line[:, 0].reshape(expert_count, chunk)
            pieces = []
            for _ in range(3):
                piece = gate_grad.astype(BF)
                pieces.append(piece)
                gate_grad = gate_grad - piece.astype(F32)
            gate_row = jnp.pad(jnp.concatenate(pieces, 1), ((0, 0), (0, width - 3 * half)))
            back = jnp.pad(back.reshape(expert_count, chunk, width), ((0, 0), (0, last_stride - chunk), (0, 0)))
            back = back.at[:, spare].set(gate_row)
        if c + 1 < chunks:
            back, arrived[c + 1] = together(back.reshape(expert_count, chunk, width), arrived[c + 1])
        else:
            back, rows_all[-1], backs = together(back, rows_all[-1], backs)
        backs.append(all_to_all(back))
    grads_cross = cross_weight_grads(rows_all, slopes, active, gated)
    gates, grads_cross = together(gates, grads_cross)
    grads_in = swap_core(grads_cross)
    results = expert_results(active, gates, seconds, expert_count)
    results, grads_in = together(results, grads_in)
    grads_far, grads_kept = kept_weight_grads(rows_all, slopes, active, gated, grads_in)
    backs[-1], results, grads_far = together(backs[-1], results, grads_far)

    across_y = swap_y(grads_far)
    results_own = all_to_all(results).reshape(expert_count * half, width)

    backs_far = [swap_core(b) for b in backs]
    residual_grad, mixed_grad, extra_early, output_sent, output_kept = combine(
        micro_arg, core_arg, length, info, out_grad, residual, mixed, gain_two, router_wide, output_own,
        backs + backs_far, half, spare,
    )

    tiles, sums, far_sent, own_parts, cross_parts, sent, kept_part = attend_back(
        core_arg, length, qkv, near, mixed, logs, mixed_grad, normed_one, output_sent, output_kept, qkv_weight
    )
    arrived_cross = all_to_all(cross_parts.reshape(dp_count, rows_here, cross_parts.shape[1]))
    far_got = swap_y(far_sent)
    sent, results_own = together(sent, results_own)
    got = swap_core(sent)
    rows_both, extra_late = both_rows(
        expert_count, micro_arg, core_arg, length, kept_part, got, layer_input, gain_one, residual_grad,
        info, residual, results_own, swap_core(results_own),
    )
    rows_both, across_y, tiles = together(rows_both, across_y, tiles)
    late_far = swap_core(extra_late)
    corner = micro * 2 + core
    corners = jnp.stack([corner, corner ^ 1, corner ^ 2, corner ^ 3]).astype(jnp.int32)
    rows_y = swap_y(rows_both)
    expert_in_grad, expert_out_grad = last_sums(grads_kept, across_y)
    placed = place_pieces(corners[:2], (rows_both, swap_core(rows_both)))

    tiles = tiles.reshape(head_total, 2 * TILE * TILE)
    tiles_high = tiles.astype(BF)
    tiles_rest = (tiles - tiles_high.astype(F32)).astype(BF)
    table = dot(tiles_high, hot_const, NT) + dot(tiles_rest, hot_const, NT)
    far_sum = jnp.sum(sums[:, :, 0], axis=1) - jnp.sum(table[:, : NB - 1], axis=1)
    table = jnp.concatenate([table[:, : NB - 1], far_sum[:, None]], 1)
    table_own = jnp.concatenate([table[0:2], table[4:5]], 0)
    table_far = jnp.concatenate([table[2:4], table[5:6]], 0)
    table_cols = heads_here * NB // rows_here
    table_both = jnp.concatenate([table_own.reshape(rows_here, table_cols), table_far.reshape(rows_here, table_cols)], 1)
    base = expert_count + 2
    kept = base + 2 * table_cols
    table_tile = jnp.tile(jnp.pad(table_both, ((0, 0), (base, TILE - kept))), (dp_count, 1))

    grads = packed_sums(kept, own_parts, far_got, extra_early, extra_late, late_far, table_tile)
    grads, arrived_cross = together(grads, arrived_cross)
    cross_own, cross_far = first_sums(arrived_cross)
    arrived_grads = all_to_all(grads.reshape(dp_count, rows_here, grads.shape[1]))
    rows_y, expert_in_grad, expert_out_grad, placed, arrived_grads = together(
        rows_y, expert_in_grad, expert_out_grad, placed, arrived_grads
    )
    placed = place_pieces(corners[2:], (rows_y, swap_core(rows_y)), placed)
    cross_got = swap_y(cross_far)
    layer_output, input_grad = (out.reshape(2, SEQ, width) for out in placed)
    query_grad, key_grad, value_grad, output_grad, small = final_sums(
        kept, arrived_grads, cross_own, cross_got, shard
    )
    small_y = swap_y(small)
    both = small + small_y
    table_sum = small[:, base : base + table_cols] + small_y[:, base + table_cols : kept]
    return (
        layer_output,
        input_grad,
        both[:, expert_count],
        query_grad,
        key_grad,
        value_grad,
        output_grad.T,
        table_sum.reshape(heads_here, NB),
        both[:, expert_count + 1],
        both[:, :expert_count],
        expert_in_grad[None],
        expert_out_grad[None],
    )


def solution(mesh):
    return jax.shard_map(
        local,
        mesh=mesh,
        in_specs=(
            P(None, "dp", None),
            P(None, "dp", None),
            P("dp"),
            P("dp", "tensor"),
            P("dp", "tensor"),
            P("dp", "tensor"),
            P("tensor", "dp"),
            P("tensor", None),
            P("dp"),
            P("dp", None),
            P("dp", None, "tensor"),
            P("dp", "tensor", None),
            P(None, "dp"),
            P(None, "dp", None),
        ),
        out_specs=(
            P(None, "dp", None),
            P(None, "dp", None),
            P("dp"),
            P("dp", "tensor"),
            P("dp", "tensor"),
            P("dp", "tensor"),
            P("tensor", "dp"),
            P("tensor", None),
            P("dp"),
            P("dp", None),
            P("dp", None, "tensor"),
            P("dp", "tensor", None),
        ),
        check_vma=False,
    )
```
